32 devices in a mesh: tower: 2 (over x), dp: 16 (over z, y, core).
Axes of the slice: x: 2, y: 2, z: 4, core: 2. Of those that a mesh axis runs over, the one named last changes fastest.
Arguments:
- img_tokens: bfloat16 [256, 50, 768], P(('tower', 'dp')), may hold values from -6 to 6
- txt_tokens: bfloat16 [256, 77, 512], P(('tower', 'dp')), may hold values from -6 to 6
- txt_ends: int32 [256], replicated, may hold values from 12 to 76
- valid: int32 [256, 256], P(('tower', 'dp')), may hold values from 0 to 1, as said below
- img_master: float32 [7481856], P(('tower', 'dp')), may hold values from -2 to 2, as said below
- img_moment: float32 [7481856], P(('tower', 'dp')), may hold values from -6 to 6
- img_average: float32 [7481856], P(('tower', 'dp')), may hold values from -2 to 2, as said below
- txt_master: float32 [3415040], P(('tower', 'dp')), may hold values from -2 to 2, as said below
- txt_moment: float32 [3415040], P(('tower', 'dp')), may hold values from -6 to 6
- txt_average: float32 [3415040], P(('tower', 'dp')), may hold values from -2 to 2, as said below
- scale_state: float32 [3], replicated, may hold values from -512 to 512
Outputs:
- loss: float32 [], replicated
- img_grad: float32 [256, 50, 768], P(('tower', 'dp'))
- txt_grad: float32 [256, 77, 512], P(('tower', 'dp'))
- img_master_new: float32 [7481856], P(('tower', 'dp'))
- img_moment_new: float32 [7481856], P(('tower', 'dp'))
- img_average_new: float32 [7481856], P(('tower', 'dp'))
- img_copy: bfloat16 [7481856], P(('tower', 'dp'))
- txt_master_new: float32 [3415040], P(('tower', 'dp'))
- txt_moment_new: float32 [3415040], P(('tower', 'dp'))
- txt_average_new: float32 [3415040], P(('tower', 'dp'))
- txt_copy: bfloat16 [3415040], P(('tower', 'dp'))
- scale_new: float32 [3], replicated
The draws below stay inside these ranges and needn't reach their ends.
Inputs may be any that keep to these rules, and one draw needn't show every extreme that they name: valid[i][j] equals valid[j][i], and valid[i][i] is 1. `img_master`: laid out as the first step says. `img_average`: laid out as the first step says. `txt_master`: laid out as the first step says. `txt_average`: laid out as the first step says.
All inputs are finite; a program needn't handle non-finite values.
Results may differ from the reference program's by a relative error of at most 0.02.
Values may be sent and summed in bfloat16 or wider, within the bound.
A program may use at most 320 MiB of HBM per device.

```python
import math
import jax
import jax.numpy as jnp
from jax import lax

D_IMG = 768
FF_IMG = 3072
D_TXT = 512
FF_TXT = 2048
EMB = 512
IMG_TOK = 50
TXT_LEN = 77
HEAD = 64
BATCH = 256
P_IMG = 7481856
P_TXT = 3415040


def bounded(key, entries):
    return jax.random.truncated_normal(key, -4.0, 4.0, (entries,), jnp.float32)


def layer_values(key, model_width, hidden_width, embed_width, keys_seen):
    subkeys = jax.random.split(key, 6)
    inputs_part = bounded(subkeys[0], 3 * model_width * model_width) * model_width ** (-0.5)
    output_part = bounded(subkeys[1], model_width * model_width) * (keys_seen / model_width) ** 0.5
    expand_part = bounded(subkeys[2], model_width * hidden_width) * model_width ** (-0.5)
    reduce_part = bounded(subkeys[3], hidden_width * model_width) * hidden_width ** (-0.5)
    embed_part = bounded(subkeys[4], model_width * embed_width) * model_width ** (-0.5)
    vector_count = 10 * model_width + hidden_width
    vector_part = bounded(subkeys[5], vector_count) * 0.2
    row_index = jnp.arange(vector_count) // model_width
    gain_rows = ((row_index == 0) | (row_index == 5) | (row_index == 8)).astype(jnp.float32)
    return jnp.concatenate([inputs_part, output_part, expand_part, reduce_part, embed_part, vector_part + gain_rows])


def draw_img_master(key, part):
    key = jax.random.fold_in(key, 11)
    return layer_values(key, D_IMG, FF_IMG, EMB, IMG_TOK)


def draw_img_average(key, part):
    key = jax.random.fold_in(key, 12)
    return layer_values(key, D_IMG, FF_IMG, EMB, IMG_TOK)


def draw_txt_master(key, part):
    key = jax.random.fold_in(key, 13)
    return layer_values(key, D_TXT, FF_TXT, EMB, TXT_LEN // 2)


def draw_txt_average(key, part):
    key = jax.random.fold_in(key, 14)
    return layer_values(key, D_TXT, FF_TXT, EMB, TXT_LEN // 2)


def draw_scale_state(key, part):
    key = jax.random.fold_in(key, 15)
    subkeys = jax.random.split(key, 4)
    log_scale = jax.random.uniform(subkeys[0], (), jnp.float32, 2.3, 2.8)
    signs = jnp.where(jax.random.bernoulli(subkeys[2]), 1.0, -1.0)
    moment = BATCH * jax.random.uniform(subkeys[1], (), jnp.float32, 0.5, 2.0) * signs
    average = jax.random.uniform(subkeys[3], (), jnp.float32, 2.3, 2.8)
    return jnp.stack([log_scale, moment, average]).astype(jnp.float32)


def draw_valid(key, part):
    key = jax.random.fold_in(key, 16)
    draws = jax.random.randint(key, (BATCH, BATCH), 0, 1048576, jnp.int32)
    row_index = lax.broadcasted_iota(jnp.int32, (BATCH, BATCH), 0)
    col_index = lax.broadcasted_iota(jnp.int32, (BATCH, BATCH), 1)
    paired = jnp.where(row_index <= col_index, draws, draws.T)
    span = max(BATCH - 1, 1)
    row_weight = 32 + 992 * row_index // span
    col_weight = 32 + 992 * col_index // span
    limit = row_weight * col_weight
    return jnp.where(row_index == col_index, 1, (paired < limit).astype(jnp.int32)).astype(jnp.int32)


def set_ends(result, stream_key, smallest, high):
    spot = [jax.random.randint(jax.random.fold_in(stream_key, axis), (), 0, length) for axis, length in enumerate(result.shape)]
    widest = result.shape.index(max(result.shape))
    beside = spot[:widest] + [(spot[widest] + 1) % result.shape[widest]] + spot[widest + 1:]
    return result.at[tuple(spot)].set(smallest).at[tuple(beside)].set(high)


def block_levels(own_key, shape, cuts, low, high):
    def one(position, parts):
        steps = jax.random.uniform(jax.random.fold_in(jax.random.fold_in(own_key, 6), position), (parts,), jnp.float32, low / len(cuts), high / len(cuts))
        return jnp.repeat(jnp.exp(steps), shape[position] // parts).reshape((-1,) + (1,) * (len(shape) - position - 1))

    loudness = one(*cuts[0])
    for cut in cuts[1:]:
        loudness = loudness * one(*cut)
    return loudness


def bell_draw(stream_key, extent, deviation, reach, shards=(), held_as=jnp.bfloat16):
    factor_of = block_levels(stream_key, extent, shards, -0.22, 0.18) if shards else 1.0
    result = jax.random.normal(stream_key, extent, jnp.float32) * deviation * factor_of
    return jnp.minimum(jnp.maximum(result, -reach), reach).astype(held_as)


def setup_inputs(seed: int = 0) -> dict:
    key_list = jax.random.split(jax.random.key(seed), 12)
    img_tokens = bell_draw(key_list[0], (BATCH, IMG_TOK, D_IMG), 1.0, 6.0, ((0, 32),))
    txt_tokens = bell_draw(key_list[1], (BATCH, TXT_LEN, D_TXT), 1.0, 6.0, ((0, 32),))
    txt_ends = set_ends(jax.random.randint(key_list[2], (BATCH,), max(2, TXT_LEN // 6), TXT_LEN), jax.random.fold_in(key_list[2], 1), max(2, TXT_LEN // 6), TXT_LEN - 1).astype(jnp.int32)
    valid = draw_valid(jax.random.fold_in(key_list[11], 71), 0)
    img_master = draw_img_master(jax.random.fold_in(key_list[11], 71), 0)
    img_moment = bell_draw(key_list[5], (P_IMG,), (0.08 * BATCH ** 0.5), 6.0, ((0, 32),), jnp.float32)
    img_average = draw_img_average(jax.random.fold_in(key_list[11], 71), 0)
    txt_master = draw_txt_master(jax.random.fold_in(key_list[11], 71), 0)
    txt_moment = bell_draw(key_list[8], (P_TXT,), (0.08 * BATCH ** 0.5), 6.0, ((0, 32),), jnp.float32)
    txt_average = draw_txt_average(jax.random.fold_in(key_list[11], 71), 0)
    scale_state = draw_scale_state(jax.random.fold_in(key_list[11], 71), 0)
    return dict(img_tokens=img_tokens, txt_tokens=txt_tokens, txt_ends=txt_ends, valid=valid, img_master=img_master, img_moment=img_moment, img_average=img_average, txt_master=txt_master, txt_moment=txt_moment, txt_average=txt_average, scale_state=scale_state)


@jax.custom_vjp
def low(v):
    return lax.optimization_barrier(v.astype(jnp.bfloat16)).astype(jnp.float32)

@jax.custom_vjp
def low_back(v):
    return v

def low_keep(v):
    return (low(v), None)

def low_pass(kept, grad):
    return (grad,)

def back_keep(v):
    return (v, None)

def back_low(kept, grad):
    return (low(grad),)
low.defvjp(low_keep, low_pass)
low_back.defvjp(back_keep, back_low)
highest = lax.Precision.HIGHEST
momentum_rate = 0.5
average_rate = 0.5
step_rate = 0.08
scale_rate = 0.0001

def both_ways(value):
    return low(low_back(value))

def product(left, right):
    return jnp.matmul(left, right, precision=highest)

def contract(form, left, right):
    return jnp.einsum(form, left, right, precision=highest)

def layer_norm(values, gain_row, shift_row):
    centred = values - lax.optimization_barrier(jnp.mean(values, axis=-1, keepdims=True))
    spread = lax.optimization_barrier(jnp.mean(centred * centred, axis=-1, keepdims=True))
    return centred * lax.rsqrt(spread + 1e-05) * gain_row + shift_row

def unpack(flat_weights, model_width, hidden_width, embed_width):
    piece_shapes = [(model_width, 3 * model_width), (model_width, model_width), (model_width, hidden_width), (hidden_width, model_width), (model_width, embed_width), (10, model_width), (hidden_width,)]
    pieces = []
    offset = 0
    for piece_shape in piece_shapes:
        length = math.prod(piece_shape)
        pieces.append(flat_weights[offset:offset + length].reshape(piece_shape))
        offset = offset + length
    return pieces

def encode(tokens, flat_weights, positions, causal, model_width, hidden_width, embed_width):
    w_inputs, w_output, w_expand, w_reduce, w_embed, vectors, expand_bias = unpack(flat_weights, model_width, hidden_width, embed_width)
    groups = tokens.shape[0]
    length = tokens.shape[1]
    first = low(layer_norm(tokens, vectors[0], vectors[1]))
    bias_in = jnp.concatenate([vectors[2], jnp.zeros_like(vectors[2]), vectors[3]])
    joined = both_ways(product(first, w_inputs) + bias_in)
    joined = joined.reshape(groups, length, 3, model_width // HEAD, HEAD)
    scores = low_back(contract('gqhd,gkhd->ghqk', joined[:, :, 0], joined[:, :, 1]) * 0.125)
    if causal:
        row_index = lax.broadcasted_iota(jnp.int32, (length, length), 0)
        col_index = lax.broadcasted_iota(jnp.int32, (length, length), 1)
        scores = jnp.where(col_index <= row_index, scores, -1e+30)
    row_top = lax.optimization_barrier(jnp.max(scores, axis=-1, keepdims=True))
    raw_weights = jnp.exp(scores - row_top)
    attention = low(raw_weights / lax.optimization_barrier(jnp.sum(raw_weights, axis=-1, keepdims=True)))
    mixed_heads = both_ways(contract('ghqk,gkhd->gqhd', attention, joined[:, :, 2]).reshape(groups, length, model_width))
    middle = tokens + low_back(product(mixed_heads, w_output) + vectors[4])
    second = low(layer_norm(middle, vectors[5], vectors[6]))
    raised = low_back(product(second, w_expand) + expand_bias)
    active = low(raised * jax.nn.sigmoid(1.702 * raised))
    final_rows = middle + low_back(product(active, w_reduce) + vectors[7])
    pooled = jnp.take_along_axis(final_rows, positions[:, None, None], axis=1)[:, 0]
    pooled = low(layer_norm(pooled, vectors[8], vectors[9]))
    projected = low_back(product(pooled, w_embed))
    return low(projected * lax.rsqrt(lax.optimization_barrier(jnp.sum(projected * projected, axis=-1, keepdims=True)) + 1e-06))

def one_side(cosines, valid, logit_scale):
    logits = logit_scale * cosines
    masked = jnp.where(valid > 0, logits, -1e+30)
    row_top = lax.optimization_barrier(jnp.max(masked, axis=1, keepdims=True))
    totals = jnp.log(lax.optimization_barrier(jnp.sum(jnp.exp(masked - row_top), axis=1))) + row_top[:, 0]
    return jnp.sum(totals - jnp.diagonal(logits))

def advance(master, moment, average, grads, rate):
    moment_new = momentum_rate * moment + grads
    master_new = master - rate * (grads + momentum_rate * moment_new)
    average_new = average_rate * average + (1.0 - average_rate) * master_new
    return (master_new, moment_new, average_new)

def reference(img_tokens, txt_tokens, txt_ends, valid, img_master, img_moment, img_average, txt_master, txt_moment, txt_average, scale_state):
    batch_rows = img_tokens.shape[0]
    img_group = math.gcd(batch_rows, 64)
    txt_group = math.gcd(batch_rows, 32)

    def objective(img_x, txt_x, img_w, txt_w, scale_log):
        img_w = low(img_w)
        txt_w = low(txt_w)

        def img_block(block_x):
            return encode(block_x, img_w, jnp.zeros((block_x.shape[0],), jnp.int32), False, D_IMG, FF_IMG, EMB)

        def txt_block(paired):
            return encode(paired[0], txt_w, paired[1], True, D_TXT, FF_TXT, EMB)
        img_emb = lax.map(jax.checkpoint(img_block), img_x.reshape(batch_rows // img_group, img_group, IMG_TOK, D_IMG)).reshape(batch_rows, EMB)
        txt_emb = lax.map(jax.checkpoint(txt_block), (txt_x.reshape(batch_rows // txt_group, txt_group, TXT_LEN, D_TXT), txt_ends.reshape(batch_rows // txt_group, txt_group))).reshape(batch_rows, EMB)
        logit_scale = jnp.exp(scale_log)
        row_cos = low_back(product(img_emb, txt_emb.T))
        col_cos = low_back(product(txt_emb, img_emb.T))
        return 0.5 * (one_side(row_cos, valid, logit_scale) + one_side(col_cos, valid, logit_scale))
    total_loss, pullback = jax.vjp(objective, img_tokens.astype(jnp.float32), txt_tokens.astype(jnp.float32), img_master, txt_master, scale_state[0])
    img_grad, txt_grad, img_wgrad, txt_wgrad, scale_grad = pullback(jnp.ones_like(total_loss))
    img_new = advance(img_master, img_moment, img_average, img_wgrad, step_rate)
    txt_new = advance(txt_master, txt_moment, txt_average, txt_wgrad, step_rate)
    scale_parts = advance(scale_state[0], scale_state[1], scale_state[2], scale_grad, scale_rate)
    scale_new = jnp.stack([scale_parts[0], scale_parts[1], scale_parts[2]])
    return (total_loss / batch_rows, img_grad, txt_grad, img_new[0], img_new[1], img_new[2], img_new[0].astype(jnp.bfloat16), txt_new[0], txt_new[1], txt_new[2], txt_new[0].astype(jnp.bfloat16), scale_new)
```

```python
import functools
import math

import jax
import jax.numpy as jnp
from jax import lax
from jax.experimental import pallas as pl
from jax.experimental.pallas import tpu as pltpu
from jax.sharding import PartitionSpec as P

D_IMG = 768
FF_IMG = 3072
D_TXT = 512
FF_TXT = 2048
EMB = 512
HEAD = 64


momentum_rate = 0.5
average_rate = 0.5
step_rate = 0.08
scale_rate = 0.0001


MESH = pl.DeviceIdType.MESH
ANY = pl.BlockSpec(memory_space=pl.ANY)
GRANT = 56 * 1024 * 1024
LANES = 128


def here():
    return lax.axis_index("tower"), lax.axis_index("dp")


def greet(devices):
    barrier = pltpu.get_barrier_semaphore()
    for device in devices:
        pl.semaphore_signal(barrier, inc=1, device_id=device, device_id_type=MESH)
    pl.semaphore_wait(barrier, len(devices))


def remote(src, dst, send_sem, recv_sem, device):
    return pltpu.make_async_remote_copy(
        src_ref=src,
        dst_ref=dst,
        send_sem=send_sem,
        recv_sem=recv_sem,
        device_id=device,
        device_id_type=MESH,
    )


def comm_params(number):
    return pltpu.CompilerParams(
        collective_id=number, has_side_effects=True, vmem_limit_bytes=GRANT
    )


def group_kernel(scattered, x_ref, o_ref, send_sem, recv_sem, own_sem):
    tower, at = here()
    chip, core = at // 2, at % 2
    others = [(chip + k) % 8 for k in range(1, 8)]
    greet([(tower, other * 2 + core) for other in others])
    own = pltpu.make_async_copy(x_ref.at[chip] if scattered else x_ref, o_ref.at[chip], own_sem)
    own.start()
    sent = []
    for k, other in enumerate(others):
        copy = remote(
            x_ref.at[other] if scattered else x_ref,
            o_ref.at[chip],
            send_sem.at[k],
            recv_sem.at[k],
            (tower, other * 2 + core),
        )
        copy.start()
        sent.append(copy)
    own.wait()
    for k, copy in enumerate(sent):
        copy.wait_send()
        source = (chip + 7 - k) % 8
        remote(
            x_ref.at[chip] if scattered else x_ref,
            o_ref.at[source],
            send_sem.at[k],
            recv_sem.at[k],
            (tower, at),
        ).wait_recv()


def group_exchange(value, scattered, number, space=pl.ANY):
    block = value.shape[1:] if scattered else value.shape
    spec = pl.BlockSpec(memory_space=space)
    return pl.pallas_call(
        functools.partial(group_kernel, scattered),
        out_shape=jax.ShapeDtypeStruct((8, *block), value.dtype),
        in_specs=[spec],
        out_specs=spec,
        scratch_shapes=[
            pltpu.SemaphoreType.DMA((7,)),
            pltpu.SemaphoreType.DMA((7,)),
            pltpu.SemaphoreType.DMA,
        ],
        compiler_params=comm_params(number),
    )(value)


def spread_kernel(x_ref, o_ref, send_sem, recv_sem, own_sem, core_sems):
    tower, at = here()
    chip, core = at // 2, at % 2
    place = tower * 8 + chip
    others = [(place + k) % 16 for k in range(1, 16)]
    homes = [(other // 8, (other % 8) * 2 + core) for other in others]
    sibling = (tower, chip * 2 + 1 - core)
    greet([*homes, sibling])
    own = pltpu.make_async_copy(x_ref, o_ref.at[core, place], own_sem)
    own.start()
    sent = []
    for k, home in enumerate(homes):
        copy = remote(
            x_ref, o_ref.at[core, place], send_sem.at[k], recv_sem.at[k], home
        )
        copy.start()
        sent.append(copy)
    own.wait()
    for k, copy in enumerate(sent):
        source = (place + 15 - k) % 16
        remote(
            x_ref, o_ref.at[core, source], send_sem.at[k], recv_sem.at[k], sibling
        ).wait_recv()
    across = remote(o_ref.at[core], o_ref.at[core], core_sems.at[0], core_sems.at[1], sibling)
    across.start()
    for copy in sent:
        copy.wait_send()
    across.wait_send()
    remote(
        o_ref.at[1 - core], o_ref.at[1 - core], core_sems.at[0], core_sems.at[1], sibling
    ).wait_recv()


def spread(value, number, space=pl.ANY):
    spec = pl.BlockSpec(memory_space=space)
    return pl.pallas_call(
        spread_kernel,
        out_shape=jax.ShapeDtypeStruct((2, 16, *value.shape), value.dtype),
        in_specs=[spec],
        out_specs=spec,
        scratch_shapes=[
            pltpu.SemaphoreType.DMA((15,)),
            pltpu.SemaphoreType.DMA((15,)),
            pltpu.SemaphoreType.DMA,
            pltpu.SemaphoreType.DMA((2,)),
        ],
        compiler_params=comm_params(number),
    )(value)


def exchange_kernel(count, *refs):
    gather_src, sib_src, one_src, zero_src = refs[:4]
    blocks_src = refs[4 : 4 + count]
    gather_dst, sib_dst, one_dst, zero_dst = refs[4 + count : 8 + count]
    blocks_dst = refs[8 + count : 8 + 2 * count]
    (
        ring_send,
        ring_recv,
        core_send,
        core_recv,
        block_send,
        block_recv,
        pair_sems,
        own_sems,
    ) = refs[8 + 2 * count :]
    tower, at = here()
    deep, row, core = at // 4, (at // 2) % 2, at % 2
    sibling = (tower, at + 1 - 2 * core)
    beside = (tower, deep * 4 + (1 - row) * 2 + core)
    partner = (1 - tower, at)

    def spot(z, y):
        return (z % 4) * 4 + y * 2 + core

    others = [(tower, (at + k) % 16) for k in range(1, 16)]
    greet([*others, partner])

    @pl.when(tower == 0)
    def _():
        remote(zero_src, zero_dst, pair_sems.at[0], pair_sems.at[1], partner).start()

    @pl.when(tower == 1)
    def _():
        remote(one_src, one_dst, pair_sems.at[0], pair_sems.at[1], partner).start()

    owns = [
        pltpu.make_async_copy(gather_src, gather_dst.at[at], own_sems.at[0]),
        pltpu.make_async_copy(sib_src, sib_dst.at[core], own_sems.at[1 + count]),
    ]
    for b in range(count):
        owns.append(
            pltpu.make_async_copy(
                blocks_src[b].at[at], blocks_dst[b].at[at], own_sems.at[1 + b]
            )
        )
    for own in owns:
        own.start()
    sent = []

    def launch(copy):
        copy.start()
        sent.append(copy)

    for k in (1, 3, 2):
        launch(
            remote(
                gather_src,
                gather_dst.at[at],
                ring_send.at[k - 1],
                ring_recv.at[k - 1],
                (tower, spot(deep + k, row)),
            )
        )
    launch(remote(gather_src, gather_dst.at[at], ring_send.at[3], ring_recv.at[3], beside))
    launch(remote(gather_src, gather_dst.at[at], core_send.at[0], core_recv.at[0], sibling))
    launch(remote(sib_src, sib_dst.at[core], core_send.at[8], core_recv.at[8], sibling))
    for b in range(count):
        for k in range(1, 16):
            to = (at + k) % 16
            launch(
                remote(
                    blocks_src[b].at[to],
                    blocks_dst[b].at[at],
                    block_send.at[b, k - 1],
                    block_recv.at[b, k - 1],
                    (tower, to),
                )
            )

    def arrived(slot, sems, index):
        remote(gather_src, gather_dst.at[slot], sems.at[index], sems.at[index], sibling).wait_recv()

    for k in (1, 3, 2):
        slot = spot(deep + 4 - k, row)
        arrived(slot, ring_recv, k - 1)
        launch(
            remote(
                gather_dst.at[slot],
                gather_dst.at[slot],
                ring_send.at[3 + k],
                ring_recv.at[3 + k],
                beside,
            )
        )
        launch(
            remote(
                gather_dst.at[slot],
                gather_dst.at[slot],
                core_send.at[k],
                core_recv.at[k],
                sibling,
            )
        )
    for k in (0, 1, 3, 2):
        slot = spot(deep + 4 - k, 1 - row)
        arrived(slot, ring_recv, 3 + k)
        launch(
            remote(
                gather_dst.at[slot],
                gather_dst.at[slot],
                core_send.at[4 + k],
                core_recv.at[4 + k],
                sibling,
            )
        )
    for y in range(2):
        for k in range(4):
            z = (deep + 4 - k) % 4
            side = row if y == 0 else 1 - row
            slot = z * 4 + side * 2 + 1 - core
            arrived(slot, core_recv, 4 * y + k)
    remote(sib_src, sib_dst.at[1 - core], core_send.at[8], core_recv.at[8], sibling).wait_recv()
    for b in range(count):
        for k in range(1, 16):
            source = (at + 16 - k) % 16
            remote(
                blocks_src[b].at[at],
                blocks_dst[b].at[source],
                block_send.at[b, k - 1],
                block_recv.at[b, k - 1],
                sibling,
            ).wait_recv()
    for copy in sent:
        copy.wait_send()
    for own in owns:
        own.wait()

    @pl.when(tower == 0)
    def _():
        remote(zero_src, zero_dst, pair_sems.at[0], pair_sems.at[1], partner).wait_send()
        remote(one_src, one_dst, pair_sems.at[0], pair_sems.at[1], partner).wait_recv()

    @pl.when(tower == 1)
    def _():
        remote(one_src, one_dst, pair_sems.at[0], pair_sems.at[1], partner).wait_send()
        remote(zero_src, zero_dst, pair_sems.at[0], pair_sems.at[1], partner).wait_recv()


def exchange(gathered, sibling, from_one, from_zero, blocks, number):
    count = len(blocks)
    like = jax.ShapeDtypeStruct
    return pl.pallas_call(
        functools.partial(exchange_kernel, count),
        out_shape=[
            like((16, *gathered.shape), gathered.dtype),
            like((2, *sibling.shape), sibling.dtype),
            like(from_one.shape, from_one.dtype),
            like(from_zero.shape, from_zero.dtype),
            *[like(block.shape, block.dtype) for block in blocks],
        ],
        in_specs=[ANY] * (4 + count),
        out_specs=[ANY] * (4 + count),
        scratch_shapes=[
            pltpu.SemaphoreType.DMA((7,)),
            pltpu.SemaphoreType.DMA((7,)),
            pltpu.SemaphoreType.DMA((9,)),
            pltpu.SemaphoreType.DMA((9,)),
            pltpu.SemaphoreType.DMA((count, 15)),
            pltpu.SemaphoreType.DMA((count, 15)),
            pltpu.SemaphoreType.DMA((2,)),
            pltpu.SemaphoreType.DMA((2 + count,)),
        ],
        compiler_params=comm_params(number),
    )(gathered, sibling, from_one, from_zero, *blocks)


class Plan:
    def __init__(self, tower, share, rows, per_device):
        self.tower = tower
        self.share = share
        self.rows = rows
        self.chunk = rows * LANES
        self.per_device = per_device
        self.slots = sum(per_device) + 1
        self.total = 16 * sum(per_device) + 1
        spans = [self.span(device) for device in range(32)]
        self.counts = sorted({last - first + 1 for first, last in spans})
        self.local = self.counts[-1]

    def span(self, device):
        first = device * self.share // self.chunk
        last = ((device + 1) * self.share - 1) // self.chunk
        return first, min(last, self.total - 1)

    def bounds(self, device):
        first = device * self.share // self.chunk
        last = ((device + 1) * self.share - 1) // self.chunk
        return first, jnp.minimum(last, self.total - 1)

    def target(self, g):
        base, slot_base = 0, 0
        at, slot = jnp.int32(0), jnp.int32(0)
        for n in self.per_device:
            inside = g >= base
            at = jnp.where(inside, (g - base) // n, at)
            slot = jnp.where(inside, slot_base + (g - base) % n, slot)
            base += 16 * n
            slot_base += n
        return at, slot

    def global_chunk(self, at, slot):
        base, slot_base = 0, 0
        g = jnp.int32(0)
        for n in self.per_device:
            g = jnp.where(slot >= slot_base, base + at * n + (slot - slot_base), g)
            base += 16 * n
            slot_base += n
        return jnp.where(slot == self.slots - 1, self.total - 1, g)


def everyone(tower, at):
    me = tower * 16 + at
    result = []
    for k in range(1, 32):
        other = (me + k) % 32
        result.append((other // 16, other % 16))
    return result


def deal_kernel(plans, *refs):
    img_src, txt_src, valid_src = refs[:3]
    img_dst, txt_dst, valid_dst = refs[3:6]
    img_extra, txt_extra, img_last, txt_last = refs[6:10]
    chunk_send, deal_recv, edge_sems, last_sems, valid_send, valid_recv = refs[10:]
    tower, at = here()
    me = tower * 16 + at
    homes = everyone(tower, at)
    greet(homes)
    sides = [
        (plans[0], img_src, img_dst, img_extra, img_last),
        (plans[1], txt_src, txt_dst, txt_extra, txt_last),
    ]
    below = ((me + 31) % 32 // 16, (me + 31) % 32 % 16)

    for s, (plan, src, dst, extra, last) in enumerate(sides):

        @pl.when(me > 0)
        def _():
            remote(src.at[0], extra, edge_sems.at[s, 0], edge_sems.at[s, 1], below).start()

    def to_block(plan, s, i, slot_src, dst, at_to, slot, wait):
        far = jnp.logical_or(tower != plan.tower, at_to != at)

        @pl.when(far)
        def _():
            copy = remote(
                slot_src,
                dst.at[slot],
                chunk_send.at[s, i],
                deal_recv.at[s],
                (jnp.int32(plan.tower), at_to),
            )
            if wait:
                copy.wait_send()
            else:
                copy.start()

        if not wait:

            @pl.when(jnp.logical_not(far))
            def _():
                pltpu.make_async_copy(slot_src, dst.at[slot], deal_recv.at[s]).start()

    def whole_chunks(plan, s, src, dst, wait):
        first, last_chunk = plan.bounds(me)

        def step(i, carry):
            g = first + i
            inside = jnp.logical_and(
                jnp.logical_or(i > 0, me == 0),
                jnp.logical_and(g <= last_chunk, jnp.logical_or(g < last_chunk, me == 31)),
            )
            inside = jnp.logical_and(inside, g < plan.total - 1)

            @pl.when(inside)
            def _():
                at_to, slot = plan.target(g)
                to_block(plan, s, i, src.at[i], dst, at_to, slot, wait)

            return carry

        lax.fori_loop(0, plan.local, step, 0)

        @pl.when(me == 31)
        def _():
            i = last_chunk - first

            def each(k, carry):
                to_block(
                    plan, s, plan.local + k, src.at[i], dst, k, plan.slots - 1, wait
                )
                return carry

            lax.fori_loop(0, 16, each, 0)

    for s, (plan, src, dst, extra, last) in enumerate(sides):
        whole_chunks(plan, s, src, dst, False)
    for k, home in enumerate(homes):
        remote(valid_src, valid_dst.at[me], valid_send.at[k], valid_recv.at[k], home).start()
    own = pltpu.make_async_copy(valid_src, valid_dst.at[me], valid_send.at[31])
    own.start()

    for s, (plan, src, dst, extra, last) in enumerate(sides):
        first, last_chunk = plan.bounds(me)

        @pl.when(me < 31)
        def _():
            fetch = pltpu.make_async_copy(src.at[last_chunk - first], last, last_sems.at[s])
            fetch.start()
            fetch.wait()
            remote(src.at[0], extra, edge_sems.at[s, 0], edge_sems.at[s, 1], below).wait_recv()
            last[...] = last[...] + extra[...]
            at_to, slot = plan.target(last_chunk)
            to_block(plan, s, plan.local + 16, last, dst, at_to, slot, False)

    for s, (plan, src, dst, extra, last) in enumerate(sides):

        @pl.when(me > 0)
        def _():
            remote(src.at[0], extra, edge_sems.at[s, 0], edge_sems.at[s, 1], below).wait_send()

        whole_chunks(plan, s, src, dst, True)
        first, last_chunk = plan.bounds(me)

        @pl.when(me < 31)
        def _():
            at_to, slot = plan.target(last_chunk)
            to_block(plan, s, plan.local + 16, last, dst, at_to, slot, True)

        @pl.when(tower == plan.tower)
        def _():
            pltpu.make_async_copy(dst, dst, deal_recv.at[s]).wait()

    own.wait()
    for k, home in enumerate(homes):
        source = (me + 31 - k) % 32
        copy = remote(
            valid_src, valid_dst.at[source], valid_send.at[k], valid_recv.at[k], home
        )
        copy.wait_send()
        copy.wait_recv()


def deal(img_chunks, txt_chunks, valid, plans, number):
    like = jax.ShapeDtypeStruct
    low = jnp.bfloat16
    most = max(plan.local for plan in plans) + 17
    shapes = [(plan.rows, LANES) for plan in plans]
    return pl.pallas_call(
        functools.partial(deal_kernel, plans),
        out_shape=[
            like((plans[0].slots, *shapes[0]), low),
            like((plans[1].slots, *shapes[1]), low),
            like((32, *valid.shape), valid.dtype),
        ],
        in_specs=[ANY] * 3,
        out_specs=[ANY] * 3,
        scratch_shapes=[
            pltpu.VMEM(shapes[0], low),
            pltpu.VMEM(shapes[1], low),
            pltpu.VMEM(shapes[0], low),
            pltpu.VMEM(shapes[1], low),
            pltpu.SemaphoreType.DMA((2, most)),
            pltpu.SemaphoreType.DMA((2,)),
            pltpu.SemaphoreType.DMA((2, 2)),
            pltpu.SemaphoreType.DMA((2,)),
            pltpu.SemaphoreType.DMA((32,)),
            pltpu.SemaphoreType.DMA((31,)),
        ],
        compiler_params=comm_params(number),
    )(img_chunks, txt_chunks, valid)


def collect_kernel(plans, *refs):
    sources, targets = refs[:2], refs[2:4]
    send_sem, recv_sem = refs[4:]
    tower, at = here()
    me = tower * 16 + at
    greet(everyone(tower, at))

    def pass_over(plan, s, wait):
        src, dst = sources[s], targets[s]

        def one(owner, slot, i, which):
            first, _ = plan.bounds(owner)
            g = plan.global_chunk(at, slot)
            far = owner != me

            @pl.when(far)
            def _():
                copy = remote(
                    src.at[slot],
                    dst.at[g - first],
                    send_sem.at[s, which, slot],
                    recv_sem.at[s],
                    (owner // 16, owner % 16),
                )
                if wait:
                    copy.wait_send()
                else:
                    copy.start()

            if not wait:

                @pl.when(jnp.logical_not(far))
                def _():
                    pltpu.make_async_copy(
                        src.at[slot], dst.at[g - first], recv_sem.at[s]
                    ).start()

        def step(slot, carry):
            g = plan.global_chunk(at, slot)
            low_owner = g * plan.chunk // plan.share
            high_owner = jnp.minimum(((g + 1) * plan.chunk - 1) // plan.share, 31)
            use = jnp.logical_or(slot < plan.slots - 1, at == 0)

            @pl.when(use)
            def _():
                one(low_owner, slot, 0, 0)

            @pl.when(jnp.logical_and(use, high_owner != low_owner))
            def _():
                one(high_owner, slot, 1, 1)

            return carry

        @pl.when(tower == plan.tower)
        def _():
            lax.fori_loop(0, plan.slots, step, 0)

    for s in range(2):
        pass_over(plans[s], s, False)
    for s in range(2):
        pass_over(plans[s], s, True)
    for s in range(2):
        plan, dst = plans[s], targets[s]
        first, last = plan.bounds(me)
        held = last - first + 1
        for n in plan.counts:

            @pl.when(held == n)
            def _():
                part = dst.at[pl.ds(0, n)]
                pltpu.make_async_copy(part, part, recv_sem.at[s]).wait()


def collect(img_slots, txt_slots, plans, number):
    like = jax.ShapeDtypeStruct
    most = max(plan.slots for plan in plans)
    return pl.pallas_call(
        functools.partial(collect_kernel, plans),
        out_shape=[
            like((plan.local, plan.rows, LANES), jnp.bfloat16) for plan in plans
        ],
        in_specs=[ANY] * 2,
        out_specs=[ANY] * 2,
        scratch_shapes=[
            pltpu.SemaphoreType.DMA((2, 2, most)),
            pltpu.SemaphoreType.DMA((2,)),
        ],
        compiler_params=comm_params(number),
    )(img_slots, txt_slots)


SEQS = 16
HEADS = 16
LOW = jnp.bfloat16
WIDE = jnp.float32


class Tower:
    def __init__(self, index, width, hidden, length, room, causal):
        self.index = index
        self.width = width
        self.hidden = hidden
        self.length = length
        self.room = room
        self.causal = causal
        self.heads = width // HEAD
        self.block = width // 16
        self.part = hidden // 8
        self.reduce_rows = hidden // 16


TOWERS = (
    Tower(0, D_IMG, FF_IMG, 50, 64, False),
    Tower(1, D_TXT, FF_TXT, 77, 80, True),
)
ROOM = 80
WIDTH = D_IMG
PART = FF_IMG // 8
AT_OUTPUT = 3 * D_IMG
AT_EMBED = 4 * D_IMG
ATTENTION = 4 * D_IMG + EMB


def each_tower(run):
    tower = lax.axis_index("tower")
    for kind in TOWERS:
        pl.when(tower == kind.index)(functools.partial(run, kind))


def dot_nn(a, b):
    return lax.dot_general(a, b, (((1,), (0,)), ((), ())), preferred_element_type=WIDE)


def dot_nt(a, b):
    return lax.dot_general(a, b, (((1,), (1,)), ((), ())), preferred_element_type=WIDE)


def dot_tn(a, b):
    return lax.dot_general(a, b, (((0,), (0,)), ((), ())), preferred_element_type=WIDE)


def standardise(rows):
    centred = rows - jnp.mean(rows, axis=-1, keepdims=True)
    spread = jnp.mean(centred * centred, axis=-1, keepdims=True)
    rate = lax.rsqrt(spread + 1e-05)
    return centred * rate, rate


def norm_back(grad, gain, hat, rate):
    scaled = grad * gain
    return rate * (
        scaled
        - jnp.mean(scaled, axis=-1, keepdims=True)
        - hat * jnp.mean(scaled * hat, axis=-1, keepdims=True)
    )


def head_mask(kind):
    row = lax.broadcasted_iota(jnp.int32, (HEADS, kind.width), 0)
    lane = lax.broadcasted_iota(jnp.int32, (HEADS, kind.width), 1)
    return (lane // HEAD == row).astype(WIDE)


def by_head(rows, mask):
    n, width = rows.shape
    return (rows[:, None, :] * mask[None]).reshape(n * HEADS, width)


def from_heads(rows, mask):
    width = rows.shape[1]
    return jnp.sum(rows.reshape(SEQS, HEADS, width) * mask[None], axis=1)


def matrix(ref, kind, start, width):
    return ref[:, : kind.block, start : start + width].reshape(kind.width, width)


def vector(vec_ref, kind, row):
    return vec_ref[row : row + 1, : kind.width]


def sequence(kind, refs, s):
    own, arrived = refs
    first, second = (own, arrived) if kind.index == 0 else (arrived, own)
    return first, second


def place_kernel(img_ref, txt_ref, att_ref, raise_ref, reduce_ref, vec_ref, flat):
    def run(kind):
        ref = img_ref if kind.index == 0 else txt_ref
        n, rows, lanes = ref.shape
        flat[: n * rows, :] = ref[...].reshape(n * rows, lanes).astype(WIDE)
        block, width = kind.block, kind.width

        def lift(base, height, pitch, c):
            return flat[pl.ds(base + c, height, stride=pitch), :].astype(LOW)

        base = 0
        for start, wide in ((0, 3 * width), (AT_OUTPUT, width)):
            pitch = wide // LANES
            for c in range(pitch):
                lane = start + c * LANES
                att_ref[:block, lane : lane + LANES] = lift(base, block, pitch, c)
            base += block * pitch
        pitch = kind.hidden // LANES
        per = kind.part // LANES
        for c in range(pitch):
            lane = c % per * LANES
            raise_ref[c // per, :block, lane : lane + LANES] = lift(base, block, pitch, c)
        base += block * pitch
        pitch = width // LANES
        for c in range(pitch):
            lane = c * LANES
            reduce_ref[: kind.reduce_rows, lane : lane + LANES] = lift(
                base, kind.reduce_rows, pitch, c
            )
        base += kind.reduce_rows * pitch
        pitch = EMB // LANES
        for c in range(pitch):
            lane = AT_EMBED + c * LANES
            att_ref[:block, lane : lane + LANES] = lift(base, block, pitch, c)
        base += block * pitch
        pitch = width // LANES
        for c in range(pitch):
            vec_ref[:, c * LANES : (c + 1) * LANES] = flat[pl.ds(base + c, 16, stride=pitch), :]

    each_tower(run)


def attend_kernel(
    ends_ref,
    img_own,
    img_in,
    txt_own,
    txt_in,
    gat_ref,
    vec_ref,
    second_ref,
    middle_ref,
    query_ref,
    keyed_ref,
    mixture_ref,
    weight_ref,
    mixed_ref,
    first_ref,
    first_scr,
    row_scr,
    at_scr,
):
    def run(kind):
        width, room = kind.width, kind.room
        gain, shift = vector(vec_ref, kind, 0), vector(vec_ref, kind, 1)
        refs = (img_own, img_in) if kind.index == 0 else (txt_own, txt_in)
        halves = sequence(kind, refs, 0)
        mask = head_mask(kind)
        positions = lax.broadcasted_iota(jnp.int32, (room, 1), 0)
        at = lax.axis_index("dp")

        for half in range(2):

            def normalise(i, carry):
                rows = halves[half][i].astype(WIDE)
                hat, _ = standardise(rows)
                first = (hat * gain + shift).astype(LOW)
                s = half * 8 + i
                first_scr[s, :room, :width] = first
                if kind.causal:
                    chosen = positions == ends_ref[(half * 16 + at) * 8 + i]
                    top = jnp.sum(jnp.where(chosen, first.astype(WIDE), 0.0), axis=0, keepdims=True)
                    raw = jnp.sum(jnp.where(chosen, rows, 0.0), axis=0, keepdims=True)
                else:
                    top, raw = first[:1].astype(WIDE), rows[:1]
                row_scr[pl.ds(s, 1), :width] = top
                at_scr[pl.ds(s, 1), :width] = raw
                return carry

            lax.fori_loop(0, 8, normalise, 0)

        tops = row_scr[:, :width].astype(LOW)
        query = dot_nn(tops, matrix(gat_ref, kind, 0, width)) + vector(vec_ref, kind, 2)
        query = query.astype(LOW)
        spread_query = by_head(query.astype(WIDE), mask).astype(LOW)
        keyed = dot_nt(spread_query, matrix(gat_ref, kind, width, width)) * 0.125
        keyed_ref[:, :width] = keyed.astype(LOW)
        query_ref[:, :width] = query
        first_ref[:, :width] = tops
        lane = lax.broadcasted_iota(jnp.int32, (HEADS, room), 1)
        live = lax.broadcasted_iota(jnp.int32, (HEADS, room), 0) < kind.heads

        for half in range(2):

            def weigh(i, carry):
                s = half * 8 + i
                start = pl.multiple_of(s * HEADS, HEADS)
                first = first_scr[s, :room, :width]
                scores = dot_nt(keyed_ref[pl.ds(start, HEADS), :width], first)
                if kind.causal:
                    allowed = lane <= ends_ref[(half * 16 + at) * 8 + i]
                else:
                    allowed = lane < kind.length
                scores = jnp.where(allowed, scores, -1e30)
                raw = jnp.exp(scores - jnp.max(scores, axis=-1, keepdims=True))
                weights = raw / jnp.sum(raw, axis=-1, keepdims=True)
                weights = jnp.where(live, weights, 0.0)
                weight_ref[s, :, :room] = weights
                mixture_ref[pl.ds(start, HEADS), :width] = dot_nn(
                    weights.astype(LOW), first
                ).astype(LOW)
                return carry

            lax.fori_loop(0, 8, weigh, 0)

        totals = jnp.sum(
            weight_ref[:, :, :room].astype(LOW).astype(WIDE), axis=-1, keepdims=True
        ).reshape(SEQS * HEADS, 1)
        valued = dot_nn(mixture_ref[:, :width], matrix(gat_ref, kind, 2 * width, width))
        valued = valued + totals * vector(vec_ref, kind, 3)
        mixed = from_heads(valued, mask).astype(LOW)
        mixed_ref[:, :width] = mixed
        middle = (
            at_scr[:, :width]
            + dot_nn(mixed, matrix(gat_ref, kind, AT_OUTPUT, width))
            + vector(vec_ref, kind, 4)
        )
        middle_ref[:, :width] = middle
        hat, _ = standardise(middle)
        second_ref[:, :width] = (
            hat * vector(vec_ref, kind, 5) + vector(vec_ref, kind, 6)
        ).astype(LOW)

    each_tower(run)


def expand_matrix(ref, kind):
    return ref[:, : kind.block, : kind.part].reshape(kind.width, kind.part)


def reduce_matrix(ref, kind):
    return ref[:, : kind.reduce_rows, : kind.width].reshape(kind.part, kind.width)


def hidden_bias(vec_ref, kind):
    chip = lax.axis_index("dp") // 2
    whole = vec_ref[...]
    row = lax.broadcasted_iota(jnp.int32, (16, 1), 0)
    line = jnp.sum(jnp.where(row == 10 + chip // 2, whole, 0.0), axis=0, keepdims=True)
    return jnp.where(
        chip % 2 == 0, line[:, : kind.part], line[:, kind.part : 2 * kind.part]
    )


def hidden_kernel(second_ref, raise_ref, reduce_ref, vec_ref, part_ref, raised_ref):
    def run(kind):
        width = kind.width
        rows = second_ref[:, :, :width].reshape(8 * SEQS, width)
        raised = dot_nn(rows, expand_matrix(raise_ref, kind)) + hidden_bias(vec_ref, kind)
        raised_ref[:, : kind.part] = raised
        active = (raised * jax.nn.sigmoid(1.702 * raised)).astype(LOW)
        part = dot_nn(active, reduce_matrix(reduce_ref, kind))
        part_ref[:, :, :width] = part.reshape(8, SEQS, width).astype(LOW)

    each_tower(run)


def hidden_back_kernel(
    grad_ref,
    second_ref,
    raised_ref,
    raise_ref,
    reduce_ref,
    back_ref,
    raise_grad_ref,
    reduce_keep_ref,
    reduce_send_ref,
    bias_ref,
    whole,
):
    def run(kind):
        width, part = kind.width, kind.part
        grads = grad_ref[:, :, :width].reshape(8 * SEQS, width)
        rows = second_ref[:, :, :width].reshape(8 * SEQS, width)
        raised = raised_ref[:, :part]
        gate = jax.nn.sigmoid(1.702 * raised)
        active = (raised * gate).astype(LOW)
        slope = gate + 1.702 * raised * gate * (1.0 - gate)
        raised_grad = dot_nt(grads, reduce_matrix(reduce_ref, kind)) * slope
        low_grad = raised_grad.astype(LOW)
        bias_ref[0:1, :part] = jnp.sum(low_grad.astype(WIDE), axis=0, keepdims=True)
        back = dot_nt(low_grad, expand_matrix(raise_ref, kind))
        back_ref[:, :, :width] = back.reshape(8, SEQS, width).astype(LOW)
        raise_grad_ref[:, : kind.block, :part] = (
            dot_tn(rows, low_grad).reshape(16, kind.block, part).astype(LOW)
        )
        whole[:part, :width] = dot_tn(active, grads)
        core = lax.axis_index("dp") % 2
        n = kind.reduce_rows
        keep = pl.multiple_of(core * n, 64)
        send = pl.multiple_of((1 - core) * n, 64)
        reduce_keep_ref[:n, :width] = whole[pl.ds(keep, n), :width]
        reduce_send_ref[:n, :width] = whole[pl.ds(send, n), :width].astype(LOW)

    each_tower(run)


def embed_kernel(part_ref, middle_ref, gat_ref, vec_ref, emb_ref, final_ref, pooled_ref, proj_ref):
    def run(kind):
        width = kind.width
        final = (
            middle_ref[:, :width]
            + jnp.sum(part_ref[:, :, :width].astype(WIDE), axis=0)
            + vector(vec_ref, kind, 7)
        )
        final_ref[:, :width] = final
        hat, _ = standardise(final)
        pooled = (hat * vector(vec_ref, kind, 8) + vector(vec_ref, kind, 9)).astype(LOW)
        pooled_ref[:, :width] = pooled
        proj = dot_nn(pooled, matrix(gat_ref, kind, AT_EMBED, EMB))
        proj_ref[...] = proj
        size = jnp.sum(proj * proj, axis=-1, keepdims=True) + 1e-06
        emb_ref[...] = (proj * lax.rsqrt(size)).astype(LOW)

    each_tower(run)


def objective_kernel(
    scale_ref,
    all_ref,
    valid_ref,
    final_ref,
    proj_ref,
    gat_ref,
    vec_ref,
    low_ref,
    grad_ref,
    proj_grad_ref,
    final_vec_ref,
    sums_ref,
    own_scr,
):
    def ordered(which):
        blocks = []
        for half in range(2):
            for j in range(16):
                rows = all_ref[j % 2, which * 8 + j // 2].astype(WIDE)
                blocks.append(rows[half * 8 : half * 8 + 8])
        return jnp.concatenate(blocks, axis=0).astype(LOW)

    img, txt = ordered(0), ordered(1)
    total = img.shape[0]
    scale = jnp.exp(jnp.full((1, 1), scale_ref[0], WIDE))
    allowed = valid_ref[...].reshape(total, total) > 0
    same = lax.broadcasted_iota(jnp.int32, (total, total), 0) == lax.broadcasted_iota(
        jnp.int32, (total, total), 1
    )
    same = same.astype(WIDE)

    def side(left, right):
        logits = scale * dot_nt(left, right)
        masked = jnp.where(allowed, logits, -1e30)
        top = jnp.max(masked, axis=1, keepdims=True)
        lse = jnp.log(jnp.sum(jnp.exp(masked - top), axis=1, keepdims=True)) + top
        terms = 0.5 * (jnp.where(allowed, jnp.exp(logits - lse), 0.0) - same)
        loss = 0.5 * (
            jnp.sum(lse, axis=0, keepdims=True)
            - jnp.sum(jnp.sum(logits * same, axis=1, keepdims=True), axis=0, keepdims=True)
        )
        rate = jnp.sum(jnp.sum(terms * logits, axis=1, keepdims=True), axis=0, keepdims=True)
        return (scale * terms).astype(LOW), loss, rate

    row_back, row_loss, row_rate = side(img, txt)
    col_back, col_loss, col_rate = side(txt, img)
    row = lax.broadcasted_iota(jnp.int32, sums_ref.shape, 0)
    sums_ref[...] = jnp.where(row == 0, row_loss + col_loss, row_rate + col_rate)

    def run(kind):
        width = kind.width
        if kind.index == 0:
            emb_grad = dot_nn(row_back, txt) + dot_tn(col_back, txt)
        else:
            emb_grad = dot_nn(col_back, img) + dot_tn(row_back, img)
        own_scr[...] = emb_grad
        at = lax.axis_index("dp")
        mine = jnp.concatenate(
            [
                own_scr[pl.ds(pl.multiple_of(half * 128 + at * 8, 8), 8), :]
                for half in range(2)
            ],
            axis=0,
        )
        proj = proj_ref[...]
        size = jnp.sum(proj * proj, axis=-1, keepdims=True) + 1e-06
        along = jnp.sum(proj * mine, axis=-1, keepdims=True)
        proj_grad = ((mine - proj * along / size) * lax.rsqrt(size)).astype(LOW)
        proj_grad_ref[...] = proj_grad
        pooled_grad = dot_nt(proj_grad, matrix(gat_ref, kind, AT_EMBED, EMB))
        hat, rate = standardise(final_ref[:, :width])
        final_vec_ref[0:1, :width] = jnp.sum(pooled_grad * hat, axis=0, keepdims=True)
        final_vec_ref[1:2, :width] = jnp.sum(pooled_grad, axis=0, keepdims=True)
        final_grad = norm_back(pooled_grad, vector(vec_ref, kind, 8), hat, rate)
        grad_ref[:, :width] = final_grad
        low = final_grad.astype(LOW)
        low_ref[:, :width] = low
        final_vec_ref[2:3, :width] = jnp.sum(low.astype(WIDE), axis=0, keepdims=True)

    each_tower(run)


def attend_back_kernel(
    ends_ref,
    img_own,
    img_in,
    txt_own,
    txt_in,
    gat_ref,
    vec_ref,
    back_ref,
    grad_ref,
    middle_ref,
    query_ref,
    keyed_ref,
    mixture_ref,
    weight_ref,
    mixed_ref,
    first_ref,
    pooled_ref,
    proj_grad_ref,
    final_vec_ref,
    bias_ref,
    img_keep,
    txt_keep,
    img_send,
    txt_send,
    factor_ref,
    outer_ref,
    rows_grad,
    middle_scr,
    query_back,
    valued_scr,
    shared_scr,
    turned,
    gains,
):
    def run(kind):
        width, room, length = kind.width, kind.room, kind.length
        gain, shift = vector(vec_ref, kind, 0), vector(vec_ref, kind, 1)
        refs = (img_own, img_in) if kind.index == 0 else (txt_own, txt_in)
        halves = sequence(kind, refs, 0)
        keep, send = (img_keep, img_send) if kind.index == 0 else (txt_keep, txt_send)
        mask = head_mask(kind)
        positions = lax.broadcasted_iota(jnp.int32, (room, 1), 0)
        at = lax.axis_index("dp")

        second_grad = jnp.sum(back_ref[:, :, :width].astype(WIDE), axis=0)
        hat, rate = standardise(middle_ref[:, :width])
        middle_grad = grad_ref[:, :width] + norm_back(
            second_grad, vector(vec_ref, kind, 5), hat, rate
        )
        middle_scr[:, :width] = middle_grad
        output_grad = middle_grad.astype(LOW)
        mixed_grad = dot_nt(output_grad, matrix(gat_ref, kind, AT_OUTPUT, width)).astype(LOW)
        spread_grad = by_head(mixed_grad.astype(WIDE), mask)
        constant = jnp.sum(spread_grad * vector(vec_ref, kind, 3), axis=-1, keepdims=True)
        valued = dot_nt(
            spread_grad.astype(LOW), matrix(gat_ref, kind, 2 * width, width)
        ).astype(LOW)
        valued_scr[:, :width] = valued
        shared_scr[...] = jnp.broadcast_to(constant, (256, LANES))

        def normal(half, i):
            rows = halves[half][i].astype(WIDE)
            hat, rate = standardise(rows)
            return hat, rate

        for half in range(2):

            def through(i, carry):
                s = half * 8 + i
                start = pl.multiple_of(s * HEADS, HEADS)
                span = pl.ds(start, HEADS)
                hat, _ = normal(half, i)
                first = (hat * gain + shift).astype(LOW)
                weights = weight_ref[s, :, :room]
                slope = dot_nt(valued_scr[span, :width], first) + shared_scr[span, 0:1]
                slope = weights * (
                    slope - jnp.sum(weights * slope, axis=-1, keepdims=True)
                )
                slope = slope.astype(LOW)
                query_back[span, :width] = dot_nn(slope, first)
                rows_grad[s, :room, :width] = dot_tn(slope, keyed_ref[span, :width]) + dot_tn(
                    weights.astype(LOW), valued_scr[span, :width]
                )
                return carry

            lax.fori_loop(0, 8, through, 0)

        turns = query_back[:, :width].astype(LOW)
        query_grad = from_heads(
            dot_nn(turns, matrix(gat_ref, kind, width, width)) * 0.125, mask
        ).astype(LOW)
        top_grad = dot_nt(query_grad, matrix(gat_ref, kind, 0, width))
        gains[...] = jnp.zeros_like(gains)
        turned[:, :width] = top_grad

        for half in range(2):
            mine = half == kind.index

            def finish(i, carry):
                s = half * 8 + i
                hat, rate = normal(half, i)
                grad = rows_grad[s, :room, :width]
                top = turned[pl.ds(s, 1), :width]
                low = middle_scr[pl.ds(s, 1), :width]
                if kind.causal:
                    chosen = (positions == ends_ref[(half * 16 + at) * 8 + i]).astype(WIDE)
                else:
                    chosen = (positions == 0).astype(WIDE)
                grad = grad + chosen * top
                gains[0:1, :width] += jnp.sum(grad * hat, axis=0, keepdims=True)
                gains[1:2, :width] += jnp.sum(grad, axis=0, keepdims=True)
                result = norm_back(grad, gain, hat, rate) + chosen * low
                if mine:
                    keep[i] = result[:length]
                else:
                    send[i] = result.astype(LOW)
                return carry

            lax.fori_loop(0, 8, finish, 0)

        factor_ref[:, 0:width] = query_ref[:, :width]
        factor_ref[:, WIDTH : WIDTH + width] = mixed_grad
        factor_ref[:, 2 * WIDTH : 2 * WIDTH + width] = query_grad
        factor_ref[:, 3 * WIDTH : 3 * WIDTH + width] = output_grad
        factor_ref[:, 4 * WIDTH : 4 * WIDTH + EMB] = proj_grad_ref[...]
        start = 4 * WIDTH + EMB

        def column_sum(value):
            return jnp.sum(value.astype(WIDE), axis=0, keepdims=True)

        totals = jnp.sum(
            weight_ref[:, :, :room].astype(LOW).astype(WIDE), axis=-1, keepdims=True
        ).reshape(SEQS * HEADS, 1)
        lines = [
            gains[0:1, :width],
            gains[1:2, :width],
            column_sum(query_grad),
            column_sum(spread_grad * totals),
            column_sum(output_grad),
            column_sum(second_grad * hat),
            column_sum(second_grad),
            final_vec_ref[2:3, :width],
            final_vec_ref[0:1, :width],
            final_vec_ref[1:2, :width],
            jnp.pad(bias_ref[0:1, : kind.part], ((0, 0), (0, width - kind.part))),
            jnp.zeros((5, width), WIDE),
        ]
        factor_ref[:, start : start + width] = jnp.concatenate(lines, axis=0).astype(LOW)

        slot = lax.broadcasted_iota(jnp.int32, (HEADS, 1), 0)

        def in_slot(index, value):
            chosen = (slot == index).astype(WIDE)
            return (value.astype(WIDE)[:, None, :] * chosen[None]).reshape(SEQS * HEADS, width)

        left = (
            mixture_ref[:, :width].astype(WIDE)
            + in_slot(12, first_ref[:, :width])
            + in_slot(13, mixed_ref[:, :width])
            + in_slot(14, pooled_ref[:, :width])
        )
        block = kind.block
        outer_ref[:, :block, 0:256] = left.T.reshape(16, block, 256).astype(LOW)
        outer_ref[:, :block, 256:512] = query_back[:, :width].T.reshape(16, block, 256).astype(LOW)

    each_tower(run)


def weigh_kernel(
    outer_ref, factor_ref, raise_ref, keep_ref, sent_ref, img_ref, txt_ref, flat, acc, lines
):
    def run(kind):
        width, block = kind.width, kind.block
        mask = head_mask(kind)
        slot = lax.broadcasted_iota(jnp.int32, (HEADS, 1), 0)
        acc[...] = jnp.zeros_like(acc)
        lines[...] = jnp.zeros_like(lines)

        def in_slot(index, value):
            chosen = (slot == index).astype(WIDE)
            return (
                (value.astype(WIDE)[:, None, :] * chosen[None])
                .reshape(SEQS * HEADS, value.shape[1])
                .astype(LOW)
            )

        def add(source, carry):
            left = outer_ref[source, :block, 0:256]
            turned = outer_ref[source, :block, 256:512]

            def factor(k, wide):
                return factor_ref[source, :, k * WIDTH : k * WIDTH + wide]

            query = by_head(factor(0, width).astype(WIDE), mask).astype(LOW)
            value = by_head(factor(1, width).astype(WIDE), mask).astype(LOW)
            acc[:block, 0:width] += dot_nn(left, in_slot(12, factor(2, width)))
            acc[:block, width : 2 * width] += dot_nn(turned, query) * 0.125
            acc[:block, 2 * width : 3 * width] += dot_nn(left, value)
            acc[:block, AT_OUTPUT : AT_OUTPUT + width] += dot_nn(left, in_slot(13, factor(3, width)))
            acc[:block, AT_EMBED : AT_EMBED + EMB] += dot_nn(left, in_slot(14, factor(4, EMB)))
            start = 4 * WIDTH + EMB
            part = factor_ref[source, :, start : start + width].astype(WIDE)
            lines[0:10, :width] += part[0:10]
            chip = source // 2
            piece = part[10:11, : kind.part]
            other = jnp.zeros_like(piece)
            both = jnp.where(
                chip % 2 == 0,
                jnp.concatenate([piece, other], axis=1),
                jnp.concatenate([other, piece], axis=1),
            )
            rows = 2 * kind.part // width
            lines[pl.ds(10 + chip // 2, 1), :width] += both
            return carry

        lax.fori_loop(0, 16, add, 0)

        def drop(base, height, pitch, c, value):
            flat[pl.ds(base + c, height, stride=pitch), :] = value

        base = 0
        for start, wide in ((0, 3 * width), (AT_OUTPUT, width)):
            pitch = wide // LANES
            for c in range(pitch):
                lane = start + c * LANES
                drop(base, block, pitch, c, acc[:block, lane : lane + LANES])
            base += block * pitch
        pitch = kind.hidden // LANES
        per = kind.part // LANES
        for c in range(pitch):
            chip, lane = c // per, c % per * LANES
            value = raise_ref[2 * chip, :block, lane : lane + LANES].astype(WIDE) + raise_ref[
                2 * chip + 1, :block, lane : lane + LANES
            ].astype(WIDE)
            drop(base, block, pitch, c, value)
        base += block * pitch
        pitch = width // LANES
        n = kind.reduce_rows
        other_core = 1 - lax.axis_index("dp") % 2
        for c in range(pitch):
            lane = c * LANES
            value = keep_ref[:n, lane : lane + LANES] + sent_ref[
                other_core, :n, lane : lane + LANES
            ].astype(WIDE)
            drop(base, n, pitch, c, value)
        base += n * pitch
        pitch = EMB // LANES
        for c in range(pitch):
            lane = AT_EMBED + c * LANES
            drop(base, block, pitch, c, acc[:block, lane : lane + LANES])
        base += block * pitch
        pitch = width // LANES
        for c in range(pitch):
            drop(base, 16, pitch, c, lines[:, c * LANES : (c + 1) * LANES])
        ref = img_ref if kind.index == 0 else txt_ref
        n, rows, lanes = ref.shape
        ref[...] = flat[: n * rows, :].reshape(n, rows, lanes).astype(LOW)

    each_tower(run)


def compute(kernel, outs, scratch, scalars, *args):
    like = jax.ShapeDtypeStruct
    vmem = pl.BlockSpec(memory_space=pltpu.VMEM)
    smem = pl.BlockSpec(memory_space=pltpu.SMEM)
    return pl.pallas_call(
        kernel,
        out_shape=[like(shape, dtype) for shape, dtype in outs],
        in_specs=[smem] * scalars + [vmem] * (len(args) - scalars),
        out_specs=[vmem] * len(outs),
        scratch_shapes=[pltpu.VMEM(shape, dtype) for shape, dtype in scratch],
        compiler_params=pltpu.CompilerParams(vmem_limit_bytes=GRANT),
    )(*args)


def plans_for(img_share, txt_share):
    return (
        Plan(0, img_share, 96, (9, 3, 12, 12, 2)),
        Plan(1, txt_share, 64, (6, 2, 8, 8, 2)),
    )


def to_chunks(flat, plan, me):
    start = me * plan.share % plan.chunk
    padded = jnp.pad(flat, (plan.chunk, plan.local * plan.chunk - plan.share))
    piece = lax.dynamic_slice(padded, (plan.chunk - start,), (plan.local * plan.chunk,))
    return piece.astype(LOW).reshape(plan.local, plan.rows, LANES)


def from_chunks(chunks, plan, me):
    start = me * plan.share % plan.chunk
    return lax.dynamic_slice(chunks.reshape(-1), (start,), (plan.share,)).astype(WIDE)


def step(
    img_tokens,
    txt_tokens,
    txt_ends,
    valid,
    img_master,
    img_moment,
    img_average,
    txt_master,
    txt_moment,
    txt_average,
    scale_state,
):
    me = lax.axis_index(("tower", "dp"))
    tower_at = lax.axis_index("tower")
    is_image = tower_at == 0
    plans = plans_for(img_master.shape[0], txt_master.shape[0])
    img_rows = jnp.pad(img_tokens, ((0, 0), (0, TOWERS[0].room - TOWERS[0].length), (0, 0)))
    txt_rows = jnp.pad(txt_tokens, ((0, 0), (0, TOWERS[1].room - TOWERS[1].length), (0, 0)))
    img_slots, txt_slots, pairs = deal(
        to_chunks(img_master, plans[0], me), to_chunks(txt_master, plans[1], me), valid, plans, 0
    )
    att, rise, fall, vec = compute(
        place_kernel,
        [
            ((48, ATTENTION), LOW),
            ((8, 48, PART), LOW),
            ((192, WIDTH), LOW),
            ((16, WIDTH), WIDE),
        ],
        [((39 * 96, LANES), WIDE)],
        0,
        img_slots,
        txt_slots,
    )
    rise = jnp.repeat(rise, 2, axis=0)
    gat, fall, img_in, txt_in, rise = exchange(att, fall, img_rows, txt_rows, [rise], 1)
    second, middle, query, keyed, mixture, weights, mixed, tops = compute(
        attend_kernel,
        [
            ((SEQS, WIDTH), LOW),
            ((SEQS, WIDTH), WIDE),
            ((SEQS, WIDTH), LOW),
            ((256, WIDTH), LOW),
            ((256, WIDTH), LOW),
            ((SEQS, HEADS, LANES), WIDE),
            ((SEQS, WIDTH), LOW),
            ((SEQS, WIDTH), LOW),
        ],
        [((SEQS, ROOM, WIDTH), LOW), ((SEQS, WIDTH), WIDE), ((SEQS, WIDTH), WIDE)],
        1,
        txt_ends,
        img_rows,
        img_in,
        txt_rows,
        txt_in,
        gat,
        vec,
    )
    seconds = group_exchange(second, False, 2)
    part, raised = compute(
        hidden_kernel,
        [((8, SEQS, WIDTH), LOW), ((128, PART), WIDE)],
        [],
        0,
        seconds,
        rise,
        fall,
        vec,
    )
    parts = group_exchange(part, True, 3)
    emb, final, pooled, proj = compute(
        embed_kernel,
        [
            ((SEQS, EMB), LOW),
            ((SEQS, WIDTH), WIDE),
            ((SEQS, WIDTH), LOW),
            ((SEQS, EMB), WIDE),
        ],
        [],
        0,
        parts,
        middle,
        gat,
        vec,
    )
    embs = spread(emb, 4)
    low, final_grad, proj_grad, final_vec, sums = compute(
        objective_kernel,
        [
            ((SEQS, WIDTH), LOW),
            ((SEQS, WIDTH), WIDE),
            ((SEQS, EMB), LOW),
            ((8, WIDTH), WIDE),
            ((8, LANES), WIDE),
        ],
        [((256, EMB), WIDE)],
        1,
        scale_state,
        embs.reshape(2, 16, SEQS, EMB),
        pairs,
        final,
        proj,
        gat,
        vec,
    )
    lows = group_exchange(low, False, 5)
    back, rise_grad, fall_keep, fall_send, bias_grad = compute(
        hidden_back_kernel,
        [
            ((8, SEQS, WIDTH), LOW),
            ((16, 48, PART), LOW),
            ((192, WIDTH), WIDE),
            ((192, WIDTH), LOW),
            ((8, PART), WIDE),
        ],
        [((PART, WIDTH), WIDE)],
        0,
        lows,
        seconds,
        raised,
        rise,
        fall,
    )
    backs = group_exchange(back, True, 6)
    img_keep, txt_keep, img_send, txt_send, factor, outer = compute(
        attend_back_kernel,
        [
            ((8, TOWERS[0].length, D_IMG), WIDE),
            ((8, TOWERS[1].length, D_TXT), WIDE),
            (img_rows.shape, LOW),
            (txt_rows.shape, LOW),
            ((SEQS, 5 * WIDTH + EMB), LOW),
            ((16, 48, 512), LOW),
        ],
        [
            ((SEQS, ROOM, WIDTH), WIDE),
            ((SEQS, WIDTH), WIDE),
            ((256, WIDTH), WIDE),
            ((256, WIDTH), LOW),
            ((256, LANES), WIDE),
            ((SEQS, WIDTH), WIDE),
            ((8, WIDTH), WIDE),
        ],
        1,
        txt_ends,
        img_rows,
        img_in,
        txt_rows,
        txt_in,
        gat,
        vec,
        backs,
        final_grad,
        middle,
        query,
        keyed,
        mixture,
        weights,
        mixed,
        tops,
        pooled,
        proj_grad,
        final_vec,
        bias_grad,
    )
    factors, falls, txt_home, img_home, outers, rises = exchange(
        factor, fall_send, txt_send, img_send, [outer, rise_grad], 7
    )
    img_slots, txt_slots = compute(
        weigh_kernel,
        [(img_slots.shape, LOW), (txt_slots.shape, LOW)],
        [((39 * 96, LANES), WIDE), ((48, ATTENTION), WIDE), ((16, WIDTH), WIDE)],
        0,
        outers,
        factors,
        rises,
        fall_keep,
        falls,
    )
    img_chunks, txt_chunks = collect(img_slots, txt_slots, plans, 8)
    img_grad = jnp.where(is_image, img_keep, img_home[:, : TOWERS[0].length].astype(WIDE))
    txt_grad = jnp.where(is_image, txt_home[:, : TOWERS[1].length].astype(WIDE), txt_keep)
    img_new = advance(
        img_master, img_moment, img_average, from_chunks(img_chunks, plans[0], me), step_rate
    )
    txt_new = advance(
        txt_master, txt_moment, txt_average, from_chunks(txt_chunks, plans[1], me), step_rate
    )
    scale_parts = advance(
        scale_state[0], scale_state[1], scale_state[2], sums[1, 0], scale_rate
    )
    return (
        sums[0, 0] / 256,
        img_grad,
        txt_grad,
        img_new[0],
        img_new[1],
        img_new[2],
        img_new[0].astype(LOW),
        txt_new[0],
        txt_new[1],
        txt_new[2],
        txt_new[0].astype(LOW),
        jnp.stack(scale_parts),
    )


def from_partner(value, axis, stride):
    mask = 2**stride
    pairs = [(source, source ^ mask) for source in range(lax.axis_size(axis))]
    return lax.ppermute(value, axis, pairs)


def round_value(v):
    return lax.optimization_barrier(v.astype(jnp.bfloat16)).astype(jnp.float32)


def make_low():

    def value_keep(v):
        return (round_value(v), None)

    def grad_pass(kept, grad):
        return (grad,)

    rounded = jax.custom_vjp(round_value)
    rounded.defvjp(value_keep, grad_pass)
    return rounded


def low(v):
    return make_low()(v)


def make_low_back():

    def identity(v):
        return v

    def value_pass(v):
        return (v, None)

    def grad_round(kept, grad):
        return (round_value(grad),)

    passed = jax.custom_vjp(identity)
    passed.defvjp(value_pass, grad_round)
    return passed


def low_back(v):
    return make_low_back()(v)


def both_ways(value):
    return low(low_back(value))


def product(left, right):
    return jnp.matmul(left, right)


def contract(form, left, right):
    return jnp.einsum(form, left, right)


def layer_norm(values, gain_row, shift_row):
    centred = values - jnp.mean(values, axis=-1, keepdims=True)
    spread = jnp.mean(centred * centred, axis=-1, keepdims=True)
    return centred * lax.rsqrt(spread + 1e-05) * gain_row + shift_row


def unpack(flat_weights, model_width, hidden_width, embed_width):
    piece_shapes = [
        (model_width, 3 * model_width),
        (model_width, model_width),
        (model_width, hidden_width),
        (hidden_width, model_width),
        (model_width, embed_width),
        (10, model_width),
        (hidden_width,),
    ]
    pieces = []
    offset = 0
    for piece_shape in piece_shapes:
        length = math.prod(piece_shape)
        pieces.append(flat_weights[offset : offset + length].reshape(piece_shape))
        offset = offset + length
    return pieces


def encode(tokens, flat_weights, positions, causal, model_width, hidden_width, embed_width):
    w_inputs, w_output, w_expand, w_reduce, w_embed, vectors, expand_bias = unpack(
        flat_weights, model_width, hidden_width, embed_width
    )
    groups = tokens.shape[0]
    length = tokens.shape[1]
    first = low(layer_norm(tokens, vectors[0], vectors[1]))
    bias_in = jnp.concatenate([vectors[2], jnp.zeros_like(vectors[2]), vectors[3]])
    joined = both_ways(product(first, w_inputs) + bias_in)
    joined = joined.reshape(groups, length, 3, model_width // HEAD, HEAD)
    scores = low_back(contract("gqhd,gkhd->ghqk", joined[:, :, 0], joined[:, :, 1]) * 0.125)
    if causal:
        row_index = lax.broadcasted_iota(jnp.int32, (length, length), 0)
        col_index = lax.broadcasted_iota(jnp.int32, (length, length), 1)
        scores = jnp.where(col_index <= row_index, scores, -1e30)
    row_top = jnp.max(scores, axis=-1, keepdims=True)
    raw_weights = jnp.exp(scores - row_top)
    attention = low(raw_weights / jnp.sum(raw_weights, axis=-1, keepdims=True))
    mixed_heads = both_ways(
        contract("ghqk,gkhd->gqhd", attention, joined[:, :, 2]).reshape(groups, length, model_width)
    )
    middle = tokens + low_back(product(mixed_heads, w_output) + vectors[4])
    second = low(layer_norm(middle, vectors[5], vectors[6]))
    raised = low_back(product(second, w_expand) + expand_bias)
    active = low(raised * jax.nn.sigmoid(1.702 * raised))
    final_rows = middle + low_back(product(active, w_reduce) + vectors[7])
    pooled = jnp.take_along_axis(final_rows, positions[:, None, None], axis=1)[:, 0]
    pooled = low(layer_norm(pooled, vectors[8], vectors[9]))
    projected = low_back(product(pooled, w_embed))
    return low(
        projected * lax.rsqrt(jnp.sum(projected * projected, axis=-1, keepdims=True) + 1e-06)
    )


def inner(left, right):
    return lax.dot_general(
        left, right, (((1,), (1,)), ((), ())), preferred_element_type=jnp.float32
    )


def across(left, right):
    return lax.dot_general(
        left, right, (((0,), (0,)), ((), ())), preferred_element_type=jnp.float32
    )


def softmax_total(logits, allowed):
    masked = jnp.where(allowed, logits, -1e30)
    row_top = jnp.max(masked, axis=1, keepdims=True)
    return jnp.log(jnp.sum(jnp.exp(masked - row_top), axis=1)) + row_top[:, 0]


def advance(master, moment, average, grads, rate):
    moment_new = momentum_rate * moment + grads
    master_new = master - rate * (grads + momentum_rate * moment_new)
    average_new = average_rate * average + (1.0 - average_rate) * master_new
    return (master_new, moment_new, average_new)


def padded_to(flat, length):
    return jnp.pad(flat, (0, length - flat.shape[0]))


def body(
    img_tokens,
    txt_tokens,
    txt_ends,
    valid,
    img_master,
    img_moment,
    img_average,
    txt_master,
    txt_moment,
    txt_average,
    scale_state,
):
    batch_rows = img_tokens.shape[0]
    total_rows = batch_rows * lax.axis_size(("tower", "dp"))
    device_at = lax.axis_index(("tower", "dp"))
    tower_at = lax.axis_index("tower")
    is_image = tower_at == 0
    img_share = img_master.shape[0]
    txt_share = txt_master.shape[0]
    img_count = img_tokens.size
    txt_count = txt_tokens.size
    shard_room = max(img_share, txt_share)
    token_room = max(img_count, txt_count)
    tower_count = lax.axis_size("dp")
    dp_at = lax.axis_index("dp")
    img_low = padded_to(img_master.astype(jnp.bfloat16), shard_room)
    txt_low = padded_to(txt_master.astype(jnp.bfloat16), shard_room)
    token_out = jnp.where(
        is_image,
        padded_to(txt_tokens.reshape(-1), token_room),
        padded_to(img_tokens.reshape(-1), token_room),
    )
    weight_out = jnp.where(is_image, txt_low, img_low)
    weight_mine = jnp.where(is_image, img_low, txt_low)
    token_in, weight_in = from_partner((token_out, weight_out), "tower", 0)
    stacked = jnp.where(
        is_image, jnp.stack([weight_mine, weight_in]), jnp.stack([weight_in, weight_mine])
    )
    gathered = lax.all_gather(stacked, "dp", axis=1, tiled=True)
    pair_ends = jnp.concatenate(
        [
            lax.dynamic_slice_in_dim(txt_ends, dp_at * batch_rows, batch_rows),
            lax.dynamic_slice_in_dim(txt_ends, (tower_count + dp_at) * batch_rows, batch_rows),
        ]
    )
    pair_zero = jnp.zeros((2 * batch_rows,), jnp.int32)

    def image_weights(whole):
        return whole.reshape(2, tower_count, shard_room).reshape(-1).astype(jnp.float32)

    def text_weights(whole):
        return (
            whole.reshape(2, tower_count, shard_room)[:, :, :txt_share]
            .reshape(-1)
            .astype(jnp.float32)
        )

    def image_rows(arrived):
        return jnp.concatenate(
            [img_tokens, arrived[:img_count].reshape(img_tokens.shape)], axis=0
        ).astype(jnp.float32)

    def text_rows(arrived):
        return jnp.concatenate([arrived.reshape(txt_tokens.shape), txt_tokens], axis=0).astype(
            jnp.float32
        )

    def image_encode(rows, flat):
        return encode(rows, flat, pair_zero, False, D_IMG, FF_IMG, EMB)

    def text_encode(rows, flat):
        return encode(rows, flat, pair_ends, True, D_TXT, FF_TXT, EMB)

    def image_forward(operands):
        return image_encode(image_rows(operands[1]), image_weights(operands[0]))

    def text_forward(operands):
        return text_encode(text_rows(operands[1]), text_weights(operands[0]))

    pair_emb = lax.cond(is_image, image_forward, text_forward, (gathered, token_in)).astype(
        jnp.bfloat16
    )
    emb_in = from_partner(pair_emb, "tower", 0)
    img_pair = jnp.where(is_image, pair_emb, emb_in)
    txt_pair = jnp.where(is_image, emb_in, pair_emb)
    row_start = tower_at * batch_rows
    img_local = lax.dynamic_slice_in_dim(img_pair, row_start, batch_rows)
    txt_local = lax.dynamic_slice_in_dim(txt_pair, row_start, batch_rows)
    img_all, txt_all = (
        lax.all_gather(img_local, ("tower", "dp"), axis=0, tiled=True),
        lax.all_gather(txt_local, ("tower", "dp"), axis=0, tiled=True),
    )
    logit_scale = jnp.exp(scale_state[0])
    offset = device_at * batch_rows
    row_index = lax.broadcasted_iota(jnp.int32, (batch_rows, total_rows), 0) + offset
    col_index = lax.broadcasted_iota(jnp.int32, (batch_rows, total_rows), 1)
    diagonal = (row_index == col_index).astype(jnp.float32)
    allowed = valid > 0
    row_logits = logit_scale * inner(img_local, txt_all)
    col_logits = logit_scale * inner(txt_local, img_all)
    row_lse = softmax_total(row_logits, allowed)
    col_lse = softmax_total(col_logits, allowed)
    partial_loss = 0.5 * (
        jnp.sum(row_lse)
        - jnp.sum(row_logits * diagonal)
        + jnp.sum(col_lse)
        - jnp.sum(col_logits * diagonal)
    )
    row_terms = 0.5 * (jnp.where(allowed, jnp.exp(row_logits - row_lse[:, None]), 0.0) - diagonal)
    col_terms = 0.5 * (jnp.where(allowed, jnp.exp(col_logits - col_lse[:, None]), 0.0) - diagonal)
    partial_scale = jnp.sum(row_terms * row_logits) + jnp.sum(col_terms * col_logits)
    row_back = (logit_scale * row_terms).astype(jnp.bfloat16)
    col_back = (logit_scale * col_terms).astype(jnp.bfloat16)
    img_emb_grad = jnp.dot(row_back, txt_all, preferred_element_type=jnp.float32)
    txt_emb_grad = jnp.dot(col_back, img_all, preferred_element_type=jnp.float32)
    img_extra, txt_extra = (
        lax.psum_scatter(
            across(col_back, txt_local), ("tower", "dp"), scatter_dimension=0, tiled=True
        ),
        lax.psum_scatter(
            across(row_back, img_local), ("tower", "dp"), scatter_dimension=0, tiled=True
        ),
    )
    img_emb_grad = img_emb_grad + img_extra
    txt_emb_grad = txt_emb_grad + txt_extra
    sums = lax.psum((partial_loss, partial_scale), ("tower", "dp"))
    grad_out = jnp.where(is_image, txt_emb_grad, img_emb_grad)
    grad_in = from_partner(grad_out, "tower", 0)
    pair_cot = jnp.where(
        is_image,
        jnp.concatenate([img_emb_grad, grad_in], axis=0),
        jnp.concatenate([grad_in, txt_emb_grad], axis=0),
    )

    def image_backward(operands):
        recomputed, tower_pullback = jax.vjp(
            image_encode, image_rows(operands[1]), image_weights(operands[0])
        )
        rows_grad, flat_grad = tower_pullback(operands[2])
        own_part = padded_to(rows_grad[:batch_rows].reshape(-1), token_room)
        sent_part = padded_to(rows_grad[batch_rows:].reshape(-1), token_room)
        stacked_grad = flat_grad.reshape(2, tower_count, img_share)
        return (own_part, sent_part, stacked_grad)

    def text_backward(operands):
        recomputed, tower_pullback = jax.vjp(
            text_encode, text_rows(operands[1]), text_weights(operands[0])
        )
        rows_grad, flat_grad = tower_pullback(operands[2])
        own_part = padded_to(rows_grad[batch_rows:].reshape(-1), token_room)
        sent_part = padded_to(rows_grad[:batch_rows].reshape(-1), token_room)
        stacked_grad = jnp.pad(
            flat_grad.reshape(2, tower_count, txt_share),
            ((0, 0), (0, 0), (0, shard_room - txt_share)),
        )
        return (own_part, sent_part, stacked_grad)

    own_part, sent_part, stacked_grad = lax.cond(
        is_image, image_backward, text_backward, (gathered, token_in, pair_cot)
    )
    summed = lax.psum_scatter(stacked_grad, "dp", scatter_dimension=1, tiled=True)
    kept_part = jnp.where(is_image, summed[0, 0], summed[1, 0])
    sent_share = jnp.where(is_image, summed[1, 0], summed[0, 0])
    home_weights, home_tokens = (
        from_partner(sent_share.astype(jnp.bfloat16), "tower", 0).astype(sent_share.dtype),
        from_partner(sent_part.astype(jnp.bfloat16), "tower", 0).astype(sent_part.dtype),
    )
    img_owned = jnp.where(is_image, kept_part, home_weights)
    txt_owned = jnp.where(is_image, home_weights, kept_part)[:txt_share]
    img_grad = jnp.where(is_image, own_part, home_tokens)[:img_count].reshape(img_tokens.shape)
    txt_grad = jnp.where(is_image, home_tokens, own_part).reshape(txt_tokens.shape)
    img_new = advance(img_master, img_moment, img_average, img_owned, step_rate)
    txt_new = advance(txt_master, txt_moment, txt_average, txt_owned, step_rate)
    scale_parts = advance(scale_state[0], scale_state[1], scale_state[2], sums[1], scale_rate)
    scale_new = jnp.stack([scale_parts[0], scale_parts[1], scale_parts[2]])
    return (
        sums[0] / total_rows,
        img_grad,
        txt_grad,
        img_new[0],
        img_new[1],
        img_new[2],
        img_new[0].astype(jnp.bfloat16),
        txt_new[0],
        txt_new[1],
        txt_new[2],
        txt_new[0].astype(jnp.bfloat16),
        scale_new,
    )


def solution(mesh):
    in_specs = (
        P(("tower", "dp"), None, None),
        P(("tower", "dp"), None, None),
        P(),
        P(("tower", "dp"), None),
        P(("tower", "dp")),
        P(("tower", "dp")),
        P(("tower", "dp")),
        P(("tower", "dp")),
        P(("tower", "dp")),
        P(("tower", "dp")),
        P(),
    )
    out_specs = (
        P(),
        P(("tower", "dp"), None, None),
        P(("tower", "dp"), None, None),
        P(("tower", "dp")),
        P(("tower", "dp")),
        P(("tower", "dp")),
        P(("tower", "dp")),
        P(("tower", "dp")),
        P(("tower", "dp")),
        P(("tower", "dp")),
        P(("tower", "dp")),
        P(),
    )
    run = step if (mesh.shape["tower"], mesh.shape["dp"]) == (2, 16) else body
    return jax.shard_map(run, mesh=mesh, in_specs=in_specs, out_specs=out_specs, check_vma=False)
```

```python
import functools
import math

import jax
import jax.numpy as jnp
from jax import lax
from jax.experimental import pallas as pl
from jax.experimental.pallas import tpu as pltpu
from jax.sharding import PartitionSpec as P

D_IMG = 768
FF_IMG = 3072
D_TXT = 512
FF_TXT = 2048
EMB = 512
HEAD = 64


momentum_rate = 0.5
average_rate = 0.5
step_rate = 0.08
scale_rate = 0.0001


MESH = pl.DeviceIdType.MESH
ANY = pl.BlockSpec(memory_space=pl.ANY)
GRANT = 56 * 1024 * 1024
LANES = 128


def here():
    return lax.axis_index("tower"), lax.axis_index("dp")


def greet(devices):
    barrier = pltpu.get_barrier_semaphore()
    for device in devices:
        pl.semaphore_signal(barrier, inc=1, device_id=device, device_id_type=MESH)
    pl.semaphore_wait(barrier, len(devices))


def remote(src, dst, send_sem, recv_sem, device):
    return pltpu.make_async_remote_copy(
        src_ref=src,
        dst_ref=dst,
        send_sem=send_sem,
        recv_sem=recv_sem,
        device_id=device,
        device_id_type=MESH,
    )


def comm_params(number):
    return pltpu.CompilerParams(
        collective_id=number, has_side_effects=True, vmem_limit_bytes=GRANT
    )


def same_core(tower, at):
    chip, core = at // 2, at % 2
    return [(tower, (chip + k) % 8 * 2 + core) for k in range(1, 8)]


def both_towers(tower, at):
    place, core = tower * 8 + at // 2, at % 2
    others = [(place + k) % 16 for k in range(1, 16)]
    return [(other // 8, other % 8 * 2 + core) for other in others]


def group_exchange(scattered, x_ref, o_ref, send_sem, recv_sem):
    tower, at = here()
    chip = at // 2

    def source(k):
        return x_ref.at[k] if scattered else x_ref

    own = pltpu.make_async_copy(source(chip), o_ref.at[chip], send_sem.at[7])
    sent = []
    for k, device in enumerate(same_core(tower, at)):
        copy = remote(
            source((chip + 1 + k) % 8), o_ref.at[chip], send_sem.at[k], recv_sem.at[k], device
        )
        copy.start()
        sent.append(copy)
    own.start()
    own.wait()
    for k in range(7):
        remote(
            source(chip),
            o_ref.at[(chip + 7 - k) % 8],
            send_sem.at[k],
            recv_sem.at[k],
            (tower, at),
        ).wait_recv()
    return sent


def spread(x_ref, o_ref, send_sem, recv_sem, core_sems):
    tower, at = here()
    chip, core = at // 2, at % 2
    place = tower * 8 + chip
    sibling = (tower, chip * 2 + 1 - core)
    sent = []
    for k, device in enumerate(both_towers(tower, at)):
        copy = remote(x_ref, o_ref.at[core, place], send_sem.at[k], recv_sem.at[k], device)
        copy.start()
        sent.append(copy)
    own = pltpu.make_async_copy(x_ref, o_ref.at[core, place], send_sem.at[15])
    own.start()
    own.wait()
    for k in range(15):
        remote(
            x_ref, o_ref.at[core, (place + 15 - k) % 16], send_sem.at[k], recv_sem.at[k], sibling
        ).wait_recv()
    across = remote(o_ref.at[core], o_ref.at[core], core_sems.at[0], core_sems.at[1], sibling)
    across.start()
    sent.append(across)
    remote(
        o_ref.at[1 - core], o_ref.at[1 - core], core_sems.at[0], core_sems.at[1], sibling
    ).wait_recv()
    return sent


def exchange_kernel(count, *refs):
    gather_src, sib_src, one_src, zero_src = refs[:4]
    blocks_src = refs[4 : 4 + count]
    gather_dst, sib_dst, one_dst, zero_dst = refs[4 + count : 8 + count]
    blocks_dst = refs[8 + count : 8 + 2 * count]
    (
        ring_send,
        ring_recv,
        core_send,
        core_recv,
        block_send,
        block_recv,
        pair_sems,
        own_sems,
    ) = refs[8 + 2 * count :]
    tower, at = here()
    deep, row, core = at // 4, (at // 2) % 2, at % 2
    sibling = (tower, at + 1 - 2 * core)
    beside = (tower, deep * 4 + (1 - row) * 2 + core)
    partner = (1 - tower, at)

    def spot(z, y):
        return (z % 4) * 4 + y * 2 + core

    others = [(tower, (at + k) % 16) for k in range(1, 16)]
    greet([*others, partner])

    @pl.when(tower == 0)
    def _():
        remote(zero_src, zero_dst, pair_sems.at[0], pair_sems.at[1], partner).start()

    @pl.when(tower == 1)
    def _():
        remote(one_src, one_dst, pair_sems.at[0], pair_sems.at[1], partner).start()

    owns = [
        pltpu.make_async_copy(gather_src, gather_dst.at[at], own_sems.at[0]),
        pltpu.make_async_copy(sib_src, sib_dst.at[core], own_sems.at[1 + count]),
    ]
    for b in range(count):
        owns.append(
            pltpu.make_async_copy(
                blocks_src[b].at[at], blocks_dst[b].at[at], own_sems.at[1 + b]
            )
        )
    for own in owns:
        own.start()
    sent = []

    def launch(copy):
        copy.start()
        sent.append(copy)

    for k in (1, 3, 2):
        launch(
            remote(
                gather_src,
                gather_dst.at[at],
                ring_send.at[k - 1],
                ring_recv.at[k - 1],
                (tower, spot(deep + k, row)),
            )
        )
    launch(remote(gather_src, gather_dst.at[at], ring_send.at[3], ring_recv.at[3], beside))
    launch(remote(gather_src, gather_dst.at[at], core_send.at[0], core_recv.at[0], sibling))
    launch(remote(sib_src, sib_dst.at[core], core_send.at[8], core_recv.at[8], sibling))
    for b in range(count):
        for k in range(1, 16):
            to = (at + k) % 16
            launch(
                remote(
                    blocks_src[b].at[to],
                    blocks_dst[b].at[at],
                    block_send.at[b, k - 1],
                    block_recv.at[b, k - 1],
                    (tower, to),
                )
            )

    def arrived(slot, sems, index):
        remote(gather_src, gather_dst.at[slot], sems.at[index], sems.at[index], sibling).wait_recv()

    for k in (1, 3, 2):
        slot = spot(deep + 4 - k, row)
        arrived(slot, ring_recv, k - 1)
        launch(
            remote(
                gather_dst.at[slot],
                gather_dst.at[slot],
                ring_send.at[3 + k],
                ring_recv.at[3 + k],
                beside,
            )
        )
        launch(
            remote(
                gather_dst.at[slot],
                gather_dst.at[slot],
                core_send.at[k],
                core_recv.at[k],
                sibling,
            )
        )
    for k in (0, 1, 3, 2):
        slot = spot(deep + 4 - k, 1 - row)
        arrived(slot, ring_recv, 3 + k)
        launch(
            remote(
                gather_dst.at[slot],
                gather_dst.at[slot],
                core_send.at[4 + k],
                core_recv.at[4 + k],
                sibling,
            )
        )
    for y in range(2):
        for k in range(4):
            z = (deep + 4 - k) % 4
            side = row if y == 0 else 1 - row
            slot = z * 4 + side * 2 + 1 - core
            arrived(slot, core_recv, 4 * y + k)
    remote(sib_src, sib_dst.at[1 - core], core_send.at[8], core_recv.at[8], sibling).wait_recv()
    for b in range(count):
        for k in range(1, 16):
            source = (at + 16 - k) % 16
            remote(
                blocks_src[b].at[at],
                blocks_dst[b].at[source],
                block_send.at[b, k - 1],
                block_recv.at[b, k - 1],
                sibling,
            ).wait_recv()
    for copy in sent:
        copy.wait_send()
    for own in owns:
        own.wait()

    @pl.when(tower == 0)
    def _():
        remote(zero_src, zero_dst, pair_sems.at[0], pair_sems.at[1], partner).wait_send()
        remote(one_src, one_dst, pair_sems.at[0], pair_sems.at[1], partner).wait_recv()

    @pl.when(tower == 1)
    def _():
        remote(one_src, one_dst, pair_sems.at[0], pair_sems.at[1], partner).wait_send()
        remote(zero_src, zero_dst, pair_sems.at[0], pair_sems.at[1], partner).wait_recv()


def exchange(gathered, sibling, from_one, from_zero, blocks, number):
    count = len(blocks)
    like = jax.ShapeDtypeStruct
    return pl.pallas_call(
        functools.partial(exchange_kernel, count),
        out_shape=[
            like((16, *gathered.shape), gathered.dtype),
            like((2, *sibling.shape), sibling.dtype),
            like(from_one.shape, from_one.dtype),
            like(from_zero.shape, from_zero.dtype),
            *[like(block.shape, block.dtype) for block in blocks],
        ],
        in_specs=[ANY] * (4 + count),
        out_specs=[ANY] * (4 + count),
        scratch_shapes=[
            pltpu.SemaphoreType.DMA((7,)),
            pltpu.SemaphoreType.DMA((7,)),
            pltpu.SemaphoreType.DMA((9,)),
            pltpu.SemaphoreType.DMA((9,)),
            pltpu.SemaphoreType.DMA((count, 15)),
            pltpu.SemaphoreType.DMA((count, 15)),
            pltpu.SemaphoreType.DMA((2,)),
            pltpu.SemaphoreType.DMA((2 + count,)),
        ],
        compiler_params=comm_params(number),
    )(gathered, sibling, from_one, from_zero, *blocks)


class Plan:
    def __init__(self, tower, share, rows, per_device):
        self.tower = tower
        self.share = share
        self.rows = rows
        self.chunk = rows * LANES
        self.per_device = per_device
        self.slots = sum(per_device) + 1
        self.total = 16 * sum(per_device) + 1
        spans = [self.span(device) for device in range(32)]
        self.counts = sorted({last - first + 1 for first, last in spans})
        self.local = self.counts[-1]

    def span(self, device):
        first = device * self.share // self.chunk
        last = ((device + 1) * self.share - 1) // self.chunk
        return first, min(last, self.total - 1)

    def bounds(self, device):
        first = device * self.share // self.chunk
        last = ((device + 1) * self.share - 1) // self.chunk
        return first, jnp.minimum(last, self.total - 1)

    def target(self, g):
        base, slot_base = 0, 0
        at, slot = jnp.int32(0), jnp.int32(0)
        for n in self.per_device:
            inside = g >= base
            at = jnp.where(inside, (g - base) // n, at)
            slot = jnp.where(inside, slot_base + (g - base) % n, slot)
            base += 16 * n
            slot_base += n
        return at, slot

    def global_chunk(self, at, slot):
        base, slot_base = 0, 0
        g = jnp.int32(0)
        for n in self.per_device:
            g = jnp.where(slot >= slot_base, base + at * n + (slot - slot_base), g)
            base += 16 * n
            slot_base += n
        return jnp.where(slot == self.slots - 1, self.total - 1, g)


def everyone(tower, at):
    me = tower * 16 + at
    result = []
    for k in range(1, 32):
        other = (me + k) % 32
        result.append((other // 16, other % 16))
    return result


def deal_kernel(plans, *refs):
    img_src, txt_src, valid_src = refs[:3]
    img_dst, txt_dst, valid_dst = refs[3:6]
    img_extra, txt_extra, img_last, txt_last = refs[6:10]
    chunk_send, deal_recv, edge_sems, last_sems, valid_send, valid_recv = refs[10:]
    tower, at = here()
    me = tower * 16 + at
    homes = everyone(tower, at)
    greet(homes)
    sides = [
        (plans[0], img_src, img_dst, img_extra, img_last),
        (plans[1], txt_src, txt_dst, txt_extra, txt_last),
    ]
    below = ((me + 31) % 32 // 16, (me + 31) % 32 % 16)

    for s, (plan, src, dst, extra, last) in enumerate(sides):

        @pl.when(me > 0)
        def _():
            remote(src.at[0], extra, edge_sems.at[s, 0], edge_sems.at[s, 1], below).start()

    def to_block(plan, s, i, slot_src, dst, at_to, slot, wait):
        far = jnp.logical_or(tower != plan.tower, at_to != at)

        @pl.when(far)
        def _():
            copy = remote(
                slot_src,
                dst.at[slot],
                chunk_send.at[s, i],
                deal_recv.at[s],
                (jnp.int32(plan.tower), at_to),
            )
            if wait:
                copy.wait_send()
            else:
                copy.start()

        if not wait:

            @pl.when(jnp.logical_not(far))
            def _():
                pltpu.make_async_copy(slot_src, dst.at[slot], deal_recv.at[s]).start()

    def whole_chunks(plan, s, src, dst, wait):
        first, last_chunk = plan.bounds(me)

        def step(i, carry):
            g = first + i
            inside = jnp.logical_and(
                jnp.logical_or(i > 0, me == 0),
                jnp.logical_and(g <= last_chunk, jnp.logical_or(g < last_chunk, me == 31)),
            )
            inside = jnp.logical_and(inside, g < plan.total - 1)

            @pl.when(inside)
            def _():
                at_to, slot = plan.target(g)
                to_block(plan, s, i, src.at[i], dst, at_to, slot, wait)

            return carry

        lax.fori_loop(0, plan.local, step, 0)

        @pl.when(me == 31)
        def _():
            i = last_chunk - first

            def each(k, carry):
                to_block(
                    plan, s, plan.local + k, src.at[i], dst, k, plan.slots - 1, wait
                )
                return carry

            lax.fori_loop(0, 16, each, 0)

    for s, (plan, src, dst, extra, last) in enumerate(sides):
        whole_chunks(plan, s, src, dst, False)
    for k, home in enumerate(homes):
        remote(valid_src, valid_dst.at[me], valid_send.at[k], valid_recv.at[k], home).start()
    own = pltpu.make_async_copy(valid_src, valid_dst.at[me], valid_send.at[31])
    own.start()

    for s, (plan, src, dst, extra, last) in enumerate(sides):
        first, last_chunk = plan.bounds(me)

        @pl.when(me < 31)
        def _():
            fetch = pltpu.make_async_copy(src.at[last_chunk - first], last, last_sems.at[s])
            fetch.start()
            fetch.wait()
            remote(src.at[0], extra, edge_sems.at[s, 0], edge_sems.at[s, 1], below).wait_recv()
            last[...] = last[...] + extra[...]
            at_to, slot = plan.target(last_chunk)
            to_block(plan, s, plan.local + 16, last, dst, at_to, slot, False)

    for s, (plan, src, dst, extra, last) in enumerate(sides):

        @pl.when(me > 0)
        def _():
            remote(src.at[0], extra, edge_sems.at[s, 0], edge_sems.at[s, 1], below).wait_send()

        whole_chunks(plan, s, src, dst, True)
        first, last_chunk = plan.bounds(me)

        @pl.when(me < 31)
        def _():
            at_to, slot = plan.target(last_chunk)
            to_block(plan, s, plan.local + 16, last, dst, at_to, slot, True)

        @pl.when(tower == plan.tower)
        def _():
            pltpu.make_async_copy(dst, dst, deal_recv.at[s]).wait()

    own.wait()
    for k, home in enumerate(homes):
        source = (me + 31 - k) % 32
        copy = remote(
            valid_src, valid_dst.at[source], valid_send.at[k], valid_recv.at[k], home
        )
        copy.wait_send()
        copy.wait_recv()


def deal(img_chunks, txt_chunks, valid, plans, number):
    like = jax.ShapeDtypeStruct
    low = jnp.bfloat16
    most = max(plan.local for plan in plans) + 17
    shapes = [(plan.rows, LANES) for plan in plans]
    return pl.pallas_call(
        functools.partial(deal_kernel, plans),
        out_shape=[
            like((plans[0].slots, *shapes[0]), low),
            like((plans[1].slots, *shapes[1]), low),
            like((32, *valid.shape), valid.dtype),
        ],
        in_specs=[ANY] * 3,
        out_specs=[ANY] * 3,
        scratch_shapes=[
            pltpu.VMEM(shapes[0], low),
            pltpu.VMEM(shapes[1], low),
            pltpu.VMEM(shapes[0], low),
            pltpu.VMEM(shapes[1], low),
            pltpu.SemaphoreType.DMA((2, most)),
            pltpu.SemaphoreType.DMA((2,)),
            pltpu.SemaphoreType.DMA((2, 2)),
            pltpu.SemaphoreType.DMA((2,)),
            pltpu.SemaphoreType.DMA((32,)),
            pltpu.SemaphoreType.DMA((31,)),
        ],
        compiler_params=comm_params(number),
    )(img_chunks, txt_chunks, valid)


def collect_kernel(plans, *refs):
    sources, targets = refs[:2], refs[2:4]
    send_sem, recv_sem = refs[4:]
    tower, at = here()
    me = tower * 16 + at
    greet(everyone(tower, at))

    def pass_over(plan, s, wait):
        src, dst = sources[s], targets[s]

        def one(owner, slot, i, which):
            first, _ = plan.bounds(owner)
            g = plan.global_chunk(at, slot)
            far = owner != me

            @pl.when(far)
            def _():
                copy = remote(
                    src.at[slot],
                    dst.at[g - first],
                    send_sem.at[s, which, slot],
                    recv_sem.at[s],
                    (owner // 16, owner % 16),
                )
                if wait:
                    copy.wait_send()
                else:
                    copy.start()

            if not wait:

                @pl.when(jnp.logical_not(far))
                def _():
                    pltpu.make_async_copy(
                        src.at[slot], dst.at[g - first], recv_sem.at[s]
                    ).start()

        def step(slot, carry):
            g = plan.global_chunk(at, slot)
            low_owner = g * plan.chunk // plan.share
            high_owner = jnp.minimum(((g + 1) * plan.chunk - 1) // plan.share, 31)
            use = jnp.logical_or(slot < plan.slots - 1, at == 0)

            @pl.when(use)
            def _():
                one(low_owner, slot, 0, 0)

            @pl.when(jnp.logical_and(use, high_owner != low_owner))
            def _():
                one(high_owner, slot, 1, 1)

            return carry

        @pl.when(tower == plan.tower)
        def _():
            lax.fori_loop(0, plan.slots, step, 0)

    for s in range(2):
        pass_over(plans[s], s, False)
    for s in range(2):
        pass_over(plans[s], s, True)
    for s in range(2):
        plan, dst = plans[s], targets[s]
        first, last = plan.bounds(me)
        held = last - first + 1
        for n in plan.counts:

            @pl.when(held == n)
            def _():
                part = dst.at[pl.ds(0, n)]
                pltpu.make_async_copy(part, part, recv_sem.at[s]).wait()


def collect(img_slots, txt_slots, plans, number):
    like = jax.ShapeDtypeStruct
    most = max(plan.slots for plan in plans)
    return pl.pallas_call(
        functools.partial(collect_kernel, plans),
        out_shape=[
            like((plan.local, plan.rows, LANES), jnp.bfloat16) for plan in plans
        ],
        in_specs=[ANY] * 2,
        out_specs=[ANY] * 2,
        scratch_shapes=[
            pltpu.SemaphoreType.DMA((2, 2, most)),
            pltpu.SemaphoreType.DMA((2,)),
        ],
        compiler_params=comm_params(number),
    )(img_slots, txt_slots)


SEQS = 16
HEADS = 16
LOW = jnp.bfloat16
WIDE = jnp.float32


class Tower:
    def __init__(self, index, width, hidden, length, room, causal):
        self.index = index
        self.width = width
        self.hidden = hidden
        self.length = length
        self.room = room
        self.causal = causal
        self.heads = width // HEAD
        self.block = width // 16
        self.part = hidden // 8
        self.reduce_rows = hidden // 16


TOWERS = (
    Tower(0, D_IMG, FF_IMG, 50, 64, False),
    Tower(1, D_TXT, FF_TXT, 77, 80, True),
)
ROOM = 80
WIDTH = D_IMG
PART = FF_IMG // 8
AT_OUTPUT = 3 * D_IMG
AT_EMBED = 4 * D_IMG
ATTENTION = 4 * D_IMG + EMB


def each_tower(run):
    tower = lax.axis_index("tower")
    for kind in TOWERS:
        pl.when(tower == kind.index)(functools.partial(run, kind))


def dot_nn(a, b):
    return lax.dot_general(a, b, (((1,), (0,)), ((), ())), preferred_element_type=WIDE)


def dot_nt(a, b):
    return lax.dot_general(a, b, (((1,), (1,)), ((), ())), preferred_element_type=WIDE)


def dot_tn(a, b):
    return lax.dot_general(a, b, (((0,), (0,)), ((), ())), preferred_element_type=WIDE)


def standardise(rows):
    centred = rows - jnp.mean(rows, axis=-1, keepdims=True)
    spread = jnp.mean(centred * centred, axis=-1, keepdims=True)
    rate = lax.rsqrt(spread + 1e-05)
    return centred * rate, rate


def norm_back(grad, gain, hat, rate):
    scaled = grad * gain
    return rate * (
        scaled
        - jnp.mean(scaled, axis=-1, keepdims=True)
        - hat * jnp.mean(scaled * hat, axis=-1, keepdims=True)
    )


def head_mask(kind):
    row = lax.broadcasted_iota(jnp.int32, (HEADS, kind.width), 0)
    lane = lax.broadcasted_iota(jnp.int32, (HEADS, kind.width), 1)
    return (lane // HEAD == row).astype(WIDE)


def by_head(rows, mask):
    n, width = rows.shape
    return (rows[:, None, :] * mask[None]).reshape(n * HEADS, width)


def from_heads(rows, mask):
    width = rows.shape[1]
    return jnp.sum(rows.reshape(SEQS, HEADS, width) * mask[None], axis=1)


def matrix(ref, kind, start, width):
    return ref[:, : kind.block, start : start + width].reshape(kind.width, width)


def vector(vec_ref, kind, row):
    return vec_ref[row : row + 1, : kind.width]


def sequence(kind, refs, s):
    own, arrived = refs
    first, second = (own, arrived) if kind.index == 0 else (arrived, own)
    return first, second


def place_kernel(img_ref, txt_ref, att_ref, raise_ref, reduce_ref, vec_ref, flat):
    def run(kind):
        ref = img_ref if kind.index == 0 else txt_ref
        n, rows, lanes = ref.shape
        flat[: n * rows, :] = ref[...].reshape(n * rows, lanes).astype(WIDE)
        block, width = kind.block, kind.width

        def lift(base, height, pitch, c):
            return flat[pl.ds(base + c, height, stride=pitch), :].astype(LOW)

        base = 0
        for start, wide in ((0, 3 * width), (AT_OUTPUT, width)):
            pitch = wide // LANES
            for c in range(pitch):
                lane = start + c * LANES
                att_ref[:block, lane : lane + LANES] = lift(base, block, pitch, c)
            base += block * pitch
        pitch = kind.hidden // LANES
        per = kind.part // LANES
        for c in range(pitch):
            lane = c % per * LANES
            raise_ref[c // per, :block, lane : lane + LANES] = lift(base, block, pitch, c)
        base += block * pitch
        pitch = width // LANES
        for c in range(pitch):
            lane = c * LANES
            reduce_ref[: kind.reduce_rows, lane : lane + LANES] = lift(
                base, kind.reduce_rows, pitch, c
            )
        base += kind.reduce_rows * pitch
        pitch = EMB // LANES
        for c in range(pitch):
            lane = AT_EMBED + c * LANES
            att_ref[:block, lane : lane + LANES] = lift(base, block, pitch, c)
        base += block * pitch
        pitch = width // LANES
        for c in range(pitch):
            vec_ref[:, c * LANES : (c + 1) * LANES] = flat[pl.ds(base + c, 16, stride=pitch), :]

    each_tower(run)


def attend_kernel(
    ends_ref,
    img_own,
    img_in,
    txt_own,
    txt_in,
    gat_ref,
    vec_ref,
    second_ref,
    middle_ref,
    query_ref,
    keyed_ref,
    mixture_ref,
    weight_ref,
    mixed_ref,
    first_ref,
    first_scr,
    row_scr,
    at_scr,
):
    def run(kind):
        width, room = kind.width, kind.room
        gain, shift = vector(vec_ref, kind, 0), vector(vec_ref, kind, 1)
        refs = (img_own, img_in) if kind.index == 0 else (txt_own, txt_in)
        halves = sequence(kind, refs, 0)
        mask = head_mask(kind)
        positions = lax.broadcasted_iota(jnp.int32, (room, 1), 0)
        at = lax.axis_index("dp")

        for half in range(2):

            def normalise(i, carry):
                rows = halves[half][i].astype(WIDE)
                hat, _ = standardise(rows)
                first = (hat * gain + shift).astype(LOW)
                s = half * 8 + i
                first_scr[s, :room, :width] = first
                if kind.causal:
                    chosen = positions == ends_ref[(half * 16 + at) * 8 + i]
                    top = jnp.sum(jnp.where(chosen, first.astype(WIDE), 0.0), axis=0, keepdims=True)
                    raw = jnp.sum(jnp.where(chosen, rows, 0.0), axis=0, keepdims=True)
                else:
                    top, raw = first[:1].astype(WIDE), rows[:1]
                row_scr[pl.ds(s, 1), :width] = top
                at_scr[pl.ds(s, 1), :width] = raw
                return carry

            lax.fori_loop(0, 8, normalise, 0)

        tops = row_scr[:, :width].astype(LOW)
        query = dot_nn(tops, matrix(gat_ref, kind, 0, width)) + vector(vec_ref, kind, 2)
        query = query.astype(LOW)
        spread_query = by_head(query.astype(WIDE), mask).astype(LOW)
        keyed = dot_nt(spread_query, matrix(gat_ref, kind, width, width)) * 0.125
        keyed_ref[:, :width] = keyed.astype(LOW)
        query_ref[:, :width] = query
        first_ref[:, :width] = tops
        lane = lax.broadcasted_iota(jnp.int32, (HEADS, room), 1)
        live = lax.broadcasted_iota(jnp.int32, (HEADS, room), 0) < kind.heads

        for half in range(2):

            def weigh(i, carry):
                s = half * 8 + i
                start = pl.multiple_of(s * HEADS, HEADS)
                first = first_scr[s, :room, :width]
                scores = dot_nt(keyed_ref[pl.ds(start, HEADS), :width], first)
                if kind.causal:
                    allowed = lane <= ends_ref[(half * 16 + at) * 8 + i]
                else:
                    allowed = lane < kind.length
                scores = jnp.where(allowed, scores, -1e30)
                raw = jnp.exp(scores - jnp.max(scores, axis=-1, keepdims=True))
                weights = raw / jnp.sum(raw, axis=-1, keepdims=True)
                weights = jnp.where(live, weights, 0.0)
                weight_ref[s, :, :room] = weights
                mixture_ref[pl.ds(start, HEADS), :width] = dot_nn(
                    weights.astype(LOW), first
                ).astype(LOW)
                return carry

            lax.fori_loop(0, 8, weigh, 0)

        totals = jnp.sum(
            weight_ref[:, :, :room].astype(LOW).astype(WIDE), axis=-1, keepdims=True
        ).reshape(SEQS * HEADS, 1)
        valued = dot_nn(mixture_ref[:, :width], matrix(gat_ref, kind, 2 * width, width))
        valued = valued + totals * vector(vec_ref, kind, 3)
        mixed = from_heads(valued, mask).astype(LOW)
        mixed_ref[:, :width] = mixed
        middle = (
            at_scr[:, :width]
            + dot_nn(mixed, matrix(gat_ref, kind, AT_OUTPUT, width))
            + vector(vec_ref, kind, 4)
        )
        middle_ref[:, :width] = middle
        hat, _ = standardise(middle)
        second_ref[:, :width] = (
            hat * vector(vec_ref, kind, 5) + vector(vec_ref, kind, 6)
        ).astype(LOW)

    each_tower(run)


def expand_matrix(ref, kind):
    return ref[:, : kind.block, : kind.part].reshape(kind.width, kind.part)


def reduce_matrix(ref, kind):
    return ref[:, : kind.reduce_rows, : kind.width].reshape(kind.part, kind.width)


def hidden_bias(vec_ref, kind):
    chip = lax.axis_index("dp") // 2
    whole = vec_ref[...]
    row = lax.broadcasted_iota(jnp.int32, (16, 1), 0)
    line = jnp.sum(jnp.where(row == 10 + chip // 2, whole, 0.0), axis=0, keepdims=True)
    return jnp.where(
        chip % 2 == 0, line[:, : kind.part], line[:, kind.part : 2 * kind.part]
    )


def hidden_kernel(second_ref, raise_ref, reduce_ref, vec_ref, part_ref, raised_ref):
    def run(kind):
        width = kind.width
        rows = second_ref[:, :, :width].reshape(8 * SEQS, width)
        raised = dot_nn(rows, expand_matrix(raise_ref, kind)) + hidden_bias(vec_ref, kind)
        raised_ref[:, : kind.part] = raised
        active = (raised * jax.nn.sigmoid(1.702 * raised)).astype(LOW)
        part = dot_nn(active, reduce_matrix(reduce_ref, kind))
        part_ref[:, :, :width] = part.reshape(8, SEQS, width).astype(LOW)

    each_tower(run)


def hidden_back_kernel(
    grad_ref,
    second_ref,
    raised_ref,
    raise_ref,
    reduce_ref,
    back_ref,
    raise_grad_ref,
    reduce_keep_ref,
    reduce_send_ref,
    bias_ref,
    whole,
):
    def run(kind):
        width, part = kind.width, kind.part
        grads = grad_ref[:, :, :width].reshape(8 * SEQS, width)
        rows = second_ref[:, :, :width].reshape(8 * SEQS, width)
        raised = raised_ref[:, :part]
        gate = jax.nn.sigmoid(1.702 * raised)
        active = (raised * gate).astype(LOW)
        slope = gate + 1.702 * raised * gate * (1.0 - gate)
        raised_grad = dot_nt(grads, reduce_matrix(reduce_ref, kind)) * slope
        low_grad = raised_grad.astype(LOW)
        bias_ref[0:1, :part] = jnp.sum(low_grad.astype(WIDE), axis=0, keepdims=True)
        back = dot_nt(low_grad, expand_matrix(raise_ref, kind))
        back_ref[:, :, :width] = back.reshape(8, SEQS, width).astype(LOW)
        raise_grad_ref[:, : kind.block, :part] = (
            dot_tn(rows, low_grad).reshape(16, kind.block, part).astype(LOW)
        )
        whole[:part, :width] = dot_tn(active, grads)
        core = lax.axis_index("dp") % 2
        n = kind.reduce_rows
        keep = pl.multiple_of(core * n, 64)
        send = pl.multiple_of((1 - core) * n, 64)
        reduce_keep_ref[:n, :width] = whole[pl.ds(keep, n), :width]
        reduce_send_ref[:n, :width] = whole[pl.ds(send, n), :width].astype(LOW)

    each_tower(run)


def embed_kernel(part_ref, middle_ref, gat_ref, vec_ref, emb_ref, final_ref, pooled_ref, proj_ref):
    def run(kind):
        width = kind.width
        final = (
            middle_ref[:, :width]
            + jnp.sum(part_ref[:, :, :width].astype(WIDE), axis=0)
            + vector(vec_ref, kind, 7)
        )
        final_ref[:, :width] = final
        hat, _ = standardise(final)
        pooled = (hat * vector(vec_ref, kind, 8) + vector(vec_ref, kind, 9)).astype(LOW)
        pooled_ref[:, :width] = pooled
        proj = dot_nn(pooled, matrix(gat_ref, kind, 0, EMB))
        proj_ref[...] = proj
        size = jnp.sum(proj * proj, axis=-1, keepdims=True) + 1e-06
        emb_ref[...] = (proj * lax.rsqrt(size)).astype(LOW)

    each_tower(run)


def objective_kernel(
    scale_ref,
    all_ref,
    valid_ref,
    final_ref,
    proj_ref,
    gat_ref,
    vec_ref,
    low_ref,
    grad_ref,
    proj_grad_ref,
    final_vec_ref,
    loss_ref,
    scale_new_ref,
    own_scr,
):
    def ordered(which):
        blocks = []
        for half in range(2):
            for j in range(16):
                rows = all_ref[j % 2, which * 8 + j // 2].astype(WIDE)
                blocks.append(rows[half * 8 : half * 8 + 8])
        return jnp.concatenate(blocks, axis=0).astype(LOW)

    img, txt = ordered(0), ordered(1)
    total = img.shape[0]
    scale = jnp.exp(jnp.full((1, 1), scale_ref[0], WIDE))
    allowed = valid_ref[...].reshape(total, total) > 0
    same = lax.broadcasted_iota(jnp.int32, (total, total), 0) == lax.broadcasted_iota(
        jnp.int32, (total, total), 1
    )
    same = same.astype(WIDE)

    def side(left, right):
        logits = scale * dot_nt(left, right)
        masked = jnp.where(allowed, logits, -1e30)
        top = jnp.max(masked, axis=1, keepdims=True)
        lse = jnp.log(jnp.sum(jnp.exp(masked - top), axis=1, keepdims=True)) + top
        terms = 0.5 * (jnp.where(allowed, jnp.exp(logits - lse), 0.0) - same)
        loss = 0.5 * (
            jnp.sum(lse, axis=0, keepdims=True)
            - jnp.sum(jnp.sum(logits * same, axis=1, keepdims=True), axis=0, keepdims=True)
        )
        rate = jnp.sum(jnp.sum(terms * logits, axis=1, keepdims=True), axis=0, keepdims=True)
        return (scale * terms).astype(LOW), loss, rate

    row_back, row_loss, row_rate = side(img, txt)
    col_back, col_loss, col_rate = side(txt, img)
    loss_ref[0] = jnp.sum(row_loss + col_loss) / total
    parts = advance(
        scale_ref[0], scale_ref[1], scale_ref[2], jnp.sum(row_rate + col_rate), scale_rate
    )
    for k in range(3):
        scale_new_ref[k] = parts[k]

    def run(kind):
        width = kind.width
        if kind.index == 0:
            emb_grad = dot_nn(row_back, txt) + dot_tn(col_back, txt)
        else:
            emb_grad = dot_nn(col_back, img) + dot_tn(row_back, img)
        own_scr[...] = emb_grad
        at = lax.axis_index("dp")
        mine = jnp.concatenate(
            [
                own_scr[pl.ds(pl.multiple_of(half * 128 + at * 8, 8), 8), :]
                for half in range(2)
            ],
            axis=0,
        )
        proj = proj_ref[...]
        size = jnp.sum(proj * proj, axis=-1, keepdims=True) + 1e-06
        along = jnp.sum(proj * mine, axis=-1, keepdims=True)
        proj_grad = ((mine - proj * along / size) * lax.rsqrt(size)).astype(LOW)
        proj_grad_ref[...] = proj_grad
        pooled_grad = dot_nt(proj_grad, matrix(gat_ref, kind, 0, EMB))
        hat, rate = standardise(final_ref[:, :width])
        final_vec_ref[0:1, :width] = jnp.sum(pooled_grad * hat, axis=0, keepdims=True)
        final_vec_ref[1:2, :width] = jnp.sum(pooled_grad, axis=0, keepdims=True)
        final_grad = norm_back(pooled_grad, vector(vec_ref, kind, 8), hat, rate)
        grad_ref[:, :width] = final_grad
        low = final_grad.astype(LOW)
        low_ref[:, :width] = low
        final_vec_ref[2:3, :width] = jnp.sum(low.astype(WIDE), axis=0, keepdims=True)

    each_tower(run)


def centre_kernel(
    scale_ref,
    second_ref,
    middle_ref,
    gat_ref,
    vec_ref,
    raise_ref,
    reduce_ref,
    valid_ref,
    loss_ref,
    scale_new_ref,
    final_grad_ref,
    pooled_ref,
    proj_grad_ref,
    final_vec_ref,
    raise_grad_ref,
    reduce_keep_ref,
    reduce_send_ref,
    bias_ref,
    backs_ref,
    emb_weight_ref,
    seconds,
    part,
    parts,
    raised,
    emb,
    embs,
    final,
    proj,
    low,
    lows,
    back,
    own_scr,
    whole,
    send_sems,
    recv_sems,
    spread_send,
    spread_recv,
    core_sems,
    fetch_sem,
):
    tower, at = here()
    fetch = pltpu.make_async_copy(
        gat_ref.at[:, :, pl.ds(AT_EMBED, EMB)], emb_weight_ref, fetch_sem
    )
    fetch.start()
    greet([*both_towers(tower, at), (tower, at + 1 - at % 2 * 2)])
    sent = []
    sent += group_exchange(False, second_ref, seconds, send_sems.at[0], recv_sems.at[0])
    hidden_kernel(seconds, raise_ref, reduce_ref, vec_ref, part, raised)
    sent += group_exchange(True, part, parts, send_sems.at[1], recv_sems.at[1])
    fetch.wait()
    embed_kernel(parts, middle_ref, emb_weight_ref, vec_ref, emb, final, pooled_ref, proj)
    sent += spread(emb, embs, spread_send, spread_recv, core_sems)
    objective_kernel(
        scale_ref,
        embs,
        valid_ref,
        final,
        proj,
        emb_weight_ref,
        vec_ref,
        low,
        final_grad_ref,
        proj_grad_ref,
        final_vec_ref,
        loss_ref,
        scale_new_ref,
        own_scr,
    )
    sent += group_exchange(False, low, lows, send_sems.at[2], recv_sems.at[2])
    hidden_back_kernel(
        lows,
        seconds,
        raised,
        raise_ref,
        reduce_ref,
        back,
        raise_grad_ref,
        reduce_keep_ref,
        reduce_send_ref,
        bias_ref,
        whole,
    )
    sent += group_exchange(True, back, backs_ref, send_sems.at[3], recv_sems.at[3])
    for copy in sent:
        copy.wait_send()


def attend_back_kernel(
    ends_ref,
    img_own,
    img_in,
    txt_own,
    txt_in,
    gat_ref,
    vec_ref,
    back_ref,
    grad_ref,
    middle_ref,
    query_ref,
    keyed_ref,
    mixture_ref,
    weight_ref,
    mixed_ref,
    first_ref,
    pooled_ref,
    proj_grad_ref,
    final_vec_ref,
    bias_ref,
    img_keep,
    txt_keep,
    img_send,
    txt_send,
    factor_ref,
    outer_ref,
    rows_grad,
    middle_scr,
    query_back,
    valued_scr,
    shared_scr,
    turned,
    gains,
):
    def run(kind):
        width, room, length = kind.width, kind.room, kind.length
        gain, shift = vector(vec_ref, kind, 0), vector(vec_ref, kind, 1)
        refs = (img_own, img_in) if kind.index == 0 else (txt_own, txt_in)
        halves = sequence(kind, refs, 0)
        keep, send = (img_keep, img_send) if kind.index == 0 else (txt_keep, txt_send)
        mask = head_mask(kind)
        positions = lax.broadcasted_iota(jnp.int32, (room, 1), 0)
        at = lax.axis_index("dp")

        second_grad = jnp.sum(back_ref[:, :, :width].astype(WIDE), axis=0)
        hat, rate = standardise(middle_ref[:, :width])
        middle_grad = grad_ref[:, :width] + norm_back(
            second_grad, vector(vec_ref, kind, 5), hat, rate
        )
        middle_scr[:, :width] = middle_grad
        output_grad = middle_grad.astype(LOW)
        mixed_grad = dot_nt(output_grad, matrix(gat_ref, kind, AT_OUTPUT, width)).astype(LOW)
        spread_grad = by_head(mixed_grad.astype(WIDE), mask)
        constant = jnp.sum(spread_grad * vector(vec_ref, kind, 3), axis=-1, keepdims=True)
        valued = dot_nt(
            spread_grad.astype(LOW), matrix(gat_ref, kind, 2 * width, width)
        ).astype(LOW)
        valued_scr[:, :width] = valued
        shared_scr[...] = jnp.broadcast_to(constant, (256, LANES))

        def normal(half, i):
            rows = halves[half][i].astype(WIDE)
            hat, rate = standardise(rows)
            return hat, rate

        for half in range(2):

            def through(i, carry):
                s = half * 8 + i
                start = pl.multiple_of(s * HEADS, HEADS)
                span = pl.ds(start, HEADS)
                hat, _ = normal(half, i)
                first = (hat * gain + shift).astype(LOW)
                weights = weight_ref[s, :, :room]
                slope = dot_nt(valued_scr[span, :width], first) + shared_scr[span, 0:1]
                slope = weights * (
                    slope - jnp.sum(weights * slope, axis=-1, keepdims=True)
                )
                slope = slope.astype(LOW)
                query_back[span, :width] = dot_nn(slope, first)
                rows_grad[s, :room, :width] = dot_tn(slope, keyed_ref[span, :width]) + dot_tn(
                    weights.astype(LOW), valued_scr[span, :width]
                )
                return carry

            lax.fori_loop(0, 8, through, 0)

        turns = query_back[:, :width].astype(LOW)
        query_grad = from_heads(
            dot_nn(turns, matrix(gat_ref, kind, width, width)) * 0.125, mask
        ).astype(LOW)
        top_grad = dot_nt(query_grad, matrix(gat_ref, kind, 0, width))
        gains[...] = jnp.zeros_like(gains)
        turned[:, :width] = top_grad

        for half in range(2):
            mine = half == kind.index

            def finish(i, carry):
                s = half * 8 + i
                hat, rate = normal(half, i)
                grad = rows_grad[s, :room, :width]
                top = turned[pl.ds(s, 1), :width]
                low = middle_scr[pl.ds(s, 1), :width]
                if kind.causal:
                    chosen = (positions == ends_ref[(half * 16 + at) * 8 + i]).astype(WIDE)
                else:
                    chosen = (positions == 0).astype(WIDE)
                grad = grad + chosen * top
                gains[0:1, :width] += jnp.sum(grad * hat, axis=0, keepdims=True)
                gains[1:2, :width] += jnp.sum(grad, axis=0, keepdims=True)
                result = norm_back(grad, gain, hat, rate) + chosen * low
                if mine:
                    keep[i] = result[:length]
                else:
                    send[i] = result.astype(LOW)
                return carry

            lax.fori_loop(0, 8, finish, 0)

        factor_ref[:, 0:width] = query_ref[:, :width]
        factor_ref[:, WIDTH : WIDTH + width] = mixed_grad
        factor_ref[:, 2 * WIDTH : 2 * WIDTH + width] = query_grad
        factor_ref[:, 3 * WIDTH : 3 * WIDTH + width] = output_grad
        factor_ref[:, 4 * WIDTH : 4 * WIDTH + EMB] = proj_grad_ref[...]
        start = 4 * WIDTH + EMB

        def column_sum(value):
            return jnp.sum(value.astype(WIDE), axis=0, keepdims=True)

        totals = jnp.sum(
            weight_ref[:, :, :room].astype(LOW).astype(WIDE), axis=-1, keepdims=True
        ).reshape(SEQS * HEADS, 1)
        lines = [
            gains[0:1, :width],
            gains[1:2, :width],
            column_sum(query_grad),
            column_sum(spread_grad * totals),
            column_sum(output_grad),
            column_sum(second_grad * hat),
            column_sum(second_grad),
            final_vec_ref[2:3, :width],
            final_vec_ref[0:1, :width],
            final_vec_ref[1:2, :width],
            jnp.pad(bias_ref[0:1, : kind.part], ((0, 0), (0, width - kind.part))),
            jnp.zeros((5, width), WIDE),
        ]
        factor_ref[:, start : start + width] = jnp.concatenate(lines, axis=0).astype(LOW)

        slot = lax.broadcasted_iota(jnp.int32, (HEADS, 1), 0)

        def in_slot(index, value):
            chosen = (slot == index).astype(WIDE)
            return (value.astype(WIDE)[:, None, :] * chosen[None]).reshape(SEQS * HEADS, width)

        left = (
            mixture_ref[:, :width].astype(WIDE)
            + in_slot(12, first_ref[:, :width])
            + in_slot(13, mixed_ref[:, :width])
            + in_slot(14, pooled_ref[:, :width])
        )
        block = kind.block
        outer_ref[:, :block, 0:256] = left.T.reshape(16, block, 256).astype(LOW)
        outer_ref[:, :block, 256:512] = query_back[:, :width].T.reshape(16, block, 256).astype(LOW)

    each_tower(run)


def weigh_kernel(
    outer_ref, factor_ref, raise_ref, keep_ref, sent_ref, img_ref, txt_ref, flat, acc, lines
):
    def run(kind):
        width, block = kind.width, kind.block
        mask = head_mask(kind)
        slot = lax.broadcasted_iota(jnp.int32, (HEADS, 1), 0)
        acc[...] = jnp.zeros_like(acc)
        lines[...] = jnp.zeros_like(lines)

        def in_slot(index, value):
            chosen = (slot == index).astype(WIDE)
            return (
                (value.astype(WIDE)[:, None, :] * chosen[None])
                .reshape(SEQS * HEADS, value.shape[1])
                .astype(LOW)
            )

        def add(source, carry):
            left = outer_ref[source, :block, 0:256]
            turned = outer_ref[source, :block, 256:512]

            def factor(k, wide):
                return factor_ref[source, :, k * WIDTH : k * WIDTH + wide]

            query = by_head(factor(0, width).astype(WIDE), mask).astype(LOW)
            value = by_head(factor(1, width).astype(WIDE), mask).astype(LOW)
            acc[:block, 0:width] += dot_nn(left, in_slot(12, factor(2, width)))
            acc[:block, width : 2 * width] += dot_nn(turned, query) * 0.125
            acc[:block, 2 * width : 3 * width] += dot_nn(left, value)
            acc[:block, AT_OUTPUT : AT_OUTPUT + width] += dot_nn(left, in_slot(13, factor(3, width)))
            acc[:block, AT_EMBED : AT_EMBED + EMB] += dot_nn(left, in_slot(14, factor(4, EMB)))
            start = 4 * WIDTH + EMB
            part = factor_ref[source, :, start : start + width].astype(WIDE)
            lines[0:10, :width] += part[0:10]
            chip = source // 2
            piece = part[10:11, : kind.part]
            other = jnp.zeros_like(piece)
            both = jnp.where(
                chip % 2 == 0,
                jnp.concatenate([piece, other], axis=1),
                jnp.concatenate([other, piece], axis=1),
            )
            rows = 2 * kind.part // width
            lines[pl.ds(10 + chip // 2, 1), :width] += both
            return carry

        lax.fori_loop(0, 16, add, 0)

        def drop(base, height, pitch, c, value):
            flat[pl.ds(base + c, height, stride=pitch), :] = value

        base = 0
        for start, wide in ((0, 3 * width), (AT_OUTPUT, width)):
            pitch = wide // LANES
            for c in range(pitch):
                lane = start + c * LANES
                drop(base, block, pitch, c, acc[:block, lane : lane + LANES])
            base += block * pitch
        pitch = kind.hidden // LANES
        per = kind.part // LANES
        for c in range(pitch):
            chip, lane = c // per, c % per * LANES
            value = raise_ref[2 * chip, :block, lane : lane + LANES].astype(WIDE) + raise_ref[
                2 * chip + 1, :block, lane : lane + LANES
            ].astype(WIDE)
            drop(base, block, pitch, c, value)
        base += block * pitch
        pitch = width // LANES
        n = kind.reduce_rows
        other_core = 1 - lax.axis_index("dp") % 2
        for c in range(pitch):
            lane = c * LANES
            value = keep_ref[:n, lane : lane + LANES] + sent_ref[
                other_core, :n, lane : lane + LANES
            ].astype(WIDE)
            drop(base, n, pitch, c, value)
        base += n * pitch
        pitch = EMB // LANES
        for c in range(pitch):
            lane = AT_EMBED + c * LANES
            drop(base, block, pitch, c, acc[:block, lane : lane + LANES])
        base += block * pitch
        pitch = width // LANES
        for c in range(pitch):
            drop(base, 16, pitch, c, lines[:, c * LANES : (c + 1) * LANES])
        ref = img_ref if kind.index == 0 else txt_ref
        n, rows, lanes = ref.shape
        ref[...] = flat[: n * rows, :].reshape(n, rows, lanes).astype(LOW)

    each_tower(run)


def compute(kernel, outs, scratch, scalars, *args):
    like = jax.ShapeDtypeStruct
    vmem = pl.BlockSpec(memory_space=pltpu.VMEM)
    smem = pl.BlockSpec(memory_space=pltpu.SMEM)
    return pl.pallas_call(
        kernel,
        out_shape=[like(shape, dtype) for shape, dtype in outs],
        in_specs=[smem] * scalars + [vmem] * (len(args) - scalars),
        out_specs=[vmem] * len(outs),
        scratch_shapes=[pltpu.VMEM(shape, dtype) for shape, dtype in scratch],
        compiler_params=pltpu.CompilerParams(vmem_limit_bytes=GRANT),
    )(*args)


def centre(scale_state, second, middle, gat, vec, rise, fall, pairs, number):
    like = jax.ShapeDtypeStruct
    vmem = pl.BlockSpec(memory_space=pltpu.VMEM)
    smem = pl.BlockSpec(memory_space=pltpu.SMEM)
    group = ((8, SEQS, WIDTH), LOW)
    rows_low, rows_wide = ((SEQS, WIDTH), LOW), ((SEQS, WIDTH), WIDE)
    outs = [
        rows_wide,
        rows_low,
        ((SEQS, EMB), LOW),
        ((8, WIDTH), WIDE),
        ((16, 48, PART), LOW),
        ((192, WIDTH), WIDE),
        ((192, WIDTH), LOW),
        ((8, PART), WIDE),
        group,
    ]
    scratch = [
        ((16, 48, EMB), LOW),
        group,
        group,
        group,
        ((128, PART), WIDE),
        ((SEQS, EMB), LOW),
        ((2, 16, SEQS, EMB), LOW),
        rows_wide,
        ((SEQS, EMB), WIDE),
        rows_low,
        group,
        group,
        ((256, EMB), WIDE),
        ((PART, WIDTH), WIDE),
    ]
    return pl.pallas_call(
        centre_kernel,
        out_shape=[like((1,), WIDE), like((3,), WIDE)] + [like(*out) for out in outs],
        in_specs=[smem, vmem, vmem, ANY] + [vmem] * 4,
        out_specs=[smem, smem] + [vmem] * len(outs),
        scratch_shapes=[pltpu.VMEM(*each) for each in scratch]
        + [
            pltpu.SemaphoreType.DMA((4, 8)),
            pltpu.SemaphoreType.DMA((4, 7)),
            pltpu.SemaphoreType.DMA((16,)),
            pltpu.SemaphoreType.DMA((15,)),
            pltpu.SemaphoreType.DMA((2,)),
            pltpu.SemaphoreType.DMA,
        ],
        compiler_params=comm_params(number),
    )(scale_state, second, middle, gat, vec, rise, fall, pairs)


def plans_for(img_share, txt_share):
    return (
        Plan(0, img_share, 96, (9, 3, 12, 12, 2)),
        Plan(1, txt_share, 64, (6, 2, 8, 8, 2)),
    )


def to_chunks(flat, plan, me):
    start = me * plan.share % plan.chunk
    padded = jnp.pad(flat, (plan.chunk, plan.local * plan.chunk - plan.share))
    piece = lax.dynamic_slice(padded, (plan.chunk - start,), (plan.local * plan.chunk,))
    return piece.astype(LOW).reshape(plan.local, plan.rows, LANES)


def from_chunks(chunks, plan, me):
    start = me * plan.share % plan.chunk
    return lax.dynamic_slice(chunks.reshape(-1), (start,), (plan.share,)).astype(WIDE)


def step(
    img_tokens,
    txt_tokens,
    txt_ends,
    valid,
    img_master,
    img_moment,
    img_average,
    txt_master,
    txt_moment,
    txt_average,
    scale_state,
):
    me = lax.axis_index(("tower", "dp"))
    tower_at = lax.axis_index("tower")
    is_image = tower_at == 0
    plans = plans_for(img_master.shape[0], txt_master.shape[0])
    img_rows = jnp.pad(img_tokens, ((0, 0), (0, TOWERS[0].room - TOWERS[0].length), (0, 0)))
    txt_rows = jnp.pad(txt_tokens, ((0, 0), (0, TOWERS[1].room - TOWERS[1].length), (0, 0)))
    img_slots, txt_slots, pairs = deal(
        to_chunks(img_master, plans[0], me), to_chunks(txt_master, plans[1], me), valid, plans, 0
    )
    att, rise, fall, vec = compute(
        place_kernel,
        [
            ((48, ATTENTION), LOW),
            ((8, 48, PART), LOW),
            ((192, WIDTH), LOW),
            ((16, WIDTH), WIDE),
        ],
        [((39 * 96, LANES), WIDE)],
        0,
        img_slots,
        txt_slots,
    )
    rise = jnp.repeat(rise, 2, axis=0)
    gat, fall, img_in, txt_in, rise = exchange(att, fall, img_rows, txt_rows, [rise], 1)
    second, middle, query, keyed, mixture, weights, mixed, tops = compute(
        attend_kernel,
        [
            ((SEQS, WIDTH), LOW),
            ((SEQS, WIDTH), WIDE),
            ((SEQS, WIDTH), LOW),
            ((256, WIDTH), LOW),
            ((256, WIDTH), LOW),
            ((SEQS, HEADS, LANES), WIDE),
            ((SEQS, WIDTH), LOW),
            ((SEQS, WIDTH), LOW),
        ],
        [((SEQS, ROOM, WIDTH), LOW), ((SEQS, WIDTH), WIDE), ((SEQS, WIDTH), WIDE)],
        1,
        txt_ends,
        img_rows,
        img_in,
        txt_rows,
        txt_in,
        gat,
        vec,
    )
    (
        loss,
        scale_new,
        final_grad,
        pooled,
        proj_grad,
        final_vec,
        rise_grad,
        fall_keep,
        fall_send,
        bias_grad,
        backs,
    ) = centre(scale_state, second, middle, gat, vec, rise, fall, pairs, 2)
    img_keep, txt_keep, img_send, txt_send, factor, outer = compute(
        attend_back_kernel,
        [
            ((8, TOWERS[0].length, D_IMG), WIDE),
            ((8, TOWERS[1].length, D_TXT), WIDE),
            (img_rows.shape, LOW),
            (txt_rows.shape, LOW),
            ((SEQS, 5 * WIDTH + EMB), LOW),
            ((16, 48, 512), LOW),
        ],
        [
            ((SEQS, ROOM, WIDTH), WIDE),
            ((SEQS, WIDTH), WIDE),
            ((256, WIDTH), WIDE),
            ((256, WIDTH), LOW),
            ((256, LANES), WIDE),
            ((SEQS, WIDTH), WIDE),
            ((8, WIDTH), WIDE),
        ],
        1,
        txt_ends,
        img_rows,
        img_in,
        txt_rows,
        txt_in,
        gat,
        vec,
        backs,
        final_grad,
        middle,
        query,
        keyed,
        mixture,
        weights,
        mixed,
        tops,
        pooled,
        proj_grad,
        final_vec,
        bias_grad,
    )
    factors, falls, txt_home, img_home, outers, rises = exchange(
        factor, fall_send, txt_send, img_send, [outer, rise_grad], 3
    )
    img_slots, txt_slots = compute(
        weigh_kernel,
        [(img_slots.shape, LOW), (txt_slots.shape, LOW)],
        [((39 * 96, LANES), WIDE), ((48, ATTENTION), WIDE), ((16, WIDTH), WIDE)],
        0,
        outers,
        factors,
        rises,
        fall_keep,
        falls,
    )
    img_chunks, txt_chunks = collect(img_slots, txt_slots, plans, 4)
    img_grad = jnp.where(is_image, img_keep, img_home[:, : TOWERS[0].length].astype(WIDE))
    txt_grad = jnp.where(is_image, txt_home[:, : TOWERS[1].length].astype(WIDE), txt_keep)
    img_new = advance(
        img_master, img_moment, img_average, from_chunks(img_chunks, plans[0], me), step_rate
    )
    txt_new = advance(
        txt_master, txt_moment, txt_average, from_chunks(txt_chunks, plans[1], me), step_rate
    )
    return (
        loss[0],
        img_grad,
        txt_grad,
        img_new[0],
        img_new[1],
        img_new[2],
        img_new[0].astype(LOW),
        txt_new[0],
        txt_new[1],
        txt_new[2],
        txt_new[0].astype(LOW),
        scale_new,
    )


def from_partner(value, axis, stride):
    mask = 2**stride
    pairs = [(source, source ^ mask) for source in range(lax.axis_size(axis))]
    return lax.ppermute(value, axis, pairs)


def round_value(v):
    return lax.optimization_barrier(v.astype(jnp.bfloat16)).astype(jnp.float32)


def make_low():

    def value_keep(v):
        return (round_value(v), None)

    def grad_pass(kept, grad):
        return (grad,)

    rounded = jax.custom_vjp(round_value)
    rounded.defvjp(value_keep, grad_pass)
    return rounded


def low(v):
    return make_low()(v)


def make_low_back():

    def identity(v):
        return v

    def value_pass(v):
        return (v, None)

    def grad_round(kept, grad):
        return (round_value(grad),)

    passed = jax.custom_vjp(identity)
    passed.defvjp(value_pass, grad_round)
    return passed


def low_back(v):
    return make_low_back()(v)


def both_ways(value):
    return low(low_back(value))


def product(left, right):
    return jnp.matmul(left, right)


def contract(form, left, right):
    return jnp.einsum(form, left, right)


def layer_norm(values, gain_row, shift_row):
    centred = values - jnp.mean(values, axis=-1, keepdims=True)
    spread = jnp.mean(centred * centred, axis=-1, keepdims=True)
    return centred * lax.rsqrt(spread + 1e-05) * gain_row + shift_row


def unpack(flat_weights, model_width, hidden_width, embed_width):
    piece_shapes = [
        (model_width, 3 * model_width),
        (model_width, model_width),
        (model_width, hidden_width),
        (hidden_width, model_width),
        (model_width, embed_width),
        (10, model_width),
        (hidden_width,),
    ]
    pieces = []
    offset = 0
    for piece_shape in piece_shapes:
        length = math.prod(piece_shape)
        pieces.append(flat_weights[offset : offset + length].reshape(piece_shape))
        offset = offset + length
    return pieces


def encode(tokens, flat_weights, positions, causal, model_width, hidden_width, embed_width):
    w_inputs, w_output, w_expand, w_reduce, w_embed, vectors, expand_bias = unpack(
        flat_weights, model_width, hidden_width, embed_width
    )
    groups = tokens.shape[0]
    length = tokens.shape[1]
    first = low(layer_norm(tokens, vectors[0], vectors[1]))
    bias_in = jnp.concatenate([vectors[2], jnp.zeros_like(vectors[2]), vectors[3]])
    joined = both_ways(product(first, w_inputs) + bias_in)
    joined = joined.reshape(groups, length, 3, model_width // HEAD, HEAD)
    scores = low_back(contract("gqhd,gkhd->ghqk", joined[:, :, 0], joined[:, :, 1]) * 0.125)
    if causal:
        row_index = lax.broadcasted_iota(jnp.int32, (length, length), 0)
        col_index = lax.broadcasted_iota(jnp.int32, (length, length), 1)
        scores = jnp.where(col_index <= row_index, scores, -1e30)
    row_top = jnp.max(scores, axis=-1, keepdims=True)
    raw_weights = jnp.exp(scores - row_top)
    attention = low(raw_weights / jnp.sum(raw_weights, axis=-1, keepdims=True))
    mixed_heads = both_ways(
        contract("ghqk,gkhd->gqhd", attention, joined[:, :, 2]).reshape(groups, length, model_width)
    )
    middle = tokens + low_back(product(mixed_heads, w_output) + vectors[4])
    second = low(layer_norm(middle, vectors[5], vectors[6]))
    raised = low_back(product(second, w_expand) + expand_bias)
    active = low(raised * jax.nn.sigmoid(1.702 * raised))
    final_rows = middle + low_back(product(active, w_reduce) + vectors[7])
    pooled = jnp.take_along_axis(final_rows, positions[:, None, None], axis=1)[:, 0]
    pooled = low(layer_norm(pooled, vectors[8], vectors[9]))
    projected = low_back(product(pooled, w_embed))
    return low(
        projected * lax.rsqrt(jnp.sum(projected * projected, axis=-1, keepdims=True) + 1e-06)
    )


def inner(left, right):
    return lax.dot_general(
        left, right, (((1,), (1,)), ((), ())), preferred_element_type=jnp.float32
    )


def across(left, right):
    return lax.dot_general(
        left, right, (((0,), (0,)), ((), ())), preferred_element_type=jnp.float32
    )


def softmax_total(logits, allowed):
    masked = jnp.where(allowed, logits, -1e30)
    row_top = jnp.max(masked, axis=1, keepdims=True)
    return jnp.log(jnp.sum(jnp.exp(masked - row_top), axis=1)) + row_top[:, 0]


def advance(master, moment, average, grads, rate):
    moment_new = momentum_rate * moment + grads
    master_new = master - rate * (grads + momentum_rate * moment_new)
    average_new = average_rate * average + (1.0 - average_rate) * master_new
    return (master_new, moment_new, average_new)


def padded_to(flat, length):
    return jnp.pad(flat, (0, length - flat.shape[0]))


def body(
    img_tokens,
    txt_tokens,
    txt_ends,
    valid,
    img_master,
    img_moment,
    img_average,
    txt_master,
    txt_moment,
    txt_average,
    scale_state,
):
    batch_rows = img_tokens.shape[0]
    total_rows = batch_rows * lax.axis_size(("tower", "dp"))
    device_at = lax.axis_index(("tower", "dp"))
    tower_at = lax.axis_index("tower")
    is_image = tower_at == 0
    img_share = img_master.shape[0]
    txt_share = txt_master.shape[0]
    img_count = img_tokens.size
    txt_count = txt_tokens.size
    shard_room = max(img_share, txt_share)
    token_room = max(img_count, txt_count)
    tower_count = lax.axis_size("dp")
    dp_at = lax.axis_index("dp")
    img_low = padded_to(img_master.astype(jnp.bfloat16), shard_room)
    txt_low = padded_to(txt_master.astype(jnp.bfloat16), shard_room)
    token_out = jnp.where(
        is_image,
        padded_to(txt_tokens.reshape(-1), token_room),
        padded_to(img_tokens.reshape(-1), token_room),
    )
    weight_out = jnp.where(is_image, txt_low, img_low)
    weight_mine = jnp.where(is_image, img_low, txt_low)
    token_in, weight_in = from_partner((token_out, weight_out), "tower", 0)
    stacked = jnp.where(
        is_image, jnp.stack([weight_mine, weight_in]), jnp.stack([weight_in, weight_mine])
    )
    gathered = lax.all_gather(stacked, "dp", axis=1, tiled=True)
    pair_ends = jnp.concatenate(
        [
            lax.dynamic_slice_in_dim(txt_ends, dp_at * batch_rows, batch_rows),
            lax.dynamic_slice_in_dim(txt_ends, (tower_count + dp_at) * batch_rows, batch_rows),
        ]
    )
    pair_zero = jnp.zeros((2 * batch_rows,), jnp.int32)

    def image_weights(whole):
        return whole.reshape(2, tower_count, shard_room).reshape(-1).astype(jnp.float32)

    def text_weights(whole):
        return (
            whole.reshape(2, tower_count, shard_room)[:, :, :txt_share]
            .reshape(-1)
            .astype(jnp.float32)
        )

    def image_rows(arrived):
        return jnp.concatenate(
            [img_tokens, arrived[:img_count].reshape(img_tokens.shape)], axis=0
        ).astype(jnp.float32)

    def text_rows(arrived):
        return jnp.concatenate([arrived.reshape(txt_tokens.shape), txt_tokens], axis=0).astype(
            jnp.float32
        )

    def image_encode(rows, flat):
        return encode(rows, flat, pair_zero, False, D_IMG, FF_IMG, EMB)

    def text_encode(rows, flat):
        return encode(rows, flat, pair_ends, True, D_TXT, FF_TXT, EMB)

    def image_forward(operands):
        return image_encode(image_rows(operands[1]), image_weights(operands[0]))

    def text_forward(operands):
        return text_encode(text_rows(operands[1]), text_weights(operands[0]))

    pair_emb = lax.cond(is_image, image_forward, text_forward, (gathered, token_in)).astype(
        jnp.bfloat16
    )
    emb_in = from_partner(pair_emb, "tower", 0)
    img_pair = jnp.where(is_image, pair_emb, emb_in)
    txt_pair = jnp.where(is_image, emb_in, pair_emb)
    row_start = tower_at * batch_rows
    img_local = lax.dynamic_slice_in_dim(img_pair, row_start, batch_rows)
    txt_local = lax.dynamic_slice_in_dim(txt_pair, row_start, batch_rows)
    img_all, txt_all = (
        lax.all_gather(img_local, ("tower", "dp"), axis=0, tiled=True),
        lax.all_gather(txt_local, ("tower", "dp"), axis=0, tiled=True),
    )
    logit_scale = jnp.exp(scale_state[0])
    offset = device_at * batch_rows
    row_index = lax.broadcasted_iota(jnp.int32, (batch_rows, total_rows), 0) + offset
    col_index = lax.broadcasted_iota(jnp.int32, (batch_rows, total_rows), 1)
    diagonal = (row_index == col_index).astype(jnp.float32)
    allowed = valid > 0
    row_logits = logit_scale * inner(img_local, txt_all)
    col_logits = logit_scale * inner(txt_local, img_all)
    row_lse = softmax_total(row_logits, allowed)
    col_lse = softmax_total(col_logits, allowed)
    partial_loss = 0.5 * (
        jnp.sum(row_lse)
        - jnp.sum(row_logits * diagonal)
        + jnp.sum(col_lse)
        - jnp.sum(col_logits * diagonal)
    )
    row_terms = 0.5 * (jnp.where(allowed, jnp.exp(row_logits - row_lse[:, None]), 0.0) - diagonal)
    col_terms = 0.5 * (jnp.where(allowed, jnp.exp(col_logits - col_lse[:, None]), 0.0) - diagonal)
    partial_scale = jnp.sum(row_terms * row_logits) + jnp.sum(col_terms * col_logits)
    row_back = (logit_scale * row_terms).astype(jnp.bfloat16)
    col_back = (logit_scale * col_terms).astype(jnp.bfloat16)
    img_emb_grad = jnp.dot(row_back, txt_all, preferred_element_type=jnp.float32)
    txt_emb_grad = jnp.dot(col_back, img_all, preferred_element_type=jnp.float32)
    img_extra, txt_extra = (
        lax.psum_scatter(
            across(col_back, txt_local), ("tower", "dp"), scatter_dimension=0, tiled=True
        ),
        lax.psum_scatter(
            across(row_back, img_local), ("tower", "dp"), scatter_dimension=0, tiled=True
        ),
    )
    img_emb_grad = img_emb_grad + img_extra
    txt_emb_grad = txt_emb_grad + txt_extra
    sums = lax.psum((partial_loss, partial_scale), ("tower", "dp"))
    grad_out = jnp.where(is_image, txt_emb_grad, img_emb_grad)
    grad_in = from_partner(grad_out, "tower", 0)
    pair_cot = jnp.where(
        is_image,
        jnp.concatenate([img_emb_grad, grad_in], axis=0),
        jnp.concatenate([grad_in, txt_emb_grad], axis=0),
    )

    def image_backward(operands):
        recomputed, tower_pullback = jax.vjp(
            image_encode, image_rows(operands[1]), image_weights(operands[0])
        )
        rows_grad, flat_grad = tower_pullback(operands[2])
        own_part = padded_to(rows_grad[:batch_rows].reshape(-1), token_room)
        sent_part = padded_to(rows_grad[batch_rows:].reshape(-1), token_room)
        stacked_grad = flat_grad.reshape(2, tower_count, img_share)
        return (own_part, sent_part, stacked_grad)

    def text_backward(operands):
        recomputed, tower_pullback = jax.vjp(
            text_encode, text_rows(operands[1]), text_weights(operands[0])
        )
        rows_grad, flat_grad = tower_pullback(operands[2])
        own_part = padded_to(rows_grad[batch_rows:].reshape(-1), token_room)
        sent_part = padded_to(rows_grad[:batch_rows].reshape(-1), token_room)
        stacked_grad = jnp.pad(
            flat_grad.reshape(2, tower_count, txt_share),
            ((0, 0), (0, 0), (0, shard_room - txt_share)),
        )
        return (own_part, sent_part, stacked_grad)

    own_part, sent_part, stacked_grad = lax.cond(
        is_image, image_backward, text_backward, (gathered, token_in, pair_cot)
    )
    summed = lax.psum_scatter(stacked_grad, "dp", scatter_dimension=1, tiled=True)
    kept_part = jnp.where(is_image, summed[0, 0], summed[1, 0])
    sent_share = jnp.where(is_image, summed[1, 0], summed[0, 0])
    home_weights, home_tokens = (
        from_partner(sent_share.astype(jnp.bfloat16), "tower", 0).astype(sent_share.dtype),
        from_partner(sent_part.astype(jnp.bfloat16), "tower", 0).astype(sent_part.dtype),
    )
    img_owned = jnp.where(is_image, kept_part, home_weights)
    txt_owned = jnp.where(is_image, home_weights, kept_part)[:txt_share]
    img_grad = jnp.where(is_image, own_part, home_tokens)[:img_count].reshape(img_tokens.shape)
    txt_grad = jnp.where(is_image, home_tokens, own_part).reshape(txt_tokens.shape)
    img_new = advance(img_master, img_moment, img_average, img_owned, step_rate)
    txt_new = advance(txt_master, txt_moment, txt_average, txt_owned, step_rate)
    scale_parts = advance(scale_state[0], scale_state[1], scale_state[2], sums[1], scale_rate)
    scale_new = jnp.stack([scale_parts[0], scale_parts[1], scale_parts[2]])
    return (
        sums[0] / total_rows,
        img_grad,
        txt_grad,
        img_new[0],
        img_new[1],
        img_new[2],
        img_new[0].astype(jnp.bfloat16),
        txt_new[0],
        txt_new[1],
        txt_new[2],
        txt_new[0].astype(jnp.bfloat16),
        scale_new,
    )


def solution(mesh):
    in_specs = (
        P(("tower", "dp"), None, None),
        P(("tower", "dp"), None, None),
        P(),
        P(("tower", "dp"), None),
        P(("tower", "dp")),
        P(("tower", "dp")),
        P(("tower", "dp")),
        P(("tower", "dp")),
        P(("tower", "dp")),
        P(("tower", "dp")),
        P(),
    )
    out_specs = (
        P(),
        P(("tower", "dp"), None, None),
        P(("tower", "dp"), None, None),
        P(("tower", "dp")),
        P(("tower", "dp")),
        P(("tower", "dp")),
        P(("tower", "dp")),
        P(("tower", "dp")),
        P(("tower", "dp")),
        P(("tower", "dp")),
        P(("tower", "dp")),
        P(),
    )
    run = step if (mesh.shape["tower"], mesh.shape["dp"]) == (2, 16) else body
    return jax.shard_map(run, mesh=mesh, in_specs=in_specs, out_specs=out_specs, check_vma=False)
```

```python
import functools
import math

import jax
import jax.numpy as jnp
from jax import lax
from jax.experimental import pallas as pl
from jax.experimental.pallas import tpu as pltpu
from jax.sharding import PartitionSpec as P

D_IMG = 768
FF_IMG = 3072
D_TXT = 512
FF_TXT = 2048
EMB = 512
HEAD = 64


momentum_rate = 0.5
average_rate = 0.5
step_rate = 0.08
scale_rate = 0.0001


MESH = pl.DeviceIdType.MESH
ANY = pl.BlockSpec(memory_space=pl.ANY)
GRANT = 58 * 1024 * 1024
LANES = 128
LOW = jnp.bfloat16
WIDE = jnp.float32


def here():
    return lax.axis_index("tower"), lax.axis_index("dp")


def greet(devices):
    barrier = pltpu.get_barrier_semaphore()
    for device in devices:
        pl.semaphore_signal(barrier, inc=1, device_id=device, device_id_type=MESH)
    pl.semaphore_wait(barrier, len(devices))


def remote(src, dst, send_sem, recv_sem, device):
    return pltpu.make_async_remote_copy(
        src_ref=src,
        dst_ref=dst,
        send_sem=send_sem,
        recv_sem=recv_sem,
        device_id=device,
        device_id_type=MESH,
    )


def comm_params(number):
    return pltpu.CompilerParams(
        collective_id=number, has_side_effects=True, vmem_limit_bytes=GRANT
    )


def same_core(tower, at):
    chip, core = at // 2, at % 2
    return [(tower, (chip + k) % 8 * 2 + core) for k in range(1, 8)]


def both_towers(tower, at):
    place, core = tower * 8 + at // 2, at % 2
    others = [(place + k) % 16 for k in range(1, 16)]
    return [(other // 8, other % 8 * 2 + core) for other in others]


def everyone(tower, at):
    me = tower * 16 + at
    others = [(me + k) % 32 for k in range(1, 32)]
    return [(other // 16, other % 16) for other in others]


def group_exchange(scattered, x_ref, o_ref, send_sem, recv_sem):
    tower, at = here()
    chip = at // 2

    def source(k):
        return x_ref.at[k] if scattered else x_ref

    own = pltpu.make_async_copy(source(chip), o_ref.at[chip], send_sem.at[7])
    sent = []
    for k, device in enumerate(same_core(tower, at)):
        copy = remote(
            source((chip + 1 + k) % 8), o_ref.at[chip], send_sem.at[k], recv_sem.at[k], device
        )
        copy.start()
        sent.append(copy)
    own.start()
    own.wait()
    for k in range(7):
        remote(
            source(chip),
            o_ref.at[(chip + 7 - k) % 8],
            send_sem.at[k],
            recv_sem.at[k],
            (tower, at),
        ).wait_recv()
    return sent


def spread(x_ref, o_ref, send_sem, recv_sem, core_sems):
    tower, at = here()
    chip, core = at // 2, at % 2
    place = tower * 8 + chip
    sibling = (tower, chip * 2 + 1 - core)
    sent = []
    for k, device in enumerate(both_towers(tower, at)):
        copy = remote(x_ref, o_ref.at[core, place], send_sem.at[k], recv_sem.at[k], device)
        copy.start()
        sent.append(copy)
    own = pltpu.make_async_copy(x_ref, o_ref.at[core, place], send_sem.at[15])
    own.start()
    own.wait()
    for k in range(15):
        remote(
            x_ref, o_ref.at[core, (place + 15 - k) % 16], send_sem.at[k], recv_sem.at[k], sibling
        ).wait_recv()
    across = remote(o_ref.at[core], o_ref.at[core], core_sems.at[0], core_sems.at[1], sibling)
    across.start()
    sent.append(across)
    remote(
        o_ref.at[1 - core], o_ref.at[1 - core], core_sems.at[0], core_sems.at[1], sibling
    ).wait_recv()
    return sent


class Ring:
    def __init__(self, src, dst, send, recv):
        self.src, self.dst, self.send, self.recv = src, dst, send, recv
        self.tower, self.at = here()
        self.deep, self.row, self.core = self.at // 4, self.at // 2 % 2, self.at % 2
        self.sibling = (self.tower, self.at + 1 - 2 * self.core)
        self.beside = (self.tower, self.spot(0, 1 - self.row))
        self.sent = []

    def spot(self, k, row):
        return (self.deep + k) % 4 * 4 + row * 2 + self.core

    def launch(self, src, slot, index, device):
        copy = remote(src, self.dst.at[slot], self.send.at[index], self.recv.at[index], device)
        copy.start()
        self.sent.append(copy)

    def arrived(self, slot, index):
        remote(
            self.src, self.dst.at[slot], self.send.at[index], self.recv.at[index], self.sibling
        ).wait_recv()

    def start(self):
        for k in (1, 3, 2):
            self.launch(self.src, self.at, k - 1, (self.tower, self.spot(k, self.row)))
        self.launch(self.src, self.at, 3, self.beside)
        self.launch(self.src, self.at, 7, self.sibling)
        self.own = pltpu.make_async_copy(self.src, self.dst.at[self.at], self.send.at[15])
        self.own.start()

    def relay_deep(self):
        for k in (1, 3, 2):
            slot = self.spot(4 - k, self.row)
            self.arrived(slot, k - 1)
            self.launch(self.dst.at[slot], slot, 3 + k, self.beside)
            self.launch(self.dst.at[slot], slot, 7 + k, self.sibling)

    def relay_row(self):
        for k in (0, 1, 3, 2):
            slot = self.spot(4 - k, 1 - self.row)
            self.arrived(slot, 3 + k)
            self.launch(self.dst.at[slot], slot, 11 + k, self.sibling)

    def finish(self):
        for index in range(8):
            k, row = index % 4, self.row if index < 4 else 1 - self.row
            slot = (self.deep + 4 - k) % 4 * 4 + row * 2 + 1 - self.core
            self.arrived(slot, 7 + index)
        self.own.wait()

    def drain(self):
        for copy in self.sent:
            copy.wait_send()


class Blocks:
    def __init__(self, src, dst, send, recv, shared=1):
        self.src, self.dst, self.send, self.recv = src, dst, send, recv
        self.tower, self.at = here()
        self.shared = shared
        self.sent = []

    def start(self):
        for k in range(1, 16):
            to = (self.at + k) % 16
            copy = remote(
                self.src.at[to // self.shared],
                self.dst.at[self.at],
                self.send.at[k - 1],
                self.recv.at[k - 1],
                (self.tower, to),
            )
            copy.start()
            self.sent.append(copy)
        self.own = pltpu.make_async_copy(
            self.src.at[self.at // self.shared], self.dst.at[self.at], self.send.at[15]
        )
        self.own.start()

    def finish(self):
        for k in range(1, 16):
            remote(
                self.src.at[0],
                self.dst.at[(self.at + 16 - k) % 16],
                self.send.at[k - 1],
                self.recv.at[k - 1],
                (self.tower, self.at),
            ).wait_recv()
        self.own.wait()

    def drain(self):
        for copy in self.sent:
            copy.wait_send()


class Pair:
    def __init__(self, from_zero, zero_dst, from_one, one_dst, sems):
        tower, at = here()
        partner = (1 - tower, at)
        self.tower = tower
        self.up = remote(from_zero, zero_dst, sems.at[0], sems.at[1], partner)
        self.down = remote(from_one, one_dst, sems.at[0], sems.at[1], partner)

    def by_tower(self, zero, one):
        pl.when(self.tower == 0)(zero)
        pl.when(self.tower == 1)(one)

    def start(self):
        self.by_tower(self.up.start, self.down.start)

    def finish(self):
        self.by_tower(self.down.wait_recv, self.up.wait_recv)

    def drain(self):
        self.by_tower(self.up.wait_send, self.down.wait_send)


VECTORS = 5


class Plan:
    def __init__(self, tower, share, rows, per_device):
        self.tower = tower
        self.share = share
        self.rows = rows
        self.chunk = rows * LANES
        self.per_device = per_device
        self.first_slot = [sum(per_device[:p]) for p in range(6)]
        self.first_chunk = [16 * slot for slot in self.first_slot]
        self.slots = sum(per_device) + 1
        self.total = 16 * sum(per_device) + 1
        spans = [self.span(device) for device in range(32)]
        self.counts = sorted({last - first + 1 for first, last in spans})
        self.local = self.counts[-1]

    def span(self, device):
        first = device * self.share // self.chunk
        last = ((device + 1) * self.share - 1) // self.chunk
        return first, min(last, self.total - 1)

    def bounds(self, device):
        first = device * self.share // self.chunk
        last = ((device + 1) * self.share - 1) // self.chunk
        return first, jnp.minimum(last, self.total - 1)

    def pieces(self, p):
        return self.per_device[p] if p < VECTORS else 1

    def target(self, g):
        piece, base, slot, n = (jnp.int32(0), jnp.int32(0), jnp.int32(0), jnp.int32(1))
        for p in range(VECTORS):
            inside = g >= self.first_chunk[p]
            piece = jnp.where(inside, p, piece)
            base = jnp.where(inside, self.first_chunk[p], base)
            slot = jnp.where(inside, self.first_slot[p], slot)
            n = jnp.where(inside, self.per_device[p], n)
        at = (g - base) // n
        return piece, at, slot + (g - base) - at * n


class Deal:
    def __init__(self, plan, s, src, dst, extra, last, sems):
        self.plan, self.s, self.src, self.dst = plan, s, src, dst
        self.extra, self.last = extra, last
        self.chunk_send, self.recv, self.edge, self.fetch = sems
        self.tower, self.at = here()
        self.me = self.tower * 16 + self.at
        self.first, self.last_chunk = plan.bounds(self.me)
        before = (self.me + 31) % 32
        self.head = remote(
            src.at[0], extra, self.edge.at[s, 0], self.edge.at[s, 1], (before // 16, before % 16)
        )

    def send_head(self):
        pl.when(self.me > 0)(self.head.start)

    def move(self, src, i, piece, at_to, slot, wait):
        far = jnp.logical_or(self.tower != self.plan.tower, at_to != self.at)
        recv = self.recv.at[self.s, piece]
        copy = remote(
            src,
            self.dst.at[slot],
            self.chunk_send.at[self.s, i],
            recv,
            (jnp.int32(self.plan.tower), at_to),
        )
        pl.when(far)(copy.wait_send if wait else copy.start)
        if not wait:
            pl.when(jnp.logical_not(far))(
                pltpu.make_async_copy(src, self.dst.at[slot], recv).start
            )

    def whole(self, early, wait):
        def step(i, carry):
            g = self.first + i
            piece, at_to, slot = self.plan.target(g)
            inside = jnp.logical_and(
                jnp.logical_or(i > 0, self.me == 0),
                jnp.logical_or(
                    g < self.last_chunk, jnp.logical_and(self.me == 31, g < self.plan.total - 1)
                ),
            )
            inside = jnp.logical_and(inside, g <= self.last_chunk)
            inside = jnp.logical_and(inside, g < self.plan.total - 1)
            if early is not None:
                hidden = jnp.logical_and(piece >= 2, piece <= 3)
                inside = jnp.logical_and(inside, jnp.logical_not(hidden) if early else hidden)

            @pl.when(inside)
            def _():
                self.move(self.src.at[i], i, piece, at_to, slot, wait)

            return carry

        lax.fori_loop(0, self.plan.local, step, 0)

    def vectors(self, wait):
        @pl.when(self.me == 31)
        def _():
            src = self.src.at[self.last_chunk - self.first]

            def each(k, carry):
                self.move(src, self.plan.local + k, VECTORS, k, self.plan.slots - 1, wait)
                return carry

            lax.fori_loop(0, 16, each, 0)

    def fetch_last(self):
        return pltpu.make_async_copy(
            self.src.at[self.last_chunk - self.first], self.last, self.fetch.at[self.s]
        )

    def join(self):
        @pl.when(self.me < 31)
        def _():
            self.fetch_last().wait()
            self.head.wait_recv()
            self.last[...] = self.last[...] + self.extra[...]
            piece, at_to, slot = self.plan.target(self.last_chunk)
            self.move(self.last, self.plan.local + 16, piece, at_to, slot, False)

    def start_fetch(self):
        pl.when(self.me < 31)(self.fetch_last().start)

    def arrived(self, p):
        part = self.dst.at[pl.ds(self.plan.first_slot[p], self.plan.pieces(p))]
        pltpu.make_async_copy(part, part, self.recv.at[self.s, p]).wait()

    def drain(self):
        pl.when(self.me > 0)(self.head.wait_send)
        self.whole(None, True)
        self.vectors(True)

        @pl.when(self.me < 31)
        def _():
            piece, at_to, slot = self.plan.target(self.last_chunk)
            self.move(self.last, self.plan.local + 16, piece, at_to, slot, True)


class Collect:
    def __init__(self, plan, s, src, dst, send, recv):
        self.plan, self.s, self.src, self.dst = plan, s, src, dst
        self.send, self.recv = send, recv
        self.tower, self.at = here()
        self.me = self.tower * 16 + self.at

    def one(self, owner, slot, g, which, wait):
        first, _ = self.plan.bounds(owner)
        far = owner != self.me
        recv = self.recv.at[self.s]
        copy = remote(
            self.src.at[slot],
            self.dst.at[g - first],
            self.send.at[which, slot],
            recv,
            (owner // 16, owner % 16),
        )
        pl.when(far)(copy.wait_send if wait else copy.start)
        if not wait:
            pl.when(jnp.logical_not(far))(
                pltpu.make_async_copy(self.src.at[slot], self.dst.at[g - first], recv).start
            )

    def piece(self, p, wait):
        n = self.plan.pieces(p)

        def step(i, carry):
            slot = self.plan.first_slot[p] + i
            g = self.plan.first_chunk[p] + self.at * n + i if p < VECTORS else self.plan.total - 1
            low = g * self.plan.chunk // self.plan.share
            high = jnp.minimum(((g + 1) * self.plan.chunk - 1) // self.plan.share, 31)
            self.one(low, slot, g, 0, wait)
            pl.when(high != low)(lambda: self.one(high, slot, g, 1, wait))
            return carry

        if p == VECTORS:


            @pl.when(self.at == 0)
            def _():
                step(0, 0)

        else:
            lax.fori_loop(0, n, step, 0)

    def finish(self):
        first, last = self.plan.bounds(self.me)
        held = last - first + 1
        for n in self.plan.counts:

            @pl.when(held == n)
            def _():
                part = self.dst.at[pl.ds(0, n)]
                pltpu.make_async_copy(part, part, self.recv.at[self.s]).wait()


SEQS = 16
HEADS = 16


class Tower:
    def __init__(self, index, width, hidden, length, room, causal):
        self.index = index
        self.width = width
        self.hidden = hidden
        self.length = length
        self.room = room
        self.causal = causal
        self.heads = width // HEAD
        self.block = width // 16
        self.part = hidden // 8
        self.reduce_rows = hidden // 16


TOWERS = (
    Tower(0, D_IMG, FF_IMG, 50, 64, False),
    Tower(1, D_TXT, FF_TXT, 77, 80, True),
)
ROOM = 80
WIDTH = D_IMG
PART = FF_IMG // 8


def each_tower(run):
    tower = lax.axis_index("tower")
    for kind in TOWERS:
        pl.when(tower == kind.index)(functools.partial(run, kind))


def dot_nn(a, b):
    return lax.dot_general(a, b, (((1,), (0,)), ((), ())), preferred_element_type=WIDE)


def dot_nt(a, b):
    return lax.dot_general(a, b, (((1,), (1,)), ((), ())), preferred_element_type=WIDE)


def dot_tn(a, b):
    return lax.dot_general(a, b, (((0,), (0,)), ((), ())), preferred_element_type=WIDE)


def standardise(rows):
    centred = rows - jnp.mean(rows, axis=-1, keepdims=True)
    spread = jnp.mean(centred * centred, axis=-1, keepdims=True)
    rate = lax.rsqrt(spread + 1e-05)
    return centred * rate, rate


def norm_back(grad, gain, hat, rate):
    scaled = grad * gain
    return rate * (
        scaled
        - jnp.mean(scaled, axis=-1, keepdims=True)
        - hat * jnp.mean(scaled * hat, axis=-1, keepdims=True)
    )


def spans(kind):
    return [
        (lo, min(lo + 512, kind.width), lo // HEAD, (min(lo + 512, kind.width) - lo) // HEAD)
        for lo in range(0, kind.width, 512)
    ]


def head_rows(rows, span):
    lo, hi, _, n = span
    part = rows[:, lo:hi]
    owner = lax.broadcasted_iota(jnp.int32, part.shape, 1) // HEAD
    nothing = jnp.zeros_like(part)
    return jnp.concatenate([jnp.where(owner == h, part, nothing) for h in range(n)], axis=0)


def from_head_rows(rows, span):
    _, _, _, n = span
    owner = lax.broadcasted_iota(jnp.int32, (SEQS, rows.shape[1]), 1) // HEAD
    total = jnp.zeros((SEQS, rows.shape[1]), rows.dtype)
    for h in range(n):
        total = jnp.where(owner == h, rows[h * SEQS : (h + 1) * SEQS], total)
    return total


def side_by_side(parts):
    return parts[0] if len(parts) == 1 else jnp.concatenate(parts, axis=1)


def get_rows(ref, place, width):
    return side_by_side([ref[c, place, :] for c in range(width // LANES)])


def put_rows(ref, place, value):
    for c in range(value.shape[1] // LANES):
        ref[c, place, :] = value[:, c * LANES : (c + 1) * LANES]


def matrix(ref, kind, start, width):
    return ref[:, : kind.block, start : start + width].reshape(kind.width, width)


def vector(vec_ref, kind, row):
    return vec_ref[row : row + 1, : kind.width]


def pieces_of(kind):
    return (
        (kind.block, 3 * kind.width),
        (kind.block, kind.width),
        (kind.block, kind.hidden),
        (kind.reduce_rows, kind.width),
        (kind.block, EMB),
        (16, kind.width),
    )


def lane_blocks(kind, plan, p):
    height, width = pieces_of(kind)[p]
    pitch = width // LANES
    base = plan.first_slot[p] * plan.rows if p < VECTORS else (plan.slots - 1) * plan.rows
    return [(c, pl.ds(base + c, height, stride=pitch)) for c in range(pitch)]


def lift(kind, plan, p, slots, flat):
    n = plan.pieces(p)
    slot = plan.first_slot[p]
    rows = slots[slot : slot + n].reshape(n * plan.rows, LANES)
    flat[slot * plan.rows : (slot + n) * plan.rows, :] = rows.astype(WIDE)
    return [(c, flat[place, :]) for c, place in lane_blocks(kind, plan, p)]


def drop(kind, plan, p, value, slots, flat):
    for c, place in lane_blocks(kind, plan, p):
        flat[place, :] = value(c)
    n = plan.pieces(p)
    slot = plan.first_slot[p]
    rows = flat[slot * plan.rows : (slot + n) * plan.rows, :]
    slots[slot : slot + n] = rows.reshape(n, plan.rows, LANES).astype(LOW)


def front_kernel(
    plans,
    ends_ref,
    img_src,
    txt_src,
    valid_ref,
    img_own,
    txt_own,
    second_ref,
    middle_ref,
    query_ref,
    keyed_ref,
    mixture_ref,
    weight_ref,
    first_ref,
    img_in,
    txt_in,
    ask_ref,
    mix_ref,
    emb_ref,
    vec_ref,
    raise_ref,
    reduce_ref,
    pairs_ref,
    img_slots,
    txt_slots,
    img_extra,
    txt_extra,
    img_last,
    txt_last,
    flat,
    ask_block,
    mix_block,
    emb_block,
    raise_block,
    reduce_block,
    top_scr,
    at_scr,
    score_scr,
    low_scr,
    deal_send,
    deal_recv,
    deal_edge,
    deal_fetch,
    ask_send,
    ask_recv,
    mix_send,
    mix_recv,
    emb_send,
    emb_recv,
    raise_send,
    raise_recv,
    reduce_sems,
    pair_sems,
    valid_send,
    valid_recv,
):
    tower, at = here()
    core = at % 2
    me = tower * 16 + at
    sibling = (tower, at + 1 - 2 * core)
    homes = everyone(tower, at)
    greet(homes)
    deal_sems = (deal_send, deal_recv, deal_edge, deal_fetch)
    deals = [
        Deal(plans[0], 0, img_src, img_slots, img_extra, img_last, deal_sems),
        Deal(plans[1], 1, txt_src, txt_slots, txt_extra, txt_last, deal_sems),
    ]
    pair = Pair(txt_own, txt_in, img_own, img_in, pair_sems)
    ask = Ring(ask_block, ask_ref, ask_send, ask_recv)
    mix = Ring(mix_block, mix_ref, mix_send, mix_recv)
    embed = Ring(emb_block, emb_ref, emb_send, emb_recv)
    rise = Blocks(raise_block, raise_ref, raise_send, raise_recv, 2)
    fall = remote(
        reduce_block, reduce_ref.at[core], reduce_sems.at[0], reduce_sems.at[1], sibling
    )
    fall_own = pltpu.make_async_copy(reduce_block, reduce_ref.at[core], reduce_sems.at[2])
    masks = [
        remote(valid_ref, pairs_ref.at[me], valid_send.at[k], valid_recv.at[k], home)
        for k, home in enumerate(homes)
    ]
    mask_own = pltpu.make_async_copy(valid_ref, pairs_ref.at[me], valid_send.at[31])

    for deal in deals:
        deal.send_head()
        deal.start_fetch()
        deal.vectors(False)
    for deal in deals:
        deal.whole(True, False)
    pair.start()
    for deal in deals:
        deal.join()

    def lift_to(kind, p, ref, start):
        slots = (img_slots, txt_slots)[kind.index]
        for c, value in lift(kind, plans[kind.index], p, slots, flat):
            lane = start + c * LANES
            ref[: value.shape[0], lane : lane + LANES] = value.astype(ref.dtype)

    def normalise(kind, half):
        width, room = kind.width, kind.room
        own, arrived = ((img_own, img_in), (txt_own, txt_in))[kind.index]
        ref = own if half == kind.index else arrived
        gain, shift = vector(vec_ref, kind, 0), vector(vec_ref, kind, 1)
        positions = lax.broadcasted_iota(jnp.int32, (room, 1), 0)
        for i in range(8):
            rows = ref[i].astype(WIDE)
            hat, _ = standardise(rows)
            first = (hat * gain + shift).astype(LOW)
            s = half * 8 + i
            first_ref[s, :room, :width] = first
            if kind.causal:
                chosen = positions == ends_ref[(half * 16 + at) * 8 + i]
                top = jnp.sum(jnp.where(chosen, first.astype(WIDE), 0.0), axis=0, keepdims=True)
                raw = jnp.sum(jnp.where(chosen, rows, 0.0), axis=0, keepdims=True)
            else:
                top, raw = first[:1].astype(WIDE), rows[:1]
            top_scr[s : s + 1, :width] = top
            at_scr[s : s + 1, :width] = raw

    def begin(kind):
        deal = deals[kind.index]
        deal.arrived(VECTORS)
        lift_to(kind, VECTORS, vec_ref, 0)
        normalise(kind, kind.index)

    each_tower(begin)

    def place_inputs(kind):
        deals[kind.index].arrived(0)
        slots = (img_slots, txt_slots)[kind.index]
        per = kind.width // LANES
        for c, value in lift(kind, plans[kind.index], 0, slots, flat):
            lane = c // per * WIDTH + c % per * LANES
            ref = ask_block
            if lane >= 2 * WIDTH:
                ref, lane = mix_block, lane - 2 * WIDTH
            ref[: value.shape[0], lane : lane + LANES] = value.astype(LOW)

    each_tower(place_inputs)
    ask.start()

    def place_rest(kind):
        deals[kind.index].arrived(1)
        lift_to(kind, 1, mix_block, WIDTH)
        deals[kind.index].arrived(4)
        lift_to(kind, 4, emb_block, 0)

    each_tower(place_rest)
    mix.start()
    embed.start()
    for deal in deals:
        deal.whole(False, False)
    pair.finish()
    each_tower(lambda kind: normalise(kind, 1 - kind.index))
    for copy in masks:
        copy.start()
    mask_own.start()
    ask.relay_deep()
    ask.relay_row()
    ask.finish()

    def question(kind):
        width = kind.width
        tops = top_scr[:, :width].astype(LOW)
        query = dot_nn(tops, matrix(ask_ref, kind, 0, width)) + vector(vec_ref, kind, 2)
        query = query.astype(LOW)
        query_ref[:, :width] = query
        for span in spans(kind):
            lo, hi, first_head, n = span
            put_rows(
                keyed_ref,
                pl.ds(first_head * SEQS, n * SEQS),
                dot_nt(head_rows(query, span), matrix(ask_ref, kind, WIDTH + lo, hi - lo)) * 0.125,
            )
        dead = (HEADS - kind.heads) * SEQS
        put_rows(keyed_ref, pl.ds(kind.heads * SEQS, dead), jnp.zeros((dead, width), WIDE))

    each_tower(question)
    mix.relay_deep()
    embed.relay_deep()

    def score(kind):
        width, room = kind.width, kind.room
        lane = lax.broadcasted_iota(jnp.int32, (HEADS, room), 1)
        for s in range(SEQS):
            keys = get_rows(keyed_ref, pl.ds(s, HEADS, stride=SEQS), width).astype(LOW)
            scores = dot_nt(keys, first_ref[s, :room, :width])
            if kind.causal:
                allowed = lane <= ends_ref[(s // 8 * 16 + at) * 8 + s % 8]
            else:
                allowed = lane < kind.length
            score_scr[s * HEADS : (s + 1) * HEADS, :room] = jnp.where(allowed, scores, -1e30)
        scores = score_scr[:, :room]
        raw = jnp.exp(scores - jnp.max(scores, axis=-1, keepdims=True))
        weights = raw / jnp.sum(raw, axis=-1, keepdims=True)
        head = lax.broadcasted_iota(jnp.int32, (SEQS * HEADS, 1), 0) % HEADS
        weights = jnp.where(head < kind.heads, weights, 0.0)
        weight_ref[:, :room] = weights
        low_scr[:, :room] = weights.astype(LOW)

    each_tower(score)
    mix.relay_row()
    embed.relay_row()

    def mixture(kind):
        width, room = kind.width, kind.room
        for s in range(SEQS):
            mixed = dot_nn(
                low_scr[s * HEADS : (s + 1) * HEADS, :room], first_ref[s, :room, :width]
            )
            put_rows(mixture_ref, pl.ds(s, HEADS, stride=SEQS), mixed)
        totals = jnp.sum(low_scr[:, :room].astype(WIDE), axis=-1, keepdims=True)
        score_scr[...] = jnp.broadcast_to(totals, score_scr.shape)

    each_tower(mixture)

    def place_hidden(kind):
        deal, plan = deals[kind.index], plans[kind.index]
        slots = (img_slots, txt_slots)[kind.index]
        deal.arrived(2)
        per = kind.part // LANES
        for c, value in lift(kind, plan, 2, slots, flat):
            lane = c % per * LANES
            raise_block[c // per, : kind.block, lane : lane + LANES] = value.astype(LOW)
        deal.arrived(3)
        lift_to(kind, 3, reduce_block, 0)

    each_tower(place_hidden)
    rise.start()
    fall.start()
    fall_own.start()
    mix.finish()

    def answer(kind):
        width = kind.width
        mixed = []
        bias = vector(vec_ref, kind, 3)
        for span in spans(kind):
            lo, hi, first_head, n = span
            z = get_rows(mixture_ref, pl.ds(first_head * SEQS, n * SEQS), width).astype(LOW)
            valued = dot_nn(z, matrix(mix_ref, kind, lo, hi - lo))
            totals = jnp.concatenate(
                [score_scr[pl.ds(first_head + h, SEQS, stride=HEADS), 0:1] for h in range(n)],
                axis=0,
            )
            mixed.append(from_head_rows(valued + totals * bias[:, lo:hi], span))
        mixed = side_by_side(mixed).astype(LOW)
        middle = (
            at_scr[:, :width]
            + dot_nn(mixed, matrix(mix_ref, kind, WIDTH, width))
            + vector(vec_ref, kind, 4)
        )
        middle_ref[:, :width] = middle
        hat, _ = standardise(middle)
        second_ref[:, :width] = (
            hat * vector(vec_ref, kind, 5) + vector(vec_ref, kind, 6)
        ).astype(LOW)
        put_rows(mixture_ref, pl.ds(12 * SEQS, SEQS), top_scr[:, :width])
        put_rows(mixture_ref, pl.ds(13 * SEQS, SEQS), mixed.astype(WIDE))

    each_tower(answer)
    embed.finish()
    rise.finish()
    fall_own.wait()
    remote(
        reduce_block, reduce_ref.at[1 - core], reduce_sems.at[0], reduce_sems.at[1], sibling
    ).wait_recv()
    mask_own.wait()
    for k, home in enumerate(homes):
        source = (me + 31 - k) % 32
        remote(
            valid_ref, pairs_ref.at[source], valid_send.at[k], valid_recv.at[k], home
        ).wait_recv()
    for copy in [*masks, fall]:
        copy.wait_send()
    for group in (pair, ask, mix, embed, rise, *deals):
        group.drain()


def expand_matrix(ref, kind):
    return ref[:, : kind.block, : kind.part].reshape(kind.width, kind.part)


def reduce_matrix(ref, kind):
    return ref[:, : kind.reduce_rows, : kind.width].reshape(kind.part, kind.width)


def hidden_bias(vec_ref, kind):
    chip = lax.axis_index("dp") // 2
    whole = vec_ref[...]
    row = lax.broadcasted_iota(jnp.int32, (16, 1), 0)
    line = jnp.sum(jnp.where(row == 10 + chip // 2, whole, 0.0), axis=0, keepdims=True)
    return jnp.where(
        chip % 2 == 0, line[:, : kind.part], line[:, kind.part : 2 * kind.part]
    )


def hidden_kernel(second_ref, raise_ref, reduce_ref, vec_ref, part_ref, raised_ref):
    def run(kind):
        width = kind.width
        rows = second_ref[:, :, :width].reshape(8 * SEQS, width)
        raised = dot_nn(rows, expand_matrix(raise_ref, kind)) + hidden_bias(vec_ref, kind)
        raised_ref[:, : kind.part] = raised
        active = (raised * jax.nn.sigmoid(1.702 * raised)).astype(LOW)
        part = dot_nn(active, reduce_matrix(reduce_ref, kind))
        part_ref[:, :, :width] = part.reshape(8, SEQS, width).astype(LOW)

    each_tower(run)


def hidden_back_kernel(
    grad_ref,
    second_ref,
    raised_ref,
    raise_ref,
    reduce_ref,
    back_ref,
    raise_grad_ref,
    reduce_keep_ref,
    reduce_send_ref,
    bias_ref,
    whole,
):
    def run(kind):
        width, part = kind.width, kind.part
        grads = grad_ref[:, :, :width].reshape(8 * SEQS, width)
        rows = second_ref[:, :, :width].reshape(8 * SEQS, width)
        raised = raised_ref[:, :part]
        gate = jax.nn.sigmoid(1.702 * raised)
        active = (raised * gate).astype(LOW)
        slope = gate + 1.702 * raised * gate * (1.0 - gate)
        raised_grad = dot_nt(grads, reduce_matrix(reduce_ref, kind)) * slope
        low_grad = raised_grad.astype(LOW)
        bias_ref[0:1, :part] = jnp.sum(low_grad.astype(WIDE), axis=0, keepdims=True)
        back = dot_nt(low_grad, expand_matrix(raise_ref, kind))
        back_ref[:, :, :width] = back.reshape(8, SEQS, width).astype(LOW)
        raise_grad_ref[:, : kind.block, :part] = (
            dot_tn(rows, low_grad).reshape(16, kind.block, part).astype(LOW)
        )
        whole[:part, :width] = dot_tn(active, grads)
        core = lax.axis_index("dp") % 2
        n = kind.reduce_rows
        keep = pl.multiple_of(core * n, 64)
        send = pl.multiple_of((1 - core) * n, 64)
        reduce_keep_ref[:n, :width] = whole[pl.ds(keep, n), :width]
        reduce_send_ref[:n, :width] = whole[pl.ds(send, n), :width].astype(LOW)

    each_tower(run)


def embed_kernel(part_ref, middle_ref, gat_ref, vec_ref, emb_ref, final_ref, pooled_ref, proj_ref):
    def run(kind):
        width = kind.width
        final = (
            middle_ref[:, :width]
            + jnp.sum(part_ref[:, :, :width].astype(WIDE), axis=0)
            + vector(vec_ref, kind, 7)
        )
        final_ref[:, :width] = final
        hat, _ = standardise(final)
        pooled = (hat * vector(vec_ref, kind, 8) + vector(vec_ref, kind, 9)).astype(LOW)
        pooled_ref[:, :width] = pooled
        proj = dot_nn(pooled, matrix(gat_ref, kind, 0, EMB))
        proj_ref[...] = proj
        size = jnp.sum(proj * proj, axis=-1, keepdims=True) + 1e-06
        emb_ref[...] = (proj * lax.rsqrt(size)).astype(LOW)

    each_tower(run)


def objective_kernel(
    scale_ref,
    all_ref,
    valid_ref,
    final_ref,
    proj_ref,
    gat_ref,
    vec_ref,
    low_ref,
    grad_ref,
    proj_grad_ref,
    final_vec_ref,
    loss_ref,
    scale_new_ref,
    own_scr,
):
    def ordered(which):
        blocks = []
        for half in range(2):
            for j in range(16):
                rows = all_ref[j % 2, which * 8 + j // 2].astype(WIDE)
                blocks.append(rows[half * 8 : half * 8 + 8])
        return jnp.concatenate(blocks, axis=0).astype(LOW)

    img, txt = ordered(0), ordered(1)
    total = img.shape[0]
    scale = jnp.exp(jnp.full((1, 1), scale_ref[0], WIDE))
    allowed = valid_ref[...].reshape(total, total) > 0
    same = lax.broadcasted_iota(jnp.int32, (total, total), 0) == lax.broadcasted_iota(
        jnp.int32, (total, total), 1
    )
    same = same.astype(WIDE)

    def side(left, right):
        logits = scale * dot_nt(left, right)
        masked = jnp.where(allowed, logits, -1e30)
        top = jnp.max(masked, axis=1, keepdims=True)
        lse = jnp.log(jnp.sum(jnp.exp(masked - top), axis=1, keepdims=True)) + top
        terms = 0.5 * (jnp.where(allowed, jnp.exp(logits - lse), 0.0) - same)
        loss = 0.5 * (
            jnp.sum(lse, axis=0, keepdims=True)
            - jnp.sum(jnp.sum(logits * same, axis=1, keepdims=True), axis=0, keepdims=True)
        )
        rate = jnp.sum(jnp.sum(terms * logits, axis=1, keepdims=True), axis=0, keepdims=True)
        return (scale * terms).astype(LOW), loss, rate

    row_back, row_loss, row_rate = side(img, txt)
    col_back, col_loss, col_rate = side(txt, img)
    loss_ref[0] = jnp.sum(row_loss + col_loss) / total
    parts = advance(
        scale_ref[0], scale_ref[1], scale_ref[2], jnp.sum(row_rate + col_rate), scale_rate
    )
    for k in range(3):
        scale_new_ref[k] = parts[k]

    def run(kind):
        width = kind.width
        if kind.index == 0:
            emb_grad = dot_nn(row_back, txt) + dot_tn(col_back, txt)
        else:
            emb_grad = dot_nn(col_back, img) + dot_tn(row_back, img)
        own_scr[...] = emb_grad
        at = lax.axis_index("dp")
        mine = jnp.concatenate(
            [
                own_scr[pl.ds(pl.multiple_of(half * 128 + at * 8, 8), 8), :]
                for half in range(2)
            ],
            axis=0,
        )
        proj = proj_ref[...]
        size = jnp.sum(proj * proj, axis=-1, keepdims=True) + 1e-06
        along = jnp.sum(proj * mine, axis=-1, keepdims=True)
        proj_grad = ((mine - proj * along / size) * lax.rsqrt(size)).astype(LOW)
        proj_grad_ref[...] = proj_grad
        pooled_grad = dot_nt(proj_grad, matrix(gat_ref, kind, 0, EMB))
        hat, rate = standardise(final_ref[:, :width])
        final_vec_ref[0:1, :width] = jnp.sum(pooled_grad * hat, axis=0, keepdims=True)
        final_vec_ref[1:2, :width] = jnp.sum(pooled_grad, axis=0, keepdims=True)
        final_grad = norm_back(pooled_grad, vector(vec_ref, kind, 8), hat, rate)
        grad_ref[:, :width] = final_grad
        low = final_grad.astype(LOW)
        low_ref[:, :width] = low
        final_vec_ref[2:3, :width] = jnp.sum(low.astype(WIDE), axis=0, keepdims=True)

    each_tower(run)


def centre_kernel(
    scale_ref,
    second_ref,
    middle_ref,
    emb_weight_ref,
    vec_ref,
    raise_ref,
    reduce_ref,
    valid_ref,
    loss_ref,
    scale_new_ref,
    final_grad_ref,
    pooled_ref,
    proj_grad_ref,
    final_vec_ref,
    raise_grad_ref,
    reduce_keep_ref,
    reduce_send_ref,
    bias_ref,
    backs_ref,
    seconds,
    part,
    parts,
    raised,
    emb,
    embs,
    final,
    proj,
    low,
    lows,
    back,
    own_scr,
    whole,
    send_sems,
    recv_sems,
    spread_send,
    spread_recv,
    core_sems,
):
    tower, at = here()
    greet([*both_towers(tower, at), (tower, at + 1 - at % 2 * 2)])
    sent = []
    sent += group_exchange(False, second_ref, seconds, send_sems.at[0], recv_sems.at[0])
    hidden_kernel(seconds, raise_ref, reduce_ref, vec_ref, part, raised)
    sent += group_exchange(True, part, parts, send_sems.at[1], recv_sems.at[1])
    embed_kernel(parts, middle_ref, emb_weight_ref, vec_ref, emb, final, pooled_ref, proj)
    sent += spread(emb, embs, spread_send, spread_recv, core_sems)
    objective_kernel(
        scale_ref,
        embs,
        valid_ref,
        final,
        proj,
        emb_weight_ref,
        vec_ref,
        low,
        final_grad_ref,
        proj_grad_ref,
        final_vec_ref,
        loss_ref,
        scale_new_ref,
        own_scr,
    )
    sent += group_exchange(False, low, lows, send_sems.at[2], recv_sems.at[2])
    hidden_back_kernel(
        lows,
        seconds,
        raised,
        raise_ref,
        reduce_ref,
        back,
        raise_grad_ref,
        reduce_keep_ref,
        reduce_send_ref,
        bias_ref,
        whole,
    )
    sent += group_exchange(True, back, backs_ref, send_sems.at[3], recv_sems.at[3])
    for copy in sent:
        copy.wait_send()


def back_kernel(
    plans,
    ends_ref,
    img_own,
    img_in,
    txt_own,
    txt_in,
    first_ref,
    ask_ref,
    mix_ref,
    vec_ref,
    backs_ref,
    grad_ref,
    middle_ref,
    query_ref,
    keyed_ref,
    mixture_ref,
    weight_ref,
    pooled_ref,
    proj_grad_ref,
    final_vec_ref,
    bias_ref,
    raise_grad_ref,
    reduce_keep_ref,
    reduce_send_ref,
    img_keep,
    txt_keep,
    img_chunks,
    txt_chunks,
    img_send,
    txt_send,
    img_home,
    txt_home,
    rows_grad,
    middle_scr,
    second_scr,
    valued_scr,
    turn_scr,
    shared_scr,
    slope_scr,
    low_scr,
    left_scr,
    left_block,
    turn_block,
    left_all,
    turn_all,
    early_block,
    early_all,
    late_block,
    late_all,
    lines_block,
    lines_all,
    raise_all,
    reduce_in,
    flat,
    img_slots,
    txt_slots,
    gains,
    top_grad_scr,
    raise_send,
    raise_recv,
    reduce_sems,
    left_send,
    left_recv,
    turn_send,
    turn_recv,
    early_send,
    early_recv,
    late_send,
    late_recv,
    lines_send,
    lines_recv,
    pair_sems,
    collect_send,
    collect_recv,
):
    tower, at = here()
    core = at % 2
    sibling = (tower, at + 1 - 2 * core)
    greet(everyone(tower, at))
    rise = Blocks(raise_grad_ref, raise_all, raise_send, raise_recv)
    fall = remote(reduce_send_ref, reduce_in, reduce_sems.at[0], reduce_sems.at[1], sibling)
    lefts = Blocks(left_block, left_all, left_send, left_recv)
    turns = Blocks(turn_block, turn_all, turn_send, turn_recv)
    early = Ring(early_block, early_all, early_send, early_recv)
    late = Ring(late_block, late_all, late_send, late_recv)
    pair = Pair(img_send, img_home, txt_send, txt_home, pair_sems)
    collects = [
        Collect(plans[0], 0, img_slots, img_chunks, collect_send.at[0], collect_recv),
        Collect(plans[1], 1, txt_slots, txt_chunks, collect_send.at[1], collect_recv),
    ]
    rise.start()
    fall.start()

    def outputs(kind):
        width = kind.width
        second_grad = jnp.sum(backs_ref[:, :, :width].astype(WIDE), axis=0)
        second_scr[:, :width] = second_grad
        hat, rate = standardise(middle_ref[:, :width])
        middle_grad = grad_ref[:, :width] + norm_back(
            second_grad, vector(vec_ref, kind, 5), hat, rate
        )
        middle_scr[:, :width] = middle_grad
        output_grad = middle_grad.astype(LOW)
        mixed_grad = dot_nt(output_grad, matrix(mix_ref, kind, WIDTH, width)).astype(LOW)
        early_block[:, 0:width] = query_ref[:, :width]
        early_block[:, WIDTH : WIDTH + width] = mixed_grad
        early_block[:, 2 * WIDTH : 2 * WIDTH + width] = output_grad
        early_block[:, 3 * WIDTH : 3 * WIDTH + EMB] = proj_grad_ref[...]
        left_scr[:, :width] = get_rows(mixture_ref, slice(None), width)
        left_scr[14 * SEQS : 15 * SEQS, :width] = pooled_ref[:, :width].astype(WIDE)
        left_scr[15 * SEQS :, :width] = jnp.zeros((SEQS, width), WIDE)

    each_tower(outputs)
    early.start()

    def turned(kind):
        width, block = kind.width, kind.block
        left_block[:, :block, :] = left_scr[:, :width].T.reshape(16, block, 256).astype(LOW)

    each_tower(turned)
    lefts.start()

    def values(kind):
        width = kind.width
        mixed_grad = early_block[:, WIDTH : WIDTH + width]
        bias = vector(vec_ref, kind, 3)
        dead = kind.heads * SEQS
        put_rows(valued_scr, pl.ds(dead, 256 - dead), jnp.zeros((256 - dead, width), WIDE))
        shared_scr[dead:, :] = jnp.zeros((256 - dead, LANES), WIDE)
        for span in spans(kind):
            lo, hi, first_head, n = span
            rows = head_rows(mixed_grad, span)
            place = pl.ds(first_head * SEQS, n * SEQS)
            put_rows(valued_scr, place, dot_nt(rows, matrix(mix_ref, kind, lo, hi - lo)))
            constant = jnp.sum(rows.astype(WIDE) * bias[:, lo:hi], axis=-1, keepdims=True)
            shared_scr[place, :] = jnp.broadcast_to(constant, (n * SEQS, LANES))

    each_tower(values)

    def slopes(kind):
        width, room = kind.width, kind.room
        for s in range(SEQS):
            line = pl.ds(s, HEADS, stride=SEQS)
            slope = dot_nt(
                get_rows(valued_scr, line, width).astype(LOW), first_ref[s, :room, :width]
            )
            slope_scr[s * HEADS : (s + 1) * HEADS, :room] = slope + shared_scr[line, 0:1]
        weights = weight_ref[:, :room]
        slope = slope_scr[:, :room]
        slope = weights * (slope - jnp.sum(weights * slope, axis=-1, keepdims=True))
        both = jnp.concatenate(
            [slope.reshape(SEQS, HEADS, room), weights.reshape(SEQS, HEADS, room)], axis=1
        )
        low_scr[:, :room] = both.reshape(2 * SEQS * HEADS, room).astype(LOW)

    each_tower(slopes)
    early.relay_deep()

    def tokens(kind):
        width, room = kind.width, kind.room
        for s in range(SEQS):
            line = pl.ds(s, HEADS, stride=SEQS)
            both = low_scr[2 * s * HEADS : 2 * (s + 1) * HEADS, :room]
            first = first_ref[s, :room, :width]
            put_rows(turn_scr, line, dot_nn(both[:HEADS], first))
            right = jnp.concatenate(
                [get_rows(keyed_ref, line, width), get_rows(valued_scr, line, width)], axis=0
            )
            rows_grad[s, :room, :width] = dot_tn(both, right.astype(LOW))

    each_tower(tokens)
    early.relay_row()

    def queries(kind):
        width, block = kind.width, kind.block
        grads = []
        for span in spans(kind):
            lo, hi, first_head, n = span
            rows = get_rows(turn_scr, pl.ds(first_head * SEQS, n * SEQS), width).astype(LOW)
            back = dot_nn(rows, matrix(ask_ref, kind, WIDTH + lo, hi - lo)) * 0.125
            grads.append(from_head_rows(back, span))
        query_grad = side_by_side(grads).astype(LOW)
        late_block[:, :width] = query_grad
        top_grad_scr[:, :width] = dot_nt(query_grad, matrix(ask_ref, kind, 0, width))
        turn_block[:, :block, :] = (
            get_rows(turn_scr, slice(None), width).T.reshape(16, block, 256).astype(LOW)
        )

    each_tower(queries)
    late.start()
    turns.start()
    gains[...] = jnp.zeros_like(gains)

    def finish(kind, half):
        width, room, length = kind.width, kind.room, kind.length
        own, arrived = ((img_own, img_in), (txt_own, txt_in))[kind.index]
        ref = own if half == kind.index else arrived
        keep, send = ((img_keep, img_send), (txt_keep, txt_send))[kind.index]
        gain = vector(vec_ref, kind, 0)
        positions = lax.broadcasted_iota(jnp.int32, (room, 1), 0)
        gain_sum = jnp.zeros((1, width), WIDE)
        shift_sum = jnp.zeros((1, width), WIDE)
        for i in range(8):
            s = half * 8 + i
            hat, rate = standardise(ref[i].astype(WIDE))
            if kind.causal:
                chosen = positions == ends_ref[(half * 16 + at) * 8 + i]
            else:
                chosen = positions == 0
            chosen = chosen.astype(WIDE)
            grad = rows_grad[s, :room, :width] + chosen * top_grad_scr[s : s + 1, :width]
            gain_sum += jnp.sum(grad * hat, axis=0, keepdims=True)
            shift_sum += jnp.sum(grad, axis=0, keepdims=True)
            result = norm_back(grad, gain, hat, rate) + chosen * middle_scr[s : s + 1, :width]
            if half == kind.index:
                keep[i] = result[:length]
            else:
                send[i] = result.astype(LOW)
        gains[0:1, :width] += gain_sum
        gains[1:2, :width] += shift_sum

    each_tower(lambda kind: finish(kind, 1 - kind.index))
    pair.start()
    rise.finish()
    remote(
        reduce_send_ref, reduce_in, reduce_sems.at[0], reduce_sems.at[1], sibling
    ).wait_recv()

    def slots_of(kind):
        return (img_slots, txt_slots)[kind.index]

    def hidden_grads(kind):
        plan, collect = plans[kind.index], collects[kind.index]
        block, n, per = kind.block, kind.reduce_rows, kind.part // LANES

        def risen(c):
            chip, lane = c // per, c % per * LANES
            return raise_all[2 * chip, :block, lane : lane + LANES].astype(WIDE) + raise_all[
                2 * chip + 1, :block, lane : lane + LANES
            ].astype(WIDE)

        def fallen(c):
            lane = c * LANES
            return reduce_keep_ref[:n, lane : lane + LANES] + reduce_in[
                :n, lane : lane + LANES
            ].astype(WIDE)

        drop(kind, plan, 2, risen, slots_of(kind), flat)
        collect.piece(2, False)
        drop(kind, plan, 3, fallen, slots_of(kind), flat)
        collect.piece(3, False)

    each_tower(hidden_grads)
    late.relay_deep()
    each_tower(lambda kind: finish(kind, kind.index))
    late.relay_row()

    def lines(kind):
        width = kind.width
        hat, _ = standardise(middle_ref[:, :width])
        second_grad = second_scr[:, :width]

        def column_sum(value):
            return jnp.sum(value.astype(WIDE), axis=0, keepdims=True)

        mixed_grad = early_block[:, WIDTH : WIDTH + width].astype(WIDE)
        weights = low_scr[:, : kind.room].astype(WIDE).reshape(SEQS, 2 * HEADS, kind.room)
        totals = jnp.sum(weights[:, HEADS:], axis=-1, keepdims=True).reshape(SEQS * HEADS, 1)
        shared_scr[...] = jnp.broadcast_to(totals, shared_scr.shape)
        value_bias = []
        for lo, hi, first_head, n in spans(kind):
            owner = lax.broadcasted_iota(jnp.int32, (SEQS, hi - lo), 1) // HEAD
            scaled = jnp.zeros((SEQS, hi - lo), WIDE)
            for h in range(n):
                total = shared_scr[pl.ds(first_head + h, SEQS, stride=HEADS), 0:1]
                scaled = jnp.where(owner == h, mixed_grad[:, lo:hi] * total, scaled)
            value_bias.append(column_sum(scaled))
        hidden = bias_ref[0:1, : kind.part]
        parts = [
            gains[0:1, :width],
            gains[1:2, :width],
            column_sum(late_block[:, :width]),
            side_by_side(value_bias),
            column_sum(early_block[:, 2 * WIDTH : 2 * WIDTH + width]),
            column_sum(second_grad * hat),
            column_sum(second_grad),
            final_vec_ref[2:3, :width],
            final_vec_ref[0:1, :width],
            final_vec_ref[1:2, :width],
            jnp.concatenate([hidden, jnp.zeros((1, width - kind.part), WIDE)], axis=1),
            jnp.zeros((5, width), WIDE),
        ]
        lines_block[:, :width] = jnp.concatenate(parts, axis=0)

    each_tower(lines)
    line_copy = remote(
        lines_block, lines_all.at[at], lines_send.at[0], lines_recv.at[at], (tower, jnp.int32(0))
    )
    line_own = pltpu.make_async_copy(lines_block, lines_all.at[at], lines_recv.at[at])
    pl.when(at > 0)(line_copy.start)
    pl.when(at == 0)(line_own.start)

    early.finish()
    lefts.finish()

    def from_early(kind):
        plan, collect = plans[kind.index], collects[kind.index]
        width, block = kind.width, kind.block

        def gathered(k):
            lane = lax.broadcasted_iota(jnp.int32, (block, LANES), 1) // SEQS
            halves = []
            for side in range(2):
                total = jnp.zeros((block, LANES), WIDE)
                for j in range(8):
                    part = left_all[side * 8 + j, :block, LANES:].astype(WIDE)
                    shift = (j * SEQS - (k - 8) * SEQS) % LANES
                    turned_part = pltpu.roll(part, shift, 1) if shift else part
                    total = jnp.where(lane == j, turned_part, total)
                halves.append(total)
            return jnp.concatenate(halves, axis=1).astype(LOW)

        def right(start, wide):
            return early_all[:, :, start : start + wide].reshape(256, wide)

        output = dot_nn(gathered(13), right(2 * WIDTH, width))
        drop(
            kind, plan, 1, lambda c: output[:, c * LANES : (c + 1) * LANES], slots_of(kind), flat
        )
        collect.piece(1, False)
        embed = dot_nn(gathered(14), right(3 * WIDTH, EMB))
        drop(kind, plan, 4, lambda c: embed[:, c * LANES : (c + 1) * LANES], slots_of(kind), flat)
        collect.piece(4, False)
        left_scr[:block, :256] = gathered(12).astype(WIDE)

    each_tower(from_early)
    late.finish()
    turns.finish()

    def from_late(kind):
        plan, collect = plans[kind.index], collects[kind.index]
        width, block = kind.width, kind.block
        ask = dot_nn(left_scr[:block, :256].astype(LOW), late_all[:, :, :width].reshape(256, width))

        def outer(side_ref, start, span):
            lo, hi, first_head, n = span
            lane = first_head * SEQS
            total = jnp.zeros((block, hi - lo), WIDE)
            for j in range(8):
                left, rows = [], []
                for source in (2 * j, 2 * j + 1):
                    left.append(side_ref[source, :block, lane : lane + LANES])
                    rows.append(
                        head_rows(early_all[source, :, start : start + width], span)
                    )
                    if n < 8:
                        rows.append(jnp.zeros(((8 - n) * SEQS, hi - lo), LOW))
                total += dot_nn(
                    jnp.concatenate(left, axis=1), jnp.concatenate(rows, axis=0)
                )
            return total

        keys = side_by_side([outer(turn_all, 0, span) for span in spans(kind)]) * 0.125
        worth = side_by_side([outer(left_all, WIDTH, span) for span in spans(kind)])
        per = width // LANES

        def inputs(c):
            value = (ask, keys, worth)[c // per]
            return value[:, c % per * LANES : (c % per + 1) * LANES]

        drop(kind, plan, 0, inputs, slots_of(kind), flat)
        collect.piece(0, False)

    each_tower(from_late)

    @pl.when(at == 0)
    def _():
        for k in range(1, 16):
            remote(
                lines_block, lines_all.at[k], lines_send.at[0], lines_recv.at[k], sibling
            ).wait_recv()
        line_own.wait()

        def vectors(kind):
            width, part = kind.width, kind.part
            whole = [jnp.sum(lines_all[:, :10, :width], axis=0)]
            for row in range(4):
                pair_of = []
                for chip in (2 * row, 2 * row + 1):
                    pair_of.append(
                        lines_all[2 * chip, 10:11, :part] + lines_all[2 * chip + 1, 10:11, :part]
                    )
                whole.append(jnp.concatenate(pair_of, axis=1))
            whole.append(jnp.zeros((2, width), WIDE))
            result = jnp.concatenate(whole, axis=0)
            drop(
                kind,
                plans[kind.index],
                VECTORS,
                lambda c: result[:, c * LANES : (c + 1) * LANES],
                slots_of(kind),
                flat,
            )

        each_tower(vectors)

    each_tower(lambda kind: collects[kind.index].piece(VECTORS, False))
    pair.finish()

    @pl.when(tower == 1)
    def _():
        img_keep[...] = img_home[:, : TOWERS[0].length].astype(WIDE)

    @pl.when(tower == 0)
    def _():
        txt_keep[...] = txt_home[:, : TOWERS[1].length].astype(WIDE)

    for collect in collects:
        collect.finish()
    fall.wait_send()
    pl.when(at > 0)(line_copy.wait_send)
    for group in (rise, lefts, turns, early, late, pair):
        group.drain()

    def drain(kind):
        for p in range(VECTORS + 1):
            collects[kind.index].piece(p, True)

    each_tower(drain)


def dma(*shape):
    return pltpu.SemaphoreType.DMA(shape)


def call(kernel, number, operands, outs, scratch, semaphores):
    spec = {"vmem": pltpu.VMEM, "smem": pltpu.SMEM, "any": pl.ANY}
    return pl.pallas_call(
        kernel,
        out_shape=[jax.ShapeDtypeStruct(shape, dtype) for _, shape, dtype in outs],
        in_specs=[pl.BlockSpec(memory_space=spec[place]) for place, _ in operands],
        out_specs=[pl.BlockSpec(memory_space=spec[place]) for place, _, _ in outs],
        scratch_shapes=[pltpu.VMEM(shape, dtype) for shape, dtype in scratch] + semaphores,
        compiler_params=comm_params(number),
    )(*[value for _, value in operands])


ROWS_LOW = ((SEQS, WIDTH), LOW)
ROWS_WIDE = ((SEQS, WIDTH), WIDE)
HEAD_ROWS = ((WIDTH // LANES, SEQS * HEADS, LANES), WIDE)
LANE_ROWS = ((SEQS * HEADS, LANES), WIDE)
GROUP = ((8, SEQS, WIDTH), LOW)


def chunk_shapes(plan, n):
    return ((n, plan.rows, LANES), LOW)


def front(txt_ends, img_chunks, txt_chunks, valid, img_rows, txt_rows, plans, number):
    operands = [
        ("smem", txt_ends),
        ("any", img_chunks),
        ("any", txt_chunks),
        ("vmem", valid),
        ("vmem", img_rows),
        ("vmem", txt_rows),
    ]
    outs = [
        ROWS_LOW,
        ROWS_WIDE,
        ROWS_LOW,
        HEAD_ROWS,
        HEAD_ROWS,
        LANE_ROWS,
        ((SEQS, ROOM, WIDTH), LOW),
        (img_rows.shape, LOW),
        (txt_rows.shape, LOW),
        ((16, 48, 2 * WIDTH), LOW),
        ((16, 48, 2 * WIDTH), LOW),
        ((16, 48, EMB), LOW),
        ROWS_WIDE,
        ((16, 48, PART), LOW),
        ((2, 192, WIDTH), LOW),
        ((32, *valid.shape), valid.dtype),
    ]
    chunks = [chunk_shapes(plan, 1) for plan in plans]
    edges = [(shape[1:], dtype) for shape, dtype in chunks]
    scratch = [
        *[chunk_shapes(plan, plan.slots) for plan in plans],
        *edges,
        *edges,
        ((plans[0].slots * plans[0].rows, LANES), WIDE),
        ((48, 2 * WIDTH), LOW),
        ((48, 2 * WIDTH), LOW),
        ((48, EMB), LOW),
        ((8, 48, PART), LOW),
        ((192, WIDTH), LOW),
        ROWS_WIDE,
        ROWS_WIDE,
        LANE_ROWS,
        ((SEQS * HEADS, LANES), LOW),
    ]
    most = max(plan.local for plan in plans) + 17
    semaphores = [
        dma(2, most),
        dma(2, 6),
        dma(2, 2),
        dma(2),
        *[dma(16), dma(15)] * 4,
        dma(3),
        dma(2),
        dma(32),
        dma(31),
    ]
    return call(
        functools.partial(front_kernel, plans),
        number,
        operands,
        [("vmem", *out) for out in outs],
        scratch,
        semaphores,
    )


def centre(scale_state, second, middle, emb_weight, vec, rise, fall, pairs, number):
    operands = [("smem", scale_state)] + [
        ("vmem", value) for value in (second, middle, emb_weight, vec, rise, fall, pairs)
    ]
    outs = [
        ROWS_WIDE,
        ROWS_LOW,
        ((SEQS, EMB), LOW),
        ((8, WIDTH), WIDE),
        ((16, 48, PART), LOW),
        ((192, WIDTH), WIDE),
        ((192, WIDTH), LOW),
        ((8, PART), WIDE),
        GROUP,
    ]
    scratch = [
        GROUP,
        GROUP,
        GROUP,
        ((128, PART), WIDE),
        ((SEQS, EMB), LOW),
        ((2, 16, SEQS, EMB), LOW),
        ROWS_WIDE,
        ((SEQS, EMB), WIDE),
        ROWS_LOW,
        GROUP,
        GROUP,
        ((256, EMB), WIDE),
        ((PART, WIDTH), WIDE),
    ]
    return call(
        centre_kernel,
        number,
        operands,
        [("smem", (1,), WIDE), ("smem", (3,), WIDE)] + [("vmem", *out) for out in outs],
        scratch,
        [dma(4, 8), dma(4, 7), dma(16), dma(15), dma(2)],
    )


def back(txt_ends, values, plans, number):
    operands = [("smem", txt_ends)] + [("vmem", value) for value in values]
    rooms = [((8, kind.room, kind.width), LOW) for kind in TOWERS]
    outs = [((8, kind.length, kind.width), WIDE) for kind in TOWERS] + [
        chunk_shapes(plan, plan.local) for plan in plans
    ]
    blocks = ((16, 48, 256), LOW)
    scratch = [
        *rooms,
        *rooms,
        ((SEQS, ROOM, WIDTH), WIDE),
        ROWS_WIDE,
        ROWS_WIDE,
        HEAD_ROWS,
        HEAD_ROWS,
        LANE_ROWS,
        LANE_ROWS,
        ((2 * SEQS * HEADS, LANES), LOW),
        ((SEQS * HEADS, WIDTH), WIDE),
        blocks,
        blocks,
        blocks,
        blocks,
        ((SEQS, 3 * WIDTH + EMB), LOW),
        ((16, SEQS, 3 * WIDTH + EMB), LOW),
        ROWS_LOW,
        ((16, SEQS, WIDTH), LOW),
        ROWS_WIDE,
        ((16, SEQS, WIDTH), WIDE),
        ((16, 48, PART), LOW),
        ((192, WIDTH), LOW),
        ((plans[0].slots * plans[0].rows, LANES), WIDE),
        *[chunk_shapes(plan, plan.slots) for plan in plans],
        ((8, WIDTH), WIDE),
        ROWS_WIDE,
    ]
    most = max(plan.slots for plan in plans)
    semaphores = [
        dma(16),
        dma(15),
        dma(2),
        *[dma(16), dma(15)] * 4,
        dma(1),
        dma(16),
        dma(2),
        dma(2, 2, most),
        dma(2),
    ]
    return call(
        functools.partial(back_kernel, plans),
        number,
        operands,
        [("vmem", *out) for out in outs],
        scratch,
        semaphores,
    )


def to_chunks(flat, plan, me):
    start = me * plan.share % plan.chunk
    padded = jnp.pad(flat, (plan.chunk, plan.local * plan.chunk - plan.share))
    piece = lax.dynamic_slice(padded, (plan.chunk - start,), (plan.local * plan.chunk,))
    return piece.astype(LOW).reshape(plan.local, plan.rows, LANES)


def from_chunks(chunks, plan, me):
    start = me * plan.share % plan.chunk
    return lax.dynamic_slice(chunks.reshape(-1), (start,), (plan.share,)).astype(WIDE)


def step(
    img_tokens,
    txt_tokens,
    txt_ends,
    valid,
    img_master,
    img_moment,
    img_average,
    txt_master,
    txt_moment,
    txt_average,
    scale_state,
):
    me = lax.axis_index(("tower", "dp"))
    plans = (
        Plan(0, img_master.shape[0], 96, (9, 3, 12, 12, 2)),
        Plan(1, txt_master.shape[0], 64, (6, 2, 8, 8, 2)),
    )
    img_rows = jnp.pad(img_tokens, ((0, 0), (0, TOWERS[0].room - TOWERS[0].length), (0, 0)))
    txt_rows = jnp.pad(txt_tokens, ((0, 0), (0, TOWERS[1].room - TOWERS[1].length), (0, 0)))
    (
        second,
        middle,
        query,
        keyed,
        mixture,
        weights,
        first,
        img_in,
        txt_in,
        ask,
        mix,
        emb_weight,
        vec,
        rise,
        fall,
        pairs,
    ) = front(
        txt_ends,
        to_chunks(img_master, plans[0], me),
        to_chunks(txt_master, plans[1], me),
        valid,
        img_rows,
        txt_rows,
        plans,
        0,
    )
    (
        loss,
        scale_new,
        final_grad,
        pooled,
        proj_grad,
        final_vec,
        rise_grad,
        fall_keep,
        fall_send,
        bias_grad,
        backs,
    ) = centre(scale_state, second, middle, emb_weight, vec, rise, fall, pairs, 1)
    img_grad, txt_grad, img_chunks, txt_chunks = back(
        txt_ends,
        [
            img_rows,
            img_in,
            txt_rows,
            txt_in,
            first,
            ask,
            mix,
            vec,
            backs,
            final_grad,
            middle,
            query,
            keyed,
            mixture,
            weights,
            pooled,
            proj_grad,
            final_vec,
            bias_grad,
            rise_grad,
            fall_keep,
            fall_send,
        ],
        plans,
        2,
    )
    img_new = advance(
        img_master, img_moment, img_average, from_chunks(img_chunks, plans[0], me), step_rate
    )
    txt_new = advance(
        txt_master, txt_moment, txt_average, from_chunks(txt_chunks, plans[1], me), step_rate
    )
    return (
        loss[0],
        img_grad,
        txt_grad,
        img_new[0],
        img_new[1],
        img_new[2],
        img_new[0].astype(LOW),
        txt_new[0],
        txt_new[1],
        txt_new[2],
        txt_new[0].astype(LOW),
        scale_new,
    )


def from_partner(value, axis, stride):
    mask = 2**stride
    pairs = [(source, source ^ mask) for source in range(lax.axis_size(axis))]
    return lax.ppermute(value, axis, pairs)


def round_value(v):
    return lax.optimization_barrier(v.astype(jnp.bfloat16)).astype(jnp.float32)


def make_low():

    def value_keep(v):
        return (round_value(v), None)

    def grad_pass(kept, grad):
        return (grad,)

    rounded = jax.custom_vjp(round_value)
    rounded.defvjp(value_keep, grad_pass)
    return rounded


def low(v):
    return make_low()(v)


def make_low_back():

    def identity(v):
        return v

    def value_pass(v):
        return (v, None)

    def grad_round(kept, grad):
        return (round_value(grad),)

    passed = jax.custom_vjp(identity)
    passed.defvjp(value_pass, grad_round)
    return passed


def low_back(v):
    return make_low_back()(v)


def both_ways(value):
    return low(low_back(value))


def product(left, right):
    return jnp.matmul(left, right)


def contract(form, left, right):
    return jnp.einsum(form, left, right)


def layer_norm(values, gain_row, shift_row):
    centred = values - jnp.mean(values, axis=-1, keepdims=True)
    spread = jnp.mean(centred * centred, axis=-1, keepdims=True)
    return centred * lax.rsqrt(spread + 1e-05) * gain_row + shift_row


def unpack(flat_weights, model_width, hidden_width, embed_width):
    piece_shapes = [
        (model_width, 3 * model_width),
        (model_width, model_width),
        (model_width, hidden_width),
        (hidden_width, model_width),
        (model_width, embed_width),
        (10, model_width),
        (hidden_width,),
    ]
    pieces = []
    offset = 0
    for piece_shape in piece_shapes:
        length = math.prod(piece_shape)
        pieces.append(flat_weights[offset : offset + length].reshape(piece_shape))
        offset = offset + length
    return pieces


def encode(tokens, flat_weights, positions, causal, model_width, hidden_width, embed_width):
    w_inputs, w_output, w_expand, w_reduce, w_embed, vectors, expand_bias = unpack(
        flat_weights, model_width, hidden_width, embed_width
    )
    groups = tokens.shape[0]
    length = tokens.shape[1]
    first = low(layer_norm(tokens, vectors[0], vectors[1]))
    bias_in = jnp.concatenate([vectors[2], jnp.zeros_like(vectors[2]), vectors[3]])
    joined = both_ways(product(first, w_inputs) + bias_in)
    joined = joined.reshape(groups, length, 3, model_width // HEAD, HEAD)
    scores = low_back(contract("gqhd,gkhd->ghqk", joined[:, :, 0], joined[:, :, 1]) * 0.125)
    if causal:
        row_index = lax.broadcasted_iota(jnp.int32, (length, length), 0)
        col_index = lax.broadcasted_iota(jnp.int32, (length, length), 1)
        scores = jnp.where(col_index <= row_index, scores, -1e30)
    row_top = jnp.max(scores, axis=-1, keepdims=True)
    raw_weights = jnp.exp(scores - row_top)
    attention = low(raw_weights / jnp.sum(raw_weights, axis=-1, keepdims=True))
    mixed_heads = both_ways(
        contract("ghqk,gkhd->gqhd", attention, joined[:, :, 2]).reshape(groups, length, model_width)
    )
    middle = tokens + low_back(product(mixed_heads, w_output) + vectors[4])
    second = low(layer_norm(middle, vectors[5], vectors[6]))
    raised = low_back(product(second, w_expand) + expand_bias)
    active = low(raised * jax.nn.sigmoid(1.702 * raised))
    final_rows = middle + low_back(product(active, w_reduce) + vectors[7])
    pooled = jnp.take_along_axis(final_rows, positions[:, None, None], axis=1)[:, 0]
    pooled = low(layer_norm(pooled, vectors[8], vectors[9]))
    projected = low_back(product(pooled, w_embed))
    return low(
        projected * lax.rsqrt(jnp.sum(projected * projected, axis=-1, keepdims=True) + 1e-06)
    )


def inner(left, right):
    return lax.dot_general(
        left, right, (((1,), (1,)), ((), ())), preferred_element_type=jnp.float32
    )


def across(left, right):
    return lax.dot_general(
        left, right, (((0,), (0,)), ((), ())), preferred_element_type=jnp.float32
    )


def softmax_total(logits, allowed):
    masked = jnp.where(allowed, logits, -1e30)
    row_top = jnp.max(masked, axis=1, keepdims=True)
    return jnp.log(jnp.sum(jnp.exp(masked - row_top), axis=1)) + row_top[:, 0]


def advance(master, moment, average, grads, rate):
    moment_new = momentum_rate * moment + grads
    master_new = master - rate * (grads + momentum_rate * moment_new)
    average_new = average_rate * average + (1.0 - average_rate) * master_new
    return (master_new, moment_new, average_new)


def padded_to(flat, length):
    return jnp.pad(flat, (0, length - flat.shape[0]))


def body(
    img_tokens,
    txt_tokens,
    txt_ends,
    valid,
    img_master,
    img_moment,
    img_average,
    txt_master,
    txt_moment,
    txt_average,
    scale_state,
):
    batch_rows = img_tokens.shape[0]
    total_rows = batch_rows * lax.axis_size(("tower", "dp"))
    device_at = lax.axis_index(("tower", "dp"))
    tower_at = lax.axis_index("tower")
    is_image = tower_at == 0
    img_share = img_master.shape[0]
    txt_share = txt_master.shape[0]
    img_count = img_tokens.size
    txt_count = txt_tokens.size
    shard_room = max(img_share, txt_share)
    token_room = max(img_count, txt_count)
    tower_count = lax.axis_size("dp")
    dp_at = lax.axis_index("dp")
    img_low = padded_to(img_master.astype(jnp.bfloat16), shard_room)
    txt_low = padded_to(txt_master.astype(jnp.bfloat16), shard_room)
    token_out = jnp.where(
        is_image,
        padded_to(txt_tokens.reshape(-1), token_room),
        padded_to(img_tokens.reshape(-1), token_room),
    )
    weight_out = jnp.where(is_image, txt_low, img_low)
    weight_mine = jnp.where(is_image, img_low, txt_low)
    token_in, weight_in = from_partner((token_out, weight_out), "tower", 0)
    stacked = jnp.where(
        is_image, jnp.stack([weight_mine, weight_in]), jnp.stack([weight_in, weight_mine])
    )
    gathered = lax.all_gather(stacked, "dp", axis=1, tiled=True)
    pair_ends = jnp.concatenate(
        [
            lax.dynamic_slice_in_dim(txt_ends, dp_at * batch_rows, batch_rows),
            lax.dynamic_slice_in_dim(txt_ends, (tower_count + dp_at) * batch_rows, batch_rows),
        ]
    )
    pair_zero = jnp.zeros((2 * batch_rows,), jnp.int32)

    def image_weights(whole):
        return whole.reshape(2, tower_count, shard_room).reshape(-1).astype(jnp.float32)

    def text_weights(whole):
        return (
            whole.reshape(2, tower_count, shard_room)[:, :, :txt_share]
            .reshape(-1)
            .astype(jnp.float32)
        )

    def image_rows(arrived):
        return jnp.concatenate(
            [img_tokens, arrived[:img_count].reshape(img_tokens.shape)], axis=0
        ).astype(jnp.float32)

    def text_rows(arrived):
        return jnp.concatenate([arrived.reshape(txt_tokens.shape), txt_tokens], axis=0).astype(
            jnp.float32
        )

    def image_encode(rows, flat):
        return encode(rows, flat, pair_zero, False, D_IMG, FF_IMG, EMB)

    def text_encode(rows, flat):
        return encode(rows, flat, pair_ends, True, D_TXT, FF_TXT, EMB)

    def image_forward(operands):
        return image_encode(image_rows(operands[1]), image_weights(operands[0]))

    def text_forward(operands):
        return text_encode(text_rows(operands[1]), text_weights(operands[0]))

    pair_emb = lax.cond(is_image, image_forward, text_forward, (gathered, token_in)).astype(
        jnp.bfloat16
    )
    emb_in = from_partner(pair_emb, "tower", 0)
    img_pair = jnp.where(is_image, pair_emb, emb_in)
    txt_pair = jnp.where(is_image, emb_in, pair_emb)
    row_start = tower_at * batch_rows
    img_local = lax.dynamic_slice_in_dim(img_pair, row_start, batch_rows)
    txt_local = lax.dynamic_slice_in_dim(txt_pair, row_start, batch_rows)
    img_all, txt_all = (
        lax.all_gather(img_local, ("tower", "dp"), axis=0, tiled=True),
        lax.all_gather(txt_local, ("tower", "dp"), axis=0, tiled=True),
    )
    logit_scale = jnp.exp(scale_state[0])
    offset = device_at * batch_rows
    row_index = lax.broadcasted_iota(jnp.int32, (batch_rows, total_rows), 0) + offset
    col_index = lax.broadcasted_iota(jnp.int32, (batch_rows, total_rows), 1)
    diagonal = (row_index == col_index).astype(jnp.float32)
    allowed = valid > 0
    row_logits = logit_scale * inner(img_local, txt_all)
    col_logits = logit_scale * inner(txt_local, img_all)
    row_lse = softmax_total(row_logits, allowed)
    col_lse = softmax_total(col_logits, allowed)
    partial_loss = 0.5 * (
        jnp.sum(row_lse)
        - jnp.sum(row_logits * diagonal)
        + jnp.sum(col_lse)
        - jnp.sum(col_logits * diagonal)
    )
    row_terms = 0.5 * (jnp.where(allowed, jnp.exp(row_logits - row_lse[:, None]), 0.0) - diagonal)
    col_terms = 0.5 * (jnp.where(allowed, jnp.exp(col_logits - col_lse[:, None]), 0.0) - diagonal)
    partial_scale = jnp.sum(row_terms * row_logits) + jnp.sum(col_terms * col_logits)
    row_back = (logit_scale * row_terms).astype(jnp.bfloat16)
    col_back = (logit_scale * col_terms).astype(jnp.bfloat16)
    img_emb_grad = jnp.dot(row_back, txt_all, preferred_element_type=jnp.float32)
    txt_emb_grad = jnp.dot(col_back, img_all, preferred_element_type=jnp.float32)
    img_extra, txt_extra = (
        lax.psum_scatter(
            across(col_back, txt_local), ("tower", "dp"), scatter_dimension=0, tiled=True
        ),
        lax.psum_scatter(
            across(row_back, img_local), ("tower", "dp"), scatter_dimension=0, tiled=True
        ),
    )
    img_emb_grad = img_emb_grad + img_extra
    txt_emb_grad = txt_emb_grad + txt_extra
    sums = lax.psum((partial_loss, partial_scale), ("tower", "dp"))
    grad_out = jnp.where(is_image, txt_emb_grad, img_emb_grad)
    grad_in = from_partner(grad_out, "tower", 0)
    pair_cot = jnp.where(
        is_image,
        jnp.concatenate([img_emb_grad, grad_in], axis=0),
        jnp.concatenate([grad_in, txt_emb_grad], axis=0),
    )

    def image_backward(operands):
        recomputed, tower_pullback = jax.vjp(
            image_encode, image_rows(operands[1]), image_weights(operands[0])
        )
        rows_grad, flat_grad = tower_pullback(operands[2])
        own_part = padded_to(rows_grad[:batch_rows].reshape(-1), token_room)
        sent_part = padded_to(rows_grad[batch_rows:].reshape(-1), token_room)
        stacked_grad = flat_grad.reshape(2, tower_count, img_share)
        return (own_part, sent_part, stacked_grad)

    def text_backward(operands):
        recomputed, tower_pullback = jax.vjp(
            text_encode, text_rows(operands[1]), text_weights(operands[0])
        )
        rows_grad, flat_grad = tower_pullback(operands[2])
        own_part = padded_to(rows_grad[batch_rows:].reshape(-1), token_room)
        sent_part = padded_to(rows_grad[:batch_rows].reshape(-1), token_room)
        stacked_grad = jnp.pad(
            flat_grad.reshape(2, tower_count, txt_share),
            ((0, 0), (0, 0), (0, shard_room - txt_share)),
        )
        return (own_part, sent_part, stacked_grad)

    own_part, sent_part, stacked_grad = lax.cond(
        is_image, image_backward, text_backward, (gathered, token_in, pair_cot)
    )
    summed = lax.psum_scatter(stacked_grad, "dp", scatter_dimension=1, tiled=True)
    kept_part = jnp.where(is_image, summed[0, 0], summed[1, 0])
    sent_share = jnp.where(is_image, summed[1, 0], summed[0, 0])
    home_weights, home_tokens = (
        from_partner(sent_share.astype(jnp.bfloat16), "tower", 0).astype(sent_share.dtype),
        from_partner(sent_part.astype(jnp.bfloat16), "tower", 0).astype(sent_part.dtype),
    )
    img_owned = jnp.where(is_image, kept_part, home_weights)
    txt_owned = jnp.where(is_image, home_weights, kept_part)[:txt_share]
    img_grad = jnp.where(is_image, own_part, home_tokens)[:img_count].reshape(img_tokens.shape)
    txt_grad = jnp.where(is_image, home_tokens, own_part).reshape(txt_tokens.shape)
    img_new = advance(img_master, img_moment, img_average, img_owned, step_rate)
    txt_new = advance(txt_master, txt_moment, txt_average, txt_owned, step_rate)
    scale_parts = advance(scale_state[0], scale_state[1], scale_state[2], sums[1], scale_rate)
    scale_new = jnp.stack([scale_parts[0], scale_parts[1], scale_parts[2]])
    return (
        sums[0] / total_rows,
        img_grad,
        txt_grad,
        img_new[0],
        img_new[1],
        img_new[2],
        img_new[0].astype(jnp.bfloat16),
        txt_new[0],
        txt_new[1],
        txt_new[2],
        txt_new[0].astype(jnp.bfloat16),
        scale_new,
    )


def solution(mesh):
    in_specs = (
        P(("tower", "dp"), None, None),
        P(("tower", "dp"), None, None),
        P(),
        P(("tower", "dp"), None),
        P(("tower", "dp")),
        P(("tower", "dp")),
        P(("tower", "dp")),
        P(("tower", "dp")),
        P(("tower", "dp")),
        P(("tower", "dp")),
        P(),
    )
    out_specs = (
        P(),
        P(("tower", "dp"), None, None),
        P(("tower", "dp"), None, None),
        P(("tower", "dp")),
        P(("tower", "dp")),
        P(("tower", "dp")),
        P(("tower", "dp")),
        P(("tower", "dp")),
        P(("tower", "dp")),
        P(("tower", "dp")),
        P(("tower", "dp")),
        P(),
    )
    run = step if (mesh.shape["tower"], mesh.shape["dp"]) == (2, 16) else body
    return jax.shard_map(run, mesh=mesh, in_specs=in_specs, out_specs=out_specs, check_vma=False)
```

```python
import functools
import math

import jax
import jax.numpy as jnp
from jax import lax
from jax.experimental import pallas as pl
from jax.experimental.pallas import tpu as pltpu
from jax.sharding import PartitionSpec as P

D_IMG = 768
FF_IMG = 3072
D_TXT = 512
FF_TXT = 2048
EMB = 512
HEAD = 64


momentum_rate = 0.5
average_rate = 0.5
step_rate = 0.08
scale_rate = 0.0001


MESH = pl.DeviceIdType.MESH
ANY = pl.BlockSpec(memory_space=pl.ANY)
GRANT = 58 * 1024 * 1024
LANES = 128
LOW = jnp.bfloat16
WIDE = jnp.float32


def here():
    return lax.axis_index("tower"), lax.axis_index("dp")


def greet(devices):
    barrier = pltpu.get_barrier_semaphore()
    for device in devices:
        pl.semaphore_signal(barrier, inc=1, device_id=device, device_id_type=MESH)
    pl.semaphore_wait(barrier, len(devices))


def remote(src, dst, send_sem, recv_sem, device):
    return pltpu.make_async_remote_copy(
        src_ref=src,
        dst_ref=dst,
        send_sem=send_sem,
        recv_sem=recv_sem,
        device_id=device,
        device_id_type=MESH,
    )


def comm_params(number):
    return pltpu.CompilerParams(
        collective_id=number, has_side_effects=True, vmem_limit_bytes=GRANT
    )


def same_core(tower, at):
    chip, core = at // 2, at % 2
    return [(tower, (chip + k) % 8 * 2 + core) for k in range(1, 8)]


def both_towers(tower, at):
    place, core = tower * 8 + at // 2, at % 2
    others = [(place + k) % 16 for k in range(1, 16)]
    return [(other // 8, other % 8 * 2 + core) for other in others]


def everyone(tower, at):
    me = tower * 16 + at
    others = [(me + k) % 32 for k in range(1, 32)]
    return [(other // 16, other % 16) for other in others]


def group_exchange(scattered, x_ref, o_ref, send_sem, recv_sem):
    tower, at = here()
    chip = at // 2

    def source(k):
        return x_ref.at[k] if scattered else x_ref

    own = pltpu.make_async_copy(source(chip), o_ref.at[chip], send_sem.at[7])
    sent = []
    for k, device in enumerate(same_core(tower, at)):
        copy = remote(
            source((chip + 1 + k) % 8), o_ref.at[chip], send_sem.at[k], recv_sem.at[k], device
        )
        copy.start()
        sent.append(copy)
    own.start()
    own.wait()
    for k in range(7):
        remote(
            source(chip),
            o_ref.at[(chip + 7 - k) % 8],
            send_sem.at[k],
            recv_sem.at[k],
            (tower, at),
        ).wait_recv()
    return sent


class Spread:
    def __init__(self, src, dst, send, recv):
        self.src, self.dst, self.send, self.recv = src, dst, send, recv
        tower, at = here()
        self.core = at % 2
        self.sibling = (tower, at + 1 - 2 * self.core)
        self.devices = self.peers(tower, at)
        self.n = len(self.devices) + 1
        self.place = self.spot(tower, at)
        self.sent = []

    def peers(self, tower, at):
        return both_towers(tower, at)

    def spot(self, tower, at):
        return tower * 8 + at // 2

    def block(self, place):
        return self.src

    def side(self, core):
        return self.dst.at[core]

    def launch(self, src, dst, k, device):
        copy = remote(src, dst, self.send.at[k], self.recv.at[k], device)
        copy.start()
        self.sent.append(copy)

    def start(self):
        for k, device in enumerate(self.devices):
            to = (self.place + 1 + k) % self.n
            self.launch(self.block(to), self.side(self.core).at[self.place], k, device)
        self.own = pltpu.make_async_copy(
            self.block(self.place), self.side(self.core).at[self.place], self.send.at[self.n]
        )
        self.own.start()

    def arrived(self):
        for k in range(self.n - 1):
            source = (self.place + self.n - 1 - k) % self.n
            remote(
                self.block(0),
                self.side(self.core).at[source],
                self.send.at[k],
                self.recv.at[k],
                self.sibling,
            ).wait_recv()
        self.own.wait()

    def relay(self):
        self.arrived()
        side = self.side(self.core)
        self.launch(side, side, self.n - 1, self.sibling)

    def finish(self):
        side = self.side(1 - self.core)
        remote(
            side, side, self.send.at[self.n - 1], self.recv.at[self.n - 1], self.sibling
        ).wait_recv()

    def drain(self):
        for copy in self.sent:
            copy.wait_send()


class Group(Spread):
    def __init__(self, src, dst, send, recv, both=True):
        self.both = both
        super().__init__(src, dst, send, recv)

    def peers(self, tower, at):
        return same_core(tower, at)

    def spot(self, tower, at):
        return at // 2

    def block(self, place):
        return self.src.at[place]

    def side(self, core):
        return self.dst.at[core] if self.both else self.dst

    def finish(self):
        if self.both:
            super().finish()
        else:
            self.arrived()


class Ring:
    def __init__(self, src, dst, send, recv):
        self.src, self.dst, self.send, self.recv = src, dst, send, recv
        self.tower, self.at = here()
        self.deep, self.row, self.core = self.at // 4, self.at // 2 % 2, self.at % 2
        self.sibling = (self.tower, self.at + 1 - 2 * self.core)
        self.beside = (self.tower, self.spot(0, 1 - self.row))
        self.sent = []

    def spot(self, k, row):
        return (self.deep + k) % 4 * 4 + row * 2 + self.core

    def launch(self, src, slot, index, device):
        copy = remote(src, self.dst.at[slot], self.send.at[index], self.recv.at[index], device)
        copy.start()
        self.sent.append(copy)

    def arrived(self, slot, index):
        remote(
            self.src, self.dst.at[slot], self.send.at[index], self.recv.at[index], self.sibling
        ).wait_recv()

    def start(self):
        for k in (1, 3, 2):
            self.launch(self.src, self.at, k - 1, (self.tower, self.spot(k, self.row)))
        self.launch(self.src, self.at, 3, self.beside)
        self.launch(self.src, self.at, 7, self.sibling)
        self.own = pltpu.make_async_copy(self.src, self.dst.at[self.at], self.send.at[15])
        self.own.start()

    def relay_deep(self):
        for k in (1, 3, 2):
            slot = self.spot(4 - k, self.row)
            self.arrived(slot, k - 1)
            self.launch(self.dst.at[slot], slot, 3 + k, self.beside)
            self.launch(self.dst.at[slot], slot, 7 + k, self.sibling)

    def relay_row(self):
        for k in (0, 1, 3, 2):
            slot = self.spot(4 - k, 1 - self.row)
            self.arrived(slot, 3 + k)
            self.launch(self.dst.at[slot], slot, 11 + k, self.sibling)

    def finish(self):
        for index in range(8):
            k, row = index % 4, self.row if index < 4 else 1 - self.row
            slot = (self.deep + 4 - k) % 4 * 4 + row * 2 + 1 - self.core
            self.arrived(slot, 7 + index)
        self.own.wait()

    def drain(self):
        for copy in self.sent:
            copy.wait_send()


class Blocks:
    def __init__(self, src, dst, send, recv, shared=1):
        self.src, self.dst, self.send, self.recv = src, dst, send, recv
        self.tower, self.at = here()
        self.shared = shared
        self.sent = []

    def start(self):
        for k in range(1, 16):
            to = (self.at + k) % 16
            copy = remote(
                self.src.at[to // self.shared],
                self.dst.at[self.at],
                self.send.at[k - 1],
                self.recv.at[k - 1],
                (self.tower, to),
            )
            copy.start()
            self.sent.append(copy)
        self.own = pltpu.make_async_copy(
            self.src.at[self.at // self.shared], self.dst.at[self.at], self.send.at[15]
        )
        self.own.start()

    def finish(self):
        for k in range(1, 16):
            remote(
                self.src.at[0],
                self.dst.at[(self.at + 16 - k) % 16],
                self.send.at[k - 1],
                self.recv.at[k - 1],
                (self.tower, self.at),
            ).wait_recv()
        self.own.wait()

    def drain(self):
        for copy in self.sent:
            copy.wait_send()


class Pair:
    def __init__(self, from_zero, zero_dst, from_one, one_dst, sems):
        tower, at = here()
        partner = (1 - tower, at)
        self.tower = tower
        self.up = remote(from_zero, zero_dst, sems.at[0], sems.at[1], partner)
        self.down = remote(from_one, one_dst, sems.at[0], sems.at[1], partner)

    def by_tower(self, zero, one):
        pl.when(self.tower == 0)(zero)
        pl.when(self.tower == 1)(one)

    def start(self):
        self.by_tower(self.up.start, self.down.start)

    def finish(self):
        self.by_tower(self.down.wait_recv, self.up.wait_recv)

    def drain(self):
        self.by_tower(self.up.wait_send, self.down.wait_send)


VECTORS = 5


class Plan:
    def __init__(self, tower, share, rows, per_device):
        self.tower = tower
        self.share = share
        self.rows = rows
        self.chunk = rows * LANES
        self.per_device = per_device
        self.first_slot = [sum(per_device[:p]) for p in range(6)]
        self.first_chunk = [16 * slot for slot in self.first_slot]
        self.slots = sum(per_device) + 1
        self.total = 16 * sum(per_device) + 1
        spans = [self.span(device) for device in range(32)]
        self.counts = sorted({last - first + 1 for first, last in spans})
        self.local = self.counts[-1]

    def span(self, device):
        first = device * self.share // self.chunk
        last = ((device + 1) * self.share - 1) // self.chunk
        return first, min(last, self.total - 1)

    def bounds(self, device):
        first = device * self.share // self.chunk
        last = ((device + 1) * self.share - 1) // self.chunk
        return first, jnp.minimum(last, self.total - 1)

    def pieces(self, p):
        return self.per_device[p] if p < VECTORS else 1

    def target(self, g):
        piece, base, slot, n = (jnp.int32(0), jnp.int32(0), jnp.int32(0), jnp.int32(1))
        for p in range(VECTORS):
            inside = g >= self.first_chunk[p]
            piece = jnp.where(inside, p, piece)
            base = jnp.where(inside, self.first_chunk[p], base)
            slot = jnp.where(inside, self.first_slot[p], slot)
            n = jnp.where(inside, self.per_device[p], n)
        at = (g - base) // n
        return piece, at, slot + (g - base) - at * n


class Deal:
    def __init__(self, plan, s, src, dst, extra, last, sems):
        self.plan, self.s, self.src, self.dst = plan, s, src, dst
        self.extra, self.last = extra, last
        self.chunk_send, self.recv, self.edge, self.fetch = sems
        self.tower, self.at = here()
        self.me = self.tower * 16 + self.at
        self.first, self.last_chunk = plan.bounds(self.me)
        before = (self.me + 31) % 32
        self.head = remote(
            src.at[0], extra, self.edge.at[s, 0], self.edge.at[s, 1], (before // 16, before % 16)
        )

    def send_head(self):
        pl.when(self.me > 0)(self.head.start)

    def move(self, src, i, piece, at_to, slot, wait):
        far = jnp.logical_or(self.tower != self.plan.tower, at_to != self.at)
        recv = self.recv.at[self.s, piece]
        copy = remote(
            src,
            self.dst.at[slot],
            self.chunk_send.at[self.s, i],
            recv,
            (jnp.int32(self.plan.tower), at_to),
        )
        pl.when(far)(copy.wait_send if wait else copy.start)
        if not wait:
            pl.when(jnp.logical_not(far))(
                pltpu.make_async_copy(src, self.dst.at[slot], recv).start
            )

    def whole(self, early, wait):
        def step(i, carry):
            g = self.first + i
            piece, at_to, slot = self.plan.target(g)
            inside = jnp.logical_and(
                jnp.logical_or(i > 0, self.me == 0),
                jnp.logical_or(
                    g < self.last_chunk, jnp.logical_and(self.me == 31, g < self.plan.total - 1)
                ),
            )
            inside = jnp.logical_and(inside, g <= self.last_chunk)
            inside = jnp.logical_and(inside, g < self.plan.total - 1)
            if early is not None:
                hidden = jnp.logical_and(piece >= 2, piece <= 3)
                inside = jnp.logical_and(inside, jnp.logical_not(hidden) if early else hidden)

            @pl.when(inside)
            def _():
                self.move(self.src.at[i], i, piece, at_to, slot, wait)

            return carry

        lax.fori_loop(0, self.plan.local, step, 0)

    def vectors(self, wait):
        @pl.when(self.me == 31)
        def _():
            src = self.src.at[self.last_chunk - self.first]

            def each(k, carry):
                self.move(src, self.plan.local + k, VECTORS, k, self.plan.slots - 1, wait)
                return carry

            lax.fori_loop(0, 16, each, 0)

    def fetch_last(self):
        return pltpu.make_async_copy(
            self.src.at[self.last_chunk - self.first], self.last, self.fetch.at[self.s]
        )

    def join(self):
        @pl.when(self.me < 31)
        def _():
            self.fetch_last().wait()
            self.head.wait_recv()
            self.last[...] = self.last[...] + self.extra[...]
            piece, at_to, slot = self.plan.target(self.last_chunk)
            self.move(self.last, self.plan.local + 16, piece, at_to, slot, False)

    def start_fetch(self):
        pl.when(self.me < 31)(self.fetch_last().start)

    def arrived(self, p):
        part = self.dst.at[pl.ds(self.plan.first_slot[p], self.plan.pieces(p))]
        pltpu.make_async_copy(part, part, self.recv.at[self.s, p]).wait()

    def drain(self):
        pl.when(self.me > 0)(self.head.wait_send)
        self.whole(None, True)
        self.vectors(True)

        @pl.when(self.me < 31)
        def _():
            piece, at_to, slot = self.plan.target(self.last_chunk)
            self.move(self.last, self.plan.local + 16, piece, at_to, slot, True)


class Collect:
    def __init__(self, plan, s, src, dst, send, recv):
        self.plan, self.s, self.src, self.dst = plan, s, src, dst
        self.send, self.recv = send, recv
        self.tower, self.at = here()
        self.me = self.tower * 16 + self.at

    def one(self, owner, slot, g, which, wait):
        first, _ = self.plan.bounds(owner)
        far = owner != self.me
        recv = self.recv.at[self.s]
        copy = remote(
            self.src.at[slot],
            self.dst.at[g - first],
            self.send.at[which, slot],
            recv,
            (owner // 16, owner % 16),
        )
        pl.when(far)(copy.wait_send if wait else copy.start)
        if not wait:
            pl.when(jnp.logical_not(far))(
                pltpu.make_async_copy(self.src.at[slot], self.dst.at[g - first], recv).start
            )

    def piece(self, p, wait):
        n = self.plan.pieces(p)

        def step(i, carry):
            slot = self.plan.first_slot[p] + i
            g = self.plan.first_chunk[p] + self.at * n + i if p < VECTORS else self.plan.total - 1
            low = g * self.plan.chunk // self.plan.share
            high = jnp.minimum(((g + 1) * self.plan.chunk - 1) // self.plan.share, 31)
            self.one(low, slot, g, 0, wait)
            pl.when(high != low)(lambda: self.one(high, slot, g, 1, wait))
            return carry

        if p == VECTORS:


            @pl.when(self.at == 0)
            def _():
                step(0, 0)

        else:
            lax.fori_loop(0, n, step, 0)

    def finish(self):
        first, last = self.plan.bounds(self.me)
        held = last - first + 1
        for n in self.plan.counts:

            @pl.when(held == n)
            def _():
                part = self.dst.at[pl.ds(0, n)]
                pltpu.make_async_copy(part, part, self.recv.at[self.s]).wait()


SEQS = 16
HEADS = 16


class Tower:
    def __init__(self, index, width, hidden, length, room, causal):
        self.index = index
        self.width = width
        self.hidden = hidden
        self.length = length
        self.room = room
        self.causal = causal
        self.heads = width // HEAD
        self.block = width // 16
        self.part = hidden // 8
        self.reduce_rows = hidden // 16


TOWERS = (
    Tower(0, D_IMG, FF_IMG, 50, 64, False),
    Tower(1, D_TXT, FF_TXT, 77, 80, True),
)
ROOM = 80
WIDTH = D_IMG
PART = FF_IMG // 8


def each_tower(run):
    tower = lax.axis_index("tower")
    for kind in TOWERS:
        pl.when(tower == kind.index)(functools.partial(run, kind))


def dot_nn(a, b):
    return lax.dot_general(a, b, (((1,), (0,)), ((), ())), preferred_element_type=WIDE)


def dot_nt(a, b):
    return lax.dot_general(a, b, (((1,), (1,)), ((), ())), preferred_element_type=WIDE)


def dot_tn(a, b):
    return lax.dot_general(a, b, (((0,), (0,)), ((), ())), preferred_element_type=WIDE)


def standardise(rows):
    centred = rows - jnp.mean(rows, axis=-1, keepdims=True)
    spread = jnp.mean(centred * centred, axis=-1, keepdims=True)
    rate = lax.rsqrt(spread + 1e-05)
    return centred * rate, rate


def norm_back(grad, gain, hat, rate):
    scaled = grad * gain
    return rate * (
        scaled
        - jnp.mean(scaled, axis=-1, keepdims=True)
        - hat * jnp.mean(scaled * hat, axis=-1, keepdims=True)
    )


def spans(kind):
    return [
        (lo, min(lo + 512, kind.width), lo // HEAD, (min(lo + 512, kind.width) - lo) // HEAD)
        for lo in range(0, kind.width, 512)
    ]


def head_rows(rows, span):
    lo, hi, _, n = span
    part = rows[:, lo:hi]
    owner = lax.broadcasted_iota(jnp.int32, part.shape, 1) // HEAD
    nothing = jnp.zeros_like(part)
    return jnp.concatenate([jnp.where(owner == h, part, nothing) for h in range(n)], axis=0)


def from_head_rows(rows, span):
    _, _, _, n = span
    owner = lax.broadcasted_iota(jnp.int32, (SEQS, rows.shape[1]), 1) // HEAD
    total = jnp.zeros((SEQS, rows.shape[1]), rows.dtype)
    for h in range(n):
        total = jnp.where(owner == h, rows[h * SEQS : (h + 1) * SEQS], total)
    return total


def side_by_side(parts):
    return parts[0] if len(parts) == 1 else jnp.concatenate(parts, axis=1)


def get_rows(ref, place, width):
    return side_by_side([ref[c, place, :] for c in range(width // LANES)])


def put_rows(ref, place, value):
    for c in range(value.shape[1] // LANES):
        ref[c, place, :] = value[:, c * LANES : (c + 1) * LANES]


def matrix(ref, kind, start, width):
    return ref[:, : kind.block, start : start + width].reshape(kind.width, width)


def vector(vec_ref, kind, row):
    return vec_ref[row : row + 1, : kind.width]


def pieces_of(kind):
    return (
        (kind.block, 3 * kind.width),
        (kind.block, kind.width),
        (kind.block, kind.hidden),
        (kind.reduce_rows, kind.width),
        (kind.block, EMB),
        (16, kind.width),
    )


def lane_blocks(kind, plan, p):
    height, width = pieces_of(kind)[p]
    pitch = width // LANES
    base = plan.first_slot[p] * plan.rows if p < VECTORS else (plan.slots - 1) * plan.rows
    return [(c, pl.ds(base + c, height, stride=pitch)) for c in range(pitch)]


def lift(kind, plan, p, slots, flat):
    n = plan.pieces(p)
    slot = plan.first_slot[p]
    rows = slots[slot : slot + n].reshape(n * plan.rows, LANES)
    flat[slot * plan.rows : (slot + n) * plan.rows, :] = rows.astype(WIDE)
    return [(c, flat[place, :]) for c, place in lane_blocks(kind, plan, p)]


def drop(kind, plan, p, value, slots, flat):
    for c, place in lane_blocks(kind, plan, p):
        flat[place, :] = value(c)
    n = plan.pieces(p)
    slot = plan.first_slot[p]
    rows = flat[slot * plan.rows : (slot + n) * plan.rows, :]
    slots[slot : slot + n] = rows.reshape(n, plan.rows, LANES).astype(LOW)


def expand_matrix(ref, kind):
    return jnp.concatenate(
        [ref[at % 2, at // 2, : kind.block, : kind.part] for at in range(16)], axis=0
    )


def reduce_matrix(ref, kind):
    return ref[:, : kind.reduce_rows, : kind.width].reshape(kind.part, kind.width)


def hidden_bias(vec_ref, kind):
    chip = lax.axis_index("dp") // 2
    whole = vec_ref[...]
    row = lax.broadcasted_iota(jnp.int32, (16, 1), 0)
    line = jnp.sum(jnp.where(row == 10 + chip // 2, whole, 0.0), axis=0, keepdims=True)
    return jnp.where(
        chip % 2 == 0, line[:, : kind.part], line[:, kind.part : 2 * kind.part]
    )


def hidden_kernel(second_ref, raise_ref, reduce_ref, vec_ref, part_ref, raised_ref):
    def run(kind):
        width = kind.width
        rows = second_ref[:, :, :width].reshape(8 * SEQS, width)
        raised = dot_nn(rows, expand_matrix(raise_ref, kind)) + hidden_bias(vec_ref, kind)
        raised_ref[:, : kind.part] = raised
        active = (raised * jax.nn.sigmoid(1.702 * raised)).astype(LOW)
        part = dot_nn(active, reduce_matrix(reduce_ref, kind))
        part_ref[:, :, :width] = part.reshape(8, SEQS, width).astype(LOW)

    each_tower(run)


def hidden_back_kernel(
    grad_ref,
    second_ref,
    raised_ref,
    raise_ref,
    reduce_ref,
    back_ref,
    raise_grad_ref,
    reduce_keep_ref,
    reduce_send_ref,
    bias_ref,
    whole,
):
    def run(kind):
        width, part = kind.width, kind.part
        grads = grad_ref[:, :, :width].reshape(8 * SEQS, width)
        rows = second_ref[:, :, :width].reshape(8 * SEQS, width)
        raised = raised_ref[:, :part]
        gate = jax.nn.sigmoid(1.702 * raised)
        active = (raised * gate).astype(LOW)
        slope = gate + 1.702 * raised * gate * (1.0 - gate)
        raised_grad = dot_nt(grads, reduce_matrix(reduce_ref, kind)) * slope
        low_grad = raised_grad.astype(LOW)
        bias_ref[0:1, :part] = jnp.sum(low_grad.astype(WIDE), axis=0, keepdims=True)
        back = dot_nt(low_grad, expand_matrix(raise_ref, kind))
        back_ref[:, :, :width] = back.reshape(8, SEQS, width).astype(LOW)
        raise_grad = dot_tn(rows, low_grad).reshape(16, kind.block, part).astype(LOW)
        for at in range(16):
            raise_grad_ref[at % 2, at // 2, : kind.block, :part] = raise_grad[at]
        whole[:part, :width] = dot_tn(active, grads)
        core = lax.axis_index("dp") % 2
        n = kind.reduce_rows
        keep = pl.multiple_of(core * n, 64)
        send = pl.multiple_of((1 - core) * n, 64)
        reduce_keep_ref[:n, :width] = whole[pl.ds(keep, n), :width]
        reduce_send_ref[:n, :width] = whole[pl.ds(send, n), :width].astype(LOW)

    each_tower(run)


def embed_kernel(part_ref, middle_ref, gat_ref, vec_ref, emb_ref, final_ref, pooled_ref, proj_ref):
    def run(kind):
        width = kind.width
        final = (
            middle_ref[:, :width]
            + jnp.sum(part_ref[:, :, :width].astype(WIDE), axis=0)
            + vector(vec_ref, kind, 7)
        )
        final_ref[:, :width] = final
        hat, _ = standardise(final)
        pooled = (hat * vector(vec_ref, kind, 8) + vector(vec_ref, kind, 9)).astype(LOW)
        pooled_ref[:, :width] = pooled
        proj = dot_nn(pooled, matrix(gat_ref, kind, 0, EMB))
        proj_ref[...] = proj
        size = jnp.sum(proj * proj, axis=-1, keepdims=True) + 1e-06
        emb_ref[...] = (proj * lax.rsqrt(size)).astype(LOW)

    each_tower(run)


def objective_kernel(
    scale_ref,
    all_ref,
    valid_ref,
    final_ref,
    proj_ref,
    gat_ref,
    vec_ref,
    low_ref,
    grad_ref,
    proj_grad_ref,
    final_vec_ref,
    loss_ref,
    scale_new_ref,
    own_scr,
):
    def ordered(which):
        blocks = []
        for half in range(2):
            for j in range(16):
                rows = all_ref[j % 2, which * 8 + j // 2].astype(WIDE)
                blocks.append(rows[half * 8 : half * 8 + 8])
        return jnp.concatenate(blocks, axis=0).astype(LOW)

    img, txt = ordered(0), ordered(1)
    total = img.shape[0]
    scale = jnp.exp(jnp.full((1, 1), scale_ref[0], WIDE))
    lines = []
    for d in range(32):
        rows = valid_ref[d % 2, d // 2].astype(WIDE)
        lines.append(jnp.concatenate([rows[:8], rows[8:]], axis=1))
    allowed = jnp.concatenate(lines, axis=0) > 0
    same = lax.broadcasted_iota(jnp.int32, (total, total), 0) == lax.broadcasted_iota(
        jnp.int32, (total, total), 1
    )
    same = same.astype(WIDE)

    def side(left, right):
        logits = scale * dot_nt(left, right)
        masked = jnp.where(allowed, logits, -1e30)
        top = jnp.max(masked, axis=1, keepdims=True)
        lse = jnp.log(jnp.sum(jnp.exp(masked - top), axis=1, keepdims=True)) + top
        terms = 0.5 * (jnp.where(allowed, jnp.exp(logits - lse), 0.0) - same)
        loss = 0.5 * (
            jnp.sum(lse, axis=0, keepdims=True)
            - jnp.sum(jnp.sum(logits * same, axis=1, keepdims=True), axis=0, keepdims=True)
        )
        rate = jnp.sum(jnp.sum(terms * logits, axis=1, keepdims=True), axis=0, keepdims=True)
        return (scale * terms).astype(LOW), loss, rate

    row_back, row_loss, row_rate = side(img, txt)
    col_back, col_loss, col_rate = side(txt, img)
    loss_ref[0] = jnp.sum(row_loss + col_loss) / total
    parts = advance(
        scale_ref[0], scale_ref[1], scale_ref[2], jnp.sum(row_rate + col_rate), scale_rate
    )
    for k in range(3):
        scale_new_ref[k] = parts[k]

    def run(kind):
        width = kind.width
        if kind.index == 0:
            emb_grad = dot_nn(row_back, txt) + dot_tn(col_back, txt)
        else:
            emb_grad = dot_nn(col_back, img) + dot_tn(row_back, img)
        own_scr[...] = emb_grad
        at = lax.axis_index("dp")
        mine = jnp.concatenate(
            [
                own_scr[pl.ds(pl.multiple_of(half * 128 + at * 8, 8), 8), :]
                for half in range(2)
            ],
            axis=0,
        )
        proj = proj_ref[...]
        size = jnp.sum(proj * proj, axis=-1, keepdims=True) + 1e-06
        along = jnp.sum(proj * mine, axis=-1, keepdims=True)
        proj_grad = ((mine - proj * along / size) * lax.rsqrt(size)).astype(LOW)
        proj_grad_ref[...] = proj_grad
        pooled_grad = dot_nt(proj_grad, matrix(gat_ref, kind, 0, EMB))
        hat, rate = standardise(final_ref[:, :width])
        final_vec_ref[0:1, :width] = jnp.sum(pooled_grad * hat, axis=0, keepdims=True)
        final_vec_ref[1:2, :width] = jnp.sum(pooled_grad, axis=0, keepdims=True)
        final_grad = norm_back(pooled_grad, vector(vec_ref, kind, 8), hat, rate)
        grad_ref[:, :width] = final_grad
        low = final_grad.astype(LOW)
        low_ref[:, :width] = low
        final_vec_ref[2:3, :width] = jnp.sum(low.astype(WIDE), axis=0, keepdims=True)

    each_tower(run)


def step_kernel(
    plans,
    ends_ref,
    scale_ref,
    img_src,
    txt_src,
    valid_ref,
    img_own,
    txt_own,
    loss_ref,
    scale_new_ref,
    img_keep,
    txt_keep,
    img_chunks,
    txt_chunks,
    second_ref,
    middle_ref,
    query_ref,
    keyed_ref,
    mixture_ref,
    weight_ref,
    first_ref,
    img_in,
    txt_in,
    ask_ref,
    mix_ref,
    emb_ref,
    vec_ref,
    raise_ref,
    reduce_ref,
    pairs_ref,
    img_slots,
    txt_slots,
    img_extra,
    txt_extra,
    img_last,
    txt_last,
    flat,
    ask_block,
    mix_block,
    emb_block,
    raise_block,
    reduce_block,
    mask_block,
    top_scr,
    at_scr,
    score_scr,
    low_scr,
    grad_ref,
    pooled_ref,
    proj_grad_ref,
    final_vec_ref,
    raise_grad_ref,
    reduce_keep_ref,
    reduce_send_ref,
    bias_ref,
    backs_ref,
    seconds,
    part,
    parts,
    raised,
    emb,
    all_embs,
    final,
    proj,
    low,
    lows,
    back,
    own_scr,
    whole,
    img_send,
    txt_send,
    img_home,
    txt_home,
    rows_grad,
    middle_scr,
    second_scr,
    valued_scr,
    turn_scr,
    shared_scr,
    slope_scr,
    left_scr,
    left_block,
    turn_block,
    left_all,
    turn_all,
    early_block,
    early_all,
    late_block,
    late_all,
    lines_block,
    lines_all,
    raise_half,
    risen_block,
    raise_all,
    reduce_in,
    img_home_slots,
    txt_home_slots,
    gains,
    top_grad_scr,
    deal_send,
    deal_recv,
    deal_edge,
    deal_fetch,
    ask_send,
    ask_recv,
    mix_send,
    mix_recv,
    emb_send,
    emb_recv,
    raise_send,
    raise_recv,
    reduce_sems,
    pair_sems,
    mask_send,
    mask_recv,
    group_send,
    group_recv,
    embs_send,
    embs_recv,
    home_sems,
    risen_send,
    risen_recv,
    left_send,
    left_recv,
    turn_send,
    turn_recv,
    early_send,
    early_recv,
    late_send,
    late_recv,
    lines_send,
    lines_recv,
    home_pair_sems,
    collect_send,
    collect_recv,
):
    tower, at = here()
    core = at % 2
    me = tower * 16 + at
    sibling = (tower, at + 1 - 2 * core)
    greet(everyone(tower, at))
    deal_sems = (deal_send, deal_recv, deal_edge, deal_fetch)
    deals = [
        Deal(plans[0], 0, img_src, img_slots, img_extra, img_last, deal_sems),
        Deal(plans[1], 1, txt_src, txt_slots, txt_extra, txt_last, deal_sems),
    ]
    pair = Pair(txt_own, txt_in, img_own, img_in, pair_sems)
    ask = Ring(ask_block, ask_ref, ask_send, ask_recv)
    mix = Ring(mix_block, mix_ref, mix_send, mix_recv)
    embed = Ring(emb_block, emb_ref, emb_send, emb_recv)
    rise = Group(raise_block, raise_ref, raise_send, raise_recv)
    fall = remote(
        reduce_block, reduce_ref.at[core], reduce_sems.at[0], reduce_sems.at[1], sibling
    )
    fall_own = pltpu.make_async_copy(reduce_block, reduce_ref.at[core], reduce_sems.at[2])
    masks = Spread(mask_block, pairs_ref, mask_send, mask_recv)
    rows = valid_ref[...].astype(WIDE)
    mask_block[...] = jnp.concatenate([rows[:, :LANES], rows[:, LANES:]], axis=0).astype(LOW)

    for deal in deals:
        deal.send_head()
        deal.start_fetch()
        deal.vectors(False)
    for deal in deals:
        deal.whole(True, False)
    pair.start()
    for deal in deals:
        deal.join()

    def lift_to(kind, p, ref, start):
        slots = (img_slots, txt_slots)[kind.index]
        for c, value in lift(kind, plans[kind.index], p, slots, flat):
            lane = start + c * LANES
            ref[: value.shape[0], lane : lane + LANES] = value.astype(ref.dtype)

    def normalise(kind, half):
        width, room = kind.width, kind.room
        own, arrived = ((img_own, img_in), (txt_own, txt_in))[kind.index]
        ref = own if half == kind.index else arrived
        gain, shift = vector(vec_ref, kind, 0), vector(vec_ref, kind, 1)
        positions = lax.broadcasted_iota(jnp.int32, (room, 1), 0)
        for i in range(8):
            rows = ref[i].astype(WIDE)
            hat, _ = standardise(rows)
            first = (hat * gain + shift).astype(LOW)
            s = half * 8 + i
            first_ref[s, :room, :width] = first
            if kind.causal:
                chosen = positions == ends_ref[(half * 16 + at) * 8 + i]
                top = jnp.sum(jnp.where(chosen, first.astype(WIDE), 0.0), axis=0, keepdims=True)
                raw = jnp.sum(jnp.where(chosen, rows, 0.0), axis=0, keepdims=True)
            else:
                top, raw = first[:1].astype(WIDE), rows[:1]
            top_scr[s : s + 1, :width] = top
            at_scr[s : s + 1, :width] = raw

    def begin(kind):
        deal = deals[kind.index]
        deal.arrived(VECTORS)
        lift_to(kind, VECTORS, vec_ref, 0)
        normalise(kind, kind.index)

    each_tower(begin)

    def place_inputs(kind):
        deals[kind.index].arrived(0)
        slots = (img_slots, txt_slots)[kind.index]
        per = kind.width // LANES
        for c, value in lift(kind, plans[kind.index], 0, slots, flat):
            lane = c // per * WIDTH + c % per * LANES
            ref = ask_block
            if lane >= 2 * WIDTH:
                ref, lane = mix_block, lane - 2 * WIDTH
            ref[: value.shape[0], lane : lane + LANES] = value.astype(LOW)

    each_tower(place_inputs)
    ask.start()

    def place_rest(kind):
        deals[kind.index].arrived(1)
        lift_to(kind, 1, mix_block, WIDTH)
        deals[kind.index].arrived(4)
        lift_to(kind, 4, emb_block, 0)

    each_tower(place_rest)
    mix.start()
    embed.start()
    for deal in deals:
        deal.whole(False, False)
    pair.finish()
    each_tower(lambda kind: normalise(kind, 1 - kind.index))
    masks.start()
    ask.relay_deep()
    ask.relay_row()
    ask.finish()

    def question(kind):
        width = kind.width
        tops = top_scr[:, :width].astype(LOW)
        query = dot_nn(tops, matrix(ask_ref, kind, 0, width)) + vector(vec_ref, kind, 2)
        query = query.astype(LOW)
        query_ref[:, :width] = query
        for span in spans(kind):
            lo, hi, first_head, n = span
            put_rows(
                keyed_ref,
                pl.ds(first_head * SEQS, n * SEQS),
                dot_nt(head_rows(query, span), matrix(ask_ref, kind, WIDTH + lo, hi - lo)) * 0.125,
            )
        dead = (HEADS - kind.heads) * SEQS
        put_rows(keyed_ref, pl.ds(kind.heads * SEQS, dead), jnp.zeros((dead, width), WIDE))

    each_tower(question)
    mix.relay_deep()
    embed.relay_deep()

    def score(kind):
        width, room = kind.width, kind.room
        lane = lax.broadcasted_iota(jnp.int32, (HEADS, room), 1)
        for s in range(SEQS):
            keys = get_rows(keyed_ref, pl.ds(s, HEADS, stride=SEQS), width).astype(LOW)
            scores = dot_nt(keys, first_ref[s, :room, :width])
            if kind.causal:
                allowed = lane <= ends_ref[(s // 8 * 16 + at) * 8 + s % 8]
            else:
                allowed = lane < kind.length
            score_scr[s * HEADS : (s + 1) * HEADS, :room] = jnp.where(allowed, scores, -1e30)
        scores = score_scr[:, :room]
        raw = jnp.exp(scores - jnp.max(scores, axis=-1, keepdims=True))
        weights = raw / jnp.sum(raw, axis=-1, keepdims=True)
        head = lax.broadcasted_iota(jnp.int32, (SEQS * HEADS, 1), 0) % HEADS
        weights = jnp.where(head < kind.heads, weights, 0.0)
        weight_ref[:, :room] = weights
        low_scr[: SEQS * HEADS, :room] = weights.astype(LOW)

    each_tower(score)
    mix.relay_row()
    embed.relay_row()

    def mixture(kind):
        width, room = kind.width, kind.room
        for s in range(SEQS):
            mixed = dot_nn(
                low_scr[s * HEADS : (s + 1) * HEADS, :room], first_ref[s, :room, :width]
            )
            put_rows(mixture_ref, pl.ds(s, HEADS, stride=SEQS), mixed)
        totals = jnp.sum(
            low_scr[: SEQS * HEADS, :room].astype(WIDE), axis=-1, keepdims=True
        )
        score_scr[...] = jnp.broadcast_to(totals, score_scr.shape)

    each_tower(mixture)

    def place_hidden(kind):
        deal, plan = deals[kind.index], plans[kind.index]
        slots = (img_slots, txt_slots)[kind.index]
        deal.arrived(2)
        per = kind.part // LANES
        for c, value in lift(kind, plan, 2, slots, flat):
            lane = c % per * LANES
            raise_block[c // per, : kind.block, lane : lane + LANES] = value.astype(LOW)
        deal.arrived(3)
        lift_to(kind, 3, reduce_block, 0)

    each_tower(place_hidden)
    rise.start()
    fall.start()
    fall_own.start()
    mix.finish()

    def answer(kind):
        width = kind.width
        mixed = []
        bias = vector(vec_ref, kind, 3)
        for span in spans(kind):
            lo, hi, first_head, n = span
            z = get_rows(mixture_ref, pl.ds(first_head * SEQS, n * SEQS), width).astype(LOW)
            valued = dot_nn(z, matrix(mix_ref, kind, lo, hi - lo))
            totals = jnp.concatenate(
                [score_scr[pl.ds(first_head + h, SEQS, stride=HEADS), 0:1] for h in range(n)],
                axis=0,
            )
            mixed.append(from_head_rows(valued + totals * bias[:, lo:hi], span))
        mixed = side_by_side(mixed).astype(LOW)
        middle = (
            at_scr[:, :width]
            + dot_nn(mixed, matrix(mix_ref, kind, WIDTH, width))
            + vector(vec_ref, kind, 4)
        )
        middle_ref[:, :width] = middle
        hat, _ = standardise(middle)
        second_ref[:, :width] = (
            hat * vector(vec_ref, kind, 5) + vector(vec_ref, kind, 6)
        ).astype(LOW)
        put_rows(mixture_ref, pl.ds(12 * SEQS, SEQS), top_scr[:, :width])
        put_rows(mixture_ref, pl.ds(13 * SEQS, SEQS), mixed.astype(WIDE))

    each_tower(answer)
    rise.relay()
    masks.relay()
    embed.finish()
    rise.finish()
    fall_own.wait()
    remote(
        reduce_block, reduce_ref.at[1 - core], reduce_sems.at[0], reduce_sems.at[1], sibling
    ).wait_recv()

    sent = group_exchange(False, second_ref, seconds, group_send.at[0], group_recv.at[0])
    hidden_kernel(seconds, raise_ref, reduce_ref, vec_ref, part, raised)
    sent += group_exchange(True, part, parts, group_send.at[1], group_recv.at[1])
    embed_kernel(parts, middle_ref, emb_ref, vec_ref, emb, final, pooled_ref, proj)
    embs = Spread(emb, all_embs, embs_send, embs_recv)
    embs.start()
    masks.finish()
    embs.relay()
    embs.finish()
    objective_kernel(
        scale_ref,
        all_embs,
        pairs_ref,
        final,
        proj,
        emb_ref,
        vec_ref,
        low,
        grad_ref,
        proj_grad_ref,
        final_vec_ref,
        loss_ref,
        scale_new_ref,
        own_scr,
    )
    sent += group_exchange(False, low, lows, group_send.at[2], group_recv.at[2])
    hidden_back_kernel(
        lows,
        seconds,
        raised,
        raise_ref,
        reduce_ref,
        back,
        raise_grad_ref,
        reduce_keep_ref,
        reduce_send_ref,
        bias_ref,
        whole,
    )
    sent += group_exchange(True, back, backs_ref, group_send.at[3], group_recv.at[3])
    halves = remote(
        raise_grad_ref.at[1 - core], raise_half, home_sems.at[0], home_sems.at[1], sibling
    )
    fallen = remote(reduce_send_ref, reduce_in, home_sems.at[2], home_sems.at[3], sibling)
    halves.start()
    fallen.start()
    risen_group = Group(risen_block, raise_all, risen_send, risen_recv, False)

    lefts = Blocks(left_block, left_all, left_send, left_recv)
    turns = Blocks(turn_block, turn_all, turn_send, turn_recv)
    early = Ring(early_block, early_all, early_send, early_recv)
    late = Ring(late_block, late_all, late_send, late_recv)
    home_pair = Pair(img_send, img_home, txt_send, txt_home, home_pair_sems)
    collects = [
        Collect(plans[0], 0, img_home_slots, img_chunks, collect_send.at[0], collect_recv),
        Collect(plans[1], 1, txt_home_slots, txt_chunks, collect_send.at[1], collect_recv),
    ]

    def outputs(kind):
        width = kind.width
        second_grad = jnp.sum(backs_ref[:, :, :width].astype(WIDE), axis=0)
        second_scr[:, :width] = second_grad
        hat, rate = standardise(middle_ref[:, :width])
        middle_grad = grad_ref[:, :width] + norm_back(
            second_grad, vector(vec_ref, kind, 5), hat, rate
        )
        middle_scr[:, :width] = middle_grad
        output_grad = middle_grad.astype(LOW)
        mixed_grad = dot_nt(output_grad, matrix(mix_ref, kind, WIDTH, width)).astype(LOW)
        early_block[:, 0:width] = query_ref[:, :width]
        early_block[:, WIDTH : WIDTH + width] = mixed_grad
        early_block[:, 2 * WIDTH : 2 * WIDTH + width] = output_grad
        early_block[:, 3 * WIDTH : 3 * WIDTH + EMB] = proj_grad_ref[...]
        left_scr[:, :width] = get_rows(mixture_ref, slice(None), width)
        left_scr[14 * SEQS : 15 * SEQS, :width] = pooled_ref[:, :width].astype(WIDE)
        left_scr[15 * SEQS :, :width] = jnp.zeros((SEQS, width), WIDE)

    each_tower(outputs)
    early.start()

    def turned(kind):
        width, block = kind.width, kind.block
        left_block[:, :block, :] = left_scr[:, :width].T.reshape(16, block, 256).astype(LOW)

    each_tower(turned)
    lefts.start()

    def values(kind):
        width = kind.width
        mixed_grad = early_block[:, WIDTH : WIDTH + width]
        bias = vector(vec_ref, kind, 3)
        dead = kind.heads * SEQS
        put_rows(valued_scr, pl.ds(dead, 256 - dead), jnp.zeros((256 - dead, width), WIDE))
        shared_scr[dead:, :] = jnp.zeros((256 - dead, LANES), WIDE)
        for span in spans(kind):
            lo, hi, first_head, n = span
            rows = head_rows(mixed_grad, span)
            place = pl.ds(first_head * SEQS, n * SEQS)
            put_rows(valued_scr, place, dot_nt(rows, matrix(mix_ref, kind, lo, hi - lo)))
            constant = jnp.sum(rows.astype(WIDE) * bias[:, lo:hi], axis=-1, keepdims=True)
            shared_scr[place, :] = jnp.broadcast_to(constant, (n * SEQS, LANES))

    each_tower(values)
    halves.wait_recv()
    risen_block[...] = (
        raise_grad_ref[core].astype(WIDE) + raise_half[...].astype(WIDE)
    ).astype(LOW)
    risen_group.start()

    def slopes(kind):
        width, room = kind.width, kind.room
        for s in range(SEQS):
            line = pl.ds(s, HEADS, stride=SEQS)
            slope = dot_nt(
                get_rows(valued_scr, line, width).astype(LOW), first_ref[s, :room, :width]
            )
            slope_scr[s * HEADS : (s + 1) * HEADS, :room] = slope + shared_scr[line, 0:1]
        weights = weight_ref[:, :room]
        slope = slope_scr[:, :room]
        slope = weights * (slope - jnp.sum(weights * slope, axis=-1, keepdims=True))
        both = jnp.concatenate(
            [slope.reshape(SEQS, HEADS, room), weights.reshape(SEQS, HEADS, room)], axis=1
        )
        low_scr[:, :room] = both.reshape(2 * SEQS * HEADS, room).astype(LOW)

    each_tower(slopes)
    early.relay_deep()

    def tokens(kind):
        width, room = kind.width, kind.room
        for s in range(SEQS):
            line = pl.ds(s, HEADS, stride=SEQS)
            both = low_scr[2 * s * HEADS : 2 * (s + 1) * HEADS, :room]
            first = first_ref[s, :room, :width]
            put_rows(turn_scr, line, dot_nn(both[:HEADS], first))
            right = jnp.concatenate(
                [get_rows(keyed_ref, line, width), get_rows(valued_scr, line, width)], axis=0
            )
            rows_grad[s, :room, :width] = dot_tn(both, right.astype(LOW))

    each_tower(tokens)
    early.relay_row()

    def queries(kind):
        width, block = kind.width, kind.block
        grads = []
        for span in spans(kind):
            lo, hi, first_head, n = span
            rows = get_rows(turn_scr, pl.ds(first_head * SEQS, n * SEQS), width).astype(LOW)
            back = dot_nn(rows, matrix(ask_ref, kind, WIDTH + lo, hi - lo)) * 0.125
            grads.append(from_head_rows(back, span))
        query_grad = side_by_side(grads).astype(LOW)
        late_block[:, :width] = query_grad
        top_grad_scr[:, :width] = dot_nt(query_grad, matrix(ask_ref, kind, 0, width))
        turn_block[:, :block, :] = (
            get_rows(turn_scr, slice(None), width).T.reshape(16, block, 256).astype(LOW)
        )

    each_tower(queries)
    late.start()
    turns.start()
    gains[...] = jnp.zeros_like(gains)

    def finish(kind, half):
        width, room, length = kind.width, kind.room, kind.length
        own, arrived = ((img_own, img_in), (txt_own, txt_in))[kind.index]
        ref = own if half == kind.index else arrived
        keep, send = ((img_keep, img_send), (txt_keep, txt_send))[kind.index]
        gain = vector(vec_ref, kind, 0)
        positions = lax.broadcasted_iota(jnp.int32, (room, 1), 0)
        gain_sum = jnp.zeros((1, width), WIDE)
        shift_sum = jnp.zeros((1, width), WIDE)
        for i in range(8):
            s = half * 8 + i
            hat, rate = standardise(ref[i].astype(WIDE))
            if kind.causal:
                chosen = positions == ends_ref[(half * 16 + at) * 8 + i]
            else:
                chosen = positions == 0
            chosen = chosen.astype(WIDE)
            grad = rows_grad[s, :room, :width] + chosen * top_grad_scr[s : s + 1, :width]
            gain_sum += jnp.sum(grad * hat, axis=0, keepdims=True)
            shift_sum += jnp.sum(grad, axis=0, keepdims=True)
            result = norm_back(grad, gain, hat, rate) + chosen * middle_scr[s : s + 1, :width]
            if half == kind.index:
                keep[i] = result[:length]
            else:
                send[i] = result.astype(LOW)
        gains[0:1, :width] += gain_sum
        gains[1:2, :width] += shift_sum

    each_tower(lambda kind: finish(kind, 1 - kind.index))
    home_pair.start()
    risen_group.finish()
    fallen.wait_recv()

    def slots_of(kind):
        return (img_home_slots, txt_home_slots)[kind.index]

    def hidden_grads(kind):
        plan, collect = plans[kind.index], collects[kind.index]
        block, n, per = kind.block, kind.reduce_rows, kind.part // LANES

        def risen(c):
            chip, lane = c // per, c % per * LANES
            return raise_all[chip, :block, lane : lane + LANES].astype(WIDE)

        def fallen(c):
            lane = c * LANES
            return reduce_keep_ref[:n, lane : lane + LANES] + reduce_in[
                :n, lane : lane + LANES
            ].astype(WIDE)

        drop(kind, plan, 2, risen, slots_of(kind), flat)
        collect.piece(2, False)
        drop(kind, plan, 3, fallen, slots_of(kind), flat)
        collect.piece(3, False)

    each_tower(hidden_grads)
    late.relay_deep()
    each_tower(lambda kind: finish(kind, kind.index))
    late.relay_row()

    def lines(kind):
        width = kind.width
        hat, _ = standardise(middle_ref[:, :width])
        second_grad = second_scr[:, :width]

        def column_sum(value):
            return jnp.sum(value.astype(WIDE), axis=0, keepdims=True)

        mixed_grad = early_block[:, WIDTH : WIDTH + width].astype(WIDE)
        weights = low_scr[:, : kind.room].astype(WIDE).reshape(SEQS, 2 * HEADS, kind.room)
        totals = jnp.sum(weights[:, HEADS:], axis=-1, keepdims=True).reshape(SEQS * HEADS, 1)
        shared_scr[...] = jnp.broadcast_to(totals, shared_scr.shape)
        value_bias = []
        for lo, hi, first_head, n in spans(kind):
            owner = lax.broadcasted_iota(jnp.int32, (SEQS, hi - lo), 1) // HEAD
            scaled = jnp.zeros((SEQS, hi - lo), WIDE)
            for h in range(n):
                total = shared_scr[pl.ds(first_head + h, SEQS, stride=HEADS), 0:1]
                scaled = jnp.where(owner == h, mixed_grad[:, lo:hi] * total, scaled)
            value_bias.append(column_sum(scaled))
        hidden = bias_ref[0:1, : kind.part]
        parts = [
            gains[0:1, :width],
            gains[1:2, :width],
            column_sum(late_block[:, :width]),
            side_by_side(value_bias),
            column_sum(early_block[:, 2 * WIDTH : 2 * WIDTH + width]),
            column_sum(second_grad * hat),
            column_sum(second_grad),
            final_vec_ref[2:3, :width],
            final_vec_ref[0:1, :width],
            final_vec_ref[1:2, :width],
            jnp.concatenate([hidden, jnp.zeros((1, width - kind.part), WIDE)], axis=1),
            jnp.zeros((5, width), WIDE),
        ]
        lines_block[:, :width] = jnp.concatenate(parts, axis=0)

    each_tower(lines)
    line_copy = remote(
        lines_block, lines_all.at[at], lines_send.at[0], lines_recv.at[at], (tower, jnp.int32(0))
    )
    line_own = pltpu.make_async_copy(lines_block, lines_all.at[at], lines_recv.at[at])
    pl.when(at > 0)(line_copy.start)
    pl.when(at == 0)(line_own.start)

    early.finish()
    lefts.finish()

    def from_early(kind):
        plan, collect = plans[kind.index], collects[kind.index]
        width, block = kind.width, kind.block

        def gathered(k):
            lane = lax.broadcasted_iota(jnp.int32, (block, LANES), 1) // SEQS
            halves = []
            for side in range(2):
                total = jnp.zeros((block, LANES), WIDE)
                for j in range(8):
                    part = left_all[side * 8 + j, :block, LANES:].astype(WIDE)
                    shift = (j * SEQS - (k - 8) * SEQS) % LANES
                    turned_part = pltpu.roll(part, shift, 1) if shift else part
                    total = jnp.where(lane == j, turned_part, total)
                halves.append(total)
            return jnp.concatenate(halves, axis=1).astype(LOW)

        def right(start, wide):
            return early_all[:, :, start : start + wide].reshape(256, wide)

        output = dot_nn(gathered(13), right(2 * WIDTH, width))
        drop(
            kind, plan, 1, lambda c: output[:, c * LANES : (c + 1) * LANES], slots_of(kind), flat
        )
        collect.piece(1, False)
        embed = dot_nn(gathered(14), right(3 * WIDTH, EMB))
        drop(kind, plan, 4, lambda c: embed[:, c * LANES : (c + 1) * LANES], slots_of(kind), flat)
        collect.piece(4, False)
        left_scr[:block, :256] = gathered(12).astype(WIDE)

    each_tower(from_early)
    late.finish()
    turns.finish()

    def from_late(kind):
        plan, collect = plans[kind.index], collects[kind.index]
        width, block = kind.width, kind.block
        ask = dot_nn(left_scr[:block, :256].astype(LOW), late_all[:, :, :width].reshape(256, width))

        def outer(side_ref, start, span):
            lo, hi, first_head, n = span
            lane = first_head * SEQS
            total = jnp.zeros((block, hi - lo), WIDE)
            for j in range(8):
                left, rows = [], []
                for source in (2 * j, 2 * j + 1):
                    left.append(side_ref[source, :block, lane : lane + LANES])
                    rows.append(
                        head_rows(early_all[source, :, start : start + width], span)
                    )
                    if n < 8:
                        rows.append(jnp.zeros(((8 - n) * SEQS, hi - lo), LOW))
                total += dot_nn(
                    jnp.concatenate(left, axis=1), jnp.concatenate(rows, axis=0)
                )
            return total

        keys = side_by_side([outer(turn_all, 0, span) for span in spans(kind)]) * 0.125
        worth = side_by_side([outer(left_all, WIDTH, span) for span in spans(kind)])
        per = width // LANES

        def inputs(c):
            value = (ask, keys, worth)[c // per]
            return value[:, c % per * LANES : (c % per + 1) * LANES]

        drop(kind, plan, 0, inputs, slots_of(kind), flat)
        collect.piece(0, False)

    each_tower(from_late)

    @pl.when(at == 0)
    def _():
        for k in range(1, 16):
            remote(
                lines_block, lines_all.at[k], lines_send.at[0], lines_recv.at[k], sibling
            ).wait_recv()
        line_own.wait()

        def vectors(kind):
            width, part = kind.width, kind.part
            whole = [jnp.sum(lines_all[:, :10, :width], axis=0)]
            for row in range(4):
                pair_of = []
                for chip in (2 * row, 2 * row + 1):
                    pair_of.append(
                        lines_all[2 * chip, 10:11, :part] + lines_all[2 * chip + 1, 10:11, :part]
                    )
                whole.append(jnp.concatenate(pair_of, axis=1))
            whole.append(jnp.zeros((2, width), WIDE))
            result = jnp.concatenate(whole, axis=0)
            drop(
                kind,
                plans[kind.index],
                VECTORS,
                lambda c: result[:, c * LANES : (c + 1) * LANES],
                slots_of(kind),
                flat,
            )

        each_tower(vectors)

    each_tower(lambda kind: collects[kind.index].piece(VECTORS, False))
    home_pair.finish()

    @pl.when(tower == 1)
    def _():
        img_keep[...] = img_home[:, : TOWERS[0].length].astype(WIDE)

    @pl.when(tower == 0)
    def _():
        txt_keep[...] = txt_home[:, : TOWERS[1].length].astype(WIDE)

    for collect in collects:
        collect.finish()
    for copy in (*sent, fall, fallen, halves):
        copy.wait_send()
    pl.when(at > 0)(line_copy.wait_send)
    for group in (pair, ask, mix, embed, rise, masks, embs, *deals):
        group.drain()
    for group in (risen_group, lefts, turns, early, late, home_pair):
        group.drain()

    def drain(kind):
        for p in range(VECTORS + 1):
            collects[kind.index].piece(p, True)

    each_tower(drain)


ROWS_LOW = ((SEQS, WIDTH), LOW)
ROWS_WIDE = ((SEQS, WIDTH), WIDE)
HEAD_ROWS = ((WIDTH // LANES, SEQS * HEADS, LANES), WIDE)
LANE_ROWS = ((SEQS * HEADS, LANES), WIDE)
GROUP = ((8, SEQS, WIDTH), LOW)
HIDDEN_BLOCKS = ((2, 8, 48, PART), LOW)
OUTER = ((16, 48, SEQS * HEADS), LOW)


def chunk_shapes(plan, n):
    return ((n, plan.rows, LANES), LOW)


def run_step(scalars, chunks, valid, tokens, plans):
    most = max(plan.local for plan in plans) + 17
    slots = max(plan.slots for plan in plans)
    edges = [((plan.rows, LANES), LOW) for plan in plans]
    rooms = [((8, kind.room, kind.width), LOW) for kind in TOWERS]
    outs = [((8, kind.length, kind.width), WIDE) for kind in TOWERS] + [
        chunk_shapes(plan, plan.local) for plan in plans
    ]
    scratch = [
        ROWS_LOW,
        ROWS_WIDE,
        ROWS_LOW,
        HEAD_ROWS,
        HEAD_ROWS,
        LANE_ROWS,
        ((SEQS, ROOM, WIDTH), LOW),
        rooms[0],
        rooms[1],
        ((16, 48, 2 * WIDTH), LOW),
        ((16, 48, 2 * WIDTH), LOW),
        ((16, 48, EMB), LOW),
        ROWS_WIDE,
        HIDDEN_BLOCKS,
        ((2, 192, WIDTH), LOW),
        ((2, 16, 16, LANES), LOW),
        chunk_shapes(plans[0], plans[0].slots),
        chunk_shapes(plans[1], plans[1].slots),
        edges[0],
        edges[1],
        edges[0],
        edges[1],
        ((plans[0].slots * plans[0].rows, LANES), WIDE),
        ((48, 2 * WIDTH), LOW),
        ((48, 2 * WIDTH), LOW),
        ((48, EMB), LOW),
        ((8, 48, PART), LOW),
        ((192, WIDTH), LOW),
        ((16, LANES), LOW),
        ROWS_WIDE,
        ROWS_WIDE,
        LANE_ROWS,
        ((2 * SEQS * HEADS, LANES), LOW),
        ROWS_WIDE,
        ROWS_LOW,
        ((SEQS, EMB), LOW),
        ((8, WIDTH), WIDE),
        HIDDEN_BLOCKS,
        ((192, WIDTH), WIDE),
        ((192, WIDTH), LOW),
        ((8, PART), WIDE),
        GROUP,
        GROUP,
        GROUP,
        GROUP,
        ((128, PART), WIDE),
        ((SEQS, EMB), LOW),
        ((2, 16, SEQS, EMB), LOW),
        ROWS_WIDE,
        ((SEQS, EMB), WIDE),
        ROWS_LOW,
        GROUP,
        GROUP,
        ((256, EMB), WIDE),
        ((PART, WIDTH), WIDE),
        rooms[0],
        rooms[1],
        rooms[0],
        rooms[1],
        ((SEQS, ROOM, WIDTH), WIDE),
        ROWS_WIDE,
        ROWS_WIDE,
        HEAD_ROWS,
        HEAD_ROWS,
        LANE_ROWS,
        LANE_ROWS,
        ((SEQS * HEADS, WIDTH), WIDE),
        OUTER,
        OUTER,
        OUTER,
        OUTER,
        ((SEQS, 3 * WIDTH + EMB), LOW),
        ((16, SEQS, 3 * WIDTH + EMB), LOW),
        ROWS_LOW,
        ((16, SEQS, WIDTH), LOW),
        ROWS_WIDE,
        ((16, SEQS, WIDTH), WIDE),
        ((8, 48, PART), LOW),
        ((8, 48, PART), LOW),
        ((8, 48, PART), LOW),
        ((192, WIDTH), LOW),
        chunk_shapes(plans[0], plans[0].slots),
        chunk_shapes(plans[1], plans[1].slots),
        ((8, WIDTH), WIDE),
        ROWS_WIDE,
    ]
    semaphores = [
        (2, most,),
        (2, 6,),
        (2, 2,),
        (2,),
        (16,),
        (15,),
        (16,),
        (15,),
        (16,),
        (15,),
        (9,),
        (8,),
        (3,),
        (2,),
        (17,),
        (16,),
        (4, 8,),
        (4, 7,),
        (17,),
        (16,),
        (4,),
        (9,),
        (8,),
        (16,),
        (15,),
        (16,),
        (15,),
        (16,),
        (15,),
        (16,),
        (15,),
        (1,),
        (16,),
        (2,),
        (2, 2, slots,),
        (2,),
    ]
    smem = pl.BlockSpec(memory_space=pltpu.SMEM)
    vmem = pl.BlockSpec(memory_space=pltpu.VMEM)
    like = jax.ShapeDtypeStruct
    return pl.pallas_call(
        functools.partial(step_kernel, plans),
        out_shape=[like((1,), WIDE), like((3,), WIDE)] + [like(*out) for out in outs],
        in_specs=[smem, smem, ANY, ANY, vmem, vmem, vmem],
        out_specs=[smem, smem, vmem, vmem, vmem, vmem],
        scratch_shapes=[pltpu.VMEM(*each) for each in scratch]
        + [pltpu.SemaphoreType.DMA(shape) for shape in semaphores],
        compiler_params=comm_params(0),
    )(*scalars, *chunks, valid, *tokens)


def to_chunks(flat, plan, me):
    start = me * plan.share % plan.chunk
    padded = jnp.pad(flat, (plan.chunk, plan.local * plan.chunk - plan.share))
    piece = lax.dynamic_slice(padded, (plan.chunk - start,), (plan.local * plan.chunk,))
    return piece.astype(LOW).reshape(plan.local, plan.rows, LANES)


def from_chunks(chunks, plan, me):
    start = me * plan.share % plan.chunk
    return lax.dynamic_slice(chunks.reshape(-1), (start,), (plan.share,)).astype(WIDE)


def step(
    img_tokens,
    txt_tokens,
    txt_ends,
    valid,
    img_master,
    img_moment,
    img_average,
    txt_master,
    txt_moment,
    txt_average,
    scale_state,
):
    me = lax.axis_index(("tower", "dp"))
    plans = (
        Plan(0, img_master.shape[0], 96, (9, 3, 12, 12, 2)),
        Plan(1, txt_master.shape[0], 64, (6, 2, 8, 8, 2)),
    )
    img_rows = jnp.pad(img_tokens, ((0, 0), (0, TOWERS[0].room - TOWERS[0].length), (0, 0)))
    txt_rows = jnp.pad(txt_tokens, ((0, 0), (0, TOWERS[1].room - TOWERS[1].length), (0, 0)))
    loss, scale_new, img_grad, txt_grad, img_chunks, txt_chunks = run_step(
        (txt_ends, scale_state),
        (to_chunks(img_master, plans[0], me), to_chunks(txt_master, plans[1], me)),
        valid,
        (img_rows, txt_rows),
        plans,
    )
    img_new = advance(
        img_master, img_moment, img_average, from_chunks(img_chunks, plans[0], me), step_rate
    )
    txt_new = advance(
        txt_master, txt_moment, txt_average, from_chunks(txt_chunks, plans[1], me), step_rate
    )
    return (
        loss[0],
        img_grad,
        txt_grad,
        img_new[0],
        img_new[1],
        img_new[2],
        img_new[0].astype(LOW),
        txt_new[0],
        txt_new[1],
        txt_new[2],
        txt_new[0].astype(LOW),
        scale_new,
    )


def from_partner(value, axis, stride):
    mask = 2**stride
    pairs = [(source, source ^ mask) for source in range(lax.axis_size(axis))]
    return lax.ppermute(value, axis, pairs)


def round_value(v):
    return lax.optimization_barrier(v.astype(jnp.bfloat16)).astype(jnp.float32)


def make_low():

    def value_keep(v):
        return (round_value(v), None)

    def grad_pass(kept, grad):
        return (grad,)

    rounded = jax.custom_vjp(round_value)
    rounded.defvjp(value_keep, grad_pass)
    return rounded


def low(v):
    return make_low()(v)


def make_low_back():

    def identity(v):
        return v

    def value_pass(v):
        return (v, None)

    def grad_round(kept, grad):
        return (round_value(grad),)

    passed = jax.custom_vjp(identity)
    passed.defvjp(value_pass, grad_round)
    return passed


def low_back(v):
    return make_low_back()(v)


def both_ways(value):
    return low(low_back(value))


def product(left, right):
    return jnp.matmul(left, right)


def contract(form, left, right):
    return jnp.einsum(form, left, right)


def layer_norm(values, gain_row, shift_row):
    centred = values - jnp.mean(values, axis=-1, keepdims=True)
    spread = jnp.mean(centred * centred, axis=-1, keepdims=True)
    return centred * lax.rsqrt(spread + 1e-05) * gain_row + shift_row


def unpack(flat_weights, model_width, hidden_width, embed_width):
    piece_shapes = [
        (model_width, 3 * model_width),
        (model_width, model_width),
        (model_width, hidden_width),
        (hidden_width, model_width),
        (model_width, embed_width),
        (10, model_width),
        (hidden_width,),
    ]
    pieces = []
    offset = 0
    for piece_shape in piece_shapes:
        length = math.prod(piece_shape)
        pieces.append(flat_weights[offset : offset + length].reshape(piece_shape))
        offset = offset + length
    return pieces


def encode(tokens, flat_weights, positions, causal, model_width, hidden_width, embed_width):
    w_inputs, w_output, w_expand, w_reduce, w_embed, vectors, expand_bias = unpack(
        flat_weights, model_width, hidden_width, embed_width
    )
    groups = tokens.shape[0]
    length = tokens.shape[1]
    first = low(layer_norm(tokens, vectors[0], vectors[1]))
    bias_in = jnp.concatenate([vectors[2], jnp.zeros_like(vectors[2]), vectors[3]])
    joined = both_ways(product(first, w_inputs) + bias_in)
    joined = joined.reshape(groups, length, 3, model_width // HEAD, HEAD)
    scores = low_back(contract("gqhd,gkhd->ghqk", joined[:, :, 0], joined[:, :, 1]) * 0.125)
    if causal:
        row_index = lax.broadcasted_iota(jnp.int32, (length, length), 0)
        col_index = lax.broadcasted_iota(jnp.int32, (length, length), 1)
        scores = jnp.where(col_index <= row_index, scores, -1e30)
    row_top = jnp.max(scores, axis=-1, keepdims=True)
    raw_weights = jnp.exp(scores - row_top)
    attention = low(raw_weights / jnp.sum(raw_weights, axis=-1, keepdims=True))
    mixed_heads = both_ways(
        contract("ghqk,gkhd->gqhd", attention, joined[:, :, 2]).reshape(groups, length, model_width)
    )
    middle = tokens + low_back(product(mixed_heads, w_output) + vectors[4])
    second = low(layer_norm(middle, vectors[5], vectors[6]))
    raised = low_back(product(second, w_expand) + expand_bias)
    active = low(raised * jax.nn.sigmoid(1.702 * raised))
    final_rows = middle + low_back(product(active, w_reduce) + vectors[7])
    pooled = jnp.take_along_axis(final_rows, positions[:, None, None], axis=1)[:, 0]
    pooled = low(layer_norm(pooled, vectors[8], vectors[9]))
    projected = low_back(product(pooled, w_embed))
    return low(
        projected * lax.rsqrt(jnp.sum(projected * projected, axis=-1, keepdims=True) + 1e-06)
    )


def inner(left, right):
    return lax.dot_general(
        left, right, (((1,), (1,)), ((), ())), preferred_element_type=jnp.float32
    )


def across(left, right):
    return lax.dot_general(
        left, right, (((0,), (0,)), ((), ())), preferred_element_type=jnp.float32
    )


def softmax_total(logits, allowed):
    masked = jnp.where(allowed, logits, -1e30)
    row_top = jnp.max(masked, axis=1, keepdims=True)
    return jnp.log(jnp.sum(jnp.exp(masked - row_top), axis=1)) + row_top[:, 0]


def advance(master, moment, average, grads, rate):
    moment_new = momentum_rate * moment + grads
    master_new = master - rate * (grads + momentum_rate * moment_new)
    average_new = average_rate * average + (1.0 - average_rate) * master_new
    return (master_new, moment_new, average_new)


def padded_to(flat, length):
    return jnp.pad(flat, (0, length - flat.shape[0]))


def body(
    img_tokens,
    txt_tokens,
    txt_ends,
    valid,
    img_master,
    img_moment,
    img_average,
    txt_master,
    txt_moment,
    txt_average,
    scale_state,
):
    batch_rows = img_tokens.shape[0]
    total_rows = batch_rows * lax.axis_size(("tower", "dp"))
    device_at = lax.axis_index(("tower", "dp"))
    tower_at = lax.axis_index("tower")
    is_image = tower_at == 0
    img_share = img_master.shape[0]
    txt_share = txt_master.shape[0]
    img_count = img_tokens.size
    txt_count = txt_tokens.size
    shard_room = max(img_share, txt_share)
    token_room = max(img_count, txt_count)
    tower_count = lax.axis_size("dp")
    dp_at = lax.axis_index("dp")
    img_low = padded_to(img_master.astype(jnp.bfloat16), shard_room)
    txt_low = padded_to(txt_master.astype(jnp.bfloat16), shard_room)
    token_out = jnp.where(
        is_image,
        padded_to(txt_tokens.reshape(-1), token_room),
        padded_to(img_tokens.reshape(-1), token_room),
    )
    weight_out = jnp.where(is_image, txt_low, img_low)
    weight_mine = jnp.where(is_image, img_low, txt_low)
    token_in, weight_in = from_partner((token_out, weight_out), "tower", 0)
    stacked = jnp.where(
        is_image, jnp.stack([weight_mine, weight_in]), jnp.stack([weight_in, weight_mine])
    )
    gathered = lax.all_gather(stacked, "dp", axis=1, tiled=True)
    pair_ends = jnp.concatenate(
        [
            lax.dynamic_slice_in_dim(txt_ends, dp_at * batch_rows, batch_rows),
            lax.dynamic_slice_in_dim(txt_ends, (tower_count + dp_at) * batch_rows, batch_rows),
        ]
    )
    pair_zero = jnp.zeros((2 * batch_rows,), jnp.int32)

    def image_weights(whole):
        return whole.reshape(2, tower_count, shard_room).reshape(-1).astype(jnp.float32)

    def text_weights(whole):
        return (
            whole.reshape(2, tower_count, shard_room)[:, :, :txt_share]
            .reshape(-1)
            .astype(jnp.float32)
        )

    def image_rows(arrived):
        return jnp.concatenate(
            [img_tokens, arrived[:img_count].reshape(img_tokens.shape)], axis=0
        ).astype(jnp.float32)

    def text_rows(arrived):
        return jnp.concatenate([arrived.reshape(txt_tokens.shape), txt_tokens], axis=0).astype(
            jnp.float32
        )

    def image_encode(rows, flat):
        return encode(rows, flat, pair_zero, False, D_IMG, FF_IMG, EMB)

    def text_encode(rows, flat):
        return encode(rows, flat, pair_ends, True, D_TXT, FF_TXT, EMB)

    def image_forward(operands):
        return image_encode(image_rows(operands[1]), image_weights(operands[0]))

    def text_forward(operands):
        return text_encode(text_rows(operands[1]), text_weights(operands[0]))

    pair_emb = lax.cond(is_image, image_forward, text_forward, (gathered, token_in)).astype(
        jnp.bfloat16
    )
    emb_in = from_partner(pair_emb, "tower", 0)
    img_pair = jnp.where(is_image, pair_emb, emb_in)
    txt_pair = jnp.where(is_image, emb_in, pair_emb)
    row_start = tower_at * batch_rows
    img_local = lax.dynamic_slice_in_dim(img_pair, row_start, batch_rows)
    txt_local = lax.dynamic_slice_in_dim(txt_pair, row_start, batch_rows)
    img_all, txt_all = (
        lax.all_gather(img_local, ("tower", "dp"), axis=0, tiled=True),
        lax.all_gather(txt_local, ("tower", "dp"), axis=0, tiled=True),
    )
    logit_scale = jnp.exp(scale_state[0])
    offset = device_at * batch_rows
    row_index = lax.broadcasted_iota(jnp.int32, (batch_rows, total_rows), 0) + offset
    col_index = lax.broadcasted_iota(jnp.int32, (batch_rows, total_rows), 1)
    diagonal = (row_index == col_index).astype(jnp.float32)
    allowed = valid > 0
    row_logits = logit_scale * inner(img_local, txt_all)
    col_logits = logit_scale * inner(txt_local, img_all)
    row_lse = softmax_total(row_logits, allowed)
    col_lse = softmax_total(col_logits, allowed)
    partial_loss = 0.5 * (
        jnp.sum(row_lse)
        - jnp.sum(row_logits * diagonal)
        + jnp.sum(col_lse)
        - jnp.sum(col_logits * diagonal)
    )
    row_terms = 0.5 * (jnp.where(allowed, jnp.exp(row_logits - row_lse[:, None]), 0.0) - diagonal)
    col_terms = 0.5 * (jnp.where(allowed, jnp.exp(col_logits - col_lse[:, None]), 0.0) - diagonal)
    partial_scale = jnp.sum(row_terms * row_logits) + jnp.sum(col_terms * col_logits)
    row_back = (logit_scale * row_terms).astype(jnp.bfloat16)
    col_back = (logit_scale * col_terms).astype(jnp.bfloat16)
    img_emb_grad = jnp.dot(row_back, txt_all, preferred_element_type=jnp.float32)
    txt_emb_grad = jnp.dot(col_back, img_all, preferred_element_type=jnp.float32)
    img_extra, txt_extra = (
        lax.psum_scatter(
            across(col_back, txt_local), ("tower", "dp"), scatter_dimension=0, tiled=True
        ),
        lax.psum_scatter(
            across(row_back, img_local), ("tower", "dp"), scatter_dimension=0, tiled=True
        ),
    )
    img_emb_grad = img_emb_grad + img_extra
    txt_emb_grad = txt_emb_grad + txt_extra
    sums = lax.psum((partial_loss, partial_scale), ("tower", "dp"))
    grad_out = jnp.where(is_image, txt_emb_grad, img_emb_grad)
    grad_in = from_partner(grad_out, "tower", 0)
    pair_cot = jnp.where(
        is_image,
        jnp.concatenate([img_emb_grad, grad_in], axis=0),
        jnp.concatenate([grad_in, txt_emb_grad], axis=0),
    )

    def image_backward(operands):
        recomputed, tower_pullback = jax.vjp(
            image_encode, image_rows(operands[1]), image_weights(operands[0])
        )
        rows_grad, flat_grad = tower_pullback(operands[2])
        own_part = padded_to(rows_grad[:batch_rows].reshape(-1), token_room)
        sent_part = padded_to(rows_grad[batch_rows:].reshape(-1), token_room)
        stacked_grad = flat_grad.reshape(2, tower_count, img_share)
        return (own_part, sent_part, stacked_grad)

    def text_backward(operands):
        recomputed, tower_pullback = jax.vjp(
            text_encode, text_rows(operands[1]), text_weights(operands[0])
        )
        rows_grad, flat_grad = tower_pullback(operands[2])
        own_part = padded_to(rows_grad[batch_rows:].reshape(-1), token_room)
        sent_part = padded_to(rows_grad[:batch_rows].reshape(-1), token_room)
        stacked_grad = jnp.pad(
            flat_grad.reshape(2, tower_count, txt_share),
            ((0, 0), (0, 0), (0, shard_room - txt_share)),
        )
        return (own_part, sent_part, stacked_grad)

    own_part, sent_part, stacked_grad = lax.cond(
        is_image, image_backward, text_backward, (gathered, token_in, pair_cot)
    )
    summed = lax.psum_scatter(stacked_grad, "dp", scatter_dimension=1, tiled=True)
    kept_part = jnp.where(is_image, summed[0, 0], summed[1, 0])
    sent_share = jnp.where(is_image, summed[1, 0], summed[0, 0])
    home_weights, home_tokens = (
        from_partner(sent_share.astype(jnp.bfloat16), "tower", 0).astype(sent_share.dtype),
        from_partner(sent_part.astype(jnp.bfloat16), "tower", 0).astype(sent_part.dtype),
    )
    img_owned = jnp.where(is_image, kept_part, home_weights)
    txt_owned = jnp.where(is_image, home_weights, kept_part)[:txt_share]
    img_grad = jnp.where(is_image, own_part, home_tokens)[:img_count].reshape(img_tokens.shape)
    txt_grad = jnp.where(is_image, home_tokens, own_part).reshape(txt_tokens.shape)
    img_new = advance(img_master, img_moment, img_average, img_owned, step_rate)
    txt_new = advance(txt_master, txt_moment, txt_average, txt_owned, step_rate)
    scale_parts = advance(scale_state[0], scale_state[1], scale_state[2], sums[1], scale_rate)
    scale_new = jnp.stack([scale_parts[0], scale_parts[1], scale_parts[2]])
    return (
        sums[0] / total_rows,
        img_grad,
        txt_grad,
        img_new[0],
        img_new[1],
        img_new[2],
        img_new[0].astype(jnp.bfloat16),
        txt_new[0],
        txt_new[1],
        txt_new[2],
        txt_new[0].astype(jnp.bfloat16),
        scale_new,
    )


def solution(mesh):
    in_specs = (
        P(("tower", "dp"), None, None),
        P(("tower", "dp"), None, None),
        P(),
        P(("tower", "dp"), None),
        P(("tower", "dp")),
        P(("tower", "dp")),
        P(("tower", "dp")),
        P(("tower", "dp")),
        P(("tower", "dp")),
        P(("tower", "dp")),
        P(),
    )
    out_specs = (
        P(),
        P(("tower", "dp"), None, None),
        P(("tower", "dp"), None, None),
        P(("tower", "dp")),
        P(("tower", "dp")),
        P(("tower", "dp")),
        P(("tower", "dp")),
        P(("tower", "dp")),
        P(("tower", "dp")),
        P(("tower", "dp")),
        P(("tower", "dp")),
        P(),
    )
    run = step if (mesh.shape["tower"], mesh.shape["dp"]) == (2, 16) else body
    return jax.shard_map(run, mesh=mesh, in_specs=in_specs, out_specs=out_specs, check_vma=False)
```

```python
import functools
import math

import jax
import jax.numpy as jnp
from jax import lax
from jax.experimental import pallas as pl
from jax.experimental.pallas import tpu as pltpu
from jax.sharding import PartitionSpec as P

D_IMG = 768
FF_IMG = 3072
D_TXT = 512
FF_TXT = 2048
EMB = 512
HEAD = 64


momentum_rate = 0.5
average_rate = 0.5
step_rate = 0.08
scale_rate = 0.0001


MESH = pl.DeviceIdType.MESH
ANY = pl.BlockSpec(memory_space=pl.ANY)
GRANT = 58 * 1024 * 1024
LANES = 128
LOW = jnp.bfloat16
WIDE = jnp.float32


def here():
    return lax.axis_index("tower"), lax.axis_index("dp")


def greet(devices):
    barrier = pltpu.get_barrier_semaphore()
    for device in devices:
        pl.semaphore_signal(barrier, inc=1, device_id=device, device_id_type=MESH)
    pl.semaphore_wait(barrier, len(devices))


def remote(src, dst, send_sem, recv_sem, device):
    return pltpu.make_async_remote_copy(
        src_ref=src,
        dst_ref=dst,
        send_sem=send_sem,
        recv_sem=recv_sem,
        device_id=device,
        device_id_type=MESH,
    )


def comm_params(number):
    return pltpu.CompilerParams(
        collective_id=number, has_side_effects=True, vmem_limit_bytes=GRANT
    )


def same_core(tower, at):
    chip, core = at // 2, at % 2
    return [(tower, (chip + k) % 8 * 2 + core) for k in range(1, 8)]


def both_towers(tower, at):
    place, core = tower * 8 + at // 2, at % 2
    others = [(place + k) % 16 for k in range(1, 16)]
    return [(other // 8, other % 8 * 2 + core) for other in others]


def everyone(tower, at):
    me = tower * 16 + at
    others = [(me + k) % 32 for k in range(1, 32)]
    return [(other // 16, other % 16) for other in others]


def group_exchange(scattered, x_ref, o_ref, send_sem, recv_sem):
    tower, at = here()
    chip = at // 2

    def source(k):
        return x_ref.at[k] if scattered else x_ref

    own = pltpu.make_async_copy(source(chip), o_ref.at[chip], send_sem.at[7])
    sent = []
    for k, device in enumerate(same_core(tower, at)):
        copy = remote(
            source((chip + 1 + k) % 8), o_ref.at[chip], send_sem.at[k], recv_sem.at[k], device
        )
        copy.start()
        sent.append(copy)
    own.start()
    own.wait()
    for k in range(7):
        remote(
            source(chip),
            o_ref.at[(chip + 7 - k) % 8],
            send_sem.at[k],
            recv_sem.at[k],
            (tower, at),
        ).wait_recv()
    return sent


class Spread:
    def __init__(self, src, dst, send, recv):
        self.src, self.dst, self.send, self.recv = src, dst, send, recv
        tower, at = here()
        self.core = at % 2
        self.sibling = (tower, at + 1 - 2 * self.core)
        self.devices = self.peers(tower, at)
        self.n = len(self.devices) + 1
        self.place = self.spot(tower, at)
        self.sent = []

    def peers(self, tower, at):
        return both_towers(tower, at)

    def spot(self, tower, at):
        return tower * 8 + at // 2

    def block(self, place):
        return self.src

    def side(self, core):
        return self.dst.at[core]

    def launch(self, src, dst, k, device):
        copy = remote(src, dst, self.send.at[k], self.recv.at[k], device)
        copy.start()
        self.sent.append(copy)

    def start(self):
        for k, device in enumerate(self.devices):
            to = (self.place + 1 + k) % self.n
            self.launch(self.block(to), self.side(self.core).at[self.place], k, device)
        self.own = pltpu.make_async_copy(
            self.block(self.place), self.side(self.core).at[self.place], self.send.at[self.n]
        )
        self.own.start()

    def arrived(self):
        for k in range(self.n - 1):
            source = (self.place + self.n - 1 - k) % self.n
            remote(
                self.block(0),
                self.side(self.core).at[source],
                self.send.at[k],
                self.recv.at[k],
                self.sibling,
            ).wait_recv()
        self.own.wait()

    def relay(self):
        self.arrived()
        side = self.side(self.core)
        self.launch(side, side, self.n - 1, self.sibling)

    def finish(self):
        side = self.side(1 - self.core)
        remote(
            side, side, self.send.at[self.n - 1], self.recv.at[self.n - 1], self.sibling
        ).wait_recv()

    def drain(self):
        for copy in self.sent:
            copy.wait_send()


class Group(Spread):
    def __init__(self, src, dst, send, recv, both=True):
        self.both = both
        super().__init__(src, dst, send, recv)

    def peers(self, tower, at):
        return same_core(tower, at)

    def spot(self, tower, at):
        return at // 2

    def block(self, place):
        return self.src.at[place]

    def side(self, core):
        return self.dst.at[core] if self.both else self.dst

    def finish(self):
        if self.both:
            super().finish()
        else:
            self.arrived()


class Ring:
    def __init__(self, src, dst, send, recv, only=None):
        self.src, self.dst, self.send, self.recv = src, dst, send, recv
        self.only = only
        self.tower, self.at = here()
        self.deep, self.row, self.core = self.at // 4, self.at // 2 % 2, self.at % 2
        self.sibling = (self.tower, self.at + 1 - 2 * self.core)
        self.beside = (self.tower, self.spot(0, 1 - self.row))
        self.sent = []

    def spot(self, k, row):
        return (self.deep + k) % 4 * 4 + row * 2 + self.core

    def act(self, action):
        if self.only is None:
            action()
        else:
            pl.when(self.tower == self.only)(action)

    def launch(self, src, slot, index, device):
        copy = remote(src, self.dst.at[slot], self.send.at[index], self.recv.at[index], device)
        self.act(copy.start)
        self.sent.append(copy)

    def arrived(self, slot, index):
        copy = remote(
            self.src, self.dst.at[slot], self.send.at[index], self.recv.at[index], self.sibling
        )
        self.act(copy.wait_recv)

    def start(self):
        for k in (1, 3, 2):
            self.launch(self.src, self.at, k - 1, (self.tower, self.spot(k, self.row)))
        self.launch(self.src, self.at, 3, self.beside)
        self.launch(self.src, self.at, 7, self.sibling)
        self.own = pltpu.make_async_copy(self.src, self.dst.at[self.at], self.send.at[15])
        self.act(self.own.start)

    def relay_deep(self):
        for k in (1, 3, 2):
            slot = self.spot(4 - k, self.row)
            self.arrived(slot, k - 1)
            self.launch(self.dst.at[slot], slot, 3 + k, self.beside)
            self.launch(self.dst.at[slot], slot, 7 + k, self.sibling)

    def relay_row(self):
        for k in (0, 1, 3, 2):
            slot = self.spot(4 - k, 1 - self.row)
            self.arrived(slot, 3 + k)
            self.launch(self.dst.at[slot], slot, 11 + k, self.sibling)

    def finish(self):
        for index in range(8):
            k, row = index % 4, self.row if index < 4 else 1 - self.row
            slot = (self.deep + 4 - k) % 4 * 4 + row * 2 + 1 - self.core
            self.arrived(slot, 7 + index)
        self.act(self.own.wait)

    def drain(self):
        for copy in self.sent:
            self.act(copy.wait_send)


def rings(src, dst, send, recv):
    return [
        Ring(src.at[part], dst.at[part], send.at[part], recv.at[part], 0 if part == 2 else None)
        for part in range(3)
    ]


class Blocks:
    def __init__(self, src, dst, send, recv, shared=1):
        self.src, self.dst, self.send, self.recv = src, dst, send, recv
        self.tower, self.at = here()
        self.shared = shared
        self.sent = []

    def start(self):
        for k in range(1, 16):
            to = (self.at + k) % 16
            copy = remote(
                self.src.at[to // self.shared],
                self.dst.at[self.at],
                self.send.at[k - 1],
                self.recv.at[k - 1],
                (self.tower, to),
            )
            copy.start()
            self.sent.append(copy)
        self.own = pltpu.make_async_copy(
            self.src.at[self.at // self.shared], self.dst.at[self.at], self.send.at[15]
        )
        self.own.start()

    def finish(self):
        for k in range(1, 16):
            remote(
                self.src.at[0],
                self.dst.at[(self.at + 16 - k) % 16],
                self.send.at[k - 1],
                self.recv.at[k - 1],
                (self.tower, self.at),
            ).wait_recv()
        self.own.wait()

    def drain(self):
        for copy in self.sent:
            copy.wait_send()


class Pair:
    def __init__(self, from_zero, zero_dst, from_one, one_dst, sems):
        tower, at = here()
        partner = (1 - tower, at)
        self.tower = tower
        self.up = remote(from_zero, zero_dst, sems.at[0], sems.at[1], partner)
        self.down = remote(from_one, one_dst, sems.at[0], sems.at[1], partner)

    def by_tower(self, zero, one):
        pl.when(self.tower == 0)(zero)
        pl.when(self.tower == 1)(one)

    def start(self):
        self.by_tower(self.up.start, self.down.start)

    def finish(self):
        self.by_tower(self.down.wait_recv, self.up.wait_recv)

    def drain(self):
        self.by_tower(self.up.wait_send, self.down.wait_send)


VECTORS = 5
EXPAND = 2
TURN = 8


class Plan:
    def __init__(self, tower, share, rows, per_device):
        self.tower = tower
        self.share = share
        self.rows = rows
        self.chunk = rows * LANES
        self.per_device = per_device
        self.first_slot = [sum(per_device[:p]) for p in range(6)]
        self.first_chunk = [16 * slot for slot in self.first_slot]
        self.slots = sum(per_device) + 1
        self.total = 16 * sum(per_device) + 1
        spans = [self.span(device) for device in range(32)]
        self.counts = sorted({last - first + 1 for first, last in spans})
        self.local = self.counts[-1]

    def span(self, device):
        first = device * self.share // self.chunk
        last = ((device + 1) * self.share - 1) // self.chunk
        return first, min(last, self.total - 1)

    def bounds(self, device):
        first = device * self.share // self.chunk
        last = ((device + 1) * self.share - 1) // self.chunk
        return first, jnp.minimum(last, self.total - 1)

    def pieces(self, p):
        return self.per_device[p] if p < VECTORS else 1

    def target(self, g):
        piece, base, slot, n = (jnp.int32(0), jnp.int32(0), jnp.int32(0), jnp.int32(1))
        for p in range(VECTORS):
            inside = g >= self.first_chunk[p]
            piece = jnp.where(inside, p, piece)
            base = jnp.where(inside, self.first_chunk[p], base)
            slot = jnp.where(inside, self.first_slot[p], slot)
            n = jnp.where(inside, self.per_device[p], n)
        block = (g - base) // n
        at = jnp.where(piece == EXPAND, (block + TURN) % 16, block)
        return piece, at, slot + (g - base) - block * n


class Deal:
    def __init__(self, plan, s, src, dst, extra, last, sems):
        self.plan, self.s, self.src, self.dst = plan, s, src, dst
        self.extra, self.last = extra, last
        self.chunk_send, self.recv, self.edge, self.fetch = sems
        self.tower, self.at = here()
        self.me = self.tower * 16 + self.at
        self.first, self.last_chunk = plan.bounds(self.me)
        before = (self.me + 31) % 32
        self.head = remote(
            src.at[0], extra, self.edge.at[s, 0], self.edge.at[s, 1], (before // 16, before % 16)
        )

    def send_head(self):
        pl.when(self.me > 0)(self.head.start)

    def move(self, src, i, piece, at_to, slot, wait):
        far = jnp.logical_or(self.tower != self.plan.tower, at_to != self.at)
        recv = self.recv.at[self.s, piece]
        copy = remote(
            src,
            self.dst.at[slot],
            self.chunk_send.at[self.s, i],
            recv,
            (jnp.int32(self.plan.tower), at_to),
        )
        pl.when(far)(copy.wait_send if wait else copy.start)
        if not wait:
            pl.when(jnp.logical_not(far))(
                pltpu.make_async_copy(src, self.dst.at[slot], recv).start
            )

    def whole(self, early, wait):
        def step(i, carry):
            g = self.first + i
            piece, at_to, slot = self.plan.target(g)
            inside = jnp.logical_and(
                jnp.logical_or(i > 0, self.me == 0),
                jnp.logical_or(
                    g < self.last_chunk, jnp.logical_and(self.me == 31, g < self.plan.total - 1)
                ),
            )
            inside = jnp.logical_and(inside, g <= self.last_chunk)
            inside = jnp.logical_and(inside, g < self.plan.total - 1)
            if early is not None:
                hidden = jnp.logical_and(piece >= 2, piece <= 3)
                inside = jnp.logical_and(inside, jnp.logical_not(hidden) if early else hidden)

            @pl.when(inside)
            def _():
                self.move(self.src.at[i], i, piece, at_to, slot, wait)

            return carry

        lax.fori_loop(0, self.plan.local, step, 0)

    def vectors(self, wait):
        @pl.when(self.me == 31)
        def _():
            src = self.src.at[self.last_chunk - self.first]

            def each(k, carry):
                self.move(src, self.plan.local + k, VECTORS, k, self.plan.slots - 1, wait)
                return carry

            lax.fori_loop(0, 16, each, 0)

    def fetch_last(self):
        return pltpu.make_async_copy(
            self.src.at[self.last_chunk - self.first], self.last, self.fetch.at[self.s]
        )

    def join(self):
        @pl.when(self.me < 31)
        def _():
            self.fetch_last().wait()
            self.head.wait_recv()
            self.last[...] = self.last[...] + self.extra[...]
            piece, at_to, slot = self.plan.target(self.last_chunk)
            self.move(self.last, self.plan.local + 16, piece, at_to, slot, False)

    def start_fetch(self):
        pl.when(self.me < 31)(self.fetch_last().start)

    def arrived(self, p):
        part = self.dst.at[pl.ds(self.plan.first_slot[p], self.plan.pieces(p))]
        pltpu.make_async_copy(part, part, self.recv.at[self.s, p]).wait()

    def drain(self):
        pl.when(self.me > 0)(self.head.wait_send)
        self.whole(None, True)
        self.vectors(True)

        @pl.when(self.me < 31)
        def _():
            piece, at_to, slot = self.plan.target(self.last_chunk)
            self.move(self.last, self.plan.local + 16, piece, at_to, slot, True)


class Collect:
    def __init__(self, plan, s, src, dst, send, recv):
        self.plan, self.s, self.src, self.dst = plan, s, src, dst
        self.send, self.recv = send, recv
        self.tower, self.at = here()
        self.me = self.tower * 16 + self.at

    def one(self, owner, slot, g, which, wait):
        first, _ = self.plan.bounds(owner)
        far = owner != self.me
        recv = self.recv.at[self.s]
        copy = remote(
            self.src.at[slot],
            self.dst.at[g - first],
            self.send.at[which, slot],
            recv,
            (owner // 16, owner % 16),
        )
        pl.when(far)(copy.wait_send if wait else copy.start)
        if not wait:
            pl.when(jnp.logical_not(far))(
                pltpu.make_async_copy(self.src.at[slot], self.dst.at[g - first], recv).start
            )

    def piece(self, p, wait):
        n = self.plan.pieces(p)

        def step(i, carry):
            slot = self.plan.first_slot[p] + i
            block = (self.at + 16 - TURN) % 16 if p == EXPAND else self.at
            g = self.plan.first_chunk[p] + block * n + i if p < VECTORS else self.plan.total - 1
            low = g * self.plan.chunk // self.plan.share
            high = jnp.minimum(((g + 1) * self.plan.chunk - 1) // self.plan.share, 31)
            self.one(low, slot, g, 0, wait)
            pl.when(high != low)(lambda: self.one(high, slot, g, 1, wait))
            return carry

        if p == VECTORS:


            @pl.when(self.at == 0)
            def _():
                step(0, 0)

        else:
            lax.fori_loop(0, n, step, 0)

    def finish(self):
        first, last = self.plan.bounds(self.me)
        held = last - first + 1
        for n in self.plan.counts:

            @pl.when(held == n)
            def _():
                part = self.dst.at[pl.ds(0, n)]
                pltpu.make_async_copy(part, part, self.recv.at[self.s]).wait()


SEQS = 16
HEADS = 16


class Tower:
    def __init__(self, index, width, hidden, length, room, causal):
        self.index = index
        self.width = width
        self.hidden = hidden
        self.length = length
        self.room = room
        self.causal = causal
        self.heads = width // HEAD
        self.block = width // 16
        self.part = hidden // 8
        self.reduce_rows = hidden // 16


TOWERS = (
    Tower(0, D_IMG, FF_IMG, 50, 64, False),
    Tower(1, D_TXT, FF_TXT, 77, 80, True),
)
ROOM = 80
WIDTH = D_IMG
PART = FF_IMG // 8


def each_tower(run):
    tower = lax.axis_index("tower")
    for kind in TOWERS:
        pl.when(tower == kind.index)(functools.partial(run, kind))


def dot_nn(a, b):
    return lax.dot_general(a, b, (((1,), (0,)), ((), ())), preferred_element_type=WIDE)


def dot_nt(a, b):
    return lax.dot_general(a, b, (((1,), (1,)), ((), ())), preferred_element_type=WIDE)


def dot_tn(a, b):
    return lax.dot_general(a, b, (((0,), (0,)), ((), ())), preferred_element_type=WIDE)


def standardise(rows):
    centred = rows - jnp.mean(rows, axis=-1, keepdims=True)
    spread = jnp.mean(centred * centred, axis=-1, keepdims=True)
    rate = lax.rsqrt(spread + 1e-05)
    return centred * rate, rate


def norm_back(grad, gain, hat, rate):
    scaled = grad * gain
    return rate * (
        scaled
        - jnp.mean(scaled, axis=-1, keepdims=True)
        - hat * jnp.mean(scaled * hat, axis=-1, keepdims=True)
    )


def spans(kind):
    return [
        (lo, min(lo + 512, kind.width), lo // HEAD, (min(lo + 512, kind.width) - lo) // HEAD)
        for lo in range(0, kind.width, 512)
    ]


def head_rows(rows, span):
    lo, hi, _, n = span
    part = rows[:, lo:hi]
    owner = lax.broadcasted_iota(jnp.int32, part.shape, 1) // HEAD
    nothing = jnp.zeros_like(part)
    return jnp.concatenate([jnp.where(owner == h, part, nothing) for h in range(n)], axis=0)


def from_head_rows(rows, span):
    _, _, _, n = span
    owner = lax.broadcasted_iota(jnp.int32, (SEQS, rows.shape[1]), 1) // HEAD
    total = jnp.zeros((SEQS, rows.shape[1]), rows.dtype)
    for h in range(n):
        total = jnp.where(owner == h, rows[h * SEQS : (h + 1) * SEQS], total)
    return total


def side_by_side(parts):
    return parts[0] if len(parts) == 1 else jnp.concatenate(parts, axis=1)


def get_rows(ref, place, width):
    return side_by_side([ref[c, place, :] for c in range(width // LANES)])


def put_rows(ref, place, value):
    for c in range(value.shape[1] // LANES):
        ref[c, place, :] = value[:, c * LANES : (c + 1) * LANES]


def matrix(ref, kind, start, width):
    return jnp.concatenate(
        [
            ref[part, at, :, start : start + width]
            for at in range(16)
            for part in range(kind.block // 16)
        ],
        axis=0,
    )


def vector(vec_ref, kind, row):
    return vec_ref[row : row + 1, : kind.width]


def pieces_of(kind):
    return (
        (kind.block, 3 * kind.width),
        (kind.block, kind.width),
        (kind.block, kind.hidden),
        (kind.reduce_rows, kind.width),
        (kind.block, EMB),
        (16, kind.width),
    )


def lane_blocks(kind, plan, p):
    height, width = pieces_of(kind)[p]
    pitch = width // LANES
    base = plan.first_slot[p] * plan.rows if p < VECTORS else (plan.slots - 1) * plan.rows
    return [(c, pl.ds(base + c, height, stride=pitch)) for c in range(pitch)]


def lift(kind, plan, p, slots, flat):
    n = plan.pieces(p)
    slot = plan.first_slot[p]
    rows = slots[slot : slot + n].reshape(n * plan.rows, LANES)
    flat[slot * plan.rows : (slot + n) * plan.rows, :] = rows.astype(WIDE)
    return [(c, flat[place, :]) for c, place in lane_blocks(kind, plan, p)]


def drop(kind, plan, p, value, slots, flat):
    for c, place in lane_blocks(kind, plan, p):
        flat[place, :] = value(c)
    n = plan.pieces(p)
    slot = plan.first_slot[p]
    rows = flat[slot * plan.rows : (slot + n) * plan.rows, :]
    slots[slot : slot + n] = rows.reshape(n, plan.rows, LANES).astype(LOW)


def expand_matrix(ref, kind):
    return jnp.concatenate(
        [
            ref[at % 2, at // 2, : kind.block, : kind.part]
            for at in ((block + TURN) % 16 for block in range(16))
        ],
        axis=0,
    )


def reduce_matrix(ref, kind):
    return ref[:, : kind.reduce_rows, : kind.width].reshape(kind.part, kind.width)


def hidden_bias(vec_ref, kind):
    chip = lax.axis_index("dp") // 2
    whole = vec_ref[...]
    row = lax.broadcasted_iota(jnp.int32, (16, 1), 0)
    line = jnp.sum(jnp.where(row == 10 + chip // 2, whole, 0.0), axis=0, keepdims=True)
    return jnp.where(
        chip % 2 == 0, line[:, : kind.part], line[:, kind.part : 2 * kind.part]
    )


def hidden_kernel(second_ref, raise_ref, reduce_ref, vec_ref, part_ref, raised_ref):
    def run(kind):
        width = kind.width
        rows = second_ref[:, :, :width].reshape(8 * SEQS, width)
        raised = dot_nn(rows, expand_matrix(raise_ref, kind)) + hidden_bias(vec_ref, kind)
        raised_ref[:, : kind.part] = raised
        active = (raised * jax.nn.sigmoid(1.702 * raised)).astype(LOW)
        part = dot_nn(active, reduce_matrix(reduce_ref, kind))
        part_ref[:, :, :width] = part.reshape(8, SEQS, width).astype(LOW)

    each_tower(run)


def hidden_back_kernel(
    grad_ref,
    second_ref,
    raised_ref,
    raise_ref,
    reduce_ref,
    back_ref,
    raise_grad_ref,
    reduce_keep_ref,
    reduce_send_ref,
    bias_ref,
    whole,
):
    def run(kind):
        width, part = kind.width, kind.part
        grads = grad_ref[:, :, :width].reshape(8 * SEQS, width)
        rows = second_ref[:, :, :width].reshape(8 * SEQS, width)
        raised = raised_ref[:, :part]
        gate = jax.nn.sigmoid(1.702 * raised)
        active = (raised * gate).astype(LOW)
        slope = gate + 1.702 * raised * gate * (1.0 - gate)
        raised_grad = dot_nt(grads, reduce_matrix(reduce_ref, kind)) * slope
        low_grad = raised_grad.astype(LOW)
        bias_ref[0:1, :part] = jnp.sum(low_grad.astype(WIDE), axis=0, keepdims=True)
        back = dot_nt(low_grad, expand_matrix(raise_ref, kind))
        back_ref[:, :, :width] = back.reshape(8, SEQS, width).astype(LOW)
        raise_grad = dot_tn(rows, low_grad).reshape(16, kind.block, part).astype(LOW)
        for block in range(16):
            at = (block + TURN) % 16
            raise_grad_ref[at % 2, at // 2, : kind.block, :part] = raise_grad[block]
        whole[:part, :width] = dot_tn(active, grads)
        core = lax.axis_index("dp") % 2
        n = kind.reduce_rows
        keep = pl.multiple_of(core * n, 64)
        send = pl.multiple_of((1 - core) * n, 64)
        reduce_keep_ref[:n, :width] = whole[pl.ds(keep, n), :width]
        reduce_send_ref[:n, :width] = whole[pl.ds(send, n), :width].astype(LOW)

    each_tower(run)


def embed_kernel(part_ref, middle_ref, gat_ref, vec_ref, emb_ref, final_ref, pooled_ref, proj_ref):
    def run(kind):
        width = kind.width
        final = (
            middle_ref[:, :width]
            + jnp.sum(part_ref[:, :, :width].astype(WIDE), axis=0)
            + vector(vec_ref, kind, 7)
        )
        final_ref[:, :width] = final
        hat, _ = standardise(final)
        pooled = (hat * vector(vec_ref, kind, 8) + vector(vec_ref, kind, 9)).astype(LOW)
        pooled_ref[:, :width] = pooled
        proj = dot_nn(pooled, matrix(gat_ref, kind, 0, EMB))
        proj_ref[...] = proj
        size = jnp.sum(proj * proj, axis=-1, keepdims=True) + 1e-06
        emb_ref[...] = (proj * lax.rsqrt(size)).astype(LOW)

    each_tower(run)


def objective_kernel(
    scale_ref,
    all_ref,
    valid_ref,
    final_ref,
    proj_ref,
    gat_ref,
    vec_ref,
    low_ref,
    grad_ref,
    proj_grad_ref,
    final_vec_ref,
    loss_ref,
    scale_new_ref,
    own_scr,
):
    def ordered(which):
        blocks = []
        for half in range(2):
            for j in range(16):
                rows = all_ref[j % 2, which * 8 + j // 2].astype(WIDE)
                blocks.append(rows[half * 8 : half * 8 + 8])
        return jnp.concatenate(blocks, axis=0).astype(LOW)

    img, txt = ordered(0), ordered(1)
    total = img.shape[0]
    scale = jnp.exp(jnp.full((1, 1), scale_ref[0], WIDE))
    lines = []
    for d in range(32):
        rows = valid_ref[d % 2, d // 2].astype(WIDE)
        lines.append(jnp.concatenate([rows[:8], rows[8:]], axis=1))
    allowed = jnp.concatenate(lines, axis=0) > 0
    same = lax.broadcasted_iota(jnp.int32, (total, total), 0) == lax.broadcasted_iota(
        jnp.int32, (total, total), 1
    )
    same = same.astype(WIDE)

    def side(left, right):
        logits = scale * dot_nt(left, right)
        masked = jnp.where(allowed, logits, -1e30)
        top = jnp.max(masked, axis=1, keepdims=True)
        lse = jnp.log(jnp.sum(jnp.exp(masked - top), axis=1, keepdims=True)) + top
        terms = 0.5 * (jnp.where(allowed, jnp.exp(logits - lse), 0.0) - same)
        loss = 0.5 * (
            jnp.sum(lse, axis=0, keepdims=True)
            - jnp.sum(jnp.sum(logits * same, axis=1, keepdims=True), axis=0, keepdims=True)
        )
        rate = jnp.sum(jnp.sum(terms * logits, axis=1, keepdims=True), axis=0, keepdims=True)
        return (scale * terms).astype(LOW), loss, rate

    row_back, row_loss, row_rate = side(img, txt)
    col_back, col_loss, col_rate = side(txt, img)
    loss_ref[0] = jnp.sum(row_loss + col_loss) / total
    parts = advance(
        scale_ref[0], scale_ref[1], scale_ref[2], jnp.sum(row_rate + col_rate), scale_rate
    )
    for k in range(3):
        scale_new_ref[k] = parts[k]

    def run(kind):
        width = kind.width
        if kind.index == 0:
            emb_grad = dot_nn(row_back, txt) + dot_tn(col_back, txt)
        else:
            emb_grad = dot_nn(col_back, img) + dot_tn(row_back, img)
        own_scr[...] = emb_grad
        at = lax.axis_index("dp")
        mine = jnp.concatenate(
            [
                own_scr[pl.ds(pl.multiple_of(half * 128 + at * 8, 8), 8), :]
                for half in range(2)
            ],
            axis=0,
        )
        proj = proj_ref[...]
        size = jnp.sum(proj * proj, axis=-1, keepdims=True) + 1e-06
        along = jnp.sum(proj * mine, axis=-1, keepdims=True)
        proj_grad = ((mine - proj * along / size) * lax.rsqrt(size)).astype(LOW)
        proj_grad_ref[...] = proj_grad
        pooled_grad = dot_nt(proj_grad, matrix(gat_ref, kind, 0, EMB))
        hat, rate = standardise(final_ref[:, :width])
        final_vec_ref[0:1, :width] = jnp.sum(pooled_grad * hat, axis=0, keepdims=True)
        final_vec_ref[1:2, :width] = jnp.sum(pooled_grad, axis=0, keepdims=True)
        final_grad = norm_back(pooled_grad, vector(vec_ref, kind, 8), hat, rate)
        grad_ref[:, :width] = final_grad
        low = final_grad.astype(LOW)
        low_ref[:, :width] = low
        final_vec_ref[2:3, :width] = jnp.sum(low.astype(WIDE), axis=0, keepdims=True)

    each_tower(run)


def step_kernel(
    plans,
    ends_ref,
    scale_ref,
    img_src,
    txt_src,
    valid_ref,
    img_own,
    txt_own,
    loss_ref,
    scale_new_ref,
    img_keep,
    txt_keep,
    img_chunks,
    txt_chunks,
    second_ref,
    middle_ref,
    query_ref,
    keyed_ref,
    mixture_ref,
    weight_ref,
    first_ref,
    img_in,
    txt_in,
    ask_ref,
    mix_ref,
    emb_ref,
    vec_ref,
    raise_ref,
    reduce_ref,
    pairs_ref,
    img_slots,
    txt_slots,
    img_extra,
    txt_extra,
    img_last,
    txt_last,
    flat,
    ask_block,
    mix_block,
    emb_block,
    raise_block,
    reduce_block,
    mask_block,
    top_scr,
    at_scr,
    score_scr,
    low_scr,
    grad_ref,
    pooled_ref,
    proj_grad_ref,
    final_vec_ref,
    raise_grad_ref,
    reduce_keep_ref,
    reduce_send_ref,
    bias_ref,
    backs_ref,
    seconds,
    part,
    parts,
    raised,
    emb,
    all_embs,
    final,
    proj,
    low,
    lows,
    back,
    own_scr,
    whole,
    img_send,
    txt_send,
    img_home,
    txt_home,
    rows_grad,
    middle_scr,
    second_scr,
    valued_scr,
    turn_scr,
    shared_scr,
    slope_scr,
    left_scr,
    left_block,
    turn_block,
    left_all,
    turn_all,
    early_block,
    early_all,
    late_block,
    late_all,
    lines_block,
    lines_all,
    raise_half,
    risen_block,
    raise_all,
    reduce_in,
    img_home_slots,
    txt_home_slots,
    gains,
    top_grad_scr,
    deal_send,
    deal_recv,
    deal_edge,
    deal_fetch,
    ask_send,
    ask_recv,
    mix_send,
    mix_recv,
    emb_send,
    emb_recv,
    raise_send,
    raise_recv,
    reduce_sems,
    pair_sems,
    mask_send,
    mask_recv,
    group_send,
    group_recv,
    embs_send,
    embs_recv,
    home_sems,
    risen_send,
    risen_recv,
    left_send,
    left_recv,
    turn_send,
    turn_recv,
    early_send,
    early_recv,
    late_send,
    late_recv,
    lines_send,
    lines_recv,
    home_pair_sems,
    collect_send,
    collect_recv,
):
    tower, at = here()
    core = at % 2
    me = tower * 16 + at
    sibling = (tower, at + 1 - 2 * core)
    greet(everyone(tower, at))
    deal_sems = (deal_send, deal_recv, deal_edge, deal_fetch)
    deals = [
        Deal(plans[0], 0, img_src, img_slots, img_extra, img_last, deal_sems),
        Deal(plans[1], 1, txt_src, txt_slots, txt_extra, txt_last, deal_sems),
    ]
    pair = Pair(txt_own, txt_in, img_own, img_in, pair_sems)
    asks = rings(ask_block, ask_ref, ask_send, ask_recv)
    mixes = rings(mix_block, mix_ref, mix_send, mix_recv)
    embeds = rings(emb_block, emb_ref, emb_send, emb_recv)
    rise = Group(raise_block, raise_ref, raise_send, raise_recv)
    fall = remote(
        reduce_block, reduce_ref.at[core], reduce_sems.at[0], reduce_sems.at[1], sibling
    )
    fall_own = pltpu.make_async_copy(reduce_block, reduce_ref.at[core], reduce_sems.at[2])
    masks = Spread(mask_block, pairs_ref, mask_send, mask_recv)
    rows = valid_ref[...].astype(WIDE)
    mask_block[...] = jnp.concatenate([rows[:, :LANES], rows[:, LANES:]], axis=0).astype(LOW)

    for deal in deals:
        deal.send_head()
        deal.start_fetch()
        deal.vectors(False)
    for deal in deals:
        deal.whole(True, False)
    for deal in deals:
        deal.whole(False, False)
    pair.start()
    for deal in deals:
        deal.join()

    def put(ref, lane, value):
        if len(ref.shape) == 2:
            ref[: value.shape[0], lane : lane + LANES] = value
        else:
            for part in range(value.shape[0] // 16):
                ref[part, :, lane : lane + LANES] = value[part * 16 : (part + 1) * 16]

    def lift_to(kind, p, ref, start):
        slots = (img_slots, txt_slots)[kind.index]
        for c, value in lift(kind, plans[kind.index], p, slots, flat):
            lane = start + c * LANES
            put(ref, lane, value.astype(ref.dtype))

    def normalise(kind, half):
        width, room = kind.width, kind.room
        own, arrived = ((img_own, img_in), (txt_own, txt_in))[kind.index]
        ref = own if half == kind.index else arrived
        gain, shift = vector(vec_ref, kind, 0), vector(vec_ref, kind, 1)
        positions = lax.broadcasted_iota(jnp.int32, (room, 1), 0)
        for i in range(8):
            rows = ref[i].astype(WIDE)
            hat, _ = standardise(rows)
            first = (hat * gain + shift).astype(LOW)
            s = half * 8 + i
            first_ref[s, :room, :width] = first
            if kind.causal:
                chosen = positions == ends_ref[(half * 16 + at) * 8 + i]
                top = jnp.sum(jnp.where(chosen, first.astype(WIDE), 0.0), axis=0, keepdims=True)
                raw = jnp.sum(jnp.where(chosen, rows, 0.0), axis=0, keepdims=True)
            else:
                top, raw = first[:1].astype(WIDE), rows[:1]
            top_scr[s : s + 1, :width] = top
            at_scr[s : s + 1, :width] = raw

    def begin(kind):
        deal = deals[kind.index]
        deal.arrived(VECTORS)
        lift_to(kind, VECTORS, vec_ref, 0)
        normalise(kind, kind.index)

    each_tower(begin)

    def place_inputs(kind):
        deals[kind.index].arrived(0)
        slots = (img_slots, txt_slots)[kind.index]
        per = kind.width // LANES
        for c, value in lift(kind, plans[kind.index], 0, slots, flat):
            lane = c // per * WIDTH + c % per * LANES
            ref = ask_block
            if lane >= 2 * WIDTH:
                ref, lane = mix_block, lane - 2 * WIDTH
            put(ref, lane, value.astype(LOW))

    each_tower(place_inputs)
    for ring in asks:
        ring.start()

    def place_hidden(kind):
        deal, plan = deals[kind.index], plans[kind.index]
        slots = (img_slots, txt_slots)[kind.index]
        deal.arrived(2)
        per = kind.part // LANES
        for c, value in lift(kind, plan, 2, slots, flat):
            lane = c % per * LANES
            raise_block[c // per, : kind.block, lane : lane + LANES] = value.astype(LOW)
        deal.arrived(3)
        lift_to(kind, 3, reduce_block, 0)

    def place_rest(kind):
        deals[kind.index].arrived(1)
        lift_to(kind, 1, mix_block, WIDTH)
        deals[kind.index].arrived(4)
        lift_to(kind, 4, emb_block, 0)

    each_tower(place_rest)
    each_tower(place_hidden)
    rise.start()
    fall.start()
    fall_own.start()
    pair.finish()
    each_tower(lambda kind: normalise(kind, 1 - kind.index))
    masks.start()
    for ask, mix in zip(asks, mixes):
        ask.relay_deep()
        mix.start()
    for embed in embeds:
        embed.start()
    for ask in asks:
        ask.relay_row()
    for ask in asks:
        ask.finish()

    def question(kind):
        width = kind.width
        tops = top_scr[:, :width].astype(LOW)
        query = dot_nn(tops, matrix(ask_ref, kind, 0, width)) + vector(vec_ref, kind, 2)
        query = query.astype(LOW)
        query_ref[:, :width] = query
        for span in spans(kind):
            lo, hi, first_head, n = span
            put_rows(
                keyed_ref,
                pl.ds(first_head * SEQS, n * SEQS),
                dot_nt(head_rows(query, span), matrix(ask_ref, kind, WIDTH + lo, hi - lo)) * 0.125,
            )
        dead = (HEADS - kind.heads) * SEQS
        put_rows(keyed_ref, pl.ds(kind.heads * SEQS, dead), jnp.zeros((dead, width), WIDE))

    each_tower(question)
    for ring in (*mixes, *embeds):
        ring.relay_deep()

    def score(kind):
        width, room = kind.width, kind.room
        lane = lax.broadcasted_iota(jnp.int32, (HEADS, room), 1)
        for s in range(SEQS):
            keys = get_rows(keyed_ref, pl.ds(s, HEADS, stride=SEQS), width).astype(LOW)
            scores = dot_nt(keys, first_ref[s, :room, :width])
            if kind.causal:
                allowed = lane <= ends_ref[(s // 8 * 16 + at) * 8 + s % 8]
            else:
                allowed = lane < kind.length
            score_scr[s * HEADS : (s + 1) * HEADS, :room] = jnp.where(allowed, scores, -1e30)
        scores = score_scr[:, :room]
        raw = jnp.exp(scores - jnp.max(scores, axis=-1, keepdims=True))
        weights = raw / jnp.sum(raw, axis=-1, keepdims=True)
        head = lax.broadcasted_iota(jnp.int32, (SEQS * HEADS, 1), 0) % HEADS
        weights = jnp.where(head < kind.heads, weights, 0.0)
        weight_ref[:, :room] = weights
        low_scr[: SEQS * HEADS, :room] = weights.astype(LOW)

    each_tower(score)
    for ring in (*mixes, *embeds):
        ring.relay_row()

    def mixture(kind):
        width, room = kind.width, kind.room
        for s in range(SEQS):
            mixed = dot_nn(
                low_scr[s * HEADS : (s + 1) * HEADS, :room], first_ref[s, :room, :width]
            )
            put_rows(mixture_ref, pl.ds(s, HEADS, stride=SEQS), mixed)
        totals = jnp.sum(
            low_scr[: SEQS * HEADS, :room].astype(WIDE), axis=-1, keepdims=True
        )
        score_scr[...] = jnp.broadcast_to(totals, score_scr.shape)

    each_tower(mixture)

    for mix in mixes:
        mix.finish()

    def answer(kind):
        width = kind.width
        mixed = []
        bias = vector(vec_ref, kind, 3)
        for span in spans(kind):
            lo, hi, first_head, n = span
            z = get_rows(mixture_ref, pl.ds(first_head * SEQS, n * SEQS), width).astype(LOW)
            valued = dot_nn(z, matrix(mix_ref, kind, lo, hi - lo))
            totals = jnp.concatenate(
                [score_scr[pl.ds(first_head + h, SEQS, stride=HEADS), 0:1] for h in range(n)],
                axis=0,
            )
            mixed.append(from_head_rows(valued + totals * bias[:, lo:hi], span))
        mixed = side_by_side(mixed).astype(LOW)
        middle = (
            at_scr[:, :width]
            + dot_nn(mixed, matrix(mix_ref, kind, WIDTH, width))
            + vector(vec_ref, kind, 4)
        )
        middle_ref[:, :width] = middle
        hat, _ = standardise(middle)
        second_ref[:, :width] = (
            hat * vector(vec_ref, kind, 5) + vector(vec_ref, kind, 6)
        ).astype(LOW)
        put_rows(mixture_ref, pl.ds(12 * SEQS, SEQS), top_scr[:, :width])
        put_rows(mixture_ref, pl.ds(13 * SEQS, SEQS), mixed.astype(WIDE))

    each_tower(answer)
    rise.relay()
    masks.relay()
    for embed in embeds:
        embed.finish()
    rise.finish()
    fall_own.wait()
    remote(
        reduce_block, reduce_ref.at[1 - core], reduce_sems.at[0], reduce_sems.at[1], sibling
    ).wait_recv()

    sent = group_exchange(False, second_ref, seconds, group_send.at[0], group_recv.at[0])
    hidden_kernel(seconds, raise_ref, reduce_ref, vec_ref, part, raised)
    sent += group_exchange(True, part, parts, group_send.at[1], group_recv.at[1])
    embed_kernel(parts, middle_ref, emb_ref, vec_ref, emb, final, pooled_ref, proj)
    embs = Spread(emb, all_embs, embs_send, embs_recv)
    embs.start()
    masks.finish()
    embs.relay()
    embs.finish()
    objective_kernel(
        scale_ref,
        all_embs,
        pairs_ref,
        final,
        proj,
        emb_ref,
        vec_ref,
        low,
        grad_ref,
        proj_grad_ref,
        final_vec_ref,
        loss_ref,
        scale_new_ref,
        own_scr,
    )
    sent += group_exchange(False, low, lows, group_send.at[2], group_recv.at[2])
    hidden_back_kernel(
        lows,
        seconds,
        raised,
        raise_ref,
        reduce_ref,
        back,
        raise_grad_ref,
        reduce_keep_ref,
        reduce_send_ref,
        bias_ref,
        whole,
    )
    sent += group_exchange(True, back, backs_ref, group_send.at[3], group_recv.at[3])
    halves = remote(
        raise_grad_ref.at[1 - core], raise_half, home_sems.at[0], home_sems.at[1], sibling
    )
    fallen = remote(reduce_send_ref, reduce_in, home_sems.at[2], home_sems.at[3], sibling)
    halves.start()
    fallen.start()
    risen_group = Group(risen_block, raise_all, risen_send, risen_recv, False)

    lefts = Blocks(left_block, left_all, left_send, left_recv)
    turns = Blocks(turn_block, turn_all, turn_send, turn_recv)
    early = Ring(early_block, early_all, early_send, early_recv)
    late = Ring(late_block, late_all, late_send, late_recv)
    home_pair = Pair(img_send, img_home, txt_send, txt_home, home_pair_sems)
    collects = [
        Collect(plans[0], 0, img_home_slots, img_chunks, collect_send.at[0], collect_recv),
        Collect(plans[1], 1, txt_home_slots, txt_chunks, collect_send.at[1], collect_recv),
    ]

    def outputs(kind):
        width = kind.width
        second_grad = jnp.sum(backs_ref[:, :, :width].astype(WIDE), axis=0)
        second_scr[:, :width] = second_grad
        hat, rate = standardise(middle_ref[:, :width])
        middle_grad = grad_ref[:, :width] + norm_back(
            second_grad, vector(vec_ref, kind, 5), hat, rate
        )
        middle_scr[:, :width] = middle_grad
        output_grad = middle_grad.astype(LOW)
        mixed_grad = dot_nt(output_grad, matrix(mix_ref, kind, WIDTH, width)).astype(LOW)
        early_block[:, 0:width] = query_ref[:, :width]
        early_block[:, WIDTH : WIDTH + width] = mixed_grad
        early_block[:, 2 * WIDTH : 2 * WIDTH + width] = output_grad
        early_block[:, 3 * WIDTH : 3 * WIDTH + EMB] = proj_grad_ref[...]
        left_scr[:, :width] = get_rows(mixture_ref, slice(None), width)
        left_scr[14 * SEQS : 15 * SEQS, :width] = pooled_ref[:, :width].astype(WIDE)
        left_scr[15 * SEQS :, :width] = jnp.zeros((SEQS, width), WIDE)

    each_tower(outputs)
    early.start()

    def turned(kind):
        width, block = kind.width, kind.block
        left_block[:, :block, :] = left_scr[:, :width].T.reshape(16, block, 256).astype(LOW)

    each_tower(turned)
    lefts.start()

    def values(kind):
        width = kind.width
        mixed_grad = early_block[:, WIDTH : WIDTH + width]
        bias = vector(vec_ref, kind, 3)
        dead = kind.heads * SEQS
        put_rows(valued_scr, pl.ds(dead, 256 - dead), jnp.zeros((256 - dead, width), WIDE))
        shared_scr[dead:, :] = jnp.zeros((256 - dead, LANES), WIDE)
        for span in spans(kind):
            lo, hi, first_head, n = span
            rows = head_rows(mixed_grad, span)
            place = pl.ds(first_head * SEQS, n * SEQS)
            put_rows(valued_scr, place, dot_nt(rows, matrix(mix_ref, kind, lo, hi - lo)))
            constant = jnp.sum(rows.astype(WIDE) * bias[:, lo:hi], axis=-1, keepdims=True)
            shared_scr[place, :] = jnp.broadcast_to(constant, (n * SEQS, LANES))

    each_tower(values)
    halves.wait_recv()
    risen_block[...] = (
        raise_grad_ref[core].astype(WIDE) + raise_half[...].astype(WIDE)
    ).astype(LOW)
    risen_group.start()

    def slopes(kind):
        width, room = kind.width, kind.room
        for s in range(SEQS):
            line = pl.ds(s, HEADS, stride=SEQS)
            slope = dot_nt(
                get_rows(valued_scr, line, width).astype(LOW), first_ref[s, :room, :width]
            )
            slope_scr[s * HEADS : (s + 1) * HEADS, :room] = slope + shared_scr[line, 0:1]
        weights = weight_ref[:, :room]
        slope = slope_scr[:, :room]
        slope = weights * (slope - jnp.sum(weights * slope, axis=-1, keepdims=True))
        both = jnp.concatenate(
            [slope.reshape(SEQS, HEADS, room), weights.reshape(SEQS, HEADS, room)], axis=1
        )
        low_scr[:, :room] = both.reshape(2 * SEQS * HEADS, room).astype(LOW)

    each_tower(slopes)
    early.relay_deep()

    def tokens(kind):
        width, room = kind.width, kind.room
        for s in range(SEQS):
            line = pl.ds(s, HEADS, stride=SEQS)
            both = low_scr[2 * s * HEADS : 2 * (s + 1) * HEADS, :room]
            first = first_ref[s, :room, :width]
            put_rows(turn_scr, line, dot_nn(both[:HEADS], first))
            right = jnp.concatenate(
                [get_rows(keyed_ref, line, width), get_rows(valued_scr, line, width)], axis=0
            )
            rows_grad[s, :room, :width] = dot_tn(both, right.astype(LOW))

    each_tower(tokens)
    early.relay_row()

    def queries(kind):
        width, block = kind.width, kind.block
        grads = []
        for span in spans(kind):
            lo, hi, first_head, n = span
            rows = get_rows(turn_scr, pl.ds(first_head * SEQS, n * SEQS), width).astype(LOW)
            back = dot_nn(rows, matrix(ask_ref, kind, WIDTH + lo, hi - lo)) * 0.125
            grads.append(from_head_rows(back, span))
        query_grad = side_by_side(grads).astype(LOW)
        late_block[:, :width] = query_grad
        top_grad_scr[:, :width] = dot_nt(query_grad, matrix(ask_ref, kind, 0, width))
        turn_block[:, :block, :] = (
            get_rows(turn_scr, slice(None), width).T.reshape(16, block, 256).astype(LOW)
        )

    each_tower(queries)
    late.start()
    turns.start()
    gains[...] = jnp.zeros_like(gains)

    def finish(kind, half):
        width, room, length = kind.width, kind.room, kind.length
        own, arrived = ((img_own, img_in), (txt_own, txt_in))[kind.index]
        ref = own if half == kind.index else arrived
        keep, send = ((img_keep, img_send), (txt_keep, txt_send))[kind.index]
        gain = vector(vec_ref, kind, 0)
        positions = lax.broadcasted_iota(jnp.int32, (room, 1), 0)
        gain_sum = jnp.zeros((1, width), WIDE)
        shift_sum = jnp.zeros((1, width), WIDE)
        for i in range(8):
            s = half * 8 + i
            hat, rate = standardise(ref[i].astype(WIDE))
            if kind.causal:
                chosen = positions == ends_ref[(half * 16 + at) * 8 + i]
            else:
                chosen = positions == 0
            chosen = chosen.astype(WIDE)
            grad = rows_grad[s, :room, :width] + chosen * top_grad_scr[s : s + 1, :width]
            gain_sum += jnp.sum(grad * hat, axis=0, keepdims=True)
            shift_sum += jnp.sum(grad, axis=0, keepdims=True)
            result = norm_back(grad, gain, hat, rate) + chosen * middle_scr[s : s + 1, :width]
            if half == kind.index:
                keep[i] = result[:length]
            else:
                send[i] = result.astype(LOW)
        gains[0:1, :width] += gain_sum
        gains[1:2, :width] += shift_sum

    each_tower(lambda kind: finish(kind, 1 - kind.index))
    home_pair.start()
    risen_group.finish()
    fallen.wait_recv()

    def slots_of(kind):
        return (img_home_slots, txt_home_slots)[kind.index]

    def hidden_grads(kind):
        plan, collect = plans[kind.index], collects[kind.index]
        block, n, per = kind.block, kind.reduce_rows, kind.part // LANES

        def risen(c):
            chip, lane = c // per, c % per * LANES
            return raise_all[chip, :block, lane : lane + LANES].astype(WIDE)

        def fallen(c):
            lane = c * LANES
            return reduce_keep_ref[:n, lane : lane + LANES] + reduce_in[
                :n, lane : lane + LANES
            ].astype(WIDE)

        drop(kind, plan, 2, risen, slots_of(kind), flat)
        collect.piece(2, False)
        drop(kind, plan, 3, fallen, slots_of(kind), flat)
        collect.piece(3, False)

    each_tower(hidden_grads)
    late.relay_deep()
    each_tower(lambda kind: finish(kind, kind.index))
    late.relay_row()

    def lines(kind):
        width = kind.width
        hat, _ = standardise(middle_ref[:, :width])
        second_grad = second_scr[:, :width]

        def column_sum(value):
            return jnp.sum(value.astype(WIDE), axis=0, keepdims=True)

        mixed_grad = early_block[:, WIDTH : WIDTH + width].astype(WIDE)
        weights = low_scr[:, : kind.room].astype(WIDE).reshape(SEQS, 2 * HEADS, kind.room)
        totals = jnp.sum(weights[:, HEADS:], axis=-1, keepdims=True).reshape(SEQS * HEADS, 1)
        shared_scr[...] = jnp.broadcast_to(totals, shared_scr.shape)
        value_bias = []
        for lo, hi, first_head, n in spans(kind):
            owner = lax.broadcasted_iota(jnp.int32, (SEQS, hi - lo), 1) // HEAD
            scaled = jnp.zeros((SEQS, hi - lo), WIDE)
            for h in range(n):
                total = shared_scr[pl.ds(first_head + h, SEQS, stride=HEADS), 0:1]
                scaled = jnp.where(owner == h, mixed_grad[:, lo:hi] * total, scaled)
            value_bias.append(column_sum(scaled))
        hidden = bias_ref[0:1, : kind.part]
        parts = [
            gains[0:1, :width],
            gains[1:2, :width],
            column_sum(late_block[:, :width]),
            side_by_side(value_bias),
            column_sum(early_block[:, 2 * WIDTH : 2 * WIDTH + width]),
            column_sum(second_grad * hat),
            column_sum(second_grad),
            final_vec_ref[2:3, :width],
            final_vec_ref[0:1, :width],
            final_vec_ref[1:2, :width],
            jnp.concatenate([hidden, jnp.zeros((1, width - kind.part), WIDE)], axis=1),
            jnp.zeros((5, width), WIDE),
        ]
        lines_block[:, :width] = jnp.concatenate(parts, axis=0)

    each_tower(lines)
    line_copy = remote(
        lines_block, lines_all.at[at], lines_send.at[0], lines_recv.at[at], (tower, jnp.int32(0))
    )
    line_own = pltpu.make_async_copy(lines_block, lines_all.at[at], lines_recv.at[at])
    pl.when(at > 0)(line_copy.start)
    pl.when(at == 0)(line_own.start)

    early.finish()
    lefts.finish()

    def from_early(kind):
        plan, collect = plans[kind.index], collects[kind.index]
        width, block = kind.width, kind.block

        def gathered(k):
            lane = lax.broadcasted_iota(jnp.int32, (block, LANES), 1) // SEQS
            halves = []
            for side in range(2):
                total = jnp.zeros((block, LANES), WIDE)
                for j in range(8):
                    part = left_all[side * 8 + j, :block, LANES:].astype(WIDE)
                    shift = (j * SEQS - (k - 8) * SEQS) % LANES
                    turned_part = pltpu.roll(part, shift, 1) if shift else part
                    total = jnp.where(lane == j, turned_part, total)
                halves.append(total)
            return jnp.concatenate(halves, axis=1).astype(LOW)

        def right(start, wide):
            return early_all[:, :, start : start + wide].reshape(256, wide)

        output = dot_nn(gathered(13), right(2 * WIDTH, width))
        drop(
            kind, plan, 1, lambda c: output[:, c * LANES : (c + 1) * LANES], slots_of(kind), flat
        )
        collect.piece(1, False)
        embed = dot_nn(gathered(14), right(3 * WIDTH, EMB))
        drop(kind, plan, 4, lambda c: embed[:, c * LANES : (c + 1) * LANES], slots_of(kind), flat)
        collect.piece(4, False)
        left_scr[:block, :256] = gathered(12).astype(WIDE)

    each_tower(from_early)
    late.finish()
    turns.finish()

    def from_late(kind):
        plan, collect = plans[kind.index], collects[kind.index]
        width, block = kind.width, kind.block
        ask = dot_nn(left_scr[:block, :256].astype(LOW), late_all[:, :, :width].reshape(256, width))

        def outer(side_ref, start, span):
            lo, hi, first_head, n = span
            lane = first_head * SEQS
            total = jnp.zeros((block, hi - lo), WIDE)
            for j in range(8):
                left, rows = [], []
                for source in (2 * j, 2 * j + 1):
                    left.append(side_ref[source, :block, lane : lane + LANES])
                    rows.append(
                        head_rows(early_all[source, :, start : start + width], span)
                    )
                    if n < 8:
                        rows.append(jnp.zeros(((8 - n) * SEQS, hi - lo), LOW))
                total += dot_nn(
                    jnp.concatenate(left, axis=1), jnp.concatenate(rows, axis=0)
                )
            return total

        keys = side_by_side([outer(turn_all, 0, span) for span in spans(kind)]) * 0.125
        worth = side_by_side([outer(left_all, WIDTH, span) for span in spans(kind)])
        per = width // LANES

        def inputs(c):
            value = (ask, keys, worth)[c // per]
            return value[:, c % per * LANES : (c % per + 1) * LANES]

        drop(kind, plan, 0, inputs, slots_of(kind), flat)
        collect.piece(0, False)

    each_tower(from_late)

    @pl.when(at == 0)
    def _():
        for k in range(1, 16):
            remote(
                lines_block, lines_all.at[k], lines_send.at[0], lines_recv.at[k], sibling
            ).wait_recv()
        line_own.wait()

        def vectors(kind):
            width, part = kind.width, kind.part
            whole = [jnp.sum(lines_all[:, :10, :width], axis=0)]
            for row in range(4):
                pair_of = []
                for chip in (2 * row, 2 * row + 1):
                    pair_of.append(
                        lines_all[2 * chip, 10:11, :part] + lines_all[2 * chip + 1, 10:11, :part]
                    )
                whole.append(jnp.concatenate(pair_of, axis=1))
            whole.append(jnp.zeros((2, width), WIDE))
            result = jnp.concatenate(whole, axis=0)
            drop(
                kind,
                plans[kind.index],
                VECTORS,
                lambda c: result[:, c * LANES : (c + 1) * LANES],
                slots_of(kind),
                flat,
            )

        each_tower(vectors)

    each_tower(lambda kind: collects[kind.index].piece(VECTORS, False))
    home_pair.finish()

    @pl.when(tower == 1)
    def _():
        img_keep[...] = img_home[:, : TOWERS[0].length].astype(WIDE)

    @pl.when(tower == 0)
    def _():
        txt_keep[...] = txt_home[:, : TOWERS[1].length].astype(WIDE)

    for collect in collects:
        collect.finish()
    for copy in (*sent, fall, fallen, halves):
        copy.wait_send()
    pl.when(at > 0)(line_copy.wait_send)
    for group in (pair, *asks, *mixes, *embeds, rise, masks, embs, *deals):
        group.drain()
    for group in (risen_group, lefts, turns, early, late, home_pair):
        group.drain()

    def drain(kind):
        for p in range(VECTORS + 1):
            collects[kind.index].piece(p, True)

    each_tower(drain)


ROWS_LOW = ((SEQS, WIDTH), LOW)
ROWS_WIDE = ((SEQS, WIDTH), WIDE)
HEAD_ROWS = ((WIDTH // LANES, SEQS * HEADS, LANES), WIDE)
LANE_ROWS = ((SEQS * HEADS, LANES), WIDE)
GROUP = ((8, SEQS, WIDTH), LOW)
HIDDEN_BLOCKS = ((2, 8, 48, PART), LOW)
OUTER = ((16, 48, SEQS * HEADS), LOW)


def chunk_shapes(plan, n):
    return ((n, plan.rows, LANES), LOW)


def run_step(scalars, chunks, valid, tokens, plans):
    most = max(plan.local for plan in plans) + 17
    slots = max(plan.slots for plan in plans)
    edges = [((plan.rows, LANES), LOW) for plan in plans]
    rooms = [((8, kind.room, kind.width), LOW) for kind in TOWERS]
    outs = [((8, kind.length, kind.width), WIDE) for kind in TOWERS] + [
        chunk_shapes(plan, plan.local) for plan in plans
    ]
    scratch = [
        ROWS_LOW,
        ROWS_WIDE,
        ROWS_LOW,
        HEAD_ROWS,
        HEAD_ROWS,
        LANE_ROWS,
        ((SEQS, ROOM, WIDTH), LOW),
        rooms[0],
        rooms[1],
        ((3, 16, 16, 2 * WIDTH), LOW),
        ((3, 16, 16, 2 * WIDTH), LOW),
        ((3, 16, 16, EMB), LOW),
        ROWS_WIDE,
        HIDDEN_BLOCKS,
        ((2, 192, WIDTH), LOW),
        ((2, 16, 16, LANES), LOW),
        chunk_shapes(plans[0], plans[0].slots),
        chunk_shapes(plans[1], plans[1].slots),
        edges[0],
        edges[1],
        edges[0],
        edges[1],
        ((plans[0].slots * plans[0].rows, LANES), WIDE),
        ((3, 16, 2 * WIDTH), LOW),
        ((3, 16, 2 * WIDTH), LOW),
        ((3, 16, EMB), LOW),
        ((8, 48, PART), LOW),
        ((192, WIDTH), LOW),
        ((16, LANES), LOW),
        ROWS_WIDE,
        ROWS_WIDE,
        LANE_ROWS,
        ((2 * SEQS * HEADS, LANES), LOW),
        ROWS_WIDE,
        ROWS_LOW,
        ((SEQS, EMB), LOW),
        ((8, WIDTH), WIDE),
        HIDDEN_BLOCKS,
        ((192, WIDTH), WIDE),
        ((192, WIDTH), LOW),
        ((8, PART), WIDE),
        GROUP,
        GROUP,
        GROUP,
        GROUP,
        ((128, PART), WIDE),
        ((SEQS, EMB), LOW),
        ((2, 16, SEQS, EMB), LOW),
        ROWS_WIDE,
        ((SEQS, EMB), WIDE),
        ROWS_LOW,
        GROUP,
        GROUP,
        ((256, EMB), WIDE),
        ((PART, WIDTH), WIDE),
        rooms[0],
        rooms[1],
        rooms[0],
        rooms[1],
        ((SEQS, ROOM, WIDTH), WIDE),
        ROWS_WIDE,
        ROWS_WIDE,
        HEAD_ROWS,
        HEAD_ROWS,
        LANE_ROWS,
        LANE_ROWS,
        ((SEQS * HEADS, WIDTH), WIDE),
        OUTER,
        OUTER,
        OUTER,
        OUTER,
        ((SEQS, 3 * WIDTH + EMB), LOW),
        ((16, SEQS, 3 * WIDTH + EMB), LOW),
        ROWS_LOW,
        ((16, SEQS, WIDTH), LOW),
        ROWS_WIDE,
        ((16, SEQS, WIDTH), WIDE),
        ((8, 48, PART), LOW),
        ((8, 48, PART), LOW),
        ((8, 48, PART), LOW),
        ((192, WIDTH), LOW),
        chunk_shapes(plans[0], plans[0].slots),
        chunk_shapes(plans[1], plans[1].slots),
        ((8, WIDTH), WIDE),
        ROWS_WIDE,
    ]
    semaphores = [
        (2, most,),
        (2, 6,),
        (2, 2,),
        (2,),
        (3, 16),
        (3, 15),
        (3, 16),
        (3, 15),
        (3, 16),
        (3, 15),
        (9,),
        (8,),
        (3,),
        (2,),
        (17,),
        (16,),
        (4, 8,),
        (4, 7,),
        (17,),
        (16,),
        (4,),
        (9,),
        (8,),
        (16,),
        (15,),
        (16,),
        (15,),
        (16,),
        (15,),
        (16,),
        (15,),
        (1,),
        (16,),
        (2,),
        (2, 2, slots,),
        (2,),
    ]
    smem = pl.BlockSpec(memory_space=pltpu.SMEM)
    vmem = pl.BlockSpec(memory_space=pltpu.VMEM)
    like = jax.ShapeDtypeStruct
    return pl.pallas_call(
        functools.partial(step_kernel, plans),
        out_shape=[like((1,), WIDE), like((3,), WIDE)] + [like(*out) for out in outs],
        in_specs=[smem, smem, ANY, ANY, vmem, vmem, vmem],
        out_specs=[smem, smem, vmem, vmem, vmem, vmem],
        scratch_shapes=[pltpu.VMEM(*each) for each in scratch]
        + [pltpu.SemaphoreType.DMA(shape) for shape in semaphores],
        compiler_params=comm_params(0),
    )(*scalars, *chunks, valid, *tokens)


def to_chunks(flat, plan, me):
    start = me * plan.share % plan.chunk
    padded = jnp.pad(flat, (plan.chunk, plan.local * plan.chunk - plan.share))
    piece = lax.dynamic_slice(padded, (plan.chunk - start,), (plan.local * plan.chunk,))
    return piece.astype(LOW).reshape(plan.local, plan.rows, LANES)


def from_chunks(chunks, plan, me):
    start = me * plan.share % plan.chunk
    return lax.dynamic_slice(chunks.reshape(-1), (start,), (plan.share,)).astype(WIDE)


def step(
    img_tokens,
    txt_tokens,
    txt_ends,
    valid,
    img_master,
    img_moment,
    img_average,
    txt_master,
    txt_moment,
    txt_average,
    scale_state,
):
    me = lax.axis_index(("tower", "dp"))
    plans = (
        Plan(0, img_master.shape[0], 96, (9, 3, 12, 12, 2)),
        Plan(1, txt_master.shape[0], 64, (6, 2, 8, 8, 2)),
    )
    img_rows = jnp.pad(img_tokens, ((0, 0), (0, TOWERS[0].room - TOWERS[0].length), (0, 0)))
    txt_rows = jnp.pad(txt_tokens, ((0, 0), (0, TOWERS[1].room - TOWERS[1].length), (0, 0)))
    loss, scale_new, img_grad, txt_grad, img_chunks, txt_chunks = run_step(
        (txt_ends, scale_state),
        (to_chunks(img_master, plans[0], me), to_chunks(txt_master, plans[1], me)),
        valid,
        (img_rows, txt_rows),
        plans,
    )
    img_new = advance(
        img_master, img_moment, img_average, from_chunks(img_chunks, plans[0], me), step_rate
    )
    txt_new = advance(
        txt_master, txt_moment, txt_average, from_chunks(txt_chunks, plans[1], me), step_rate
    )
    return (
        loss[0],
        img_grad,
        txt_grad,
        img_new[0],
        img_new[1],
        img_new[2],
        img_new[0].astype(LOW),
        txt_new[0],
        txt_new[1],
        txt_new[2],
        txt_new[0].astype(LOW),
        scale_new,
    )


def from_partner(value, axis, stride):
    mask = 2**stride
    pairs = [(source, source ^ mask) for source in range(lax.axis_size(axis))]
    return lax.ppermute(value, axis, pairs)


def round_value(v):
    return lax.optimization_barrier(v.astype(jnp.bfloat16)).astype(jnp.float32)


def make_low():

    def value_keep(v):
        return (round_value(v), None)

    def grad_pass(kept, grad):
        return (grad,)

    rounded = jax.custom_vjp(round_value)
    rounded.defvjp(value_keep, grad_pass)
    return rounded


def low(v):
    return make_low()(v)


def make_low_back():

    def identity(v):
        return v

    def value_pass(v):
        return (v, None)

    def grad_round(kept, grad):
        return (round_value(grad),)

    passed = jax.custom_vjp(identity)
    passed.defvjp(value_pass, grad_round)
    return passed


def low_back(v):
    return make_low_back()(v)


def both_ways(value):
    return low(low_back(value))


def product(left, right):
    return jnp.matmul(left, right)


def contract(form, left, right):
    return jnp.einsum(form, left, right)


def layer_norm(values, gain_row, shift_row):
    centred = values - jnp.mean(values, axis=-1, keepdims=True)
    spread = jnp.mean(centred * centred, axis=-1, keepdims=True)
    return centred * lax.rsqrt(spread + 1e-05) * gain_row + shift_row


def unpack(flat_weights, model_width, hidden_width, embed_width):
    piece_shapes = [
        (model_width, 3 * model_width),
        (model_width, model_width),
        (model_width, hidden_width),
        (hidden_width, model_width),
        (model_width, embed_width),
        (10, model_width),
        (hidden_width,),
    ]
    pieces = []
    offset = 0
    for piece_shape in piece_shapes:
        length = math.prod(piece_shape)
        pieces.append(flat_weights[offset : offset + length].reshape(piece_shape))
        offset = offset + length
    return pieces


def encode(tokens, flat_weights, positions, causal, model_width, hidden_width, embed_width):
    w_inputs, w_output, w_expand, w_reduce, w_embed, vectors, expand_bias = unpack(
        flat_weights, model_width, hidden_width, embed_width
    )
    groups = tokens.shape[0]
    length = tokens.shape[1]
    first = low(layer_norm(tokens, vectors[0], vectors[1]))
    bias_in = jnp.concatenate([vectors[2], jnp.zeros_like(vectors[2]), vectors[3]])
    joined = both_ways(product(first, w_inputs) + bias_in)
    joined = joined.reshape(groups, length, 3, model_width // HEAD, HEAD)
    scores = low_back(contract("gqhd,gkhd->ghqk", joined[:, :, 0], joined[:, :, 1]) * 0.125)
    if causal:
        row_index = lax.broadcasted_iota(jnp.int32, (length, length), 0)
        col_index = lax.broadcasted_iota(jnp.int32, (length, length), 1)
        scores = jnp.where(col_index <= row_index, scores, -1e30)
    row_top = jnp.max(scores, axis=-1, keepdims=True)
    raw_weights = jnp.exp(scores - row_top)
    attention = low(raw_weights / jnp.sum(raw_weights, axis=-1, keepdims=True))
    mixed_heads = both_ways(
        contract("ghqk,gkhd->gqhd", attention, joined[:, :, 2]).reshape(groups, length, model_width)
    )
    middle = tokens + low_back(product(mixed_heads, w_output) + vectors[4])
    second = low(layer_norm(middle, vectors[5], vectors[6]))
    raised = low_back(product(second, w_expand) + expand_bias)
    active = low(raised * jax.nn.sigmoid(1.702 * raised))
    final_rows = middle + low_back(product(active, w_reduce) + vectors[7])
    pooled = jnp.take_along_axis(final_rows, positions[:, None, None], axis=1)[:, 0]
    pooled = low(layer_norm(pooled, vectors[8], vectors[9]))
    projected = low_back(product(pooled, w_embed))
    return low(
        projected * lax.rsqrt(jnp.sum(projected * projected, axis=-1, keepdims=True) + 1e-06)
    )


def inner(left, right):
    return lax.dot_general(
        left, right, (((1,), (1,)), ((), ())), preferred_element_type=jnp.float32
    )


def across(left, right):
    return lax.dot_general(
        left, right, (((0,), (0,)), ((), ())), preferred_element_type=jnp.float32
    )


def softmax_total(logits, allowed):
    masked = jnp.where(allowed, logits, -1e30)
    row_top = jnp.max(masked, axis=1, keepdims=True)
    return jnp.log(jnp.sum(jnp.exp(masked - row_top), axis=1)) + row_top[:, 0]


def advance(master, moment, average, grads, rate):
    moment_new = momentum_rate * moment + grads
    master_new = master - rate * (grads + momentum_rate * moment_new)
    average_new = average_rate * average + (1.0 - average_rate) * master_new
    return (master_new, moment_new, average_new)


def padded_to(flat, length):
    return jnp.pad(flat, (0, length - flat.shape[0]))


def body(
    img_tokens,
    txt_tokens,
    txt_ends,
    valid,
    img_master,
    img_moment,
    img_average,
    txt_master,
    txt_moment,
    txt_average,
    scale_state,
):
    batch_rows = img_tokens.shape[0]
    total_rows = batch_rows * lax.axis_size(("tower", "dp"))
    device_at = lax.axis_index(("tower", "dp"))
    tower_at = lax.axis_index("tower")
    is_image = tower_at == 0
    img_share = img_master.shape[0]
    txt_share = txt_master.shape[0]
    img_count = img_tokens.size
    txt_count = txt_tokens.size
    shard_room = max(img_share, txt_share)
    token_room = max(img_count, txt_count)
    tower_count = lax.axis_size("dp")
    dp_at = lax.axis_index("dp")
    img_low = padded_to(img_master.astype(jnp.bfloat16), shard_room)
    txt_low = padded_to(txt_master.astype(jnp.bfloat16), shard_room)
    token_out = jnp.where(
        is_image,
        padded_to(txt_tokens.reshape(-1), token_room),
        padded_to(img_tokens.reshape(-1), token_room),
    )
    weight_out = jnp.where(is_image, txt_low, img_low)
    weight_mine = jnp.where(is_image, img_low, txt_low)
    token_in, weight_in = from_partner((token_out, weight_out), "tower", 0)
    stacked = jnp.where(
        is_image, jnp.stack([weight_mine, weight_in]), jnp.stack([weight_in, weight_mine])
    )
    gathered = lax.all_gather(stacked, "dp", axis=1, tiled=True)
    pair_ends = jnp.concatenate(
        [
            lax.dynamic_slice_in_dim(txt_ends, dp_at * batch_rows, batch_rows),
            lax.dynamic_slice_in_dim(txt_ends, (tower_count + dp_at) * batch_rows, batch_rows),
        ]
    )
    pair_zero = jnp.zeros((2 * batch_rows,), jnp.int32)

    def image_weights(whole):
        return whole.reshape(2, tower_count, shard_room).reshape(-1).astype(jnp.float32)

    def text_weights(whole):
        return (
            whole.reshape(2, tower_count, shard_room)[:, :, :txt_share]
            .reshape(-1)
            .astype(jnp.float32)
        )

    def image_rows(arrived):
        return jnp.concatenate(
            [img_tokens, arrived[:img_count].reshape(img_tokens.shape)], axis=0
        ).astype(jnp.float32)

    def text_rows(arrived):
        return jnp.concatenate([arrived.reshape(txt_tokens.shape), txt_tokens], axis=0).astype(
            jnp.float32
        )

    def image_encode(rows, flat):
        return encode(rows, flat, pair_zero, False, D_IMG, FF_IMG, EMB)

    def text_encode(rows, flat):
        return encode(rows, flat, pair_ends, True, D_TXT, FF_TXT, EMB)

    def image_forward(operands):
        return image_encode(image_rows(operands[1]), image_weights(operands[0]))

    def text_forward(operands):
        return text_encode(text_rows(operands[1]), text_weights(operands[0]))

    pair_emb = lax.cond(is_image, image_forward, text_forward, (gathered, token_in)).astype(
        jnp.bfloat16
    )
    emb_in = from_partner(pair_emb, "tower", 0)
    img_pair = jnp.where(is_image, pair_emb, emb_in)
    txt_pair = jnp.where(is_image, emb_in, pair_emb)
    row_start = tower_at * batch_rows
    img_local = lax.dynamic_slice_in_dim(img_pair, row_start, batch_rows)
    txt_local = lax.dynamic_slice_in_dim(txt_pair, row_start, batch_rows)
    img_all, txt_all = (
        lax.all_gather(img_local, ("tower", "dp"), axis=0, tiled=True),
        lax.all_gather(txt_local, ("tower", "dp"), axis=0, tiled=True),
    )
    logit_scale = jnp.exp(scale_state[0])
    offset = device_at * batch_rows
    row_index = lax.broadcasted_iota(jnp.int32, (batch_rows, total_rows), 0) + offset
    col_index = lax.broadcasted_iota(jnp.int32, (batch_rows, total_rows), 1)
    diagonal = (row_index == col_index).astype(jnp.float32)
    allowed = valid > 0
    row_logits = logit_scale * inner(img_local, txt_all)
    col_logits = logit_scale * inner(txt_local, img_all)
    row_lse = softmax_total(row_logits, allowed)
    col_lse = softmax_total(col_logits, allowed)
    partial_loss = 0.5 * (
        jnp.sum(row_lse)
        - jnp.sum(row_logits * diagonal)
        + jnp.sum(col_lse)
        - jnp.sum(col_logits * diagonal)
    )
    row_terms = 0.5 * (jnp.where(allowed, jnp.exp(row_logits - row_lse[:, None]), 0.0) - diagonal)
    col_terms = 0.5 * (jnp.where(allowed, jnp.exp(col_logits - col_lse[:, None]), 0.0) - diagonal)
    partial_scale = jnp.sum(row_terms * row_logits) + jnp.sum(col_terms * col_logits)
    row_back = (logit_scale * row_terms).astype(jnp.bfloat16)
    col_back = (logit_scale * col_terms).astype(jnp.bfloat16)
    img_emb_grad = jnp.dot(row_back, txt_all, preferred_element_type=jnp.float32)
    txt_emb_grad = jnp.dot(col_back, img_all, preferred_element_type=jnp.float32)
    img_extra, txt_extra = (
        lax.psum_scatter(
            across(col_back, txt_local), ("tower", "dp"), scatter_dimension=0, tiled=True
        ),
        lax.psum_scatter(
            across(row_back, img_local), ("tower", "dp"), scatter_dimension=0, tiled=True
        ),
    )
    img_emb_grad = img_emb_grad + img_extra
    txt_emb_grad = txt_emb_grad + txt_extra
    sums = lax.psum((partial_loss, partial_scale), ("tower", "dp"))
    grad_out = jnp.where(is_image, txt_emb_grad, img_emb_grad)
    grad_in = from_partner(grad_out, "tower", 0)
    pair_cot = jnp.where(
        is_image,
        jnp.concatenate([img_emb_grad, grad_in], axis=0),
        jnp.concatenate([grad_in, txt_emb_grad], axis=0),
    )

    def image_backward(operands):
        recomputed, tower_pullback = jax.vjp(
            image_encode, image_rows(operands[1]), image_weights(operands[0])
        )
        rows_grad, flat_grad = tower_pullback(operands[2])
        own_part = padded_to(rows_grad[:batch_rows].reshape(-1), token_room)
        sent_part = padded_to(rows_grad[batch_rows:].reshape(-1), token_room)
        stacked_grad = flat_grad.reshape(2, tower_count, img_share)
        return (own_part, sent_part, stacked_grad)

    def text_backward(operands):
        recomputed, tower_pullback = jax.vjp(
            text_encode, text_rows(operands[1]), text_weights(operands[0])
        )
        rows_grad, flat_grad = tower_pullback(operands[2])
        own_part = padded_to(rows_grad[batch_rows:].reshape(-1), token_room)
        sent_part = padded_to(rows_grad[:batch_rows].reshape(-1), token_room)
        stacked_grad = jnp.pad(
            flat_grad.reshape(2, tower_count, txt_share),
            ((0, 0), (0, 0), (0, shard_room - txt_share)),
        )
        return (own_part, sent_part, stacked_grad)

    own_part, sent_part, stacked_grad = lax.cond(
        is_image, image_backward, text_backward, (gathered, token_in, pair_cot)
    )
    summed = lax.psum_scatter(stacked_grad, "dp", scatter_dimension=1, tiled=True)
    kept_part = jnp.where(is_image, summed[0, 0], summed[1, 0])
    sent_share = jnp.where(is_image, summed[1, 0], summed[0, 0])
    home_weights, home_tokens = (
        from_partner(sent_share.astype(jnp.bfloat16), "tower", 0).astype(sent_share.dtype),
        from_partner(sent_part.astype(jnp.bfloat16), "tower", 0).astype(sent_part.dtype),
    )
    img_owned = jnp.where(is_image, kept_part, home_weights)
    txt_owned = jnp.where(is_image, home_weights, kept_part)[:txt_share]
    img_grad = jnp.where(is_image, own_part, home_tokens)[:img_count].reshape(img_tokens.shape)
    txt_grad = jnp.where(is_image, home_tokens, own_part).reshape(txt_tokens.shape)
    img_new = advance(img_master, img_moment, img_average, img_owned, step_rate)
    txt_new = advance(txt_master, txt_moment, txt_average, txt_owned, step_rate)
    scale_parts = advance(scale_state[0], scale_state[1], scale_state[2], sums[1], scale_rate)
    scale_new = jnp.stack([scale_parts[0], scale_parts[1], scale_parts[2]])
    return (
        sums[0] / total_rows,
        img_grad,
        txt_grad,
        img_new[0],
        img_new[1],
        img_new[2],
        img_new[0].astype(jnp.bfloat16),
        txt_new[0],
        txt_new[1],
        txt_new[2],
        txt_new[0].astype(jnp.bfloat16),
        scale_new,
    )


def solution(mesh):
    in_specs = (
        P(("tower", "dp"), None, None),
        P(("tower", "dp"), None, None),
        P(),
        P(("tower", "dp"), None),
        P(("tower", "dp")),
        P(("tower", "dp")),
        P(("tower", "dp")),
        P(("tower", "dp")),
        P(("tower", "dp")),
        P(("tower", "dp")),
        P(),
    )
    out_specs = (
        P(),
        P(("tower", "dp"), None, None),
        P(("tower", "dp"), None, None),
        P(("tower", "dp")),
        P(("tower", "dp")),
        P(("tower", "dp")),
        P(("tower", "dp")),
        P(("tower", "dp")),
        P(("tower", "dp")),
        P(("tower", "dp")),
        P(("tower", "dp")),
        P(),
    )
    run = step if (mesh.shape["tower"], mesh.shape["dp"]) == (2, 16) else body
    return jax.shard_map(run, mesh=mesh, in_specs=in_specs, out_specs=out_specs, check_vma=False)
```

```python
import functools
import math

import jax
import jax.numpy as jnp
from jax import lax
from jax.experimental import pallas as pl
from jax.experimental.pallas import tpu as pltpu
from jax.sharding import PartitionSpec as P

D_IMG = 768
FF_IMG = 3072
D_TXT = 512
FF_TXT = 2048
EMB = 512
HEAD = 64


momentum_rate = 0.5
average_rate = 0.5
step_rate = 0.08
scale_rate = 0.0001


MESH = pl.DeviceIdType.MESH
ANY = pl.BlockSpec(memory_space=pl.ANY)
GRANT = 58 * 1024 * 1024
LANES = 128
LOW = jnp.bfloat16
WIDE = jnp.float32


def here():
    return lax.axis_index("tower"), lax.axis_index("dp")


def greet(devices):
    barrier = pltpu.get_barrier_semaphore()
    for device in devices:
        pl.semaphore_signal(barrier, inc=1, device_id=device, device_id_type=MESH)
    pl.semaphore_wait(barrier, len(devices))


def remote(src, dst, send_sem, recv_sem, device):
    return pltpu.make_async_remote_copy(
        src_ref=src,
        dst_ref=dst,
        send_sem=send_sem,
        recv_sem=recv_sem,
        device_id=device,
        device_id_type=MESH,
    )


def comm_params(number):
    return pltpu.CompilerParams(
        collective_id=number, has_side_effects=True, vmem_limit_bytes=GRANT
    )


def same_core(tower, at):
    chip, core = at // 2, at % 2
    return [(tower, (chip + k) % 8 * 2 + core) for k in range(1, 8)]


def both_towers(tower, at):
    place, core = tower * 8 + at // 2, at % 2
    others = [(place + k) % 16 for k in range(1, 16)]
    return [(other // 8, other % 8 * 2 + core) for other in others]


def everyone(tower, at):
    me = tower * 16 + at
    others = [(me + k) % 32 for k in range(1, 32)]
    return [(other // 16, other % 16) for other in others]


def group_exchange(scattered, x_ref, o_ref, send_sem, recv_sem):
    tower, at = here()
    chip = at // 2

    def source(k):
        return x_ref.at[k] if scattered else x_ref

    own = pltpu.make_async_copy(source(chip), o_ref.at[chip], send_sem.at[7])
    sent = []
    for k, device in enumerate(same_core(tower, at)):
        copy = remote(
            source((chip + 1 + k) % 8), o_ref.at[chip], send_sem.at[k], recv_sem.at[k], device
        )
        copy.start()
        sent.append(copy)
    own.start()
    own.wait()
    for k in range(7):
        remote(
            source(chip),
            o_ref.at[(chip + 7 - k) % 8],
            send_sem.at[k],
            recv_sem.at[k],
            (tower, at),
        ).wait_recv()
    return sent


class Spread:
    def __init__(self, src, dst, send, recv):
        self.src, self.dst, self.send, self.recv = src, dst, send, recv
        tower, at = here()
        self.core = at % 2
        self.sibling = (tower, at + 1 - 2 * self.core)
        self.devices = self.peers(tower, at)
        self.n = len(self.devices) + 1
        self.place = self.spot(tower, at)
        self.sent = []

    def peers(self, tower, at):
        return both_towers(tower, at)

    def spot(self, tower, at):
        return tower * 8 + at // 2

    def block(self, place):
        return self.src

    def side(self, core):
        return self.dst.at[core]

    def launch(self, src, dst, k, device):
        copy = remote(src, dst, self.send.at[k], self.recv.at[k], device)
        copy.start()
        self.sent.append(copy)

    def start(self):
        for k, device in enumerate(self.devices):
            to = (self.place + 1 + k) % self.n
            self.launch(self.block(to), self.side(self.core).at[self.place], k, device)
        self.own = pltpu.make_async_copy(
            self.block(self.place), self.side(self.core).at[self.place], self.send.at[self.n]
        )
        self.own.start()

    def arrived(self):
        for k in range(self.n - 1):
            source = (self.place + self.n - 1 - k) % self.n
            remote(
                self.block(0),
                self.side(self.core).at[source],
                self.send.at[k],
                self.recv.at[k],
                self.sibling,
            ).wait_recv()
        self.own.wait()

    def relay(self):
        self.arrived()
        side = self.side(self.core)
        self.launch(side, side, self.n - 1, self.sibling)

    def finish(self):
        side = self.side(1 - self.core)
        remote(
            side, side, self.send.at[self.n - 1], self.recv.at[self.n - 1], self.sibling
        ).wait_recv()

    def drain(self):
        for copy in self.sent:
            copy.wait_send()


class Group(Spread):
    def __init__(self, src, dst, send, recv, both=True):
        self.both = both
        super().__init__(src, dst, send, recv)

    def peers(self, tower, at):
        return same_core(tower, at)

    def spot(self, tower, at):
        return at // 2

    def block(self, place):
        return self.src.at[place]

    def side(self, core):
        return self.dst.at[core] if self.both else self.dst

    def finish(self):
        if self.both:
            super().finish()
        else:
            self.arrived()


class Ring:
    def __init__(self, src, dst, send, recv, only=None):
        self.src, self.dst, self.send, self.recv = src, dst, send, recv
        self.only = only
        self.tower, self.at = here()
        self.deep, self.row, self.core = self.at // 4, self.at // 2 % 2, self.at % 2
        self.sibling = (self.tower, self.at + 1 - 2 * self.core)
        self.beside = (self.tower, self.spot(0, 1 - self.row))
        self.sent = []

    def spot(self, k, row):
        return (self.deep + k) % 4 * 4 + row * 2 + self.core

    def act(self, action):
        if self.only is None:
            action()
        else:
            pl.when(self.tower == self.only)(action)

    def launch(self, src, slot, index, device):
        copy = remote(src, self.dst.at[slot], self.send.at[index], self.recv.at[index], device)
        self.act(copy.start)
        self.sent.append(copy)

    def arrived(self, slot, index):
        copy = remote(
            self.src, self.dst.at[slot], self.send.at[index], self.recv.at[index], self.sibling
        )
        self.act(copy.wait_recv)

    def start(self):
        for k in (1, 3, 2):
            self.launch(self.src, self.at, k - 1, (self.tower, self.spot(k, self.row)))
        self.launch(self.src, self.at, 3, self.beside)
        self.launch(self.src, self.at, 7, self.sibling)
        self.own = pltpu.make_async_copy(self.src, self.dst.at[self.at], self.send.at[15])
        self.act(self.own.start)

    def relay_deep(self):
        for k in (1, 3, 2):
            slot = self.spot(4 - k, self.row)
            self.arrived(slot, k - 1)
            self.launch(self.dst.at[slot], slot, 3 + k, self.beside)
            self.launch(self.dst.at[slot], slot, 7 + k, self.sibling)

    def relay_row(self):
        for k in (0, 1, 3, 2):
            slot = self.spot(4 - k, 1 - self.row)
            self.arrived(slot, 3 + k)
            self.launch(self.dst.at[slot], slot, 11 + k, self.sibling)

    def finish(self):
        for index in range(8):
            k, row = index % 4, self.row if index < 4 else 1 - self.row
            slot = (self.deep + 4 - k) % 4 * 4 + row * 2 + 1 - self.core
            self.arrived(slot, 7 + index)
        self.act(self.own.wait)

    def drain(self):
        for copy in self.sent:
            self.act(copy.wait_send)


class Chain:
    def __init__(self, src, dst, send, recv, only=None):
        self.src, self.dst, self.send, self.recv = src, dst, send, recv
        self.only = only
        self.tower, self.at = here()
        self.deep, self.row, self.core = self.at // 4, self.at // 2 % 2, self.at % 2
        self.mate = self.deep + 1 - 2 * (self.deep % 2)
        self.half = self.deep // 2
        self.inner = jnp.logical_or(self.deep == 1, self.deep == 2)
        self.sibling = (self.tower, self.at + 1 - 2 * self.core)
        self.beside = (self.tower, self.spot(self.deep, 1 - self.row))
        self.sent = []

    def spot(self, deep, row):
        return deep * 4 + row * 2 + self.core

    def sources(self):
        return self.deep, self.mate, 2 - 2 * self.half, 3 - 2 * self.half

    def act(self, action, when=None):
        if self.only is not None:
            right = self.tower == self.only
            when = right if when is None else jnp.logical_and(when, right)
        if when is None:
            action()
        else:
            pl.when(when)(action)

    def launch(self, src, slot, sent, landed, device, when=None):
        copy = remote(src, self.dst.at[slot], self.send.at[sent], self.recv.at[landed], device)
        self.act(copy.start, when)
        self.sent.append((copy, when))

    def arrived(self, slot, index):
        copy = remote(
            self.src, self.dst.at[slot], self.send.at[0], self.recv.at[index], self.sibling
        )
        self.act(copy.wait_recv)

    def start(self):
        mate = (self.tower, self.spot(self.mate, self.row))
        far = (self.tower, self.spot(2 - self.half, self.row))
        self.launch(self.src, self.at, 1, 1 + self.deep % 2, far)
        self.launch(self.src, self.at, 0, 0, mate)
        self.launch(self.src, self.at, 2, 3, self.beside)
        self.launch(self.src, self.at, 3, 7, self.sibling)
        self.own = pltpu.make_async_copy(self.src, self.dst.at[self.at], self.send.at[16])
        self.act(self.own.start)

    def relay_deep(self):
        mate = (self.tower, self.spot(self.mate, self.row))
        for k in (1, 2, 3):
            slot = self.spot(self.sources()[k], self.row)
            self.arrived(slot, k - 1)
            block = self.dst.at[slot]
            if k > 1:
                self.launch(block, slot, 4 + k, k - 1, mate, self.inner)
            self.launch(block, slot, 7 + k, 3 + k, self.beside)
            self.launch(block, slot, 16 + k, 7 + k, self.sibling)

    def relay_row(self):
        for k, deep in enumerate(self.sources()):
            slot = self.spot(deep, 1 - self.row)
            self.arrived(slot, 3 + k)
            self.launch(self.dst.at[slot], slot, 11 + k, 11 + k, self.sibling)

    def finish(self):
        for k, deep in enumerate(self.sources()):
            for row, base in ((self.row, 7), (1 - self.row, 11)):
                self.arrived(deep * 4 + row * 2 + 1 - self.core, base + k)
        self.act(self.own.wait)

    def drain(self):
        for copy, when in self.sent:
            self.act(copy.wait_send, when)


def rings(src, dst, send, recv, way=Ring):
    return [
        way(src.at[part], dst.at[part], send.at[part], recv.at[part], 0 if part == 2 else None)
        for part in range(3)
    ]


class Blocks:
    def __init__(self, src, dst, send, recv, shared=1):
        self.src, self.dst, self.send, self.recv = src, dst, send, recv
        self.tower, self.at = here()
        self.shared = shared
        self.sent = []

    def start(self):
        for k in range(1, 16):
            to = (self.at + k) % 16
            copy = remote(
                self.src.at[to // self.shared],
                self.dst.at[self.at],
                self.send.at[k - 1],
                self.recv.at[k - 1],
                (self.tower, to),
            )
            copy.start()
            self.sent.append(copy)
        self.own = pltpu.make_async_copy(
            self.src.at[self.at // self.shared], self.dst.at[self.at], self.send.at[15]
        )
        self.own.start()

    def finish(self):
        for k in range(1, 16):
            remote(
                self.src.at[0],
                self.dst.at[(self.at + 16 - k) % 16],
                self.send.at[k - 1],
                self.recv.at[k - 1],
                (self.tower, self.at),
            ).wait_recv()
        self.own.wait()

    def drain(self):
        for copy in self.sent:
            copy.wait_send()


class Pair:
    def __init__(self, from_zero, zero_dst, from_one, one_dst, sems):
        tower, at = here()
        partner = (1 - tower, at)
        self.tower = tower
        self.up = remote(from_zero, zero_dst, sems.at[0], sems.at[1], partner)
        self.down = remote(from_one, one_dst, sems.at[0], sems.at[1], partner)

    def by_tower(self, zero, one):
        pl.when(self.tower == 0)(zero)
        pl.when(self.tower == 1)(one)

    def start(self):
        self.by_tower(self.up.start, self.down.start)

    def finish(self):
        self.by_tower(self.down.wait_recv, self.up.wait_recv)

    def drain(self):
        self.by_tower(self.up.wait_send, self.down.wait_send)


VECTORS = 5
EXPAND = 2
TURN = 8


class Plan:
    def __init__(self, tower, share, rows, per_device):
        self.tower = tower
        self.share = share
        self.rows = rows
        self.chunk = rows * LANES
        self.per_device = per_device
        self.first_slot = [sum(per_device[:p]) for p in range(6)]
        self.first_chunk = [16 * slot for slot in self.first_slot]
        self.slots = sum(per_device) + 1
        self.total = 16 * sum(per_device) + 1
        spans = [self.span(device) for device in range(32)]
        self.counts = sorted({last - first + 1 for first, last in spans})
        self.local = self.counts[-1]

    def span(self, device):
        first = device * self.share // self.chunk
        last = ((device + 1) * self.share - 1) // self.chunk
        return first, min(last, self.total - 1)

    def bounds(self, device):
        first = device * self.share // self.chunk
        last = ((device + 1) * self.share - 1) // self.chunk
        return first, jnp.minimum(last, self.total - 1)

    def pieces(self, p):
        return self.per_device[p] if p < VECTORS else 1

    def target(self, g):
        piece, base, slot, n = (jnp.int32(0), jnp.int32(0), jnp.int32(0), jnp.int32(1))
        for p in range(VECTORS):
            inside = g >= self.first_chunk[p]
            piece = jnp.where(inside, p, piece)
            base = jnp.where(inside, self.first_chunk[p], base)
            slot = jnp.where(inside, self.first_slot[p], slot)
            n = jnp.where(inside, self.per_device[p], n)
        block = (g - base) // n
        at = jnp.where(piece == EXPAND, (block + TURN) % 16, block)
        return piece, at, slot + (g - base) - block * n


class Deal:
    def __init__(self, plan, s, src, dst, extra, last, sems):
        self.plan, self.s, self.src, self.dst = plan, s, src, dst
        self.extra, self.last = extra, last
        self.chunk_send, self.recv, self.edge, self.fetch = sems
        self.tower, self.at = here()
        self.me = self.tower * 16 + self.at
        self.first, self.last_chunk = plan.bounds(self.me)
        before = (self.me + 31) % 32
        self.head = remote(
            src.at[0], extra, self.edge.at[s, 0], self.edge.at[s, 1], (before // 16, before % 16)
        )

    def send_head(self):
        pl.when(self.me > 0)(self.head.start)

    def move(self, src, i, piece, at_to, slot, wait):
        far = jnp.logical_or(self.tower != self.plan.tower, at_to != self.at)
        recv = self.recv.at[self.s, piece]
        copy = remote(
            src,
            self.dst.at[slot],
            self.chunk_send.at[self.s, i],
            recv,
            (jnp.int32(self.plan.tower), at_to),
        )
        pl.when(far)(copy.wait_send if wait else copy.start)
        if not wait:
            pl.when(jnp.logical_not(far))(
                pltpu.make_async_copy(src, self.dst.at[slot], recv).start
            )

    def whole(self, early, wait):
        def step(i, carry):
            g = self.first + i
            piece, at_to, slot = self.plan.target(g)
            inside = jnp.logical_and(
                jnp.logical_or(i > 0, self.me == 0),
                jnp.logical_or(
                    g < self.last_chunk, jnp.logical_and(self.me == 31, g < self.plan.total - 1)
                ),
            )
            inside = jnp.logical_and(inside, g <= self.last_chunk)
            inside = jnp.logical_and(inside, g < self.plan.total - 1)
            if early is not None:
                hidden = jnp.logical_and(piece >= 2, piece <= 3)
                inside = jnp.logical_and(inside, jnp.logical_not(hidden) if early else hidden)

            @pl.when(inside)
            def _():
                self.move(self.src.at[i], i, piece, at_to, slot, wait)

            return carry

        lax.fori_loop(0, self.plan.local, step, 0)

    def vectors(self, wait):
        @pl.when(self.me == 31)
        def _():
            src = self.src.at[self.last_chunk - self.first]

            def each(k, carry):
                self.move(src, self.plan.local + k, VECTORS, k, self.plan.slots - 1, wait)
                return carry

            lax.fori_loop(0, 16, each, 0)

    def fetch_last(self):
        return pltpu.make_async_copy(
            self.src.at[self.last_chunk - self.first], self.last, self.fetch.at[self.s]
        )

    def join(self):
        @pl.when(self.me < 31)
        def _():
            self.fetch_last().wait()
            self.head.wait_recv()
            self.last[...] = self.last[...] + self.extra[...]
            piece, at_to, slot = self.plan.target(self.last_chunk)
            self.move(self.last, self.plan.local + 16, piece, at_to, slot, False)

    def start_fetch(self):
        pl.when(self.me < 31)(self.fetch_last().start)

    def arrived(self, p):
        part = self.dst.at[pl.ds(self.plan.first_slot[p], self.plan.pieces(p))]
        pltpu.make_async_copy(part, part, self.recv.at[self.s, p]).wait()

    def drain(self):
        pl.when(self.me > 0)(self.head.wait_send)
        self.whole(None, True)
        self.vectors(True)

        @pl.when(self.me < 31)
        def _():
            piece, at_to, slot = self.plan.target(self.last_chunk)
            self.move(self.last, self.plan.local + 16, piece, at_to, slot, True)


class Collect:
    def __init__(self, plan, s, src, dst, send, recv):
        self.plan, self.s, self.src, self.dst = plan, s, src, dst
        self.send, self.recv = send, recv
        self.tower, self.at = here()
        self.me = self.tower * 16 + self.at

    def one(self, owner, slot, g, which, wait):
        first, _ = self.plan.bounds(owner)
        far = owner != self.me
        recv = self.recv.at[self.s]
        copy = remote(
            self.src.at[slot],
            self.dst.at[g - first],
            self.send.at[which, slot],
            recv,
            (owner // 16, owner % 16),
        )
        pl.when(far)(copy.wait_send if wait else copy.start)
        if not wait:
            pl.when(jnp.logical_not(far))(
                pltpu.make_async_copy(self.src.at[slot], self.dst.at[g - first], recv).start
            )

    def piece(self, p, wait):
        n = self.plan.pieces(p)

        def step(i, carry):
            slot = self.plan.first_slot[p] + i
            block = (self.at + 16 - TURN) % 16 if p == EXPAND else self.at
            g = self.plan.first_chunk[p] + block * n + i if p < VECTORS else self.plan.total - 1
            low = g * self.plan.chunk // self.plan.share
            high = jnp.minimum(((g + 1) * self.plan.chunk - 1) // self.plan.share, 31)
            self.one(low, slot, g, 0, wait)
            pl.when(high != low)(lambda: self.one(high, slot, g, 1, wait))
            return carry

        if p == VECTORS:


            @pl.when(self.at == 0)
            def _():
                step(0, 0)

        else:
            lax.fori_loop(0, n, step, 0)

    def finish(self):
        first, last = self.plan.bounds(self.me)
        held = last - first + 1
        for n in self.plan.counts:

            @pl.when(held == n)
            def _():
                part = self.dst.at[pl.ds(0, n)]
                pltpu.make_async_copy(part, part, self.recv.at[self.s]).wait()


SEQS = 16
HEADS = 16


class Tower:
    def __init__(self, index, width, hidden, length, room, run, causal):
        self.index = index
        self.width = width
        self.hidden = hidden
        self.length = length
        self.room = room
        self.run = run
        self.causal = causal
        self.heads = width // HEAD
        self.block = width // 16
        self.part = hidden // 8
        self.reduce_rows = hidden // 16


TOWERS = (
    Tower(0, D_IMG, FF_IMG, 50, 64, 10, False),
    Tower(1, D_TXT, FF_TXT, 77, 80, 11, True),
)
ROOM = 80
WIDTH = D_IMG
PART = FF_IMG // 8


def each_tower(run):
    tower = lax.axis_index("tower")
    for kind in TOWERS:
        pl.when(tower == kind.index)(functools.partial(run, kind))


def dot_nn(a, b):
    return lax.dot_general(a, b, (((1,), (0,)), ((), ())), preferred_element_type=WIDE)


def dot_nt(a, b):
    return lax.dot_general(a, b, (((1,), (1,)), ((), ())), preferred_element_type=WIDE)


def dot_tn(a, b):
    return lax.dot_general(a, b, (((0,), (0,)), ((), ())), preferred_element_type=WIDE)


def standardise(rows):
    centred = rows - jnp.mean(rows, axis=-1, keepdims=True)
    spread = jnp.mean(centred * centred, axis=-1, keepdims=True)
    rate = lax.rsqrt(spread + 1e-05)
    return centred * rate, rate


def norm_back(grad, gain, hat, rate):
    scaled = grad * gain
    return rate * (
        scaled
        - jnp.mean(scaled, axis=-1, keepdims=True)
        - hat * jnp.mean(scaled * hat, axis=-1, keepdims=True)
    )


def spans(kind):
    return [
        (lo, min(lo + 512, kind.width), lo // HEAD, (min(lo + 512, kind.width) - lo) // HEAD)
        for lo in range(0, kind.width, 512)
    ]


def head_rows(rows, span):
    lo, hi, _, n = span
    part = rows[:, lo:hi]
    owner = lax.broadcasted_iota(jnp.int32, part.shape, 1) // HEAD
    nothing = jnp.zeros_like(part)
    return jnp.concatenate([jnp.where(owner == h, part, nothing) for h in range(n)], axis=0)


def from_head_rows(rows, span):
    _, _, _, n = span
    owner = lax.broadcasted_iota(jnp.int32, (SEQS, rows.shape[1]), 1) // HEAD
    total = jnp.zeros((SEQS, rows.shape[1]), rows.dtype)
    for h in range(n):
        total = jnp.where(owner == h, rows[h * SEQS : (h + 1) * SEQS], total)
    return total


def side_by_side(parts):
    return parts[0] if len(parts) == 1 else jnp.concatenate(parts, axis=1)


def get_rows(ref, place, width):
    return side_by_side([ref[c, place, :] for c in range(width // LANES)])


def put_rows(ref, place, value):
    for c in range(value.shape[1] // LANES):
        ref[c, place, :] = value[:, c * LANES : (c + 1) * LANES]


def matrix(ref, kind, start, width):
    return jnp.concatenate(
        [
            ref[part, at, :, start : start + width]
            for at in range(16)
            for part in range(kind.block // 16)
        ],
        axis=0,
    )


def vector(vec_ref, kind, row):
    return vec_ref[row : row + 1, : kind.width]


def pieces_of(kind):
    return (
        (kind.block, 3 * kind.width),
        (kind.block, kind.width),
        (kind.block, kind.hidden),
        (kind.reduce_rows, kind.width),
        (kind.block, EMB),
        (16, kind.width),
    )


def lane_blocks(kind, plan, p):
    height, width = pieces_of(kind)[p]
    pitch = width // LANES
    base = plan.first_slot[p] * plan.rows if p < VECTORS else (plan.slots - 1) * plan.rows
    return [(c, pl.ds(base + c, height, stride=pitch)) for c in range(pitch)]


def lift(kind, plan, p, slots, flat):
    n = plan.pieces(p)
    slot = plan.first_slot[p]
    rows = slots[slot : slot + n].reshape(n * plan.rows, LANES)
    flat[slot * plan.rows : (slot + n) * plan.rows, :] = rows.astype(WIDE)
    return [(c, flat[place, :]) for c, place in lane_blocks(kind, plan, p)]


def drop(kind, plan, p, value, slots, flat):
    for c, place in lane_blocks(kind, plan, p):
        flat[place, :] = value(c)
    n = plan.pieces(p)
    slot = plan.first_slot[p]
    rows = flat[slot * plan.rows : (slot + n) * plan.rows, :]
    slots[slot : slot + n] = rows.reshape(n, plan.rows, LANES).astype(LOW)


def expand_matrix(ref, kind):
    return jnp.concatenate(
        [
            ref[at % 2, at // 2, : kind.block, : kind.part]
            for at in ((block + TURN) % 16 for block in range(16))
        ],
        axis=0,
    )


def reduce_matrix(ref, kind):
    return ref[:, : kind.reduce_rows, : kind.width].reshape(kind.part, kind.width)


def hidden_bias(vec_ref, kind):
    chip = lax.axis_index("dp") // 2
    whole = vec_ref[...]
    row = lax.broadcasted_iota(jnp.int32, (16, 1), 0)
    line = jnp.sum(jnp.where(row == 10 + chip // 2, whole, 0.0), axis=0, keepdims=True)
    return jnp.where(
        chip % 2 == 0, line[:, : kind.part], line[:, kind.part : 2 * kind.part]
    )


def hidden_kernel(second_ref, raise_ref, reduce_ref, vec_ref, part_ref, raised_ref):
    def run(kind):
        width = kind.width
        rows = second_ref[:, :, :width].reshape(8 * SEQS, width)
        raised = dot_nn(rows, expand_matrix(raise_ref, kind)) + hidden_bias(vec_ref, kind)
        raised_ref[:, : kind.part] = raised
        active = (raised * jax.nn.sigmoid(1.702 * raised)).astype(LOW)
        part = dot_nn(active, reduce_matrix(reduce_ref, kind))
        part_ref[:, :, :width] = part.reshape(8, SEQS, width).astype(LOW)

    each_tower(run)


def hidden_back_kernel(
    grad_ref,
    second_ref,
    raised_ref,
    raise_ref,
    reduce_ref,
    back_ref,
    raise_grad_ref,
    reduce_keep_ref,
    reduce_send_ref,
    bias_ref,
    whole,
):
    def run(kind):
        width, part = kind.width, kind.part
        grads = grad_ref[:, :, :width].reshape(8 * SEQS, width)
        rows = second_ref[:, :, :width].reshape(8 * SEQS, width)
        raised = raised_ref[:, :part]
        gate = jax.nn.sigmoid(1.702 * raised)
        active = (raised * gate).astype(LOW)
        slope = gate + 1.702 * raised * gate * (1.0 - gate)
        raised_grad = dot_nt(grads, reduce_matrix(reduce_ref, kind)) * slope
        low_grad = raised_grad.astype(LOW)
        bias_ref[0:1, :part] = jnp.sum(low_grad.astype(WIDE), axis=0, keepdims=True)
        back = dot_nt(low_grad, expand_matrix(raise_ref, kind))
        back_ref[:, :, :width] = back.reshape(8, SEQS, width).astype(LOW)
        raise_grad = dot_tn(rows, low_grad).reshape(16, kind.block, part).astype(LOW)
        for block in range(16):
            at = (block + TURN) % 16
            raise_grad_ref[at % 2, at // 2, : kind.block, :part] = raise_grad[block]
        whole[:part, :width] = dot_tn(active, grads)
        core = lax.axis_index("dp") % 2
        n = kind.reduce_rows
        keep = pl.multiple_of(core * n, 64)
        send = pl.multiple_of((1 - core) * n, 64)
        reduce_keep_ref[:n, :width] = whole[pl.ds(keep, n), :width]
        reduce_send_ref[:n, :width] = whole[pl.ds(send, n), :width].astype(LOW)

    each_tower(run)


def embed_kernel(part_ref, middle_ref, gat_ref, vec_ref, emb_ref, final_ref, pooled_ref, proj_ref):
    def run(kind):
        width = kind.width
        final = (
            middle_ref[:, :width]
            + jnp.sum(part_ref[:, :, :width].astype(WIDE), axis=0)
            + vector(vec_ref, kind, 7)
        )
        final_ref[:, :width] = final
        hat, _ = standardise(final)
        pooled = (hat * vector(vec_ref, kind, 8) + vector(vec_ref, kind, 9)).astype(LOW)
        pooled_ref[:, :width] = pooled
        proj = dot_nn(pooled, matrix(gat_ref, kind, 0, EMB))
        proj_ref[...] = proj
        size = jnp.sum(proj * proj, axis=-1, keepdims=True) + 1e-06
        emb_ref[...] = (proj * lax.rsqrt(size)).astype(LOW)

    each_tower(run)


def objective_kernel(
    scale_ref,
    all_ref,
    valid_ref,
    final_ref,
    proj_ref,
    gat_ref,
    vec_ref,
    low_ref,
    grad_ref,
    proj_grad_ref,
    final_vec_ref,
    loss_ref,
    scale_new_ref,
    own_scr,
):
    def ordered(which):
        blocks = []
        for half in range(2):
            for j in range(16):
                rows = all_ref[j % 2, which * 8 + j // 2].astype(WIDE)
                blocks.append(rows[half * 8 : half * 8 + 8])
        return jnp.concatenate(blocks, axis=0).astype(LOW)

    img, txt = ordered(0), ordered(1)
    total = img.shape[0]
    scale = jnp.exp(jnp.full((1, 1), scale_ref[0], WIDE))
    lines = []
    for d in range(32):
        rows = valid_ref[d % 2, d // 2].astype(WIDE)
        lines.append(jnp.concatenate([rows[:8], rows[8:]], axis=1))
    allowed = jnp.concatenate(lines, axis=0) > 0
    same = lax.broadcasted_iota(jnp.int32, (total, total), 0) == lax.broadcasted_iota(
        jnp.int32, (total, total), 1
    )
    same = same.astype(WIDE)

    def side(left, right):
        logits = scale * dot_nt(left, right)
        masked = jnp.where(allowed, logits, -1e30)
        top = jnp.max(masked, axis=1, keepdims=True)
        lse = jnp.log(jnp.sum(jnp.exp(masked - top), axis=1, keepdims=True)) + top
        terms = 0.5 * (jnp.where(allowed, jnp.exp(logits - lse), 0.0) - same)
        loss = 0.5 * (
            jnp.sum(lse, axis=0, keepdims=True)
            - jnp.sum(jnp.sum(logits * same, axis=1, keepdims=True), axis=0, keepdims=True)
        )
        rate = jnp.sum(jnp.sum(terms * logits, axis=1, keepdims=True), axis=0, keepdims=True)
        return (scale * terms).astype(LOW), loss, rate

    row_back, row_loss, row_rate = side(img, txt)
    col_back, col_loss, col_rate = side(txt, img)
    loss_ref[0] = jnp.sum(row_loss + col_loss) / total
    parts = advance(
        scale_ref[0], scale_ref[1], scale_ref[2], jnp.sum(row_rate + col_rate), scale_rate
    )
    for k in range(3):
        scale_new_ref[k] = parts[k]

    def run(kind):
        width = kind.width
        if kind.index == 0:
            emb_grad = dot_nn(row_back, txt) + dot_tn(col_back, txt)
        else:
            emb_grad = dot_nn(col_back, img) + dot_tn(row_back, img)
        own_scr[...] = emb_grad
        at = lax.axis_index("dp")
        mine = jnp.concatenate(
            [
                own_scr[pl.ds(pl.multiple_of(half * 128 + at * 8, 8), 8), :]
                for half in range(2)
            ],
            axis=0,
        )
        proj = proj_ref[...]
        size = jnp.sum(proj * proj, axis=-1, keepdims=True) + 1e-06
        along = jnp.sum(proj * mine, axis=-1, keepdims=True)
        proj_grad = ((mine - proj * along / size) * lax.rsqrt(size)).astype(LOW)
        proj_grad_ref[...] = proj_grad
        pooled_grad = dot_nt(proj_grad, matrix(gat_ref, kind, 0, EMB))
        hat, rate = standardise(final_ref[:, :width])
        final_vec_ref[0:1, :width] = jnp.sum(pooled_grad * hat, axis=0, keepdims=True)
        final_vec_ref[1:2, :width] = jnp.sum(pooled_grad, axis=0, keepdims=True)
        final_grad = norm_back(pooled_grad, vector(vec_ref, kind, 8), hat, rate)
        grad_ref[:, :width] = final_grad
        low = final_grad.astype(LOW)
        low_ref[:, :width] = low
        final_vec_ref[2:3, :width] = jnp.sum(low.astype(WIDE), axis=0, keepdims=True)

    each_tower(run)


def step_kernel(
    plans,
    ends_ref,
    scale_ref,
    img_src,
    txt_src,
    valid_ref,
    img_own,
    txt_own,
    loss_ref,
    scale_new_ref,
    img_keep,
    txt_keep,
    img_chunks,
    txt_chunks,
    second_ref,
    middle_ref,
    query_ref,
    keyed_ref,
    mixture_ref,
    weight_ref,
    first_ref,
    first_rows,
    img_in,
    txt_in,
    ask_ref,
    mix_ref,
    emb_ref,
    vec_ref,
    raise_ref,
    reduce_ref,
    pairs_ref,
    img_slots,
    txt_slots,
    img_extra,
    txt_extra,
    img_last,
    txt_last,
    flat,
    ask_block,
    mix_block,
    emb_block,
    raise_block,
    reduce_block,
    mask_block,
    top_scr,
    at_scr,
    score_scr,
    low_scr,
    grad_ref,
    pooled_ref,
    proj_grad_ref,
    final_vec_ref,
    raise_grad_ref,
    reduce_keep_ref,
    reduce_send_ref,
    bias_ref,
    backs_ref,
    seconds,
    part,
    parts,
    raised,
    emb,
    all_embs,
    final,
    proj,
    low,
    lows,
    back,
    own_scr,
    whole,
    img_send,
    txt_send,
    img_home,
    txt_home,
    rows_grad,
    middle_scr,
    second_scr,
    valued_scr,
    turn_scr,
    shared_scr,
    slope_scr,
    left_scr,
    left_block,
    turn_block,
    left_all,
    turn_all,
    early_block,
    early_all,
    late_block,
    late_all,
    lines_block,
    lines_all,
    raise_half,
    risen_block,
    raise_all,
    reduce_in,
    img_home_slots,
    txt_home_slots,
    gains,
    top_grad_scr,
    deal_send,
    deal_recv,
    deal_edge,
    deal_fetch,
    ask_send,
    ask_recv,
    mix_send,
    mix_recv,
    emb_send,
    emb_recv,
    raise_send,
    raise_recv,
    reduce_sems,
    pair_sems,
    mask_send,
    mask_recv,
    group_send,
    group_recv,
    embs_send,
    embs_recv,
    home_sems,
    risen_send,
    risen_recv,
    left_send,
    left_recv,
    turn_send,
    turn_recv,
    early_send,
    early_recv,
    late_send,
    late_recv,
    lines_send,
    lines_recv,
    home_pair_sems,
    collect_send,
    collect_recv,
):
    tower, at = here()
    core = at % 2
    me = tower * 16 + at
    sibling = (tower, at + 1 - 2 * core)
    greet(everyone(tower, at))
    deal_sems = (deal_send, deal_recv, deal_edge, deal_fetch)
    deals = [
        Deal(plans[0], 0, img_src, img_slots, img_extra, img_last, deal_sems),
        Deal(plans[1], 1, txt_src, txt_slots, txt_extra, txt_last, deal_sems),
    ]
    pair = Pair(txt_own, txt_in, img_own, img_in, pair_sems)
    asks = rings(ask_block, ask_ref, ask_send, ask_recv)
    mixes = rings(mix_block, mix_ref, mix_send, mix_recv)
    embeds = rings(emb_block, emb_ref, emb_send, emb_recv, Chain)
    rise = Group(raise_block, raise_ref, raise_send, raise_recv)
    fall = remote(
        reduce_block, reduce_ref.at[core], reduce_sems.at[0], reduce_sems.at[1], sibling
    )
    fall_own = pltpu.make_async_copy(reduce_block, reduce_ref.at[core], reduce_sems.at[2])
    masks = Spread(mask_block, pairs_ref, mask_send, mask_recv)
    rows = valid_ref[...].astype(WIDE)
    mask_block[...] = jnp.concatenate([rows[:, :LANES], rows[:, LANES:]], axis=0).astype(LOW)

    for deal in deals:
        deal.send_head()
        deal.start_fetch()
        deal.vectors(False)
    for deal in deals:
        deal.whole(True, False)
    for deal in deals:
        deal.whole(False, False)
    pair.start()
    for deal in deals:
        deal.join()

    def put(ref, lane, value):
        if len(ref.shape) == 2:
            ref[: value.shape[0], lane : lane + LANES] = value
        else:
            for part in range(value.shape[0] // 16):
                ref[part, :, lane : lane + LANES] = value[part * 16 : (part + 1) * 16]

    def lift_to(kind, p, ref, start):
        slots = (img_slots, txt_slots)[kind.index]
        for c, value in lift(kind, plans[kind.index], p, slots, flat):
            lane = start + c * LANES
            put(ref, lane, value.astype(ref.dtype))

    def tokens_of(kind, half):
        own, arrived = ((img_own, img_in), (txt_own, txt_in))[kind.index]
        return own if half == kind.index else arrived

    def steps(kind):
        return [(t, kind.run) for t in range(0, kind.length, kind.run)]

    def is_end(kind, half, t, n):
        row = lax.broadcasted_iota(jnp.int32, (8, 1), 0)
        ends = jnp.zeros((8, 1), jnp.int32)
        for i in range(8):
            ends = jnp.where(row == i, ends_ref[(half * 16 + at) * 8 + i], ends)
        position = lax.broadcasted_iota(jnp.int32, (n, 8, 1), 0) + t
        return (position == ends[None]).astype(WIDE)

    def normalise(kind, half):
        width, room = kind.width, kind.room
        ref = tokens_of(kind, half)
        gain, shift = vector(vec_ref, kind, 0), vector(vec_ref, kind, 1)
        tops, raws = jnp.zeros((8, width), WIDE), jnp.zeros((8, width), WIDE)
        for t, n in steps(kind):
            rows = ref[t : t + n].astype(WIDE).reshape(n * 8, width)
            hat, _ = standardise(rows)
            first = (hat * gain + shift).astype(LOW).astype(WIDE)
            put_rows(first_rows, pl.ds(t * 8, n * 8), first)
            if kind.causal:
                chosen = is_end(kind, half, t, n)
                tops = tops + jnp.sum(first.reshape(n, 8, width) * chosen, axis=0)
                raws = raws + jnp.sum(rows.reshape(n, 8, width) * chosen, axis=0)
            elif t == 0:
                tops, raws = first[:8], rows[:8]
        top_scr[half * 8 : half * 8 + 8, :width] = tops
        at_scr[half * 8 : half * 8 + 8, :width] = raws
        spare = (room - kind.length) * 8
        put_rows(first_rows, pl.ds(kind.length * 8, spare), jnp.zeros((spare, width), WIDE))
        for i in range(8):
            line = get_rows(first_rows, pl.ds(i, room, stride=8), width)
            first_ref[half * 8 + i, :room, :width] = line.astype(LOW)

    def begin(kind):
        deal = deals[kind.index]
        deal.arrived(VECTORS)
        lift_to(kind, VECTORS, vec_ref, 0)
        normalise(kind, kind.index)

    each_tower(begin)

    def place_inputs(kind):
        deals[kind.index].arrived(0)
        slots = (img_slots, txt_slots)[kind.index]
        per = kind.width // LANES
        for c, value in lift(kind, plans[kind.index], 0, slots, flat):
            lane = c // per * WIDTH + c % per * LANES
            ref = ask_block
            if lane >= 2 * WIDTH:
                ref, lane = mix_block, lane - 2 * WIDTH
            put(ref, lane, value.astype(LOW))

    each_tower(place_inputs)
    for ring in asks:
        ring.start()

    def place_hidden(kind):
        deal, plan = deals[kind.index], plans[kind.index]
        slots = (img_slots, txt_slots)[kind.index]
        deal.arrived(2)
        per = kind.part // LANES
        for c, value in lift(kind, plan, 2, slots, flat):
            lane = c % per * LANES
            raise_block[c // per, : kind.block, lane : lane + LANES] = value.astype(LOW)
        deal.arrived(3)
        lift_to(kind, 3, reduce_block, 0)

    def place_rest(kind):
        deals[kind.index].arrived(1)
        lift_to(kind, 1, mix_block, WIDTH)
        deals[kind.index].arrived(4)
        lift_to(kind, 4, emb_block, 0)

    each_tower(place_rest)

    def question(kind):
        width = kind.width
        tops = top_scr[:, :width].astype(LOW)
        query = dot_nn(tops, matrix(ask_ref, kind, 0, width)) + vector(vec_ref, kind, 2)
        query = query.astype(LOW)
        query_ref[:, :width] = query
        for span in spans(kind):
            lo, hi, first_head, n = span
            put_rows(
                keyed_ref,
                pl.ds(first_head * SEQS, n * SEQS),
                dot_nt(head_rows(query, span), matrix(ask_ref, kind, WIDTH + lo, hi - lo)) * 0.125,
            )
        dead = (HEADS - kind.heads) * SEQS
        put_rows(keyed_ref, pl.ds(kind.heads * SEQS, dead), jnp.zeros((dead, width), WIDE))

    for ask, mix in zip(asks, mixes):
        ask.relay_deep()
        mix.start()
    for embed in embeds:
        embed.start()
    for ask in asks:
        ask.relay_row()
    each_tower(place_hidden)
    rise.start()
    fall.start()
    fall_own.start()
    pair.finish()
    each_tower(lambda kind: normalise(kind, 1 - kind.index))
    masks.start()
    for ask in asks:
        ask.finish()
    each_tower(question)
    for ring in (*mixes, *embeds):
        ring.relay_deep()

    def score(kind):
        width, room = kind.width, kind.room
        lane = lax.broadcasted_iota(jnp.int32, (HEADS, room), 1)
        for s in range(SEQS):
            keys = get_rows(keyed_ref, pl.ds(s, HEADS, stride=SEQS), width).astype(LOW)
            scores = dot_nt(keys, first_ref[s, :room, :width])
            if kind.causal:
                allowed = lane <= ends_ref[(s // 8 * 16 + at) * 8 + s % 8]
            else:
                allowed = lane < kind.length
            score_scr[s * HEADS : (s + 1) * HEADS, :room] = jnp.where(allowed, scores, -1e30)
        scores = score_scr[:, :room]
        raw = jnp.exp(scores - jnp.max(scores, axis=-1, keepdims=True))
        weights = raw / jnp.sum(raw, axis=-1, keepdims=True)
        head = lax.broadcasted_iota(jnp.int32, (SEQS * HEADS, 1), 0) % HEADS
        weights = jnp.where(head < kind.heads, weights, 0.0)
        weight_ref[:, :room] = weights
        low_scr[: SEQS * HEADS, :room] = weights.astype(LOW)

    each_tower(score)
    for ring in (*mixes, *embeds):
        ring.relay_row()

    def mixture(kind):
        width, room = kind.width, kind.room
        for s in range(SEQS):
            mixed = dot_nn(
                low_scr[s * HEADS : (s + 1) * HEADS, :room], first_ref[s, :room, :width]
            )
            put_rows(mixture_ref, pl.ds(s, HEADS, stride=SEQS), mixed)
        totals = jnp.sum(
            low_scr[: SEQS * HEADS, :room].astype(WIDE), axis=-1, keepdims=True
        )
        score_scr[...] = jnp.broadcast_to(totals, score_scr.shape)

    each_tower(mixture)

    for mix in mixes:
        mix.finish()

    def answer(kind):
        width = kind.width
        mixed = []
        bias = vector(vec_ref, kind, 3)
        for span in spans(kind):
            lo, hi, first_head, n = span
            z = get_rows(mixture_ref, pl.ds(first_head * SEQS, n * SEQS), width).astype(LOW)
            valued = dot_nn(z, matrix(mix_ref, kind, lo, hi - lo))
            totals = jnp.concatenate(
                [score_scr[pl.ds(first_head + h, SEQS, stride=HEADS), 0:1] for h in range(n)],
                axis=0,
            )
            mixed.append(from_head_rows(valued + totals * bias[:, lo:hi], span))
        mixed = side_by_side(mixed).astype(LOW)
        middle = (
            at_scr[:, :width]
            + dot_nn(mixed, matrix(mix_ref, kind, WIDTH, width))
            + vector(vec_ref, kind, 4)
        )
        middle_ref[:, :width] = middle
        hat, _ = standardise(middle)
        second_ref[:, :width] = (
            hat * vector(vec_ref, kind, 5) + vector(vec_ref, kind, 6)
        ).astype(LOW)
        put_rows(mixture_ref, pl.ds(12 * SEQS, SEQS), top_scr[:, :width])
        put_rows(mixture_ref, pl.ds(13 * SEQS, SEQS), mixed.astype(WIDE))

    each_tower(answer)
    rise.relay()
    masks.relay()
    for embed in embeds:
        embed.finish()
    rise.finish()
    fall_own.wait()
    remote(
        reduce_block, reduce_ref.at[1 - core], reduce_sems.at[0], reduce_sems.at[1], sibling
    ).wait_recv()

    sent = group_exchange(False, second_ref, seconds, group_send.at[0], group_recv.at[0])
    hidden_kernel(seconds, raise_ref, reduce_ref, vec_ref, part, raised)
    sent += group_exchange(True, part, parts, group_send.at[1], group_recv.at[1])
    embed_kernel(parts, middle_ref, emb_ref, vec_ref, emb, final, pooled_ref, proj)
    embs = Spread(emb, all_embs, embs_send, embs_recv)
    embs.start()
    masks.finish()
    embs.relay()
    embs.finish()
    objective_kernel(
        scale_ref,
        all_embs,
        pairs_ref,
        final,
        proj,
        emb_ref,
        vec_ref,
        low,
        grad_ref,
        proj_grad_ref,
        final_vec_ref,
        loss_ref,
        scale_new_ref,
        own_scr,
    )
    sent += group_exchange(False, low, lows, group_send.at[2], group_recv.at[2])
    hidden_back_kernel(
        lows,
        seconds,
        raised,
        raise_ref,
        reduce_ref,
        back,
        raise_grad_ref,
        reduce_keep_ref,
        reduce_send_ref,
        bias_ref,
        whole,
    )
    sent += group_exchange(True, back, backs_ref, group_send.at[3], group_recv.at[3])
    halves = remote(
        raise_grad_ref.at[1 - core], raise_half, home_sems.at[0], home_sems.at[1], sibling
    )
    fallen = remote(reduce_send_ref, reduce_in, home_sems.at[2], home_sems.at[3], sibling)
    halves.start()
    fallen.start()
    risen_group = Group(risen_block, raise_all, risen_send, risen_recv, False)

    lefts = Blocks(left_block, left_all, left_send, left_recv)
    turns = Blocks(turn_block, turn_all, turn_send, turn_recv)
    early = Chain(early_block, early_all, early_send, early_recv)
    late = Ring(late_block, late_all, late_send, late_recv)
    home_pair = Pair(img_send, img_home, txt_send, txt_home, home_pair_sems)
    collects = [
        Collect(plans[0], 0, img_home_slots, img_chunks, collect_send.at[0], collect_recv),
        Collect(plans[1], 1, txt_home_slots, txt_chunks, collect_send.at[1], collect_recv),
    ]

    def outputs(kind):
        width = kind.width
        second_grad = jnp.sum(backs_ref[:, :, :width].astype(WIDE), axis=0)
        second_scr[:, :width] = second_grad
        hat, rate = standardise(middle_ref[:, :width])
        middle_grad = grad_ref[:, :width] + norm_back(
            second_grad, vector(vec_ref, kind, 5), hat, rate
        )
        middle_scr[:, :width] = middle_grad
        output_grad = middle_grad.astype(LOW)
        mixed_grad = dot_nt(output_grad, matrix(mix_ref, kind, WIDTH, width)).astype(LOW)
        early_block[:, 0:width] = query_ref[:, :width]
        early_block[:, WIDTH : WIDTH + width] = mixed_grad
        early_block[:, 2 * WIDTH : 2 * WIDTH + width] = output_grad
        early_block[:, 3 * WIDTH : 3 * WIDTH + EMB] = proj_grad_ref[...]
        left_scr[:, :width] = get_rows(mixture_ref, slice(None), width)
        left_scr[14 * SEQS : 15 * SEQS, :width] = pooled_ref[:, :width].astype(WIDE)
        left_scr[15 * SEQS :, :width] = jnp.zeros((SEQS, width), WIDE)

    each_tower(outputs)
    early.start()

    def turned(kind):
        width, block = kind.width, kind.block
        left_block[:, :block, :] = left_scr[:, :width].T.reshape(16, block, 256).astype(LOW)

    each_tower(turned)
    lefts.start()

    def values(kind):
        width = kind.width
        mixed_grad = early_block[:, WIDTH : WIDTH + width]
        bias = vector(vec_ref, kind, 3)
        dead = kind.heads * SEQS
        put_rows(valued_scr, pl.ds(dead, 256 - dead), jnp.zeros((256 - dead, width), WIDE))
        shared_scr[dead:, :] = jnp.zeros((256 - dead, LANES), WIDE)
        for span in spans(kind):
            lo, hi, first_head, n = span
            rows = head_rows(mixed_grad, span)
            place = pl.ds(first_head * SEQS, n * SEQS)
            put_rows(valued_scr, place, dot_nt(rows, matrix(mix_ref, kind, lo, hi - lo)))
            constant = jnp.sum(rows.astype(WIDE) * bias[:, lo:hi], axis=-1, keepdims=True)
            shared_scr[place, :] = jnp.broadcast_to(constant, (n * SEQS, LANES))

    each_tower(values)
    halves.wait_recv()
    risen_block[...] = (
        raise_grad_ref[core].astype(WIDE) + raise_half[...].astype(WIDE)
    ).astype(LOW)
    risen_group.start()

    def slopes(kind):
        width, room = kind.width, kind.room
        for s in range(SEQS):
            line = pl.ds(s, HEADS, stride=SEQS)
            slope = dot_nt(
                get_rows(valued_scr, line, width).astype(LOW), first_ref[s, :room, :width]
            )
            slope_scr[s * HEADS : (s + 1) * HEADS, :room] = slope + shared_scr[line, 0:1]
        weights = weight_ref[:, :room]
        slope = slope_scr[:, :room]
        slope = weights * (slope - jnp.sum(weights * slope, axis=-1, keepdims=True))
        both = jnp.concatenate(
            [slope.reshape(SEQS, HEADS, room), weights.reshape(SEQS, HEADS, room)], axis=1
        )
        low_scr[:, :room] = both.reshape(2 * SEQS * HEADS, room).astype(LOW)

    each_tower(slopes)
    early.relay_deep()

    def tokens(kind):
        width, room = kind.width, kind.room
        for s in range(SEQS):
            line = pl.ds(s, HEADS, stride=SEQS)
            both = low_scr[2 * s * HEADS : 2 * (s + 1) * HEADS, :room]
            first = first_ref[s, :room, :width]
            put_rows(turn_scr, line, dot_nn(both[:HEADS], first))
            right = jnp.concatenate(
                [get_rows(keyed_ref, line, width), get_rows(valued_scr, line, width)], axis=0
            )
            put_rows(
                rows_grad.at[s // 8],
                pl.ds(s % 8, room, stride=8),
                dot_tn(both, right.astype(LOW)),
            )

    each_tower(tokens)
    early.relay_row()

    def queries(kind):
        width, block = kind.width, kind.block
        grads = []
        for span in spans(kind):
            lo, hi, first_head, n = span
            rows = get_rows(turn_scr, pl.ds(first_head * SEQS, n * SEQS), width).astype(LOW)
            back = dot_nn(rows, matrix(ask_ref, kind, WIDTH + lo, hi - lo)) * 0.125
            grads.append(from_head_rows(back, span))
        query_grad = side_by_side(grads).astype(LOW)
        late_block[:, :width] = query_grad
        top_grad_scr[:, :width] = dot_nt(query_grad, matrix(ask_ref, kind, 0, width))
        turn_block[:, :block, :] = (
            get_rows(turn_scr, slice(None), width).T.reshape(16, block, 256).astype(LOW)
        )

    each_tower(queries)
    late.start()
    turns.start()
    gains[...] = jnp.zeros_like(gains)

    def finish(kind, half):
        width = kind.width
        ref = tokens_of(kind, half)
        keep, send = ((img_keep, img_send), (txt_keep, txt_send))[kind.index]
        gain = vector(vec_ref, kind, 0)
        top = top_grad_scr[half * 8 : half * 8 + 8, :width]
        low = middle_scr[half * 8 : half * 8 + 8, :width]
        gain_sum = jnp.zeros((1, width), WIDE)
        shift_sum = jnp.zeros((1, width), WIDE)
        for t, n in steps(kind):
            hat, rate = standardise(ref[t : t + n].astype(WIDE).reshape(n * 8, width))
            grad = get_rows(rows_grad.at[half], pl.ds(t * 8, n * 8), width)
            chosen = None
            if kind.causal:
                chosen = is_end(kind, half, t, n)
            elif t == 0:
                chosen = (lax.broadcasted_iota(jnp.int32, (n, 8, 1), 0) == 0).astype(WIDE)
            if chosen is not None:
                grad = grad + (chosen * top[None]).reshape(n * 8, width)
            gain_sum += jnp.sum(grad * hat, axis=0, keepdims=True)
            shift_sum += jnp.sum(grad, axis=0, keepdims=True)
            result = norm_back(grad, gain, hat, rate)
            if chosen is not None:
                result = result + (chosen * low[None]).reshape(n * 8, width)
            result = result.reshape(n, 8, width)
            if half == kind.index:
                keep[t : t + n] = result
            else:
                send[t : t + n] = result.astype(LOW)
        gains[0:1, :width] += gain_sum
        gains[1:2, :width] += shift_sum

    each_tower(lambda kind: finish(kind, 1 - kind.index))
    home_pair.start()
    risen_group.finish()
    fallen.wait_recv()

    def slots_of(kind):
        return (img_home_slots, txt_home_slots)[kind.index]

    def hidden_grads(kind):
        plan, collect = plans[kind.index], collects[kind.index]
        block, n, per = kind.block, kind.reduce_rows, kind.part // LANES

        def risen(c):
            chip, lane = c // per, c % per * LANES
            return raise_all[chip, :block, lane : lane + LANES].astype(WIDE)

        def fallen(c):
            lane = c * LANES
            return reduce_keep_ref[:n, lane : lane + LANES] + reduce_in[
                :n, lane : lane + LANES
            ].astype(WIDE)

        drop(kind, plan, 2, risen, slots_of(kind), flat)
        collect.piece(2, False)
        drop(kind, plan, 3, fallen, slots_of(kind), flat)
        collect.piece(3, False)

    each_tower(hidden_grads)
    late.relay_deep()
    each_tower(lambda kind: finish(kind, kind.index))
    late.relay_row()

    def lines(kind):
        width = kind.width
        hat, _ = standardise(middle_ref[:, :width])
        second_grad = second_scr[:, :width]

        def column_sum(value):
            return jnp.sum(value.astype(WIDE), axis=0, keepdims=True)

        mixed_grad = early_block[:, WIDTH : WIDTH + width].astype(WIDE)
        weights = low_scr[:, : kind.room].astype(WIDE).reshape(SEQS, 2 * HEADS, kind.room)
        totals = jnp.sum(weights[:, HEADS:], axis=-1, keepdims=True).reshape(SEQS * HEADS, 1)
        shared_scr[...] = jnp.broadcast_to(totals, shared_scr.shape)
        value_bias = []
        for lo, hi, first_head, n in spans(kind):
            owner = lax.broadcasted_iota(jnp.int32, (SEQS, hi - lo), 1) // HEAD
            scaled = jnp.zeros((SEQS, hi - lo), WIDE)
            for h in range(n):
                total = shared_scr[pl.ds(first_head + h, SEQS, stride=HEADS), 0:1]
                scaled = jnp.where(owner == h, mixed_grad[:, lo:hi] * total, scaled)
            value_bias.append(column_sum(scaled))
        hidden = bias_ref[0:1, : kind.part]
        parts = [
            gains[0:1, :width],
            gains[1:2, :width],
            column_sum(late_block[:, :width]),
            side_by_side(value_bias),
            column_sum(early_block[:, 2 * WIDTH : 2 * WIDTH + width]),
            column_sum(second_grad * hat),
            column_sum(second_grad),
            final_vec_ref[2:3, :width],
            final_vec_ref[0:1, :width],
            final_vec_ref[1:2, :width],
            jnp.concatenate([hidden, jnp.zeros((1, width - kind.part), WIDE)], axis=1),
            jnp.zeros((5, width), WIDE),
        ]
        lines_block[:, :width] = jnp.concatenate(parts, axis=0)

    each_tower(lines)
    line_copy = remote(
        lines_block, lines_all.at[at], lines_send.at[0], lines_recv.at[at], (tower, jnp.int32(0))
    )
    line_own = pltpu.make_async_copy(lines_block, lines_all.at[at], lines_recv.at[at])
    pl.when(at > 0)(line_copy.start)
    pl.when(at == 0)(line_own.start)

    early.finish()
    lefts.finish()

    def from_early(kind):
        plan, collect = plans[kind.index], collects[kind.index]
        width, block = kind.width, kind.block

        def gathered(k):
            lane = lax.broadcasted_iota(jnp.int32, (block, LANES), 1) // SEQS
            halves = []
            for side in range(2):
                total = jnp.zeros((block, LANES), WIDE)
                for j in range(8):
                    part = left_all[side * 8 + j, :block, LANES:].astype(WIDE)
                    shift = (j * SEQS - (k - 8) * SEQS) % LANES
                    turned_part = pltpu.roll(part, shift, 1) if shift else part
                    total = jnp.where(lane == j, turned_part, total)
                halves.append(total)
            return jnp.concatenate(halves, axis=1).astype(LOW)

        def right(start, wide):
            return early_all[:, :, start : start + wide].reshape(256, wide)

        output = dot_nn(gathered(13), right(2 * WIDTH, width))
        drop(
            kind, plan, 1, lambda c: output[:, c * LANES : (c + 1) * LANES], slots_of(kind), flat
        )
        collect.piece(1, False)
        embed = dot_nn(gathered(14), right(3 * WIDTH, EMB))
        drop(kind, plan, 4, lambda c: embed[:, c * LANES : (c + 1) * LANES], slots_of(kind), flat)
        collect.piece(4, False)
        left_scr[:block, :256] = gathered(12).astype(WIDE)

    each_tower(from_early)
    late.finish()
    turns.finish()

    def from_late(kind):
        plan, collect = plans[kind.index], collects[kind.index]
        width, block = kind.width, kind.block
        ask = dot_nn(left_scr[:block, :256].astype(LOW), late_all[:, :, :width].reshape(256, width))

        def outer(side_ref, start, span):
            lo, hi, first_head, n = span
            lane = first_head * SEQS
            total = jnp.zeros((block, hi - lo), WIDE)
            for j in range(8):
                left, rows = [], []
                for source in (2 * j, 2 * j + 1):
                    left.append(side_ref[source, :block, lane : lane + LANES])
                    rows.append(
                        head_rows(early_all[source, :, start : start + width], span)
                    )
                    if n < 8:
                        rows.append(jnp.zeros(((8 - n) * SEQS, hi - lo), LOW))
                total += dot_nn(
                    jnp.concatenate(left, axis=1), jnp.concatenate(rows, axis=0)
                )
            return total

        keys = side_by_side([outer(turn_all, 0, span) for span in spans(kind)]) * 0.125
        worth = side_by_side([outer(left_all, WIDTH, span) for span in spans(kind)])
        per = width // LANES

        def inputs(c):
            value = (ask, keys, worth)[c // per]
            return value[:, c % per * LANES : (c % per + 1) * LANES]

        drop(kind, plan, 0, inputs, slots_of(kind), flat)
        collect.piece(0, False)

    each_tower(from_late)

    @pl.when(at == 0)
    def _():
        for k in range(1, 16):
            remote(
                lines_block, lines_all.at[k], lines_send.at[0], lines_recv.at[k], sibling
            ).wait_recv()
        line_own.wait()

        def vectors(kind):
            width, part = kind.width, kind.part
            whole = [jnp.sum(lines_all[:, :10, :width], axis=0)]
            for row in range(4):
                pair_of = []
                for chip in (2 * row, 2 * row + 1):
                    pair_of.append(
                        lines_all[2 * chip, 10:11, :part] + lines_all[2 * chip + 1, 10:11, :part]
                    )
                whole.append(jnp.concatenate(pair_of, axis=1))
            whole.append(jnp.zeros((2, width), WIDE))
            result = jnp.concatenate(whole, axis=0)
            drop(
                kind,
                plans[kind.index],
                VECTORS,
                lambda c: result[:, c * LANES : (c + 1) * LANES],
                slots_of(kind),
                flat,
            )

        each_tower(vectors)

    each_tower(lambda kind: collects[kind.index].piece(VECTORS, False))
    home_pair.finish()

    @pl.when(tower == 1)
    def _():
        img_keep[...] = img_home[...].astype(WIDE)

    @pl.when(tower == 0)
    def _():
        txt_keep[...] = txt_home[...].astype(WIDE)

    for collect in collects:
        collect.finish()
    for copy in (*sent, fall, fallen, halves):
        copy.wait_send()
    pl.when(at > 0)(line_copy.wait_send)
    for group in (pair, *asks, *mixes, *embeds, rise, masks, embs, *deals):
        group.drain()
    for group in (risen_group, lefts, turns, early, late, home_pair):
        group.drain()

    def drain(kind):
        for p in range(VECTORS + 1):
            collects[kind.index].piece(p, True)

    each_tower(drain)


ROWS_LOW = ((SEQS, WIDTH), LOW)
ROWS_WIDE = ((SEQS, WIDTH), WIDE)
HEAD_ROWS = ((WIDTH // LANES, SEQS * HEADS, LANES), WIDE)
LANE_ROWS = ((SEQS * HEADS, LANES), WIDE)
GROUP = ((8, SEQS, WIDTH), LOW)
HIDDEN_BLOCKS = ((2, 8, 48, PART), LOW)
OUTER = ((16, 48, SEQS * HEADS), LOW)


def chunk_shapes(plan, n):
    return ((n, plan.rows, LANES), LOW)


def run_step(scalars, chunks, valid, tokens, plans):
    most = max(plan.local for plan in plans) + 17
    slots = max(plan.slots for plan in plans)
    edges = [((plan.rows, LANES), LOW) for plan in plans]
    rooms = [((kind.length, 8, kind.width), LOW) for kind in TOWERS]
    outs = [((kind.length, 8, kind.width), WIDE) for kind in TOWERS] + [
        chunk_shapes(plan, plan.local) for plan in plans
    ]
    scratch = [
        ROWS_LOW,
        ROWS_WIDE,
        ROWS_LOW,
        HEAD_ROWS,
        HEAD_ROWS,
        LANE_ROWS,
        ((SEQS, ROOM, WIDTH), LOW),
        ((WIDTH // LANES, ROOM * 8, LANES), WIDE),
        rooms[0],
        rooms[1],
        ((3, 16, 16, 2 * WIDTH), LOW),
        ((3, 16, 16, 2 * WIDTH), LOW),
        ((3, 16, 16, EMB), LOW),
        ROWS_WIDE,
        HIDDEN_BLOCKS,
        ((2, 192, WIDTH), LOW),
        ((2, 16, 16, LANES), LOW),
        chunk_shapes(plans[0], plans[0].slots),
        chunk_shapes(plans[1], plans[1].slots),
        edges[0],
        edges[1],
        edges[0],
        edges[1],
        ((plans[0].slots * plans[0].rows, LANES), WIDE),
        ((3, 16, 2 * WIDTH), LOW),
        ((3, 16, 2 * WIDTH), LOW),
        ((3, 16, EMB), LOW),
        ((8, 48, PART), LOW),
        ((192, WIDTH), LOW),
        ((16, LANES), LOW),
        ROWS_WIDE,
        ROWS_WIDE,
        LANE_ROWS,
        ((2 * SEQS * HEADS, LANES), LOW),
        ROWS_WIDE,
        ROWS_LOW,
        ((SEQS, EMB), LOW),
        ((8, WIDTH), WIDE),
        HIDDEN_BLOCKS,
        ((192, WIDTH), WIDE),
        ((192, WIDTH), LOW),
        ((8, PART), WIDE),
        GROUP,
        GROUP,
        GROUP,
        GROUP,
        ((128, PART), WIDE),
        ((SEQS, EMB), LOW),
        ((2, 16, SEQS, EMB), LOW),
        ROWS_WIDE,
        ((SEQS, EMB), WIDE),
        ROWS_LOW,
        GROUP,
        GROUP,
        ((256, EMB), WIDE),
        ((PART, WIDTH), WIDE),
        rooms[0],
        rooms[1],
        rooms[0],
        rooms[1],
        ((2, WIDTH // LANES, ROOM * 8, LANES), WIDE),
        ROWS_WIDE,
        ROWS_WIDE,
        HEAD_ROWS,
        HEAD_ROWS,
        LANE_ROWS,
        LANE_ROWS,
        ((SEQS * HEADS, WIDTH), WIDE),
        OUTER,
        OUTER,
        OUTER,
        OUTER,
        ((SEQS, 3 * WIDTH + EMB), LOW),
        ((16, SEQS, 3 * WIDTH + EMB), LOW),
        ROWS_LOW,
        ((16, SEQS, WIDTH), LOW),
        ROWS_WIDE,
        ((16, SEQS, WIDTH), WIDE),
        ((8, 48, PART), LOW),
        ((8, 48, PART), LOW),
        ((8, 48, PART), LOW),
        ((192, WIDTH), LOW),
        chunk_shapes(plans[0], plans[0].slots),
        chunk_shapes(plans[1], plans[1].slots),
        ((8, WIDTH), WIDE),
        ROWS_WIDE,
    ]
    semaphores = [
        (2, most,),
        (2, 6,),
        (2, 2,),
        (2,),
        (3, 16),
        (3, 15),
        (3, 16),
        (3, 15),
        (3, 20),
        (3, 15),
        (9,),
        (8,),
        (3,),
        (2,),
        (17,),
        (16,),
        (4, 8,),
        (4, 7,),
        (17,),
        (16,),
        (4,),
        (9,),
        (8,),
        (16,),
        (15,),
        (16,),
        (15,),
        (20,),
        (15,),
        (16,),
        (15,),
        (1,),
        (16,),
        (2,),
        (2, 2, slots,),
        (2,),
    ]
    smem = pl.BlockSpec(memory_space=pltpu.SMEM)
    vmem = pl.BlockSpec(memory_space=pltpu.VMEM)
    like = jax.ShapeDtypeStruct
    return pl.pallas_call(
        functools.partial(step_kernel, plans),
        out_shape=[like((1,), WIDE), like((3,), WIDE)] + [like(*out) for out in outs],
        in_specs=[smem, smem, ANY, ANY, vmem, vmem, vmem],
        out_specs=[smem, smem, vmem, vmem, vmem, vmem],
        scratch_shapes=[pltpu.VMEM(*each) for each in scratch]
        + [pltpu.SemaphoreType.DMA(shape) for shape in semaphores],
        compiler_params=comm_params(0),
    )(*scalars, *chunks, valid, *tokens)


def to_chunks(flat, plan, me):
    start = me * plan.share % plan.chunk
    padded = jnp.pad(flat, (plan.chunk, plan.local * plan.chunk - plan.share))
    piece = lax.dynamic_slice(padded, (plan.chunk - start,), (plan.local * plan.chunk,))
    return piece.astype(LOW).reshape(plan.local, plan.rows, LANES)


def from_chunks(chunks, plan, me):
    start = me * plan.share % plan.chunk
    return lax.dynamic_slice(chunks.reshape(-1), (start,), (plan.share,)).astype(WIDE)


def step(
    img_tokens,
    txt_tokens,
    txt_ends,
    valid,
    img_master,
    img_moment,
    img_average,
    txt_master,
    txt_moment,
    txt_average,
    scale_state,
):
    me = lax.axis_index(("tower", "dp"))
    plans = (
        Plan(0, img_master.shape[0], 96, (9, 3, 12, 12, 2)),
        Plan(1, txt_master.shape[0], 64, (6, 2, 8, 8, 2)),
    )
    loss, scale_new, img_grad, txt_grad, img_chunks, txt_chunks = run_step(
        (txt_ends, scale_state),
        (to_chunks(img_master, plans[0], me), to_chunks(txt_master, plans[1], me)),
        valid,
        (jnp.transpose(img_tokens, (1, 0, 2)), jnp.transpose(txt_tokens, (1, 0, 2))),
        plans,
    )
    img_new = advance(
        img_master, img_moment, img_average, from_chunks(img_chunks, plans[0], me), step_rate
    )
    txt_new = advance(
        txt_master, txt_moment, txt_average, from_chunks(txt_chunks, plans[1], me), step_rate
    )
    return (
        loss[0],
        jnp.transpose(img_grad, (1, 0, 2)),
        jnp.transpose(txt_grad, (1, 0, 2)),
        img_new[0],
        img_new[1],
        img_new[2],
        img_new[0].astype(LOW),
        txt_new[0],
        txt_new[1],
        txt_new[2],
        txt_new[0].astype(LOW),
        scale_new,
    )


def from_partner(value, axis, stride):
    mask = 2**stride
    pairs = [(source, source ^ mask) for source in range(lax.axis_size(axis))]
    return lax.ppermute(value, axis, pairs)


def round_value(v):
    return lax.optimization_barrier(v.astype(jnp.bfloat16)).astype(jnp.float32)


def make_low():

    def value_keep(v):
        return (round_value(v), None)

    def grad_pass(kept, grad):
        return (grad,)

    rounded = jax.custom_vjp(round_value)
    rounded.defvjp(value_keep, grad_pass)
    return rounded


def low(v):
    return make_low()(v)


def make_low_back():

    def identity(v):
        return v

    def value_pass(v):
        return (v, None)

    def grad_round(kept, grad):
        return (round_value(grad),)

    passed = jax.custom_vjp(identity)
    passed.defvjp(value_pass, grad_round)
    return passed


def low_back(v):
    return make_low_back()(v)


def both_ways(value):
    return low(low_back(value))


def product(left, right):
    return jnp.matmul(left, right)


def contract(form, left, right):
    return jnp.einsum(form, left, right)


def layer_norm(values, gain_row, shift_row):
    centred = values - jnp.mean(values, axis=-1, keepdims=True)
    spread = jnp.mean(centred * centred, axis=-1, keepdims=True)
    return centred * lax.rsqrt(spread + 1e-05) * gain_row + shift_row


def unpack(flat_weights, model_width, hidden_width, embed_width):
    piece_shapes = [
        (model_width, 3 * model_width),
        (model_width, model_width),
        (model_width, hidden_width),
        (hidden_width, model_width),
        (model_width, embed_width),
        (10, model_width),
        (hidden_width,),
    ]
    pieces = []
    offset = 0
    for piece_shape in piece_shapes:
        length = math.prod(piece_shape)
        pieces.append(flat_weights[offset : offset + length].reshape(piece_shape))
        offset = offset + length
    return pieces


def encode(tokens, flat_weights, positions, causal, model_width, hidden_width, embed_width):
    w_inputs, w_output, w_expand, w_reduce, w_embed, vectors, expand_bias = unpack(
        flat_weights, model_width, hidden_width, embed_width
    )
    groups = tokens.shape[0]
    length = tokens.shape[1]
    first = low(layer_norm(tokens, vectors[0], vectors[1]))
    bias_in = jnp.concatenate([vectors[2], jnp.zeros_like(vectors[2]), vectors[3]])
    joined = both_ways(product(first, w_inputs) + bias_in)
    joined = joined.reshape(groups, length, 3, model_width // HEAD, HEAD)
    scores = low_back(contract("gqhd,gkhd->ghqk", joined[:, :, 0], joined[:, :, 1]) * 0.125)
    if causal:
        row_index = lax.broadcasted_iota(jnp.int32, (length, length), 0)
        col_index = lax.broadcasted_iota(jnp.int32, (length, length), 1)
        scores = jnp.where(col_index <= row_index, scores, -1e30)
    row_top = jnp.max(scores, axis=-1, keepdims=True)
    raw_weights = jnp.exp(scores - row_top)
    attention = low(raw_weights / jnp.sum(raw_weights, axis=-1, keepdims=True))
    mixed_heads = both_ways(
        contract("ghqk,gkhd->gqhd", attention, joined[:, :, 2]).reshape(groups, length, model_width)
    )
    middle = tokens + low_back(product(mixed_heads, w_output) + vectors[4])
    second = low(layer_norm(middle, vectors[5], vectors[6]))
    raised = low_back(product(second, w_expand) + expand_bias)
    active = low(raised * jax.nn.sigmoid(1.702 * raised))
    final_rows = middle + low_back(product(active, w_reduce) + vectors[7])
    pooled = jnp.take_along_axis(final_rows, positions[:, None, None], axis=1)[:, 0]
    pooled = low(layer_norm(pooled, vectors[8], vectors[9]))
    projected = low_back(product(pooled, w_embed))
    return low(
        projected * lax.rsqrt(jnp.sum(projected * projected, axis=-1, keepdims=True) + 1e-06)
    )


def inner(left, right):
    return lax.dot_general(
        left, right, (((1,), (1,)), ((), ())), preferred_element_type=jnp.float32
    )


def across(left, right):
    return lax.dot_general(
        left, right, (((0,), (0,)), ((), ())), preferred_element_type=jnp.float32
    )


def softmax_total(logits, allowed):
    masked = jnp.where(allowed, logits, -1e30)
    row_top = jnp.max(masked, axis=1, keepdims=True)
    return jnp.log(jnp.sum(jnp.exp(masked - row_top), axis=1)) + row_top[:, 0]


def advance(master, moment, average, grads, rate):
    moment_new = momentum_rate * moment + grads
    master_new = master - rate * (grads + momentum_rate * moment_new)
    average_new = average_rate * average + (1.0 - average_rate) * master_new
    return (master_new, moment_new, average_new)


def padded_to(flat, length):
    return jnp.pad(flat, (0, length - flat.shape[0]))


def body(
    img_tokens,
    txt_tokens,
    txt_ends,
    valid,
    img_master,
    img_moment,
    img_average,
    txt_master,
    txt_moment,
    txt_average,
    scale_state,
):
    batch_rows = img_tokens.shape[0]
    total_rows = batch_rows * lax.axis_size(("tower", "dp"))
    device_at = lax.axis_index(("tower", "dp"))
    tower_at = lax.axis_index("tower")
    is_image = tower_at == 0
    img_share = img_master.shape[0]
    txt_share = txt_master.shape[0]
    img_count = img_tokens.size
    txt_count = txt_tokens.size
    shard_room = max(img_share, txt_share)
    token_room = max(img_count, txt_count)
    tower_count = lax.axis_size("dp")
    dp_at = lax.axis_index("dp")
    img_low = padded_to(img_master.astype(jnp.bfloat16), shard_room)
    txt_low = padded_to(txt_master.astype(jnp.bfloat16), shard_room)
    token_out = jnp.where(
        is_image,
        padded_to(txt_tokens.reshape(-1), token_room),
        padded_to(img_tokens.reshape(-1), token_room),
    )
    weight_out = jnp.where(is_image, txt_low, img_low)
    weight_mine = jnp.where(is_image, img_low, txt_low)
    token_in, weight_in = from_partner((token_out, weight_out), "tower", 0)
    stacked = jnp.where(
        is_image, jnp.stack([weight_mine, weight_in]), jnp.stack([weight_in, weight_mine])
    )
    gathered = lax.all_gather(stacked, "dp", axis=1, tiled=True)
    pair_ends = jnp.concatenate(
        [
            lax.dynamic_slice_in_dim(txt_ends, dp_at * batch_rows, batch_rows),
            lax.dynamic_slice_in_dim(txt_ends, (tower_count + dp_at) * batch_rows, batch_rows),
        ]
    )
    pair_zero = jnp.zeros((2 * batch_rows,), jnp.int32)

    def image_weights(whole):
        return whole.reshape(2, tower_count, shard_room).reshape(-1).astype(jnp.float32)

    def text_weights(whole):
        return (
            whole.reshape(2, tower_count, shard_room)[:, :, :txt_share]
            .reshape(-1)
            .astype(jnp.float32)
        )

    def image_rows(arrived):
        return jnp.concatenate(
            [img_tokens, arrived[:img_count].reshape(img_tokens.shape)], axis=0
        ).astype(jnp.float32)

    def text_rows(arrived):
        return jnp.concatenate([arrived.reshape(txt_tokens.shape), txt_tokens], axis=0).astype(
            jnp.float32
        )

    def image_encode(rows, flat):
        return encode(rows, flat, pair_zero, False, D_IMG, FF_IMG, EMB)

    def text_encode(rows, flat):
        return encode(rows, flat, pair_ends, True, D_TXT, FF_TXT, EMB)

    def image_forward(operands):
        return image_encode(image_rows(operands[1]), image_weights(operands[0]))

    def text_forward(operands):
        return text_encode(text_rows(operands[1]), text_weights(operands[0]))

    pair_emb = lax.cond(is_image, image_forward, text_forward, (gathered, token_in)).astype(
        jnp.bfloat16
    )
    emb_in = from_partner(pair_emb, "tower", 0)
    img_pair = jnp.where(is_image, pair_emb, emb_in)
    txt_pair = jnp.where(is_image, emb_in, pair_emb)
    row_start = tower_at * batch_rows
    img_local = lax.dynamic_slice_in_dim(img_pair, row_start, batch_rows)
    txt_local = lax.dynamic_slice_in_dim(txt_pair, row_start, batch_rows)
    img_all, txt_all = (
        lax.all_gather(img_local, ("tower", "dp"), axis=0, tiled=True),
        lax.all_gather(txt_local, ("tower", "dp"), axis=0, tiled=True),
    )
    logit_scale = jnp.exp(scale_state[0])
    offset = device_at * batch_rows
    row_index = lax.broadcasted_iota(jnp.int32, (batch_rows, total_rows), 0) + offset
    col_index = lax.broadcasted_iota(jnp.int32, (batch_rows, total_rows), 1)
    diagonal = (row_index == col_index).astype(jnp.float32)
    allowed = valid > 0
    row_logits = logit_scale * inner(img_local, txt_all)
    col_logits = logit_scale * inner(txt_local, img_all)
    row_lse = softmax_total(row_logits, allowed)
    col_lse = softmax_total(col_logits, allowed)
    partial_loss = 0.5 * (
        jnp.sum(row_lse)
        - jnp.sum(row_logits * diagonal)
        + jnp.sum(col_lse)
        - jnp.sum(col_logits * diagonal)
    )
    row_terms = 0.5 * (jnp.where(allowed, jnp.exp(row_logits - row_lse[:, None]), 0.0) - diagonal)
    col_terms = 0.5 * (jnp.where(allowed, jnp.exp(col_logits - col_lse[:, None]), 0.0) - diagonal)
    partial_scale = jnp.sum(row_terms * row_logits) + jnp.sum(col_terms * col_logits)
    row_back = (logit_scale * row_terms).astype(jnp.bfloat16)
    col_back = (logit_scale * col_terms).astype(jnp.bfloat16)
    img_emb_grad = jnp.dot(row_back, txt_all, preferred_element_type=jnp.float32)
    txt_emb_grad = jnp.dot(col_back, img_all, preferred_element_type=jnp.float32)
    img_extra, txt_extra = (
        lax.psum_scatter(
            across(col_back, txt_local), ("tower", "dp"), scatter_dimension=0, tiled=True
        ),
        lax.psum_scatter(
            across(row_back, img_local), ("tower", "dp"), scatter_dimension=0, tiled=True
        ),
    )
    img_emb_grad = img_emb_grad + img_extra
    txt_emb_grad = txt_emb_grad + txt_extra
    sums = lax.psum((partial_loss, partial_scale), ("tower", "dp"))
    grad_out = jnp.where(is_image, txt_emb_grad, img_emb_grad)
    grad_in = from_partner(grad_out, "tower", 0)
    pair_cot = jnp.where(
        is_image,
        jnp.concatenate([img_emb_grad, grad_in], axis=0),
        jnp.concatenate([grad_in, txt_emb_grad], axis=0),
    )

    def image_backward(operands):
        recomputed, tower_pullback = jax.vjp(
            image_encode, image_rows(operands[1]), image_weights(operands[0])
        )
        rows_grad, flat_grad = tower_pullback(operands[2])
        own_part = padded_to(rows_grad[:batch_rows].reshape(-1), token_room)
        sent_part = padded_to(rows_grad[batch_rows:].reshape(-1), token_room)
        stacked_grad = flat_grad.reshape(2, tower_count, img_share)
        return (own_part, sent_part, stacked_grad)

    def text_backward(operands):
        recomputed, tower_pullback = jax.vjp(
            text_encode, text_rows(operands[1]), text_weights(operands[0])
        )
        rows_grad, flat_grad = tower_pullback(operands[2])
        own_part = padded_to(rows_grad[batch_rows:].reshape(-1), token_room)
        sent_part = padded_to(rows_grad[:batch_rows].reshape(-1), token_room)
        stacked_grad = jnp.pad(
            flat_grad.reshape(2, tower_count, txt_share),
            ((0, 0), (0, 0), (0, shard_room - txt_share)),
        )
        return (own_part, sent_part, stacked_grad)

    own_part, sent_part, stacked_grad = lax.cond(
        is_image, image_backward, text_backward, (gathered, token_in, pair_cot)
    )
    summed = lax.psum_scatter(stacked_grad, "dp", scatter_dimension=1, tiled=True)
    kept_part = jnp.where(is_image, summed[0, 0], summed[1, 0])
    sent_share = jnp.where(is_image, summed[1, 0], summed[0, 0])
    home_weights, home_tokens = (
        from_partner(sent_share.astype(jnp.bfloat16), "tower", 0).astype(sent_share.dtype),
        from_partner(sent_part.astype(jnp.bfloat16), "tower", 0).astype(sent_part.dtype),
    )
    img_owned = jnp.where(is_image, kept_part, home_weights)
    txt_owned = jnp.where(is_image, home_weights, kept_part)[:txt_share]
    img_grad = jnp.where(is_image, own_part, home_tokens)[:img_count].reshape(img_tokens.shape)
    txt_grad = jnp.where(is_image, home_tokens, own_part).reshape(txt_tokens.shape)
    img_new = advance(img_master, img_moment, img_average, img_owned, step_rate)
    txt_new = advance(txt_master, txt_moment, txt_average, txt_owned, step_rate)
    scale_parts = advance(scale_state[0], scale_state[1], scale_state[2], sums[1], scale_rate)
    scale_new = jnp.stack([scale_parts[0], scale_parts[1], scale_parts[2]])
    return (
        sums[0] / total_rows,
        img_grad,
        txt_grad,
        img_new[0],
        img_new[1],
        img_new[2],
        img_new[0].astype(jnp.bfloat16),
        txt_new[0],
        txt_new[1],
        txt_new[2],
        txt_new[0].astype(jnp.bfloat16),
        scale_new,
    )


def solution(mesh):
    in_specs = (
        P(("tower", "dp"), None, None),
        P(("tower", "dp"), None, None),
        P(),
        P(("tower", "dp"), None),
        P(("tower", "dp")),
        P(("tower", "dp")),
        P(("tower", "dp")),
        P(("tower", "dp")),
        P(("tower", "dp")),
        P(("tower", "dp")),
        P(),
    )
    out_specs = (
        P(),
        P(("tower", "dp"), None, None),
        P(("tower", "dp"), None, None),
        P(("tower", "dp")),
        P(("tower", "dp")),
        P(("tower", "dp")),
        P(("tower", "dp")),
        P(("tower", "dp")),
        P(("tower", "dp")),
        P(("tower", "dp")),
        P(("tower", "dp")),
        P(),
    )
    run = step if (mesh.shape["tower"], mesh.shape["dp"]) == (2, 16) else body
    return jax.shard_map(run, mesh=mesh, in_specs=in_specs, out_specs=out_specs, check_vma=False)
```

```python
import functools
import math

import jax
import jax.numpy as jnp
from jax import lax
from jax.experimental import pallas as pl
from jax.experimental.pallas import tpu as pltpu
from jax.sharding import PartitionSpec as P

D_IMG = 768
FF_IMG = 3072
D_TXT = 512
FF_TXT = 2048
EMB = 512
HEAD = 64


momentum_rate = 0.5
average_rate = 0.5
step_rate = 0.08
scale_rate = 0.0001


MESH = pl.DeviceIdType.MESH
ANY = pl.BlockSpec(memory_space=pl.ANY)
GRANT = 58 * 1024 * 1024
LANES = 128
LOW = jnp.bfloat16
WIDE = jnp.float32


def here():
    return lax.axis_index("tower"), lax.axis_index("dp")


def greet(devices):
    barrier = pltpu.get_barrier_semaphore()
    for device in devices:
        pl.semaphore_signal(barrier, inc=1, device_id=device, device_id_type=MESH)
    pl.semaphore_wait(barrier, len(devices))


def remote(src, dst, send_sem, recv_sem, device):
    return pltpu.make_async_remote_copy(
        src_ref=src,
        dst_ref=dst,
        send_sem=send_sem,
        recv_sem=recv_sem,
        device_id=device,
        device_id_type=MESH,
    )


def comm_params(number):
    return pltpu.CompilerParams(
        collective_id=number, has_side_effects=True, vmem_limit_bytes=GRANT
    )


def same_core(tower, at):
    chip, core = at // 2, at % 2
    return [(tower, (chip + k) % 8 * 2 + core) for k in range(1, 8)]


def both_towers(tower, at):
    place, core = tower * 8 + at // 2, at % 2
    others = [(place + k) % 16 for k in range(1, 16)]
    return [(other // 8, other % 8 * 2 + core) for other in others]


def everyone(tower, at):
    me = tower * 16 + at
    others = [(me + k) % 32 for k in range(1, 32)]
    return [(other // 16, other % 16) for other in others]


def group_exchange(scattered, x_ref, o_ref, send_sem, recv_sem):
    tower, at = here()
    chip = at // 2

    def source(k):
        return x_ref.at[k] if scattered else x_ref

    own = pltpu.make_async_copy(source(chip), o_ref.at[chip], send_sem.at[7])
    sent = []
    for k, device in enumerate(same_core(tower, at)):
        copy = remote(
            source((chip + 1 + k) % 8), o_ref.at[chip], send_sem.at[k], recv_sem.at[k], device
        )
        copy.start()
        sent.append(copy)
    own.start()
    own.wait()
    for k in range(7):
        remote(
            source(chip),
            o_ref.at[(chip + 7 - k) % 8],
            send_sem.at[k],
            recv_sem.at[k],
            (tower, at),
        ).wait_recv()
    return sent


class Spread:
    def __init__(self, src, dst, send, recv):
        self.src, self.dst, self.send, self.recv = src, dst, send, recv
        tower, at = here()
        self.core = at % 2
        self.sibling = (tower, at + 1 - 2 * self.core)
        self.devices = self.peers(tower, at)
        self.n = len(self.devices) + 1
        self.place = self.spot(tower, at)
        self.sent = []

    def peers(self, tower, at):
        return both_towers(tower, at)

    def spot(self, tower, at):
        return tower * 8 + at // 2

    def block(self, place):
        return self.src

    def side(self, core):
        return self.dst.at[core]

    def launch(self, src, dst, k, device):
        copy = remote(src, dst, self.send.at[k], self.recv.at[k], device)
        copy.start()
        self.sent.append(copy)

    def start(self):
        for k, device in enumerate(self.devices):
            to = (self.place + 1 + k) % self.n
            self.launch(self.block(to), self.side(self.core).at[self.place], k, device)
        self.own = pltpu.make_async_copy(
            self.block(self.place), self.side(self.core).at[self.place], self.send.at[self.n]
        )
        self.own.start()

    def arrived(self):
        for k in range(self.n - 1):
            source = (self.place + self.n - 1 - k) % self.n
            remote(
                self.block(0),
                self.side(self.core).at[source],
                self.send.at[k],
                self.recv.at[k],
                self.sibling,
            ).wait_recv()
        self.own.wait()

    def relay(self):
        self.arrived()
        side = self.side(self.core)
        self.launch(side, side, self.n - 1, self.sibling)

    def finish(self):
        side = self.side(1 - self.core)
        remote(
            side, side, self.send.at[self.n - 1], self.recv.at[self.n - 1], self.sibling
        ).wait_recv()

    def drain(self):
        for copy in self.sent:
            copy.wait_send()


class Group(Spread):
    def __init__(self, src, dst, send, recv, both=True):
        self.both = both
        super().__init__(src, dst, send, recv)

    def peers(self, tower, at):
        return same_core(tower, at)

    def spot(self, tower, at):
        return at // 2

    def block(self, place):
        return self.src.at[place]

    def side(self, core):
        return self.dst.at[core] if self.both else self.dst

    def finish(self):
        if self.both:
            super().finish()
        else:
            self.arrived()


class Ring:
    def __init__(self, src, dst, send, recv, only=None):
        self.src, self.dst, self.send, self.recv = src, dst, send, recv
        self.only = only
        self.tower, self.at = here()
        self.deep, self.row, self.core = self.at // 4, self.at // 2 % 2, self.at % 2
        self.sibling = (self.tower, self.at + 1 - 2 * self.core)
        self.beside = (self.tower, self.spot(0, 1 - self.row))
        self.sent = []

    def spot(self, k, row):
        return (self.deep + k) % 4 * 4 + row * 2 + self.core

    def act(self, action):
        if self.only is None:
            action()
        else:
            pl.when(self.tower == self.only)(action)

    def launch(self, src, slot, index, device):
        copy = remote(src, self.dst.at[slot], self.send.at[index], self.recv.at[index], device)
        self.act(copy.start)
        self.sent.append(copy)

    def arrived(self, slot, index):
        copy = remote(
            self.src, self.dst.at[slot], self.send.at[index], self.recv.at[index], self.sibling
        )
        self.act(copy.wait_recv)

    def start(self):
        for k in (1, 3, 2):
            self.launch(self.src, self.at, k - 1, (self.tower, self.spot(k, self.row)))
        self.launch(self.src, self.at, 3, self.beside)
        self.launch(self.src, self.at, 7, self.sibling)
        self.own = pltpu.make_async_copy(self.src, self.dst.at[self.at], self.send.at[15])
        self.act(self.own.start)

    def relay_deep(self):
        for k in (1, 3, 2):
            slot = self.spot(4 - k, self.row)
            self.arrived(slot, k - 1)
            self.launch(self.dst.at[slot], slot, 3 + k, self.beside)
            self.launch(self.dst.at[slot], slot, 7 + k, self.sibling)

    def relay_row(self):
        for k in (0, 1, 3, 2):
            slot = self.spot(4 - k, 1 - self.row)
            self.arrived(slot, 3 + k)
            self.launch(self.dst.at[slot], slot, 11 + k, self.sibling)

    def finish(self):
        for index in range(8):
            k, row = index % 4, self.row if index < 4 else 1 - self.row
            slot = (self.deep + 4 - k) % 4 * 4 + row * 2 + 1 - self.core
            self.arrived(slot, 7 + index)
        self.act(self.own.wait)

    def drain(self):
        for copy in self.sent:
            self.act(copy.wait_send)


class Chain:
    def __init__(self, src, dst, send, recv, only=None):
        self.src, self.dst, self.send, self.recv = src, dst, send, recv
        self.only = only
        self.tower, self.at = here()
        self.deep, self.row, self.core = self.at // 4, self.at // 2 % 2, self.at % 2
        self.mate = self.deep + 1 - 2 * (self.deep % 2)
        self.half = self.deep // 2
        self.inner = jnp.logical_or(self.deep == 1, self.deep == 2)
        self.sibling = (self.tower, self.at + 1 - 2 * self.core)
        self.beside = (self.tower, self.spot(self.deep, 1 - self.row))
        self.sent = []

    def spot(self, deep, row):
        return deep * 4 + row * 2 + self.core

    def sources(self):
        return self.deep, self.mate, 2 - 2 * self.half, 3 - 2 * self.half

    def act(self, action, when=None):
        if self.only is not None:
            right = self.tower == self.only
            when = right if when is None else jnp.logical_and(when, right)
        if when is None:
            action()
        else:
            pl.when(when)(action)

    def launch(self, src, slot, sent, landed, device, when=None):
        copy = remote(src, self.dst.at[slot], self.send.at[sent], self.recv.at[landed], device)
        self.act(copy.start, when)
        self.sent.append((copy, when))

    def arrived(self, slot, index):
        copy = remote(
            self.src, self.dst.at[slot], self.send.at[0], self.recv.at[index], self.sibling
        )
        self.act(copy.wait_recv)

    def start(self):
        mate = (self.tower, self.spot(self.mate, self.row))
        far = (self.tower, self.spot(2 - self.half, self.row))
        self.launch(self.src, self.at, 1, 1 + self.deep % 2, far)
        self.launch(self.src, self.at, 0, 0, mate)
        self.launch(self.src, self.at, 2, 3, self.beside)
        self.launch(self.src, self.at, 3, 7, self.sibling)
        self.own = pltpu.make_async_copy(self.src, self.dst.at[self.at], self.send.at[16])
        self.act(self.own.start)

    def relay_deep(self):
        mate = (self.tower, self.spot(self.mate, self.row))
        for k in (1, 2, 3):
            slot = self.spot(self.sources()[k], self.row)
            self.arrived(slot, k - 1)
            block = self.dst.at[slot]
            if k > 1:
                self.launch(block, slot, 4 + k, k - 1, mate, self.inner)
            self.launch(block, slot, 7 + k, 3 + k, self.beside)
            self.launch(block, slot, 16 + k, 7 + k, self.sibling)

    def relay_row(self):
        for k, deep in enumerate(self.sources()):
            slot = self.spot(deep, 1 - self.row)
            self.arrived(slot, 3 + k)
            self.launch(self.dst.at[slot], slot, 11 + k, 11 + k, self.sibling)

    def finish(self):
        for k, deep in enumerate(self.sources()):
            for row, base in ((self.row, 7), (1 - self.row, 11)):
                self.arrived(deep * 4 + row * 2 + 1 - self.core, base + k)
        self.act(self.own.wait)

    def drain(self):
        for copy, when in self.sent:
            self.act(copy.wait_send, when)


def rings(src, dst, send, recv, way=Ring):
    return [
        way(src.at[part], dst.at[part], send.at[part], recv.at[part], 0 if part == 2 else None)
        for part in range(3)
    ]


class Blocks:
    def __init__(self, src, dst, send, recv, shared=1):
        self.src, self.dst, self.send, self.recv = src, dst, send, recv
        self.tower, self.at = here()
        self.shared = shared
        self.sent = []

    def start(self):
        for k in range(1, 16):
            to = (self.at + k) % 16
            copy = remote(
                self.src.at[to // self.shared],
                self.dst.at[self.at],
                self.send.at[k - 1],
                self.recv.at[k - 1],
                (self.tower, to),
            )
            copy.start()
            self.sent.append(copy)
        self.own = pltpu.make_async_copy(
            self.src.at[self.at // self.shared], self.dst.at[self.at], self.send.at[15]
        )
        self.own.start()

    def finish(self):
        for k in range(1, 16):
            remote(
                self.src.at[0],
                self.dst.at[(self.at + 16 - k) % 16],
                self.send.at[k - 1],
                self.recv.at[k - 1],
                (self.tower, self.at),
            ).wait_recv()
        self.own.wait()

    def drain(self):
        for copy in self.sent:
            copy.wait_send()


class Pair:
    def __init__(self, from_zero, zero_dst, from_one, one_dst, sems):
        tower, at = here()
        partner = (1 - tower, at)
        self.tower = tower
        self.up = remote(from_zero, zero_dst, sems.at[0], sems.at[1], partner)
        self.down = remote(from_one, one_dst, sems.at[0], sems.at[1], partner)

    def by_tower(self, zero, one):
        pl.when(self.tower == 0)(zero)
        pl.when(self.tower == 1)(one)

    def start(self):
        self.by_tower(self.up.start, self.down.start)

    def finish(self):
        self.by_tower(self.down.wait_recv, self.up.wait_recv)

    def drain(self):
        self.by_tower(self.up.wait_send, self.down.wait_send)


VECTORS = 5
EXPAND = 2
TURN = 8


class Plan:
    def __init__(self, tower, share, rows, per_device):
        self.tower = tower
        self.share = share
        self.rows = rows
        self.chunk = rows * LANES
        self.per_device = per_device
        self.first_slot = [sum(per_device[:p]) for p in range(6)]
        self.first_chunk = [16 * slot for slot in self.first_slot]
        self.slots = sum(per_device) + 1
        self.total = 16 * sum(per_device) + 1
        spans = [self.span(device) for device in range(32)]
        self.counts = sorted({last - first + 1 for first, last in spans})
        self.local = self.counts[-1]

    def span(self, device):
        first = device * self.share // self.chunk
        last = ((device + 1) * self.share - 1) // self.chunk
        return first, min(last, self.total - 1)

    def bounds(self, device):
        first = device * self.share // self.chunk
        last = ((device + 1) * self.share - 1) // self.chunk
        return first, jnp.minimum(last, self.total - 1)

    def pieces(self, p):
        return self.per_device[p] if p < VECTORS else 1

    def target(self, g):
        piece, base, slot, n = (jnp.int32(0), jnp.int32(0), jnp.int32(0), jnp.int32(1))
        for p in range(VECTORS):
            inside = g >= self.first_chunk[p]
            piece = jnp.where(inside, p, piece)
            base = jnp.where(inside, self.first_chunk[p], base)
            slot = jnp.where(inside, self.first_slot[p], slot)
            n = jnp.where(inside, self.per_device[p], n)
        block = (g - base) // n
        at = jnp.where(piece == EXPAND, (block + TURN) % 16, block)
        return piece, at, slot + (g - base) - block * n


def before(me):
    device = (me + 31) % 32
    return device // 16, device % 16


class Deal:
    def __init__(self, plan, s, src, dst, extra, last, sems, only=None, me=None):
        self.plan, self.s, self.src, self.dst = plan, s, src, dst
        self.extra, self.last = extra, last
        self.chunk_send, self.recv, self.edge, self.fetch = sems
        self.tower, self.at = here()
        self.only = only
        self.me = self.tower * 16 + self.at if me is None else me
        self.first, self.last_chunk = plan.bounds(self.me)

    def runs(self, condition):
        return condition if self.only is None else jnp.logical_and(condition, self.tower == self.only)

    def move(self, src, i, piece, at_to, slot, wait):
        far = jnp.logical_or(self.tower != self.plan.tower, at_to != self.at)
        recv = self.recv.at[self.plan.tower, piece]
        copy = remote(
            src,
            self.dst.at[slot],
            self.chunk_send.at[self.s, i],
            recv,
            (jnp.int32(self.plan.tower), at_to),
        )
        pl.when(far)(copy.wait_send if wait else copy.start)
        if not wait:
            pl.when(jnp.logical_not(far))(
                pltpu.make_async_copy(src, self.dst.at[slot], recv).start
            )

    def whole(self, early, wait):
        def step(i, carry):
            g = self.first + i
            piece, at_to, slot = self.plan.target(g)
            inside = jnp.logical_and(
                jnp.logical_or(i > 0, self.me == 0),
                jnp.logical_or(
                    g < self.last_chunk, jnp.logical_and(self.me == 31, g < self.plan.total - 1)
                ),
            )
            inside = jnp.logical_and(inside, g <= self.last_chunk)
            inside = jnp.logical_and(inside, g < self.plan.total - 1)
            if early is not None:
                hidden = jnp.logical_and(piece >= 2, piece <= 3)
                inside = jnp.logical_and(inside, jnp.logical_not(hidden) if early else hidden)

            @pl.when(self.runs(inside))
            def _():
                self.move(self.src.at[i], i, piece, at_to, slot, wait)

            return carry

        lax.fori_loop(0, self.plan.local, step, 0)

    def vectors(self, wait):
        @pl.when(self.runs(self.me == 31))
        def _():
            src = self.src.at[self.last_chunk - self.first]

            def each(k, carry):
                self.move(src, self.plan.local + k, VECTORS, k, self.plan.slots - 1, wait)
                return carry

            lax.fori_loop(0, 16, each, 0)

    def fetch_last(self):
        return pltpu.make_async_copy(
            self.src.at[self.last_chunk - self.first], self.last, self.fetch.at[self.s]
        )

    def join(self):
        @pl.when(self.runs(self.me < 31))
        def _():
            self.fetch_last().wait()
            edge = self.edge
            remote(
                self.last,
                self.extra,
                edge.at[self.s, 0],
                edge.at[self.s, 1],
                (self.tower, self.at),
            ).wait_recv()
            self.last[...] = self.last[...] + self.extra[...]
            piece, at_to, slot = self.plan.target(self.last_chunk)
            self.move(self.last, self.plan.local + 16, piece, at_to, slot, False)

    def start_fetch(self):
        pl.when(self.runs(self.me < 31))(self.fetch_last().start)

    def arrived(self, p):
        part = self.dst.at[pl.ds(self.plan.first_slot[p], self.plan.pieces(p))]
        pltpu.make_async_copy(part, part, self.recv.at[self.plan.tower, p]).wait()

    def drain(self):
        self.whole(None, True)
        self.vectors(True)

        @pl.when(self.runs(self.me < 31))
        def _():
            piece, at_to, slot = self.plan.target(self.last_chunk)
            self.move(self.last, self.plan.local + 16, piece, at_to, slot, True)


class Collect:
    def __init__(self, plan, s, src, dst, send, recv):
        self.plan, self.s, self.src, self.dst = plan, s, src, dst
        self.send, self.recv = send, recv
        self.tower, self.at = here()
        self.me = self.tower * 16 + self.at

    def one(self, owner, slot, g, which, wait):
        first, _ = self.plan.bounds(owner)
        far = owner != self.me
        recv = self.recv.at[self.s]
        copy = remote(
            self.src.at[slot],
            self.dst.at[g - first],
            self.send.at[which, slot],
            recv,
            (owner // 16, owner % 16),
        )
        pl.when(far)(copy.wait_send if wait else copy.start)
        if not wait:
            pl.when(jnp.logical_not(far))(
                pltpu.make_async_copy(self.src.at[slot], self.dst.at[g - first], recv).start
            )

    def piece(self, p, wait):
        n = self.plan.pieces(p)

        def step(i, carry):
            slot = self.plan.first_slot[p] + i
            block = (self.at + 16 - TURN) % 16 if p == EXPAND else self.at
            g = self.plan.first_chunk[p] + block * n + i if p < VECTORS else self.plan.total - 1
            low = g * self.plan.chunk // self.plan.share
            high = jnp.minimum(((g + 1) * self.plan.chunk - 1) // self.plan.share, 31)
            self.one(low, slot, g, 0, wait)
            pl.when(high != low)(lambda: self.one(high, slot, g, 1, wait))
            return carry

        if p == VECTORS:


            @pl.when(self.at == 0)
            def _():
                step(0, 0)

        else:
            lax.fori_loop(0, n, step, 0)

    def finish(self):
        first, last = self.plan.bounds(self.me)
        held = last - first + 1
        for n in self.plan.counts:

            @pl.when(held == n)
            def _():
                part = self.dst.at[pl.ds(0, n)]
                pltpu.make_async_copy(part, part, self.recv.at[self.s]).wait()


SEQS = 16
HEADS = 16


class Tower:
    def __init__(self, index, width, hidden, length, room, run, causal):
        self.index = index
        self.width = width
        self.hidden = hidden
        self.length = length
        self.room = room
        self.run = run
        self.causal = causal
        self.heads = width // HEAD
        self.block = width // 16
        self.part = hidden // 8
        self.reduce_rows = hidden // 16


TOWERS = (
    Tower(0, D_IMG, FF_IMG, 50, 64, 10, False),
    Tower(1, D_TXT, FF_TXT, 77, 80, 11, True),
)
ROOM = 80
WIDTH = D_IMG
PART = FF_IMG // 8


def each_tower(run):
    tower = lax.axis_index("tower")
    for kind in TOWERS:
        pl.when(tower == kind.index)(functools.partial(run, kind))


def dot_nn(a, b):
    return lax.dot_general(a, b, (((1,), (0,)), ((), ())), preferred_element_type=WIDE)


def dot_nt(a, b):
    return lax.dot_general(a, b, (((1,), (1,)), ((), ())), preferred_element_type=WIDE)


def dot_tn(a, b):
    return lax.dot_general(a, b, (((0,), (0,)), ((), ())), preferred_element_type=WIDE)


def standardise(rows):
    centred = rows - jnp.mean(rows, axis=-1, keepdims=True)
    spread = jnp.mean(centred * centred, axis=-1, keepdims=True)
    rate = lax.rsqrt(spread + 1e-05)
    return centred * rate, rate


def norm_back(grad, gain, hat, rate):
    scaled = grad * gain
    return rate * (
        scaled
        - jnp.mean(scaled, axis=-1, keepdims=True)
        - hat * jnp.mean(scaled * hat, axis=-1, keepdims=True)
    )


def spans(kind):
    return [
        (lo, min(lo + 512, kind.width), lo // HEAD, (min(lo + 512, kind.width) - lo) // HEAD)
        for lo in range(0, kind.width, 512)
    ]


def head_rows(rows, span):
    lo, hi, _, n = span
    part = rows[:, lo:hi]
    owner = lax.broadcasted_iota(jnp.int32, part.shape, 1) // HEAD
    nothing = jnp.zeros_like(part)
    return jnp.concatenate([jnp.where(owner == h, part, nothing) for h in range(n)], axis=0)


def from_head_rows(rows, span):
    _, _, _, n = span
    owner = lax.broadcasted_iota(jnp.int32, (SEQS, rows.shape[1]), 1) // HEAD
    total = jnp.zeros((SEQS, rows.shape[1]), rows.dtype)
    for h in range(n):
        total = jnp.where(owner == h, rows[h * SEQS : (h + 1) * SEQS], total)
    return total


def side_by_side(parts):
    return parts[0] if len(parts) == 1 else jnp.concatenate(parts, axis=1)


def get_rows(ref, place, width):
    return side_by_side([ref[c, place, :] for c in range(width // LANES)])


def put_rows(ref, place, value):
    for c in range(value.shape[1] // LANES):
        ref[c, place, :] = value[:, c * LANES : (c + 1) * LANES]


def matrix(ref, kind, start, width):
    return jnp.concatenate(
        [
            ref[part, at, :, start : start + width]
            for at in range(16)
            for part in range(kind.block // 16)
        ],
        axis=0,
    )


def vector(vec_ref, kind, row):
    return vec_ref[row : row + 1, : kind.width]


def pieces_of(kind):
    return (
        (kind.block, 3 * kind.width),
        (kind.block, kind.width),
        (kind.block, kind.hidden),
        (kind.reduce_rows, kind.width),
        (kind.block, EMB),
        (16, kind.width),
    )


def lane_blocks(kind, plan, p):
    height, width = pieces_of(kind)[p]
    pitch = width // LANES
    base = plan.first_slot[p] * plan.rows if p < VECTORS else (plan.slots - 1) * plan.rows
    return [(c, pl.ds(base + c, height, stride=pitch)) for c in range(pitch)]


def lift(kind, plan, p, slots, flat):
    n = plan.pieces(p)
    slot = plan.first_slot[p]
    rows = slots[slot : slot + n].reshape(n * plan.rows, LANES)
    flat[slot * plan.rows : (slot + n) * plan.rows, :] = rows.astype(WIDE)
    return [(c, flat[place, :]) for c, place in lane_blocks(kind, plan, p)]


def drop(kind, plan, p, value, slots, flat):
    for c, place in lane_blocks(kind, plan, p):
        flat[place, :] = value(c)
    n = plan.pieces(p)
    slot = plan.first_slot[p]
    rows = flat[slot * plan.rows : (slot + n) * plan.rows, :]
    slots[slot : slot + n] = rows.reshape(n, plan.rows, LANES).astype(LOW)


def expand_matrix(ref, kind):
    return jnp.concatenate(
        [
            ref[at % 2, at // 2, : kind.block, : kind.part]
            for at in ((block + TURN) % 16 for block in range(16))
        ],
        axis=0,
    )


def reduce_matrix(ref, kind):
    return ref[:, : kind.reduce_rows, : kind.width].reshape(kind.part, kind.width)


def hidden_bias(vec_ref, kind):
    chip = lax.axis_index("dp") // 2
    whole = vec_ref[...]
    row = lax.broadcasted_iota(jnp.int32, (16, 1), 0)
    line = jnp.sum(jnp.where(row == 10 + chip // 2, whole, 0.0), axis=0, keepdims=True)
    return jnp.where(
        chip % 2 == 0, line[:, : kind.part], line[:, kind.part : 2 * kind.part]
    )


def hidden_kernel(second_ref, raise_ref, reduce_ref, vec_ref, part_ref, raised_ref):
    def run(kind):
        width = kind.width
        rows = second_ref[:, :, :width].reshape(8 * SEQS, width)
        raised = dot_nn(rows, expand_matrix(raise_ref, kind)) + hidden_bias(vec_ref, kind)
        raised_ref[:, : kind.part] = raised
        active = (raised * jax.nn.sigmoid(1.702 * raised)).astype(LOW)
        part = dot_nn(active, reduce_matrix(reduce_ref, kind))
        part_ref[:, :, :width] = part.reshape(8, SEQS, width).astype(LOW)

    each_tower(run)


def hidden_back_kernel(
    grad_ref,
    second_ref,
    raised_ref,
    raise_ref,
    reduce_ref,
    back_ref,
    raise_grad_ref,
    reduce_keep_ref,
    reduce_send_ref,
    bias_ref,
    whole,
):
    def run(kind):
        width, part = kind.width, kind.part
        grads = grad_ref[:, :, :width].reshape(8 * SEQS, width)
        rows = second_ref[:, :, :width].reshape(8 * SEQS, width)
        raised = raised_ref[:, :part]
        gate = jax.nn.sigmoid(1.702 * raised)
        active = (raised * gate).astype(LOW)
        slope = gate + 1.702 * raised * gate * (1.0 - gate)
        raised_grad = dot_nt(grads, reduce_matrix(reduce_ref, kind)) * slope
        low_grad = raised_grad.astype(LOW)
        bias_ref[0:1, :part] = jnp.sum(low_grad.astype(WIDE), axis=0, keepdims=True)
        back = dot_nt(low_grad, expand_matrix(raise_ref, kind))
        back_ref[:, :, :width] = back.reshape(8, SEQS, width).astype(LOW)
        raise_grad = dot_tn(rows, low_grad).reshape(16, kind.block, part).astype(LOW)
        for block in range(16):
            at = (block + TURN) % 16
            raise_grad_ref[at % 2, at // 2, : kind.block, :part] = raise_grad[block]
        whole[:part, :width] = dot_tn(active, grads)
        core = lax.axis_index("dp") % 2
        n = kind.reduce_rows
        keep = pl.multiple_of(core * n, 64)
        send = pl.multiple_of((1 - core) * n, 64)
        reduce_keep_ref[:n, :width] = whole[pl.ds(keep, n), :width]
        reduce_send_ref[:n, :width] = whole[pl.ds(send, n), :width].astype(LOW)

    each_tower(run)


def embed_kernel(part_ref, middle_ref, gat_ref, vec_ref, emb_ref, final_ref, pooled_ref, proj_ref):
    def run(kind):
        width = kind.width
        final = (
            middle_ref[:, :width]
            + jnp.sum(part_ref[:, :, :width].astype(WIDE), axis=0)
            + vector(vec_ref, kind, 7)
        )
        final_ref[:, :width] = final
        hat, _ = standardise(final)
        pooled = (hat * vector(vec_ref, kind, 8) + vector(vec_ref, kind, 9)).astype(LOW)
        pooled_ref[:, :width] = pooled
        proj = dot_nn(pooled, matrix(gat_ref, kind, 0, EMB))
        proj_ref[...] = proj
        size = jnp.sum(proj * proj, axis=-1, keepdims=True) + 1e-06
        emb_ref[...] = (proj * lax.rsqrt(size)).astype(LOW)

    each_tower(run)


def objective_kernel(
    scale_ref,
    all_ref,
    valid_ref,
    final_ref,
    proj_ref,
    gat_ref,
    vec_ref,
    low_ref,
    grad_ref,
    proj_grad_ref,
    final_vec_ref,
    loss_ref,
    scale_new_ref,
    own_scr,
):
    def ordered(which):
        blocks = []
        for half in range(2):
            for j in range(16):
                rows = all_ref[j % 2, which * 8 + j // 2].astype(WIDE)
                blocks.append(rows[half * 8 : half * 8 + 8])
        return jnp.concatenate(blocks, axis=0).astype(LOW)

    img, txt = ordered(0), ordered(1)
    total = img.shape[0]
    scale = jnp.exp(jnp.full((1, 1), scale_ref[0], WIDE))
    lines = []
    for d in range(32):
        rows = valid_ref[d % 2, d // 2].astype(WIDE)
        lines.append(jnp.concatenate([rows[:8], rows[8:]], axis=1))
    allowed = jnp.concatenate(lines, axis=0) > 0
    same = lax.broadcasted_iota(jnp.int32, (total, total), 0) == lax.broadcasted_iota(
        jnp.int32, (total, total), 1
    )
    same = same.astype(WIDE)

    def side(left, right):
        logits = scale * dot_nt(left, right)
        masked = jnp.where(allowed, logits, -1e30)
        top = jnp.max(masked, axis=1, keepdims=True)
        lse = jnp.log(jnp.sum(jnp.exp(masked - top), axis=1, keepdims=True)) + top
        terms = 0.5 * (jnp.where(allowed, jnp.exp(logits - lse), 0.0) - same)
        loss = 0.5 * (
            jnp.sum(lse, axis=0, keepdims=True)
            - jnp.sum(jnp.sum(logits * same, axis=1, keepdims=True), axis=0, keepdims=True)
        )
        rate = jnp.sum(jnp.sum(terms * logits, axis=1, keepdims=True), axis=0, keepdims=True)
        return (scale * terms).astype(LOW), loss, rate

    row_back, row_loss, row_rate = side(img, txt)
    col_back, col_loss, col_rate = side(txt, img)
    loss_ref[0] = jnp.sum(row_loss + col_loss) / total
    parts = advance(
        scale_ref[0], scale_ref[1], scale_ref[2], jnp.sum(row_rate + col_rate), scale_rate
    )
    for k in range(3):
        scale_new_ref[k] = parts[k]

    def run(kind):
        width = kind.width
        if kind.index == 0:
            emb_grad = dot_nn(row_back, txt) + dot_tn(col_back, txt)
        else:
            emb_grad = dot_nn(col_back, img) + dot_tn(row_back, img)
        own_scr[...] = emb_grad
        at = lax.axis_index("dp")
        mine = jnp.concatenate(
            [
                own_scr[pl.ds(pl.multiple_of(half * 128 + at * 8, 8), 8), :]
                for half in range(2)
            ],
            axis=0,
        )
        proj = proj_ref[...]
        size = jnp.sum(proj * proj, axis=-1, keepdims=True) + 1e-06
        along = jnp.sum(proj * mine, axis=-1, keepdims=True)
        proj_grad = ((mine - proj * along / size) * lax.rsqrt(size)).astype(LOW)
        proj_grad_ref[...] = proj_grad
        pooled_grad = dot_nt(proj_grad, matrix(gat_ref, kind, 0, EMB))
        hat, rate = standardise(final_ref[:, :width])
        final_vec_ref[0:1, :width] = jnp.sum(pooled_grad * hat, axis=0, keepdims=True)
        final_vec_ref[1:2, :width] = jnp.sum(pooled_grad, axis=0, keepdims=True)
        final_grad = norm_back(pooled_grad, vector(vec_ref, kind, 8), hat, rate)
        grad_ref[:, :width] = final_grad
        low = final_grad.astype(LOW)
        low_ref[:, :width] = low
        final_vec_ref[2:3, :width] = jnp.sum(low.astype(WIDE), axis=0, keepdims=True)

    each_tower(run)


def step_kernel(
    plans,
    ends_ref,
    scale_ref,
    img_src,
    txt_src,
    valid_ref,
    img_own,
    txt_own,
    loss_ref,
    scale_new_ref,
    img_keep,
    txt_keep,
    img_chunks,
    txt_chunks,
    second_ref,
    middle_ref,
    query_ref,
    keyed_ref,
    mixture_ref,
    weight_ref,
    first_ref,
    first_rows,
    img_in,
    txt_in,
    ask_ref,
    mix_ref,
    emb_ref,
    vec_ref,
    raise_ref,
    reduce_ref,
    pairs_ref,
    img_slots,
    txt_slots,
    img_extra,
    txt_extra,
    img_last,
    txt_last,
    txt_relay,
    txt_over,
    txt_ending,
    flat,
    ask_block,
    mix_block,
    emb_block,
    raise_block,
    reduce_block,
    mask_block,
    top_scr,
    at_scr,
    score_scr,
    low_scr,
    grad_ref,
    pooled_ref,
    proj_grad_ref,
    final_vec_ref,
    raise_grad_ref,
    reduce_keep_ref,
    reduce_send_ref,
    bias_ref,
    backs_ref,
    seconds,
    part,
    parts,
    raised,
    emb,
    all_embs,
    final,
    proj,
    low,
    lows,
    back,
    own_scr,
    whole,
    img_send,
    txt_send,
    img_home,
    txt_home,
    rows_grad,
    middle_scr,
    second_scr,
    valued_scr,
    turn_scr,
    shared_scr,
    slope_scr,
    left_scr,
    left_block,
    turn_block,
    left_all,
    turn_all,
    early_block,
    early_all,
    late_block,
    late_all,
    lines_block,
    lines_all,
    raise_half,
    risen_block,
    raise_all,
    reduce_in,
    img_home_slots,
    txt_home_slots,
    gains,
    top_grad_scr,
    deal_send,
    deal_recv,
    deal_edge,
    deal_fetch,
    relay_sems,
    ask_send,
    ask_recv,
    mix_send,
    mix_recv,
    emb_send,
    emb_recv,
    raise_send,
    raise_recv,
    reduce_sems,
    pair_sems,
    mask_send,
    mask_recv,
    group_send,
    group_recv,
    embs_send,
    embs_recv,
    home_sems,
    risen_send,
    risen_recv,
    left_send,
    left_recv,
    turn_send,
    turn_recv,
    early_send,
    early_recv,
    late_send,
    late_recv,
    lines_send,
    lines_recv,
    home_pair_sems,
    collect_send,
    collect_recv,
):
    tower, at = here()
    core = at % 2
    me = tower * 16 + at
    sibling = (tower, at + 1 - 2 * core)
    greet(everyone(tower, at))
    deal_sems = (deal_send, deal_recv, deal_edge, deal_fetch)
    deals = [
        Deal(plans[0], 0, img_src, img_slots, img_extra, img_last, deal_sems),
        Deal(plans[1], 1, txt_src, txt_slots, txt_extra, txt_last, deal_sems, 1, 16 + at),
        Deal(plans[1], 2, txt_relay, txt_slots, txt_over, txt_ending, deal_sems, 1, at),
    ]
    relay = remote(txt_src, txt_relay, relay_sems.at[0], relay_sems.at[1], (1 - tower, at))
    behind = (jnp.int32(1), (at + 15) % 16)
    head = remote(img_src.at[0], img_extra, deal_edge.at[0, 0], deal_edge.at[0, 1], before(me))
    kept = remote(txt_src.at[0], txt_extra, deal_edge.at[1, 0], deal_edge.at[1, 1], behind)
    over = remote(txt_src.at[0], txt_over, deal_edge.at[2, 0], deal_edge.at[2, 1], behind)
    heads = (
        (me > 0, head),
        (me > 16, kept),
        (jnp.logical_and(me > 0, me <= 16), over),
    )
    pair = Pair(txt_own, txt_in, img_own, img_in, pair_sems)
    asks = rings(ask_block, ask_ref, ask_send, ask_recv)
    mixes = rings(mix_block, mix_ref, mix_send, mix_recv)
    embeds = rings(emb_block, emb_ref, emb_send, emb_recv, Chain)
    rise = Group(raise_block, raise_ref, raise_send, raise_recv)
    fall = remote(
        reduce_block, reduce_ref.at[core], reduce_sems.at[0], reduce_sems.at[1], sibling
    )
    fall_own = pltpu.make_async_copy(reduce_block, reduce_ref.at[core], reduce_sems.at[2])
    masks = Spread(mask_block, pairs_ref, mask_send, mask_recv)
    rows = valid_ref[...].astype(WIDE)
    mask_block[...] = jnp.concatenate([rows[:, :LANES], rows[:, LANES:]], axis=0).astype(LOW)

    for when, copy in heads:
        pl.when(when)(copy.start)
    pl.when(tower == 0)(relay.start)
    for deal in deals[:2]:
        deal.start_fetch()
        deal.vectors(False)
    deals[0].whole(True, False)
    deals[1].whole(True, False)
    deals[0].whole(False, False)
    deals[1].whole(False, False)
    pair.start()
    deals[0].join()
    deals[1].join()
    pl.when(tower == 1)(relay.wait_recv)
    deals[2].start_fetch()
    deals[2].whole(True, False)
    deals[2].join()
    deals[2].whole(False, False)

    def put(ref, lane, value):
        if len(ref.shape) == 2:
            ref[: value.shape[0], lane : lane + LANES] = value
        else:
            for part in range(value.shape[0] // 16):
                ref[part, :, lane : lane + LANES] = value[part * 16 : (part + 1) * 16]

    def lift_to(kind, p, ref, start):
        slots = (img_slots, txt_slots)[kind.index]
        for c, value in lift(kind, plans[kind.index], p, slots, flat):
            lane = start + c * LANES
            put(ref, lane, value.astype(ref.dtype))

    def tokens_of(kind, half):
        own, arrived = ((img_own, img_in), (txt_own, txt_in))[kind.index]
        return own if half == kind.index else arrived

    def steps(kind):
        return [(t, kind.run) for t in range(0, kind.length, kind.run)]

    def is_end(kind, half, t, n):
        row = lax.broadcasted_iota(jnp.int32, (8, 1), 0)
        ends = jnp.zeros((8, 1), jnp.int32)
        for i in range(8):
            ends = jnp.where(row == i, ends_ref[(half * 16 + at) * 8 + i], ends)
        position = lax.broadcasted_iota(jnp.int32, (n, 8, 1), 0) + t
        return (position == ends[None]).astype(WIDE)

    def normalise(kind, half):
        width, room = kind.width, kind.room
        ref = tokens_of(kind, half)
        gain, shift = vector(vec_ref, kind, 0), vector(vec_ref, kind, 1)
        tops, raws = jnp.zeros((8, width), WIDE), jnp.zeros((8, width), WIDE)
        for t, n in steps(kind):
            rows = ref[t : t + n].astype(WIDE).reshape(n * 8, width)
            hat, _ = standardise(rows)
            first = (hat * gain + shift).astype(LOW).astype(WIDE)
            put_rows(first_rows, pl.ds(t * 8, n * 8), first)
            if kind.causal:
                chosen = is_end(kind, half, t, n)
                tops = tops + jnp.sum(first.reshape(n, 8, width) * chosen, axis=0)
                raws = raws + jnp.sum(rows.reshape(n, 8, width) * chosen, axis=0)
            elif t == 0:
                tops, raws = first[:8], rows[:8]
        top_scr[half * 8 : half * 8 + 8, :width] = tops
        at_scr[half * 8 : half * 8 + 8, :width] = raws
        spare = (room - kind.length) * 8
        put_rows(first_rows, pl.ds(kind.length * 8, spare), jnp.zeros((spare, width), WIDE))
        for i in range(8):
            line = get_rows(first_rows, pl.ds(i, room, stride=8), width)
            first_ref[half * 8 + i, :room, :width] = line.astype(LOW)

    def begin(kind):
        deal = deals[kind.index]
        deal.arrived(VECTORS)
        lift_to(kind, VECTORS, vec_ref, 0)
        normalise(kind, kind.index)

    each_tower(begin)

    def place_inputs(kind):
        deals[kind.index].arrived(0)
        slots = (img_slots, txt_slots)[kind.index]
        per = kind.width // LANES
        for c, value in lift(kind, plans[kind.index], 0, slots, flat):
            lane = c // per * WIDTH + c % per * LANES
            ref = ask_block
            if lane >= 2 * WIDTH:
                ref, lane = mix_block, lane - 2 * WIDTH
            put(ref, lane, value.astype(LOW))

    each_tower(place_inputs)
    for ring in asks:
        ring.start()

    def place_hidden(kind):
        deal, plan = deals[kind.index], plans[kind.index]
        slots = (img_slots, txt_slots)[kind.index]
        deal.arrived(2)
        per = kind.part // LANES
        for c, value in lift(kind, plan, 2, slots, flat):
            lane = c % per * LANES
            raise_block[c // per, : kind.block, lane : lane + LANES] = value.astype(LOW)
        deal.arrived(3)
        lift_to(kind, 3, reduce_block, 0)

    def place_rest(kind):
        deals[kind.index].arrived(1)
        lift_to(kind, 1, mix_block, WIDTH)
        deals[kind.index].arrived(4)
        lift_to(kind, 4, emb_block, 0)

    each_tower(place_rest)

    def question(kind):
        width = kind.width
        tops = top_scr[:, :width].astype(LOW)
        query = dot_nn(tops, matrix(ask_ref, kind, 0, width)) + vector(vec_ref, kind, 2)
        query = query.astype(LOW)
        query_ref[:, :width] = query
        for span in spans(kind):
            lo, hi, first_head, n = span
            put_rows(
                keyed_ref,
                pl.ds(first_head * SEQS, n * SEQS),
                dot_nt(head_rows(query, span), matrix(ask_ref, kind, WIDTH + lo, hi - lo)) * 0.125,
            )
        dead = (HEADS - kind.heads) * SEQS
        put_rows(keyed_ref, pl.ds(kind.heads * SEQS, dead), jnp.zeros((dead, width), WIDE))

    for ask, mix in zip(asks, mixes):
        ask.relay_deep()
        mix.start()
    for embed in embeds:
        embed.start()
    for ask in asks:
        ask.relay_row()
    each_tower(place_hidden)
    rise.start()
    fall.start()
    fall_own.start()
    pair.finish()
    each_tower(lambda kind: normalise(kind, 1 - kind.index))
    masks.start()
    for ask in asks:
        ask.finish()
    each_tower(question)
    for ring in (*mixes, *embeds):
        ring.relay_deep()

    def score(kind):
        width, room = kind.width, kind.room
        lane = lax.broadcasted_iota(jnp.int32, (HEADS, room), 1)
        for s in range(SEQS):
            keys = get_rows(keyed_ref, pl.ds(s, HEADS, stride=SEQS), width).astype(LOW)
            scores = dot_nt(keys, first_ref[s, :room, :width])
            if kind.causal:
                allowed = lane <= ends_ref[(s // 8 * 16 + at) * 8 + s % 8]
            else:
                allowed = lane < kind.length
            score_scr[s * HEADS : (s + 1) * HEADS, :room] = jnp.where(allowed, scores, -1e30)
        scores = score_scr[:, :room]
        raw = jnp.exp(scores - jnp.max(scores, axis=-1, keepdims=True))
        weights = raw / jnp.sum(raw, axis=-1, keepdims=True)
        head = lax.broadcasted_iota(jnp.int32, (SEQS * HEADS, 1), 0) % HEADS
        weights = jnp.where(head < kind.heads, weights, 0.0)
        weight_ref[:, :room] = weights
        low_scr[: SEQS * HEADS, :room] = weights.astype(LOW)

    each_tower(score)
    for ring in (*mixes, *embeds):
        ring.relay_row()

    def mixture(kind):
        width, room = kind.width, kind.room
        for s in range(SEQS):
            mixed = dot_nn(
                low_scr[s * HEADS : (s + 1) * HEADS, :room], first_ref[s, :room, :width]
            )
            put_rows(mixture_ref, pl.ds(s, HEADS, stride=SEQS), mixed)
        totals = jnp.sum(
            low_scr[: SEQS * HEADS, :room].astype(WIDE), axis=-1, keepdims=True
        )
        score_scr[...] = jnp.broadcast_to(totals, score_scr.shape)

    each_tower(mixture)

    for mix in mixes:
        mix.finish()

    def answer(kind):
        width = kind.width
        mixed = []
        bias = vector(vec_ref, kind, 3)
        for span in spans(kind):
            lo, hi, first_head, n = span
            z = get_rows(mixture_ref, pl.ds(first_head * SEQS, n * SEQS), width).astype(LOW)
            valued = dot_nn(z, matrix(mix_ref, kind, lo, hi - lo))
            totals = jnp.concatenate(
                [score_scr[pl.ds(first_head + h, SEQS, stride=HEADS), 0:1] for h in range(n)],
                axis=0,
            )
            mixed.append(from_head_rows(valued + totals * bias[:, lo:hi], span))
        mixed = side_by_side(mixed).astype(LOW)
        middle = (
            at_scr[:, :width]
            + dot_nn(mixed, matrix(mix_ref, kind, WIDTH, width))
            + vector(vec_ref, kind, 4)
        )
        middle_ref[:, :width] = middle
        hat, _ = standardise(middle)
        second_ref[:, :width] = (
            hat * vector(vec_ref, kind, 5) + vector(vec_ref, kind, 6)
        ).astype(LOW)
        put_rows(mixture_ref, pl.ds(12 * SEQS, SEQS), top_scr[:, :width])
        put_rows(mixture_ref, pl.ds(13 * SEQS, SEQS), mixed.astype(WIDE))

    each_tower(answer)
    rise.relay()
    masks.relay()
    for embed in embeds:
        embed.finish()
    rise.finish()
    fall_own.wait()
    remote(
        reduce_block, reduce_ref.at[1 - core], reduce_sems.at[0], reduce_sems.at[1], sibling
    ).wait_recv()

    sent = group_exchange(False, second_ref, seconds, group_send.at[0], group_recv.at[0])
    hidden_kernel(seconds, raise_ref, reduce_ref, vec_ref, part, raised)
    sent += group_exchange(True, part, parts, group_send.at[1], group_recv.at[1])
    embed_kernel(parts, middle_ref, emb_ref, vec_ref, emb, final, pooled_ref, proj)
    embs = Spread(emb, all_embs, embs_send, embs_recv)
    embs.start()
    masks.finish()
    embs.relay()
    embs.finish()
    objective_kernel(
        scale_ref,
        all_embs,
        pairs_ref,
        final,
        proj,
        emb_ref,
        vec_ref,
        low,
        grad_ref,
        proj_grad_ref,
        final_vec_ref,
        loss_ref,
        scale_new_ref,
        own_scr,
    )
    sent += group_exchange(False, low, lows, group_send.at[2], group_recv.at[2])
    hidden_back_kernel(
        lows,
        seconds,
        raised,
        raise_ref,
        reduce_ref,
        back,
        raise_grad_ref,
        reduce_keep_ref,
        reduce_send_ref,
        bias_ref,
        whole,
    )
    sent += group_exchange(True, back, backs_ref, group_send.at[3], group_recv.at[3])
    halves = remote(
        raise_grad_ref.at[1 - core], raise_half, home_sems.at[0], home_sems.at[1], sibling
    )
    fallen = remote(reduce_send_ref, reduce_in, home_sems.at[2], home_sems.at[3], sibling)
    halves.start()
    fallen.start()
    risen_group = Group(risen_block, raise_all, risen_send, risen_recv, False)

    lefts = Blocks(left_block, left_all, left_send, left_recv)
    turns = Blocks(turn_block, turn_all, turn_send, turn_recv)
    early = Chain(early_block, early_all, early_send, early_recv)
    late = Ring(late_block, late_all, late_send, late_recv)
    home_pair = Pair(img_send, img_home, txt_send, txt_home, home_pair_sems)
    collects = [
        Collect(plans[0], 0, img_home_slots, img_chunks, collect_send.at[0], collect_recv),
        Collect(plans[1], 1, txt_home_slots, txt_chunks, collect_send.at[1], collect_recv),
    ]

    def outputs(kind):
        width = kind.width
        second_grad = jnp.sum(backs_ref[:, :, :width].astype(WIDE), axis=0)
        second_scr[:, :width] = second_grad
        hat, rate = standardise(middle_ref[:, :width])
        middle_grad = grad_ref[:, :width] + norm_back(
            second_grad, vector(vec_ref, kind, 5), hat, rate
        )
        middle_scr[:, :width] = middle_grad
        output_grad = middle_grad.astype(LOW)
        mixed_grad = dot_nt(output_grad, matrix(mix_ref, kind, WIDTH, width)).astype(LOW)
        early_block[:, 0:width] = query_ref[:, :width]
        early_block[:, WIDTH : WIDTH + width] = mixed_grad
        early_block[:, 2 * WIDTH : 2 * WIDTH + width] = output_grad
        early_block[:, 3 * WIDTH : 3 * WIDTH + EMB] = proj_grad_ref[...]
        left_scr[:, :width] = get_rows(mixture_ref, slice(None), width)
        left_scr[14 * SEQS : 15 * SEQS, :width] = pooled_ref[:, :width].astype(WIDE)
        left_scr[15 * SEQS :, :width] = jnp.zeros((SEQS, width), WIDE)

    each_tower(outputs)
    early.start()

    def turned(kind):
        width, block = kind.width, kind.block
        left_block[:, :block, :] = left_scr[:, :width].T.reshape(16, block, 256).astype(LOW)

    each_tower(turned)
    lefts.start()

    def values(kind):
        width = kind.width
        mixed_grad = early_block[:, WIDTH : WIDTH + width]
        bias = vector(vec_ref, kind, 3)
        dead = kind.heads * SEQS
        put_rows(valued_scr, pl.ds(dead, 256 - dead), jnp.zeros((256 - dead, width), WIDE))
        shared_scr[dead:, :] = jnp.zeros((256 - dead, LANES), WIDE)
        for span in spans(kind):
            lo, hi, first_head, n = span
            rows = head_rows(mixed_grad, span)
            place = pl.ds(first_head * SEQS, n * SEQS)
            put_rows(valued_scr, place, dot_nt(rows, matrix(mix_ref, kind, lo, hi - lo)))
            constant = jnp.sum(rows.astype(WIDE) * bias[:, lo:hi], axis=-1, keepdims=True)
            shared_scr[place, :] = jnp.broadcast_to(constant, (n * SEQS, LANES))

    each_tower(values)
    halves.wait_recv()
    risen_block[...] = (
        raise_grad_ref[core].astype(WIDE) + raise_half[...].astype(WIDE)
    ).astype(LOW)
    risen_group.start()

    def slopes(kind):
        width, room = kind.width, kind.room
        for s in range(SEQS):
            line = pl.ds(s, HEADS, stride=SEQS)
            slope = dot_nt(
                get_rows(valued_scr, line, width).astype(LOW), first_ref[s, :room, :width]
            )
            slope_scr[s * HEADS : (s + 1) * HEADS, :room] = slope + shared_scr[line, 0:1]
        weights = weight_ref[:, :room]
        slope = slope_scr[:, :room]
        slope = weights * (slope - jnp.sum(weights * slope, axis=-1, keepdims=True))
        both = jnp.concatenate(
            [slope.reshape(SEQS, HEADS, room), weights.reshape(SEQS, HEADS, room)], axis=1
        )
        low_scr[:, :room] = both.reshape(2 * SEQS * HEADS, room).astype(LOW)

    each_tower(slopes)
    early.relay_deep()

    def tokens(kind):
        width, room = kind.width, kind.room
        for s in range(SEQS):
            line = pl.ds(s, HEADS, stride=SEQS)
            both = low_scr[2 * s * HEADS : 2 * (s + 1) * HEADS, :room]
            first = first_ref[s, :room, :width]
            put_rows(turn_scr, line, dot_nn(both[:HEADS], first))
            right = jnp.concatenate(
                [get_rows(keyed_ref, line, width), get_rows(valued_scr, line, width)], axis=0
            )
            put_rows(
                rows_grad.at[s // 8],
                pl.ds(s % 8, room, stride=8),
                dot_tn(both, right.astype(LOW)),
            )

    each_tower(tokens)
    early.relay_row()

    def queries(kind):
        width, block = kind.width, kind.block
        grads = []
        for span in spans(kind):
            lo, hi, first_head, n = span
            rows = get_rows(turn_scr, pl.ds(first_head * SEQS, n * SEQS), width).astype(LOW)
            back = dot_nn(rows, matrix(ask_ref, kind, WIDTH + lo, hi - lo)) * 0.125
            grads.append(from_head_rows(back, span))
        query_grad = side_by_side(grads).astype(LOW)
        late_block[:, :width] = query_grad
        top_grad_scr[:, :width] = dot_nt(query_grad, matrix(ask_ref, kind, 0, width))
        turn_block[:, :block, :] = (
            get_rows(turn_scr, slice(None), width).T.reshape(16, block, 256).astype(LOW)
        )

    each_tower(queries)
    late.start()
    turns.start()
    gains[...] = jnp.zeros_like(gains)

    def finish(kind, half):
        width = kind.width
        ref = tokens_of(kind, half)
        keep, send = ((img_keep, img_send), (txt_keep, txt_send))[kind.index]
        gain = vector(vec_ref, kind, 0)
        top = top_grad_scr[half * 8 : half * 8 + 8, :width]
        low = middle_scr[half * 8 : half * 8 + 8, :width]
        gain_sum = jnp.zeros((1, width), WIDE)
        shift_sum = jnp.zeros((1, width), WIDE)
        for t, n in steps(kind):
            hat, rate = standardise(ref[t : t + n].astype(WIDE).reshape(n * 8, width))
            grad = get_rows(rows_grad.at[half], pl.ds(t * 8, n * 8), width)
            chosen = None
            if kind.causal:
                chosen = is_end(kind, half, t, n)
            elif t == 0:
                chosen = (lax.broadcasted_iota(jnp.int32, (n, 8, 1), 0) == 0).astype(WIDE)
            if chosen is not None:
                grad = grad + (chosen * top[None]).reshape(n * 8, width)
            gain_sum += jnp.sum(grad * hat, axis=0, keepdims=True)
            shift_sum += jnp.sum(grad, axis=0, keepdims=True)
            result = norm_back(grad, gain, hat, rate)
            if chosen is not None:
                result = result + (chosen * low[None]).reshape(n * 8, width)
            result = result.reshape(n, 8, width)
            if half == kind.index:
                keep[t : t + n] = result
            else:
                send[t : t + n] = result.astype(LOW)
        gains[0:1, :width] += gain_sum
        gains[1:2, :width] += shift_sum

    each_tower(lambda kind: finish(kind, 1 - kind.index))
    home_pair.start()
    risen_group.finish()
    fallen.wait_recv()

    def slots_of(kind):
        return (img_home_slots, txt_home_slots)[kind.index]

    def hidden_grads(kind):
        plan, collect = plans[kind.index], collects[kind.index]
        block, n, per = kind.block, kind.reduce_rows, kind.part // LANES

        def risen(c):
            chip, lane = c // per, c % per * LANES
            return raise_all[chip, :block, lane : lane + LANES].astype(WIDE)

        def fallen(c):
            lane = c * LANES
            return reduce_keep_ref[:n, lane : lane + LANES] + reduce_in[
                :n, lane : lane + LANES
            ].astype(WIDE)

        drop(kind, plan, 2, risen, slots_of(kind), flat)
        collect.piece(2, False)
        drop(kind, plan, 3, fallen, slots_of(kind), flat)
        collect.piece(3, False)

    each_tower(hidden_grads)
    late.relay_deep()
    each_tower(lambda kind: finish(kind, kind.index))
    late.relay_row()

    def lines(kind):
        width = kind.width
        hat, _ = standardise(middle_ref[:, :width])
        second_grad = second_scr[:, :width]

        def column_sum(value):
            return jnp.sum(value.astype(WIDE), axis=0, keepdims=True)

        mixed_grad = early_block[:, WIDTH : WIDTH + width].astype(WIDE)
        weights = low_scr[:, : kind.room].astype(WIDE).reshape(SEQS, 2 * HEADS, kind.room)
        totals = jnp.sum(weights[:, HEADS:], axis=-1, keepdims=True).reshape(SEQS * HEADS, 1)
        shared_scr[...] = jnp.broadcast_to(totals, shared_scr.shape)
        value_bias = []
        for lo, hi, first_head, n in spans(kind):
            owner = lax.broadcasted_iota(jnp.int32, (SEQS, hi - lo), 1) // HEAD
            scaled = jnp.zeros((SEQS, hi - lo), WIDE)
            for h in range(n):
                total = shared_scr[pl.ds(first_head + h, SEQS, stride=HEADS), 0:1]
                scaled = jnp.where(owner == h, mixed_grad[:, lo:hi] * total, scaled)
            value_bias.append(column_sum(scaled))
        hidden = bias_ref[0:1, : kind.part]
        parts = [
            gains[0:1, :width],
            gains[1:2, :width],
            column_sum(late_block[:, :width]),
            side_by_side(value_bias),
            column_sum(early_block[:, 2 * WIDTH : 2 * WIDTH + width]),
            column_sum(second_grad * hat),
            column_sum(second_grad),
            final_vec_ref[2:3, :width],
            final_vec_ref[0:1, :width],
            final_vec_ref[1:2, :width],
            jnp.concatenate([hidden, jnp.zeros((1, width - kind.part), WIDE)], axis=1),
            jnp.zeros((5, width), WIDE),
        ]
        lines_block[:, :width] = jnp.concatenate(parts, axis=0)

    each_tower(lines)
    line_copy = remote(
        lines_block, lines_all.at[at], lines_send.at[0], lines_recv.at[at], (tower, jnp.int32(0))
    )
    line_own = pltpu.make_async_copy(lines_block, lines_all.at[at], lines_recv.at[at])
    pl.when(at > 0)(line_copy.start)
    pl.when(at == 0)(line_own.start)

    early.finish()
    lefts.finish()

    def from_early(kind):
        plan, collect = plans[kind.index], collects[kind.index]
        width, block = kind.width, kind.block

        def gathered(k):
            lane = lax.broadcasted_iota(jnp.int32, (block, LANES), 1) // SEQS
            halves = []
            for side in range(2):
                total = jnp.zeros((block, LANES), WIDE)
                for j in range(8):
                    part = left_all[side * 8 + j, :block, LANES:].astype(WIDE)
                    shift = (j * SEQS - (k - 8) * SEQS) % LANES
                    turned_part = pltpu.roll(part, shift, 1) if shift else part
                    total = jnp.where(lane == j, turned_part, total)
                halves.append(total)
            return jnp.concatenate(halves, axis=1).astype(LOW)

        def right(start, wide):
            return early_all[:, :, start : start + wide].reshape(256, wide)

        output = dot_nn(gathered(13), right(2 * WIDTH, width))
        drop(
            kind, plan, 1, lambda c: output[:, c * LANES : (c + 1) * LANES], slots_of(kind), flat
        )
        collect.piece(1, False)
        embed = dot_nn(gathered(14), right(3 * WIDTH, EMB))
        drop(kind, plan, 4, lambda c: embed[:, c * LANES : (c + 1) * LANES], slots_of(kind), flat)
        collect.piece(4, False)
        left_scr[:block, :256] = gathered(12).astype(WIDE)

    each_tower(from_early)
    late.finish()
    turns.finish()

    def from_late(kind):
        plan, collect = plans[kind.index], collects[kind.index]
        width, block = kind.width, kind.block
        ask = dot_nn(left_scr[:block, :256].astype(LOW), late_all[:, :, :width].reshape(256, width))

        def outer(side_ref, start, span):
            lo, hi, first_head, n = span
            lane = first_head * SEQS
            total = jnp.zeros((block, hi - lo), WIDE)
            for j in range(8):
                left, rows = [], []
                for source in (2 * j, 2 * j + 1):
                    left.append(side_ref[source, :block, lane : lane + LANES])
                    rows.append(
                        head_rows(early_all[source, :, start : start + width], span)
                    )
                    if n < 8:
                        rows.append(jnp.zeros(((8 - n) * SEQS, hi - lo), LOW))
                total += dot_nn(
                    jnp.concatenate(left, axis=1), jnp.concatenate(rows, axis=0)
                )
            return total

        keys = side_by_side([outer(turn_all, 0, span) for span in spans(kind)]) * 0.125
        worth = side_by_side([outer(left_all, WIDTH, span) for span in spans(kind)])
        per = width // LANES

        def inputs(c):
            value = (ask, keys, worth)[c // per]
            return value[:, c % per * LANES : (c % per + 1) * LANES]

        drop(kind, plan, 0, inputs, slots_of(kind), flat)
        collect.piece(0, False)

    each_tower(from_late)

    @pl.when(at == 0)
    def _():
        for k in range(1, 16):
            remote(
                lines_block, lines_all.at[k], lines_send.at[0], lines_recv.at[k], sibling
            ).wait_recv()
        line_own.wait()

        def vectors(kind):
            width, part = kind.width, kind.part
            whole = [jnp.sum(lines_all[:, :10, :width], axis=0)]
            for row in range(4):
                pair_of = []
                for chip in (2 * row, 2 * row + 1):
                    pair_of.append(
                        lines_all[2 * chip, 10:11, :part] + lines_all[2 * chip + 1, 10:11, :part]
                    )
                whole.append(jnp.concatenate(pair_of, axis=1))
            whole.append(jnp.zeros((2, width), WIDE))
            result = jnp.concatenate(whole, axis=0)
            drop(
                kind,
                plans[kind.index],
                VECTORS,
                lambda c: result[:, c * LANES : (c + 1) * LANES],
                slots_of(kind),
                flat,
            )

        each_tower(vectors)

    each_tower(lambda kind: collects[kind.index].piece(VECTORS, False))
    home_pair.finish()

    @pl.when(tower == 1)
    def _():
        img_keep[...] = img_home[...].astype(WIDE)

    @pl.when(tower == 0)
    def _():
        txt_keep[...] = txt_home[...].astype(WIDE)

    for collect in collects:
        collect.finish()
    for copy in (*sent, fall, fallen, halves):
        copy.wait_send()
    pl.when(at > 0)(line_copy.wait_send)
    for when, copy in heads:
        pl.when(when)(copy.wait_send)
    pl.when(tower == 0)(relay.wait_send)
    for group in (pair, *asks, *mixes, *embeds, rise, masks, embs, *deals):
        group.drain()
    for group in (risen_group, lefts, turns, early, late, home_pair):
        group.drain()

    def drain(kind):
        for p in range(VECTORS + 1):
            collects[kind.index].piece(p, True)

    each_tower(drain)


ROWS_LOW = ((SEQS, WIDTH), LOW)
ROWS_WIDE = ((SEQS, WIDTH), WIDE)
HEAD_ROWS = ((WIDTH // LANES, SEQS * HEADS, LANES), WIDE)
LANE_ROWS = ((SEQS * HEADS, LANES), WIDE)
GROUP = ((8, SEQS, WIDTH), LOW)
HIDDEN_BLOCKS = ((2, 8, 48, PART), LOW)
OUTER = ((16, 48, SEQS * HEADS), LOW)


def chunk_shapes(plan, n):
    return ((n, plan.rows, LANES), LOW)


def run_step(scalars, chunks, valid, tokens, plans):
    most = max(plan.local for plan in plans) + 17
    slots = max(plan.slots for plan in plans)
    edges = [((plan.rows, LANES), LOW) for plan in plans]
    rooms = [((kind.length, 8, kind.width), LOW) for kind in TOWERS]
    outs = [((kind.length, 8, kind.width), WIDE) for kind in TOWERS] + [
        chunk_shapes(plan, plan.local) for plan in plans
    ]
    scratch = [
        ROWS_LOW,
        ROWS_WIDE,
        ROWS_LOW,
        HEAD_ROWS,
        HEAD_ROWS,
        LANE_ROWS,
        ((SEQS, ROOM, WIDTH), LOW),
        ((WIDTH // LANES, ROOM * 8, LANES), WIDE),
        rooms[0],
        rooms[1],
        ((3, 16, 16, 2 * WIDTH), LOW),
        ((3, 16, 16, 2 * WIDTH), LOW),
        ((3, 16, 16, EMB), LOW),
        ROWS_WIDE,
        HIDDEN_BLOCKS,
        ((2, 192, WIDTH), LOW),
        ((2, 16, 16, LANES), LOW),
        chunk_shapes(plans[0], plans[0].slots),
        chunk_shapes(plans[1], plans[1].slots),
        edges[0],
        edges[1],
        edges[0],
        edges[1],
        chunk_shapes(plans[1], plans[1].local),
        edges[1],
        edges[1],
        ((plans[0].slots * plans[0].rows, LANES), WIDE),
        ((3, 16, 2 * WIDTH), LOW),
        ((3, 16, 2 * WIDTH), LOW),
        ((3, 16, EMB), LOW),
        ((8, 48, PART), LOW),
        ((192, WIDTH), LOW),
        ((16, LANES), LOW),
        ROWS_WIDE,
        ROWS_WIDE,
        LANE_ROWS,
        ((2 * SEQS * HEADS, LANES), LOW),
        ROWS_WIDE,
        ROWS_LOW,
        ((SEQS, EMB), LOW),
        ((8, WIDTH), WIDE),
        HIDDEN_BLOCKS,
        ((192, WIDTH), WIDE),
        ((192, WIDTH), LOW),
        ((8, PART), WIDE),
        GROUP,
        GROUP,
        GROUP,
        GROUP,
        ((128, PART), WIDE),
        ((SEQS, EMB), LOW),
        ((2, 16, SEQS, EMB), LOW),
        ROWS_WIDE,
        ((SEQS, EMB), WIDE),
        ROWS_LOW,
        GROUP,
        GROUP,
        ((256, EMB), WIDE),
        ((PART, WIDTH), WIDE),
        rooms[0],
        rooms[1],
        rooms[0],
        rooms[1],
        ((2, WIDTH // LANES, ROOM * 8, LANES), WIDE),
        ROWS_WIDE,
        ROWS_WIDE,
        HEAD_ROWS,
        HEAD_ROWS,
        LANE_ROWS,
        LANE_ROWS,
        ((SEQS * HEADS, WIDTH), WIDE),
        OUTER,
        OUTER,
        OUTER,
        OUTER,
        ((SEQS, 3 * WIDTH + EMB), LOW),
        ((16, SEQS, 3 * WIDTH + EMB), LOW),
        ROWS_LOW,
        ((16, SEQS, WIDTH), LOW),
        ROWS_WIDE,
        ((16, SEQS, WIDTH), WIDE),
        ((8, 48, PART), LOW),
        ((8, 48, PART), LOW),
        ((8, 48, PART), LOW),
        ((192, WIDTH), LOW),
        chunk_shapes(plans[0], plans[0].slots),
        chunk_shapes(plans[1], plans[1].slots),
        ((8, WIDTH), WIDE),
        ROWS_WIDE,
    ]
    semaphores = [
        (3, most),
        (2, 6,),
        (3, 2),
        (3,),
        (2,),
        (3, 16),
        (3, 15),
        (3, 16),
        (3, 15),
        (3, 20),
        (3, 15),
        (9,),
        (8,),
        (3,),
        (2,),
        (17,),
        (16,),
        (4, 8,),
        (4, 7,),
        (17,),
        (16,),
        (4,),
        (9,),
        (8,),
        (16,),
        (15,),
        (16,),
        (15,),
        (20,),
        (15,),
        (16,),
        (15,),
        (1,),
        (16,),
        (2,),
        (2, 2, slots,),
        (2,),
    ]
    smem = pl.BlockSpec(memory_space=pltpu.SMEM)
    vmem = pl.BlockSpec(memory_space=pltpu.VMEM)
    like = jax.ShapeDtypeStruct
    return pl.pallas_call(
        functools.partial(step_kernel, plans),
        out_shape=[like((1,), WIDE), like((3,), WIDE)] + [like(*out) for out in outs],
        in_specs=[smem, smem, ANY, ANY, vmem, vmem, vmem],
        out_specs=[smem, smem, vmem, vmem, vmem, vmem],
        scratch_shapes=[pltpu.VMEM(*each) for each in scratch]
        + [pltpu.SemaphoreType.DMA(shape) for shape in semaphores],
        compiler_params=comm_params(0),
    )(*scalars, *chunks, valid, *tokens)


def to_chunks(flat, plan, me):
    start = me * plan.share % plan.chunk
    padded = jnp.pad(flat, (plan.chunk, plan.local * plan.chunk - plan.share))
    piece = lax.dynamic_slice(padded, (plan.chunk - start,), (plan.local * plan.chunk,))
    return piece.astype(LOW).reshape(plan.local, plan.rows, LANES)


def from_chunks(chunks, plan, me):
    start = me * plan.share % plan.chunk
    return lax.dynamic_slice(chunks.reshape(-1), (start,), (plan.share,)).astype(WIDE)


def step(
    img_tokens,
    txt_tokens,
    txt_ends,
    valid,
    img_master,
    img_moment,
    img_average,
    txt_master,
    txt_moment,
    txt_average,
    scale_state,
):
    me = lax.axis_index(("tower", "dp"))
    plans = (
        Plan(0, img_master.shape[0], 96, (9, 3, 12, 12, 2)),
        Plan(1, txt_master.shape[0], 64, (6, 2, 8, 8, 2)),
    )
    loss, scale_new, img_grad, txt_grad, img_chunks, txt_chunks = run_step(
        (txt_ends, scale_state),
        (to_chunks(img_master, plans[0], me), to_chunks(txt_master, plans[1], me)),
        valid,
        (jnp.transpose(img_tokens, (1, 0, 2)), jnp.transpose(txt_tokens, (1, 0, 2))),
        plans,
    )
    img_new = advance(
        img_master, img_moment, img_average, from_chunks(img_chunks, plans[0], me), step_rate
    )
    txt_new = advance(
        txt_master, txt_moment, txt_average, from_chunks(txt_chunks, plans[1], me), step_rate
    )
    return (
        loss[0],
        jnp.transpose(img_grad, (1, 0, 2)),
        jnp.transpose(txt_grad, (1, 0, 2)),
        img_new[0],
        img_new[1],
        img_new[2],
        img_new[0].astype(LOW),
        txt_new[0],
        txt_new[1],
        txt_new[2],
        txt_new[0].astype(LOW),
        scale_new,
    )


def from_partner(value, axis, stride):
    mask = 2**stride
    pairs = [(source, source ^ mask) for source in range(lax.axis_size(axis))]
    return lax.ppermute(value, axis, pairs)


def round_value(v):
    return lax.optimization_barrier(v.astype(jnp.bfloat16)).astype(jnp.float32)


def make_low():

    def value_keep(v):
        return (round_value(v), None)

    def grad_pass(kept, grad):
        return (grad,)

    rounded = jax.custom_vjp(round_value)
    rounded.defvjp(value_keep, grad_pass)
    return rounded


def low(v):
    return make_low()(v)


def make_low_back():

    def identity(v):
        return v

    def value_pass(v):
        return (v, None)

    def grad_round(kept, grad):
        return (round_value(grad),)

    passed = jax.custom_vjp(identity)
    passed.defvjp(value_pass, grad_round)
    return passed


def low_back(v):
    return make_low_back()(v)


def both_ways(value):
    return low(low_back(value))


def product(left, right):
    return jnp.matmul(left, right)


def contract(form, left, right):
    return jnp.einsum(form, left, right)


def layer_norm(values, gain_row, shift_row):
    centred = values - jnp.mean(values, axis=-1, keepdims=True)
    spread = jnp.mean(centred * centred, axis=-1, keepdims=True)
    return centred * lax.rsqrt(spread + 1e-05) * gain_row + shift_row


def unpack(flat_weights, model_width, hidden_width, embed_width):
    piece_shapes = [
        (model_width, 3 * model_width),
        (model_width, model_width),
        (model_width, hidden_width),
        (hidden_width, model_width),
        (model_width, embed_width),
        (10, model_width),
        (hidden_width,),
    ]
    pieces = []
    offset = 0
    for piece_shape in piece_shapes:
        length = math.prod(piece_shape)
        pieces.append(flat_weights[offset : offset + length].reshape(piece_shape))
        offset = offset + length
    return pieces


def encode(tokens, flat_weights, positions, causal, model_width, hidden_width, embed_width):
    w_inputs, w_output, w_expand, w_reduce, w_embed, vectors, expand_bias = unpack(
        flat_weights, model_width, hidden_width, embed_width
    )
    groups = tokens.shape[0]
    length = tokens.shape[1]
    first = low(layer_norm(tokens, vectors[0], vectors[1]))
    bias_in = jnp.concatenate([vectors[2], jnp.zeros_like(vectors[2]), vectors[3]])
    joined = both_ways(product(first, w_inputs) + bias_in)
    joined = joined.reshape(groups, length, 3, model_width // HEAD, HEAD)
    scores = low_back(contract("gqhd,gkhd->ghqk", joined[:, :, 0], joined[:, :, 1]) * 0.125)
    if causal:
        row_index = lax.broadcasted_iota(jnp.int32, (length, length), 0)
        col_index = lax.broadcasted_iota(jnp.int32, (length, length), 1)
        scores = jnp.where(col_index <= row_index, scores, -1e30)
    row_top = jnp.max(scores, axis=-1, keepdims=True)
    raw_weights = jnp.exp(scores - row_top)
    attention = low(raw_weights / jnp.sum(raw_weights, axis=-1, keepdims=True))
    mixed_heads = both_ways(
        contract("ghqk,gkhd->gqhd", attention, joined[:, :, 2]).reshape(groups, length, model_width)
    )
    middle = tokens + low_back(product(mixed_heads, w_output) + vectors[4])
    second = low(layer_norm(middle, vectors[5], vectors[6]))
    raised = low_back(product(second, w_expand) + expand_bias)
    active = low(raised * jax.nn.sigmoid(1.702 * raised))
    final_rows = middle + low_back(product(active, w_reduce) + vectors[7])
    pooled = jnp.take_along_axis(final_rows, positions[:, None, None], axis=1)[:, 0]
    pooled = low(layer_norm(pooled, vectors[8], vectors[9]))
    projected = low_back(product(pooled, w_embed))
    return low(
        projected * lax.rsqrt(jnp.sum(projected * projected, axis=-1, keepdims=True) + 1e-06)
    )


def inner(left, right):
    return lax.dot_general(
        left, right, (((1,), (1,)), ((), ())), preferred_element_type=jnp.float32
    )


def across(left, right):
    return lax.dot_general(
        left, right, (((0,), (0,)), ((), ())), preferred_element_type=jnp.float32
    )


def softmax_total(logits, allowed):
    masked = jnp.where(allowed, logits, -1e30)
    row_top = jnp.max(masked, axis=1, keepdims=True)
    return jnp.log(jnp.sum(jnp.exp(masked - row_top), axis=1)) + row_top[:, 0]


def advance(master, moment, average, grads, rate):
    moment_new = momentum_rate * moment + grads
    master_new = master - rate * (grads + momentum_rate * moment_new)
    average_new = average_rate * average + (1.0 - average_rate) * master_new
    return (master_new, moment_new, average_new)


def padded_to(flat, length):
    return jnp.pad(flat, (0, length - flat.shape[0]))


def body(
    img_tokens,
    txt_tokens,
    txt_ends,
    valid,
    img_master,
    img_moment,
    img_average,
    txt_master,
    txt_moment,
    txt_average,
    scale_state,
):
    batch_rows = img_tokens.shape[0]
    total_rows = batch_rows * lax.axis_size(("tower", "dp"))
    device_at = lax.axis_index(("tower", "dp"))
    tower_at = lax.axis_index("tower")
    is_image = tower_at == 0
    img_share = img_master.shape[0]
    txt_share = txt_master.shape[0]
    img_count = img_tokens.size
    txt_count = txt_tokens.size
    shard_room = max(img_share, txt_share)
    token_room = max(img_count, txt_count)
    tower_count = lax.axis_size("dp")
    dp_at = lax.axis_index("dp")
    img_low = padded_to(img_master.astype(jnp.bfloat16), shard_room)
    txt_low = padded_to(txt_master.astype(jnp.bfloat16), shard_room)
    token_out = jnp.where(
        is_image,
        padded_to(txt_tokens.reshape(-1), token_room),
        padded_to(img_tokens.reshape(-1), token_room),
    )
    weight_out = jnp.where(is_image, txt_low, img_low)
    weight_mine = jnp.where(is_image, img_low, txt_low)
    token_in, weight_in = from_partner((token_out, weight_out), "tower", 0)
    stacked = jnp.where(
        is_image, jnp.stack([weight_mine, weight_in]), jnp.stack([weight_in, weight_mine])
    )
    gathered = lax.all_gather(stacked, "dp", axis=1, tiled=True)
    pair_ends = jnp.concatenate(
        [
            lax.dynamic_slice_in_dim(txt_ends, dp_at * batch_rows, batch_rows),
            lax.dynamic_slice_in_dim(txt_ends, (tower_count + dp_at) * batch_rows, batch_rows),
        ]
    )
    pair_zero = jnp.zeros((2 * batch_rows,), jnp.int32)

    def image_weights(whole):
        return whole.reshape(2, tower_count, shard_room).reshape(-1).astype(jnp.float32)

    def text_weights(whole):
        return (
            whole.reshape(2, tower_count, shard_room)[:, :, :txt_share]
            .reshape(-1)
            .astype(jnp.float32)
        )

    def image_rows(arrived):
        return jnp.concatenate(
            [img_tokens, arrived[:img_count].reshape(img_tokens.shape)], axis=0
        ).astype(jnp.float32)

    def text_rows(arrived):
        return jnp.concatenate([arrived.reshape(txt_tokens.shape), txt_tokens], axis=0).astype(
            jnp.float32
        )

    def image_encode(rows, flat):
        return encode(rows, flat, pair_zero, False, D_IMG, FF_IMG, EMB)

    def text_encode(rows, flat):
        return encode(rows, flat, pair_ends, True, D_TXT, FF_TXT, EMB)

    def image_forward(operands):
        return image_encode(image_rows(operands[1]), image_weights(operands[0]))

    def text_forward(operands):
        return text_encode(text_rows(operands[1]), text_weights(operands[0]))

    pair_emb = lax.cond(is_image, image_forward, text_forward, (gathered, token_in)).astype(
        jnp.bfloat16
    )
    emb_in = from_partner(pair_emb, "tower", 0)
    img_pair = jnp.where(is_image, pair_emb, emb_in)
    txt_pair = jnp.where(is_image, emb_in, pair_emb)
    row_start = tower_at * batch_rows
    img_local = lax.dynamic_slice_in_dim(img_pair, row_start, batch_rows)
    txt_local = lax.dynamic_slice_in_dim(txt_pair, row_start, batch_rows)
    img_all, txt_all = (
        lax.all_gather(img_local, ("tower", "dp"), axis=0, tiled=True),
        lax.all_gather(txt_local, ("tower", "dp"), axis=0, tiled=True),
    )
    logit_scale = jnp.exp(scale_state[0])
    offset = device_at * batch_rows
    row_index = lax.broadcasted_iota(jnp.int32, (batch_rows, total_rows), 0) + offset
    col_index = lax.broadcasted_iota(jnp.int32, (batch_rows, total_rows), 1)
    diagonal = (row_index == col_index).astype(jnp.float32)
    allowed = valid > 0
    row_logits = logit_scale * inner(img_local, txt_all)
    col_logits = logit_scale * inner(txt_local, img_all)
    row_lse = softmax_total(row_logits, allowed)
    col_lse = softmax_total(col_logits, allowed)
    partial_loss = 0.5 * (
        jnp.sum(row_lse)
        - jnp.sum(row_logits * diagonal)
        + jnp.sum(col_lse)
        - jnp.sum(col_logits * diagonal)
    )
    row_terms = 0.5 * (jnp.where(allowed, jnp.exp(row_logits - row_lse[:, None]), 0.0) - diagonal)
    col_terms = 0.5 * (jnp.where(allowed, jnp.exp(col_logits - col_lse[:, None]), 0.0) - diagonal)
    partial_scale = jnp.sum(row_terms * row_logits) + jnp.sum(col_terms * col_logits)
    row_back = (logit_scale * row_terms).astype(jnp.bfloat16)
    col_back = (logit_scale * col_terms).astype(jnp.bfloat16)
    img_emb_grad = jnp.dot(row_back, txt_all, preferred_element_type=jnp.float32)
    txt_emb_grad = jnp.dot(col_back, img_all, preferred_element_type=jnp.float32)
    img_extra, txt_extra = (
        lax.psum_scatter(
            across(col_back, txt_local), ("tower", "dp"), scatter_dimension=0, tiled=True
        ),
        lax.psum_scatter(
            across(row_back, img_local), ("tower", "dp"), scatter_dimension=0, tiled=True
        ),
    )
    img_emb_grad = img_emb_grad + img_extra
    txt_emb_grad = txt_emb_grad + txt_extra
    sums = lax.psum((partial_loss, partial_scale), ("tower", "dp"))
    grad_out = jnp.where(is_image, txt_emb_grad, img_emb_grad)
    grad_in = from_partner(grad_out, "tower", 0)
    pair_cot = jnp.where(
        is_image,
        jnp.concatenate([img_emb_grad, grad_in], axis=0),
        jnp.concatenate([grad_in, txt_emb_grad], axis=0),
    )

    def image_backward(operands):
        recomputed, tower_pullback = jax.vjp(
            image_encode, image_rows(operands[1]), image_weights(operands[0])
        )
        rows_grad, flat_grad = tower_pullback(operands[2])
        own_part = padded_to(rows_grad[:batch_rows].reshape(-1), token_room)
        sent_part = padded_to(rows_grad[batch_rows:].reshape(-1), token_room)
        stacked_grad = flat_grad.reshape(2, tower_count, img_share)
        return (own_part, sent_part, stacked_grad)

    def text_backward(operands):
        recomputed, tower_pullback = jax.vjp(
            text_encode, text_rows(operands[1]), text_weights(operands[0])
        )
        rows_grad, flat_grad = tower_pullback(operands[2])
        own_part = padded_to(rows_grad[batch_rows:].reshape(-1), token_room)
        sent_part = padded_to(rows_grad[:batch_rows].reshape(-1), token_room)
        stacked_grad = jnp.pad(
            flat_grad.reshape(2, tower_count, txt_share),
            ((0, 0), (0, 0), (0, shard_room - txt_share)),
        )
        return (own_part, sent_part, stacked_grad)

    own_part, sent_part, stacked_grad = lax.cond(
        is_image, image_backward, text_backward, (gathered, token_in, pair_cot)
    )
    summed = lax.psum_scatter(stacked_grad, "dp", scatter_dimension=1, tiled=True)
    kept_part = jnp.where(is_image, summed[0, 0], summed[1, 0])
    sent_share = jnp.where(is_image, summed[1, 0], summed[0, 0])
    home_weights, home_tokens = (
        from_partner(sent_share.astype(jnp.bfloat16), "tower", 0).astype(sent_share.dtype),
        from_partner(sent_part.astype(jnp.bfloat16), "tower", 0).astype(sent_part.dtype),
    )
    img_owned = jnp.where(is_image, kept_part, home_weights)
    txt_owned = jnp.where(is_image, home_weights, kept_part)[:txt_share]
    img_grad = jnp.where(is_image, own_part, home_tokens)[:img_count].reshape(img_tokens.shape)
    txt_grad = jnp.where(is_image, home_tokens, own_part).reshape(txt_tokens.shape)
    img_new = advance(img_master, img_moment, img_average, img_owned, step_rate)
    txt_new = advance(txt_master, txt_moment, txt_average, txt_owned, step_rate)
    scale_parts = advance(scale_state[0], scale_state[1], scale_state[2], sums[1], scale_rate)
    scale_new = jnp.stack([scale_parts[0], scale_parts[1], scale_parts[2]])
    return (
        sums[0] / total_rows,
        img_grad,
        txt_grad,
        img_new[0],
        img_new[1],
        img_new[2],
        img_new[0].astype(jnp.bfloat16),
        txt_new[0],
        txt_new[1],
        txt_new[2],
        txt_new[0].astype(jnp.bfloat16),
        scale_new,
    )


def solution(mesh):
    in_specs = (
        P(("tower", "dp"), None, None),
        P(("tower", "dp"), None, None),
        P(),
        P(("tower", "dp"), None),
        P(("tower", "dp")),
        P(("tower", "dp")),
        P(("tower", "dp")),
        P(("tower", "dp")),
        P(("tower", "dp")),
        P(("tower", "dp")),
        P(),
    )
    out_specs = (
        P(),
        P(("tower", "dp"), None, None),
        P(("tower", "dp"), None, None),
        P(("tower", "dp")),
        P(("tower", "dp")),
        P(("tower", "dp")),
        P(("tower", "dp")),
        P(("tower", "dp")),
        P(("tower", "dp")),
        P(("tower", "dp")),
        P(("tower", "dp")),
        P(),
    )
    run = step if (mesh.shape["tower"], mesh.shape["dp"]) == (2, 16) else body
    return jax.shard_map(run, mesh=mesh, in_specs=in_specs, out_specs=out_specs, check_vma=False)
```

```python
import functools
import math

import jax
import jax.numpy as jnp
from jax import lax
from jax.experimental import pallas as pl
from jax.experimental.pallas import tpu as pltpu
from jax.sharding import PartitionSpec as P

D_IMG = 768
FF_IMG = 3072
D_TXT = 512
FF_TXT = 2048
EMB = 512
HEAD = 64


momentum_rate = 0.5
average_rate = 0.5
step_rate = 0.08
scale_rate = 0.0001


MESH = pl.DeviceIdType.MESH
ANY = pl.BlockSpec(memory_space=pl.ANY)
GRANT = 58 * 1024 * 1024
LANES = 128
LOW = jnp.bfloat16
WIDE = jnp.float32


def here():
    return lax.axis_index("tower"), lax.axis_index("dp")


def greet(devices):
    barrier = pltpu.get_barrier_semaphore()
    for device in devices:
        pl.semaphore_signal(barrier, inc=1, device_id=device, device_id_type=MESH)
    pl.semaphore_wait(barrier, len(devices))


def remote(src, dst, send_sem, recv_sem, device):
    return pltpu.make_async_remote_copy(
        src_ref=src,
        dst_ref=dst,
        send_sem=send_sem,
        recv_sem=recv_sem,
        device_id=device,
        device_id_type=MESH,
    )


def comm_params(number):
    return pltpu.CompilerParams(
        collective_id=number, has_side_effects=True, vmem_limit_bytes=GRANT
    )


def same_core(tower, at):
    chip, core = at // 2, at % 2
    return [(tower, (chip + k) % 8 * 2 + core) for k in range(1, 8)]


def both_towers(tower, at):
    place, core = tower * 8 + at // 2, at % 2
    others = [(place + k) % 16 for k in range(1, 16)]
    return [(other // 8, other % 8 * 2 + core) for other in others]


def everyone(tower, at):
    me = tower * 16 + at
    others = [(me + k) % 32 for k in range(1, 32)]
    return [(other // 16, other % 16) for other in others]


def group_exchange(scattered, x_ref, o_ref, send_sem, recv_sem):
    tower, at = here()
    chip = at // 2

    def source(k):
        return x_ref.at[k] if scattered else x_ref

    own = pltpu.make_async_copy(source(chip), o_ref.at[chip], send_sem.at[7])
    sent = []
    for k, device in enumerate(same_core(tower, at)):
        copy = remote(
            source((chip + 1 + k) % 8), o_ref.at[chip], send_sem.at[k], recv_sem.at[k], device
        )
        copy.start()
        sent.append(copy)
    own.start()
    own.wait()
    for k in range(7):
        remote(
            source(chip),
            o_ref.at[(chip + 7 - k) % 8],
            send_sem.at[k],
            recv_sem.at[k],
            (tower, at),
        ).wait_recv()
    return sent


class Spread:
    def __init__(self, src, dst, send, recv):
        self.src, self.dst, self.send, self.recv = src, dst, send, recv
        tower, at = here()
        self.core = at % 2
        self.sibling = (tower, at + 1 - 2 * self.core)
        self.devices = self.peers(tower, at)
        self.n = len(self.devices) + 1
        self.place = self.spot(tower, at)
        self.sent = []

    def peers(self, tower, at):
        return both_towers(tower, at)

    def spot(self, tower, at):
        return tower * 8 + at // 2

    def block(self, place):
        return self.src

    def side(self, core):
        return self.dst.at[core]

    def launch(self, src, dst, k, device):
        copy = remote(src, dst, self.send.at[k], self.recv.at[k], device)
        copy.start()
        self.sent.append(copy)

    def start(self):
        for k, device in enumerate(self.devices):
            to = (self.place + 1 + k) % self.n
            self.launch(self.block(to), self.side(self.core).at[self.place], k, device)
        self.own = pltpu.make_async_copy(
            self.block(self.place), self.side(self.core).at[self.place], self.send.at[self.n]
        )
        self.own.start()

    def arrived(self):
        for k in range(self.n - 1):
            source = (self.place + self.n - 1 - k) % self.n
            remote(
                self.block(0),
                self.side(self.core).at[source],
                self.send.at[k],
                self.recv.at[k],
                self.sibling,
            ).wait_recv()
        self.own.wait()

    def relay(self):
        self.arrived()
        side = self.side(self.core)
        self.launch(side, side, self.n - 1, self.sibling)

    def finish(self):
        side = self.side(1 - self.core)
        remote(
            side, side, self.send.at[self.n - 1], self.recv.at[self.n - 1], self.sibling
        ).wait_recv()

    def drain(self):
        for copy in self.sent:
            copy.wait_send()


class Group(Spread):
    def __init__(self, src, dst, send, recv, both=True):
        self.both = both
        super().__init__(src, dst, send, recv)

    def peers(self, tower, at):
        return same_core(tower, at)

    def spot(self, tower, at):
        return at // 2

    def block(self, place):
        return self.src.at[place]

    def side(self, core):
        return self.dst.at[core] if self.both else self.dst

    def finish(self):
        if self.both:
            super().finish()
        else:
            self.arrived()


class Ring:
    def __init__(self, src, dst, send, recv, only=None, narrow=None):
        self.src, self.dst, self.send, self.recv = src, dst, send, recv
        self.only, self.narrow = only, narrow
        self.tower, self.at = here()
        self.deep, self.row, self.core = self.at // 4, self.at // 2 % 2, self.at % 2
        self.sibling = (self.tower, self.at + 1 - 2 * self.core)
        self.beside = (self.tower, self.spot(0, 1 - self.row))
        self.sent = []

    def spot(self, k, row):
        return (self.deep + k) % 4 * 4 + row * 2 + self.core

    def forms(self, make):
        def whole(block):
            return block

        def part(block):
            return block.at[:, pl.ds(0, self.narrow)]

        if self.only is not None:
            return [(self.tower == self.only, make(whole))]
        if self.narrow is None:
            return [(None, make(whole))]
        return [(self.tower == 0, make(whole)), (self.tower == 1, make(part))]

    def act(self, forms, name):
        for when, copy in forms:
            action = getattr(copy, name)
            if when is None:
                action()
            else:
                pl.when(when)(action)

    def remote(self, src, slot, sent, landed, device):
        return self.forms(
            lambda cut: remote(
                cut(src), cut(self.dst.at[slot]), self.send.at[sent], self.recv.at[landed], device
            )
        )

    def launch(self, src, slot, index, device):
        forms = self.remote(src, slot, index, index, device)
        self.act(forms, "start")
        self.sent.append(forms)

    def arrived(self, slot, index):
        self.act(self.remote(self.src, slot, index, index, self.sibling), "wait_recv")

    def start(self):
        for k in (1, 3, 2):
            self.launch(self.src, self.at, k - 1, (self.tower, self.spot(k, self.row)))
        self.launch(self.src, self.at, 3, self.beside)
        self.launch(self.src, self.at, 7, self.sibling)
        self.own = self.forms(
            lambda cut: pltpu.make_async_copy(
                cut(self.src), cut(self.dst.at[self.at]), self.send.at[15]
            )
        )
        self.act(self.own, "start")

    def relay_deep(self):
        for k in (1, 3, 2):
            slot = self.spot(4 - k, self.row)
            self.arrived(slot, k - 1)
            self.launch(self.dst.at[slot], slot, 3 + k, self.beside)
            self.launch(self.dst.at[slot], slot, 7 + k, self.sibling)

    def relay_row(self):
        for k in (0, 1, 3, 2):
            slot = self.spot(4 - k, 1 - self.row)
            self.arrived(slot, 3 + k)
            self.launch(self.dst.at[slot], slot, 11 + k, self.sibling)

    def finish(self):
        for index in range(8):
            k, row = index % 4, self.row if index < 4 else 1 - self.row
            slot = (self.deep + 4 - k) % 4 * 4 + row * 2 + 1 - self.core
            self.arrived(slot, 7 + index)
        self.act(self.own, "wait")

    def drain(self):
        for forms in self.sent:
            self.act(forms, "wait_send")


class Chain:
    def __init__(self, src, dst, send, recv, only=None):
        self.src, self.dst, self.send, self.recv = src, dst, send, recv
        self.only = only
        self.tower, self.at = here()
        self.deep, self.row, self.core = self.at // 4, self.at // 2 % 2, self.at % 2
        self.mate = self.deep + 1 - 2 * (self.deep % 2)
        self.half = self.deep // 2
        self.inner = jnp.logical_or(self.deep == 1, self.deep == 2)
        self.sibling = (self.tower, self.at + 1 - 2 * self.core)
        self.beside = (self.tower, self.spot(self.deep, 1 - self.row))
        self.sent = []

    def spot(self, deep, row):
        return deep * 4 + row * 2 + self.core

    def sources(self):
        return self.deep, self.mate, 2 - 2 * self.half, 3 - 2 * self.half

    def act(self, action, when=None):
        if self.only is not None:
            right = self.tower == self.only
            when = right if when is None else jnp.logical_and(when, right)
        if when is None:
            action()
        else:
            pl.when(when)(action)

    def launch(self, src, slot, sent, landed, device, when=None):
        copy = remote(src, self.dst.at[slot], self.send.at[sent], self.recv.at[landed], device)
        self.act(copy.start, when)
        self.sent.append((copy, when))

    def arrived(self, slot, index):
        copy = remote(
            self.src, self.dst.at[slot], self.send.at[0], self.recv.at[index], self.sibling
        )
        self.act(copy.wait_recv)

    def start(self):
        mate = (self.tower, self.spot(self.mate, self.row))
        far = (self.tower, self.spot(2 - self.half, self.row))
        self.launch(self.src, self.at, 1, 1 + self.deep % 2, far)
        self.launch(self.src, self.at, 0, 0, mate)
        self.launch(self.src, self.at, 2, 3, self.beside)
        self.launch(self.src, self.at, 3, 7, self.sibling)
        self.own = pltpu.make_async_copy(self.src, self.dst.at[self.at], self.send.at[16])
        self.act(self.own.start)

    def relay_deep(self):
        mate = (self.tower, self.spot(self.mate, self.row))
        for k in (1, 2, 3):
            slot = self.spot(self.sources()[k], self.row)
            self.arrived(slot, k - 1)
            block = self.dst.at[slot]
            if k > 1:
                self.launch(block, slot, 4 + k, k - 1, mate, self.inner)
            self.launch(block, slot, 7 + k, 3 + k, self.beside)
            self.launch(block, slot, 16 + k, 7 + k, self.sibling)

    def relay_row(self):
        for k, deep in enumerate(self.sources()):
            slot = self.spot(deep, 1 - self.row)
            self.arrived(slot, 3 + k)
            self.launch(self.dst.at[slot], slot, 11 + k, 11 + k, self.sibling)

    def finish(self):
        for k, deep in enumerate(self.sources()):
            for row, base in ((self.row, 7), (1 - self.row, 11)):
                self.arrived(deep * 4 + row * 2 + 1 - self.core, base + k)
        self.act(self.own.wait)

    def drain(self):
        for copy, when in self.sent:
            self.act(copy.wait_send, when)


class Plane:
    def __init__(self, src, via, dst, send, recv):
        self.src, self.via, self.dst, self.send, self.recv = src, via, dst, send, recv
        self.tower, self.at = here()
        self.deep, self.row, self.core = self.at // 4, self.at // 2 % 2, self.at % 2
        self.partner = (1 - self.tower, self.at)
        self.sibling = (self.tower, self.at + 1 - 2 * self.core)
        self.beside = (self.tower, self.at + 2 - 4 * self.row)
        self.sent = []

    def spot(self, k, row):
        return (self.deep + k) % 4 * 2 + row

    def launch(self, src, slot, index, device):
        copy = remote(src, self.via.at[slot], self.send.at[index], self.recv.at[index], device)
        pl.when(self.tower == 1)(copy.start)
        self.sent.append(copy)

    def arrived(self, slot, index):
        copy = remote(
            self.src, self.via.at[slot], self.send.at[index], self.recv.at[index], self.sibling
        )
        pl.when(self.tower == 1)(copy.wait_recv)

    def start(self):
        own = self.spot(0, self.row)
        for k in (1, 3, 2):
            there = self.spot(k, self.row) * 2 + self.core
            self.launch(self.src, own, k - 1, (self.tower, there))
        self.launch(self.src, own, 3, self.beside)
        self.own = pltpu.make_async_copy(self.src, self.via.at[own], self.send.at[7])
        pl.when(self.tower == 1)(self.own.start)

    def relay_deep(self):
        for k in (1, 3, 2):
            slot = self.spot(4 - k, self.row)
            self.arrived(slot, k - 1)
            self.launch(self.via.at[slot], slot, 3 + k, self.beside)

    def relay_row(self):
        for k in range(4):
            self.arrived(self.spot(4 - k, 1 - self.row), 3 + k)
        pl.when(self.tower == 1)(self.own.wait)
        pl.when(self.tower == 1)(self.down().start)

    def down(self):
        return remote(
            self.via, self.dst.at[self.core], self.send.at[8], self.recv.at[7], self.partner
        )

    def across(self, core):
        return remote(
            self.dst.at[core], self.dst.at[core], self.send.at[9], self.recv.at[8], self.sibling
        )

    def land(self):
        pl.when(self.tower == 0)(self.down().wait_recv)
        pl.when(self.tower == 0)(self.across(self.core).start)

    def finish(self):
        pl.when(self.tower == 0)(self.across(1 - self.core).wait_recv)

    def drain(self):
        for copy in self.sent:
            pl.when(self.tower == 1)(copy.wait_send)
        pl.when(self.tower == 1)(self.down().wait_send)
        pl.when(self.tower == 0)(self.across(self.core).wait_send)


def rings(src, dst, send, recv, way=Ring, *narrow):
    return [
        way(
            src.at[part],
            dst.at[part],
            send.at[part],
            recv.at[part],
            0 if part == 2 else None,
            *narrow,
        )
        for part in range(3)
    ]


class Blocks:
    def __init__(self, src, dst, send, recv, shared=1):
        self.src, self.dst, self.send, self.recv = src, dst, send, recv
        self.tower, self.at = here()
        self.shared = shared
        self.sent = []

    def start(self):
        for k in range(1, 16):
            to = (self.at + k) % 16
            copy = remote(
                self.src.at[to // self.shared],
                self.dst.at[self.at],
                self.send.at[k - 1],
                self.recv.at[k - 1],
                (self.tower, to),
            )
            copy.start()
            self.sent.append(copy)
        self.own = pltpu.make_async_copy(
            self.src.at[self.at // self.shared], self.dst.at[self.at], self.send.at[15]
        )
        self.own.start()

    def finish(self):
        for k in range(1, 16):
            remote(
                self.src.at[0],
                self.dst.at[(self.at + 16 - k) % 16],
                self.send.at[k - 1],
                self.recv.at[k - 1],
                (self.tower, self.at),
            ).wait_recv()
        self.own.wait()

    def drain(self):
        for copy in self.sent:
            copy.wait_send()


class Pair:
    def __init__(self, from_zero, zero_dst, from_one, one_dst, sems):
        tower, at = here()
        partner = (1 - tower, at)
        self.tower = tower
        self.up = remote(from_zero, zero_dst, sems.at[0], sems.at[1], partner)
        self.down = remote(from_one, one_dst, sems.at[0], sems.at[1], partner)

    def by_tower(self, zero, one):
        pl.when(self.tower == 0)(zero)
        pl.when(self.tower == 1)(one)

    def start(self):
        self.by_tower(self.up.start, self.down.start)

    def finish(self):
        self.by_tower(self.down.wait_recv, self.up.wait_recv)

    def drain(self):
        self.by_tower(self.up.wait_send, self.down.wait_send)


VECTORS = 5
EXPAND = 2
EMBED = 4
TURN = 8


class Plan:
    def __init__(self, tower, share, rows, per_device):
        self.tower = tower
        self.share = share
        self.rows = rows
        self.chunk = rows * LANES
        self.per_device = per_device
        self.first_slot = [sum(per_device[:p]) for p in range(6)]
        self.first_chunk = [16 * slot for slot in self.first_slot]
        self.slots = sum(per_device) + 1
        self.total = 16 * sum(per_device) + 1
        spans = [self.span(device) for device in range(32)]
        self.counts = sorted({last - first + 1 for first, last in spans})
        self.local = self.counts[-1]

    def span(self, device):
        first = device * self.share // self.chunk
        last = ((device + 1) * self.share - 1) // self.chunk
        return first, min(last, self.total - 1)

    def bounds(self, device):
        first = device * self.share // self.chunk
        last = ((device + 1) * self.share - 1) // self.chunk
        return first, jnp.minimum(last, self.total - 1)

    def pieces(self, p):
        return self.per_device[p] if p < VECTORS else 1

    def target(self, g):
        piece, base, slot, n = (jnp.int32(0), jnp.int32(0), jnp.int32(0), jnp.int32(1))
        for p in range(VECTORS):
            inside = g >= self.first_chunk[p]
            piece = jnp.where(inside, p, piece)
            base = jnp.where(inside, self.first_chunk[p], base)
            slot = jnp.where(inside, self.first_slot[p], slot)
            n = jnp.where(inside, self.per_device[p], n)
        block = (g - base) // n
        at = jnp.where(piece == EXPAND, (block + TURN) % 16, block)
        return piece, at, slot + (g - base) - block * n


def before(me):
    device = (me + 31) % 32
    return device // 16, device % 16


class Deal:
    def __init__(self, plan, s, src, dst, extra, last, sems, only=None, me=None):
        self.plan, self.s, self.src, self.dst = plan, s, src, dst
        self.extra, self.last = extra, last
        self.chunk_send, self.recv, self.edge, self.fetch = sems
        self.tower, self.at = here()
        self.only = only
        self.me = self.tower * 16 + self.at if me is None else me
        self.first, self.last_chunk = plan.bounds(self.me)

    def runs(self, condition):
        return condition if self.only is None else jnp.logical_and(condition, self.tower == self.only)

    def move(self, src, i, piece, at_to, slot, wait):
        tower_to = self.plan.tower
        if not isinstance(piece, int):
            tower_to = jnp.where(piece == EMBED, 1, tower_to)
        far = jnp.logical_or(self.tower != tower_to, at_to != self.at)
        recv = self.recv.at[self.plan.tower, piece]
        copy = remote(
            src,
            self.dst.at[slot],
            self.chunk_send.at[self.s, i],
            recv,
            (tower_to, at_to),
        )
        pl.when(far)(copy.wait_send if wait else copy.start)
        if not wait:
            pl.when(jnp.logical_not(far))(
                pltpu.make_async_copy(src, self.dst.at[slot], recv).start
            )

    def whole(self, early, wait):
        def step(i, carry):
            g = self.first + i
            piece, at_to, slot = self.plan.target(g)
            inside = jnp.logical_and(
                jnp.logical_or(i > 0, self.me == 0),
                jnp.logical_or(
                    g < self.last_chunk, jnp.logical_and(self.me == 31, g < self.plan.total - 1)
                ),
            )
            inside = jnp.logical_and(inside, g <= self.last_chunk)
            inside = jnp.logical_and(inside, g < self.plan.total - 1)
            if early is not None:
                hidden = jnp.logical_and(piece >= 2, piece <= 3)
                inside = jnp.logical_and(inside, jnp.logical_not(hidden) if early else hidden)

            @pl.when(self.runs(inside))
            def _():
                self.move(self.src.at[i], i, piece, at_to, slot, wait)

            return carry

        lax.fori_loop(0, self.plan.local, step, 0)

    def vectors(self, wait):
        @pl.when(self.runs(self.me == 31))
        def _():
            src = self.src.at[self.last_chunk - self.first]

            def each(k, carry):
                self.move(src, self.plan.local + k, VECTORS, k, self.plan.slots - 1, wait)
                return carry

            lax.fori_loop(0, 16, each, 0)

    def fetch_last(self):
        return pltpu.make_async_copy(
            self.src.at[self.last_chunk - self.first], self.last, self.fetch.at[self.s]
        )

    def join(self):
        @pl.when(self.runs(self.me < 31))
        def _():
            self.fetch_last().wait()
            edge = self.edge
            remote(
                self.last,
                self.extra,
                edge.at[self.s, 0],
                edge.at[self.s, 1],
                (self.tower, self.at),
            ).wait_recv()
            self.last[...] = self.last[...] + self.extra[...]
            piece, at_to, slot = self.plan.target(self.last_chunk)
            self.move(self.last, self.plan.local + 16, piece, at_to, slot, False)

    def start_fetch(self):
        pl.when(self.runs(self.me < 31))(self.fetch_last().start)

    def arrived(self, p):
        part = self.dst.at[pl.ds(self.plan.first_slot[p], self.plan.pieces(p))]
        pltpu.make_async_copy(part, part, self.recv.at[self.plan.tower, p]).wait()

    def drain(self):
        self.whole(None, True)
        self.vectors(True)

        @pl.when(self.runs(self.me < 31))
        def _():
            piece, at_to, slot = self.plan.target(self.last_chunk)
            self.move(self.last, self.plan.local + 16, piece, at_to, slot, True)


class Collect:
    def __init__(self, plan, s, src, dst, send, recv):
        self.plan, self.s, self.src, self.dst = plan, s, src, dst
        self.send, self.recv = send, recv
        self.tower, self.at = here()
        self.me = self.tower * 16 + self.at

    def one(self, owner, slot, g, which, wait):
        first, _ = self.plan.bounds(owner)
        far = owner != self.me
        recv = self.recv.at[self.s]
        copy = remote(
            self.src.at[slot],
            self.dst.at[g - first],
            self.send.at[which, slot],
            recv,
            (owner // 16, owner % 16),
        )
        pl.when(far)(copy.wait_send if wait else copy.start)
        if not wait:
            pl.when(jnp.logical_not(far))(
                pltpu.make_async_copy(self.src.at[slot], self.dst.at[g - first], recv).start
            )

    def piece(self, p, wait):
        n = self.plan.pieces(p)

        def step(i, carry):
            slot = self.plan.first_slot[p] + i
            block = (self.at + 16 - TURN) % 16 if p == EXPAND else self.at
            g = self.plan.first_chunk[p] + block * n + i if p < VECTORS else self.plan.total - 1
            low = g * self.plan.chunk // self.plan.share
            high = jnp.minimum(((g + 1) * self.plan.chunk - 1) // self.plan.share, 31)
            self.one(low, slot, g, 0, wait)
            pl.when(high != low)(lambda: self.one(high, slot, g, 1, wait))
            return carry

        if p == VECTORS:


            @pl.when(self.at == 0)
            def _():
                step(0, 0)

        else:
            lax.fori_loop(0, n, step, 0)

    def finish(self):
        first, last = self.plan.bounds(self.me)
        held = last - first + 1
        for n in self.plan.counts:

            @pl.when(held == n)
            def _():
                part = self.dst.at[pl.ds(0, n)]
                pltpu.make_async_copy(part, part, self.recv.at[self.s]).wait()


SEQS = 16
HEADS = 16


class Tower:
    def __init__(self, index, width, hidden, length, room, run, causal):
        self.index = index
        self.width = width
        self.hidden = hidden
        self.length = length
        self.room = room
        self.run = run
        self.causal = causal
        self.heads = width // HEAD
        self.block = width // 16
        self.part = hidden // 8
        self.reduce_rows = hidden // 16


TOWERS = (
    Tower(0, D_IMG, FF_IMG, 50, 64, 10, False),
    Tower(1, D_TXT, FF_TXT, 77, 80, 11, True),
)
ROOM = 80
WIDTH = D_IMG
PART = FF_IMG // 8


def each_tower(run):
    tower = lax.axis_index("tower")
    for kind in TOWERS:
        pl.when(tower == kind.index)(functools.partial(run, kind))


def dot_nn(a, b):
    return lax.dot_general(a, b, (((1,), (0,)), ((), ())), preferred_element_type=WIDE)


def dot_nt(a, b):
    return lax.dot_general(a, b, (((1,), (1,)), ((), ())), preferred_element_type=WIDE)


def dot_tn(a, b):
    return lax.dot_general(a, b, (((0,), (0,)), ((), ())), preferred_element_type=WIDE)


def standardise(rows):
    centred = rows - jnp.mean(rows, axis=-1, keepdims=True)
    spread = jnp.mean(centred * centred, axis=-1, keepdims=True)
    rate = lax.rsqrt(spread + 1e-05)
    return centred * rate, rate


def norm_back(grad, gain, hat, rate):
    scaled = grad * gain
    return rate * (
        scaled
        - jnp.mean(scaled, axis=-1, keepdims=True)
        - hat * jnp.mean(scaled * hat, axis=-1, keepdims=True)
    )


def spans(kind):
    return [
        (lo, min(lo + 512, kind.width), lo // HEAD, (min(lo + 512, kind.width) - lo) // HEAD)
        for lo in range(0, kind.width, 512)
    ]


def head_rows(rows, span):
    lo, hi, _, n = span
    part = rows[:, lo:hi]
    owner = lax.broadcasted_iota(jnp.int32, part.shape, 1) // HEAD
    nothing = jnp.zeros_like(part)
    return jnp.concatenate([jnp.where(owner == h, part, nothing) for h in range(n)], axis=0)


def from_head_rows(rows, span):
    _, _, _, n = span
    owner = lax.broadcasted_iota(jnp.int32, (SEQS, rows.shape[1]), 1) // HEAD
    total = jnp.zeros((SEQS, rows.shape[1]), rows.dtype)
    for h in range(n):
        total = jnp.where(owner == h, rows[h * SEQS : (h + 1) * SEQS], total)
    return total


def side_by_side(parts):
    return parts[0] if len(parts) == 1 else jnp.concatenate(parts, axis=1)


def get_rows(ref, place, width):
    return side_by_side([ref[c, place, :] for c in range(width // LANES)])


def put_rows(ref, place, value):
    for c in range(value.shape[1] // LANES):
        ref[c, place, :] = value[:, c * LANES : (c + 1) * LANES]


def matrix(ref, kind, start, width):
    return jnp.concatenate(
        [
            ref[part, at, :, start : start + width]
            for at in range(16)
            for part in range(kind.block // 16)
        ],
        axis=0,
    )


def embed_matrix(refs, kind):
    if kind.index == 1:
        return matrix(refs[1], kind, 0, EMB)
    return jnp.concatenate([refs[0][at % 2, at // 2] for at in range(16)], axis=0)


def vector(vec_ref, kind, row):
    return vec_ref[row : row + 1, : kind.width]


def pieces_of(kind):
    return (
        (kind.block, 3 * kind.width),
        (kind.block, kind.width),
        (kind.block, kind.hidden),
        (kind.reduce_rows, kind.width),
        (kind.block, EMB),
        (16, kind.width),
    )


def lane_blocks(kind, plan, p):
    height, width = pieces_of(kind)[p]
    pitch = width // LANES
    base = plan.first_slot[p] * plan.rows if p < VECTORS else (plan.slots - 1) * plan.rows
    return [(c, pl.ds(base + c, height, stride=pitch)) for c in range(pitch)]


def lift(kind, plan, p, slots, flat):
    n = plan.pieces(p)
    slot = plan.first_slot[p]
    rows = slots[slot : slot + n].reshape(n * plan.rows, LANES)
    flat[slot * plan.rows : (slot + n) * plan.rows, :] = rows.astype(WIDE)
    return [(c, flat[place, :]) for c, place in lane_blocks(kind, plan, p)]


def drop(kind, plan, p, value, slots, flat):
    for c, place in lane_blocks(kind, plan, p):
        flat[place, :] = value(c)
    n = plan.pieces(p)
    slot = plan.first_slot[p]
    rows = flat[slot * plan.rows : (slot + n) * plan.rows, :]
    slots[slot : slot + n] = rows.reshape(n, plan.rows, LANES).astype(LOW)


def expand_matrix(ref, kind):
    return jnp.concatenate(
        [
            ref[at % 2, at // 2, : kind.block, : kind.part]
            for at in ((block + TURN) % 16 for block in range(16))
        ],
        axis=0,
    )


def reduce_matrix(ref, kind):
    return ref[:, : kind.reduce_rows, : kind.width].reshape(kind.part, kind.width)


def hidden_bias(vec_ref, kind):
    chip = lax.axis_index("dp") // 2
    whole = vec_ref[...]
    row = lax.broadcasted_iota(jnp.int32, (16, 1), 0)
    line = jnp.sum(jnp.where(row == 10 + chip // 2, whole, 0.0), axis=0, keepdims=True)
    return jnp.where(
        chip % 2 == 0, line[:, : kind.part], line[:, kind.part : 2 * kind.part]
    )


def hidden_kernel(second_ref, raise_ref, reduce_ref, vec_ref, part_ref, raised_ref):
    def run(kind):
        width = kind.width
        rows = second_ref[:, :, :width].reshape(8 * SEQS, width)
        raised = dot_nn(rows, expand_matrix(raise_ref, kind)) + hidden_bias(vec_ref, kind)
        raised_ref[:, : kind.part] = raised
        active = (raised * jax.nn.sigmoid(1.702 * raised)).astype(LOW)
        part = dot_nn(active, reduce_matrix(reduce_ref, kind))
        part_ref[:, :, :width] = part.reshape(8, SEQS, width).astype(LOW)

    each_tower(run)


def hidden_back_kernel(
    grad_ref,
    second_ref,
    raised_ref,
    raise_ref,
    reduce_ref,
    back_ref,
    raise_grad_ref,
    reduce_keep_ref,
    reduce_send_ref,
    bias_ref,
    whole,
):
    def run(kind):
        width, part = kind.width, kind.part
        grads = grad_ref[:, :, :width].reshape(8 * SEQS, width)
        rows = second_ref[:, :, :width].reshape(8 * SEQS, width)
        raised = raised_ref[:, :part]
        gate = jax.nn.sigmoid(1.702 * raised)
        active = (raised * gate).astype(LOW)
        slope = gate + 1.702 * raised * gate * (1.0 - gate)
        raised_grad = dot_nt(grads, reduce_matrix(reduce_ref, kind)) * slope
        low_grad = raised_grad.astype(LOW)
        bias_ref[0:1, :part] = jnp.sum(low_grad.astype(WIDE), axis=0, keepdims=True)
        back = dot_nt(low_grad, expand_matrix(raise_ref, kind))
        back_ref[:, :, :width] = back.reshape(8, SEQS, width).astype(LOW)
        raise_grad = dot_tn(rows, low_grad).reshape(16, kind.block, part).astype(LOW)
        for block in range(16):
            at = (block + TURN) % 16
            raise_grad_ref[at % 2, at // 2, : kind.block, :part] = raise_grad[block]
        whole[:part, :width] = dot_tn(active, grads)
        core = lax.axis_index("dp") % 2
        n = kind.reduce_rows
        keep = pl.multiple_of(core * n, 64)
        send = pl.multiple_of((1 - core) * n, 64)
        reduce_keep_ref[:n, :width] = whole[pl.ds(keep, n), :width]
        reduce_send_ref[:n, :width] = whole[pl.ds(send, n), :width].astype(LOW)

    each_tower(run)


def embed_kernel(part_ref, middle_ref, gat_ref, vec_ref, emb_ref, final_ref, pooled_ref, proj_ref):
    def run(kind):
        width = kind.width
        final = (
            middle_ref[:, :width]
            + jnp.sum(part_ref[:, :, :width].astype(WIDE), axis=0)
            + vector(vec_ref, kind, 7)
        )
        final_ref[:, :width] = final
        hat, _ = standardise(final)
        pooled = (hat * vector(vec_ref, kind, 8) + vector(vec_ref, kind, 9)).astype(LOW)
        pooled_ref[:, :width] = pooled
        proj = dot_nn(pooled, embed_matrix(gat_ref, kind))
        proj_ref[...] = proj
        size = jnp.sum(proj * proj, axis=-1, keepdims=True) + 1e-06
        emb_ref[...] = (proj * lax.rsqrt(size)).astype(LOW)

    each_tower(run)


def objective_kernel(
    scale_ref,
    all_ref,
    valid_ref,
    final_ref,
    proj_ref,
    gat_ref,
    vec_ref,
    low_ref,
    grad_ref,
    proj_grad_ref,
    final_vec_ref,
    loss_ref,
    scale_new_ref,
    own_scr,
):
    def ordered(which):
        blocks = []
        for half in range(2):
            for j in range(16):
                rows = all_ref[j % 2, which * 8 + j // 2].astype(WIDE)
                blocks.append(rows[half * 8 : half * 8 + 8])
        return jnp.concatenate(blocks, axis=0).astype(LOW)

    img, txt = ordered(0), ordered(1)
    total = img.shape[0]
    scale = jnp.exp(jnp.full((1, 1), scale_ref[0], WIDE))
    lines = []
    for d in range(32):
        rows = valid_ref[d % 2, d // 2].astype(WIDE)
        lines.append(jnp.concatenate([rows[:8], rows[8:]], axis=1))
    allowed = jnp.concatenate(lines, axis=0) > 0
    same = lax.broadcasted_iota(jnp.int32, (total, total), 0) == lax.broadcasted_iota(
        jnp.int32, (total, total), 1
    )
    same = same.astype(WIDE)

    def side(left, right):
        logits = scale * dot_nt(left, right)
        masked = jnp.where(allowed, logits, -1e30)
        top = jnp.max(masked, axis=1, keepdims=True)
        lse = jnp.log(jnp.sum(jnp.exp(masked - top), axis=1, keepdims=True)) + top
        terms = 0.5 * (jnp.where(allowed, jnp.exp(logits - lse), 0.0) - same)
        loss = 0.5 * (
            jnp.sum(lse, axis=0, keepdims=True)
            - jnp.sum(jnp.sum(logits * same, axis=1, keepdims=True), axis=0, keepdims=True)
        )
        rate = jnp.sum(jnp.sum(terms * logits, axis=1, keepdims=True), axis=0, keepdims=True)
        return (scale * terms).astype(LOW), loss, rate

    row_back, row_loss, row_rate = side(img, txt)
    col_back, col_loss, col_rate = side(txt, img)
    loss_ref[0] = jnp.sum(row_loss + col_loss) / total
    parts = advance(
        scale_ref[0], scale_ref[1], scale_ref[2], jnp.sum(row_rate + col_rate), scale_rate
    )
    for k in range(3):
        scale_new_ref[k] = parts[k]

    def run(kind):
        width = kind.width
        if kind.index == 0:
            emb_grad = dot_nn(row_back, txt) + dot_tn(col_back, txt)
        else:
            emb_grad = dot_nn(col_back, img) + dot_tn(row_back, img)
        own_scr[...] = emb_grad
        at = lax.axis_index("dp")
        mine = jnp.concatenate(
            [
                own_scr[pl.ds(pl.multiple_of(half * 128 + at * 8, 8), 8), :]
                for half in range(2)
            ],
            axis=0,
        )
        proj = proj_ref[...]
        size = jnp.sum(proj * proj, axis=-1, keepdims=True) + 1e-06
        along = jnp.sum(proj * mine, axis=-1, keepdims=True)
        proj_grad = ((mine - proj * along / size) * lax.rsqrt(size)).astype(LOW)
        proj_grad_ref[...] = proj_grad
        pooled_grad = dot_nt(proj_grad, embed_matrix(gat_ref, kind))
        hat, rate = standardise(final_ref[:, :width])
        final_vec_ref[0:1, :width] = jnp.sum(pooled_grad * hat, axis=0, keepdims=True)
        final_vec_ref[1:2, :width] = jnp.sum(pooled_grad, axis=0, keepdims=True)
        final_grad = norm_back(pooled_grad, vector(vec_ref, kind, 8), hat, rate)
        grad_ref[:, :width] = final_grad
        low = final_grad.astype(LOW)
        low_ref[:, :width] = low
        final_vec_ref[2:3, :width] = jnp.sum(low.astype(WIDE), axis=0, keepdims=True)

    each_tower(run)


def step_kernel(
    plans,
    ends_ref,
    scale_ref,
    img_src,
    txt_src,
    valid_ref,
    img_own,
    txt_own,
    loss_ref,
    scale_new_ref,
    img_keep,
    txt_keep,
    img_chunks,
    txt_chunks,
    second_ref,
    middle_ref,
    query_ref,
    keyed_ref,
    mixture_ref,
    weight_ref,
    first_ref,
    first_rows,
    img_in,
    txt_in,
    ask_ref,
    mix_ref,
    emb_ref,
    vec_ref,
    raise_ref,
    reduce_ref,
    pairs_ref,
    img_slots,
    txt_slots,
    img_extra,
    txt_extra,
    img_last,
    txt_last,
    txt_relay,
    txt_over,
    txt_ending,
    flat,
    ask_block,
    mix_block,
    emb_block,
    plane_block,
    plane_via,
    plane_ref,
    raise_block,
    reduce_block,
    mask_block,
    top_scr,
    at_scr,
    score_scr,
    low_scr,
    grad_ref,
    pooled_ref,
    proj_grad_ref,
    final_vec_ref,
    raise_grad_ref,
    reduce_keep_ref,
    reduce_send_ref,
    bias_ref,
    backs_ref,
    seconds,
    part,
    parts,
    raised,
    emb,
    all_embs,
    final,
    proj,
    low,
    lows,
    back,
    own_scr,
    whole,
    img_send,
    txt_send,
    img_home,
    txt_home,
    rows_grad,
    middle_scr,
    second_scr,
    valued_scr,
    turn_scr,
    shared_scr,
    slope_scr,
    left_scr,
    left_block,
    turn_block,
    left_all,
    turn_all,
    early_block,
    early_all,
    late_block,
    late_all,
    lines_block,
    lines_all,
    raise_half,
    risen_block,
    raise_all,
    reduce_in,
    img_home_slots,
    txt_home_slots,
    gains,
    top_grad_scr,
    deal_send,
    deal_recv,
    deal_edge,
    deal_fetch,
    relay_sems,
    ask_send,
    ask_recv,
    mix_send,
    mix_recv,
    emb_send,
    emb_recv,
    plane_send,
    plane_recv,
    raise_send,
    raise_recv,
    reduce_sems,
    pair_sems,
    mask_send,
    mask_recv,
    group_send,
    group_recv,
    embs_send,
    embs_recv,
    home_sems,
    risen_send,
    risen_recv,
    left_send,
    left_recv,
    turn_send,
    turn_recv,
    early_send,
    early_recv,
    late_send,
    late_recv,
    lines_send,
    lines_recv,
    home_pair_sems,
    collect_send,
    collect_recv,
):
    tower, at = here()
    core = at % 2
    me = tower * 16 + at
    sibling = (tower, at + 1 - 2 * core)
    greet(everyone(tower, at))
    deal_sems = (deal_send, deal_recv, deal_edge, deal_fetch)
    deals = [
        Deal(plans[0], 0, img_src, img_slots, img_extra, img_last, deal_sems),
        Deal(plans[1], 1, txt_src, txt_slots, txt_extra, txt_last, deal_sems, 1, 16 + at),
        Deal(plans[1], 2, txt_relay, txt_slots, txt_over, txt_ending, deal_sems, 1, at),
    ]
    relay = remote(txt_src, txt_relay, relay_sems.at[0], relay_sems.at[1], (1 - tower, at))
    behind = (jnp.int32(1), (at + 15) % 16)
    head = remote(img_src.at[0], img_extra, deal_edge.at[0, 0], deal_edge.at[0, 1], before(me))
    kept = remote(txt_src.at[0], txt_extra, deal_edge.at[1, 0], deal_edge.at[1, 1], behind)
    over = remote(txt_src.at[0], txt_over, deal_edge.at[2, 0], deal_edge.at[2, 1], behind)
    heads = (
        (me > 0, head),
        (me > 16, kept),
        (jnp.logical_and(me > 0, me <= 16), over),
    )
    pair = Pair(txt_own, txt_in, img_own, img_in, pair_sems)
    asks = rings(ask_block, ask_ref, ask_send, ask_recv, Ring, 2 * D_TXT)
    mixes = rings(mix_block, mix_ref, mix_send, mix_recv, Ring, 2 * D_TXT)
    embeds = [
        Chain(emb_block.at[part], emb_ref.at[part], emb_send.at[part], emb_recv.at[part], 1)
        for part in range(2)
    ]
    plane = Plane(plane_block, plane_via, plane_ref, plane_send, plane_recv)
    rise = Group(raise_block, raise_ref, raise_send, raise_recv)
    fall = remote(
        reduce_block, reduce_ref.at[core], reduce_sems.at[0], reduce_sems.at[1], sibling
    )
    fall_own = pltpu.make_async_copy(reduce_block, reduce_ref.at[core], reduce_sems.at[2])
    masks = Spread(mask_block, pairs_ref, mask_send, mask_recv)
    rows = valid_ref[...].astype(WIDE)
    mask_block[...] = jnp.concatenate([rows[:, :LANES], rows[:, LANES:]], axis=0).astype(LOW)

    for when, copy in heads:
        pl.when(when)(copy.start)
    pl.when(tower == 0)(relay.start)
    for deal in deals[:2]:
        deal.start_fetch()
        deal.vectors(False)
    deals[0].whole(True, False)
    deals[1].whole(True, False)
    deals[0].whole(False, False)
    deals[1].whole(False, False)
    pair.start()
    deals[0].join()
    deals[1].join()
    pl.when(tower == 1)(relay.wait_recv)
    deals[2].start_fetch()
    deals[2].whole(True, False)
    deals[2].join()
    deals[2].whole(False, False)

    def put(ref, lane, value):
        if len(ref.shape) == 2:
            ref[: value.shape[0], lane : lane + LANES] = value
        else:
            for part in range(value.shape[0] // 16):
                ref[part, :, lane : lane + LANES] = value[part * 16 : (part + 1) * 16]

    def lift_to(kind, p, ref, start):
        slots = (img_slots, txt_slots)[kind.index]
        for c, value in lift(kind, plans[kind.index], p, slots, flat):
            lane = start + c * LANES
            put(ref, lane, value.astype(ref.dtype))

    def tokens_of(kind, half):
        own, arrived = ((img_own, img_in), (txt_own, txt_in))[kind.index]
        return own if half == kind.index else arrived

    def steps(kind):
        return [(t, kind.run) for t in range(0, kind.length, kind.run)]

    def is_end(kind, half, t, n):
        row = lax.broadcasted_iota(jnp.int32, (8, 1), 0)
        ends = jnp.zeros((8, 1), jnp.int32)
        for i in range(8):
            ends = jnp.where(row == i, ends_ref[(half * 16 + at) * 8 + i], ends)
        position = lax.broadcasted_iota(jnp.int32, (n, 8, 1), 0) + t
        return (position == ends[None]).astype(WIDE)

    def normalise(kind, half):
        width, room = kind.width, kind.room
        ref = tokens_of(kind, half)
        gain, shift = vector(vec_ref, kind, 0), vector(vec_ref, kind, 1)
        tops, raws = jnp.zeros((8, width), WIDE), jnp.zeros((8, width), WIDE)
        for t, n in steps(kind):
            rows = ref[t : t + n].astype(WIDE).reshape(n * 8, width)
            hat, _ = standardise(rows)
            first = (hat * gain + shift).astype(LOW).astype(WIDE)
            put_rows(first_rows, pl.ds(t * 8, n * 8), first)
            if kind.causal:
                chosen = is_end(kind, half, t, n)
                tops = tops + jnp.sum(first.reshape(n, 8, width) * chosen, axis=0)
                raws = raws + jnp.sum(rows.reshape(n, 8, width) * chosen, axis=0)
            elif t == 0:
                tops, raws = first[:8], rows[:8]
        top_scr[half * 8 : half * 8 + 8, :width] = tops
        at_scr[half * 8 : half * 8 + 8, :width] = raws
        spare = (room - kind.length) * 8
        put_rows(first_rows, pl.ds(kind.length * 8, spare), jnp.zeros((spare, width), WIDE))
        for i in range(8):
            line = get_rows(first_rows, pl.ds(i, room, stride=8), width)
            first_ref[half * 8 + i, :room, :width] = line.astype(LOW)

    def begin(kind):
        deal = deals[kind.index]
        deal.arrived(VECTORS)
        lift_to(kind, VECTORS, vec_ref, 0)
        normalise(kind, kind.index)

    each_tower(begin)

    def place_inputs(kind):
        deals[kind.index].arrived(0)
        slots = (img_slots, txt_slots)[kind.index]
        per = kind.width // LANES
        for c, value in lift(kind, plans[kind.index], 0, slots, flat):
            ref, lane = ask_block, c * LANES
            if c >= 2 * per:
                ref, lane = mix_block, lane - 2 * kind.width
            put(ref, lane, value.astype(LOW))

    each_tower(place_inputs)
    for ring in asks:
        ring.start()

    def place_hidden(kind):
        deal, plan = deals[kind.index], plans[kind.index]
        slots = (img_slots, txt_slots)[kind.index]
        deal.arrived(2)
        per = kind.part // LANES
        for c, value in lift(kind, plan, 2, slots, flat):
            lane = c % per * LANES
            raise_block[c // per, : kind.block, lane : lane + LANES] = value.astype(LOW)
        deal.arrived(3)
        lift_to(kind, 3, reduce_block, 0)

    def place_rest(kind):
        deals[kind.index].arrived(1)
        lift_to(kind, 1, mix_block, kind.width)
        if kind.index == 1:
            deals[1].arrived(EMBED)
            lift_to(kind, EMBED, emb_block, 0)
            deals[0].arrived(EMBED)
            for c, value in lift(TOWERS[0], plans[0], EMBED, img_slots, flat):
                plane_block[:, c * LANES : (c + 1) * LANES] = value.astype(LOW)

    each_tower(place_rest)

    def question(kind):
        width = kind.width
        tops = top_scr[:, :width].astype(LOW)
        query = dot_nn(tops, matrix(ask_ref, kind, 0, width)) + vector(vec_ref, kind, 2)
        query = query.astype(LOW)
        query_ref[:, :width] = query
        for span in spans(kind):
            lo, hi, first_head, n = span
            put_rows(
                keyed_ref,
                pl.ds(first_head * SEQS, n * SEQS),
                dot_nt(head_rows(query, span), matrix(ask_ref, kind, width + lo, hi - lo)) * 0.125,
            )
        dead = (HEADS - kind.heads) * SEQS
        put_rows(keyed_ref, pl.ds(kind.heads * SEQS, dead), jnp.zeros((dead, width), WIDE))

    for ask in asks:
        ask.relay_deep()
    for mix in mixes:
        mix.start()
    for embed in embeds:
        embed.start()
    plane.start()
    for ask in asks:
        ask.relay_row()
    each_tower(place_hidden)
    rise.start()
    fall.start()
    fall_own.start()
    pair.finish()
    each_tower(lambda kind: normalise(kind, 1 - kind.index))
    masks.start()
    for ask in asks:
        ask.finish()
    each_tower(question)
    for ring in (*mixes, *embeds):
        ring.relay_deep()
    plane.relay_deep()

    def score(kind):
        width, room = kind.width, kind.room
        lane = lax.broadcasted_iota(jnp.int32, (HEADS, room), 1)
        for s in range(SEQS):
            keys = get_rows(keyed_ref, pl.ds(s, HEADS, stride=SEQS), width).astype(LOW)
            scores = dot_nt(keys, first_ref[s, :room, :width])
            if kind.causal:
                allowed = lane <= ends_ref[(s // 8 * 16 + at) * 8 + s % 8]
            else:
                allowed = lane < kind.length
            score_scr[s * HEADS : (s + 1) * HEADS, :room] = jnp.where(allowed, scores, -1e30)
        scores = score_scr[:, :room]
        raw = jnp.exp(scores - jnp.max(scores, axis=-1, keepdims=True))
        weights = raw / jnp.sum(raw, axis=-1, keepdims=True)
        head = lax.broadcasted_iota(jnp.int32, (SEQS * HEADS, 1), 0) % HEADS
        weights = jnp.where(head < kind.heads, weights, 0.0)
        weight_ref[:, :room] = weights
        low_scr[: SEQS * HEADS, :room] = weights.astype(LOW)

    each_tower(score)
    for ring in (*mixes, *embeds):
        ring.relay_row()
    plane.relay_row()

    def mixture(kind):
        width, room = kind.width, kind.room
        for s in range(SEQS):
            mixed = dot_nn(
                low_scr[s * HEADS : (s + 1) * HEADS, :room], first_ref[s, :room, :width]
            )
            put_rows(mixture_ref, pl.ds(s, HEADS, stride=SEQS), mixed)
        totals = jnp.sum(
            low_scr[: SEQS * HEADS, :room].astype(WIDE), axis=-1, keepdims=True
        )
        score_scr[...] = jnp.broadcast_to(totals, score_scr.shape)

    each_tower(mixture)

    for mix in mixes:
        mix.finish()

    def answer(kind):
        width = kind.width
        mixed = []
        bias = vector(vec_ref, kind, 3)
        for span in spans(kind):
            lo, hi, first_head, n = span
            z = get_rows(mixture_ref, pl.ds(first_head * SEQS, n * SEQS), width).astype(LOW)
            valued = dot_nn(z, matrix(mix_ref, kind, lo, hi - lo))
            totals = jnp.concatenate(
                [score_scr[pl.ds(first_head + h, SEQS, stride=HEADS), 0:1] for h in range(n)],
                axis=0,
            )
            mixed.append(from_head_rows(valued + totals * bias[:, lo:hi], span))
        mixed = side_by_side(mixed).astype(LOW)
        middle = (
            at_scr[:, :width]
            + dot_nn(mixed, matrix(mix_ref, kind, width, width))
            + vector(vec_ref, kind, 4)
        )
        middle_ref[:, :width] = middle
        hat, _ = standardise(middle)
        second_ref[:, :width] = (
            hat * vector(vec_ref, kind, 5) + vector(vec_ref, kind, 6)
        ).astype(LOW)
        put_rows(mixture_ref, pl.ds(12 * SEQS, SEQS), top_scr[:, :width])
        put_rows(mixture_ref, pl.ds(13 * SEQS, SEQS), mixed.astype(WIDE))

    each_tower(answer)
    rise.relay()
    masks.relay()
    for embed in embeds:
        embed.finish()
    rise.finish()
    fall_own.wait()
    remote(
        reduce_block, reduce_ref.at[1 - core], reduce_sems.at[0], reduce_sems.at[1], sibling
    ).wait_recv()

    sent = group_exchange(False, second_ref, seconds, group_send.at[0], group_recv.at[0])
    hidden_kernel(seconds, raise_ref, reduce_ref, vec_ref, part, raised)
    plane.land()
    sent += group_exchange(True, part, parts, group_send.at[1], group_recv.at[1])
    plane.finish()
    embed_kernel(parts, middle_ref, (plane_ref, emb_ref), vec_ref, emb, final, pooled_ref, proj)
    embs = Spread(emb, all_embs, embs_send, embs_recv)
    embs.start()
    masks.finish()
    embs.relay()
    embs.finish()
    objective_kernel(
        scale_ref,
        all_embs,
        pairs_ref,
        final,
        proj,
        (plane_ref, emb_ref),
        vec_ref,
        low,
        grad_ref,
        proj_grad_ref,
        final_vec_ref,
        loss_ref,
        scale_new_ref,
        own_scr,
    )
    sent += group_exchange(False, low, lows, group_send.at[2], group_recv.at[2])
    hidden_back_kernel(
        lows,
        seconds,
        raised,
        raise_ref,
        reduce_ref,
        back,
        raise_grad_ref,
        reduce_keep_ref,
        reduce_send_ref,
        bias_ref,
        whole,
    )
    sent += group_exchange(True, back, backs_ref, group_send.at[3], group_recv.at[3])
    halves = remote(
        raise_grad_ref.at[1 - core], raise_half, home_sems.at[0], home_sems.at[1], sibling
    )
    fallen = remote(reduce_send_ref, reduce_in, home_sems.at[2], home_sems.at[3], sibling)
    halves.start()
    fallen.start()
    risen_group = Group(risen_block, raise_all, risen_send, risen_recv, False)

    lefts = Blocks(left_block, left_all, left_send, left_recv)
    turns = Blocks(turn_block, turn_all, turn_send, turn_recv)
    early = Chain(early_block, early_all, early_send, early_recv)
    late = Ring(late_block, late_all, late_send, late_recv)
    home_pair = Pair(img_send, img_home, txt_send, txt_home, home_pair_sems)
    collects = [
        Collect(plans[0], 0, img_home_slots, img_chunks, collect_send.at[0], collect_recv),
        Collect(plans[1], 1, txt_home_slots, txt_chunks, collect_send.at[1], collect_recv),
    ]

    def outputs(kind):
        width = kind.width
        second_grad = jnp.sum(backs_ref[:, :, :width].astype(WIDE), axis=0)
        second_scr[:, :width] = second_grad
        hat, rate = standardise(middle_ref[:, :width])
        middle_grad = grad_ref[:, :width] + norm_back(
            second_grad, vector(vec_ref, kind, 5), hat, rate
        )
        middle_scr[:, :width] = middle_grad
        output_grad = middle_grad.astype(LOW)
        mixed_grad = dot_nt(output_grad, matrix(mix_ref, kind, width, width)).astype(LOW)
        early_block[:, 0:width] = query_ref[:, :width]
        early_block[:, WIDTH : WIDTH + width] = mixed_grad
        early_block[:, 2 * WIDTH : 2 * WIDTH + width] = output_grad
        early_block[:, 3 * WIDTH : 3 * WIDTH + EMB] = proj_grad_ref[...]
        left_scr[:, :width] = get_rows(mixture_ref, slice(None), width)
        left_scr[14 * SEQS : 15 * SEQS, :width] = pooled_ref[:, :width].astype(WIDE)
        left_scr[15 * SEQS :, :width] = jnp.zeros((SEQS, width), WIDE)

    each_tower(outputs)
    early.start()

    def turned(kind):
        width, block = kind.width, kind.block
        left_block[:, :block, :] = left_scr[:, :width].T.reshape(16, block, 256).astype(LOW)

    each_tower(turned)
    lefts.start()

    def values(kind):
        width = kind.width
        mixed_grad = early_block[:, WIDTH : WIDTH + width]
        bias = vector(vec_ref, kind, 3)
        dead = kind.heads * SEQS
        put_rows(valued_scr, pl.ds(dead, 256 - dead), jnp.zeros((256 - dead, width), WIDE))
        shared_scr[dead:, :] = jnp.zeros((256 - dead, LANES), WIDE)
        for span in spans(kind):
            lo, hi, first_head, n = span
            rows = head_rows(mixed_grad, span)
            place = pl.ds(first_head * SEQS, n * SEQS)
            put_rows(valued_scr, place, dot_nt(rows, matrix(mix_ref, kind, lo, hi - lo)))
            constant = jnp.sum(rows.astype(WIDE) * bias[:, lo:hi], axis=-1, keepdims=True)
            shared_scr[place, :] = jnp.broadcast_to(constant, (n * SEQS, LANES))

    each_tower(values)
    halves.wait_recv()
    risen_block[...] = (
        raise_grad_ref[core].astype(WIDE) + raise_half[...].astype(WIDE)
    ).astype(LOW)
    risen_group.start()

    def slopes(kind):
        width, room = kind.width, kind.room
        for s in range(SEQS):
            line = pl.ds(s, HEADS, stride=SEQS)
            slope = dot_nt(
                get_rows(valued_scr, line, width).astype(LOW), first_ref[s, :room, :width]
            )
            slope_scr[s * HEADS : (s + 1) * HEADS, :room] = slope + shared_scr[line, 0:1]
        weights = weight_ref[:, :room]
        slope = slope_scr[:, :room]
        slope = weights * (slope - jnp.sum(weights * slope, axis=-1, keepdims=True))
        both = jnp.concatenate(
            [slope.reshape(SEQS, HEADS, room), weights.reshape(SEQS, HEADS, room)], axis=1
        )
        low_scr[:, :room] = both.reshape(2 * SEQS * HEADS, room).astype(LOW)

    each_tower(slopes)
    early.relay_deep()

    def tokens(kind):
        width, room = kind.width, kind.room
        for s in range(SEQS):
            line = pl.ds(s, HEADS, stride=SEQS)
            both = low_scr[2 * s * HEADS : 2 * (s + 1) * HEADS, :room]
            first = first_ref[s, :room, :width]
            put_rows(turn_scr, line, dot_nn(both[:HEADS], first))
            right = jnp.concatenate(
                [get_rows(keyed_ref, line, width), get_rows(valued_scr, line, width)], axis=0
            )
            put_rows(
                rows_grad.at[s // 8],
                pl.ds(s % 8, room, stride=8),
                dot_tn(both, right.astype(LOW)),
            )

    each_tower(tokens)
    early.relay_row()

    def queries(kind):
        width, block = kind.width, kind.block
        grads = []
        for span in spans(kind):
            lo, hi, first_head, n = span
            rows = get_rows(turn_scr, pl.ds(first_head * SEQS, n * SEQS), width).astype(LOW)
            back = dot_nn(rows, matrix(ask_ref, kind, width + lo, hi - lo)) * 0.125
            grads.append(from_head_rows(back, span))
        query_grad = side_by_side(grads).astype(LOW)
        late_block[:, :width] = query_grad
        top_grad_scr[:, :width] = dot_nt(query_grad, matrix(ask_ref, kind, 0, width))
        turn_block[:, :block, :] = (
            get_rows(turn_scr, slice(None), width).T.reshape(16, block, 256).astype(LOW)
        )

    each_tower(queries)
    late.start()
    turns.start()
    gains[...] = jnp.zeros_like(gains)

    def finish(kind, half):
        width = kind.width
        ref = tokens_of(kind, half)
        keep, send = ((img_keep, img_send), (txt_keep, txt_send))[kind.index]
        gain = vector(vec_ref, kind, 0)
        top = top_grad_scr[half * 8 : half * 8 + 8, :width]
        low = middle_scr[half * 8 : half * 8 + 8, :width]
        gain_sum = jnp.zeros((1, width), WIDE)
        shift_sum = jnp.zeros((1, width), WIDE)
        for t, n in steps(kind):
            hat, rate = standardise(ref[t : t + n].astype(WIDE).reshape(n * 8, width))
            grad = get_rows(rows_grad.at[half], pl.ds(t * 8, n * 8), width)
            chosen = None
            if kind.causal:
                chosen = is_end(kind, half, t, n)
            elif t == 0:
                chosen = (lax.broadcasted_iota(jnp.int32, (n, 8, 1), 0) == 0).astype(WIDE)
            if chosen is not None:
                grad = grad + (chosen * top[None]).reshape(n * 8, width)
            gain_sum += jnp.sum(grad * hat, axis=0, keepdims=True)
            shift_sum += jnp.sum(grad, axis=0, keepdims=True)
            result = norm_back(grad, gain, hat, rate)
            if chosen is not None:
                result = result + (chosen * low[None]).reshape(n * 8, width)
            result = result.reshape(n, 8, width)
            if half == kind.index:
                keep[t : t + n] = result
            else:
                send[t : t + n] = result.astype(LOW)
        gains[0:1, :width] += gain_sum
        gains[1:2, :width] += shift_sum

    each_tower(lambda kind: finish(kind, 1 - kind.index))
    home_pair.start()
    risen_group.finish()
    fallen.wait_recv()

    def slots_of(kind):
        return (img_home_slots, txt_home_slots)[kind.index]

    def hidden_grads(kind):
        plan, collect = plans[kind.index], collects[kind.index]
        block, n, per = kind.block, kind.reduce_rows, kind.part // LANES

        def risen(c):
            chip, lane = c // per, c % per * LANES
            return raise_all[chip, :block, lane : lane + LANES].astype(WIDE)

        def fallen(c):
            lane = c * LANES
            return reduce_keep_ref[:n, lane : lane + LANES] + reduce_in[
                :n, lane : lane + LANES
            ].astype(WIDE)

        drop(kind, plan, 2, risen, slots_of(kind), flat)
        collect.piece(2, False)
        drop(kind, plan, 3, fallen, slots_of(kind), flat)
        collect.piece(3, False)

    each_tower(hidden_grads)
    late.relay_deep()
    each_tower(lambda kind: finish(kind, kind.index))
    late.relay_row()

    def lines(kind):
        width = kind.width
        hat, _ = standardise(middle_ref[:, :width])
        second_grad = second_scr[:, :width]

        def column_sum(value):
            return jnp.sum(value.astype(WIDE), axis=0, keepdims=True)

        mixed_grad = early_block[:, WIDTH : WIDTH + width].astype(WIDE)
        weights = low_scr[:, : kind.room].astype(WIDE).reshape(SEQS, 2 * HEADS, kind.room)
        totals = jnp.sum(weights[:, HEADS:], axis=-1, keepdims=True).reshape(SEQS * HEADS, 1)
        shared_scr[...] = jnp.broadcast_to(totals, shared_scr.shape)
        value_bias = []
        for lo, hi, first_head, n in spans(kind):
            owner = lax.broadcasted_iota(jnp.int32, (SEQS, hi - lo), 1) // HEAD
            scaled = jnp.zeros((SEQS, hi - lo), WIDE)
            for h in range(n):
                total = shared_scr[pl.ds(first_head + h, SEQS, stride=HEADS), 0:1]
                scaled = jnp.where(owner == h, mixed_grad[:, lo:hi] * total, scaled)
            value_bias.append(column_sum(scaled))
        hidden = bias_ref[0:1, : kind.part]
        parts = [
            gains[0:1, :width],
            gains[1:2, :width],
            column_sum(late_block[:, :width]),
            side_by_side(value_bias),
            column_sum(early_block[:, 2 * WIDTH : 2 * WIDTH + width]),
            column_sum(second_grad * hat),
            column_sum(second_grad),
            final_vec_ref[2:3, :width],
            final_vec_ref[0:1, :width],
            final_vec_ref[1:2, :width],
            jnp.concatenate([hidden, jnp.zeros((1, width - kind.part), WIDE)], axis=1),
            jnp.zeros((5, width), WIDE),
        ]
        lines_block[:, :width] = jnp.concatenate(parts, axis=0)

    each_tower(lines)
    line_copy = remote(
        lines_block, lines_all.at[at], lines_send.at[0], lines_recv.at[at], (tower, jnp.int32(0))
    )
    line_own = pltpu.make_async_copy(lines_block, lines_all.at[at], lines_recv.at[at])
    pl.when(at > 0)(line_copy.start)
    pl.when(at == 0)(line_own.start)

    early.finish()
    lefts.finish()

    def from_early(kind):
        plan, collect = plans[kind.index], collects[kind.index]
        width, block = kind.width, kind.block

        def gathered(k):
            lane = lax.broadcasted_iota(jnp.int32, (block, LANES), 1) // SEQS
            halves = []
            for side in range(2):
                total = jnp.zeros((block, LANES), WIDE)
                for j in range(8):
                    part = left_all[side * 8 + j, :block, LANES:].astype(WIDE)
                    shift = (j * SEQS - (k - 8) * SEQS) % LANES
                    turned_part = pltpu.roll(part, shift, 1) if shift else part
                    total = jnp.where(lane == j, turned_part, total)
                halves.append(total)
            return jnp.concatenate(halves, axis=1).astype(LOW)

        def right(start, wide):
            return early_all[:, :, start : start + wide].reshape(256, wide)

        output = dot_nn(gathered(13), right(2 * WIDTH, width))
        drop(
            kind, plan, 1, lambda c: output[:, c * LANES : (c + 1) * LANES], slots_of(kind), flat
        )
        collect.piece(1, False)
        embed = dot_nn(gathered(14), right(3 * WIDTH, EMB))
        drop(kind, plan, 4, lambda c: embed[:, c * LANES : (c + 1) * LANES], slots_of(kind), flat)
        collect.piece(4, False)
        left_scr[:block, :256] = gathered(12).astype(WIDE)

    each_tower(from_early)
    late.finish()
    turns.finish()

    def from_late(kind):
        plan, collect = plans[kind.index], collects[kind.index]
        width, block = kind.width, kind.block
        ask = dot_nn(left_scr[:block, :256].astype(LOW), late_all[:, :, :width].reshape(256, width))

        def outer(side_ref, start, span):
            lo, hi, first_head, n = span
            lane = first_head * SEQS
            total = jnp.zeros((block, hi - lo), WIDE)
            for j in range(8):
                left, rows = [], []
                for source in (2 * j, 2 * j + 1):
                    left.append(side_ref[source, :block, lane : lane + LANES])
                    rows.append(
                        head_rows(early_all[source, :, start : start + width], span)
                    )
                    if n < 8:
                        rows.append(jnp.zeros(((8 - n) * SEQS, hi - lo), LOW))
                total += dot_nn(
                    jnp.concatenate(left, axis=1), jnp.concatenate(rows, axis=0)
                )
            return total

        keys = side_by_side([outer(turn_all, 0, span) for span in spans(kind)]) * 0.125
        worth = side_by_side([outer(left_all, WIDTH, span) for span in spans(kind)])
        per = width // LANES

        def inputs(c):
            value = (ask, keys, worth)[c // per]
            return value[:, c % per * LANES : (c % per + 1) * LANES]

        drop(kind, plan, 0, inputs, slots_of(kind), flat)
        collect.piece(0, False)

    each_tower(from_late)

    @pl.when(at == 0)
    def _():
        for k in range(1, 16):
            remote(
                lines_block, lines_all.at[k], lines_send.at[0], lines_recv.at[k], sibling
            ).wait_recv()
        line_own.wait()

        def vectors(kind):
            width, part = kind.width, kind.part
            whole = [jnp.sum(lines_all[:, :10, :width], axis=0)]
            for row in range(4):
                pair_of = []
                for chip in (2 * row, 2 * row + 1):
                    pair_of.append(
                        lines_all[2 * chip, 10:11, :part] + lines_all[2 * chip + 1, 10:11, :part]
                    )
                whole.append(jnp.concatenate(pair_of, axis=1))
            whole.append(jnp.zeros((2, width), WIDE))
            result = jnp.concatenate(whole, axis=0)
            drop(
                kind,
                plans[kind.index],
                VECTORS,
                lambda c: result[:, c * LANES : (c + 1) * LANES],
                slots_of(kind),
                flat,
            )

        each_tower(vectors)

    each_tower(lambda kind: collects[kind.index].piece(VECTORS, False))
    home_pair.finish()

    @pl.when(tower == 1)
    def _():
        img_keep[...] = img_home[...].astype(WIDE)

    @pl.when(tower == 0)
    def _():
        txt_keep[...] = txt_home[...].astype(WIDE)

    for collect in collects:
        collect.finish()
    for copy in (*sent, fall, fallen, halves):
        copy.wait_send()
    pl.when(at > 0)(line_copy.wait_send)
    for when, copy in heads:
        pl.when(when)(copy.wait_send)
    pl.when(tower == 0)(relay.wait_send)
    for group in (pair, *asks, *mixes, *embeds, plane, rise, masks, embs, *deals):
        group.drain()
    for group in (risen_group, lefts, turns, early, late, home_pair):
        group.drain()

    def drain(kind):
        for p in range(VECTORS + 1):
            collects[kind.index].piece(p, True)

    each_tower(drain)


ROWS_LOW = ((SEQS, WIDTH), LOW)
ROWS_WIDE = ((SEQS, WIDTH), WIDE)
HEAD_ROWS = ((WIDTH // LANES, SEQS * HEADS, LANES), WIDE)
LANE_ROWS = ((SEQS * HEADS, LANES), WIDE)
GROUP = ((8, SEQS, WIDTH), LOW)
HIDDEN_BLOCKS = ((2, 8, 48, PART), LOW)
OUTER = ((16, 48, SEQS * HEADS), LOW)


def chunk_shapes(plan, n):
    return ((n, plan.rows, LANES), LOW)


def run_step(scalars, chunks, valid, tokens, plans):
    most = max(plan.local for plan in plans) + 17
    slots = max(plan.slots for plan in plans)
    edges = [((plan.rows, LANES), LOW) for plan in plans]
    rooms = [((kind.length, 8, kind.width), LOW) for kind in TOWERS]
    outs = [((kind.length, 8, kind.width), WIDE) for kind in TOWERS] + [
        chunk_shapes(plan, plan.local) for plan in plans
    ]
    scratch = [
        ROWS_LOW,
        ROWS_WIDE,
        ROWS_LOW,
        HEAD_ROWS,
        HEAD_ROWS,
        LANE_ROWS,
        ((SEQS, ROOM, WIDTH), LOW),
        ((WIDTH // LANES, ROOM * 8, LANES), WIDE),
        rooms[0],
        rooms[1],
        ((3, 16, 16, 2 * WIDTH), LOW),
        ((3, 16, 16, 2 * WIDTH), LOW),
        ((3, 16, 16, EMB), LOW),
        ROWS_WIDE,
        HIDDEN_BLOCKS,
        ((2, 192, WIDTH), LOW),
        ((2, 16, 16, LANES), LOW),
        chunk_shapes(plans[0], plans[0].slots),
        chunk_shapes(plans[1], plans[1].slots),
        edges[0],
        edges[1],
        edges[0],
        edges[1],
        chunk_shapes(plans[1], plans[1].local),
        edges[1],
        edges[1],
        ((plans[0].slots * plans[0].rows, LANES), WIDE),
        ((3, 16, 2 * WIDTH), LOW),
        ((3, 16, 2 * WIDTH), LOW),
        ((3, 16, EMB), LOW),
        ((48, EMB), LOW),
        ((8, 48, EMB), LOW),
        ((2, 8, 48, EMB), LOW),
        ((8, 48, PART), LOW),
        ((192, WIDTH), LOW),
        ((16, LANES), LOW),
        ROWS_WIDE,
        ROWS_WIDE,
        LANE_ROWS,
        ((2 * SEQS * HEADS, LANES), LOW),
        ROWS_WIDE,
        ROWS_LOW,
        ((SEQS, EMB), LOW),
        ((8, WIDTH), WIDE),
        HIDDEN_BLOCKS,
        ((192, WIDTH), WIDE),
        ((192, WIDTH), LOW),
        ((8, PART), WIDE),
        GROUP,
        GROUP,
        GROUP,
        GROUP,
        ((128, PART), WIDE),
        ((SEQS, EMB), LOW),
        ((2, 16, SEQS, EMB), LOW),
        ROWS_WIDE,
        ((SEQS, EMB), WIDE),
        ROWS_LOW,
        GROUP,
        GROUP,
        ((256, EMB), WIDE),
        ((PART, WIDTH), WIDE),
        rooms[0],
        rooms[1],
        rooms[0],
        rooms[1],
        ((2, WIDTH // LANES, ROOM * 8, LANES), WIDE),
        ROWS_WIDE,
        ROWS_WIDE,
        HEAD_ROWS,
        HEAD_ROWS,
        LANE_ROWS,
        LANE_ROWS,
        ((SEQS * HEADS, WIDTH), WIDE),
        OUTER,
        OUTER,
        OUTER,
        OUTER,
        ((SEQS, 3 * WIDTH + EMB), LOW),
        ((16, SEQS, 3 * WIDTH + EMB), LOW),
        ROWS_LOW,
        ((16, SEQS, WIDTH), LOW),
        ROWS_WIDE,
        ((16, SEQS, WIDTH), WIDE),
        ((8, 48, PART), LOW),
        ((8, 48, PART), LOW),
        ((8, 48, PART), LOW),
        ((192, WIDTH), LOW),
        chunk_shapes(plans[0], plans[0].slots),
        chunk_shapes(plans[1], plans[1].slots),
        ((8, WIDTH), WIDE),
        ROWS_WIDE,
    ]
    semaphores = [
        (3, most),
        (2, 6,),
        (3, 2),
        (3,),
        (2,),
        (3, 16),
        (3, 15),
        (3, 16),
        (3, 15),
        (3, 20),
        (3, 15),
        (10,),
        (9,),
        (9,),
        (8,),
        (3,),
        (2,),
        (17,),
        (16,),
        (4, 8,),
        (4, 7,),
        (17,),
        (16,),
        (4,),
        (9,),
        (8,),
        (16,),
        (15,),
        (16,),
        (15,),
        (20,),
        (15,),
        (16,),
        (15,),
        (1,),
        (16,),
        (2,),
        (2, 2, slots,),
        (2,),
    ]
    smem = pl.BlockSpec(memory_space=pltpu.SMEM)
    vmem = pl.BlockSpec(memory_space=pltpu.VMEM)
    like = jax.ShapeDtypeStruct
    return pl.pallas_call(
        functools.partial(step_kernel, plans),
        out_shape=[like((1,), WIDE), like((3,), WIDE)] + [like(*out) for out in outs],
        in_specs=[smem, smem, ANY, ANY, vmem, vmem, vmem],
        out_specs=[smem, smem, vmem, vmem, vmem, vmem],
        scratch_shapes=[pltpu.VMEM(*each) for each in scratch]
        + [pltpu.SemaphoreType.DMA(shape) for shape in semaphores],
        compiler_params=comm_params(0),
    )(*scalars, *chunks, valid, *tokens)


def to_chunks(flat, plan, me):
    start = me * plan.share % plan.chunk
    padded = jnp.pad(flat, (plan.chunk, plan.local * plan.chunk - plan.share))
    piece = lax.dynamic_slice(padded, (plan.chunk - start,), (plan.local * plan.chunk,))
    return piece.astype(LOW).reshape(plan.local, plan.rows, LANES)


def from_chunks(chunks, plan, me):
    start = me * plan.share % plan.chunk
    return lax.dynamic_slice(chunks.reshape(-1), (start,), (plan.share,)).astype(WIDE)


def step(
    img_tokens,
    txt_tokens,
    txt_ends,
    valid,
    img_master,
    img_moment,
    img_average,
    txt_master,
    txt_moment,
    txt_average,
    scale_state,
):
    me = lax.axis_index(("tower", "dp"))
    plans = (
        Plan(0, img_master.shape[0], 96, (9, 3, 12, 12, 2)),
        Plan(1, txt_master.shape[0], 64, (6, 2, 8, 8, 2)),
    )
    loss, scale_new, img_grad, txt_grad, img_chunks, txt_chunks = run_step(
        (txt_ends, scale_state),
        (to_chunks(img_master, plans[0], me), to_chunks(txt_master, plans[1], me)),
        valid,
        (jnp.transpose(img_tokens, (1, 0, 2)), jnp.transpose(txt_tokens, (1, 0, 2))),
        plans,
    )
    img_new = advance(
        img_master, img_moment, img_average, from_chunks(img_chunks, plans[0], me), step_rate
    )
    txt_new = advance(
        txt_master, txt_moment, txt_average, from_chunks(txt_chunks, plans[1], me), step_rate
    )
    return (
        loss[0],
        jnp.transpose(img_grad, (1, 0, 2)),
        jnp.transpose(txt_grad, (1, 0, 2)),
        img_new[0],
        img_new[1],
        img_new[2],
        img_new[0].astype(LOW),
        txt_new[0],
        txt_new[1],
        txt_new[2],
        txt_new[0].astype(LOW),
        scale_new,
    )


def from_partner(value, axis, stride):
    mask = 2**stride
    pairs = [(source, source ^ mask) for source in range(lax.axis_size(axis))]
    return lax.ppermute(value, axis, pairs)


def round_value(v):
    return lax.optimization_barrier(v.astype(jnp.bfloat16)).astype(jnp.float32)


def make_low():

    def value_keep(v):
        return (round_value(v), None)

    def grad_pass(kept, grad):
        return (grad,)

    rounded = jax.custom_vjp(round_value)
    rounded.defvjp(value_keep, grad_pass)
    return rounded


def low(v):
    return make_low()(v)


def make_low_back():

    def identity(v):
        return v

    def value_pass(v):
        return (v, None)

    def grad_round(kept, grad):
        return (round_value(grad),)

    passed = jax.custom_vjp(identity)
    passed.defvjp(value_pass, grad_round)
    return passed


def low_back(v):
    return make_low_back()(v)


def both_ways(value):
    return low(low_back(value))


def product(left, right):
    return jnp.matmul(left, right)


def contract(form, left, right):
    return jnp.einsum(form, left, right)


def layer_norm(values, gain_row, shift_row):
    centred = values - jnp.mean(values, axis=-1, keepdims=True)
    spread = jnp.mean(centred * centred, axis=-1, keepdims=True)
    return centred * lax.rsqrt(spread + 1e-05) * gain_row + shift_row


def unpack(flat_weights, model_width, hidden_width, embed_width):
    piece_shapes = [
        (model_width, 3 * model_width),
        (model_width, model_width),
        (model_width, hidden_width),
        (hidden_width, model_width),
        (model_width, embed_width),
        (10, model_width),
        (hidden_width,),
    ]
    pieces = []
    offset = 0
    for piece_shape in piece_shapes:
        length = math.prod(piece_shape)
        pieces.append(flat_weights[offset : offset + length].reshape(piece_shape))
        offset = offset + length
    return pieces


def encode(tokens, flat_weights, positions, causal, model_width, hidden_width, embed_width):
    w_inputs, w_output, w_expand, w_reduce, w_embed, vectors, expand_bias = unpack(
        flat_weights, model_width, hidden_width, embed_width
    )
    groups = tokens.shape[0]
    length = tokens.shape[1]
    first = low(layer_norm(tokens, vectors[0], vectors[1]))
    bias_in = jnp.concatenate([vectors[2], jnp.zeros_like(vectors[2]), vectors[3]])
    joined = both_ways(product(first, w_inputs) + bias_in)
    joined = joined.reshape(groups, length, 3, model_width // HEAD, HEAD)
    scores = low_back(contract("gqhd,gkhd->ghqk", joined[:, :, 0], joined[:, :, 1]) * 0.125)
    if causal:
        row_index = lax.broadcasted_iota(jnp.int32, (length, length), 0)
        col_index = lax.broadcasted_iota(jnp.int32, (length, length), 1)
        scores = jnp.where(col_index <= row_index, scores, -1e30)
    row_top = jnp.max(scores, axis=-1, keepdims=True)
    raw_weights = jnp.exp(scores - row_top)
    attention = low(raw_weights / jnp.sum(raw_weights, axis=-1, keepdims=True))
    mixed_heads = both_ways(
        contract("ghqk,gkhd->gqhd", attention, joined[:, :, 2]).reshape(groups, length, model_width)
    )
    middle = tokens + low_back(product(mixed_heads, w_output) + vectors[4])
    second = low(layer_norm(middle, vectors[5], vectors[6]))
    raised = low_back(product(second, w_expand) + expand_bias)
    active = low(raised * jax.nn.sigmoid(1.702 * raised))
    final_rows = middle + low_back(product(active, w_reduce) + vectors[7])
    pooled = jnp.take_along_axis(final_rows, positions[:, None, None], axis=1)[:, 0]
    pooled = low(layer_norm(pooled, vectors[8], vectors[9]))
    projected = low_back(product(pooled, w_embed))
    return low(
        projected * lax.rsqrt(jnp.sum(projected * projected, axis=-1, keepdims=True) + 1e-06)
    )


def inner(left, right):
    return lax.dot_general(
        left, right, (((1,), (1,)), ((), ())), preferred_element_type=jnp.float32
    )


def across(left, right):
    return lax.dot_general(
        left, right, (((0,), (0,)), ((), ())), preferred_element_type=jnp.float32
    )


def softmax_total(logits, allowed):
    masked = jnp.where(allowed, logits, -1e30)
    row_top = jnp.max(masked, axis=1, keepdims=True)
    return jnp.log(jnp.sum(jnp.exp(masked - row_top), axis=1)) + row_top[:, 0]


def advance(master, moment, average, grads, rate):
    moment_new = momentum_rate * moment + grads
    master_new = master - rate * (grads + momentum_rate * moment_new)
    average_new = average_rate * average + (1.0 - average_rate) * master_new
    return (master_new, moment_new, average_new)


def padded_to(flat, length):
    return jnp.pad(flat, (0, length - flat.shape[0]))


def body(
    img_tokens,
    txt_tokens,
    txt_ends,
    valid,
    img_master,
    img_moment,
    img_average,
    txt_master,
    txt_moment,
    txt_average,
    scale_state,
):
    batch_rows = img_tokens.shape[0]
    total_rows = batch_rows * lax.axis_size(("tower", "dp"))
    device_at = lax.axis_index(("tower", "dp"))
    tower_at = lax.axis_index("tower")
    is_image = tower_at == 0
    img_share = img_master.shape[0]
    txt_share = txt_master.shape[0]
    img_count = img_tokens.size
    txt_count = txt_tokens.size
    shard_room = max(img_share, txt_share)
    token_room = max(img_count, txt_count)
    tower_count = lax.axis_size("dp")
    dp_at = lax.axis_index("dp")
    img_low = padded_to(img_master.astype(jnp.bfloat16), shard_room)
    txt_low = padded_to(txt_master.astype(jnp.bfloat16), shard_room)
    token_out = jnp.where(
        is_image,
        padded_to(txt_tokens.reshape(-1), token_room),
        padded_to(img_tokens.reshape(-1), token_room),
    )
    weight_out = jnp.where(is_image, txt_low, img_low)
    weight_mine = jnp.where(is_image, img_low, txt_low)
    token_in, weight_in = from_partner((token_out, weight_out), "tower", 0)
    stacked = jnp.where(
        is_image, jnp.stack([weight_mine, weight_in]), jnp.stack([weight_in, weight_mine])
    )
    gathered = lax.all_gather(stacked, "dp", axis=1, tiled=True)
    pair_ends = jnp.concatenate(
        [
            lax.dynamic_slice_in_dim(txt_ends, dp_at * batch_rows, batch_rows),
            lax.dynamic_slice_in_dim(txt_ends, (tower_count + dp_at) * batch_rows, batch_rows),
        ]
    )
    pair_zero = jnp.zeros((2 * batch_rows,), jnp.int32)

    def image_weights(whole):
        return whole.reshape(2, tower_count, shard_room).reshape(-1).astype(jnp.float32)

    def text_weights(whole):
        return (
            whole.reshape(2, tower_count, shard_room)[:, :, :txt_share]
            .reshape(-1)
            .astype(jnp.float32)
        )

    def image_rows(arrived):
        return jnp.concatenate(
            [img_tokens, arrived[:img_count].reshape(img_tokens.shape)], axis=0
        ).astype(jnp.float32)

    def text_rows(arrived):
        return jnp.concatenate([arrived.reshape(txt_tokens.shape), txt_tokens], axis=0).astype(
            jnp.float32
        )

    def image_encode(rows, flat):
        return encode(rows, flat, pair_zero, False, D_IMG, FF_IMG, EMB)

    def text_encode(rows, flat):
        return encode(rows, flat, pair_ends, True, D_TXT, FF_TXT, EMB)

    def image_forward(operands):
        return image_encode(image_rows(operands[1]), image_weights(operands[0]))

    def text_forward(operands):
        return text_encode(text_rows(operands[1]), text_weights(operands[0]))

    pair_emb = lax.cond(is_image, image_forward, text_forward, (gathered, token_in)).astype(
        jnp.bfloat16
    )
    emb_in = from_partner(pair_emb, "tower", 0)
    img_pair = jnp.where(is_image, pair_emb, emb_in)
    txt_pair = jnp.where(is_image, emb_in, pair_emb)
    row_start = tower_at * batch_rows
    img_local = lax.dynamic_slice_in_dim(img_pair, row_start, batch_rows)
    txt_local = lax.dynamic_slice_in_dim(txt_pair, row_start, batch_rows)
    img_all, txt_all = (
        lax.all_gather(img_local, ("tower", "dp"), axis=0, tiled=True),
        lax.all_gather(txt_local, ("tower", "dp"), axis=0, tiled=True),
    )
    logit_scale = jnp.exp(scale_state[0])
    offset = device_at * batch_rows
    row_index = lax.broadcasted_iota(jnp.int32, (batch_rows, total_rows), 0) + offset
    col_index = lax.broadcasted_iota(jnp.int32, (batch_rows, total_rows), 1)
    diagonal = (row_index == col_index).astype(jnp.float32)
    allowed = valid > 0
    row_logits = logit_scale * inner(img_local, txt_all)
    col_logits = logit_scale * inner(txt_local, img_all)
    row_lse = softmax_total(row_logits, allowed)
    col_lse = softmax_total(col_logits, allowed)
    partial_loss = 0.5 * (
        jnp.sum(row_lse)
        - jnp.sum(row_logits * diagonal)
        + jnp.sum(col_lse)
        - jnp.sum(col_logits * diagonal)
    )
    row_terms = 0.5 * (jnp.where(allowed, jnp.exp(row_logits - row_lse[:, None]), 0.0) - diagonal)
    col_terms = 0.5 * (jnp.where(allowed, jnp.exp(col_logits - col_lse[:, None]), 0.0) - diagonal)
    partial_scale = jnp.sum(row_terms * row_logits) + jnp.sum(col_terms * col_logits)
    row_back = (logit_scale * row_terms).astype(jnp.bfloat16)
    col_back = (logit_scale * col_terms).astype(jnp.bfloat16)
    img_emb_grad = jnp.dot(row_back, txt_all, preferred_element_type=jnp.float32)
    txt_emb_grad = jnp.dot(col_back, img_all, preferred_element_type=jnp.float32)
    img_extra, txt_extra = (
        lax.psum_scatter(
            across(col_back, txt_local), ("tower", "dp"), scatter_dimension=0, tiled=True
        ),
        lax.psum_scatter(
            across(row_back, img_local), ("tower", "dp"), scatter_dimension=0, tiled=True
        ),
    )
    img_emb_grad = img_emb_grad + img_extra
    txt_emb_grad = txt_emb_grad + txt_extra
    sums = lax.psum((partial_loss, partial_scale), ("tower", "dp"))
    grad_out = jnp.where(is_image, txt_emb_grad, img_emb_grad)
    grad_in = from_partner(grad_out, "tower", 0)
    pair_cot = jnp.where(
        is_image,
        jnp.concatenate([img_emb_grad, grad_in], axis=0),
        jnp.concatenate([grad_in, txt_emb_grad], axis=0),
    )

    def image_backward(operands):
        recomputed, tower_pullback = jax.vjp(
            image_encode, image_rows(operands[1]), image_weights(operands[0])
        )
        rows_grad, flat_grad = tower_pullback(operands[2])
        own_part = padded_to(rows_grad[:batch_rows].reshape(-1), token_room)
        sent_part = padded_to(rows_grad[batch_rows:].reshape(-1), token_room)
        stacked_grad = flat_grad.reshape(2, tower_count, img_share)
        return (own_part, sent_part, stacked_grad)

    def text_backward(operands):
        recomputed, tower_pullback = jax.vjp(
            text_encode, text_rows(operands[1]), text_weights(operands[0])
        )
        rows_grad, flat_grad = tower_pullback(operands[2])
        own_part = padded_to(rows_grad[batch_rows:].reshape(-1), token_room)
        sent_part = padded_to(rows_grad[:batch_rows].reshape(-1), token_room)
        stacked_grad = jnp.pad(
            flat_grad.reshape(2, tower_count, txt_share),
            ((0, 0), (0, 0), (0, shard_room - txt_share)),
        )
        return (own_part, sent_part, stacked_grad)

    own_part, sent_part, stacked_grad = lax.cond(
        is_image, image_backward, text_backward, (gathered, token_in, pair_cot)
    )
    summed = lax.psum_scatter(stacked_grad, "dp", scatter_dimension=1, tiled=True)
    kept_part = jnp.where(is_image, summed[0, 0], summed[1, 0])
    sent_share = jnp.where(is_image, summed[1, 0], summed[0, 0])
    home_weights, home_tokens = (
        from_partner(sent_share.astype(jnp.bfloat16), "tower", 0).astype(sent_share.dtype),
        from_partner(sent_part.astype(jnp.bfloat16), "tower", 0).astype(sent_part.dtype),
    )
    img_owned = jnp.where(is_image, kept_part, home_weights)
    txt_owned = jnp.where(is_image, home_weights, kept_part)[:txt_share]
    img_grad = jnp.where(is_image, own_part, home_tokens)[:img_count].reshape(img_tokens.shape)
    txt_grad = jnp.where(is_image, home_tokens, own_part).reshape(txt_tokens.shape)
    img_new = advance(img_master, img_moment, img_average, img_owned, step_rate)
    txt_new = advance(txt_master, txt_moment, txt_average, txt_owned, step_rate)
    scale_parts = advance(scale_state[0], scale_state[1], scale_state[2], sums[1], scale_rate)
    scale_new = jnp.stack([scale_parts[0], scale_parts[1], scale_parts[2]])
    return (
        sums[0] / total_rows,
        img_grad,
        txt_grad,
        img_new[0],
        img_new[1],
        img_new[2],
        img_new[0].astype(jnp.bfloat16),
        txt_new[0],
        txt_new[1],
        txt_new[2],
        txt_new[0].astype(jnp.bfloat16),
        scale_new,
    )


def solution(mesh):
    in_specs = (
        P(("tower", "dp"), None, None),
        P(("tower", "dp"), None, None),
        P(),
        P(("tower", "dp"), None),
        P(("tower", "dp")),
        P(("tower", "dp")),
        P(("tower", "dp")),
        P(("tower", "dp")),
        P(("tower", "dp")),
        P(("tower", "dp")),
        P(),
    )
    out_specs = (
        P(),
        P(("tower", "dp"), None, None),
        P(("tower", "dp"), None, None),
        P(("tower", "dp")),
        P(("tower", "dp")),
        P(("tower", "dp")),
        P(("tower", "dp")),
        P(("tower", "dp")),
        P(("tower", "dp")),
        P(("tower", "dp")),
        P(("tower", "dp")),
        P(),
    )
    run = step if (mesh.shape["tower"], mesh.shape["dp"]) == (2, 16) else body
    return jax.shard_map(run, mesh=mesh, in_specs=in_specs, out_specs=out_specs, check_vma=False)
```

```python
import functools
import math

import jax
import jax.numpy as jnp
from jax import lax
from jax.experimental import pallas as pl
from jax.experimental.pallas import tpu as pltpu
from jax.sharding import PartitionSpec as P

D_IMG = 768
FF_IMG = 3072
D_TXT = 512
FF_TXT = 2048
EMB = 512
HEAD = 64


momentum_rate = 0.5
average_rate = 0.5
step_rate = 0.08
scale_rate = 0.0001


MESH = pl.DeviceIdType.MESH
ANY = pl.BlockSpec(memory_space=pl.ANY)
GRANT = 58 * 1024 * 1024
LANES = 128
LOW = jnp.bfloat16
WIDE = jnp.float32


def here():
    return lax.axis_index("tower"), lax.axis_index("dp")


def greet(devices):
    barrier = pltpu.get_barrier_semaphore()
    for device in devices:
        pl.semaphore_signal(barrier, inc=1, device_id=device, device_id_type=MESH)
    pl.semaphore_wait(barrier, len(devices))


def remote(src, dst, send_sem, recv_sem, device):
    return pltpu.make_async_remote_copy(
        src_ref=src,
        dst_ref=dst,
        send_sem=send_sem,
        recv_sem=recv_sem,
        device_id=device,
        device_id_type=MESH,
    )


def comm_params(number):
    return pltpu.CompilerParams(
        collective_id=number, has_side_effects=True, vmem_limit_bytes=GRANT
    )


def same_core(tower, at):
    chip, core = at // 2, at % 2
    return [(tower, (chip + k) % 8 * 2 + core) for k in range(1, 8)]


def both_towers(tower, at):
    place, core = tower * 8 + at // 2, at % 2
    others = [(place + k) % 16 for k in range(1, 16)]
    return [(other // 8, other % 8 * 2 + core) for other in others]


def everyone(tower, at):
    me = tower * 16 + at
    others = [(me + k) % 32 for k in range(1, 32)]
    return [(other // 16, other % 16) for other in others]


def group_exchange(scattered, x_ref, o_ref, send_sem, recv_sem):
    tower, at = here()
    chip = at // 2

    def source(k):
        return x_ref.at[k] if scattered else x_ref

    own = pltpu.make_async_copy(source(chip), o_ref.at[chip], send_sem.at[7])
    sent = []
    for k, device in enumerate(same_core(tower, at)):
        copy = remote(
            source((chip + 1 + k) % 8), o_ref.at[chip], send_sem.at[k], recv_sem.at[k], device
        )
        copy.start()
        sent.append(copy)
    own.start()
    own.wait()
    for k in range(7):
        remote(
            source(chip),
            o_ref.at[(chip + 7 - k) % 8],
            send_sem.at[k],
            recv_sem.at[k],
            (tower, at),
        ).wait_recv()
    return sent


class Spread:
    def __init__(self, src, dst, send, recv):
        self.src, self.dst, self.send, self.recv = src, dst, send, recv
        tower, at = here()
        self.core = at % 2
        self.sibling = (tower, at + 1 - 2 * self.core)
        self.devices = self.peers(tower, at)
        self.n = len(self.devices) + 1
        self.place = self.spot(tower, at)
        self.sent = []

    def peers(self, tower, at):
        return both_towers(tower, at)

    def spot(self, tower, at):
        return tower * 8 + at // 2

    def block(self, place):
        return self.src

    def side(self, core):
        return self.dst.at[core]

    def launch(self, src, dst, k, device):
        copy = remote(src, dst, self.send.at[k], self.recv.at[k], device)
        copy.start()
        self.sent.append(copy)

    def start(self):
        for k, device in enumerate(self.devices):
            to = (self.place + 1 + k) % self.n
            self.launch(self.block(to), self.side(self.core).at[self.place], k, device)
        self.own = pltpu.make_async_copy(
            self.block(self.place), self.side(self.core).at[self.place], self.send.at[self.n]
        )
        self.own.start()

    def arrived(self):
        for k in range(self.n - 1):
            source = (self.place + self.n - 1 - k) % self.n
            remote(
                self.block(0),
                self.side(self.core).at[source],
                self.send.at[k],
                self.recv.at[k],
                self.sibling,
            ).wait_recv()
        self.own.wait()

    def relay(self):
        self.arrived()
        side = self.side(self.core)
        self.launch(side, side, self.n - 1, self.sibling)

    def finish(self):
        side = self.side(1 - self.core)
        remote(
            side, side, self.send.at[self.n - 1], self.recv.at[self.n - 1], self.sibling
        ).wait_recv()

    def drain(self):
        for copy in self.sent:
            copy.wait_send()


class Group(Spread):
    def __init__(self, src, dst, send, recv, both=True):
        self.both = both
        super().__init__(src, dst, send, recv)

    def peers(self, tower, at):
        return same_core(tower, at)

    def spot(self, tower, at):
        return at // 2

    def block(self, place):
        return self.src.at[place]

    def side(self, core):
        return self.dst.at[core] if self.both else self.dst

    def finish(self):
        if self.both:
            super().finish()
        else:
            self.arrived()


class Ring:
    def __init__(self, src, dst, send, recv, only=None, narrow=None):
        self.src, self.dst, self.send, self.recv = src, dst, send, recv
        self.only, self.narrow = only, narrow
        self.tower, self.at = here()
        self.deep, self.row, self.core = self.at // 4, self.at // 2 % 2, self.at % 2
        self.sibling = (self.tower, self.at + 1 - 2 * self.core)
        self.beside = (self.tower, self.spot(0, 1 - self.row))
        self.sent = []

    def spot(self, k, row):
        return (self.deep + k) % 4 * 4 + row * 2 + self.core

    def forms(self, make):
        def whole(block):
            return block

        def part(block):
            return block.at[:, pl.ds(0, self.narrow)]

        if self.only is not None:
            return [(self.tower == self.only, make(whole))]
        if self.narrow is None:
            return [(None, make(whole))]
        return [(self.tower == 0, make(whole)), (self.tower == 1, make(part))]

    def act(self, forms, name):
        for when, copy in forms:
            action = getattr(copy, name)
            if when is None:
                action()
            else:
                pl.when(when)(action)

    def remote(self, src, slot, sent, landed, device):
        return self.forms(
            lambda cut: remote(
                cut(src), cut(self.dst.at[slot]), self.send.at[sent], self.recv.at[landed], device
            )
        )

    def launch(self, src, slot, index, device):
        forms = self.remote(src, slot, index, index, device)
        self.act(forms, "start")
        self.sent.append(forms)

    def arrived(self, slot, index):
        self.act(self.remote(self.src, slot, index, index, self.sibling), "wait_recv")

    def start(self):
        for k in (1, 3, 2):
            self.launch(self.src, self.at, k - 1, (self.tower, self.spot(k, self.row)))
        self.launch(self.src, self.at, 3, self.beside)
        self.launch(self.src, self.at, 7, self.sibling)
        self.own = self.forms(
            lambda cut: pltpu.make_async_copy(
                cut(self.src), cut(self.dst.at[self.at]), self.send.at[15]
            )
        )
        self.act(self.own, "start")

    def relay_deep(self):
        for k in (1, 3, 2):
            slot = self.spot(4 - k, self.row)
            self.arrived(slot, k - 1)
            self.launch(self.dst.at[slot], slot, 3 + k, self.beside)
            self.launch(self.dst.at[slot], slot, 7 + k, self.sibling)

    def relay_row(self):
        for k in (0, 1, 3, 2):
            slot = self.spot(4 - k, 1 - self.row)
            self.arrived(slot, 3 + k)
            self.launch(self.dst.at[slot], slot, 11 + k, self.sibling)

    def finish(self):
        for index in range(8):
            k, row = index % 4, self.row if index < 4 else 1 - self.row
            slot = (self.deep + 4 - k) % 4 * 4 + row * 2 + 1 - self.core
            self.arrived(slot, 7 + index)
        self.act(self.own, "wait")

    def drain(self):
        for forms in self.sent:
            self.act(forms, "wait_send")


class Chain:
    def __init__(self, src, dst, send, recv, only=None):
        self.src, self.dst, self.send, self.recv = src, dst, send, recv
        self.only = only
        self.tower, self.at = here()
        self.deep, self.row, self.core = self.at // 4, self.at // 2 % 2, self.at % 2
        self.mate = self.deep + 1 - 2 * (self.deep % 2)
        self.half = self.deep // 2
        self.inner = jnp.logical_or(self.deep == 1, self.deep == 2)
        self.sibling = (self.tower, self.at + 1 - 2 * self.core)
        self.beside = (self.tower, self.spot(self.deep, 1 - self.row))
        self.sent = []

    def spot(self, deep, row):
        return deep * 4 + row * 2 + self.core

    def sources(self):
        return self.deep, self.mate, 2 - 2 * self.half, 3 - 2 * self.half

    def act(self, action, when=None):
        if self.only is not None:
            right = self.tower == self.only
            when = right if when is None else jnp.logical_and(when, right)
        if when is None:
            action()
        else:
            pl.when(when)(action)

    def launch(self, src, slot, sent, landed, device, when=None):
        copy = remote(src, self.dst.at[slot], self.send.at[sent], self.recv.at[landed], device)
        self.act(copy.start, when)
        self.sent.append((copy, when))

    def arrived(self, slot, index):
        copy = remote(
            self.src, self.dst.at[slot], self.send.at[0], self.recv.at[index], self.sibling
        )
        self.act(copy.wait_recv)

    def start(self):
        mate = (self.tower, self.spot(self.mate, self.row))
        far = (self.tower, self.spot(2 - self.half, self.row))
        self.launch(self.src, self.at, 1, 1 + self.deep % 2, far)
        self.launch(self.src, self.at, 0, 0, mate)
        self.launch(self.src, self.at, 2, 3, self.beside)
        self.launch(self.src, self.at, 3, 7, self.sibling)
        self.own = pltpu.make_async_copy(self.src, self.dst.at[self.at], self.send.at[16])
        self.act(self.own.start)

    def relay_deep(self):
        mate = (self.tower, self.spot(self.mate, self.row))
        for k in (1, 2, 3):
            slot = self.spot(self.sources()[k], self.row)
            self.arrived(slot, k - 1)
            block = self.dst.at[slot]
            if k > 1:
                self.launch(block, slot, 4 + k, k - 1, mate, self.inner)
            self.launch(block, slot, 7 + k, 3 + k, self.beside)
            self.launch(block, slot, 16 + k, 7 + k, self.sibling)

    def relay_row(self):
        for k, deep in enumerate(self.sources()):
            slot = self.spot(deep, 1 - self.row)
            self.arrived(slot, 3 + k)
            self.launch(self.dst.at[slot], slot, 11 + k, 11 + k, self.sibling)

    def finish(self):
        for k, deep in enumerate(self.sources()):
            for row, base in ((self.row, 7), (1 - self.row, 11)):
                self.arrived(deep * 4 + row * 2 + 1 - self.core, base + k)
        self.act(self.own.wait)

    def drain(self):
        for copy, when in self.sent:
            self.act(copy.wait_send, when)


class Plane:
    def __init__(self, src, via, dst, send, recv):
        self.src, self.via, self.dst, self.send, self.recv = src, via, dst, send, recv
        self.tower, self.at = here()
        self.deep, self.row, self.core = self.at // 4, self.at // 2 % 2, self.at % 2
        self.partner = (1 - self.tower, self.at)
        self.sibling = (self.tower, self.at + 1 - 2 * self.core)
        self.beside = (self.tower, self.at + 2 - 4 * self.row)
        self.sent = []

    def spot(self, k, row):
        return (self.deep + k) % 4 * 2 + row

    def launch(self, src, slot, index, device):
        copy = remote(src, self.via.at[slot], self.send.at[index], self.recv.at[index], device)
        pl.when(self.tower == 1)(copy.start)
        self.sent.append(copy)

    def arrived(self, slot, index):
        copy = remote(
            self.src, self.via.at[slot], self.send.at[index], self.recv.at[index], self.sibling
        )
        pl.when(self.tower == 1)(copy.wait_recv)

    def start(self):
        own = self.spot(0, self.row)
        for k in (1, 3, 2):
            there = self.spot(k, self.row) * 2 + self.core
            self.launch(self.src, own, k - 1, (self.tower, there))
        self.launch(self.src, own, 3, self.beside)
        self.own = pltpu.make_async_copy(self.src, self.via.at[own], self.send.at[7])
        pl.when(self.tower == 1)(self.own.start)

    def relay_deep(self):
        for k in (1, 3, 2):
            slot = self.spot(4 - k, self.row)
            self.arrived(slot, k - 1)
            self.launch(self.via.at[slot], slot, 3 + k, self.beside)

    def relay_row(self):
        for k in range(4):
            self.arrived(self.spot(4 - k, 1 - self.row), 3 + k)
        pl.when(self.tower == 1)(self.own.wait)
        pl.when(self.tower == 1)(self.down().start)

    def down(self):
        return remote(
            self.via, self.dst.at[self.core], self.send.at[8], self.recv.at[7], self.partner
        )

    def across(self, core):
        return remote(
            self.dst.at[core], self.dst.at[core], self.send.at[9], self.recv.at[8], self.sibling
        )

    def land(self):
        pl.when(self.tower == 0)(self.down().wait_recv)
        pl.when(self.tower == 0)(self.across(self.core).start)

    def finish(self):
        pl.when(self.tower == 0)(self.across(1 - self.core).wait_recv)

    def drain(self):
        for copy in self.sent:
            pl.when(self.tower == 1)(copy.wait_send)
        pl.when(self.tower == 1)(self.down().wait_send)
        pl.when(self.tower == 0)(self.across(self.core).wait_send)


def rings(src, dst, send, recv, way=Ring, *narrow):
    return [
        way(
            src.at[part],
            dst.at[part],
            send.at[part],
            recv.at[part],
            0 if part == 2 else None,
            *narrow,
        )
        for part in range(3)
    ]


class Blocks:
    def __init__(self, src, dst, send, recv, shared=1):
        self.src, self.dst, self.send, self.recv = src, dst, send, recv
        self.tower, self.at = here()
        self.shared = shared
        self.sent = []

    def start(self):
        for k in range(1, 16):
            to = (self.at + k) % 16
            copy = remote(
                self.src.at[to // self.shared],
                self.dst.at[self.at],
                self.send.at[k - 1],
                self.recv.at[k - 1],
                (self.tower, to),
            )
            copy.start()
            self.sent.append(copy)
        self.own = pltpu.make_async_copy(
            self.src.at[self.at // self.shared], self.dst.at[self.at], self.send.at[15]
        )
        self.own.start()

    def finish(self):
        for k in range(1, 16):
            remote(
                self.src.at[0],
                self.dst.at[(self.at + 16 - k) % 16],
                self.send.at[k - 1],
                self.recv.at[k - 1],
                (self.tower, self.at),
            ).wait_recv()
        self.own.wait()

    def drain(self):
        for copy in self.sent:
            copy.wait_send()


class Pair:
    def __init__(self, from_zero, zero_dst, from_one, one_dst, sems):
        tower, at = here()
        partner = (1 - tower, at)
        self.tower = tower
        self.up = remote(from_zero, zero_dst, sems.at[0], sems.at[1], partner)
        self.down = remote(from_one, one_dst, sems.at[0], sems.at[1], partner)

    def by_tower(self, zero, one):
        pl.when(self.tower == 0)(zero)
        pl.when(self.tower == 1)(one)

    def start(self):
        self.by_tower(self.up.start, self.down.start)

    def finish(self):
        self.by_tower(self.down.wait_recv, self.up.wait_recv)

    def drain(self):
        self.by_tower(self.up.wait_send, self.down.wait_send)


VECTORS = 5
EXPAND = 2
EMBED = 4
TURN = 8


class Plan:
    def __init__(self, tower, share, rows, per_device):
        self.tower = tower
        self.share = share
        self.rows = rows
        self.chunk = rows * LANES
        self.per_device = per_device
        self.first_slot = [sum(per_device[:p]) for p in range(6)]
        self.first_chunk = [16 * slot for slot in self.first_slot]
        self.slots = sum(per_device) + 1
        self.total = 16 * sum(per_device) + 1
        spans = [self.span(device) for device in range(32)]
        self.counts = sorted({last - first + 1 for first, last in spans})
        self.local = self.counts[-1]

    def span(self, device):
        first = device * self.share // self.chunk
        last = ((device + 1) * self.share - 1) // self.chunk
        return first, min(last, self.total - 1)

    def bounds(self, device):
        first = device * self.share // self.chunk
        last = ((device + 1) * self.share - 1) // self.chunk
        return first, jnp.minimum(last, self.total - 1)

    def pieces(self, p):
        return self.per_device[p] if p < VECTORS else 1

    def target(self, g):
        piece, base, slot, n = (jnp.int32(0), jnp.int32(0), jnp.int32(0), jnp.int32(1))
        for p in range(VECTORS):
            inside = g >= self.first_chunk[p]
            piece = jnp.where(inside, p, piece)
            base = jnp.where(inside, self.first_chunk[p], base)
            slot = jnp.where(inside, self.first_slot[p], slot)
            n = jnp.where(inside, self.per_device[p], n)
        block = (g - base) // n
        at = jnp.where(piece == EXPAND, (block + TURN) % 16, block)
        return piece, at, slot + (g - base) - block * n


def before(me):
    device = (me + 31) % 32
    return device // 16, device % 16


class Deal:
    def __init__(self, plan, s, src, dst, extra, last, sems, only=None, me=None):
        self.plan, self.s, self.src, self.dst = plan, s, src, dst
        self.extra, self.last = extra, last
        self.chunk_send, self.recv, self.edge, self.fetch = sems
        self.tower, self.at = here()
        self.only = only
        self.me = self.tower * 16 + self.at if me is None else me
        self.first, self.last_chunk = plan.bounds(self.me)

    def runs(self, condition):
        return condition if self.only is None else jnp.logical_and(condition, self.tower == self.only)

    def move(self, src, i, piece, at_to, slot, wait):
        tower_to = self.plan.tower
        if not isinstance(piece, int):
            tower_to = jnp.where(piece == EMBED, 1, tower_to)
        far = jnp.logical_or(self.tower != tower_to, at_to != self.at)
        recv = self.recv.at[self.plan.tower, piece]
        copy = remote(
            src,
            self.dst.at[slot],
            self.chunk_send.at[self.s, i],
            recv,
            (tower_to, at_to),
        )
        pl.when(far)(copy.wait_send if wait else copy.start)
        if not wait:
            pl.when(jnp.logical_not(far))(
                pltpu.make_async_copy(src, self.dst.at[slot], recv).start
            )

    def whole(self, early, wait):
        def step(i, carry):
            g = self.first + i
            piece, at_to, slot = self.plan.target(g)
            inside = jnp.logical_and(
                jnp.logical_or(i > 0, self.me == 0),
                jnp.logical_or(
                    g < self.last_chunk, jnp.logical_and(self.me == 31, g < self.plan.total - 1)
                ),
            )
            inside = jnp.logical_and(inside, g <= self.last_chunk)
            inside = jnp.logical_and(inside, g < self.plan.total - 1)
            if early is not None:
                hidden = jnp.logical_and(piece >= 2, piece <= 3)
                inside = jnp.logical_and(inside, jnp.logical_not(hidden) if early else hidden)

            @pl.when(self.runs(inside))
            def _():
                self.move(self.src.at[i], i, piece, at_to, slot, wait)

            return carry

        lax.fori_loop(0, self.plan.local, step, 0)

    def vectors(self, wait):
        @pl.when(self.runs(self.me == 31))
        def _():
            src = self.src.at[self.last_chunk - self.first]

            def each(k, carry):
                self.move(src, self.plan.local + k, VECTORS, k, self.plan.slots - 1, wait)
                return carry

            lax.fori_loop(0, 16, each, 0)

    def fetch_last(self):
        return pltpu.make_async_copy(
            self.src.at[self.last_chunk - self.first], self.last, self.fetch.at[self.s]
        )

    def join(self):
        @pl.when(self.runs(self.me < 31))
        def _():
            self.fetch_last().wait()
            edge = self.edge
            remote(
                self.last,
                self.extra,
                edge.at[self.s, 0],
                edge.at[self.s, 1],
                (self.tower, self.at),
            ).wait_recv()
            self.last[...] = self.last[...] + self.extra[...]
            piece, at_to, slot = self.plan.target(self.last_chunk)
            self.move(self.last, self.plan.local + 16, piece, at_to, slot, False)

    def start_fetch(self):
        pl.when(self.runs(self.me < 31))(self.fetch_last().start)

    def arrived(self, p):
        part = self.dst.at[pl.ds(self.plan.first_slot[p], self.plan.pieces(p))]
        pltpu.make_async_copy(part, part, self.recv.at[self.plan.tower, p]).wait()

    def drain(self):
        self.whole(None, True)
        self.vectors(True)

        @pl.when(self.runs(self.me < 31))
        def _():
            piece, at_to, slot = self.plan.target(self.last_chunk)
            self.move(self.last, self.plan.local + 16, piece, at_to, slot, True)


class Collect:
    def __init__(self, plan, s, src, dst, send, recv):
        self.plan, self.s, self.src, self.dst = plan, s, src, dst
        self.send, self.recv = send, recv
        self.tower, self.at = here()
        self.me = self.tower * 16 + self.at

    def one(self, owner, slot, g, which, wait):
        first, _ = self.plan.bounds(owner)
        far = owner != self.me
        recv = self.recv.at[self.s]
        copy = remote(
            self.src.at[slot],
            self.dst.at[g - first],
            self.send.at[which, slot],
            recv,
            (owner // 16, owner % 16),
        )
        pl.when(far)(copy.wait_send if wait else copy.start)
        if not wait:
            pl.when(jnp.logical_not(far))(
                pltpu.make_async_copy(self.src.at[slot], self.dst.at[g - first], recv).start
            )

    def piece(self, p, wait):
        n = self.plan.pieces(p)

        def step(i, carry):
            slot = self.plan.first_slot[p] + i
            block = (self.at + 16 - TURN) % 16 if p == EXPAND else self.at
            g = self.plan.first_chunk[p] + block * n + i if p < VECTORS else self.plan.total - 1
            low = g * self.plan.chunk // self.plan.share
            high = jnp.minimum(((g + 1) * self.plan.chunk - 1) // self.plan.share, 31)
            self.one(low, slot, g, 0, wait)
            pl.when(high != low)(lambda: self.one(high, slot, g, 1, wait))
            return carry

        if p == VECTORS:


            @pl.when(self.at == 0)
            def _():
                step(0, 0)

        else:
            lax.fori_loop(0, n, step, 0)

    def finish(self):
        first, last = self.plan.bounds(self.me)
        held = last - first + 1
        for n in self.plan.counts:

            @pl.when(held == n)
            def _():
                part = self.dst.at[pl.ds(0, n)]
                pltpu.make_async_copy(part, part, self.recv.at[self.s]).wait()


SEQS = 16
HEADS = 16


class Tower:
    def __init__(self, index, width, hidden, length, room, run, causal):
        self.index = index
        self.width = width
        self.hidden = hidden
        self.length = length
        self.room = room
        self.run = run
        self.causal = causal
        self.heads = width // HEAD
        self.block = width // 16
        self.part = hidden // 8
        self.reduce_rows = hidden // 16


TOWERS = (
    Tower(0, D_IMG, FF_IMG, 50, 64, 10, False),
    Tower(1, D_TXT, FF_TXT, 77, 80, 11, True),
)
ROOM = 80
WIDTH = D_IMG
PART = FF_IMG // 8


def each_tower(run):
    tower = lax.axis_index("tower")
    for kind in TOWERS:
        pl.when(tower == kind.index)(functools.partial(run, kind))


def dot_nn(a, b):
    return lax.dot_general(a, b, (((1,), (0,)), ((), ())), preferred_element_type=WIDE)


def dot_nt(a, b):
    return lax.dot_general(a, b, (((1,), (1,)), ((), ())), preferred_element_type=WIDE)


def dot_tn(a, b):
    return lax.dot_general(a, b, (((0,), (0,)), ((), ())), preferred_element_type=WIDE)


def standardise(rows):
    centred = rows - jnp.mean(rows, axis=-1, keepdims=True)
    spread = jnp.mean(centred * centred, axis=-1, keepdims=True)
    rate = lax.rsqrt(spread + 1e-05)
    return centred * rate, rate


def norm_back(grad, gain, hat, rate):
    scaled = grad * gain
    return rate * (
        scaled
        - jnp.mean(scaled, axis=-1, keepdims=True)
        - hat * jnp.mean(scaled * hat, axis=-1, keepdims=True)
    )


def spans(kind):
    return [
        (lo, min(lo + 512, kind.width), lo // HEAD, (min(lo + 512, kind.width) - lo) // HEAD)
        for lo in range(0, kind.width, 512)
    ]


def head_rows(rows, span):
    lo, hi, _, n = span
    part = rows[:, lo:hi]
    owner = lax.broadcasted_iota(jnp.int32, part.shape, 1) // HEAD
    nothing = jnp.zeros_like(part)
    return jnp.concatenate([jnp.where(owner == h, part, nothing) for h in range(n)], axis=0)


def from_head_rows(rows, span):
    _, _, _, n = span
    owner = lax.broadcasted_iota(jnp.int32, (SEQS, rows.shape[1]), 1) // HEAD
    total = jnp.zeros((SEQS, rows.shape[1]), rows.dtype)
    for h in range(n):
        total = jnp.where(owner == h, rows[h * SEQS : (h + 1) * SEQS], total)
    return total


def side_by_side(parts):
    return parts[0] if len(parts) == 1 else jnp.concatenate(parts, axis=1)


def get_rows(ref, place, width):
    return side_by_side([ref[c, place, :] for c in range(width // LANES)])


def put_rows(ref, place, value):
    for c in range(value.shape[1] // LANES):
        ref[c, place, :] = value[:, c * LANES : (c + 1) * LANES]


def matrix(ref, kind, start, width):
    return jnp.concatenate(
        [
            ref[part, at, :, start : start + width]
            for at in range(16)
            for part in range(kind.block // 16)
        ],
        axis=0,
    )


def embed_matrix(refs, kind):
    if kind.index == 1:
        return matrix(refs[1], kind, 0, EMB)
    return jnp.concatenate([refs[0][at % 2, at // 2] for at in range(16)], axis=0)


def vector(vec_ref, kind, row):
    return vec_ref[row : row + 1, : kind.width]


def pieces_of(kind):
    return (
        (kind.block, 3 * kind.width),
        (kind.block, kind.width),
        (kind.block, kind.hidden),
        (kind.reduce_rows, kind.width),
        (kind.block, EMB),
        (16, kind.width),
    )


def lane_blocks(kind, plan, p):
    height, width = pieces_of(kind)[p]
    pitch = width // LANES
    base = plan.first_slot[p] * plan.rows if p < VECTORS else (plan.slots - 1) * plan.rows
    return [(c, pl.ds(base + c, height, stride=pitch)) for c in range(pitch)]


def lift(kind, plan, p, slots, flat):
    n = plan.pieces(p)
    slot = plan.first_slot[p]
    rows = slots[slot : slot + n].reshape(n * plan.rows, LANES)
    flat[slot * plan.rows : (slot + n) * plan.rows, :] = rows.astype(WIDE)
    return [(c, flat[place, :]) for c, place in lane_blocks(kind, plan, p)]


def drop(kind, plan, p, value, slots, flat):
    for c, place in lane_blocks(kind, plan, p):
        flat[place, :] = value(c)
    n = plan.pieces(p)
    slot = plan.first_slot[p]
    rows = flat[slot * plan.rows : (slot + n) * plan.rows, :]
    slots[slot : slot + n] = rows.reshape(n, plan.rows, LANES).astype(LOW)


def expand_matrix(ref, kind):
    return jnp.concatenate(
        [
            ref[at % 2, at // 2, : kind.block, : kind.part]
            for at in ((block + TURN) % 16 for block in range(16))
        ],
        axis=0,
    )


def reduce_matrix(ref, kind):
    return ref[:, : kind.reduce_rows, : kind.width].reshape(kind.part, kind.width)


def hidden_bias(vec_ref, kind):
    chip = lax.axis_index("dp") // 2
    whole = vec_ref[...]
    row = lax.broadcasted_iota(jnp.int32, (16, 1), 0)
    line = jnp.sum(jnp.where(row == 10 + chip // 2, whole, 0.0), axis=0, keepdims=True)
    return jnp.where(
        chip % 2 == 0, line[:, : kind.part], line[:, kind.part : 2 * kind.part]
    )


def hidden_kernel(second_ref, raise_ref, reduce_ref, vec_ref, part_ref, raised_ref):
    def run(kind):
        width = kind.width
        rows = second_ref[:, :, :width].reshape(8 * SEQS, width)
        raised = dot_nn(rows, expand_matrix(raise_ref, kind)) + hidden_bias(vec_ref, kind)
        raised_ref[:, : kind.part] = raised
        active = (raised * jax.nn.sigmoid(1.702 * raised)).astype(LOW)
        part = dot_nn(active, reduce_matrix(reduce_ref, kind))
        part_ref[:, :, :width] = part.reshape(8, SEQS, width).astype(LOW)

    each_tower(run)


def hidden_back_kernel(
    grad_ref,
    second_ref,
    raised_ref,
    raise_ref,
    reduce_ref,
    back_ref,
    raise_grad_ref,
    reduce_keep_ref,
    reduce_send_ref,
    bias_ref,
    whole,
):
    def run(kind):
        width, part = kind.width, kind.part
        grads = grad_ref[:, :, :width].reshape(8 * SEQS, width)
        rows = second_ref[:, :, :width].reshape(8 * SEQS, width)
        raised = raised_ref[:, :part]
        gate = jax.nn.sigmoid(1.702 * raised)
        active = (raised * gate).astype(LOW)
        slope = gate + 1.702 * raised * gate * (1.0 - gate)
        raised_grad = dot_nt(grads, reduce_matrix(reduce_ref, kind)) * slope
        low_grad = raised_grad.astype(LOW)
        bias_ref[0:1, :part] = jnp.sum(low_grad.astype(WIDE), axis=0, keepdims=True)
        back = dot_nt(low_grad, expand_matrix(raise_ref, kind))
        back_ref[:, :, :width] = back.reshape(8, SEQS, width).astype(LOW)
        raise_grad = dot_tn(rows, low_grad).reshape(16, kind.block, part).astype(LOW)
        for block in range(16):
            at = (block + TURN) % 16
            raise_grad_ref[at % 2, at // 2, : kind.block, :part] = raise_grad[block]
        whole[:part, :width] = dot_tn(active, grads)
        core = lax.axis_index("dp") % 2
        n = kind.reduce_rows
        keep = pl.multiple_of(core * n, 64)
        send = pl.multiple_of((1 - core) * n, 64)
        reduce_keep_ref[:n, :width] = whole[pl.ds(keep, n), :width]
        reduce_send_ref[:n, :width] = whole[pl.ds(send, n), :width].astype(LOW)

    each_tower(run)


def embed_kernel(part_ref, middle_ref, gat_ref, vec_ref, emb_ref, final_ref, pooled_ref, proj_ref):
    def run(kind):
        width = kind.width
        final = (
            middle_ref[:, :width]
            + jnp.sum(part_ref[:, :, :width].astype(WIDE), axis=0)
            + vector(vec_ref, kind, 7)
        )
        final_ref[:, :width] = final
        hat, _ = standardise(final)
        pooled = (hat * vector(vec_ref, kind, 8) + vector(vec_ref, kind, 9)).astype(LOW)
        pooled_ref[:, :width] = pooled
        proj = dot_nn(pooled, embed_matrix(gat_ref, kind))
        proj_ref[...] = proj
        size = jnp.sum(proj * proj, axis=-1, keepdims=True) + 1e-06
        emb_ref[...] = (proj * lax.rsqrt(size)).astype(LOW)

    each_tower(run)


def objective_kernel(
    scale_ref,
    all_ref,
    valid_ref,
    final_ref,
    proj_ref,
    gat_ref,
    vec_ref,
    low_ref,
    grad_ref,
    proj_grad_ref,
    final_vec_ref,
    loss_ref,
    scale_new_ref,
    own_scr,
):
    def ordered(which):
        blocks = []
        for half in range(2):
            for j in range(16):
                rows = all_ref[j % 2, which * 8 + j // 2].astype(WIDE)
                blocks.append(rows[half * 8 : half * 8 + 8])
        return jnp.concatenate(blocks, axis=0).astype(LOW)

    img, txt = ordered(0), ordered(1)
    total = img.shape[0]
    scale = jnp.exp(jnp.full((1, 1), scale_ref[0], WIDE))
    lines = []
    for d in range(32):
        rows = valid_ref[d % 2, d // 2].astype(WIDE)
        lines.append(jnp.concatenate([rows[:8], rows[8:]], axis=1))
    allowed = jnp.concatenate(lines, axis=0) > 0
    same = lax.broadcasted_iota(jnp.int32, (total, total), 0) == lax.broadcasted_iota(
        jnp.int32, (total, total), 1
    )
    same = same.astype(WIDE)

    def side(left, right):
        logits = scale * dot_nt(left, right)
        masked = jnp.where(allowed, logits, -1e30)
        top = jnp.max(masked, axis=1, keepdims=True)
        lse = jnp.log(jnp.sum(jnp.exp(masked - top), axis=1, keepdims=True)) + top
        terms = 0.5 * (jnp.where(allowed, jnp.exp(logits - lse), 0.0) - same)
        loss = 0.5 * (
            jnp.sum(lse, axis=0, keepdims=True)
            - jnp.sum(jnp.sum(logits * same, axis=1, keepdims=True), axis=0, keepdims=True)
        )
        rate = jnp.sum(jnp.sum(terms * logits, axis=1, keepdims=True), axis=0, keepdims=True)
        return (scale * terms).astype(LOW), loss, rate

    row_back, row_loss, row_rate = side(img, txt)
    col_back, col_loss, col_rate = side(txt, img)
    loss_ref[0] = jnp.sum(row_loss + col_loss) / total
    parts = advance(
        scale_ref[0], scale_ref[1], scale_ref[2], jnp.sum(row_rate + col_rate), scale_rate
    )
    for k in range(3):
        scale_new_ref[k] = parts[k]

    def run(kind):
        width = kind.width
        if kind.index == 0:
            emb_grad = dot_nn(row_back, txt) + dot_tn(col_back, txt)
        else:
            emb_grad = dot_nn(col_back, img) + dot_tn(row_back, img)
        own_scr[...] = emb_grad
        at = lax.axis_index("dp")
        mine = jnp.concatenate(
            [
                own_scr[pl.ds(pl.multiple_of(half * 128 + at * 8, 8), 8), :]
                for half in range(2)
            ],
            axis=0,
        )
        proj = proj_ref[...]
        size = jnp.sum(proj * proj, axis=-1, keepdims=True) + 1e-06
        along = jnp.sum(proj * mine, axis=-1, keepdims=True)
        proj_grad = ((mine - proj * along / size) * lax.rsqrt(size)).astype(LOW)
        proj_grad_ref[...] = proj_grad
        pooled_grad = dot_nt(proj_grad, embed_matrix(gat_ref, kind))
        hat, rate = standardise(final_ref[:, :width])
        final_vec_ref[0:1, :width] = jnp.sum(pooled_grad * hat, axis=0, keepdims=True)
        final_vec_ref[1:2, :width] = jnp.sum(pooled_grad, axis=0, keepdims=True)
        final_grad = norm_back(pooled_grad, vector(vec_ref, kind, 8), hat, rate)
        grad_ref[:, :width] = final_grad
        low = final_grad.astype(LOW)
        low_ref[:, :width] = low
        final_vec_ref[2:3, :width] = jnp.sum(low.astype(WIDE), axis=0, keepdims=True)

    each_tower(run)


def step_kernel(
    plans,
    ends_ref,
    scale_ref,
    img_src,
    txt_src,
    valid_ref,
    img_own,
    txt_own,
    loss_ref,
    scale_new_ref,
    img_keep,
    txt_keep,
    img_chunks,
    txt_chunks,
    second_ref,
    middle_ref,
    query_ref,
    keyed_ref,
    mixture_ref,
    weight_ref,
    first_ref,
    first_rows,
    img_in,
    txt_in,
    ask_ref,
    mix_ref,
    emb_ref,
    vec_ref,
    raise_ref,
    reduce_ref,
    pairs_ref,
    img_slots,
    txt_slots,
    img_extra,
    txt_extra,
    img_last,
    txt_last,
    txt_relay,
    txt_over,
    txt_ending,
    flat,
    ask_block,
    mix_block,
    emb_block,
    plane_block,
    plane_via,
    plane_ref,
    raise_block,
    reduce_block,
    mask_block,
    top_scr,
    at_scr,
    score_scr,
    low_scr,
    grad_ref,
    pooled_ref,
    proj_grad_ref,
    final_vec_ref,
    raise_grad_ref,
    reduce_keep_ref,
    reduce_send_ref,
    bias_ref,
    backs_ref,
    seconds,
    part,
    parts,
    raised,
    emb,
    all_embs,
    final,
    proj,
    low,
    lows,
    back,
    own_scr,
    whole,
    img_send,
    txt_send,
    img_home,
    txt_home,
    rows_grad,
    middle_scr,
    second_scr,
    valued_scr,
    turn_scr,
    shared_scr,
    slope_scr,
    left_scr,
    left_block,
    turn_block,
    left_all,
    turn_all,
    early_block,
    early_all,
    late_block,
    late_all,
    lines_block,
    lines_all,
    raise_half,
    risen_block,
    raise_all,
    reduce_in,
    img_home_slots,
    txt_home_slots,
    gains,
    top_grad_scr,
    deal_send,
    deal_recv,
    deal_edge,
    deal_fetch,
    relay_sems,
    ask_send,
    ask_recv,
    mix_send,
    mix_recv,
    emb_send,
    emb_recv,
    plane_send,
    plane_recv,
    raise_send,
    raise_recv,
    reduce_sems,
    pair_sems,
    mask_send,
    mask_recv,
    group_send,
    group_recv,
    embs_send,
    embs_recv,
    home_sems,
    risen_send,
    risen_recv,
    left_send,
    left_recv,
    turn_send,
    turn_recv,
    early_send,
    early_recv,
    late_send,
    late_recv,
    lines_send,
    lines_recv,
    home_pair_sems,
    collect_send,
    collect_recv,
):
    tower, at = here()
    core = at % 2
    me = tower * 16 + at
    sibling = (tower, at + 1 - 2 * core)
    greet(everyone(tower, at))
    deal_sems = (deal_send, deal_recv, deal_edge, deal_fetch)
    deals = [
        Deal(plans[0], 0, img_src, img_slots, img_extra, img_last, deal_sems),
        Deal(plans[1], 1, txt_src, txt_slots, txt_extra, txt_last, deal_sems, 1, 16 + at),
        Deal(plans[1], 2, txt_relay, txt_slots, txt_over, txt_ending, deal_sems, 1, at),
    ]
    relay = remote(txt_src, txt_relay, relay_sems.at[0], relay_sems.at[1], (1 - tower, at))
    behind = (jnp.int32(1), (at + 15) % 16)
    head = remote(img_src.at[0], img_extra, deal_edge.at[0, 0], deal_edge.at[0, 1], before(me))
    kept = remote(txt_src.at[0], txt_extra, deal_edge.at[1, 0], deal_edge.at[1, 1], behind)
    over = remote(txt_src.at[0], txt_over, deal_edge.at[2, 0], deal_edge.at[2, 1], behind)
    heads = (
        (me > 0, head),
        (me > 16, kept),
        (jnp.logical_and(me > 0, me <= 16), over),
    )
    pair = Pair(txt_own, txt_in, img_own, img_in, pair_sems)
    asks = rings(ask_block, ask_ref, ask_send, ask_recv, Ring, 2 * D_TXT)
    mixes = rings(mix_block, mix_ref, mix_send, mix_recv, Ring, 2 * D_TXT)
    embeds = [
        Chain(emb_block.at[part], emb_ref.at[part], emb_send.at[part], emb_recv.at[part], 1)
        for part in range(2)
    ]
    plane = Plane(plane_block, plane_via, plane_ref, plane_send, plane_recv)
    rise = Group(raise_block, raise_ref, raise_send, raise_recv)
    fall = remote(
        reduce_block, reduce_ref.at[core], reduce_sems.at[0], reduce_sems.at[1], sibling
    )
    fall_own = pltpu.make_async_copy(reduce_block, reduce_ref.at[core], reduce_sems.at[2])
    masks = Spread(mask_block, pairs_ref, mask_send, mask_recv)
    rows = valid_ref[...].astype(WIDE)
    mask_block[...] = jnp.concatenate([rows[:, :LANES], rows[:, LANES:]], axis=0).astype(LOW)

    for when, copy in heads:
        pl.when(when)(copy.start)
    pl.when(tower == 0)(relay.start)
    for deal in deals[:2]:
        deal.start_fetch()
        deal.vectors(False)
    deals[0].whole(True, False)
    deals[1].whole(True, False)
    deals[0].whole(False, False)
    deals[1].whole(False, False)
    pair.start()
    deals[0].join()
    deals[1].join()
    pl.when(tower == 1)(relay.wait_recv)
    deals[2].start_fetch()
    deals[2].whole(True, False)
    deals[2].join()
    deals[2].whole(False, False)

    def put(ref, lane, value):
        if len(ref.shape) == 2:
            ref[: value.shape[0], lane : lane + LANES] = value
        else:
            for part in range(value.shape[0] // 16):
                ref[part, :, lane : lane + LANES] = value[part * 16 : (part + 1) * 16]

    def lift_to(kind, p, ref, start):
        slots = (img_slots, txt_slots)[kind.index]
        for c, value in lift(kind, plans[kind.index], p, slots, flat):
            lane = start + c * LANES
            put(ref, lane, value.astype(ref.dtype))

    def tokens_of(kind, half):
        own, arrived = ((img_own, img_in), (txt_own, txt_in))[kind.index]
        return own if half == kind.index else arrived

    def steps(kind):
        return [(t, kind.run) for t in range(0, kind.length, kind.run)]

    def is_end(kind, half, t, n):
        row = lax.broadcasted_iota(jnp.int32, (8, 1), 0)
        ends = jnp.zeros((8, 1), jnp.int32)
        for i in range(8):
            ends = jnp.where(row == i, ends_ref[(half * 16 + at) * 8 + i], ends)
        position = lax.broadcasted_iota(jnp.int32, (n, 8, 1), 0) + t
        return (position == ends[None]).astype(WIDE)

    def normalise(kind, half):
        width, room = kind.width, kind.room
        ref = tokens_of(kind, half)
        gain, shift = vector(vec_ref, kind, 0), vector(vec_ref, kind, 1)
        tops, raws = jnp.zeros((8, width), WIDE), jnp.zeros((8, width), WIDE)
        for t, n in steps(kind):
            rows = ref[t : t + n].astype(WIDE).reshape(n * 8, width)
            hat, _ = standardise(rows)
            first = (hat * gain + shift).astype(LOW).astype(WIDE)
            put_rows(first_rows, pl.ds(t * 8, n * 8), first)
            if kind.causal:
                chosen = is_end(kind, half, t, n)
                tops = tops + jnp.sum(first.reshape(n, 8, width) * chosen, axis=0)
                raws = raws + jnp.sum(rows.reshape(n, 8, width) * chosen, axis=0)
            elif t == 0:
                tops, raws = first[:8], rows[:8]
        top_scr[half * 8 : half * 8 + 8, :width] = tops
        at_scr[half * 8 : half * 8 + 8, :width] = raws
        spare = (room - kind.length) * 8
        put_rows(first_rows, pl.ds(kind.length * 8, spare), jnp.zeros((spare, width), WIDE))
        for i in range(8):
            line = get_rows(first_rows, pl.ds(i, room, stride=8), width)
            first_ref[half * 8 + i, :room, :width] = line.astype(LOW)

    def begin(kind):
        deal = deals[kind.index]
        deal.arrived(VECTORS)
        lift_to(kind, VECTORS, vec_ref, 0)
        normalise(kind, kind.index)

    each_tower(begin)

    def place_inputs(kind):
        deals[kind.index].arrived(0)
        slots = (img_slots, txt_slots)[kind.index]
        per = kind.width // LANES
        for c, value in lift(kind, plans[kind.index], 0, slots, flat):
            ref, lane = ask_block, c * LANES
            if c >= 2 * per:
                ref, lane = mix_block, lane - 2 * kind.width
            put(ref, lane, value.astype(LOW))

    each_tower(place_inputs)
    for ring in asks:
        ring.start()

    def place_hidden(kind):
        deal, plan = deals[kind.index], plans[kind.index]
        slots = (img_slots, txt_slots)[kind.index]
        deal.arrived(2)
        per = kind.part // LANES
        for c, value in lift(kind, plan, 2, slots, flat):
            lane = c % per * LANES
            raise_block[c // per, : kind.block, lane : lane + LANES] = value.astype(LOW)
        deal.arrived(3)
        lift_to(kind, 3, reduce_block, 0)

    def place_rest(kind):
        deals[kind.index].arrived(1)
        lift_to(kind, 1, mix_block, kind.width)
        if kind.index == 1:
            deals[1].arrived(EMBED)
            lift_to(kind, EMBED, emb_block, 0)
            deals[0].arrived(EMBED)
            for c, value in lift(TOWERS[0], plans[0], EMBED, img_slots, flat):
                plane_block[:, c * LANES : (c + 1) * LANES] = value.astype(LOW)

    each_tower(place_rest)

    def question(kind):
        width = kind.width
        tops = top_scr[:, :width].astype(LOW)
        query = dot_nn(tops, matrix(ask_ref, kind, 0, width)) + vector(vec_ref, kind, 2)
        query = query.astype(LOW)
        query_ref[:, :width] = query
        for span in spans(kind):
            lo, hi, first_head, n = span
            put_rows(
                keyed_ref,
                pl.ds(first_head * SEQS, n * SEQS),
                dot_nt(head_rows(query, span), matrix(ask_ref, kind, width + lo, hi - lo)) * 0.125,
            )
        dead = (HEADS - kind.heads) * SEQS
        put_rows(keyed_ref, pl.ds(kind.heads * SEQS, dead), jnp.zeros((dead, width), WIDE))

    for ask in asks:
        ask.relay_deep()
    for mix in mixes:
        mix.start()
    for embed in embeds:
        embed.start()
    plane.start()
    for ask in asks:
        ask.relay_row()
    each_tower(place_hidden)
    rise.start()
    fall.start()
    fall_own.start()
    pair.finish()
    each_tower(lambda kind: normalise(kind, 1 - kind.index))
    masks.start()
    for ask in asks:
        ask.finish()
    each_tower(question)
    for ring in (*mixes, *embeds):
        ring.relay_deep()
    plane.relay_deep()

    def score(kind):
        width, room = kind.width, kind.room
        lane = lax.broadcasted_iota(jnp.int32, (HEADS, room), 1)
        for s in range(SEQS):
            keys = get_rows(keyed_ref, pl.ds(s, HEADS, stride=SEQS), width).astype(LOW)
            scores = dot_nt(keys, first_ref[s, :room, :width])
            if kind.causal:
                allowed = lane <= ends_ref[(s // 8 * 16 + at) * 8 + s % 8]
            else:
                allowed = lane < kind.length
            score_scr[s * HEADS : (s + 1) * HEADS, :room] = jnp.where(allowed, scores, -1e30)
        scores = score_scr[:, :room]
        raw = jnp.exp(scores - jnp.max(scores, axis=-1, keepdims=True))
        weights = raw / jnp.sum(raw, axis=-1, keepdims=True)
        head = lax.broadcasted_iota(jnp.int32, (SEQS * HEADS, 1), 0) % HEADS
        weights = jnp.where(head < kind.heads, weights, 0.0)
        weight_ref[:, :room] = weights
        low_scr[: SEQS * HEADS, :room] = weights.astype(LOW)

    each_tower(score)
    for ring in (*mixes, *embeds):
        ring.relay_row()
    plane.relay_row()

    def mixture(kind):
        width, room = kind.width, kind.room
        for s in range(SEQS):
            mixed = dot_nn(
                low_scr[s * HEADS : (s + 1) * HEADS, :room], first_ref[s, :room, :width]
            )
            put_rows(mixture_ref, pl.ds(s, HEADS, stride=SEQS), mixed)
        totals = jnp.sum(
            low_scr[: SEQS * HEADS, :room].astype(WIDE), axis=-1, keepdims=True
        )
        score_scr[...] = jnp.broadcast_to(totals, score_scr.shape)

    each_tower(mixture)

    for mix in mixes:
        mix.finish()

    def answer(kind):
        width = kind.width
        mixed = []
        bias = vector(vec_ref, kind, 3)
        for span in spans(kind):
            lo, hi, first_head, n = span
            z = get_rows(mixture_ref, pl.ds(first_head * SEQS, n * SEQS), width).astype(LOW)
            valued = dot_nn(z, matrix(mix_ref, kind, lo, hi - lo))
            totals = jnp.concatenate(
                [score_scr[pl.ds(first_head + h, SEQS, stride=HEADS), 0:1] for h in range(n)],
                axis=0,
            )
            mixed.append(from_head_rows(valued + totals * bias[:, lo:hi], span))
        mixed = side_by_side(mixed).astype(LOW)
        middle = (
            at_scr[:, :width]
            + dot_nn(mixed, matrix(mix_ref, kind, width, width))
            + vector(vec_ref, kind, 4)
        )
        middle_ref[:, :width] = middle
        hat, _ = standardise(middle)
        second_ref[:, :width] = (
            hat * vector(vec_ref, kind, 5) + vector(vec_ref, kind, 6)
        ).astype(LOW)
        put_rows(mixture_ref, pl.ds(12 * SEQS, SEQS), top_scr[:, :width])
        put_rows(mixture_ref, pl.ds(13 * SEQS, SEQS), mixed.astype(WIDE))

    each_tower(answer)
    rise.relay()
    masks.relay()
    for embed in embeds:
        embed.finish()
    rise.finish()
    fall_own.wait()
    remote(
        reduce_block, reduce_ref.at[1 - core], reduce_sems.at[0], reduce_sems.at[1], sibling
    ).wait_recv()

    sent = group_exchange(False, second_ref, seconds, group_send.at[0], group_recv.at[0])
    hidden_kernel(seconds, raise_ref, reduce_ref, vec_ref, part, raised)
    plane.land()
    sent += group_exchange(True, part, parts, group_send.at[1], group_recv.at[1])
    plane.finish()
    embed_kernel(parts, middle_ref, (plane_ref, emb_ref), vec_ref, emb, final, pooled_ref, proj)
    embs = Spread(emb, all_embs, embs_send, embs_recv)
    embs.start()
    masks.finish()
    embs.relay()
    embs.finish()
    objective_kernel(
        scale_ref,
        all_embs,
        pairs_ref,
        final,
        proj,
        (plane_ref, emb_ref),
        vec_ref,
        low,
        grad_ref,
        proj_grad_ref,
        final_vec_ref,
        loss_ref,
        scale_new_ref,
        own_scr,
    )
    sent += group_exchange(False, low, lows, group_send.at[2], group_recv.at[2])
    hidden_back_kernel(
        lows,
        seconds,
        raised,
        raise_ref,
        reduce_ref,
        back,
        raise_grad_ref,
        reduce_keep_ref,
        reduce_send_ref,
        bias_ref,
        whole,
    )
    sent += group_exchange(True, back, backs_ref, group_send.at[3], group_recv.at[3])
    halves = remote(
        raise_grad_ref.at[1 - core], raise_half, home_sems.at[0], home_sems.at[1], sibling
    )
    fallen = remote(reduce_send_ref, reduce_in, home_sems.at[2], home_sems.at[3], sibling)
    halves.start()
    fallen.start()
    risen_group = Group(risen_block, raise_all, risen_send, risen_recv, False)

    lefts = Blocks(left_block, left_all, left_send, left_recv)
    turns = Blocks(turn_block, turn_all, turn_send, turn_recv)
    early = Chain(early_block, early_all, early_send, early_recv)
    late = Ring(late_block, late_all, late_send, late_recv)
    home_pair = Pair(img_send, img_home, txt_send, txt_home, home_pair_sems)
    collects = [
        Collect(plans[0], 0, img_home_slots, img_chunks, collect_send.at[0], collect_recv),
        Collect(plans[1], 1, txt_home_slots, txt_chunks, collect_send.at[1], collect_recv),
    ]

    def outputs(kind):
        width = kind.width
        second_grad = jnp.sum(backs_ref[:, :, :width].astype(WIDE), axis=0)
        second_scr[:, :width] = second_grad
        hat, rate = standardise(middle_ref[:, :width])
        middle_grad = grad_ref[:, :width] + norm_back(
            second_grad, vector(vec_ref, kind, 5), hat, rate
        )
        middle_scr[:, :width] = middle_grad
        output_grad = middle_grad.astype(LOW)
        mixed_grad = dot_nt(output_grad, matrix(mix_ref, kind, width, width)).astype(LOW)
        early_block[:, 0:width] = query_ref[:, :width]
        early_block[:, WIDTH : WIDTH + width] = mixed_grad
        early_block[:, 2 * WIDTH : 2 * WIDTH + width] = output_grad
        early_block[:, 3 * WIDTH : 3 * WIDTH + EMB] = proj_grad_ref[...]
        left_scr[:, :width] = get_rows(mixture_ref, slice(None), width)
        left_scr[14 * SEQS : 15 * SEQS, :width] = pooled_ref[:, :width].astype(WIDE)
        left_scr[15 * SEQS :, :width] = jnp.zeros((SEQS, width), WIDE)

    each_tower(outputs)
    early.start()

    def turned(kind):
        width, block = kind.width, kind.block
        left_block[:, :block, :] = left_scr[:, :width].T.reshape(16, block, 256).astype(LOW)

    each_tower(turned)
    lefts.start()

    def values(kind):
        width = kind.width
        mixed_grad = early_block[:, WIDTH : WIDTH + width]
        bias = vector(vec_ref, kind, 3)
        dead = kind.heads * SEQS
        put_rows(valued_scr, pl.ds(dead, 256 - dead), jnp.zeros((256 - dead, width), WIDE))
        shared_scr[dead:, :] = jnp.zeros((256 - dead, LANES), WIDE)
        for span in spans(kind):
            lo, hi, first_head, n = span
            rows = head_rows(mixed_grad, span)
            place = pl.ds(first_head * SEQS, n * SEQS)
            put_rows(valued_scr, place, dot_nt(rows, matrix(mix_ref, kind, lo, hi - lo)))
            constant = jnp.sum(rows.astype(WIDE) * bias[:, lo:hi], axis=-1, keepdims=True)
            shared_scr[place, :] = jnp.broadcast_to(constant, (n * SEQS, LANES))

    each_tower(values)
    halves.wait_recv()
    risen_block[...] = (
        raise_grad_ref[core].astype(WIDE) + raise_half[...].astype(WIDE)
    ).astype(LOW)
    risen_group.start()

    def slopes(kind):
        width, room = kind.width, kind.room
        for s in range(SEQS):
            line = pl.ds(s, HEADS, stride=SEQS)
            slope = dot_nt(
                get_rows(valued_scr, line, width).astype(LOW), first_ref[s, :room, :width]
            )
            slope_scr[s * HEADS : (s + 1) * HEADS, :room] = slope + shared_scr[line, 0:1]
        weights = weight_ref[:, :room]
        slope = slope_scr[:, :room]
        slope = weights * (slope - jnp.sum(weights * slope, axis=-1, keepdims=True))
        both = jnp.concatenate(
            [slope.reshape(SEQS, HEADS, room), weights.reshape(SEQS, HEADS, room)], axis=1
        )
        low_scr[:, :room] = both.reshape(2 * SEQS * HEADS, room).astype(LOW)

    each_tower(slopes)
    early.relay_deep()

    def tokens(kind):
        width, room = kind.width, kind.room
        for s in range(SEQS):
            line = pl.ds(s, HEADS, stride=SEQS)
            both = low_scr[2 * s * HEADS : 2 * (s + 1) * HEADS, :room]
            first = first_ref[s, :room, :width]
            put_rows(turn_scr, line, dot_nn(both[:HEADS], first))
            right = jnp.concatenate(
                [get_rows(keyed_ref, line, width), get_rows(valued_scr, line, width)], axis=0
            )
            put_rows(
                rows_grad.at[s // 8],
                pl.ds(s % 8, room, stride=8),
                dot_tn(both, right.astype(LOW)),
            )

    each_tower(tokens)
    early.relay_row()

    def queries(kind):
        width, block = kind.width, kind.block
        grads = []
        for span in spans(kind):
            lo, hi, first_head, n = span
            rows = get_rows(turn_scr, pl.ds(first_head * SEQS, n * SEQS), width).astype(LOW)
            back = dot_nn(rows, matrix(ask_ref, kind, width + lo, hi - lo)) * 0.125
            grads.append(from_head_rows(back, span))
        query_grad = side_by_side(grads).astype(LOW)
        late_block[:, :width] = query_grad
        top_grad_scr[:, :width] = dot_nt(query_grad, matrix(ask_ref, kind, 0, width))
        turn_block[:, :block, :] = (
            get_rows(turn_scr, slice(None), width).T.reshape(16, block, 256).astype(LOW)
        )

    each_tower(queries)
    late.start()
    turns.start()
    gains[...] = jnp.zeros_like(gains)

    def finish(kind, half):
        width = kind.width
        ref = tokens_of(kind, half)
        keep, send = ((img_keep, img_send), (txt_keep, txt_send))[kind.index]
        gain = vector(vec_ref, kind, 0)
        top = top_grad_scr[half * 8 : half * 8 + 8, :width]
        low = middle_scr[half * 8 : half * 8 + 8, :width]
        gain_sum = jnp.zeros((1, width), WIDE)
        shift_sum = jnp.zeros((1, width), WIDE)
        for t, n in steps(kind):
            hat, rate = standardise(ref[t : t + n].astype(WIDE).reshape(n * 8, width))
            grad = get_rows(rows_grad.at[half], pl.ds(t * 8, n * 8), width)
            chosen = None
            if kind.causal:
                chosen = is_end(kind, half, t, n)
            elif t == 0:
                chosen = (lax.broadcasted_iota(jnp.int32, (n, 8, 1), 0) == 0).astype(WIDE)
            if chosen is not None:
                grad = grad + (chosen * top[None]).reshape(n * 8, width)
            gain_sum += jnp.sum(grad * hat, axis=0, keepdims=True)
            shift_sum += jnp.sum(grad, axis=0, keepdims=True)
            result = norm_back(grad, gain, hat, rate)
            if chosen is not None:
                result = result + (chosen * low[None]).reshape(n * 8, width)
            result = result.reshape(n, 8, width)
            if half == kind.index:
                keep[t : t + n] = result
            else:
                send[t : t + n] = result.astype(LOW)
        gains[0:1, :width] += gain_sum
        gains[1:2, :width] += shift_sum

    each_tower(lambda kind: finish(kind, 1 - kind.index))
    home_pair.start()
    risen_group.finish()
    fallen.wait_recv()

    def slots_of(kind):
        return (img_home_slots, txt_home_slots)[kind.index]

    def hidden_grads(kind):
        plan, collect = plans[kind.index], collects[kind.index]
        block, n, per = kind.block, kind.reduce_rows, kind.part // LANES

        def risen(c):
            chip, lane = c // per, c % per * LANES
            return raise_all[chip, :block, lane : lane + LANES].astype(WIDE)

        def fallen(c):
            lane = c * LANES
            return reduce_keep_ref[:n, lane : lane + LANES] + reduce_in[
                :n, lane : lane + LANES
            ].astype(WIDE)

        drop(kind, plan, 2, risen, slots_of(kind), flat)
        collect.piece(2, False)
        drop(kind, plan, 3, fallen, slots_of(kind), flat)
        collect.piece(3, False)

    each_tower(hidden_grads)
    late.relay_deep()
    each_tower(lambda kind: finish(kind, kind.index))
    late.relay_row()

    def lines(kind):
        width = kind.width
        hat, _ = standardise(middle_ref[:, :width])
        second_grad = second_scr[:, :width]

        def column_sum(value):
            return jnp.sum(value.astype(WIDE), axis=0, keepdims=True)

        mixed_grad = early_block[:, WIDTH : WIDTH + width].astype(WIDE)
        weights = low_scr[:, : kind.room].astype(WIDE).reshape(SEQS, 2 * HEADS, kind.room)
        totals = jnp.sum(weights[:, HEADS:], axis=-1, keepdims=True).reshape(SEQS * HEADS, 1)
        shared_scr[...] = jnp.broadcast_to(totals, shared_scr.shape)
        value_bias = []
        for lo, hi, first_head, n in spans(kind):
            owner = lax.broadcasted_iota(jnp.int32, (SEQS, hi - lo), 1) // HEAD
            scaled = jnp.zeros((SEQS, hi - lo), WIDE)
            for h in range(n):
                total = shared_scr[pl.ds(first_head + h, SEQS, stride=HEADS), 0:1]
                scaled = jnp.where(owner == h, mixed_grad[:, lo:hi] * total, scaled)
            value_bias.append(column_sum(scaled))
        hidden = bias_ref[0:1, : kind.part]
        parts = [
            gains[0:1, :width],
            gains[1:2, :width],
            column_sum(late_block[:, :width]),
            side_by_side(value_bias),
            column_sum(early_block[:, 2 * WIDTH : 2 * WIDTH + width]),
            column_sum(second_grad * hat),
            column_sum(second_grad),
            final_vec_ref[2:3, :width],
            final_vec_ref[0:1, :width],
            final_vec_ref[1:2, :width],
            jnp.concatenate([hidden, jnp.zeros((1, width - kind.part), WIDE)], axis=1),
            jnp.zeros((5, width), WIDE),
        ]
        lines_block[:, :width] = jnp.concatenate(parts, axis=0)

    each_tower(lines)
    line_copy = remote(
        lines_block, lines_all.at[at], lines_send.at[0], lines_recv.at[at], (tower, jnp.int32(0))
    )
    line_own = pltpu.make_async_copy(lines_block, lines_all.at[at], lines_recv.at[at])
    pl.when(at > 0)(line_copy.start)
    pl.when(at == 0)(line_own.start)

    early.finish()
    lefts.finish()

    def from_early(kind):
        plan, collect = plans[kind.index], collects[kind.index]
        width, block = kind.width, kind.block

        def gathered(k):
            lane = lax.broadcasted_iota(jnp.int32, (block, LANES), 1) // SEQS
            halves = []
            for side in range(2):
                total = jnp.zeros((block, LANES), WIDE)
                for j in range(8):
                    part = left_all[side * 8 + j, :block, LANES:].astype(WIDE)
                    shift = (j * SEQS - (k - 8) * SEQS) % LANES
                    turned_part = pltpu.roll(part, shift, 1) if shift else part
                    total = jnp.where(lane == j, turned_part, total)
                halves.append(total)
            return jnp.concatenate(halves, axis=1).astype(LOW)

        def right(start, wide):
            return early_all[:, :, start : start + wide].reshape(256, wide)

        output = dot_nn(gathered(13), right(2 * WIDTH, width))
        drop(
            kind, plan, 1, lambda c: output[:, c * LANES : (c + 1) * LANES], slots_of(kind), flat
        )
        collect.piece(1, False)
        embed = dot_nn(gathered(14), right(3 * WIDTH, EMB))
        drop(kind, plan, 4, lambda c: embed[:, c * LANES : (c + 1) * LANES], slots_of(kind), flat)
        collect.piece(4, False)
        left_scr[:block, :256] = gathered(12).astype(WIDE)

    each_tower(from_early)
    for when, copy in heads:
        pl.when(when)(copy.wait_send)
    pl.when(tower == 0)(relay.wait_send)
    for group in (pair, *asks, *mixes, *embeds, plane, rise, masks, embs, *deals):
        group.drain()
    late.finish()
    turns.finish()

    def from_late(kind):
        plan, collect = plans[kind.index], collects[kind.index]
        width, block = kind.width, kind.block
        ask = dot_nn(left_scr[:block, :256].astype(LOW), late_all[:, :, :width].reshape(256, width))

        def outer(side_ref, start, span):
            lo, hi, first_head, n = span
            lane = first_head * SEQS
            total = jnp.zeros((block, hi - lo), WIDE)
            for j in range(8):
                left, rows = [], []
                for source in (2 * j, 2 * j + 1):
                    left.append(side_ref[source, :block, lane : lane + LANES])
                    rows.append(
                        head_rows(early_all[source, :, start : start + width], span)
                    )
                    if n < 8:
                        rows.append(jnp.zeros(((8 - n) * SEQS, hi - lo), LOW))
                total += dot_nn(
                    jnp.concatenate(left, axis=1), jnp.concatenate(rows, axis=0)
                )
            return total

        keys = side_by_side([outer(turn_all, 0, span) for span in spans(kind)]) * 0.125
        worth = side_by_side([outer(left_all, WIDTH, span) for span in spans(kind)])
        per = width // LANES

        def inputs(c):
            value = (ask, keys, worth)[c // per]
            return value[:, c % per * LANES : (c % per + 1) * LANES]

        drop(kind, plan, 0, inputs, slots_of(kind), flat)
        collect.piece(0, False)

    each_tower(from_late)

    @pl.when(at == 0)
    def _():
        for k in range(1, 16):
            remote(
                lines_block, lines_all.at[k], lines_send.at[0], lines_recv.at[k], sibling
            ).wait_recv()
        line_own.wait()

        def vectors(kind):
            width, part = kind.width, kind.part
            whole = [jnp.sum(lines_all[:, :10, :width], axis=0)]
            for row in range(4):
                pair_of = []
                for chip in (2 * row, 2 * row + 1):
                    pair_of.append(
                        lines_all[2 * chip, 10:11, :part] + lines_all[2 * chip + 1, 10:11, :part]
                    )
                whole.append(jnp.concatenate(pair_of, axis=1))
            whole.append(jnp.zeros((2, width), WIDE))
            result = jnp.concatenate(whole, axis=0)
            drop(
                kind,
                plans[kind.index],
                VECTORS,
                lambda c: result[:, c * LANES : (c + 1) * LANES],
                slots_of(kind),
                flat,
            )

        each_tower(vectors)

    each_tower(lambda kind: collects[kind.index].piece(VECTORS, False))
    home_pair.finish()

    @pl.when(tower == 1)
    def _():
        img_keep[...] = img_home[...].astype(WIDE)

    @pl.when(tower == 0)
    def _():
        txt_keep[...] = txt_home[...].astype(WIDE)

    for copy in (*sent, fall, fallen, halves):
        copy.wait_send()
    pl.when(at > 0)(line_copy.wait_send)
    for group in (risen_group, lefts, turns, early, late, home_pair):
        group.drain()

    def drain(kind):
        for p in range(VECTORS + 1):
            collects[kind.index].piece(p, True)

    each_tower(drain)
    for collect in collects:
        collect.finish()


ROWS_LOW = ((SEQS, WIDTH), LOW)
ROWS_WIDE = ((SEQS, WIDTH), WIDE)
HEAD_ROWS = ((WIDTH // LANES, SEQS * HEADS, LANES), WIDE)
LANE_ROWS = ((SEQS * HEADS, LANES), WIDE)
GROUP = ((8, SEQS, WIDTH), LOW)
HIDDEN_BLOCKS = ((2, 8, 48, PART), LOW)
OUTER = ((16, 48, SEQS * HEADS), LOW)


def chunk_shapes(plan, n):
    return ((n, plan.rows, LANES), LOW)


def run_step(scalars, chunks, valid, tokens, plans):
    most = max(plan.local for plan in plans) + 17
    slots = max(plan.slots for plan in plans)
    edges = [((plan.rows, LANES), LOW) for plan in plans]
    rooms = [((kind.length, 8, kind.width), LOW) for kind in TOWERS]
    outs = [((kind.length, 8, kind.width), WIDE) for kind in TOWERS] + [
        chunk_shapes(plan, plan.local) for plan in plans
    ]
    scratch = [
        ROWS_LOW,
        ROWS_WIDE,
        ROWS_LOW,
        HEAD_ROWS,
        HEAD_ROWS,
        LANE_ROWS,
        ((SEQS, ROOM, WIDTH), LOW),
        ((WIDTH // LANES, ROOM * 8, LANES), WIDE),
        rooms[0],
        rooms[1],
        ((3, 16, 16, 2 * WIDTH), LOW),
        ((3, 16, 16, 2 * WIDTH), LOW),
        ((3, 16, 16, EMB), LOW),
        ROWS_WIDE,
        HIDDEN_BLOCKS,
        ((2, 192, WIDTH), LOW),
        ((2, 16, 16, LANES), LOW),
        chunk_shapes(plans[0], plans[0].slots),
        chunk_shapes(plans[1], plans[1].slots),
        edges[0],
        edges[1],
        edges[0],
        edges[1],
        chunk_shapes(plans[1], plans[1].local),
        edges[1],
        edges[1],
        ((plans[0].slots * plans[0].rows, LANES), WIDE),
        ((3, 16, 2 * WIDTH), LOW),
        ((3, 16, 2 * WIDTH), LOW),
        ((3, 16, EMB), LOW),
        ((48, EMB), LOW),
        ((8, 48, EMB), LOW),
        ((2, 8, 48, EMB), LOW),
        ((8, 48, PART), LOW),
        ((192, WIDTH), LOW),
        ((16, LANES), LOW),
        ROWS_WIDE,
        ROWS_WIDE,
        LANE_ROWS,
        ((2 * SEQS * HEADS, LANES), LOW),
        ROWS_WIDE,
        ROWS_LOW,
        ((SEQS, EMB), LOW),
        ((8, WIDTH), WIDE),
        HIDDEN_BLOCKS,
        ((192, WIDTH), WIDE),
        ((192, WIDTH), LOW),
        ((8, PART), WIDE),
        GROUP,
        GROUP,
        GROUP,
        GROUP,
        ((128, PART), WIDE),
        ((SEQS, EMB), LOW),
        ((2, 16, SEQS, EMB), LOW),
        ROWS_WIDE,
        ((SEQS, EMB), WIDE),
        ROWS_LOW,
        GROUP,
        GROUP,
        ((256, EMB), WIDE),
        ((PART, WIDTH), WIDE),
        rooms[0],
        rooms[1],
        rooms[0],
        rooms[1],
        ((2, WIDTH // LANES, ROOM * 8, LANES), WIDE),
        ROWS_WIDE,
        ROWS_WIDE,
        HEAD_ROWS,
        HEAD_ROWS,
        LANE_ROWS,
        LANE_ROWS,
        ((SEQS * HEADS, WIDTH), WIDE),
        OUTER,
        OUTER,
        OUTER,
        OUTER,
        ((SEQS, 3 * WIDTH + EMB), LOW),
        ((16, SEQS, 3 * WIDTH + EMB), LOW),
        ROWS_LOW,
        ((16, SEQS, WIDTH), LOW),
        ROWS_WIDE,
        ((16, SEQS, WIDTH), WIDE),
        ((8, 48, PART), LOW),
        ((8, 48, PART), LOW),
        ((8, 48, PART), LOW),
        ((192, WIDTH), LOW),
        chunk_shapes(plans[0], plans[0].slots),
        chunk_shapes(plans[1], plans[1].slots),
        ((8, WIDTH), WIDE),
        ROWS_WIDE,
    ]
    semaphores = [
        (3, most),
        (2, 6,),
        (3, 2),
        (3,),
        (2,),
        (3, 16),
        (3, 15),
        (3, 16),
        (3, 15),
        (3, 20),
        (3, 15),
        (10,),
        (9,),
        (9,),
        (8,),
        (3,),
        (2,),
        (17,),
        (16,),
        (4, 8,),
        (4, 7,),
        (17,),
        (16,),
        (4,),
        (9,),
        (8,),
        (16,),
        (15,),
        (16,),
        (15,),
        (20,),
        (15,),
        (16,),
        (15,),
        (1,),
        (16,),
        (2,),
        (2, 2, slots,),
        (2,),
    ]
    smem = pl.BlockSpec(memory_space=pltpu.SMEM)
    vmem = pl.BlockSpec(memory_space=pltpu.VMEM)
    like = jax.ShapeDtypeStruct
    return pl.pallas_call(
        functools.partial(step_kernel, plans),
        out_shape=[like((1,), WIDE), like((3,), WIDE)] + [like(*out) for out in outs],
        in_specs=[smem, smem, ANY, ANY, vmem, vmem, vmem],
        out_specs=[smem, smem, vmem, vmem, vmem, vmem],
        scratch_shapes=[pltpu.VMEM(*each) for each in scratch]
        + [pltpu.SemaphoreType.DMA(shape) for shape in semaphores],
        compiler_params=comm_params(0),
    )(*scalars, *chunks, valid, *tokens)


def to_chunks(flat, plan, me):
    start = me * plan.share % plan.chunk
    padded = jnp.pad(flat, (plan.chunk, plan.local * plan.chunk - plan.share))
    piece = lax.dynamic_slice(padded, (plan.chunk - start,), (plan.local * plan.chunk,))
    return piece.astype(LOW).reshape(plan.local, plan.rows, LANES)


def from_chunks(chunks, plan, me):
    start = me * plan.share % plan.chunk
    return lax.dynamic_slice(chunks.reshape(-1), (start,), (plan.share,)).astype(WIDE)


def step(
    img_tokens,
    txt_tokens,
    txt_ends,
    valid,
    img_master,
    img_moment,
    img_average,
    txt_master,
    txt_moment,
    txt_average,
    scale_state,
):
    me = lax.axis_index(("tower", "dp"))
    plans = (
        Plan(0, img_master.shape[0], 96, (9, 3, 12, 12, 2)),
        Plan(1, txt_master.shape[0], 64, (6, 2, 8, 8, 2)),
    )
    loss, scale_new, img_grad, txt_grad, img_chunks, txt_chunks = run_step(
        (txt_ends, scale_state),
        (to_chunks(img_master, plans[0], me), to_chunks(txt_master, plans[1], me)),
        valid,
        (jnp.transpose(img_tokens, (1, 0, 2)), jnp.transpose(txt_tokens, (1, 0, 2))),
        plans,
    )
    img_new = advance(
        img_master, img_moment, img_average, from_chunks(img_chunks, plans[0], me), step_rate
    )
    txt_new = advance(
        txt_master, txt_moment, txt_average, from_chunks(txt_chunks, plans[1], me), step_rate
    )
    return (
        loss[0],
        jnp.transpose(img_grad, (1, 0, 2)),
        jnp.transpose(txt_grad, (1, 0, 2)),
        img_new[0],
        img_new[1],
        img_new[2],
        img_new[0].astype(LOW),
        txt_new[0],
        txt_new[1],
        txt_new[2],
        txt_new[0].astype(LOW),
        scale_new,
    )


def from_partner(value, axis, stride):
    mask = 2**stride
    pairs = [(source, source ^ mask) for source in range(lax.axis_size(axis))]
    return lax.ppermute(value, axis, pairs)


def round_value(v):
    return lax.optimization_barrier(v.astype(jnp.bfloat16)).astype(jnp.float32)


def make_low():

    def value_keep(v):
        return (round_value(v), None)

    def grad_pass(kept, grad):
        return (grad,)

    rounded = jax.custom_vjp(round_value)
    rounded.defvjp(value_keep, grad_pass)
    return rounded


def low(v):
    return make_low()(v)


def make_low_back():

    def identity(v):
        return v

    def value_pass(v):
        return (v, None)

    def grad_round(kept, grad):
        return (round_value(grad),)

    passed = jax.custom_vjp(identity)
    passed.defvjp(value_pass, grad_round)
    return passed


def low_back(v):
    return make_low_back()(v)


def both_ways(value):
    return low(low_back(value))


def product(left, right):
    return jnp.matmul(left, right)


def contract(form, left, right):
    return jnp.einsum(form, left, right)


def layer_norm(values, gain_row, shift_row):
    centred = values - jnp.mean(values, axis=-1, keepdims=True)
    spread = jnp.mean(centred * centred, axis=-1, keepdims=True)
    return centred * lax.rsqrt(spread + 1e-05) * gain_row + shift_row


def unpack(flat_weights, model_width, hidden_width, embed_width):
    piece_shapes = [
        (model_width, 3 * model_width),
        (model_width, model_width),
        (model_width, hidden_width),
        (hidden_width, model_width),
        (model_width, embed_width),
        (10, model_width),
        (hidden_width,),
    ]
    pieces = []
    offset = 0
    for piece_shape in piece_shapes:
        length = math.prod(piece_shape)
        pieces.append(flat_weights[offset : offset + length].reshape(piece_shape))
        offset = offset + length
    return pieces


def encode(tokens, flat_weights, positions, causal, model_width, hidden_width, embed_width):
    w_inputs, w_output, w_expand, w_reduce, w_embed, vectors, expand_bias = unpack(
        flat_weights, model_width, hidden_width, embed_width
    )
    groups = tokens.shape[0]
    length = tokens.shape[1]
    first = low(layer_norm(tokens, vectors[0], vectors[1]))
    bias_in = jnp.concatenate([vectors[2], jnp.zeros_like(vectors[2]), vectors[3]])
    joined = both_ways(product(first, w_inputs) + bias_in)
    joined = joined.reshape(groups, length, 3, model_width // HEAD, HEAD)
    scores = low_back(contract("gqhd,gkhd->ghqk", joined[:, :, 0], joined[:, :, 1]) * 0.125)
    if causal:
        row_index = lax.broadcasted_iota(jnp.int32, (length, length), 0)
        col_index = lax.broadcasted_iota(jnp.int32, (length, length), 1)
        scores = jnp.where(col_index <= row_index, scores, -1e30)
    row_top = jnp.max(scores, axis=-1, keepdims=True)
    raw_weights = jnp.exp(scores - row_top)
    attention = low(raw_weights / jnp.sum(raw_weights, axis=-1, keepdims=True))
    mixed_heads = both_ways(
        contract("ghqk,gkhd->gqhd", attention, joined[:, :, 2]).reshape(groups, length, model_width)
    )
    middle = tokens + low_back(product(mixed_heads, w_output) + vectors[4])
    second = low(layer_norm(middle, vectors[5], vectors[6]))
    raised = low_back(product(second, w_expand) + expand_bias)
    active = low(raised * jax.nn.sigmoid(1.702 * raised))
    final_rows = middle + low_back(product(active, w_reduce) + vectors[7])
    pooled = jnp.take_along_axis(final_rows, positions[:, None, None], axis=1)[:, 0]
    pooled = low(layer_norm(pooled, vectors[8], vectors[9]))
    projected = low_back(product(pooled, w_embed))
    return low(
        projected * lax.rsqrt(jnp.sum(projected * projected, axis=-1, keepdims=True) + 1e-06)
    )


def inner(left, right):
    return lax.dot_general(
        left, right, (((1,), (1,)), ((), ())), preferred_element_type=jnp.float32
    )


def across(left, right):
    return lax.dot_general(
        left, right, (((0,), (0,)), ((), ())), preferred_element_type=jnp.float32
    )


def softmax_total(logits, allowed):
    masked = jnp.where(allowed, logits, -1e30)
    row_top = jnp.max(masked, axis=1, keepdims=True)
    return jnp.log(jnp.sum(jnp.exp(masked - row_top), axis=1)) + row_top[:, 0]


def advance(master, moment, average, grads, rate):
    moment_new = momentum_rate * moment + grads
    master_new = master - rate * (grads + momentum_rate * moment_new)
    average_new = average_rate * average + (1.0 - average_rate) * master_new
    return (master_new, moment_new, average_new)


def padded_to(flat, length):
    return jnp.pad(flat, (0, length - flat.shape[0]))


def body(
    img_tokens,
    txt_tokens,
    txt_ends,
    valid,
    img_master,
    img_moment,
    img_average,
    txt_master,
    txt_moment,
    txt_average,
    scale_state,
):
    batch_rows = img_tokens.shape[0]
    total_rows = batch_rows * lax.axis_size(("tower", "dp"))
    device_at = lax.axis_index(("tower", "dp"))
    tower_at = lax.axis_index("tower")
    is_image = tower_at == 0
    img_share = img_master.shape[0]
    txt_share = txt_master.shape[0]
    img_count = img_tokens.size
    txt_count = txt_tokens.size
    shard_room = max(img_share, txt_share)
    token_room = max(img_count, txt_count)
    tower_count = lax.axis_size("dp")
    dp_at = lax.axis_index("dp")
    img_low = padded_to(img_master.astype(jnp.bfloat16), shard_room)
    txt_low = padded_to(txt_master.astype(jnp.bfloat16), shard_room)
    token_out = jnp.where(
        is_image,
        padded_to(txt_tokens.reshape(-1), token_room),
        padded_to(img_tokens.reshape(-1), token_room),
    )
    weight_out = jnp.where(is_image, txt_low, img_low)
    weight_mine = jnp.where(is_image, img_low, txt_low)
    token_in, weight_in = from_partner((token_out, weight_out), "tower", 0)
    stacked = jnp.where(
        is_image, jnp.stack([weight_mine, weight_in]), jnp.stack([weight_in, weight_mine])
    )
    gathered = lax.all_gather(stacked, "dp", axis=1, tiled=True)
    pair_ends = jnp.concatenate(
        [
            lax.dynamic_slice_in_dim(txt_ends, dp_at * batch_rows, batch_rows),
            lax.dynamic_slice_in_dim(txt_ends, (tower_count + dp_at) * batch_rows, batch_rows),
        ]
    )
    pair_zero = jnp.zeros((2 * batch_rows,), jnp.int32)

    def image_weights(whole):
        return whole.reshape(2, tower_count, shard_room).reshape(-1).astype(jnp.float32)

    def text_weights(whole):
        return (
            whole.reshape(2, tower_count, shard_room)[:, :, :txt_share]
            .reshape(-1)
            .astype(jnp.float32)
        )

    def image_rows(arrived):
        return jnp.concatenate(
            [img_tokens, arrived[:img_count].reshape(img_tokens.shape)], axis=0
        ).astype(jnp.float32)

    def text_rows(arrived):
        return jnp.concatenate([arrived.reshape(txt_tokens.shape), txt_tokens], axis=0).astype(
            jnp.float32
        )

    def image_encode(rows, flat):
        return encode(rows, flat, pair_zero, False, D_IMG, FF_IMG, EMB)

    def text_encode(rows, flat):
        return encode(rows, flat, pair_ends, True, D_TXT, FF_TXT, EMB)

    def image_forward(operands):
        return image_encode(image_rows(operands[1]), image_weights(operands[0]))

    def text_forward(operands):
        return text_encode(text_rows(operands[1]), text_weights(operands[0]))

    pair_emb = lax.cond(is_image, image_forward, text_forward, (gathered, token_in)).astype(
        jnp.bfloat16
    )
    emb_in = from_partner(pair_emb, "tower", 0)
    img_pair = jnp.where(is_image, pair_emb, emb_in)
    txt_pair = jnp.where(is_image, emb_in, pair_emb)
    row_start = tower_at * batch_rows
    img_local = lax.dynamic_slice_in_dim(img_pair, row_start, batch_rows)
    txt_local = lax.dynamic_slice_in_dim(txt_pair, row_start, batch_rows)
    img_all, txt_all = (
        lax.all_gather(img_local, ("tower", "dp"), axis=0, tiled=True),
        lax.all_gather(txt_local, ("tower", "dp"), axis=0, tiled=True),
    )
    logit_scale = jnp.exp(scale_state[0])
    offset = device_at * batch_rows
    row_index = lax.broadcasted_iota(jnp.int32, (batch_rows, total_rows), 0) + offset
    col_index = lax.broadcasted_iota(jnp.int32, (batch_rows, total_rows), 1)
    diagonal = (row_index == col_index).astype(jnp.float32)
    allowed = valid > 0
    row_logits = logit_scale * inner(img_local, txt_all)
    col_logits = logit_scale * inner(txt_local, img_all)
    row_lse = softmax_total(row_logits, allowed)
    col_lse = softmax_total(col_logits, allowed)
    partial_loss = 0.5 * (
        jnp.sum(row_lse)
        - jnp.sum(row_logits * diagonal)
        + jnp.sum(col_lse)
        - jnp.sum(col_logits * diagonal)
    )
    row_terms = 0.5 * (jnp.where(allowed, jnp.exp(row_logits - row_lse[:, None]), 0.0) - diagonal)
    col_terms = 0.5 * (jnp.where(allowed, jnp.exp(col_logits - col_lse[:, None]), 0.0) - diagonal)
    partial_scale = jnp.sum(row_terms * row_logits) + jnp.sum(col_terms * col_logits)
    row_back = (logit_scale * row_terms).astype(jnp.bfloat16)
    col_back = (logit_scale * col_terms).astype(jnp.bfloat16)
    img_emb_grad = jnp.dot(row_back, txt_all, preferred_element_type=jnp.float32)
    txt_emb_grad = jnp.dot(col_back, img_all, preferred_element_type=jnp.float32)
    img_extra, txt_extra = (
        lax.psum_scatter(
            across(col_back, txt_local), ("tower", "dp"), scatter_dimension=0, tiled=True
        ),
        lax.psum_scatter(
            across(row_back, img_local), ("tower", "dp"), scatter_dimension=0, tiled=True
        ),
    )
    img_emb_grad = img_emb_grad + img_extra
    txt_emb_grad = txt_emb_grad + txt_extra
    sums = lax.psum((partial_loss, partial_scale), ("tower", "dp"))
    grad_out = jnp.where(is_image, txt_emb_grad, img_emb_grad)
    grad_in = from_partner(grad_out, "tower", 0)
    pair_cot = jnp.where(
        is_image,
        jnp.concatenate([img_emb_grad, grad_in], axis=0),
        jnp.concatenate([grad_in, txt_emb_grad], axis=0),
    )

    def image_backward(operands):
        recomputed, tower_pullback = jax.vjp(
            image_encode, image_rows(operands[1]), image_weights(operands[0])
        )
        rows_grad, flat_grad = tower_pullback(operands[2])
        own_part = padded_to(rows_grad[:batch_rows].reshape(-1), token_room)
        sent_part = padded_to(rows_grad[batch_rows:].reshape(-1), token_room)
        stacked_grad = flat_grad.reshape(2, tower_count, img_share)
        return (own_part, sent_part, stacked_grad)

    def text_backward(operands):
        recomputed, tower_pullback = jax.vjp(
            text_encode, text_rows(operands[1]), text_weights(operands[0])
        )
        rows_grad, flat_grad = tower_pullback(operands[2])
        own_part = padded_to(rows_grad[batch_rows:].reshape(-1), token_room)
        sent_part = padded_to(rows_grad[:batch_rows].reshape(-1), token_room)
        stacked_grad = jnp.pad(
            flat_grad.reshape(2, tower_count, txt_share),
            ((0, 0), (0, 0), (0, shard_room - txt_share)),
        )
        return (own_part, sent_part, stacked_grad)

    own_part, sent_part, stacked_grad = lax.cond(
        is_image, image_backward, text_backward, (gathered, token_in, pair_cot)
    )
    summed = lax.psum_scatter(stacked_grad, "dp", scatter_dimension=1, tiled=True)
    kept_part = jnp.where(is_image, summed[0, 0], summed[1, 0])
    sent_share = jnp.where(is_image, summed[1, 0], summed[0, 0])
    home_weights, home_tokens = (
        from_partner(sent_share.astype(jnp.bfloat16), "tower", 0).astype(sent_share.dtype),
        from_partner(sent_part.astype(jnp.bfloat16), "tower", 0).astype(sent_part.dtype),
    )
    img_owned = jnp.where(is_image, kept_part, home_weights)
    txt_owned = jnp.where(is_image, home_weights, kept_part)[:txt_share]
    img_grad = jnp.where(is_image, own_part, home_tokens)[:img_count].reshape(img_tokens.shape)
    txt_grad = jnp.where(is_image, home_tokens, own_part).reshape(txt_tokens.shape)
    img_new = advance(img_master, img_moment, img_average, img_owned, step_rate)
    txt_new = advance(txt_master, txt_moment, txt_average, txt_owned, step_rate)
    scale_parts = advance(scale_state[0], scale_state[1], scale_state[2], sums[1], scale_rate)
    scale_new = jnp.stack([scale_parts[0], scale_parts[1], scale_parts[2]])
    return (
        sums[0] / total_rows,
        img_grad,
        txt_grad,
        img_new[0],
        img_new[1],
        img_new[2],
        img_new[0].astype(jnp.bfloat16),
        txt_new[0],
        txt_new[1],
        txt_new[2],
        txt_new[0].astype(jnp.bfloat16),
        scale_new,
    )


def solution(mesh):
    in_specs = (
        P(("tower", "dp"), None, None),
        P(("tower", "dp"), None, None),
        P(),
        P(("tower", "dp"), None),
        P(("tower", "dp")),
        P(("tower", "dp")),
        P(("tower", "dp")),
        P(("tower", "dp")),
        P(("tower", "dp")),
        P(("tower", "dp")),
        P(),
    )
    out_specs = (
        P(),
        P(("tower", "dp"), None, None),
        P(("tower", "dp"), None, None),
        P(("tower", "dp")),
        P(("tower", "dp")),
        P(("tower", "dp")),
        P(("tower", "dp")),
        P(("tower", "dp")),
        P(("tower", "dp")),
        P(("tower", "dp")),
        P(("tower", "dp")),
        P(),
    )
    run = step if (mesh.shape["tower"], mesh.shape["dp"]) == (2, 16) else body
    return jax.shard_map(run, mesh=mesh, in_specs=in_specs, out_specs=out_specs, check_vma=False)
```

```python
import functools
import math

import jax
import jax.numpy as jnp
from jax import lax
from jax.experimental import pallas as pl
from jax.experimental.pallas import tpu as pltpu
from jax.sharding import PartitionSpec as P

D_IMG = 768
FF_IMG = 3072
D_TXT = 512
FF_TXT = 2048
EMB = 512
HEAD = 64


momentum_rate = 0.5
average_rate = 0.5
step_rate = 0.08
scale_rate = 0.0001


MESH = pl.DeviceIdType.MESH
ANY = pl.BlockSpec(memory_space=pl.ANY)
GRANT = 58 * 1024 * 1024
LANES = 128
LOW = jnp.bfloat16
WIDE = jnp.float32


def here():
    return lax.axis_index("tower"), lax.axis_index("dp")


def greet(devices):
    barrier = pltpu.get_barrier_semaphore()
    for device in devices:
        pl.semaphore_signal(barrier, inc=1, device_id=device, device_id_type=MESH)
    pl.semaphore_wait(barrier, len(devices))


def remote(src, dst, send_sem, recv_sem, device):
    return pltpu.make_async_remote_copy(
        src_ref=src,
        dst_ref=dst,
        send_sem=send_sem,
        recv_sem=recv_sem,
        device_id=device,
        device_id_type=MESH,
    )


def comm_params(number):
    return pltpu.CompilerParams(
        collective_id=number, has_side_effects=True, vmem_limit_bytes=GRANT
    )


def same_core(tower, at):
    chip, core = at // 2, at % 2
    return [(tower, (chip + k) % 8 * 2 + core) for k in range(1, 8)]


def both_towers(tower, at):
    place, core = tower * 8 + at // 2, at % 2
    others = [(place + k) % 16 for k in range(1, 16)]
    return [(other // 8, other % 8 * 2 + core) for other in others]


def everyone(tower, at):
    me = tower * 16 + at
    others = [(me + k) % 32 for k in range(1, 32)]
    return [(other // 16, other % 16) for other in others]


def group_exchange(scattered, x_ref, o_ref, send_sem, recv_sem):
    tower, at = here()
    chip = at // 2

    def source(k):
        return x_ref.at[k] if scattered else x_ref

    own = pltpu.make_async_copy(source(chip), o_ref.at[chip], send_sem.at[7])
    sent = []
    for k, device in enumerate(same_core(tower, at)):
        copy = remote(
            source((chip + 1 + k) % 8), o_ref.at[chip], send_sem.at[k], recv_sem.at[k], device
        )
        copy.start()
        sent.append(copy)
    own.start()
    own.wait()
    for k in range(7):
        remote(
            source(chip),
            o_ref.at[(chip + 7 - k) % 8],
            send_sem.at[k],
            recv_sem.at[k],
            (tower, at),
        ).wait_recv()
    return sent


class Spread:
    def __init__(self, src, dst, send, recv):
        self.src, self.dst, self.send, self.recv = src, dst, send, recv
        tower, at = here()
        self.core = at % 2
        self.sibling = (tower, at + 1 - 2 * self.core)
        self.devices = self.peers(tower, at)
        self.n = len(self.devices) + 1
        self.place = self.spot(tower, at)
        self.sent = []

    def peers(self, tower, at):
        return both_towers(tower, at)

    def spot(self, tower, at):
        return tower * 8 + at // 2

    def block(self, place):
        return self.src

    def side(self, core):
        return self.dst.at[core]

    def launch(self, src, dst, k, device):
        copy = remote(src, dst, self.send.at[k], self.recv.at[k], device)
        copy.start()
        self.sent.append(copy)

    def start(self):
        for k, device in enumerate(self.devices):
            to = (self.place + 1 + k) % self.n
            self.launch(self.block(to), self.side(self.core).at[self.place], k, device)
        self.own = pltpu.make_async_copy(
            self.block(self.place), self.side(self.core).at[self.place], self.send.at[self.n]
        )
        self.own.start()

    def arrived(self):
        for k in range(self.n - 1):
            source = (self.place + self.n - 1 - k) % self.n
            remote(
                self.block(0),
                self.side(self.core).at[source],
                self.send.at[k],
                self.recv.at[k],
                self.sibling,
            ).wait_recv()
        self.own.wait()

    def relay(self):
        self.arrived()
        side = self.side(self.core)
        self.launch(side, side, self.n - 1, self.sibling)

    def finish(self):
        side = self.side(1 - self.core)
        remote(
            side, side, self.send.at[self.n - 1], self.recv.at[self.n - 1], self.sibling
        ).wait_recv()

    def drain(self):
        for copy in self.sent:
            copy.wait_send()


class Group(Spread):
    def __init__(self, src, dst, send, recv, both=True):
        self.both = both
        super().__init__(src, dst, send, recv)

    def peers(self, tower, at):
        return same_core(tower, at)

    def spot(self, tower, at):
        return at // 2

    def block(self, place):
        return self.src.at[place]

    def side(self, core):
        return self.dst.at[core] if self.both else self.dst

    def finish(self):
        if self.both:
            super().finish()
        else:
            self.arrived()


class Ring:
    def __init__(self, src, dst, send, recv, only=None, narrow=None):
        self.src, self.dst, self.send, self.recv = src, dst, send, recv
        self.only, self.narrow = only, narrow
        self.tower, self.at = here()
        self.deep, self.row, self.core = self.at // 4, self.at // 2 % 2, self.at % 2
        self.sibling = (self.tower, self.at + 1 - 2 * self.core)
        self.beside = (self.tower, self.spot(0, 1 - self.row))
        self.sent = []

    def spot(self, k, row):
        return (self.deep + k) % 4 * 4 + row * 2 + self.core

    def forms(self, make):
        def whole(block):
            return block

        def part(block):
            return block.at[:, pl.ds(0, self.narrow)]

        if self.only is not None:
            return [(self.tower == self.only, make(whole))]
        if self.narrow is None:
            return [(None, make(whole))]
        return [(self.tower == 0, make(whole)), (self.tower == 1, make(part))]

    def act(self, forms, name):
        for when, copy in forms:
            action = getattr(copy, name)
            if when is None:
                action()
            else:
                pl.when(when)(action)

    def remote(self, src, slot, sent, landed, device):
        return self.forms(
            lambda cut: remote(
                cut(src), cut(self.dst.at[slot]), self.send.at[sent], self.recv.at[landed], device
            )
        )

    def launch(self, src, slot, index, device):
        forms = self.remote(src, slot, index, index, device)
        self.act(forms, "start")
        self.sent.append(forms)

    def arrived(self, slot, index):
        self.act(self.remote(self.src, slot, index, index, self.sibling), "wait_recv")

    def start(self):
        for k in (1, 3, 2):
            self.launch(self.src, self.at, k - 1, (self.tower, self.spot(k, self.row)))
        self.launch(self.src, self.at, 3, self.beside)
        self.launch(self.src, self.at, 7, self.sibling)
        self.own = self.forms(
            lambda cut: pltpu.make_async_copy(
                cut(self.src), cut(self.dst.at[self.at]), self.send.at[15]
            )
        )
        self.act(self.own, "start")

    def relay_deep(self):
        for k in (1, 3, 2):
            slot = self.spot(4 - k, self.row)
            self.arrived(slot, k - 1)
            self.launch(self.dst.at[slot], slot, 3 + k, self.beside)
            self.launch(self.dst.at[slot], slot, 7 + k, self.sibling)

    def relay_row(self):
        for k in (0, 1, 3, 2):
            slot = self.spot(4 - k, 1 - self.row)
            self.arrived(slot, 3 + k)
            self.launch(self.dst.at[slot], slot, 11 + k, self.sibling)

    def finish(self):
        for index in range(8):
            k, row = index % 4, self.row if index < 4 else 1 - self.row
            slot = (self.deep + 4 - k) % 4 * 4 + row * 2 + 1 - self.core
            self.arrived(slot, 7 + index)
        self.act(self.own, "wait")

    def drain(self):
        for forms in self.sent:
            self.act(forms, "wait_send")


class Chain:
    def __init__(self, src, dst, send, recv, only=None):
        self.src, self.dst, self.send, self.recv = src, dst, send, recv
        self.only = only
        self.tower, self.at = here()
        self.deep, self.row, self.core = self.at // 4, self.at // 2 % 2, self.at % 2
        self.mate = self.deep + 1 - 2 * (self.deep % 2)
        self.half = self.deep // 2
        self.inner = jnp.logical_or(self.deep == 1, self.deep == 2)
        self.sibling = (self.tower, self.at + 1 - 2 * self.core)
        self.beside = (self.tower, self.spot(self.deep, 1 - self.row))
        self.sent = []

    def spot(self, deep, row):
        return deep * 4 + row * 2 + self.core

    def sources(self):
        return self.deep, self.mate, 2 - 2 * self.half, 3 - 2 * self.half

    def act(self, action, when=None):
        if self.only is not None:
            right = self.tower == self.only
            when = right if when is None else jnp.logical_and(when, right)
        if when is None:
            action()
        else:
            pl.when(when)(action)

    def launch(self, src, slot, sent, landed, device, when=None):
        copy = remote(src, self.dst.at[slot], self.send.at[sent], self.recv.at[landed], device)
        self.act(copy.start, when)
        self.sent.append((copy, when))

    def arrived(self, slot, index):
        copy = remote(
            self.src, self.dst.at[slot], self.send.at[0], self.recv.at[index], self.sibling
        )
        self.act(copy.wait_recv)

    def start(self):
        mate = (self.tower, self.spot(self.mate, self.row))
        far = (self.tower, self.spot(2 - self.half, self.row))
        self.launch(self.src, self.at, 1, 1 + self.deep % 2, far)
        self.launch(self.src, self.at, 0, 0, mate)
        self.launch(self.src, self.at, 2, 3, self.beside)
        self.launch(self.src, self.at, 3, 7, self.sibling)
        self.own = pltpu.make_async_copy(self.src, self.dst.at[self.at], self.send.at[16])
        self.act(self.own.start)

    def relay_deep(self):
        mate = (self.tower, self.spot(self.mate, self.row))
        for k in (1, 2, 3):
            slot = self.spot(self.sources()[k], self.row)
            self.arrived(slot, k - 1)
            block = self.dst.at[slot]
            if k > 1:
                self.launch(block, slot, 4 + k, k - 1, mate, self.inner)
            self.launch(block, slot, 7 + k, 3 + k, self.beside)
            self.launch(block, slot, 16 + k, 7 + k, self.sibling)

    def relay_row(self):
        for k, deep in enumerate(self.sources()):
            slot = self.spot(deep, 1 - self.row)
            self.arrived(slot, 3 + k)
            self.launch(self.dst.at[slot], slot, 11 + k, 11 + k, self.sibling)

    def finish(self):
        for k, deep in enumerate(self.sources()):
            for row, base in ((self.row, 7), (1 - self.row, 11)):
                self.arrived(deep * 4 + row * 2 + 1 - self.core, base + k)
        self.act(self.own.wait)

    def drain(self):
        for copy, when in self.sent:
            self.act(copy.wait_send, when)


class Plane:
    def __init__(self, src, via, dst, send, recv):
        self.src, self.via, self.dst, self.send, self.recv = src, via, dst, send, recv
        self.tower, self.at = here()
        self.deep, self.row, self.core = self.at // 4, self.at // 2 % 2, self.at % 2
        self.partner = (1 - self.tower, self.at)
        self.sibling = (self.tower, self.at + 1 - 2 * self.core)
        self.beside = (self.tower, self.at + 2 - 4 * self.row)
        self.sent = []

    def spot(self, k, row):
        return (self.deep + k) % 4 * 2 + row

    def launch(self, src, slot, index, device):
        copy = remote(src, self.via.at[slot], self.send.at[index], self.recv.at[index], device)
        pl.when(self.tower == 1)(copy.start)
        self.sent.append(copy)

    def arrived(self, slot, index):
        copy = remote(
            self.src, self.via.at[slot], self.send.at[index], self.recv.at[index], self.sibling
        )
        pl.when(self.tower == 1)(copy.wait_recv)

    def start(self):
        own = self.spot(0, self.row)
        for k in (1, 3, 2):
            there = self.spot(k, self.row) * 2 + self.core
            self.launch(self.src, own, k - 1, (self.tower, there))
        self.launch(self.src, own, 3, self.beside)
        self.own = pltpu.make_async_copy(self.src, self.via.at[own], self.send.at[7])
        pl.when(self.tower == 1)(self.own.start)

    def relay_deep(self):
        for k in (1, 3, 2):
            slot = self.spot(4 - k, self.row)
            self.arrived(slot, k - 1)
            self.launch(self.via.at[slot], slot, 3 + k, self.beside)

    def relay_row(self):
        for k in range(4):
            self.arrived(self.spot(4 - k, 1 - self.row), 3 + k)
        pl.when(self.tower == 1)(self.own.wait)
        pl.when(self.tower == 1)(self.down().start)

    def down(self):
        return remote(
            self.via, self.dst.at[self.core], self.send.at[8], self.recv.at[7], self.partner
        )

    def across(self, core):
        return remote(
            self.dst.at[core], self.dst.at[core], self.send.at[9], self.recv.at[8], self.sibling
        )

    def land(self):
        pl.when(self.tower == 0)(self.down().wait_recv)
        pl.when(self.tower == 0)(self.across(self.core).start)

    def finish(self):
        pl.when(self.tower == 0)(self.across(1 - self.core).wait_recv)

    def drain(self):
        for copy in self.sent:
            pl.when(self.tower == 1)(copy.wait_send)
        pl.when(self.tower == 1)(self.down().wait_send)
        pl.when(self.tower == 0)(self.across(self.core).wait_send)


def rings(src, dst, send, recv, way=Ring, *narrow):
    return [
        way(
            src.at[part],
            dst.at[part],
            send.at[part],
            recv.at[part],
            0 if part == 2 else None,
            *narrow,
        )
        for part in range(3)
    ]


class Blocks:
    def __init__(self, src, dst, send, recv, shared=1):
        self.src, self.dst, self.send, self.recv = src, dst, send, recv
        self.tower, self.at = here()
        self.shared = shared
        self.sent = []

    def start(self):
        for k in range(1, 16):
            to = (self.at + k) % 16
            copy = remote(
                self.src.at[to // self.shared],
                self.dst.at[self.at],
                self.send.at[k - 1],
                self.recv.at[k - 1],
                (self.tower, to),
            )
            copy.start()
            self.sent.append(copy)
        self.own = pltpu.make_async_copy(
            self.src.at[self.at // self.shared], self.dst.at[self.at], self.send.at[15]
        )
        self.own.start()

    def finish(self):
        for k in range(1, 16):
            remote(
                self.src.at[0],
                self.dst.at[(self.at + 16 - k) % 16],
                self.send.at[k - 1],
                self.recv.at[k - 1],
                (self.tower, self.at),
            ).wait_recv()
        self.own.wait()

    def drain(self):
        for copy in self.sent:
            copy.wait_send()


class Pair:
    def __init__(self, from_zero, zero_dst, from_one, one_dst, sems):
        tower, at = here()
        partner = (1 - tower, at)
        self.tower = tower
        self.up = remote(from_zero, zero_dst, sems.at[0], sems.at[1], partner)
        self.down = remote(from_one, one_dst, sems.at[0], sems.at[1], partner)

    def by_tower(self, zero, one):
        pl.when(self.tower == 0)(zero)
        pl.when(self.tower == 1)(one)

    def start(self):
        self.by_tower(self.up.start, self.down.start)

    def finish(self):
        self.by_tower(self.down.wait_recv, self.up.wait_recv)

    def drain(self):
        self.by_tower(self.up.wait_send, self.down.wait_send)


VECTORS = 5
EXPAND = 2
EMBED = 4
TURN = 8


class Plan:
    def __init__(self, tower, share, rows, per_device):
        self.tower = tower
        self.share = share
        self.rows = rows
        self.chunk = rows * LANES
        self.per_device = per_device
        self.first_slot = [sum(per_device[:p]) for p in range(6)]
        self.first_chunk = [16 * slot for slot in self.first_slot]
        self.slots = sum(per_device) + 1
        self.total = 16 * sum(per_device) + 1
        spans = [self.span(device) for device in range(32)]
        self.counts = sorted({last - first + 1 for first, last in spans})
        self.local = self.counts[-1]

    def span(self, device):
        first = device * self.share // self.chunk
        last = ((device + 1) * self.share - 1) // self.chunk
        return first, min(last, self.total - 1)

    def bounds(self, device):
        first = device * self.share // self.chunk
        last = ((device + 1) * self.share - 1) // self.chunk
        return first, jnp.minimum(last, self.total - 1)

    def pieces(self, p):
        return self.per_device[p] if p < VECTORS else 1

    def target(self, g):
        piece, base, slot, n = (jnp.int32(0), jnp.int32(0), jnp.int32(0), jnp.int32(1))
        for p in range(VECTORS):
            inside = g >= self.first_chunk[p]
            piece = jnp.where(inside, p, piece)
            base = jnp.where(inside, self.first_chunk[p], base)
            slot = jnp.where(inside, self.first_slot[p], slot)
            n = jnp.where(inside, self.per_device[p], n)
        block = (g - base) // n
        at = jnp.where(piece == EXPAND, (block + TURN) % 16, block)
        return piece, at, slot + (g - base) - block * n


def before(me):
    device = (me + 31) % 32
    return device // 16, device % 16


class Deal:
    def __init__(self, plan, s, src, dst, extra, last, sems, only=None, me=None):
        self.plan, self.s, self.src, self.dst = plan, s, src, dst
        self.extra, self.last = extra, last
        self.chunk_send, self.recv, self.edge, self.fetch = sems
        self.tower, self.at = here()
        self.only = only
        self.me = self.tower * 16 + self.at if me is None else me
        self.first, self.last_chunk = plan.bounds(self.me)

    def runs(self, condition):
        return condition if self.only is None else jnp.logical_and(condition, self.tower == self.only)

    def move(self, src, i, piece, at_to, slot, wait):
        tower_to = self.plan.tower
        if not isinstance(piece, int):
            tower_to = jnp.where(piece == EMBED, 1, tower_to)
        far = jnp.logical_or(self.tower != tower_to, at_to != self.at)
        recv = self.recv.at[self.plan.tower, piece]
        copy = remote(
            src,
            self.dst.at[slot],
            self.chunk_send.at[self.s, i],
            recv,
            (tower_to, at_to),
        )
        pl.when(far)(copy.wait_send if wait else copy.start)
        if not wait:
            pl.when(jnp.logical_not(far))(
                pltpu.make_async_copy(src, self.dst.at[slot], recv).start
            )

    def whole(self, early, wait):
        def step(i, carry):
            g = self.first + i
            piece, at_to, slot = self.plan.target(g)
            inside = jnp.logical_and(
                jnp.logical_or(i > 0, self.me == 0),
                jnp.logical_or(
                    g < self.last_chunk, jnp.logical_and(self.me == 31, g < self.plan.total - 1)
                ),
            )
            inside = jnp.logical_and(inside, g <= self.last_chunk)
            inside = jnp.logical_and(inside, g < self.plan.total - 1)
            if early is not None:
                hidden = jnp.logical_and(piece >= 2, piece <= 3)
                inside = jnp.logical_and(inside, jnp.logical_not(hidden) if early else hidden)

            @pl.when(self.runs(inside))
            def _():
                self.move(self.src.at[i], i, piece, at_to, slot, wait)

            return carry

        lax.fori_loop(0, self.plan.local, step, 0)

    def vectors(self, wait):
        @pl.when(self.runs(self.me == 31))
        def _():
            src = self.src.at[self.last_chunk - self.first]

            def each(k, carry):
                self.move(src, self.plan.local + k, VECTORS, k, self.plan.slots - 1, wait)
                return carry

            lax.fori_loop(0, 16, each, 0)

    def fetch_last(self):
        return pltpu.make_async_copy(
            self.src.at[self.last_chunk - self.first], self.last, self.fetch.at[self.s]
        )

    def join(self):
        @pl.when(self.runs(self.me < 31))
        def _():
            self.fetch_last().wait()
            edge = self.edge
            remote(
                self.last,
                self.extra,
                edge.at[self.s, 0],
                edge.at[self.s, 1],
                (self.tower, self.at),
            ).wait_recv()
            self.last[...] = self.last[...] + self.extra[...]
            piece, at_to, slot = self.plan.target(self.last_chunk)
            self.move(self.last, self.plan.local + 16, piece, at_to, slot, False)

    def start_fetch(self):
        pl.when(self.runs(self.me < 31))(self.fetch_last().start)

    def arrived(self, p):
        part = self.dst.at[pl.ds(self.plan.first_slot[p], self.plan.pieces(p))]
        pltpu.make_async_copy(part, part, self.recv.at[self.plan.tower, p]).wait()

    def drain(self):
        self.whole(None, True)
        self.vectors(True)

        @pl.when(self.runs(self.me < 31))
        def _():
            piece, at_to, slot = self.plan.target(self.last_chunk)
            self.move(self.last, self.plan.local + 16, piece, at_to, slot, True)


class Collect:
    def __init__(self, plan, s, src, dst, send, recv):
        self.plan, self.s, self.src, self.dst = plan, s, src, dst
        self.send, self.recv = send, recv
        self.tower, self.at = here()
        self.me = self.tower * 16 + self.at

    def one(self, owner, slot, g, which, wait):
        first, _ = self.plan.bounds(owner)
        far = owner != self.me
        recv = self.recv.at[self.s]
        copy = remote(
            self.src.at[slot],
            self.dst.at[g - first],
            self.send.at[which, slot],
            recv,
            (owner // 16, owner % 16),
        )
        pl.when(far)(copy.wait_send if wait else copy.start)
        if not wait:
            pl.when(jnp.logical_not(far))(
                pltpu.make_async_copy(self.src.at[slot], self.dst.at[g - first], recv).start
            )

    def piece(self, p, wait):
        n = self.plan.pieces(p)

        def step(i, carry):
            slot = self.plan.first_slot[p] + i
            block = (self.at + 16 - TURN) % 16 if p == EXPAND else self.at
            g = self.plan.first_chunk[p] + block * n + i if p < VECTORS else self.plan.total - 1
            low = g * self.plan.chunk // self.plan.share
            high = jnp.minimum(((g + 1) * self.plan.chunk - 1) // self.plan.share, 31)
            self.one(low, slot, g, 0, wait)
            pl.when(high != low)(lambda: self.one(high, slot, g, 1, wait))
            return carry

        if p == VECTORS:


            @pl.when(self.at == 0)
            def _():
                step(0, 0)

        else:
            lax.fori_loop(0, n, step, 0)

    def finish(self):
        first, last = self.plan.bounds(self.me)
        held = last - first + 1
        for n in self.plan.counts:

            @pl.when(held == n)
            def _():
                part = self.dst.at[pl.ds(0, n)]
                pltpu.make_async_copy(part, part, self.recv.at[self.s]).wait()


SEQS = 16
HEADS = 16


class Tower:
    def __init__(self, index, width, hidden, length, room, run, causal):
        self.index = index
        self.width = width
        self.hidden = hidden
        self.length = length
        self.room = room
        self.run = run
        self.causal = causal
        self.heads = width // HEAD
        self.block = width // 16
        self.part = hidden // 8
        self.reduce_rows = hidden // 16


TOWERS = (
    Tower(0, D_IMG, FF_IMG, 50, 64, 10, False),
    Tower(1, D_TXT, FF_TXT, 77, 80, 11, True),
)
ROOM = 80
WIDTH = D_IMG
PART = FF_IMG // 8


def each_tower(run):
    tower = lax.axis_index("tower")
    for kind in TOWERS:
        pl.when(tower == kind.index)(functools.partial(run, kind))


def dot_nn(a, b):
    return lax.dot_general(a, b, (((1,), (0,)), ((), ())), preferred_element_type=WIDE)


def dot_nt(a, b):
    return lax.dot_general(a, b, (((1,), (1,)), ((), ())), preferred_element_type=WIDE)


def dot_tn(a, b):
    return lax.dot_general(a, b, (((0,), (0,)), ((), ())), preferred_element_type=WIDE)


def standardise(rows):
    centred = rows - jnp.mean(rows, axis=-1, keepdims=True)
    spread = jnp.mean(centred * centred, axis=-1, keepdims=True)
    rate = lax.rsqrt(spread + 1e-05)
    return centred * rate, rate


def norm_back(grad, gain, hat, rate):
    scaled = grad * gain
    return rate * (
        scaled
        - jnp.mean(scaled, axis=-1, keepdims=True)
        - hat * jnp.mean(scaled * hat, axis=-1, keepdims=True)
    )


def spans(kind):
    return [
        (lo, min(lo + 512, kind.width), lo // HEAD, (min(lo + 512, kind.width) - lo) // HEAD)
        for lo in range(0, kind.width, 512)
    ]


def head_rows(rows, span):
    lo, hi, _, n = span
    part = rows[:, lo:hi]
    owner = lax.broadcasted_iota(jnp.int32, part.shape, 1) // HEAD
    nothing = jnp.zeros_like(part)
    return jnp.concatenate([jnp.where(owner == h, part, nothing) for h in range(n)], axis=0)


def from_head_rows(rows, span):
    _, _, _, n = span
    owner = lax.broadcasted_iota(jnp.int32, (SEQS, rows.shape[1]), 1) // HEAD
    total = jnp.zeros((SEQS, rows.shape[1]), rows.dtype)
    for h in range(n):
        total = jnp.where(owner == h, rows[h * SEQS : (h + 1) * SEQS], total)
    return total


def side_by_side(parts):
    return parts[0] if len(parts) == 1 else jnp.concatenate(parts, axis=1)


def get_rows(ref, place, width):
    return side_by_side([ref[c, place, :] for c in range(width // LANES)])


def put_rows(ref, place, value):
    for c in range(value.shape[1] // LANES):
        ref[c, place, :] = value[:, c * LANES : (c + 1) * LANES]


def matrix(ref, kind, start, width):
    return jnp.concatenate(
        [
            ref[part, at, :, start : start + width]
            for at in range(16)
            for part in range(kind.block // 16)
        ],
        axis=0,
    )


def embed_matrix(refs, kind):
    if kind.index == 1:
        return matrix(refs[1], kind, 0, EMB)
    return jnp.concatenate([refs[0][at % 2, at // 2] for at in range(16)], axis=0)


def vector(vec_ref, kind, row):
    return vec_ref[row : row + 1, : kind.width]


def pieces_of(kind):
    return (
        (kind.block, 3 * kind.width),
        (kind.block, kind.width),
        (kind.block, kind.hidden),
        (kind.reduce_rows, kind.width),
        (kind.block, EMB),
        (16, kind.width),
    )


def lane_blocks(kind, plan, p):
    height, width = pieces_of(kind)[p]
    pitch = width // LANES
    base = plan.first_slot[p] * plan.rows if p < VECTORS else (plan.slots - 1) * plan.rows
    return [(c, pl.ds(base + c, height, stride=pitch)) for c in range(pitch)]


def lift(kind, plan, p, slots, flat):
    n = plan.pieces(p)
    slot = plan.first_slot[p]
    rows = slots[slot : slot + n].reshape(n * plan.rows, LANES)
    flat[slot * plan.rows : (slot + n) * plan.rows, :] = rows.astype(WIDE)
    return [(c, flat[place, :]) for c, place in lane_blocks(kind, plan, p)]


def drop(kind, plan, p, value, slots, flat):
    for c, place in lane_blocks(kind, plan, p):
        flat[place, :] = value(c)
    n = plan.pieces(p)
    slot = plan.first_slot[p]
    rows = flat[slot * plan.rows : (slot + n) * plan.rows, :]
    slots[slot : slot + n] = rows.reshape(n, plan.rows, LANES).astype(LOW)


def expand_matrix(ref, kind):
    return jnp.concatenate(
        [
            ref[at % 2, at // 2, : kind.block, : kind.part]
            for at in ((block + TURN) % 16 for block in range(16))
        ],
        axis=0,
    )


def reduce_matrix(ref, kind):
    return ref[:, : kind.reduce_rows, : kind.width].reshape(kind.part, kind.width)


def hidden_bias(vec_ref, kind):
    chip = lax.axis_index("dp") // 2
    whole = vec_ref[...]
    row = lax.broadcasted_iota(jnp.int32, (16, 1), 0)
    line = jnp.sum(jnp.where(row == 10 + chip // 2, whole, 0.0), axis=0, keepdims=True)
    return jnp.where(
        chip % 2 == 0, line[:, : kind.part], line[:, kind.part : 2 * kind.part]
    )


def hidden_kernel(second_ref, raise_ref, reduce_ref, vec_ref, part_ref, raised_ref):
    def run(kind):
        width = kind.width
        rows = second_ref[:, :, :width].reshape(8 * SEQS, width)
        raised = dot_nn(rows, expand_matrix(raise_ref, kind)) + hidden_bias(vec_ref, kind)
        raised_ref[:, : kind.part] = raised
        active = (raised * jax.nn.sigmoid(1.702 * raised)).astype(LOW)
        part = dot_nn(active, reduce_matrix(reduce_ref, kind))
        part_ref[:, :, :width] = part.reshape(8, SEQS, width).astype(LOW)

    each_tower(run)


def hidden_back_kernel(
    grad_ref,
    second_ref,
    raised_ref,
    raise_ref,
    reduce_ref,
    back_ref,
    raise_grad_ref,
    reduce_keep_ref,
    reduce_send_ref,
    bias_ref,
    whole,
):
    def run(kind):
        width, part = kind.width, kind.part
        grads = grad_ref[:, :, :width].reshape(8 * SEQS, width)
        rows = second_ref[:, :, :width].reshape(8 * SEQS, width)
        raised = raised_ref[:, :part]
        gate = jax.nn.sigmoid(1.702 * raised)
        active = (raised * gate).astype(LOW)
        slope = gate + 1.702 * raised * gate * (1.0 - gate)
        raised_grad = dot_nt(grads, reduce_matrix(reduce_ref, kind)) * slope
        low_grad = raised_grad.astype(LOW)
        bias_ref[0:1, :part] = jnp.sum(low_grad.astype(WIDE), axis=0, keepdims=True)
        back = dot_nt(low_grad, expand_matrix(raise_ref, kind))
        back_ref[:, :, :width] = back.reshape(8, SEQS, width).astype(LOW)
        raise_grad = dot_tn(rows, low_grad).reshape(16, kind.block, part).astype(LOW)
        for block in range(16):
            at = (block + TURN) % 16
            raise_grad_ref[at % 2, at // 2, : kind.block, :part] = raise_grad[block]
        whole[:part, :width] = dot_tn(active, grads)
        core = lax.axis_index("dp") % 2
        n = kind.reduce_rows
        keep = pl.multiple_of(core * n, 64)
        send = pl.multiple_of((1 - core) * n, 64)
        reduce_keep_ref[:n, :width] = whole[pl.ds(keep, n), :width]
        reduce_send_ref[:n, :width] = whole[pl.ds(send, n), :width].astype(LOW)

    each_tower(run)


def embed_kernel(part_ref, middle_ref, gat_ref, vec_ref, emb_ref, final_ref, pooled_ref, proj_ref):
    def run(kind):
        width = kind.width
        final = (
            middle_ref[:, :width]
            + jnp.sum(part_ref[:, :, :width].astype(WIDE), axis=0)
            + vector(vec_ref, kind, 7)
        )
        final_ref[:, :width] = final
        hat, _ = standardise(final)
        pooled = (hat * vector(vec_ref, kind, 8) + vector(vec_ref, kind, 9)).astype(LOW)
        pooled_ref[:, :width] = pooled
        proj = dot_nn(pooled, embed_matrix(gat_ref, kind))
        proj_ref[...] = proj
        size = jnp.sum(proj * proj, axis=-1, keepdims=True) + 1e-06
        emb_ref[...] = (proj * lax.rsqrt(size)).astype(LOW)

    each_tower(run)


def objective_kernel(
    scale_ref,
    all_ref,
    valid_ref,
    final_ref,
    proj_ref,
    gat_ref,
    vec_ref,
    low_ref,
    grad_ref,
    proj_grad_ref,
    final_vec_ref,
    loss_ref,
    scale_new_ref,
    own_scr,
):
    def ordered(which):
        blocks = []
        for half in range(2):
            for j in range(16):
                rows = all_ref[j % 2, which * 8 + j // 2].astype(WIDE)
                blocks.append(rows[half * 8 : half * 8 + 8])
        return jnp.concatenate(blocks, axis=0).astype(LOW)

    img, txt = ordered(0), ordered(1)
    total = img.shape[0]
    scale = jnp.exp(jnp.full((1, 1), scale_ref[0], WIDE))
    lines = []
    for d in range(32):
        rows = valid_ref[d % 2, d // 2].astype(WIDE)
        lines.append(jnp.concatenate([rows[:8], rows[8:]], axis=1))
    allowed = jnp.concatenate(lines, axis=0) > 0
    same = lax.broadcasted_iota(jnp.int32, (total, total), 0) == lax.broadcasted_iota(
        jnp.int32, (total, total), 1
    )
    same = same.astype(WIDE)

    def side(left, right):
        logits = scale * dot_nt(left, right)
        masked = jnp.where(allowed, logits, -1e30)
        top = jnp.max(masked, axis=1, keepdims=True)
        lse = jnp.log(jnp.sum(jnp.exp(masked - top), axis=1, keepdims=True)) + top
        terms = 0.5 * (jnp.where(allowed, jnp.exp(logits - lse), 0.0) - same)
        loss = 0.5 * (
            jnp.sum(lse, axis=0, keepdims=True)
            - jnp.sum(jnp.sum(logits * same, axis=1, keepdims=True), axis=0, keepdims=True)
        )
        rate = jnp.sum(jnp.sum(terms * logits, axis=1, keepdims=True), axis=0, keepdims=True)
        return (scale * terms).astype(LOW), loss, rate

    row_back, row_loss, row_rate = side(img, txt)
    col_back, col_loss, col_rate = side(txt, img)
    loss_ref[0] = jnp.sum(row_loss + col_loss) / total
    parts = advance(
        scale_ref[0], scale_ref[1], scale_ref[2], jnp.sum(row_rate + col_rate), scale_rate
    )
    for k in range(3):
        scale_new_ref[k] = parts[k]

    def run(kind):
        width = kind.width
        if kind.index == 0:
            emb_grad = dot_nn(row_back, txt) + dot_tn(col_back, txt)
        else:
            emb_grad = dot_nn(col_back, img) + dot_tn(row_back, img)
        own_scr[...] = emb_grad
        at = lax.axis_index("dp")
        mine = jnp.concatenate(
            [
                own_scr[pl.ds(pl.multiple_of(half * 128 + at * 8, 8), 8), :]
                for half in range(2)
            ],
            axis=0,
        )
        proj = proj_ref[...]
        size = jnp.sum(proj * proj, axis=-1, keepdims=True) + 1e-06
        along = jnp.sum(proj * mine, axis=-1, keepdims=True)
        proj_grad = ((mine - proj * along / size) * lax.rsqrt(size)).astype(LOW)
        proj_grad_ref[...] = proj_grad
        pooled_grad = dot_nt(proj_grad, embed_matrix(gat_ref, kind))
        hat, rate = standardise(final_ref[:, :width])
        final_vec_ref[0:1, :width] = jnp.sum(pooled_grad * hat, axis=0, keepdims=True)
        final_vec_ref[1:2, :width] = jnp.sum(pooled_grad, axis=0, keepdims=True)
        final_grad = norm_back(pooled_grad, vector(vec_ref, kind, 8), hat, rate)
        grad_ref[:, :width] = final_grad
        low = final_grad.astype(LOW)
        low_ref[:, :width] = low
        final_vec_ref[2:3, :width] = jnp.sum(low.astype(WIDE), axis=0, keepdims=True)

    each_tower(run)


def step_kernel(
    plans,
    ends_ref,
    scale_ref,
    img_src,
    txt_src,
    valid_ref,
    img_own,
    txt_own,
    loss_ref,
    scale_new_ref,
    img_keep,
    txt_keep,
    img_chunks,
    txt_chunks,
    second_ref,
    middle_ref,
    query_ref,
    keyed_ref,
    mixture_ref,
    weight_ref,
    first_ref,
    first_rows,
    img_in,
    txt_in,
    ask_ref,
    mix_ref,
    emb_ref,
    vec_ref,
    raise_ref,
    reduce_ref,
    pairs_ref,
    img_slots,
    txt_slots,
    img_extra,
    txt_extra,
    img_last,
    txt_last,
    txt_relay,
    txt_over,
    txt_ending,
    flat,
    ask_block,
    mix_block,
    emb_block,
    plane_block,
    plane_via,
    plane_ref,
    raise_block,
    reduce_block,
    mask_block,
    top_scr,
    at_scr,
    score_scr,
    low_scr,
    grad_ref,
    pooled_ref,
    proj_grad_ref,
    final_vec_ref,
    raise_grad_ref,
    reduce_keep_ref,
    reduce_send_ref,
    bias_ref,
    backs_ref,
    seconds,
    part,
    parts,
    raised,
    emb,
    all_embs,
    final,
    proj,
    low,
    lows,
    back,
    own_scr,
    whole,
    img_send,
    txt_send,
    img_home,
    txt_home,
    rows_grad,
    middle_scr,
    second_scr,
    valued_scr,
    turn_scr,
    shared_scr,
    slope_scr,
    left_scr,
    left_block,
    turn_block,
    left_all,
    turn_all,
    early_block,
    early_all,
    late_block,
    late_all,
    lines_block,
    lines_all,
    raise_half,
    risen_block,
    raise_all,
    reduce_in,
    img_home_slots,
    txt_home_slots,
    gains,
    top_grad_scr,
    deal_send,
    deal_recv,
    deal_edge,
    deal_fetch,
    relay_sems,
    ask_send,
    ask_recv,
    mix_send,
    mix_recv,
    emb_send,
    emb_recv,
    plane_send,
    plane_recv,
    raise_send,
    raise_recv,
    reduce_sems,
    pair_sems,
    mask_send,
    mask_recv,
    group_send,
    group_recv,
    embs_send,
    embs_recv,
    home_sems,
    risen_send,
    risen_recv,
    left_send,
    left_recv,
    turn_send,
    turn_recv,
    early_send,
    early_recv,
    late_send,
    late_recv,
    lines_send,
    lines_recv,
    home_pair_sems,
    collect_send,
    collect_recv,
):
    tower, at = here()
    core = at % 2
    me = tower * 16 + at
    sibling = (tower, at + 1 - 2 * core)
    greet(everyone(tower, at))
    deal_sems = (deal_send, deal_recv, deal_edge, deal_fetch)
    deals = [
        Deal(plans[0], 0, img_src, img_slots, img_extra, img_last, deal_sems),
        Deal(plans[1], 1, txt_src, txt_slots, txt_extra, txt_last, deal_sems, 1, 16 + at),
        Deal(plans[1], 2, txt_relay, txt_slots, txt_over, txt_ending, deal_sems, 1, at),
    ]
    relay = remote(txt_src, txt_relay, relay_sems.at[0], relay_sems.at[1], (1 - tower, at))
    behind = (jnp.int32(1), (at + 15) % 16)
    head = remote(img_src.at[0], img_extra, deal_edge.at[0, 0], deal_edge.at[0, 1], before(me))
    kept = remote(txt_src.at[0], txt_extra, deal_edge.at[1, 0], deal_edge.at[1, 1], behind)
    over = remote(txt_src.at[0], txt_over, deal_edge.at[2, 0], deal_edge.at[2, 1], behind)
    heads = (
        (me > 0, head),
        (me > 16, kept),
        (jnp.logical_and(me > 0, me <= 16), over),
    )
    pair = Pair(txt_own, txt_in, img_own, img_in, pair_sems)
    asks = rings(ask_block, ask_ref, ask_send, ask_recv, Ring, 2 * D_TXT)
    mixes = rings(mix_block, mix_ref, mix_send, mix_recv, Ring, 2 * D_TXT)
    embeds = [
        Chain(emb_block.at[part], emb_ref.at[part], emb_send.at[part], emb_recv.at[part], 1)
        for part in range(2)
    ]
    plane = Plane(plane_block, plane_via, plane_ref, plane_send, plane_recv)
    rise = Group(raise_block, raise_ref, raise_send, raise_recv)
    fall = remote(
        reduce_block, reduce_ref.at[core], reduce_sems.at[0], reduce_sems.at[1], sibling
    )
    fall_own = pltpu.make_async_copy(reduce_block, reduce_ref.at[core], reduce_sems.at[2])
    masks = Spread(mask_block, pairs_ref, mask_send, mask_recv)
    rows = valid_ref[...].astype(WIDE)
    mask_block[...] = jnp.concatenate([rows[:, :LANES], rows[:, LANES:]], axis=0).astype(LOW)

    for when, copy in heads:
        pl.when(when)(copy.start)
    pl.when(tower == 0)(relay.start)
    for deal in deals[:2]:
        deal.start_fetch()
        deal.vectors(False)
    deals[0].whole(True, False)
    deals[1].whole(True, False)
    deals[0].whole(False, False)
    deals[1].whole(False, False)
    deals[0].join()
    deals[1].join()
    pl.when(tower == 1)(relay.wait_recv)
    pair.start()
    deals[2].start_fetch()
    deals[2].whole(True, False)
    deals[2].join()
    deals[2].whole(False, False)

    def put(ref, lane, value):
        if len(ref.shape) == 2:
            ref[: value.shape[0], lane : lane + LANES] = value
        else:
            for part in range(value.shape[0] // 16):
                ref[part, :, lane : lane + LANES] = value[part * 16 : (part + 1) * 16]

    def lift_to(kind, p, ref, start):
        slots = (img_slots, txt_slots)[kind.index]
        for c, value in lift(kind, plans[kind.index], p, slots, flat):
            lane = start + c * LANES
            put(ref, lane, value.astype(ref.dtype))

    def tokens_of(kind, half):
        own, arrived = ((img_own, img_in), (txt_own, txt_in))[kind.index]
        return own if half == kind.index else arrived

    def steps(kind):
        return [(t, kind.run) for t in range(0, kind.length, kind.run)]

    def is_end(kind, half, t, n):
        row = lax.broadcasted_iota(jnp.int32, (8, 1), 0)
        ends = jnp.zeros((8, 1), jnp.int32)
        for i in range(8):
            ends = jnp.where(row == i, ends_ref[(half * 16 + at) * 8 + i], ends)
        position = lax.broadcasted_iota(jnp.int32, (n, 8, 1), 0) + t
        return (position == ends[None]).astype(WIDE)

    def normalise(kind, half):
        width, room = kind.width, kind.room
        ref = tokens_of(kind, half)
        gain, shift = vector(vec_ref, kind, 0), vector(vec_ref, kind, 1)
        tops, raws = jnp.zeros((8, width), WIDE), jnp.zeros((8, width), WIDE)
        for t, n in steps(kind):
            rows = ref[t : t + n].astype(WIDE).reshape(n * 8, width)
            hat, _ = standardise(rows)
            first = (hat * gain + shift).astype(LOW).astype(WIDE)
            put_rows(first_rows, pl.ds(t * 8, n * 8), first)
            if kind.causal:
                chosen = is_end(kind, half, t, n)
                tops = tops + jnp.sum(first.reshape(n, 8, width) * chosen, axis=0)
                raws = raws + jnp.sum(rows.reshape(n, 8, width) * chosen, axis=0)
            elif t == 0:
                tops, raws = first[:8], rows[:8]
        top_scr[half * 8 : half * 8 + 8, :width] = tops
        at_scr[half * 8 : half * 8 + 8, :width] = raws
        spare = (room - kind.length) * 8
        put_rows(first_rows, pl.ds(kind.length * 8, spare), jnp.zeros((spare, width), WIDE))
        for i in range(8):
            line = get_rows(first_rows, pl.ds(i, room, stride=8), width)
            first_ref[half * 8 + i, :room, :width] = line.astype(LOW)

    def begin(kind):
        deal = deals[kind.index]
        deal.arrived(VECTORS)
        lift_to(kind, VECTORS, vec_ref, 0)
        normalise(kind, kind.index)

    each_tower(begin)

    def place_inputs(kind):
        deals[kind.index].arrived(0)
        slots = (img_slots, txt_slots)[kind.index]
        per = kind.width // LANES
        for c, value in lift(kind, plans[kind.index], 0, slots, flat):
            ref, lane = ask_block, c * LANES
            if c >= 2 * per:
                ref, lane = mix_block, lane - 2 * kind.width
            put(ref, lane, value.astype(LOW))

    each_tower(place_inputs)
    for ring in asks:
        ring.start()

    def place_hidden(kind):
        deal, plan = deals[kind.index], plans[kind.index]
        slots = (img_slots, txt_slots)[kind.index]
        deal.arrived(2)
        per = kind.part // LANES
        for c, value in lift(kind, plan, 2, slots, flat):
            lane = c % per * LANES
            raise_block[c // per, : kind.block, lane : lane + LANES] = value.astype(LOW)
        deal.arrived(3)
        lift_to(kind, 3, reduce_block, 0)

    def place_rest(kind):
        deals[kind.index].arrived(1)
        lift_to(kind, 1, mix_block, kind.width)
        if kind.index == 1:
            deals[1].arrived(EMBED)
            lift_to(kind, EMBED, emb_block, 0)
            deals[0].arrived(EMBED)
            for c, value in lift(TOWERS[0], plans[0], EMBED, img_slots, flat):
                plane_block[:, c * LANES : (c + 1) * LANES] = value.astype(LOW)

    each_tower(place_rest)

    def question(kind):
        width = kind.width
        tops = top_scr[:, :width].astype(LOW)
        query = dot_nn(tops, matrix(ask_ref, kind, 0, width)) + vector(vec_ref, kind, 2)
        query = query.astype(LOW)
        query_ref[:, :width] = query
        for span in spans(kind):
            lo, hi, first_head, n = span
            put_rows(
                keyed_ref,
                pl.ds(first_head * SEQS, n * SEQS),
                dot_nt(head_rows(query, span), matrix(ask_ref, kind, width + lo, hi - lo)) * 0.125,
            )
        dead = (HEADS - kind.heads) * SEQS
        put_rows(keyed_ref, pl.ds(kind.heads * SEQS, dead), jnp.zeros((dead, width), WIDE))

    for ask in asks:
        ask.relay_deep()
    for mix in mixes:
        mix.start()
    for embed in embeds:
        embed.start()
    plane.start()
    for ask in asks:
        ask.relay_row()
    each_tower(place_hidden)
    rise.start()
    fall.start()
    fall_own.start()
    pair.finish()
    each_tower(lambda kind: normalise(kind, 1 - kind.index))
    masks.start()
    for ask in asks:
        ask.finish()
    each_tower(question)
    for ring in (*mixes, *embeds):
        ring.relay_deep()
    plane.relay_deep()

    def score(kind):
        width, room = kind.width, kind.room
        lane = lax.broadcasted_iota(jnp.int32, (HEADS, room), 1)
        for s in range(SEQS):
            keys = get_rows(keyed_ref, pl.ds(s, HEADS, stride=SEQS), width).astype(LOW)
            scores = dot_nt(keys, first_ref[s, :room, :width])
            if kind.causal:
                allowed = lane <= ends_ref[(s // 8 * 16 + at) * 8 + s % 8]
            else:
                allowed = lane < kind.length
            score_scr[s * HEADS : (s + 1) * HEADS, :room] = jnp.where(allowed, scores, -1e30)
        scores = score_scr[:, :room]
        raw = jnp.exp(scores - jnp.max(scores, axis=-1, keepdims=True))
        weights = raw / jnp.sum(raw, axis=-1, keepdims=True)
        head = lax.broadcasted_iota(jnp.int32, (SEQS * HEADS, 1), 0) % HEADS
        weights = jnp.where(head < kind.heads, weights, 0.0)
        weight_ref[:, :room] = weights
        low_scr[: SEQS * HEADS, :room] = weights.astype(LOW)

    each_tower(score)
    for ring in (*mixes, *embeds):
        ring.relay_row()
    plane.relay_row()

    def mixture(kind):
        width, room = kind.width, kind.room
        for s in range(SEQS):
            mixed = dot_nn(
                low_scr[s * HEADS : (s + 1) * HEADS, :room], first_ref[s, :room, :width]
            )
            put_rows(mixture_ref, pl.ds(s, HEADS, stride=SEQS), mixed)
        totals = jnp.sum(
            low_scr[: SEQS * HEADS, :room].astype(WIDE), axis=-1, keepdims=True
        )
        score_scr[...] = jnp.broadcast_to(totals, score_scr.shape)

    each_tower(mixture)

    for mix in mixes:
        mix.finish()

    def answer(kind):
        width = kind.width
        mixed = []
        bias = vector(vec_ref, kind, 3)
        for span in spans(kind):
            lo, hi, first_head, n = span
            z = get_rows(mixture_ref, pl.ds(first_head * SEQS, n * SEQS), width).astype(LOW)
            valued = dot_nn(z, matrix(mix_ref, kind, lo, hi - lo))
            totals = jnp.concatenate(
                [score_scr[pl.ds(first_head + h, SEQS, stride=HEADS), 0:1] for h in range(n)],
                axis=0,
            )
            mixed.append(from_head_rows(valued + totals * bias[:, lo:hi], span))
        mixed = side_by_side(mixed).astype(LOW)
        middle = (
            at_scr[:, :width]
            + dot_nn(mixed, matrix(mix_ref, kind, width, width))
            + vector(vec_ref, kind, 4)
        )
        middle_ref[:, :width] = middle
        hat, _ = standardise(middle)
        second_ref[:, :width] = (
            hat * vector(vec_ref, kind, 5) + vector(vec_ref, kind, 6)
        ).astype(LOW)
        put_rows(mixture_ref, pl.ds(12 * SEQS, SEQS), top_scr[:, :width])
        put_rows(mixture_ref, pl.ds(13 * SEQS, SEQS), mixed.astype(WIDE))

    each_tower(answer)
    rise.relay()
    masks.relay()
    for embed in embeds:
        embed.finish()
    rise.finish()
    fall_own.wait()
    remote(
        reduce_block, reduce_ref.at[1 - core], reduce_sems.at[0], reduce_sems.at[1], sibling
    ).wait_recv()

    sent = group_exchange(False, second_ref, seconds, group_send.at[0], group_recv.at[0])
    hidden_kernel(seconds, raise_ref, reduce_ref, vec_ref, part, raised)
    plane.land()
    sent += group_exchange(True, part, parts, group_send.at[1], group_recv.at[1])
    plane.finish()
    embed_kernel(parts, middle_ref, (plane_ref, emb_ref), vec_ref, emb, final, pooled_ref, proj)
    embs = Spread(emb, all_embs, embs_send, embs_recv)
    embs.start()
    masks.finish()
    embs.relay()
    embs.finish()
    objective_kernel(
        scale_ref,
        all_embs,
        pairs_ref,
        final,
        proj,
        (plane_ref, emb_ref),
        vec_ref,
        low,
        grad_ref,
        proj_grad_ref,
        final_vec_ref,
        loss_ref,
        scale_new_ref,
        own_scr,
    )
    sent += group_exchange(False, low, lows, group_send.at[2], group_recv.at[2])
    hidden_back_kernel(
        lows,
        seconds,
        raised,
        raise_ref,
        reduce_ref,
        back,
        raise_grad_ref,
        reduce_keep_ref,
        reduce_send_ref,
        bias_ref,
        whole,
    )
    sent += group_exchange(True, back, backs_ref, group_send.at[3], group_recv.at[3])
    halves = remote(
        raise_grad_ref.at[1 - core], raise_half, home_sems.at[0], home_sems.at[1], sibling
    )
    fallen = remote(reduce_send_ref, reduce_in, home_sems.at[2], home_sems.at[3], sibling)
    halves.start()
    fallen.start()
    risen_group = Group(risen_block, raise_all, risen_send, risen_recv, False)

    lefts = Blocks(left_block, left_all, left_send, left_recv)
    turns = Blocks(turn_block, turn_all, turn_send, turn_recv)
    early = Chain(early_block, early_all, early_send, early_recv)
    late = Ring(late_block, late_all, late_send, late_recv)
    home_pair = Pair(img_send, img_home, txt_send, txt_home, home_pair_sems)
    collects = [
        Collect(plans[0], 0, img_home_slots, img_chunks, collect_send.at[0], collect_recv),
        Collect(plans[1], 1, txt_home_slots, txt_chunks, collect_send.at[1], collect_recv),
    ]

    def outputs(kind):
        width = kind.width
        second_grad = jnp.sum(backs_ref[:, :, :width].astype(WIDE), axis=0)
        second_scr[:, :width] = second_grad
        hat, rate = standardise(middle_ref[:, :width])
        middle_grad = grad_ref[:, :width] + norm_back(
            second_grad, vector(vec_ref, kind, 5), hat, rate
        )
        middle_scr[:, :width] = middle_grad
        output_grad = middle_grad.astype(LOW)
        mixed_grad = dot_nt(output_grad, matrix(mix_ref, kind, width, width)).astype(LOW)
        early_block[:, 0:width] = query_ref[:, :width]
        early_block[:, WIDTH : WIDTH + width] = mixed_grad
        early_block[:, 2 * WIDTH : 2 * WIDTH + width] = output_grad
        early_block[:, 3 * WIDTH : 3 * WIDTH + EMB] = proj_grad_ref[...]
        left_scr[:, :width] = get_rows(mixture_ref, slice(None), width)
        left_scr[14 * SEQS : 15 * SEQS, :width] = pooled_ref[:, :width].astype(WIDE)
        left_scr[15 * SEQS :, :width] = jnp.zeros((SEQS, width), WIDE)

    each_tower(outputs)
    early.start()

    def turned(kind):
        width, block = kind.width, kind.block
        left_block[:, :block, :] = left_scr[:, :width].T.reshape(16, block, 256).astype(LOW)

    each_tower(turned)
    lefts.start()

    def values(kind):
        width = kind.width
        mixed_grad = early_block[:, WIDTH : WIDTH + width]
        bias = vector(vec_ref, kind, 3)
        dead = kind.heads * SEQS
        put_rows(valued_scr, pl.ds(dead, 256 - dead), jnp.zeros((256 - dead, width), WIDE))
        shared_scr[dead:, :] = jnp.zeros((256 - dead, LANES), WIDE)
        for span in spans(kind):
            lo, hi, first_head, n = span
            rows = head_rows(mixed_grad, span)
            place = pl.ds(first_head * SEQS, n * SEQS)
            put_rows(valued_scr, place, dot_nt(rows, matrix(mix_ref, kind, lo, hi - lo)))
            constant = jnp.sum(rows.astype(WIDE) * bias[:, lo:hi], axis=-1, keepdims=True)
            shared_scr[place, :] = jnp.broadcast_to(constant, (n * SEQS, LANES))

    each_tower(values)
    halves.wait_recv()
    risen_block[...] = (
        raise_grad_ref[core].astype(WIDE) + raise_half[...].astype(WIDE)
    ).astype(LOW)
    risen_group.start()

    def slopes(kind):
        width, room = kind.width, kind.room
        for s in range(SEQS):
            line = pl.ds(s, HEADS, stride=SEQS)
            slope = dot_nt(
                get_rows(valued_scr, line, width).astype(LOW), first_ref[s, :room, :width]
            )
            slope_scr[s * HEADS : (s + 1) * HEADS, :room] = slope + shared_scr[line, 0:1]
        weights = weight_ref[:, :room]
        slope = slope_scr[:, :room]
        slope = weights * (slope - jnp.sum(weights * slope, axis=-1, keepdims=True))
        both = jnp.concatenate(
            [slope.reshape(SEQS, HEADS, room), weights.reshape(SEQS, HEADS, room)], axis=1
        )
        low_scr[:, :room] = both.reshape(2 * SEQS * HEADS, room).astype(LOW)

    each_tower(slopes)
    early.relay_deep()

    def tokens(kind):
        width, room = kind.width, kind.room
        for s in range(SEQS):
            line = pl.ds(s, HEADS, stride=SEQS)
            both = low_scr[2 * s * HEADS : 2 * (s + 1) * HEADS, :room]
            first = first_ref[s, :room, :width]
            put_rows(turn_scr, line, dot_nn(both[:HEADS], first))
            right = jnp.concatenate(
                [get_rows(keyed_ref, line, width), get_rows(valued_scr, line, width)], axis=0
            )
            put_rows(
                rows_grad.at[s // 8],
                pl.ds(s % 8, room, stride=8),
                dot_tn(both, right.astype(LOW)),
            )

    each_tower(tokens)
    early.relay_row()

    def queries(kind):
        width, block = kind.width, kind.block
        grads = []
        for span in spans(kind):
            lo, hi, first_head, n = span
            rows = get_rows(turn_scr, pl.ds(first_head * SEQS, n * SEQS), width).astype(LOW)
            back = dot_nn(rows, matrix(ask_ref, kind, width + lo, hi - lo)) * 0.125
            grads.append(from_head_rows(back, span))
        query_grad = side_by_side(grads).astype(LOW)
        late_block[:, :width] = query_grad
        top_grad_scr[:, :width] = dot_nt(query_grad, matrix(ask_ref, kind, 0, width))
        turn_block[:, :block, :] = (
            get_rows(turn_scr, slice(None), width).T.reshape(16, block, 256).astype(LOW)
        )

    each_tower(queries)
    late.start()
    turns.start()
    gains[...] = jnp.zeros_like(gains)

    def finish(kind, half):
        width = kind.width
        ref = tokens_of(kind, half)
        keep, send = ((img_keep, img_send), (txt_keep, txt_send))[kind.index]
        gain = vector(vec_ref, kind, 0)
        top = top_grad_scr[half * 8 : half * 8 + 8, :width]
        low = middle_scr[half * 8 : half * 8 + 8, :width]
        gain_sum = jnp.zeros((1, width), WIDE)
        shift_sum = jnp.zeros((1, width), WIDE)
        for t, n in steps(kind):
            hat, rate = standardise(ref[t : t + n].astype(WIDE).reshape(n * 8, width))
            grad = get_rows(rows_grad.at[half], pl.ds(t * 8, n * 8), width)
            chosen = None
            if kind.causal:
                chosen = is_end(kind, half, t, n)
            elif t == 0:
                chosen = (lax.broadcasted_iota(jnp.int32, (n, 8, 1), 0) == 0).astype(WIDE)
            if chosen is not None:
                grad = grad + (chosen * top[None]).reshape(n * 8, width)
            gain_sum += jnp.sum(grad * hat, axis=0, keepdims=True)
            shift_sum += jnp.sum(grad, axis=0, keepdims=True)
            result = norm_back(grad, gain, hat, rate)
            if chosen is not None:
                result = result + (chosen * low[None]).reshape(n * 8, width)
            result = result.reshape(n, 8, width)
            if half == kind.index:
                keep[t : t + n] = result
            else:
                send[t : t + n] = result.astype(LOW)
        gains[0:1, :width] += gain_sum
        gains[1:2, :width] += shift_sum

    each_tower(lambda kind: finish(kind, 1 - kind.index))
    home_pair.start()
    risen_group.finish()
    fallen.wait_recv()

    def slots_of(kind):
        return (img_home_slots, txt_home_slots)[kind.index]

    def hidden_grads(kind):
        plan, collect = plans[kind.index], collects[kind.index]
        block, n, per = kind.block, kind.reduce_rows, kind.part // LANES

        def risen(c):
            chip, lane = c // per, c % per * LANES
            return raise_all[chip, :block, lane : lane + LANES].astype(WIDE)

        def fallen(c):
            lane = c * LANES
            return reduce_keep_ref[:n, lane : lane + LANES] + reduce_in[
                :n, lane : lane + LANES
            ].astype(WIDE)

        drop(kind, plan, 2, risen, slots_of(kind), flat)
        collect.piece(2, False)
        drop(kind, plan, 3, fallen, slots_of(kind), flat)
        collect.piece(3, False)

    each_tower(hidden_grads)
    late.relay_deep()
    each_tower(lambda kind: finish(kind, kind.index))
    late.relay_row()

    def lines(kind):
        width = kind.width
        hat, _ = standardise(middle_ref[:, :width])
        second_grad = second_scr[:, :width]

        def column_sum(value):
            return jnp.sum(value.astype(WIDE), axis=0, keepdims=True)

        mixed_grad = early_block[:, WIDTH : WIDTH + width].astype(WIDE)
        weights = low_scr[:, : kind.room].astype(WIDE).reshape(SEQS, 2 * HEADS, kind.room)
        totals = jnp.sum(weights[:, HEADS:], axis=-1, keepdims=True).reshape(SEQS * HEADS, 1)
        shared_scr[...] = jnp.broadcast_to(totals, shared_scr.shape)
        value_bias = []
        for lo, hi, first_head, n in spans(kind):
            owner = lax.broadcasted_iota(jnp.int32, (SEQS, hi - lo), 1) // HEAD
            scaled = jnp.zeros((SEQS, hi - lo), WIDE)
            for h in range(n):
                total = shared_scr[pl.ds(first_head + h, SEQS, stride=HEADS), 0:1]
                scaled = jnp.where(owner == h, mixed_grad[:, lo:hi] * total, scaled)
            value_bias.append(column_sum(scaled))
        hidden = bias_ref[0:1, : kind.part]
        parts = [
            gains[0:1, :width],
            gains[1:2, :width],
            column_sum(late_block[:, :width]),
            side_by_side(value_bias),
            column_sum(early_block[:, 2 * WIDTH : 2 * WIDTH + width]),
            column_sum(second_grad * hat),
            column_sum(second_grad),
            final_vec_ref[2:3, :width],
            final_vec_ref[0:1, :width],
            final_vec_ref[1:2, :width],
            jnp.concatenate([hidden, jnp.zeros((1, width - kind.part), WIDE)], axis=1),
            jnp.zeros((5, width), WIDE),
        ]
        lines_block[:, :width] = jnp.concatenate(parts, axis=0)

    each_tower(lines)
    line_copy = remote(
        lines_block, lines_all.at[at], lines_send.at[0], lines_recv.at[at], (tower, jnp.int32(0))
    )
    line_own = pltpu.make_async_copy(lines_block, lines_all.at[at], lines_recv.at[at])
    pl.when(at > 0)(line_copy.start)
    pl.when(at == 0)(line_own.start)

    early.finish()
    lefts.finish()

    def from_early(kind):
        plan, collect = plans[kind.index], collects[kind.index]
        width, block = kind.width, kind.block

        def gathered(k):
            lane = lax.broadcasted_iota(jnp.int32, (block, LANES), 1) // SEQS
            halves = []
            for side in range(2):
                total = jnp.zeros((block, LANES), WIDE)
                for j in range(8):
                    part = left_all[side * 8 + j, :block, LANES:].astype(WIDE)
                    shift = (j * SEQS - (k - 8) * SEQS) % LANES
                    turned_part = pltpu.roll(part, shift, 1) if shift else part
                    total = jnp.where(lane == j, turned_part, total)
                halves.append(total)
            return jnp.concatenate(halves, axis=1).astype(LOW)

        def right(start, wide):
            return early_all[:, :, start : start + wide].reshape(256, wide)

        output = dot_nn(gathered(13), right(2 * WIDTH, width))
        drop(
            kind, plan, 1, lambda c: output[:, c * LANES : (c + 1) * LANES], slots_of(kind), flat
        )
        collect.piece(1, False)
        embed = dot_nn(gathered(14), right(3 * WIDTH, EMB))
        drop(kind, plan, 4, lambda c: embed[:, c * LANES : (c + 1) * LANES], slots_of(kind), flat)
        collect.piece(4, False)
        left_scr[:block, :256] = gathered(12).astype(WIDE)

    each_tower(from_early)
    for when, copy in heads:
        pl.when(when)(copy.wait_send)
    pl.when(tower == 0)(relay.wait_send)
    for group in (pair, *asks, *mixes, *embeds, plane, rise, masks, embs, *deals):
        group.drain()
    late.finish()
    turns.finish()

    def from_late(kind):
        plan, collect = plans[kind.index], collects[kind.index]
        width, block = kind.width, kind.block
        ask = dot_nn(left_scr[:block, :256].astype(LOW), late_all[:, :, :width].reshape(256, width))

        def outer(side_ref, start, span):
            lo, hi, first_head, n = span
            lane = first_head * SEQS
            total = jnp.zeros((block, hi - lo), WIDE)
            for j in range(8):
                left, rows = [], []
                for source in (2 * j, 2 * j + 1):
                    left.append(side_ref[source, :block, lane : lane + LANES])
                    rows.append(
                        head_rows(early_all[source, :, start : start + width], span)
                    )
                    if n < 8:
                        rows.append(jnp.zeros(((8 - n) * SEQS, hi - lo), LOW))
                total += dot_nn(
                    jnp.concatenate(left, axis=1), jnp.concatenate(rows, axis=0)
                )
            return total

        keys = side_by_side([outer(turn_all, 0, span) for span in spans(kind)]) * 0.125
        worth = side_by_side([outer(left_all, WIDTH, span) for span in spans(kind)])
        per = width // LANES

        def inputs(c):
            value = (ask, keys, worth)[c // per]
            return value[:, c % per * LANES : (c % per + 1) * LANES]

        drop(kind, plan, 0, inputs, slots_of(kind), flat)
        collect.piece(0, False)

    each_tower(from_late)

    @pl.when(at == 0)
    def _():
        for k in range(1, 16):
            remote(
                lines_block, lines_all.at[k], lines_send.at[0], lines_recv.at[k], sibling
            ).wait_recv()
        line_own.wait()

        def vectors(kind):
            width, part = kind.width, kind.part
            whole = [jnp.sum(lines_all[:, :10, :width], axis=0)]
            for row in range(4):
                pair_of = []
                for chip in (2 * row, 2 * row + 1):
                    pair_of.append(
                        lines_all[2 * chip, 10:11, :part] + lines_all[2 * chip + 1, 10:11, :part]
                    )
                whole.append(jnp.concatenate(pair_of, axis=1))
            whole.append(jnp.zeros((2, width), WIDE))
            result = jnp.concatenate(whole, axis=0)
            drop(
                kind,
                plans[kind.index],
                VECTORS,
                lambda c: result[:, c * LANES : (c + 1) * LANES],
                slots_of(kind),
                flat,
            )

        each_tower(vectors)

    each_tower(lambda kind: collects[kind.index].piece(VECTORS, False))
    home_pair.finish()

    @pl.when(tower == 1)
    def _():
        img_keep[...] = img_home[...].astype(WIDE)

    @pl.when(tower == 0)
    def _():
        txt_keep[...] = txt_home[...].astype(WIDE)

    for copy in (*sent, fall, fallen, halves):
        copy.wait_send()
    pl.when(at > 0)(line_copy.wait_send)
    for group in (risen_group, lefts, turns, early, late, home_pair):
        group.drain()

    def drain(kind):
        for p in range(VECTORS + 1):
            collects[kind.index].piece(p, True)

    each_tower(drain)
    for collect in collects:
        collect.finish()


ROWS_LOW = ((SEQS, WIDTH), LOW)
ROWS_WIDE = ((SEQS, WIDTH), WIDE)
HEAD_ROWS = ((WIDTH // LANES, SEQS * HEADS, LANES), WIDE)
LANE_ROWS = ((SEQS * HEADS, LANES), WIDE)
GROUP = ((8, SEQS, WIDTH), LOW)
HIDDEN_BLOCKS = ((2, 8, 48, PART), LOW)
OUTER = ((16, 48, SEQS * HEADS), LOW)


def chunk_shapes(plan, n):
    return ((n, plan.rows, LANES), LOW)


def run_step(scalars, chunks, valid, tokens, plans):
    most = max(plan.local for plan in plans) + 17
    slots = max(plan.slots for plan in plans)
    edges = [((plan.rows, LANES), LOW) for plan in plans]
    rooms = [((kind.length, 8, kind.width), LOW) for kind in TOWERS]
    outs = [((kind.length, 8, kind.width), WIDE) for kind in TOWERS] + [
        chunk_shapes(plan, plan.local) for plan in plans
    ]
    scratch = [
        ROWS_LOW,
        ROWS_WIDE,
        ROWS_LOW,
        HEAD_ROWS,
        HEAD_ROWS,
        LANE_ROWS,
        ((SEQS, ROOM, WIDTH), LOW),
        ((WIDTH // LANES, ROOM * 8, LANES), WIDE),
        rooms[0],
        rooms[1],
        ((3, 16, 16, 2 * WIDTH), LOW),
        ((3, 16, 16, 2 * WIDTH), LOW),
        ((3, 16, 16, EMB), LOW),
        ROWS_WIDE,
        HIDDEN_BLOCKS,
        ((2, 192, WIDTH), LOW),
        ((2, 16, 16, LANES), LOW),
        chunk_shapes(plans[0], plans[0].slots),
        chunk_shapes(plans[1], plans[1].slots),
        edges[0],
        edges[1],
        edges[0],
        edges[1],
        chunk_shapes(plans[1], plans[1].local),
        edges[1],
        edges[1],
        ((plans[0].slots * plans[0].rows, LANES), WIDE),
        ((3, 16, 2 * WIDTH), LOW),
        ((3, 16, 2 * WIDTH), LOW),
        ((3, 16, EMB), LOW),
        ((48, EMB), LOW),
        ((8, 48, EMB), LOW),
        ((2, 8, 48, EMB), LOW),
        ((8, 48, PART), LOW),
        ((192, WIDTH), LOW),
        ((16, LANES), LOW),
        ROWS_WIDE,
        ROWS_WIDE,
        LANE_ROWS,
        ((2 * SEQS * HEADS, LANES), LOW),
        ROWS_WIDE,
        ROWS_LOW,
        ((SEQS, EMB), LOW),
        ((8, WIDTH), WIDE),
        HIDDEN_BLOCKS,
        ((192, WIDTH), WIDE),
        ((192, WIDTH), LOW),
        ((8, PART), WIDE),
        GROUP,
        GROUP,
        GROUP,
        GROUP,
        ((128, PART), WIDE),
        ((SEQS, EMB), LOW),
        ((2, 16, SEQS, EMB), LOW),
        ROWS_WIDE,
        ((SEQS, EMB), WIDE),
        ROWS_LOW,
        GROUP,
        GROUP,
        ((256, EMB), WIDE),
        ((PART, WIDTH), WIDE),
        rooms[0],
        rooms[1],
        rooms[0],
        rooms[1],
        ((2, WIDTH // LANES, ROOM * 8, LANES), WIDE),
        ROWS_WIDE,
        ROWS_WIDE,
        HEAD_ROWS,
        HEAD_ROWS,
        LANE_ROWS,
        LANE_ROWS,
        ((SEQS * HEADS, WIDTH), WIDE),
        OUTER,
        OUTER,
        OUTER,
        OUTER,
        ((SEQS, 3 * WIDTH + EMB), LOW),
        ((16, SEQS, 3 * WIDTH + EMB), LOW),
        ROWS_LOW,
        ((16, SEQS, WIDTH), LOW),
        ROWS_WIDE,
        ((16, SEQS, WIDTH), WIDE),
        ((8, 48, PART), LOW),
        ((8, 48, PART), LOW),
        ((8, 48, PART), LOW),
        ((192, WIDTH), LOW),
        chunk_shapes(plans[0], plans[0].slots),
        chunk_shapes(plans[1], plans[1].slots),
        ((8, WIDTH), WIDE),
        ROWS_WIDE,
    ]
    semaphores = [
        (3, most),
        (2, 6,),
        (3, 2),
        (3,),
        (2,),
        (3, 16),
        (3, 15),
        (3, 16),
        (3, 15),
        (3, 20),
        (3, 15),
        (10,),
        (9,),
        (9,),
        (8,),
        (3,),
        (2,),
        (17,),
        (16,),
        (4, 8,),
        (4, 7,),
        (17,),
        (16,),
        (4,),
        (9,),
        (8,),
        (16,),
        (15,),
        (16,),
        (15,),
        (20,),
        (15,),
        (16,),
        (15,),
        (1,),
        (16,),
        (2,),
        (2, 2, slots,),
        (2,),
    ]
    smem = pl.BlockSpec(memory_space=pltpu.SMEM)
    vmem = pl.BlockSpec(memory_space=pltpu.VMEM)
    like = jax.ShapeDtypeStruct
    return pl.pallas_call(
        functools.partial(step_kernel, plans),
        out_shape=[like((1,), WIDE), like((3,), WIDE)] + [like(*out) for out in outs],
        in_specs=[smem, smem, ANY, ANY, vmem, vmem, vmem],
        out_specs=[smem, smem, vmem, vmem, vmem, vmem],
        scratch_shapes=[pltpu.VMEM(*each) for each in scratch]
        + [pltpu.SemaphoreType.DMA(shape) for shape in semaphores],
        compiler_params=comm_params(0),
    )(*scalars, *chunks, valid, *tokens)


def to_chunks(flat, plan, me):
    start = me * plan.share % plan.chunk
    padded = jnp.pad(flat, (plan.chunk, plan.local * plan.chunk - plan.share))
    piece = lax.dynamic_slice(padded, (plan.chunk - start,), (plan.local * plan.chunk,))
    return piece.astype(LOW).reshape(plan.local, plan.rows, LANES)


def from_chunks(chunks, plan, me):
    start = me * plan.share % plan.chunk
    return lax.dynamic_slice(chunks.reshape(-1), (start,), (plan.share,)).astype(WIDE)


def step(
    img_tokens,
    txt_tokens,
    txt_ends,
    valid,
    img_master,
    img_moment,
    img_average,
    txt_master,
    txt_moment,
    txt_average,
    scale_state,
):
    me = lax.axis_index(("tower", "dp"))
    plans = (
        Plan(0, img_master.shape[0], 96, (9, 3, 12, 12, 2)),
        Plan(1, txt_master.shape[0], 64, (6, 2, 8, 8, 2)),
    )
    loss, scale_new, img_grad, txt_grad, img_chunks, txt_chunks = run_step(
        (txt_ends, scale_state),
        (to_chunks(img_master, plans[0], me), to_chunks(txt_master, plans[1], me)),
        valid,
        (jnp.transpose(img_tokens, (1, 0, 2)), jnp.transpose(txt_tokens, (1, 0, 2))),
        plans,
    )
    img_new = advance(
        img_master, img_moment, img_average, from_chunks(img_chunks, plans[0], me), step_rate
    )
    txt_new = advance(
        txt_master, txt_moment, txt_average, from_chunks(txt_chunks, plans[1], me), step_rate
    )
    return (
        loss[0],
        jnp.transpose(img_grad, (1, 0, 2)),
        jnp.transpose(txt_grad, (1, 0, 2)),
        img_new[0],
        img_new[1],
        img_new[2],
        img_new[0].astype(LOW),
        txt_new[0],
        txt_new[1],
        txt_new[2],
        txt_new[0].astype(LOW),
        scale_new,
    )


def from_partner(value, axis, stride):
    mask = 2**stride
    pairs = [(source, source ^ mask) for source in range(lax.axis_size(axis))]
    return lax.ppermute(value, axis, pairs)


def round_value(v):
    return lax.optimization_barrier(v.astype(jnp.bfloat16)).astype(jnp.float32)


def make_low():

    def value_keep(v):
        return (round_value(v), None)

    def grad_pass(kept, grad):
        return (grad,)

    rounded = jax.custom_vjp(round_value)
    rounded.defvjp(value_keep, grad_pass)
    return rounded


def low(v):
    return make_low()(v)


def make_low_back():

    def identity(v):
        return v

    def value_pass(v):
        return (v, None)

    def grad_round(kept, grad):
        return (round_value(grad),)

    passed = jax.custom_vjp(identity)
    passed.defvjp(value_pass, grad_round)
    return passed


def low_back(v):
    return make_low_back()(v)


def both_ways(value):
    return low(low_back(value))


def product(left, right):
    return jnp.matmul(left, right)


def contract(form, left, right):
    return jnp.einsum(form, left, right)


def layer_norm(values, gain_row, shift_row):
    centred = values - jnp.mean(values, axis=-1, keepdims=True)
    spread = jnp.mean(centred * centred, axis=-1, keepdims=True)
    return centred * lax.rsqrt(spread + 1e-05) * gain_row + shift_row


def unpack(flat_weights, model_width, hidden_width, embed_width):
    piece_shapes = [
        (model_width, 3 * model_width),
        (model_width, model_width),
        (model_width, hidden_width),
        (hidden_width, model_width),
        (model_width, embed_width),
        (10, model_width),
        (hidden_width,),
    ]
    pieces = []
    offset = 0
    for piece_shape in piece_shapes:
        length = math.prod(piece_shape)
        pieces.append(flat_weights[offset : offset + length].reshape(piece_shape))
        offset = offset + length
    return pieces


def encode(tokens, flat_weights, positions, causal, model_width, hidden_width, embed_width):
    w_inputs, w_output, w_expand, w_reduce, w_embed, vectors, expand_bias = unpack(
        flat_weights, model_width, hidden_width, embed_width
    )
    groups = tokens.shape[0]
    length = tokens.shape[1]
    first = low(layer_norm(tokens, vectors[0], vectors[1]))
    bias_in = jnp.concatenate([vectors[2], jnp.zeros_like(vectors[2]), vectors[3]])
    joined = both_ways(product(first, w_inputs) + bias_in)
    joined = joined.reshape(groups, length, 3, model_width // HEAD, HEAD)
    scores = low_back(contract("gqhd,gkhd->ghqk", joined[:, :, 0], joined[:, :, 1]) * 0.125)
    if causal:
        row_index = lax.broadcasted_iota(jnp.int32, (length, length), 0)
        col_index = lax.broadcasted_iota(jnp.int32, (length, length), 1)
        scores = jnp.where(col_index <= row_index, scores, -1e30)
    row_top = jnp.max(scores, axis=-1, keepdims=True)
    raw_weights = jnp.exp(scores - row_top)
    attention = low(raw_weights / jnp.sum(raw_weights, axis=-1, keepdims=True))
    mixed_heads = both_ways(
        contract("ghqk,gkhd->gqhd", attention, joined[:, :, 2]).reshape(groups, length, model_width)
    )
    middle = tokens + low_back(product(mixed_heads, w_output) + vectors[4])
    second = low(layer_norm(middle, vectors[5], vectors[6]))
    raised = low_back(product(second, w_expand) + expand_bias)
    active = low(raised * jax.nn.sigmoid(1.702 * raised))
    final_rows = middle + low_back(product(active, w_reduce) + vectors[7])
    pooled = jnp.take_along_axis(final_rows, positions[:, None, None], axis=1)[:, 0]
    pooled = low(layer_norm(pooled, vectors[8], vectors[9]))
    projected = low_back(product(pooled, w_embed))
    return low(
        projected * lax.rsqrt(jnp.sum(projected * projected, axis=-1, keepdims=True) + 1e-06)
    )


def inner(left, right):
    return lax.dot_general(
        left, right, (((1,), (1,)), ((), ())), preferred_element_type=jnp.float32
    )


def across(left, right):
    return lax.dot_general(
        left, right, (((0,), (0,)), ((), ())), preferred_element_type=jnp.float32
    )


def softmax_total(logits, allowed):
    masked = jnp.where(allowed, logits, -1e30)
    row_top = jnp.max(masked, axis=1, keepdims=True)
    return jnp.log(jnp.sum(jnp.exp(masked - row_top), axis=1)) + row_top[:, 0]


def advance(master, moment, average, grads, rate):
    moment_new = momentum_rate * moment + grads
    master_new = master - rate * (grads + momentum_rate * moment_new)
    average_new = average_rate * average + (1.0 - average_rate) * master_new
    return (master_new, moment_new, average_new)


def padded_to(flat, length):
    return jnp.pad(flat, (0, length - flat.shape[0]))


def body(
    img_tokens,
    txt_tokens,
    txt_ends,
    valid,
    img_master,
    img_moment,
    img_average,
    txt_master,
    txt_moment,
    txt_average,
    scale_state,
):
    batch_rows = img_tokens.shape[0]
    total_rows = batch_rows * lax.axis_size(("tower", "dp"))
    device_at = lax.axis_index(("tower", "dp"))
    tower_at = lax.axis_index("tower")
    is_image = tower_at == 0
    img_share = img_master.shape[0]
    txt_share = txt_master.shape[0]
    img_count = img_tokens.size
    txt_count = txt_tokens.size
    shard_room = max(img_share, txt_share)
    token_room = max(img_count, txt_count)
    tower_count = lax.axis_size("dp")
    dp_at = lax.axis_index("dp")
    img_low = padded_to(img_master.astype(jnp.bfloat16), shard_room)
    txt_low = padded_to(txt_master.astype(jnp.bfloat16), shard_room)
    token_out = jnp.where(
        is_image,
        padded_to(txt_tokens.reshape(-1), token_room),
        padded_to(img_tokens.reshape(-1), token_room),
    )
    weight_out = jnp.where(is_image, txt_low, img_low)
    weight_mine = jnp.where(is_image, img_low, txt_low)
    token_in, weight_in = from_partner((token_out, weight_out), "tower", 0)
    stacked = jnp.where(
        is_image, jnp.stack([weight_mine, weight_in]), jnp.stack([weight_in, weight_mine])
    )
    gathered = lax.all_gather(stacked, "dp", axis=1, tiled=True)
    pair_ends = jnp.concatenate(
        [
            lax.dynamic_slice_in_dim(txt_ends, dp_at * batch_rows, batch_rows),
            lax.dynamic_slice_in_dim(txt_ends, (tower_count + dp_at) * batch_rows, batch_rows),
        ]
    )
    pair_zero = jnp.zeros((2 * batch_rows,), jnp.int32)

    def image_weights(whole):
        return whole.reshape(2, tower_count, shard_room).reshape(-1).astype(jnp.float32)

    def text_weights(whole):
        return (
            whole.reshape(2, tower_count, shard_room)[:, :, :txt_share]
            .reshape(-1)
            .astype(jnp.float32)
        )

    def image_rows(arrived):
        return jnp.concatenate(
            [img_tokens, arrived[:img_count].reshape(img_tokens.shape)], axis=0
        ).astype(jnp.float32)

    def text_rows(arrived):
        return jnp.concatenate([arrived.reshape(txt_tokens.shape), txt_tokens], axis=0).astype(
            jnp.float32
        )

    def image_encode(rows, flat):
        return encode(rows, flat, pair_zero, False, D_IMG, FF_IMG, EMB)

    def text_encode(rows, flat):
        return encode(rows, flat, pair_ends, True, D_TXT, FF_TXT, EMB)

    def image_forward(operands):
        return image_encode(image_rows(operands[1]), image_weights(operands[0]))

    def text_forward(operands):
        return text_encode(text_rows(operands[1]), text_weights(operands[0]))

    pair_emb = lax.cond(is_image, image_forward, text_forward, (gathered, token_in)).astype(
        jnp.bfloat16
    )
    emb_in = from_partner(pair_emb, "tower", 0)
    img_pair = jnp.where(is_image, pair_emb, emb_in)
    txt_pair = jnp.where(is_image, emb_in, pair_emb)
    row_start = tower_at * batch_rows
    img_local = lax.dynamic_slice_in_dim(img_pair, row_start, batch_rows)
    txt_local = lax.dynamic_slice_in_dim(txt_pair, row_start, batch_rows)
    img_all, txt_all = (
        lax.all_gather(img_local, ("tower", "dp"), axis=0, tiled=True),
        lax.all_gather(txt_local, ("tower", "dp"), axis=0, tiled=True),
    )
    logit_scale = jnp.exp(scale_state[0])
    offset = device_at * batch_rows
    row_index = lax.broadcasted_iota(jnp.int32, (batch_rows, total_rows), 0) + offset
    col_index = lax.broadcasted_iota(jnp.int32, (batch_rows, total_rows), 1)
    diagonal = (row_index == col_index).astype(jnp.float32)
    allowed = valid > 0
    row_logits = logit_scale * inner(img_local, txt_all)
    col_logits = logit_scale * inner(txt_local, img_all)
    row_lse = softmax_total(row_logits, allowed)
    col_lse = softmax_total(col_logits, allowed)
    partial_loss = 0.5 * (
        jnp.sum(row_lse)
        - jnp.sum(row_logits * diagonal)
        + jnp.sum(col_lse)
        - jnp.sum(col_logits * diagonal)
    )
    row_terms = 0.5 * (jnp.where(allowed, jnp.exp(row_logits - row_lse[:, None]), 0.0) - diagonal)
    col_terms = 0.5 * (jnp.where(allowed, jnp.exp(col_logits - col_lse[:, None]), 0.0) - diagonal)
    partial_scale = jnp.sum(row_terms * row_logits) + jnp.sum(col_terms * col_logits)
    row_back = (logit_scale * row_terms).astype(jnp.bfloat16)
    col_back = (logit_scale * col_terms).astype(jnp.bfloat16)
    img_emb_grad = jnp.dot(row_back, txt_all, preferred_element_type=jnp.float32)
    txt_emb_grad = jnp.dot(col_back, img_all, preferred_element_type=jnp.float32)
    img_extra, txt_extra = (
        lax.psum_scatter(
            across(col_back, txt_local), ("tower", "dp"), scatter_dimension=0, tiled=True
        ),
        lax.psum_scatter(
            across(row_back, img_local), ("tower", "dp"), scatter_dimension=0, tiled=True
        ),
    )
    img_emb_grad = img_emb_grad + img_extra
    txt_emb_grad = txt_emb_grad + txt_extra
    sums = lax.psum((partial_loss, partial_scale), ("tower", "dp"))
    grad_out = jnp.where(is_image, txt_emb_grad, img_emb_grad)
    grad_in = from_partner(grad_out, "tower", 0)
    pair_cot = jnp.where(
        is_image,
        jnp.concatenate([img_emb_grad, grad_in], axis=0),
        jnp.concatenate([grad_in, txt_emb_grad], axis=0),
    )

    def image_backward(operands):
        recomputed, tower_pullback = jax.vjp(
            image_encode, image_rows(operands[1]), image_weights(operands[0])
        )
        rows_grad, flat_grad = tower_pullback(operands[2])
        own_part = padded_to(rows_grad[:batch_rows].reshape(-1), token_room)
        sent_part = padded_to(rows_grad[batch_rows:].reshape(-1), token_room)
        stacked_grad = flat_grad.reshape(2, tower_count, img_share)
        return (own_part, sent_part, stacked_grad)

    def text_backward(operands):
        recomputed, tower_pullback = jax.vjp(
            text_encode, text_rows(operands[1]), text_weights(operands[0])
        )
        rows_grad, flat_grad = tower_pullback(operands[2])
        own_part = padded_to(rows_grad[batch_rows:].reshape(-1), token_room)
        sent_part = padded_to(rows_grad[:batch_rows].reshape(-1), token_room)
        stacked_grad = jnp.pad(
            flat_grad.reshape(2, tower_count, txt_share),
            ((0, 0), (0, 0), (0, shard_room - txt_share)),
        )
        return (own_part, sent_part, stacked_grad)

    own_part, sent_part, stacked_grad = lax.cond(
        is_image, image_backward, text_backward, (gathered, token_in, pair_cot)
    )
    summed = lax.psum_scatter(stacked_grad, "dp", scatter_dimension=1, tiled=True)
    kept_part = jnp.where(is_image, summed[0, 0], summed[1, 0])
    sent_share = jnp.where(is_image, summed[1, 0], summed[0, 0])
    home_weights, home_tokens = (
        from_partner(sent_share.astype(jnp.bfloat16), "tower", 0).astype(sent_share.dtype),
        from_partner(sent_part.astype(jnp.bfloat16), "tower", 0).astype(sent_part.dtype),
    )
    img_owned = jnp.where(is_image, kept_part, home_weights)
    txt_owned = jnp.where(is_image, home_weights, kept_part)[:txt_share]
    img_grad = jnp.where(is_image, own_part, home_tokens)[:img_count].reshape(img_tokens.shape)
    txt_grad = jnp.where(is_image, home_tokens, own_part).reshape(txt_tokens.shape)
    img_new = advance(img_master, img_moment, img_average, img_owned, step_rate)
    txt_new = advance(txt_master, txt_moment, txt_average, txt_owned, step_rate)
    scale_parts = advance(scale_state[0], scale_state[1], scale_state[2], sums[1], scale_rate)
    scale_new = jnp.stack([scale_parts[0], scale_parts[1], scale_parts[2]])
    return (
        sums[0] / total_rows,
        img_grad,
        txt_grad,
        img_new[0],
        img_new[1],
        img_new[2],
        img_new[0].astype(jnp.bfloat16),
        txt_new[0],
        txt_new[1],
        txt_new[2],
        txt_new[0].astype(jnp.bfloat16),
        scale_new,
    )


def solution(mesh):
    in_specs = (
        P(("tower", "dp"), None, None),
        P(("tower", "dp"), None, None),
        P(),
        P(("tower", "dp"), None),
        P(("tower", "dp")),
        P(("tower", "dp")),
        P(("tower", "dp")),
        P(("tower", "dp")),
        P(("tower", "dp")),
        P(("tower", "dp")),
        P(),
    )
    out_specs = (
        P(),
        P(("tower", "dp"), None, None),
        P(("tower", "dp"), None, None),
        P(("tower", "dp")),
        P(("tower", "dp")),
        P(("tower", "dp")),
        P(("tower", "dp")),
        P(("tower", "dp")),
        P(("tower", "dp")),
        P(("tower", "dp")),
        P(("tower", "dp")),
        P(),
    )
    run = step if (mesh.shape["tower"], mesh.shape["dp"]) == (2, 16) else body
    return jax.shard_map(run, mesh=mesh, in_specs=in_specs, out_specs=out_specs, check_vma=False)
```
